32 devices in a mesh: grp: 2 (over y), blk: 4 (over z), op: 4 (over x, core).
Axes of the slice: x: 2, y: 2, z: 4, core: 2. Of those that a mesh axis runs over, the one named last changes fastest.
Arguments:
- psi: bfloat16 [8, 256, 2048], P(('grp', 'blk')), parts along dimension 0, may hold values from -6 to 6
- left_ops: bfloat16 [8, 8, 256, 256], P('op', ('grp', 'blk')), parts along dimension 1, may hold values from -0.375 to 0.375
- right_ops: bfloat16 [8, 64, 64, 64], P('op', ('grp', 'blk')), parts along dimension 1, may hold values from -0.75 to 0.75
- term_shift: int32 [8], P('op'), may hold values from -2 to 2
- slot_sector: int32 [8], P('grp'), parts along dimension 0, may hold values from 0 to 3, each once
- sector_width: int32 [8], P('grp'), parts along dimension 0, may hold values from 64 to 256, as said below
- diag_left: float32 [8, 256], P('grp'), parts along dimension 0, may hold values from 0.25 to 4
- diag_right: float32 [4096], P(('grp', 'blk')), parts along dimension 0, may hold values from 0.25 to 4
Outputs:
- new_vector: bfloat16 [8, 256, 2048], P('grp', 'op', 'blk'), parts along dimension 0
- residual: bfloat16 [8, 256, 2048], P('grp', 'op', 'blk'), parts along dimension 0
- energy: float32 [2], P('grp'), parts along dimension 0
The draws below stay inside these ranges and needn't reach their ends.
There are 2 independent parts, one for each index of `grp`. The reference program is written for one: setup_inputs(seed, part) draws one part's arguments, and reference() takes and returns one part's arrays. A program takes and returns all parts, laid end to end along the dimension named above; an argument that names none is the same for every part. Nothing has to cross between parts.
Inputs may be any that keep to these rules, and one draw needn't show every extreme that they name: `slot_sector`: slot s lies on blk index s; each left sector is held in exactly one slot. `sector_width`: one sector has 256 live rows and one has 64.
All inputs are finite; a program needn't handle non-finite values.
Results may differ from the reference program's by a relative error of at most 0.015.
Values may be sent and summed in bfloat16 or wider, within the bound.
No kernel may reach another device: no remote copies, remote signals or barrier semaphores. Data moves between devices by JAX's collectives and lax.ppermute only.
A program may use at most 64 MiB of HBM per device.

```python
import math
import jax
import jax.numpy as jnp
from jax import lax

W = 256
WR = 64
NRS = 32
TERMS = 8
NSEC = 4
NR = 2048
N_OP = 4


def draw_sector_width(key, part):
    key = jax.random.fold_in(key, 11)
    first_key, second_key = jax.random.split(key)
    widths = jax.random.randint(first_key, (NSEC,), W // 4, W + 1)
    places = jax.random.permutation(second_key, NSEC)
    widths = widths.at[places[0]].set(W)
    widths = widths.at[places[1]].set(W // 4)
    return widths.astype(jnp.int32)


def with_ends(result, stream_key, least, largest):
    extent = result.shape
    index_at = [jax.random.randint(jax.random.fold_in(stream_key, axis), (), 0, extent[axis]) for axis in range(len(extent))]
    result = result.at[tuple(index_at)].set(least)
    longest = extent.index(max(extent))
    index_at[longest] = (index_at[longest] + 1) % extent[longest]
    return result.at[tuple(index_at)].set(largest)


def block_levels(key, shape, cuts, least, largest):
    factor_of = 1.0
    for position, parts in cuts:
        heights = jax.random.uniform(jax.random.fold_in(jax.random.fold_in(key, 6), position), (parts,), jnp.float32, least / len(cuts), largest / len(cuts))
        factor_of = factor_of * jnp.repeat(jnp.exp(heights), shape[position] // parts).reshape((-1,) + (1,) * (len(shape) - 1 - position))
    return factor_of


def scatter_about(own_key, extent, spread, limit, pieces=(), dtype=jnp.bfloat16):
    loudness = block_levels(own_key, extent, pieces, -0.22, 0.18) if pieces else 1.0
    result = jax.random.normal(own_key, extent, jnp.float32) * spread * loudness
    return jnp.minimum(jnp.maximum(result, -limit), limit).astype(dtype)


def setup_inputs(seed: int = 0, part: int = 0) -> dict:
    streams_of = jax.random.split(jax.random.key(seed), 9)
    part_keys = jax.random.split(jax.random.fold_in(streams_of[8], part), 9)
    psi = scatter_about(part_keys[0], (NSEC, W, NR), 1.0, 6.0, ((0, 4),))
    left_ops = scatter_about(part_keys[1], (TERMS, NSEC, W, W), W ** -0.5, 0.375, ((0, 4), (1, 4)))
    right_ops = scatter_about(part_keys[2], (TERMS, NRS, WR, WR), WR ** -0.5, 0.75, ((0, 4), (1, 4)))
    term_shift = with_ends(jax.random.randint(streams_of[3], (TERMS,), -2, 3), jax.random.fold_in(streams_of[3], 1), -2, 2).astype(jnp.int32)
    slot_sector = jax.random.permutation(part_keys[4], NSEC).astype(jnp.int32)
    sector_width = draw_sector_width(jax.random.fold_in(jax.random.fold_in(streams_of[8], part), 71), part)
    diag_left = jnp.clip(jnp.exp(jax.random.uniform(part_keys[6], (NSEC, W), jnp.float32, math.log(0.25), math.log(4.0))), 0.25, 4.0)
    diag_right = jnp.clip(jnp.exp(math.log(4.0) - 2.7725887 * jax.random.uniform(part_keys[7], (NR,), jnp.float32) ** block_levels(part_keys[7], (NR,), ((0, 4),), -0.2, 0.2)), 0.25, 4.0)
    return dict(psi=psi, left_ops=left_ops, right_ops=right_ops, term_shift=term_shift, slot_sector=slot_sector, sector_width=sector_width, diag_left=diag_left, diag_right=diag_right)


EPS = 1e-06

def inner(first, second):
    return jnp.sum(first * second) / (NSEC * W * NR)

def apply_h(field, left_ops, right_ops, term_shift, slot_sector, mask, dmat):
    group = TERMS // N_OP
    field32 = field.astype(jnp.float32)
    total = jnp.zeros((NSEC, W, NR), jnp.float32)
    for index in range(N_OP):
        accum = jnp.zeros((NSEC, W, NR), jnp.float32)
        for offset in range(group):
            term = index * group + offset
            product = jnp.einsum('sij,sjc->sic', left_ops[term].astype(jnp.float32), field32)
            product = lax.optimization_barrier(product.astype(jnp.bfloat16)).astype(jnp.float32)
            onehot = (slot_sector[None, :] == slot_sector[:, None] - term_shift[term]).astype(jnp.float32)
            moved = jnp.einsum('ts,sic->tic', onehot, product).reshape(NSEC, W, NRS, WR)
            right = jnp.einsum('twrc,rdc->twrd', moved, right_ops[term].astype(jnp.float32))
            accum = accum + right.reshape(NSEC, W, NR)
        partial_value = lax.optimization_barrier((accum * mask[:, :, None]).astype(jnp.bfloat16))
        total = total + partial_value.astype(jnp.float32)
    return total + dmat * field32

def reference(psi, left_ops, right_ops, term_shift, slot_sector, sector_width, diag_left, diag_right):
    widths = sector_width[slot_sector]
    mask = (jnp.arange(W)[None, :] < widths[:, None]).astype(jnp.float32)
    dmat = diag_left[:, :, None] + diag_right[None, None, :]
    raw = psi.astype(jnp.float32) * mask[:, :, None]
    vector = (raw * lax.rsqrt(inner(raw, raw) + EPS)).astype(jnp.bfloat16)
    vec32 = vector.astype(jnp.float32)
    first_sigma = apply_h(vector, left_ops, right_ops, term_shift, slot_sector, mask, dmat)
    theta = inner(vec32, first_sigma)
    resid = first_sigma - theta * vec32
    den = dmat - theta
    corr = resid * den / jnp.maximum(den * den, 0.25)
    along = inner(vec32, corr)
    orth = corr - along * vec32
    update = (orth * lax.rsqrt(inner(orth, orth) + EPS)).astype(jnp.bfloat16)
    upd32 = update.astype(jnp.float32)
    second_sigma = apply_h(update, left_ops, right_ops, term_shift, slot_sector, mask, dmat)
    h_one = theta
    h_mix = 0.5 * (inner(vec32, second_sigma) + inner(upd32, first_sigma))
    h_two = inner(upd32, second_sigma)
    angle = 0.5 * jnp.arctan2(2.0 * h_mix, h_one - h_two)
    sine = jnp.sin(angle)
    flip = jnp.where(sine > 0, -1.0, 1.0)
    coef_v = -sine * flip
    coef_u = jnp.cos(angle) * flip
    half = 0.5 * (h_one - h_two)
    energy = 0.5 * (h_one + h_two) - jnp.sqrt(half * half + h_mix * h_mix)
    newvec = coef_v * vec32 + coef_u * upd32
    image = coef_v * first_sigma + coef_u * second_sigma
    return (newvec.astype(jnp.bfloat16), (image - energy * newvec).astype(jnp.bfloat16), jnp.reshape(energy, (1,)).astype(jnp.float32))
```

```python
import functools

import jax
import jax.numpy as jnp
from jax import lax
from jax.experimental import pallas as pl
from jax.experimental.pallas import tpu as pltpu
from jax.sharding import PartitionSpec as P

EPS = 1e-06
LANES = 128
VMEM_LIMIT = 40 * 1024 * 1024


def per_device_general(
    psi, left_ops, right_ops, term_shift, slot_sector, sector_width, diag_left, diag_right
):
    sec_dev, rows, ncols = psi.shape
    nsec = slot_sector.shape[0]
    terms_dev = left_ops.shape[0]
    right_local = right_ops.shape[1]
    right_width = right_ops.shape[2]
    local_cols = diag_right.shape[0]
    count = float(nsec * rows * ncols)
    match = slot_sector[:, None] == jnp.arange(nsec)[None, :]
    widths = jnp.sum(jnp.where(match, sector_width[None, :], 0), axis=1)
    mask_all = (jnp.arange(rows)[None, :] < widths[:, None]).astype(jnp.float32)
    own_mask = lax.dynamic_slice_in_dim(mask_all, lax.axis_index("blk") * sec_dev, sec_dev, 0)
    raw = psi.astype(jnp.float32) * own_mask[:, :, None]
    squares = lax.psum(jnp.sum(raw * raw), "blk")
    v_left = (raw * lax.rsqrt(squares / count + EPS)).astype(jnp.bfloat16)
    onehots = (
        slot_sector[None, None, :] == slot_sector[None, :, None] - term_shift[:, None, None]
    ).astype(jnp.bfloat16)
    op_rows = rows // lax.axis_size("op")
    op_start = lax.axis_index("op") * op_rows
    dmat = diag_left[:, :, None] + diag_right[None, None, :]

    def left_local(field):
        return jnp.einsum(
            "ksij,sjc->ksic", left_ops, field, preferred_element_type=jnp.float32
        ).astype(jnp.bfloat16)

    def right_part(moved_in):
        flat = moved_in.reshape(terms_dev, nsec, rows * local_cols)
        shifted = jnp.einsum(
            "kts,ksx->ktx", onehots, flat, preferred_element_type=jnp.float32
        ).astype(jnp.bfloat16)
        shifted = shifted.reshape(terms_dev, nsec, rows, right_local, right_width)
        accum = jnp.einsum(
            "ktwrc,krdc->twrd", shifted, right_ops, preferred_element_type=jnp.float32
        )
        return accum.reshape(nsec, rows, local_cols) * mask_all[:, :, None]

    def op_total(partial_value):
        return lax.psum(partial_value.astype(jnp.bfloat16), "op").astype(jnp.float32)

    def final_rows(array):
        return lax.dynamic_slice_in_dim(array, op_start, op_rows, 1)

    def reduce_dots(values):
        sums = lax.psum(values, "blk")
        return tuple((item / count for item in sums))

    moved_first, v_moved = (
        lax.all_to_all(left_local(v_left), "blk", split_axis=3, concat_axis=1, tiled=True),
        lax.all_to_all(v_left[None], "blk", split_axis=3, concat_axis=1, tiled=True),
    )
    v_right = v_moved[0]
    vec32 = v_right.astype(jnp.float32)
    first_sigma = op_total(right_part(moved_first)) + dmat * vec32
    theta = reduce_dots((jnp.sum(vec32 * first_sigma),))[0]
    resid = first_sigma - theta * vec32
    den = dmat - theta
    corr = resid * den / jnp.maximum(den * den, 0.25)
    along = reduce_dots((jnp.sum(vec32 * corr),))[0]
    orth = corr - along * vec32
    norm_sq = reduce_dots((jnp.sum(orth * orth),))[0]
    update = (orth * lax.rsqrt(norm_sq + EPS)).astype(jnp.bfloat16)
    upd32 = update.astype(jnp.float32)
    upd_left = lax.all_to_all(update, "blk", split_axis=0, concat_axis=2, tiled=True)
    moved_second = lax.all_to_all(
        left_local(upd_left), "blk", split_axis=3, concat_axis=1, tiled=True
    )
    second_sigma = op_total(right_part(moved_second)) + dmat * upd32
    v_s1, u_s0, u_s1 = reduce_dots(
        (jnp.sum(vec32 * second_sigma), jnp.sum(upd32 * first_sigma), jnp.sum(upd32 * second_sigma))
    )
    h_mix = 0.5 * (v_s1 + u_s0)
    coef_v, coef_u, energy = ritz(theta, h_mix, u_s1)
    newvec = coef_v * vec32 + coef_u * upd32
    image = coef_v * first_sigma + coef_u * second_sigma
    new_out = final_rows(newvec.astype(jnp.bfloat16))
    res_out = final_rows((image - energy * newvec).astype(jnp.bfloat16))
    return (new_out, res_out, jnp.reshape(energy, (1,)))


def ritz(theta, h_mix, h_two):
    angle = 0.5 * jnp.arctan2(2.0 * h_mix, theta - h_two)
    sine = jnp.sin(angle)
    flip = jnp.where(sine > 0, -1.0, 1.0)
    coef_v = -sine * flip
    coef_u = jnp.cos(angle) * flip
    half = 0.5 * (theta - h_two)
    energy = 0.5 * (theta + h_two) - jnp.sqrt(half * half + h_mix * h_mix)
    return coef_v, coef_u, energy


def call(body, out_shape, scratch=(), scalars=0, flops=0, nbytes=0, n_in=0):
    return pl.pallas_call(
        body,
        out_shape=out_shape,
        in_specs=[pl.BlockSpec(memory_space=pltpu.SMEM)] * scalars
        + [pl.BlockSpec(memory_space=pltpu.VMEM)] * n_in,
        out_specs=jax.tree.map(lambda _: pl.BlockSpec(memory_space=pltpu.VMEM), out_shape),
        scratch_shapes=list(scratch),
        compiler_params=pltpu.CompilerParams(vmem_limit_bytes=VMEM_LIMIT),
        cost_estimate=pl.CostEstimate(flops=flops, bytes_accessed=nbytes, transcendentals=0),
    )


def pack_body(meta, psi, right, psi_out, right_out):
    n_blk, _, cols = psi_out.shape
    n_op = right_out.shape[0]
    terms, _, width, _ = right.shape
    per = cols // width
    own = meta[0]
    for b in range(n_blk):
        start = pl.multiple_of((b * n_op + own) * cols, LANES)
        psi_out[b] = psi[0, :, pl.ds(start, cols)]
    right_out[...] = jnp.zeros_like(right_out)
    for d in range(n_op):
        for k in range(terms):
            for r in range(per):
                row = (k * per + r) * width
                right_out[d, row : row + width, r * width : (r + 1) * width] = right[k, d * per + r]


def apply_h(src, field, left, right, gmat, emit):
    nsec = len(field)
    cols = field[0].shape[1]
    n_dev, terms_dev = left.shape[0], left.shape[1]
    n_op = n_dev // nsec
    terms = n_op * terms_dev
    for s in range(nsec):
        prod = lax.dot_general(
            field[s], right[...], (((1,), (1,)), ((), ())), preferred_element_type=jnp.float32
        )
        gmat[s] = prod.astype(jnp.bfloat16)
    gmat[nsec] = jnp.zeros_like(gmat[nsec])
    for t in range(nsec):
        total = None
        for k in range(terms):
            s = src[k * nsec + t]
            held = jnp.minimum(s, nsec - 1) * n_op + k // terms_dev
            part = jnp.dot(
                left[held, k % terms_dev],
                gmat[s, :, k * cols : (k + 1) * cols],
                preferred_element_type=jnp.float32,
            )
            total = part if total is None else total + part
        emit(t, total)


def row_mask(width, shape):
    return lax.broadcasted_iota(jnp.int32, shape, 0) < width


def fold(x):
    return jnp.sum(x.reshape(-1, 8, x.shape[-1]), axis=0)


def whole(x):
    return jnp.sum(jnp.sum(x, axis=0, keepdims=True), axis=1, keepdims=True)


def first_body(src, widths, psi, left, right, dmat, sig_out, raw_out, dots_out, gmat):
    nsec = psi.shape[0]
    field = []
    for t in range(nsec):
        block = psi[t]
        raw = jnp.where(row_mask(widths[t], block.shape), block.astype(jnp.float32), 0.0)
        field.append(raw.astype(jnp.bfloat16))
        raw_out[t] = field[t]
    sums = [jnp.zeros((8, psi.shape[2]), jnp.float32) for _ in range(2)]

    def emit(t, total):
        raw = field[t].astype(jnp.float32)
        sigma = jnp.where(row_mask(widths[t], total.shape), total, 0.0) + dmat[t] * raw
        sig_out[t] = sigma
        sums[0] = sums[0] + fold(raw * raw)
        sums[1] = sums[1] + fold(raw * sigma)

    apply_h(src, field, left, right, gmat, emit)
    tile = spread([whole(x) for x in sums], dots_out.shape[1:])
    for d in range(dots_out.shape[0]):
        dots_out[d] = tile


def spread(values, shape):
    line = lax.broadcasted_iota(jnp.int32, shape, 0)
    tile = jnp.zeros(shape, jnp.float32)
    for j, value in enumerate(values):
        tile = jnp.where(line == j, value, tile)
    return tile


def norm_theta(parts, count):
    tot = jnp.sum(parts, axis=0) * (1.0 / count)
    scale = lax.rsqrt(tot[0:1] + EPS)
    theta = tot[1:2] * scale * scale
    return scale[:, 0:1], theta[:, 0:1]


def second_body(count, src, widths, parts, raw_in, sig_in, left, right, dmat, f_out, t_out, dots_out, gmat, corr):
    nsec = raw_in.shape[0]
    scale, theta = norm_theta(parts[...], count)
    zero = jnp.zeros((8, raw_in.shape[2]), jnp.float32)
    vv, vc, vs = zero, zero, zero
    for t in range(nsec):
        vec = raw_in[t].astype(jnp.float32) * scale
        sigma = sig_in[t] * scale
        den = dmat[t] - theta
        item = (sigma - theta * vec) * den / jnp.maximum(den * den, 0.25)
        corr[t] = item
        vv, vc, vs = vv + fold(vec * vec), vc + fold(vec * item), vs + fold(vec * sigma)
    vv, vc, vs = whole(vv), whole(vc), whole(vs)
    along = vc / jnp.maximum(vv, 1e-30)
    field = []
    for t in range(nsec):
        vec = raw_in[t].astype(jnp.float32) * scale
        block = (corr[t] - along * vec).astype(jnp.bfloat16)
        field.append(block)
        f_out[t] = block
    sums = [zero for _ in range(5)]

    def emit(t, total):
        fld = f_out[t].astype(jnp.float32)
        image = jnp.where(row_mask(widths[t], total.shape), total, 0.0) + dmat[t] * fld
        t_out[t] = image
        vec = raw_in[t].astype(jnp.float32) * scale
        sigma = sig_in[t] * scale
        for j, prod in enumerate((fld * fld, vec * fld, vec * image, fld * sigma, fld * image)):
            sums[j] = sums[j] + fold(prod)

    apply_h(src, field, left, right, gmat, emit)
    tile = spread([vv, vc, vs] + [whole(x) for x in sums], dots_out.shape[1:])
    for d in range(dots_out.shape[0]):
        dots_out[d] = tile


def third_body(count, meta, parts1, parts2, raw_in, sig_in, f_in, t_in, coefs, new_out, res_out):
    nsec, rows, _ = raw_in.shape
    n_op = new_out.shape[0]
    step = rows // n_op
    scale, theta = norm_theta(parts1[...], count)
    cv, cu, energy, beta = coefs[0], coefs[1], coefs[2], coefs[3]
    for t in range(nsec):
        vec = raw_in[t].astype(jnp.float32) * scale
        sigma = sig_in[t] * scale
        newvec = cv * vec + cu * (f_in[t].astype(jnp.float32) + beta * vec)
        image = cv * sigma + cu * (t_in[t] + beta * sigma)
        res = (image - energy * newvec).astype(jnp.bfloat16)
        newvec = newvec.astype(jnp.bfloat16)
        for d in range(n_op):
            new_out[d, t] = newvec[d * step : (d + 1) * step]
            res_out[d, t] = res[d * step : (d + 1) * step]


def combine_scalars(parts1, parts2, count, own):
    tot = jnp.sum(parts1[:, :2, 0], axis=0) / count
    scale = lax.rsqrt(tot[0] + EPS)
    theta = tot[1] * scale * scale
    vv, vc, vs, ff, vf, vt, fs, ft = (parts2[:, j, 0] for j in range(8))
    local = vc / jnp.maximum(vv, 1e-30)
    along = jnp.sum(vc) / count
    beta = local - along
    norm_sq = jnp.sum(ff + 2.0 * beta * vf + beta * beta * vv) / count
    unit = lax.rsqrt(jnp.maximum(norm_sq, 0.0) + EPS)
    v_s1 = unit * jnp.sum(vt + beta * vs) / count
    u_s0 = unit * jnp.sum(fs + beta * vs) / count
    u_s1 = unit * unit * jnp.sum(ft + beta * (vt + fs) + beta * beta * vs) / count
    h_mix = 0.5 * (v_s1 + u_s0)
    cv, cu, energy = ritz(theta, h_mix, u_s1)
    own_beta = jnp.sum(jnp.where(jnp.arange(beta.shape[0]) == own, beta, 0.0))
    return jnp.stack([cv, cu * unit, energy, own_beta]), energy


def per_device(
    psi, left_ops, right_ops, term_shift, slot_sector, sector_width, diag_left, diag_right
):
    n_blk, n_op = lax.axis_size("blk"), lax.axis_size("op")
    _, rows, ncols = psi.shape
    nsec = slot_sector.shape[0]
    terms_dev, _, width, _ = right_ops.shape[0], 0, right_ops.shape[2], 0
    terms = terms_dev * n_op
    cols = diag_right.shape[0] // n_op
    count = float(nsec * rows * ncols)
    n_dev = n_blk * n_op
    both = ("blk", "op")
    own_op = lax.axis_index("op")
    own = lax.axis_index("blk") * n_op + own_op
    bf16, f32 = jnp.bfloat16, jnp.float32

    left = lax.all_gather(left_ops[:, 0], both, axis=0, tiled=False)
    shifts = lax.all_gather(term_shift, "op", axis=0, tiled=True)

    psi_send, right_send = call(
        pack_body,
        (
            jax.ShapeDtypeStruct((n_blk, rows, cols), bf16),
            jax.ShapeDtypeStruct((n_op, terms_dev * cols, cols), bf16),
        ),
        scalars=1,
        n_in=2,
        nbytes=3 << 20,
    )(jnp.reshape(own_op, (1,)).astype(jnp.int32), psi, right_ops)
    psi_cols = lax.all_to_all(psi_send, "blk", 0, 0, tiled=True)
    right = lax.all_to_all(right_send, "op", 0, 0, tiled=True).reshape(terms * cols, cols)

    match = slot_sector[:, None] == jnp.arange(nsec)[None, :]
    widths = jnp.sum(jnp.where(match, sector_width[None, :], 0), axis=1).astype(jnp.int32)
    hit = slot_sector[None, None, :] == slot_sector[None, :, None] - shifts[:, None, None]
    src = jnp.min(jnp.where(hit, jnp.arange(nsec), nsec), axis=2).astype(jnp.int32).reshape(-1)
    dr = lax.dynamic_slice_in_dim(diag_right, own_op * cols, cols, 0)
    dmat = diag_left[:, :, None] + dr[None, None, :]

    field_f32 = jax.ShapeDtypeStruct((nsec, rows, cols), f32)
    field_bf16 = jax.ShapeDtypeStruct((nsec, rows, cols), bf16)
    dots = jax.ShapeDtypeStruct((n_dev, 8, LANES), f32)
    gmat = pltpu.VMEM((nsec + 1, rows, terms * cols), bf16)
    flops = 2 * nsec * rows * cols * terms * (rows + cols)

    sig, raw, dots1 = call(
        first_body, (field_f32, field_bf16, dots), [gmat], 2, flops, 8 << 20, 4
    )(src, widths, psi_cols, left, right, dmat)
    parts1 = lax.all_to_all(dots1, both, 0, 0, tiled=True)

    fld, img, dots2 = call(
        functools.partial(second_body, count),
        (field_bf16, field_f32, dots),
        [gmat, pltpu.VMEM((nsec, rows, cols), f32)],
        2,
        flops,
        8 << 20,
        6,
    )(src, widths, parts1, raw, sig, left, right, dmat)
    parts2 = lax.all_to_all(dots2, both, 0, 0, tiled=True)

    coefs, energy = combine_scalars(parts1, parts2, count, own)
    pieces = jax.ShapeDtypeStruct((n_op, nsec, rows // n_op, cols), bf16)
    new_send, res_send = pl.pallas_call(
        functools.partial(third_body, count, None),
        out_shape=(pieces, pieces),
        in_specs=[pl.BlockSpec(memory_space=pltpu.VMEM)] * 6 + [pl.BlockSpec(memory_space=pltpu.SMEM)],
        out_specs=(pl.BlockSpec(memory_space=pltpu.VMEM),) * 2,
        compiler_params=pltpu.CompilerParams(vmem_limit_bytes=VMEM_LIMIT),
    )(parts1, parts2, raw, sig, fld, img, coefs)

    def final(send):
        got = lax.all_to_all(send, "op", 0, 0, tiled=True)
        return got.transpose(1, 2, 0, 3).reshape(nsec, rows // n_op, n_op * cols)

    return final(new_send), final(res_send), jnp.reshape(energy, (1,))


def solution(mesh):
    placed = (
        P(("grp", "blk"), None, None),
        P("op", ("grp", "blk"), None, None),
        P("op", ("grp", "blk"), None, None),
        P("op"),
        P("grp"),
        P("grp"),
        P("grp", None),
        P(("grp", "blk")),
    )

    def body(*args):
        psi, left_ops, right_ops, diag_right = args[0], args[1], args[2], args[7]
        n_op = mesh.shape["op"]
        cols = diag_right.shape[0] // n_op
        fits = (
            psi.shape[0] == 1
            and diag_right.shape[0] % n_op == 0
            and cols % LANES == 0
            and cols % right_ops.shape[2] == 0
            and cols // right_ops.shape[2] * n_op == right_ops.shape[1]
            and psi.shape[1] % (16 * n_op) == 0
        )
        return (per_device if fits else per_device_general)(*args)

    return jax.shard_map(
        body,
        mesh=mesh,
        in_specs=placed,
        out_specs=(P("grp", "op", "blk"), P("grp", "op", "blk"), P("grp")),
        check_vma=False,
    )
```

```python
import functools

import jax
import jax.numpy as jnp
from jax import lax
from jax.experimental import pallas as pl
from jax.experimental.pallas import tpu as pltpu
from jax.sharding import PartitionSpec as P

EPS = 1e-06
LANES = 128
VMEM_LIMIT = 40 * 1024 * 1024


def per_device_general(
    psi, left_ops, right_ops, term_shift, slot_sector, sector_width, diag_left, diag_right
):
    sec_dev, rows, ncols = psi.shape
    nsec = slot_sector.shape[0]
    terms_dev = left_ops.shape[0]
    right_local = right_ops.shape[1]
    right_width = right_ops.shape[2]
    local_cols = diag_right.shape[0]
    count = float(nsec * rows * ncols)
    match = slot_sector[:, None] == jnp.arange(nsec)[None, :]
    widths = jnp.sum(jnp.where(match, sector_width[None, :], 0), axis=1)
    mask_all = (jnp.arange(rows)[None, :] < widths[:, None]).astype(jnp.float32)
    own_mask = lax.dynamic_slice_in_dim(mask_all, lax.axis_index("blk") * sec_dev, sec_dev, 0)
    raw = psi.astype(jnp.float32) * own_mask[:, :, None]
    squares = lax.psum(jnp.sum(raw * raw), "blk")
    v_left = (raw * lax.rsqrt(squares / count + EPS)).astype(jnp.bfloat16)
    onehots = (
        slot_sector[None, None, :] == slot_sector[None, :, None] - term_shift[:, None, None]
    ).astype(jnp.bfloat16)
    op_rows = rows // lax.axis_size("op")
    op_start = lax.axis_index("op") * op_rows
    dmat = diag_left[:, :, None] + diag_right[None, None, :]

    def left_local(field):
        return jnp.einsum(
            "ksij,sjc->ksic", left_ops, field, preferred_element_type=jnp.float32
        ).astype(jnp.bfloat16)

    def right_part(moved_in):
        flat = moved_in.reshape(terms_dev, nsec, rows * local_cols)
        shifted = jnp.einsum(
            "kts,ksx->ktx", onehots, flat, preferred_element_type=jnp.float32
        ).astype(jnp.bfloat16)
        shifted = shifted.reshape(terms_dev, nsec, rows, right_local, right_width)
        accum = jnp.einsum(
            "ktwrc,krdc->twrd", shifted, right_ops, preferred_element_type=jnp.float32
        )
        return accum.reshape(nsec, rows, local_cols) * mask_all[:, :, None]

    def op_total(partial_value):
        return lax.psum(partial_value.astype(jnp.bfloat16), "op").astype(jnp.float32)

    def final_rows(array):
        return lax.dynamic_slice_in_dim(array, op_start, op_rows, 1)

    def reduce_dots(values):
        sums = lax.psum(values, "blk")
        return tuple((item / count for item in sums))

    moved_first, v_moved = (
        lax.all_to_all(left_local(v_left), "blk", split_axis=3, concat_axis=1, tiled=True),
        lax.all_to_all(v_left[None], "blk", split_axis=3, concat_axis=1, tiled=True),
    )
    v_right = v_moved[0]
    vec32 = v_right.astype(jnp.float32)
    first_sigma = op_total(right_part(moved_first)) + dmat * vec32
    theta = reduce_dots((jnp.sum(vec32 * first_sigma),))[0]
    resid = first_sigma - theta * vec32
    den = dmat - theta
    corr = resid * den / jnp.maximum(den * den, 0.25)
    along = reduce_dots((jnp.sum(vec32 * corr),))[0]
    orth = corr - along * vec32
    norm_sq = reduce_dots((jnp.sum(orth * orth),))[0]
    update = (orth * lax.rsqrt(norm_sq + EPS)).astype(jnp.bfloat16)
    upd32 = update.astype(jnp.float32)
    upd_left = lax.all_to_all(update, "blk", split_axis=0, concat_axis=2, tiled=True)
    moved_second = lax.all_to_all(
        left_local(upd_left), "blk", split_axis=3, concat_axis=1, tiled=True
    )
    second_sigma = op_total(right_part(moved_second)) + dmat * upd32
    v_s1, u_s0, u_s1 = reduce_dots(
        (jnp.sum(vec32 * second_sigma), jnp.sum(upd32 * first_sigma), jnp.sum(upd32 * second_sigma))
    )
    h_mix = 0.5 * (v_s1 + u_s0)
    coef_v, coef_u, energy = ritz(theta, h_mix, u_s1)
    newvec = coef_v * vec32 + coef_u * upd32
    image = coef_v * first_sigma + coef_u * second_sigma
    new_out = final_rows(newvec.astype(jnp.bfloat16))
    res_out = final_rows((image - energy * newvec).astype(jnp.bfloat16))
    return (new_out, res_out, jnp.reshape(energy, (1,)))


def ritz(theta, h_mix, h_two):
    angle = 0.5 * jnp.arctan2(2.0 * h_mix, theta - h_two)
    sine = jnp.sin(angle)
    flip = jnp.where(sine > 0, -1.0, 1.0)
    coef_v = -sine * flip
    coef_u = jnp.cos(angle) * flip
    half = 0.5 * (theta - h_two)
    energy = 0.5 * (theta + h_two) - jnp.sqrt(half * half + h_mix * h_mix)
    return coef_v, coef_u, energy


def call(body, out_shape, scratch=(), scalars=0, flops=0, nbytes=0, n_in=0, n_any=0):
    return pl.pallas_call(
        body,
        out_shape=out_shape,
        in_specs=[pl.BlockSpec(memory_space=pltpu.SMEM)] * scalars
        + [pl.BlockSpec(memory_space=pl.ANY)] * n_any
        + [pl.BlockSpec(memory_space=pltpu.VMEM)] * n_in,
        out_specs=jax.tree.map(lambda _: pl.BlockSpec(memory_space=pltpu.VMEM), out_shape),
        scratch_shapes=list(scratch),
        compiler_params=pltpu.CompilerParams(vmem_limit_bytes=VMEM_LIMIT),
        cost_estimate=pl.CostEstimate(flops=flops, bytes_accessed=nbytes, transcendentals=0),
    )


def pack_body(meta, psi, right, psi_out, right_out):
    n_blk, _, cols = psi_out.shape
    n_op = right_out.shape[0]
    terms, _, width, _ = right.shape
    per = cols // width
    own = meta[0]
    for b in range(n_blk):
        start = pl.multiple_of((b * n_op + own) * cols, LANES)
        psi_out[b] = psi[0, :, pl.ds(start, cols)]
    right_out[...] = jnp.zeros_like(right_out)
    for d in range(n_op):
        for k in range(terms):
            for r in range(per):
                row = (k * per + r) * width
                right_out[d, row : row + width, r * width : (r + 1) * width] = right[k, d * per + r]


def apply_h(src, field, left, right, gmat, emit, ready=None):
    nsec = len(field)
    cols = field[0].shape[1]
    n_dev, terms_dev = left.shape[0], left.shape[1]
    n_op = n_dev // nsec
    terms = n_op * terms_dev
    for s in range(nsec):
        prod = lax.dot_general(
            field[s], right[...], (((1,), (1,)), ((), ())), preferred_element_type=jnp.float32
        )
        gmat[s] = prod.astype(jnp.bfloat16)
    gmat[nsec] = jnp.zeros_like(gmat[nsec])
    if ready is not None:
        ready()
    for t in range(nsec):
        total = None
        for k in range(terms):
            s = src[k * nsec + t]
            held = jnp.minimum(s, nsec - 1) * n_op + k // terms_dev
            part = jnp.dot(
                left[held, k % terms_dev],
                gmat[s, :, k * cols : (k + 1) * cols],
                preferred_element_type=jnp.float32,
            )
            total = part if total is None else total + part
        emit(t, total)


def row_mask(width, shape):
    return lax.broadcasted_iota(jnp.int32, shape, 0) < width


def fold(x):
    return jnp.sum(x.reshape(-1, 8, x.shape[-1]), axis=0)


def whole(x):
    return jnp.sum(jnp.sum(x, axis=0, keepdims=True), axis=1, keepdims=True)


def first_body(place, src, widths, *refs):
    pieces, refs = refs[: place.shape[0]], refs[place.shape[0] :]
    psi, right, dmat, sig_out, raw_out, dots_out, left, gmat, sems = refs
    nsec = psi.shape[0]
    copies = [
        pltpu.make_async_copy(piece, left.at[place[j]], sems.at[j])
        for j, piece in enumerate(pieces)
    ]
    for copy in copies:
        copy.start()

    def ready():
        for copy in copies:
            copy.wait()

    field = []
    for t in range(nsec):
        block = psi[t]
        raw = jnp.where(row_mask(widths[t], block.shape), block.astype(jnp.float32), 0.0)
        field.append(raw.astype(jnp.bfloat16))
        raw_out[t] = field[t]
    sums = [jnp.zeros((8, psi.shape[2]), jnp.float32) for _ in range(2)]

    def emit(t, total):
        raw = field[t].astype(jnp.float32)
        sigma = jnp.where(row_mask(widths[t], total.shape), total, 0.0) + dmat[t] * raw
        sig_out[t] = sigma
        sums[0] = sums[0] + fold(raw * raw)
        sums[1] = sums[1] + fold(raw * sigma)

    apply_h(src, field, left, right, gmat, emit, ready)
    tile = spread([whole(x) for x in sums], dots_out.shape[1:])
    for d in range(dots_out.shape[0]):
        dots_out[d] = tile


def spread(values, shape):
    line = lax.broadcasted_iota(jnp.int32, shape, 0)
    tile = jnp.zeros(shape, jnp.float32)
    for j, value in enumerate(values):
        tile = jnp.where(line == j, value, tile)
    return tile


def norm_theta(parts, count):
    tot = jnp.sum(parts, axis=0) * (1.0 / count)
    scale = lax.rsqrt(tot[0:1] + EPS)
    theta = tot[1:2] * scale * scale
    return scale[:, 0:1], theta[:, 0:1]


def second_body(count, src, widths, parts, raw_in, sig_in, left, right, dmat, f_out, t_out, dots_out, gmat, corr):
    nsec = raw_in.shape[0]
    scale, theta = norm_theta(parts[...], count)
    zero = jnp.zeros((8, raw_in.shape[2]), jnp.float32)
    vv, vc, vs = zero, zero, zero
    for t in range(nsec):
        vec = raw_in[t].astype(jnp.float32) * scale
        sigma = sig_in[t] * scale
        den = dmat[t] - theta
        item = (sigma - theta * vec) * den / jnp.maximum(den * den, 0.25)
        corr[t] = item
        vv, vc, vs = vv + fold(vec * vec), vc + fold(vec * item), vs + fold(vec * sigma)
    vv, vc, vs = whole(vv), whole(vc), whole(vs)
    along = vc / jnp.maximum(vv, 1e-30)
    field = []
    for t in range(nsec):
        vec = raw_in[t].astype(jnp.float32) * scale
        block = (corr[t] - along * vec).astype(jnp.bfloat16)
        field.append(block)
        f_out[t] = block
    sums = [zero for _ in range(5)]

    def emit(t, total):
        fld = f_out[t].astype(jnp.float32)
        image = jnp.where(row_mask(widths[t], total.shape), total, 0.0) + dmat[t] * fld
        t_out[t] = image
        vec = raw_in[t].astype(jnp.float32) * scale
        sigma = sig_in[t] * scale
        for j, prod in enumerate((fld * fld, vec * fld, vec * image, fld * sigma, fld * image)):
            sums[j] = sums[j] + fold(prod)

    apply_h(src, field, left, right, gmat, emit)
    tile = spread([vv, vc, vs] + [whole(x) for x in sums], dots_out.shape[1:])
    for d in range(dots_out.shape[0]):
        dots_out[d] = tile


def third_body(count, meta, parts1, parts2, raw_in, sig_in, f_in, t_in, coefs, new_out, res_out):
    nsec, rows, _ = raw_in.shape
    n_op = new_out.shape[0]
    step = rows // n_op
    scale, theta = norm_theta(parts1[...], count)
    cv, cu, energy, beta = coefs[0], coefs[1], coefs[2], coefs[3]
    for t in range(nsec):
        vec = raw_in[t].astype(jnp.float32) * scale
        sigma = sig_in[t] * scale
        newvec = cv * vec + cu * (f_in[t].astype(jnp.float32) + beta * vec)
        image = cv * sigma + cu * (t_in[t] + beta * sigma)
        res = (image - energy * newvec).astype(jnp.bfloat16)
        newvec = newvec.astype(jnp.bfloat16)
        for d in range(n_op):
            new_out[d, t] = newvec[d * step : (d + 1) * step]
            res_out[d, t] = res[d * step : (d + 1) * step]


def combine_scalars(parts1, parts2, count, own):
    tot = jnp.sum(parts1[:, :2, 0], axis=0) / count
    scale = lax.rsqrt(tot[0] + EPS)
    theta = tot[1] * scale * scale
    vv, vc, vs, ff, vf, vt, fs, ft = (parts2[:, j, 0] for j in range(8))
    local = vc / jnp.maximum(vv, 1e-30)
    along = jnp.sum(vc) / count
    beta = local - along
    norm_sq = jnp.sum(ff + 2.0 * beta * vf + beta * beta * vv) / count
    unit = lax.rsqrt(jnp.maximum(norm_sq, 0.0) + EPS)
    v_s1 = unit * jnp.sum(vt + beta * vs) / count
    u_s0 = unit * jnp.sum(fs + beta * vs) / count
    u_s1 = unit * unit * jnp.sum(ft + beta * (vt + fs) + beta * beta * vs) / count
    h_mix = 0.5 * (v_s1 + u_s0)
    cv, cu, energy = ritz(theta, h_mix, u_s1)
    own_beta = jnp.sum(jnp.where(jnp.arange(beta.shape[0]) == own, beta, 0.0))
    return jnp.stack([cv, cu * unit, energy, own_beta]), energy


def gather_pieces(own, n_blk, n_op):
    pieces, held = [own], [(0, 0)]
    for d in sorted(range(1, n_blk), key=lambda d: min(d, n_blk - d)):
        pairs = [(i, (i + d) % n_blk) for i in range(n_blk)]
        pieces.append(lax.ppermute(own, "blk", pairs))
        held.append((d, 0))
    bit = n_op // 2
    while bit:
        pairs = [(i, i ^ bit) for i in range(n_op)]
        pieces += [lax.ppermute(piece, "op", pairs) for piece in pieces]
        held += [(d, e ^ bit) for d, e in held]
        bit //= 2
    return pieces, held


def per_device(
    psi, left_ops, right_ops, term_shift, slot_sector, sector_width, diag_left, diag_right
):
    n_blk, n_op = lax.axis_size("blk"), lax.axis_size("op")
    _, rows, ncols = psi.shape
    nsec = slot_sector.shape[0]
    terms_dev, _, width, _ = right_ops.shape[0], 0, right_ops.shape[2], 0
    terms = terms_dev * n_op
    cols = diag_right.shape[0] // n_op
    count = float(nsec * rows * ncols)
    n_dev = n_blk * n_op
    both = ("blk", "op")
    own_op = lax.axis_index("op")
    own = lax.axis_index("blk") * n_op + own_op
    bf16, f32 = jnp.bfloat16, jnp.float32

    pieces, held = gather_pieces(left_ops[:, 0], n_blk, n_op)
    own_blk = lax.axis_index("blk")
    place = jnp.stack([lax.rem(own_blk - d + n_blk, n_blk) * n_op + (own_op ^ e) for d, e in held])
    shifts = lax.all_gather(term_shift, "op", axis=0, tiled=True)

    psi_send, right_send = call(
        pack_body,
        (
            jax.ShapeDtypeStruct((n_blk, rows, cols), bf16),
            jax.ShapeDtypeStruct((n_op, terms_dev * cols, cols), bf16),
        ),
        scalars=1,
        n_in=2,
        nbytes=3 << 20,
    )(jnp.reshape(own_op, (1,)).astype(jnp.int32), psi, right_ops)
    psi_cols = lax.all_to_all(psi_send, "blk", 0, 0, tiled=True)
    right = lax.all_to_all(right_send, "op", 0, 0, tiled=True).reshape(terms * cols, cols)

    match = slot_sector[:, None] == jnp.arange(nsec)[None, :]
    widths = jnp.sum(jnp.where(match, sector_width[None, :], 0), axis=1).astype(jnp.int32)
    hit = slot_sector[None, None, :] == slot_sector[None, :, None] - shifts[:, None, None]
    src = jnp.min(jnp.where(hit, jnp.arange(nsec), nsec), axis=2).astype(jnp.int32).reshape(-1)
    dr = lax.dynamic_slice_in_dim(diag_right, own_op * cols, cols, 0)
    dmat = diag_left[:, :, None] + dr[None, None, :]

    field_f32 = jax.ShapeDtypeStruct((nsec, rows, cols), f32)
    field_bf16 = jax.ShapeDtypeStruct((nsec, rows, cols), bf16)
    dots = jax.ShapeDtypeStruct((n_dev, 8, LANES), f32)
    gmat = pltpu.VMEM((nsec + 1, rows, terms * cols), bf16)
    flops = 2 * nsec * rows * cols * terms * (rows + cols)

    left_all = jax.ShapeDtypeStruct((n_dev, terms_dev, rows, rows), bf16)
    sig, raw, dots1, left = call(
        first_body,
        (field_f32, field_bf16, dots, left_all),
        [gmat, pltpu.SemaphoreType.DMA((n_dev,))],
        3,
        flops,
        8 << 20,
        3,
        n_dev,
    )(place, src, widths, *pieces, psi_cols, right, dmat)
    parts1 = lax.all_to_all(dots1, both, 0, 0, tiled=True)

    fld, img, dots2 = call(
        functools.partial(second_body, count),
        (field_bf16, field_f32, dots),
        [gmat, pltpu.VMEM((nsec, rows, cols), f32)],
        2,
        flops,
        8 << 20,
        6,
    )(src, widths, parts1, raw, sig, left, right, dmat)
    parts2 = lax.all_to_all(dots2, both, 0, 0, tiled=True)

    coefs, energy = combine_scalars(parts1, parts2, count, own)
    pieces = jax.ShapeDtypeStruct((n_op, nsec, rows // n_op, cols), bf16)
    new_send, res_send = pl.pallas_call(
        functools.partial(third_body, count, None),
        out_shape=(pieces, pieces),
        in_specs=[pl.BlockSpec(memory_space=pltpu.VMEM)] * 6 + [pl.BlockSpec(memory_space=pltpu.SMEM)],
        out_specs=(pl.BlockSpec(memory_space=pltpu.VMEM),) * 2,
        compiler_params=pltpu.CompilerParams(vmem_limit_bytes=VMEM_LIMIT),
    )(parts1, parts2, raw, sig, fld, img, coefs)

    def final(send):
        got = lax.all_to_all(send, "op", 0, 0, tiled=True)
        return got.transpose(1, 2, 0, 3).reshape(nsec, rows // n_op, n_op * cols)

    return final(new_send), final(res_send), jnp.reshape(energy, (1,))


def solution(mesh):
    placed = (
        P(("grp", "blk"), None, None),
        P("op", ("grp", "blk"), None, None),
        P("op", ("grp", "blk"), None, None),
        P("op"),
        P("grp"),
        P("grp"),
        P("grp", None),
        P(("grp", "blk")),
    )

    def body(*args):
        psi, left_ops, right_ops, diag_right = args[0], args[1], args[2], args[7]
        n_op = mesh.shape["op"]
        cols = diag_right.shape[0] // n_op
        fits = (
            psi.shape[0] == 1
            and diag_right.shape[0] % n_op == 0
            and cols % LANES == 0
            and cols % right_ops.shape[2] == 0
            and cols // right_ops.shape[2] * n_op == right_ops.shape[1]
            and psi.shape[1] % (16 * n_op) == 0
            and n_op & (n_op - 1) == 0
        )
        return (per_device if fits else per_device_general)(*args)

    return jax.shard_map(
        body,
        mesh=mesh,
        in_specs=placed,
        out_specs=(P("grp", "op", "blk"), P("grp", "op", "blk"), P("grp")),
        check_vma=False,
    )
```

```python
import functools

import jax
import jax.numpy as jnp
from jax import lax
from jax.experimental import pallas as pl
from jax.experimental.pallas import tpu as pltpu
from jax.sharding import PartitionSpec as P

EPS = 1e-06
LANES = 128
VMEM_LIMIT = 40 * 1024 * 1024


def per_device_general(
    psi, left_ops, right_ops, term_shift, slot_sector, sector_width, diag_left, diag_right
):
    sec_dev, rows, ncols = psi.shape
    nsec = slot_sector.shape[0]
    terms_dev = left_ops.shape[0]
    right_local = right_ops.shape[1]
    right_width = right_ops.shape[2]
    local_cols = diag_right.shape[0]
    count = float(nsec * rows * ncols)
    match = slot_sector[:, None] == jnp.arange(nsec)[None, :]
    widths = jnp.sum(jnp.where(match, sector_width[None, :], 0), axis=1)
    mask_all = (jnp.arange(rows)[None, :] < widths[:, None]).astype(jnp.float32)
    own_mask = lax.dynamic_slice_in_dim(mask_all, lax.axis_index("blk") * sec_dev, sec_dev, 0)
    raw = psi.astype(jnp.float32) * own_mask[:, :, None]
    squares = lax.psum(jnp.sum(raw * raw), "blk")
    v_left = (raw * lax.rsqrt(squares / count + EPS)).astype(jnp.bfloat16)
    onehots = (
        slot_sector[None, None, :] == slot_sector[None, :, None] - term_shift[:, None, None]
    ).astype(jnp.bfloat16)
    op_rows = rows // lax.axis_size("op")
    op_start = lax.axis_index("op") * op_rows
    dmat = diag_left[:, :, None] + diag_right[None, None, :]

    def left_local(field):
        return jnp.einsum(
            "ksij,sjc->ksic", left_ops, field, preferred_element_type=jnp.float32
        ).astype(jnp.bfloat16)

    def right_part(moved_in):
        flat = moved_in.reshape(terms_dev, nsec, rows * local_cols)
        shifted = jnp.einsum(
            "kts,ksx->ktx", onehots, flat, preferred_element_type=jnp.float32
        ).astype(jnp.bfloat16)
        shifted = shifted.reshape(terms_dev, nsec, rows, right_local, right_width)
        accum = jnp.einsum(
            "ktwrc,krdc->twrd", shifted, right_ops, preferred_element_type=jnp.float32
        )
        return accum.reshape(nsec, rows, local_cols) * mask_all[:, :, None]

    def op_total(partial_value):
        return lax.psum(partial_value.astype(jnp.bfloat16), "op").astype(jnp.float32)

    def final_rows(array):
        return lax.dynamic_slice_in_dim(array, op_start, op_rows, 1)

    def reduce_dots(values):
        sums = lax.psum(values, "blk")
        return tuple((item / count for item in sums))

    moved_first, v_moved = (
        lax.all_to_all(left_local(v_left), "blk", split_axis=3, concat_axis=1, tiled=True),
        lax.all_to_all(v_left[None], "blk", split_axis=3, concat_axis=1, tiled=True),
    )
    v_right = v_moved[0]
    vec32 = v_right.astype(jnp.float32)
    first_sigma = op_total(right_part(moved_first)) + dmat * vec32
    theta = reduce_dots((jnp.sum(vec32 * first_sigma),))[0]
    resid = first_sigma - theta * vec32
    den = dmat - theta
    corr = resid * den / jnp.maximum(den * den, 0.25)
    along = reduce_dots((jnp.sum(vec32 * corr),))[0]
    orth = corr - along * vec32
    norm_sq = reduce_dots((jnp.sum(orth * orth),))[0]
    update = (orth * lax.rsqrt(norm_sq + EPS)).astype(jnp.bfloat16)
    upd32 = update.astype(jnp.float32)
    upd_left = lax.all_to_all(update, "blk", split_axis=0, concat_axis=2, tiled=True)
    moved_second = lax.all_to_all(
        left_local(upd_left), "blk", split_axis=3, concat_axis=1, tiled=True
    )
    second_sigma = op_total(right_part(moved_second)) + dmat * upd32
    v_s1, u_s0, u_s1 = reduce_dots(
        (jnp.sum(vec32 * second_sigma), jnp.sum(upd32 * first_sigma), jnp.sum(upd32 * second_sigma))
    )
    h_mix = 0.5 * (v_s1 + u_s0)
    coef_v, coef_u, energy = ritz(theta, h_mix, u_s1)
    newvec = coef_v * vec32 + coef_u * upd32
    image = coef_v * first_sigma + coef_u * second_sigma
    new_out = final_rows(newvec.astype(jnp.bfloat16))
    res_out = final_rows((image - energy * newvec).astype(jnp.bfloat16))
    return (new_out, res_out, jnp.reshape(energy, (1,)))


def ritz(theta, h_mix, h_two):
    angle = 0.5 * jnp.arctan2(2.0 * h_mix, theta - h_two)
    sine = jnp.sin(angle)
    flip = jnp.where(sine > 0, -1.0, 1.0)
    coef_v = -sine * flip
    coef_u = jnp.cos(angle) * flip
    half = 0.5 * (theta - h_two)
    energy = 0.5 * (theta + h_two) - jnp.sqrt(half * half + h_mix * h_mix)
    return coef_v, coef_u, energy


VMEM, SMEM, ANY = pltpu.VMEM, pltpu.SMEM, pl.ANY


def kernel(body, ins, outs, scratch=(), flops=0, nbytes=0):
    return pl.pallas_call(
        body,
        out_shape=[jax.ShapeDtypeStruct(shape, dtype) for shape, dtype, _ in outs],
        in_specs=[pl.BlockSpec(memory_space=space) for _, space in ins],
        out_specs=[pl.BlockSpec(memory_space=space) for _, _, space in outs],
        scratch_shapes=list(scratch),
        compiler_params=pltpu.CompilerParams(vmem_limit_bytes=VMEM_LIMIT),
        cost_estimate=pl.CostEstimate(flops=flops, bytes_accessed=nbytes, transcendentals=0),
    )(*[array for array, _ in ins])


def by_distance(own, n_blk, start):
    out = [own]
    for d in range(1, n_blk):
        pairs = [(i, (i + d) % n_blk) for i in range(n_blk)]
        out.append(lax.ppermute(start(d), "blk", pairs))
    return out


def swap(block, e, n_op):
    return lax.ppermute(block, "op", [(i, i ^ e) for i in range(n_op)])


def gather_left(own, n_blk, n_op):
    held = dict(enumerate(by_distance(own, n_blk, lambda d: own)))
    held = {(d, 0): block for d, block in held.items()}
    bit = n_op // 2
    while bit:
        held.update({(d, e ^ bit): swap(block, bit, n_op) for (d, e), block in held.items()})
        bit //= 2
    return held


def pack_body(n_blk, n_op, meta, shift, psi, right, *outs):
    psi_out, right_out, sems = outs[:n_blk], outs[n_blk : n_blk + n_op], outs[-1]
    cols = psi_out[0].shape[1]
    terms, _, width, _ = right.shape
    per = cols // width
    own_blk, own_op = meta[0], meta[1]
    copies = []
    for d in range(n_blk):
        there = lax.rem(own_blk + d, n_blk)
        start = pl.multiple_of((there * n_op + own_op) * cols, LANES)
        copies.append(
            pltpu.make_async_copy(psi.at[0, :, pl.ds(start, cols)], psi_out[d], sems.at[d])
        )
        copies[-1].start()
    lane = lax.broadcasted_iota(jnp.int32, (16, cols), 1)
    line = jnp.zeros((16, cols), jnp.float32)
    for k in range(terms):
        line = jnp.where(lane == k, shift[k].astype(jnp.float32), line)
    for e in range(n_op):
        there = (own_op ^ e) * per
        right_out[e][...] = jnp.zeros_like(right_out[e])
        for k in range(terms):
            for r in range(per):
                row = (k * per + r) * width
                right_out[e][row : row + width, r * width : (r + 1) * width] = right[k, there + r]
        right_out[e][terms * cols :] = line.astype(jnp.bfloat16)
    for copy in copies:
        copy.wait()


def row_mask(width, shape):
    return lax.broadcasted_iota(jnp.int32, shape, 0) < width


def fold(x):
    return jnp.sum(x.reshape(-1, 8, x.shape[-1]), axis=0)


def whole(x):
    return jnp.sum(jnp.sum(x, axis=0, keepdims=True), axis=1, keepdims=True)


def spread(values, out):
    line = lax.broadcasted_iota(jnp.int32, out.shape[1:], 0)
    tile = jnp.zeros(out.shape[1:], jnp.float32)
    for j, value in enumerate(values):
        tile = jnp.where(line == j, value, tile)
    for d in range(out.shape[0]):
        out[d] = tile


def apply_h(dst, field, left, right, acc):
    n_blk, n_op = len(left), len(right)
    terms, cols = left[0][0].shape[0], acc.shape[2]
    acc[...] = jnp.zeros_like(acc)
    for d in range(n_blk):
        block = field(d)
        for e in range(n_op):
            prod = lax.dot_general(
                block,
                right[e][: terms * cols],
                (((1,), (1,)), ((), ())),
                preferred_element_type=jnp.float32,
            ).astype(jnp.bfloat16)
            for k in range(terms):
                there = dst[(d * n_op + e) * terms + k]
                acc[there] += jnp.dot(
                    left[d][e][k],
                    prod[:, k * cols : (k + 1) * cols],
                    preferred_element_type=jnp.float32,
                )


def split_refs(refs, n_blk, n_op):
    left = [refs[d * n_op : (d + 1) * n_op] for d in range(n_blk)]
    right = refs[n_blk * n_op : (n_blk + 1) * n_op]
    return left, right, refs[(n_blk + 1) * n_op :]


def send_rows(own_op, sends, j, d, ref):
    step = sends[0].shape[2]
    for e, send in enumerate(sends, 1):
        start = pl.multiple_of((own_op ^ e) * step, step)
        send[j, d] = ref[d, pl.ds(start, step)].astype(send.dtype)


def first_body(n_blk, n_op, meta, dst, slots, widths, *refs):
    left, right, refs = split_refs(refs, n_blk, n_op)
    psi, refs = refs[:n_blk], refs[n_blk:]
    dmat, sig_out, raw_out, dots_out = refs[:4]
    sends, acc = refs[4:-1], refs[-1]

    def field(d):
        block = psi[d][...].astype(jnp.float32)
        block = jnp.where(row_mask(widths[slots[d]], block.shape), block, 0.0)
        raw_out[d] = block.astype(jnp.bfloat16)
        return raw_out[d]

    apply_h(dst, field, left, right, acc)
    zero = jnp.zeros((8, dmat.shape[2]), jnp.float32)
    sums = [zero, zero]
    for d in range(n_blk):
        raw = raw_out[d].astype(jnp.float32)
        total = jnp.where(row_mask(widths[slots[d]], raw.shape), acc[d], 0.0)
        sigma = total + dmat[slots[d]] * raw
        sig_out[d] = sigma
        sums = [sums[0] + fold(raw * raw), sums[1] + fold(raw * sigma)]
        send_rows(meta[1], sends, 0, d, raw_out)
        send_rows(meta[1], sends, 1, d, sig_out)
    spread([whole(x) for x in sums], dots_out)


def norm_theta(parts, count):
    tot = jnp.sum(parts, axis=0) * (1.0 / count)
    scale = lax.rsqrt(tot[0:1] + EPS)
    return scale, tot[1:2] * scale * scale


def second_body(n_blk, n_op, count, meta, dst, slots, widths, *refs):
    left, right, refs = split_refs(refs, n_blk, n_op)
    parts, raw_in, sig_in, dmat, f_out, t_out, dots_out = refs[:7]
    sends, acc, corr = refs[7:-2], refs[-2], refs[-1]
    scale, theta = norm_theta(parts[...], count)
    zero = jnp.zeros((8, raw_in.shape[2]), jnp.float32)
    vv, vc, vs = zero, zero, zero
    for d in range(n_blk):
        vec = raw_in[d].astype(jnp.float32) * scale
        sigma = sig_in[d] * scale
        den = dmat[slots[d]] - theta
        item = (sigma - theta * vec) * den / jnp.maximum(den * den, 0.25)
        corr[d] = item
        vv, vc, vs = vv + fold(vec * vec), vc + fold(vec * item), vs + fold(vec * sigma)
    vv, vc, vs = whole(vv), whole(vc), whole(vs)
    along = vc / jnp.maximum(vv, 1e-30)

    def field(d):
        vec = raw_in[d].astype(jnp.float32) * scale
        f_out[d] = (corr[d] - along * vec).astype(jnp.bfloat16)
        return f_out[d]

    apply_h(dst, field, left, right, acc)
    sums = [zero for _ in range(5)]
    for d in range(n_blk):
        fld = f_out[d].astype(jnp.float32)
        total = jnp.where(row_mask(widths[slots[d]], fld.shape), acc[d], 0.0)
        image = total + dmat[slots[d]] * fld
        t_out[d] = image
        vec = raw_in[d].astype(jnp.float32) * scale
        sigma = sig_in[d] * scale
        prods = (fld * fld, vec * fld, vec * image, fld * sigma, fld * image)
        sums = [held + fold(prod) for held, prod in zip(sums, prods)]
        send_rows(meta[1], sends, 0, d, f_out)
        send_rows(meta[1], sends, 1, d, t_out)
    spread([vv, vc, vs] + [whole(x) for x in sums], dots_out)


def ritz_pair(theta, h_mix, h_two):
    diff, twice = theta - h_two, 2.0 * h_mix
    size = jnp.sqrt(diff * diff + twice * twice)
    some = size > 0.0
    safe = jnp.where(some, size, 1.0)
    big = jnp.sqrt(0.5 + 0.5 * jnp.abs(diff) / safe)
    small = 0.5 * jnp.abs(twice) / (safe * big)
    sine = jnp.where(diff >= 0.0, small, big)
    cosine = jnp.where(diff >= 0.0, big, small)
    sine = jnp.where(some, sine, 0.0)
    cosine = jnp.where(some, cosine, 1.0)
    upward = (twice > 0.0) | ((twice == 0.0) & (diff < 0.0))
    return sine, jnp.where(upward, -cosine, cosine), 0.5 * (theta + h_two) - 0.5 * size


def third_body(n_blk, n_op, count, meta, slots, parts1, parts2, raw_in, sig_in, f_in, t_in, *refs):
    got1, got2 = refs[: n_op - 1], refs[n_op - 1 : 2 * (n_op - 1)]
    new_out, res_out, energy_out = refs[2 * (n_op - 1) :]
    step, cols = new_out.shape[1], raw_in.shape[2]
    own_blk, own_op = meta[0], meta[1]
    scale, theta = norm_theta(parts1[...], count)
    vv, vc, vs, ff, vf, vt, fs, ft = (parts2[:, j, :] for j in range(8))

    def mean(x):
        return jnp.sum(x, axis=0, keepdims=True) * (1.0 / count)

    along = mean(vc)
    beta = vc / jnp.maximum(vv, 1e-30) - along
    norm_sq = mean(ff + 2.0 * beta * vf + beta * beta * vv)
    unit = lax.rsqrt(jnp.maximum(norm_sq, 0.0) + EPS)
    v_s1 = unit * mean(vt + beta * vs)
    u_s0 = unit * mean(fs + beta * vs)
    u_s1 = unit * unit * mean(ft + beta * (vt + fs) + beta * beta * vs)
    cv, cu, energy = ritz_pair(theta, 0.5 * (v_s1 + u_s0), u_s1)
    energy_out[0] = jnp.max(energy)
    cu = cu * unit
    for e in range(n_op):
        there = own_op ^ e
        tile = parts2[own_blk * n_op + there]
        back = tile[1:2] / jnp.maximum(tile[0:1], 1e-30) - along
        on_vec = (cv + cu * back) * scale
        at = pl.multiple_of(there * cols, LANES)
        for d in range(n_blk):
            if e:
                blocks = got1[e - 1][0, d], got1[e - 1][1, d], got2[e - 1][0, d], got2[e - 1][1, d]
            else:
                rows = pl.ds(pl.multiple_of(own_op * step, step), step)
                blocks = raw_in[d, rows], sig_in[d, rows], f_in[d, rows], t_in[d, rows]
            raw, sigma, fld, image = (block.astype(jnp.float32) for block in blocks)
            newvec = on_vec * raw + cu * fld
            res = on_vec * sigma + cu * image - energy * newvec
            new_out[slots[d], :, pl.ds(at, cols)] = newvec.astype(jnp.bfloat16)
            res_out[slots[d], :, pl.ds(at, cols)] = res.astype(jnp.bfloat16)


def per_device(
    psi, left_ops, right_ops, term_shift, slot_sector, sector_width, diag_left, diag_right
):
    n_blk, n_op = lax.axis_size("blk"), lax.axis_size("op")
    _, rows, ncols = psi.shape
    terms = right_ops.shape[0]
    cols = diag_right.shape[0] // n_op
    step = rows // n_op
    count = float(n_blk * rows * ncols)
    n_dev = n_blk * n_op
    own_blk, own_op = lax.axis_index("blk"), lax.axis_index("op")
    meta = jnp.stack([own_blk, own_op]).astype(jnp.int32)
    bf16, f32 = jnp.bfloat16, jnp.float32

    left = gather_left(left_ops[:, 0], n_blk, n_op)
    left_ins = [(left[d, e], VMEM) for d in range(n_blk) for e in range(n_op)]

    sent = kernel(
        functools.partial(pack_body, n_blk, n_op),
        [(meta, SMEM), (term_shift, SMEM), (psi, ANY), (right_ops, VMEM)],
        [((rows, cols), bf16, VMEM)] * n_blk + [((terms * cols + 16, cols), bf16, VMEM)] * n_op,
        [pltpu.SemaphoreType.DMA((n_blk,))],
        nbytes=1 << 20,
    )
    right = [sent[n_blk]] + [swap(sent[n_blk + e], e, n_op) for e in range(1, n_op)]
    right_ins = [(block, VMEM) for block in right]
    psi_ins = [(block, VMEM) for block in by_distance(sent[0], n_blk, lambda d: sent[d])]

    places = jnp.arange(n_blk)
    slots = lax.rem(own_blk - places + n_blk, n_blk).astype(jnp.int32)
    shifts = jnp.stack([block[terms * cols, :terms] for block in right]).astype(jnp.int32)
    match = slot_sector[:, None] == places[None, :]
    widths = jnp.sum(jnp.where(match, sector_width[None, :], 0), axis=1).astype(jnp.int32)
    turned = jnp.sum(jnp.where(slots[:, None] == places[None, :], slot_sector[None, :], 0), axis=1)
    hit = turned[None, None, None, :] == turned[:, None, None, None] + shifts[None, :, :, None]
    dst = jnp.min(jnp.where(hit, places, n_blk), axis=3).astype(jnp.int32).reshape(-1)
    dr = lax.dynamic_slice_in_dim(diag_right, own_op * cols, cols, 0)
    dmat = diag_left[:, :, None] + dr[None, None, :]

    tables = [(meta, SMEM), (dst, SMEM), (slots, SMEM), (widths, SMEM)]
    wide = ((n_blk, rows, cols), f32, VMEM)
    narrow = ((n_blk, rows, cols), bf16, VMEM)
    dots = ((n_dev, 8, LANES), f32, VMEM)
    sends = [((2, n_blk, step, cols), bf16, VMEM)] * (n_op - 1)
    acc = pltpu.VMEM((n_blk + 1, rows, cols), f32)
    flops = 2 * n_blk * rows * cols * terms * n_op * (rows + cols)
    cost = dict(flops=flops, nbytes=8 << 20)

    def totals(parts):
        return lax.all_to_all(parts, ("blk", "op"), 0, 0, tiled=True)

    sig, raw, dots1, *out1 = kernel(
        functools.partial(first_body, n_blk, n_op),
        tables + left_ins + right_ins + psi_ins + [(dmat, VMEM)],
        [wide, narrow, dots] + sends,
        [acc],
        **cost,
    )
    parts1 = totals(dots1)
    got1 = [swap(block, e, n_op) for e, block in enumerate(out1, 1)]
    fld, img, dots2, *out2 = kernel(
        functools.partial(second_body, n_blk, n_op, count),
        tables + left_ins + right_ins + [(x, VMEM) for x in (parts1, raw, sig, dmat)],
        [narrow, wide, dots] + sends,
        [acc, pltpu.VMEM((n_blk, rows, cols), f32)],
        **cost,
    )
    parts2 = totals(dots2)
    got2 = [swap(block, e, n_op) for e, block in enumerate(out2, 1)]
    final = ((n_blk, step, n_op * cols), bf16, VMEM)
    new, res, energy = kernel(
        functools.partial(third_body, n_blk, n_op, count),
        [(meta, SMEM), (slots, SMEM)]
        + [(x, VMEM) for x in (parts1, parts2, raw, sig, fld, img, *got1, *got2)],
        [final, final, ((1,), f32, SMEM)],
        nbytes=4 << 20,
    )
    return new, res, energy


def solution(mesh):
    placed = (
        P(("grp", "blk"), None, None),
        P("op", ("grp", "blk"), None, None),
        P("op", ("grp", "blk"), None, None),
        P("op"),
        P("grp"),
        P("grp"),
        P("grp", None),
        P(("grp", "blk")),
    )

    def body(*args):
        psi, left_ops, right_ops, diag_right = args[0], args[1], args[2], args[7]
        n_op = mesh.shape["op"]
        cols = diag_right.shape[0] // n_op
        fits = (
            psi.shape[0] == 1
            and diag_right.shape[0] % n_op == 0
            and cols % LANES == 0
            and cols % right_ops.shape[2] == 0
            and cols // right_ops.shape[2] * n_op == right_ops.shape[1]
            and psi.shape[1] % (16 * n_op) == 0
            and n_op & (n_op - 1) == 0
        )
        return (per_device if fits else per_device_general)(*args)

    return jax.shard_map(
        body,
        mesh=mesh,
        in_specs=placed,
        out_specs=(P("grp", "op", "blk"), P("grp", "op", "blk"), P("grp")),
        check_vma=False,
    )
```

```python
import functools

import jax
import jax.numpy as jnp
from jax import lax
from jax.experimental import pallas as pl
from jax.experimental.pallas import tpu as pltpu
from jax.sharding import PartitionSpec as P

EPS = 1e-06
LANES = 128
VMEM_LIMIT = 20 * 1024 * 1024


def per_device_general(
    psi, left_ops, right_ops, term_shift, slot_sector, sector_width, diag_left, diag_right
):
    sec_dev, rows, ncols = psi.shape
    nsec = slot_sector.shape[0]
    terms_dev = left_ops.shape[0]
    right_local = right_ops.shape[1]
    right_width = right_ops.shape[2]
    local_cols = diag_right.shape[0]
    count = float(nsec * rows * ncols)
    match = slot_sector[:, None] == jnp.arange(nsec)[None, :]
    widths = jnp.sum(jnp.where(match, sector_width[None, :], 0), axis=1)
    mask_all = (jnp.arange(rows)[None, :] < widths[:, None]).astype(jnp.float32)
    own_mask = lax.dynamic_slice_in_dim(mask_all, lax.axis_index("blk") * sec_dev, sec_dev, 0)
    raw = psi.astype(jnp.float32) * own_mask[:, :, None]
    squares = lax.psum(jnp.sum(raw * raw), "blk")
    v_left = (raw * lax.rsqrt(squares / count + EPS)).astype(jnp.bfloat16)
    onehots = (
        slot_sector[None, None, :] == slot_sector[None, :, None] - term_shift[:, None, None]
    ).astype(jnp.bfloat16)
    op_rows = rows // lax.axis_size("op")
    op_start = lax.axis_index("op") * op_rows
    dmat = diag_left[:, :, None] + diag_right[None, None, :]

    def left_local(field):
        return jnp.einsum(
            "ksij,sjc->ksic", left_ops, field, preferred_element_type=jnp.float32
        ).astype(jnp.bfloat16)

    def right_part(moved_in):
        flat = moved_in.reshape(terms_dev, nsec, rows * local_cols)
        shifted = jnp.einsum(
            "kts,ksx->ktx", onehots, flat, preferred_element_type=jnp.float32
        ).astype(jnp.bfloat16)
        shifted = shifted.reshape(terms_dev, nsec, rows, right_local, right_width)
        accum = jnp.einsum(
            "ktwrc,krdc->twrd", shifted, right_ops, preferred_element_type=jnp.float32
        )
        return accum.reshape(nsec, rows, local_cols) * mask_all[:, :, None]

    def op_total(partial_value):
        return lax.psum(partial_value.astype(jnp.bfloat16), "op").astype(jnp.float32)

    def final_rows(array):
        return lax.dynamic_slice_in_dim(array, op_start, op_rows, 1)

    def reduce_dots(values):
        sums = lax.psum(values, "blk")
        return tuple((item / count for item in sums))

    moved_first, v_moved = (
        lax.all_to_all(left_local(v_left), "blk", split_axis=3, concat_axis=1, tiled=True),
        lax.all_to_all(v_left[None], "blk", split_axis=3, concat_axis=1, tiled=True),
    )
    v_right = v_moved[0]
    vec32 = v_right.astype(jnp.float32)
    first_sigma = op_total(right_part(moved_first)) + dmat * vec32
    theta = reduce_dots((jnp.sum(vec32 * first_sigma),))[0]
    resid = first_sigma - theta * vec32
    den = dmat - theta
    corr = resid * den / jnp.maximum(den * den, 0.25)
    along = reduce_dots((jnp.sum(vec32 * corr),))[0]
    orth = corr - along * vec32
    norm_sq = reduce_dots((jnp.sum(orth * orth),))[0]
    update = (orth * lax.rsqrt(norm_sq + EPS)).astype(jnp.bfloat16)
    upd32 = update.astype(jnp.float32)
    upd_left = lax.all_to_all(update, "blk", split_axis=0, concat_axis=2, tiled=True)
    moved_second = lax.all_to_all(
        left_local(upd_left), "blk", split_axis=3, concat_axis=1, tiled=True
    )
    second_sigma = op_total(right_part(moved_second)) + dmat * upd32
    v_s1, u_s0, u_s1 = reduce_dots(
        (jnp.sum(vec32 * second_sigma), jnp.sum(upd32 * first_sigma), jnp.sum(upd32 * second_sigma))
    )
    h_mix = 0.5 * (v_s1 + u_s0)
    coef_v, coef_u, energy = ritz(theta, h_mix, u_s1)
    newvec = coef_v * vec32 + coef_u * upd32
    image = coef_v * first_sigma + coef_u * second_sigma
    new_out = final_rows(newvec.astype(jnp.bfloat16))
    res_out = final_rows((image - energy * newvec).astype(jnp.bfloat16))
    return (new_out, res_out, jnp.reshape(energy, (1,)))


def ritz(theta, h_mix, h_two):
    angle = 0.5 * jnp.arctan2(2.0 * h_mix, theta - h_two)
    sine = jnp.sin(angle)
    flip = jnp.where(sine > 0, -1.0, 1.0)
    coef_v = -sine * flip
    coef_u = jnp.cos(angle) * flip
    half = 0.5 * (theta - h_two)
    energy = 0.5 * (theta + h_two) - jnp.sqrt(half * half + h_mix * h_mix)
    return coef_v, coef_u, energy


VMEM, SMEM, HBM, ANY = pltpu.VMEM, pltpu.SMEM, pltpu.HBM, pl.ANY


def kernel(body, ins, outs, scratch=(), flops=0, nbytes=0):
    return pl.pallas_call(
        body,
        out_shape=[jax.ShapeDtypeStruct(shape, dtype) for shape, dtype, _ in outs],
        in_specs=[pl.BlockSpec(memory_space=space) for _, space in ins],
        out_specs=[pl.BlockSpec(memory_space=space) for _, _, space in outs],
        scratch_shapes=list(scratch),
        compiler_params=pltpu.CompilerParams(vmem_limit_bytes=VMEM_LIMIT),
        cost_estimate=pl.CostEstimate(flops=flops, bytes_accessed=nbytes, transcendentals=0),
    )(*[array for array, _ in ins])


def by_distance(own, n_blk, start):
    out = [own]
    for d in range(1, n_blk):
        pairs = [(i, (i + d) % n_blk) for i in range(n_blk)]
        out.append(lax.ppermute(start(d), "blk", pairs))
    return out


def swap(block, e, n_op):
    return lax.ppermute(block, "op", [(i, i ^ e) for i in range(n_op)])


def gather_left(own, n_blk, n_op):
    held = dict(enumerate(by_distance(own, n_blk, lambda d: own)))
    held = {(d, 0): block for d, block in held.items()}
    bit = n_op // 2
    while bit:
        held.update({(d, e ^ bit): swap(block, bit, n_op) for (d, e), block in held.items()})
        bit //= 2
    return held


def pack_body(n_blk, n_op, meta, shift, psi, right, _, *outs):
    psi_out, right_out, sems = outs[:n_blk], outs[n_blk : n_blk + n_op], outs[-1]
    cols = psi_out[0].shape[1]
    terms, _, width, _ = right.shape
    per = cols // width
    own_blk, own_op = meta[0], meta[1]
    copies = []
    for d in range(n_blk):
        there = lax.rem(own_blk + d, n_blk)
        start = pl.multiple_of((there * n_op + own_op) * cols, LANES)
        copies.append(
            pltpu.make_async_copy(psi.at[0, :, pl.ds(start, cols)], psi_out[d], sems.at[d])
        )
        copies[-1].start()
    lane = lax.broadcasted_iota(jnp.int32, (16, cols), 1)
    line = jnp.zeros((16, cols), jnp.float32)
    for k in range(terms):
        line = jnp.where(lane == k, shift[k].astype(jnp.float32), line)
    square = [lax.broadcasted_iota(jnp.int32, (width, width), axis) for axis in (0, 1)]
    unit = (square[0] == square[1]).astype(jnp.bfloat16)
    for e in range(n_op):
        there = (own_op ^ e) * per
        right_out[e][...] = jnp.zeros_like(right_out[e])
        for k in range(terms):
            for r in range(per):
                row = (k * per + r) * width
                turned = lax.dot_general(
                    right[k, there + r], unit, (((0,), (0,)), ((), ())),
                    preferred_element_type=jnp.float32,
                )
                right_out[e][row : row + width, r * width : (r + 1) * width] = turned.astype(jnp.bfloat16)
        right_out[e][terms * cols :] = line.astype(jnp.bfloat16)
    for copy in copies:
        copy.wait()


def table_body(n_blk, n_op, terms, meta, sector, width, left_diag, right_diag, *refs):
    tails, src, widths, slots, dmat = refs[:n_op], *refs[n_op:]
    cols = tails[0].shape[1]
    own_blk = meta[0]
    lane = lax.broadcasted_iota(jnp.int32, (16, cols), 1)
    for d in range(n_blk):
        slot = lax.rem(own_blk - d + n_blk, n_blk)
        slots[d] = slot
        widths[d] = width[sector[slot]]
    for e in range(n_op):
        tail = tails[e][terms * cols :].astype(jnp.float32)
        for k in range(terms):
            shift = jnp.max(jnp.where(lane == k, tail, -1e9)).astype(jnp.int32)
            for t in range(n_blk):
                want = sector[slots[t]] - shift
                found = jnp.int32(n_blk)
                for d in range(n_blk):
                    found = jnp.where(sector[slots[d]] == want, d, found)
                src[(t * n_op + e) * terms + k] = found
    for d in range(n_blk):
        row = left_diag[pl.ds(slots[d], 1), :]
        dmat[d] = jnp.transpose(jnp.broadcast_to(row, (cols, row.shape[1]))) + right_diag[...]


def row_mask(width, shape):
    return lax.broadcasted_iota(jnp.int32, shape, 0) < width


def fold(x):
    return jnp.sum(x.reshape(-1, 8, x.shape[-1]), axis=0)


def whole(x):
    return jnp.sum(jnp.sum(x, axis=0, keepdims=True), axis=1, keepdims=True)


def spread(values, out):
    line = lax.broadcasted_iota(jnp.int32, out.shape[1:], 0)
    tile = jnp.zeros(out.shape[1:], jnp.float32)
    for j, value in enumerate(values):
        tile = jnp.where(line == j, value, tile)
    for d in range(out.shape[0]):
        out[d] = tile


def apply_h(src, field, left, right, inter, emit):
    n_blk, n_op = inter.shape[0] - 1, len(right)
    rows, cols = inter.shape[2], inter.shape[3]
    terms = inter.shape[1] // n_op
    inter[n_blk] = jnp.zeros_like(inter[n_blk])
    for d in range(n_blk):
        block = field(d)
        for e in range(n_op):
            ops = left(d, e).reshape(terms * rows, rows)
            prod = jnp.dot(ops, block, preferred_element_type=jnp.float32)
            prod = prod.astype(jnp.bfloat16).reshape(terms, rows, cols)
            inter[d, e * terms : (e + 1) * terms] = prod
    for t in range(n_blk):
        total = None
        for e in range(n_op):
            js = range(e * terms, (e + 1) * terms)
            moved = jnp.concatenate([inter[src[t * n_op * terms + j], j] for j in js], axis=1)
            part = jnp.dot(moved, right[e][: terms * cols], preferred_element_type=jnp.float32)
            total = part if total is None else total + part
        emit(t, total)


def split_refs(refs, n_blk, n_op):
    left = [refs[d * n_op : (d + 1) * n_op] for d in range(n_blk)]
    return left, refs[n_blk * n_op :]


def send_rows(own_op, sends, j, d, ref):
    step = sends[0].shape[2]
    for e, send in enumerate(sends, 1):
        start = pl.multiple_of((own_op ^ e) * step, step)
        send[j, d] = ref[d, pl.ds(start, step)].astype(send.dtype)


def first_body(n_blk, n_op, meta, src, widths, *refs):
    left, refs = split_refs(refs, n_blk, n_op)
    right, psi, refs = refs[:n_op], refs[n_op : n_op + n_blk], refs[n_op + n_blk :]
    dmat, sig_out, raw_out, dots_out, left_out = refs[:5]
    sends, inter, sems = refs[5:-2], refs[-2], refs[-1]
    copies = []
    for d in range(n_blk):
        for e in range(n_op):
            copies.append(
                pltpu.make_async_copy(left[d][e], left_out.at[d, e], sems.at[d * n_op + e])
            )
            copies[-1].start()

    def field(d):
        block = psi[d][...].astype(jnp.float32)
        block = jnp.where(row_mask(widths[d], block.shape), block, 0.0)
        raw_out[d] = block.astype(jnp.bfloat16)
        return raw_out[d]

    zero = jnp.zeros((8, dmat.shape[2]), jnp.float32)
    sums = [zero, zero]

    def emit(d, total):
        raw = raw_out[d].astype(jnp.float32)
        sigma = jnp.where(row_mask(widths[d], raw.shape), total, 0.0) + dmat[d] * raw
        sig_out[d] = sigma
        sums[0] = sums[0] + fold(raw * raw)
        sums[1] = sums[1] + fold(raw * sigma)
        send_rows(meta[1], sends, 0, d, raw_out)
        send_rows(meta[1], sends, 1, d, sig_out)

    apply_h(src, field, lambda d, e: left[d][e][...], right, inter, emit)
    spread([whole(x) for x in sums], dots_out)
    for copy in copies:
        copy.wait()


def norm_theta(parts, count):
    tot = jnp.sum(parts, axis=0) * (1.0 / count)
    scale = lax.rsqrt(tot[0:1] + EPS)
    return scale, tot[1:2] * scale * scale


def second_body(n_blk, n_op, count, meta, src, widths, left_in, *refs):
    right, refs = refs[:n_op], refs[n_op:]
    parts, raw_in, sig_in, dmat, f_out, t_out, dots_out = refs[:7]
    sends, inter, corr, held, sems = refs[7:-4], *refs[-4:]
    copies = [pltpu.make_async_copy(left_in.at[d], held.at[d], sems.at[d]) for d in range(n_blk)]
    for copy in copies:
        copy.start()
    scale, theta = norm_theta(parts[...], count)
    zero = jnp.zeros((8, raw_in.shape[2]), jnp.float32)
    vv, vc, vs = zero, zero, zero
    for d in range(n_blk):
        vec = raw_in[d].astype(jnp.float32) * scale
        sigma = sig_in[d] * scale
        den = dmat[d] - theta
        item = (sigma - theta * vec) * den / jnp.maximum(den * den, 0.25)
        corr[d] = item
        vv, vc, vs = vv + fold(vec * vec), vc + fold(vec * item), vs + fold(vec * sigma)
    vv, vc, vs = whole(vv), whole(vc), whole(vs)
    along = vc / jnp.maximum(vv, 1e-30)

    def field(d):
        vec = raw_in[d].astype(jnp.float32) * scale
        f_out[d] = (corr[d] - along * vec).astype(jnp.bfloat16)
        copies[d].wait()
        return f_out[d]

    sums = [zero for _ in range(5)]

    def emit(d, total):
        fld = f_out[d].astype(jnp.float32)
        image = jnp.where(row_mask(widths[d], fld.shape), total, 0.0) + dmat[d] * fld
        t_out[d] = image
        vec = raw_in[d].astype(jnp.float32) * scale
        sigma = sig_in[d] * scale
        prods = (fld * fld, vec * fld, vec * image, fld * sigma, fld * image)
        sums[:] = [one + fold(prod) for one, prod in zip(sums, prods)]
        send_rows(meta[1], sends, 0, d, f_out)
        send_rows(meta[1], sends, 1, d, t_out)

    apply_h(src, field, lambda d, e: held[d, e], right, inter, emit)
    spread([vv, vc, vs] + [whole(x) for x in sums], dots_out)


def ritz_pair(theta, h_mix, h_two):
    diff, twice = theta - h_two, 2.0 * h_mix
    size = jnp.sqrt(diff * diff + twice * twice)
    some = size > 0.0
    safe = jnp.where(some, size, 1.0)
    big = jnp.sqrt(0.5 + 0.5 * jnp.abs(diff) / safe)
    small = 0.5 * jnp.abs(twice) / (safe * big)
    sine = jnp.where(diff >= 0.0, small, big)
    cosine = jnp.where(diff >= 0.0, big, small)
    sine = jnp.where(some, sine, 0.0)
    cosine = jnp.where(some, cosine, 1.0)
    upward = (twice > 0.0) | ((twice == 0.0) & (diff < 0.0))
    return sine, jnp.where(upward, -cosine, cosine), 0.5 * (theta + h_two) - 0.5 * size


def third_body(n_blk, n_op, count, meta, slots, parts1, parts2, raw_in, sig_in, f_in, t_in, *refs):
    got1, got2 = refs[: n_op - 1], refs[n_op - 1 : 2 * (n_op - 1)]
    new_out, res_out, energy_out = refs[2 * (n_op - 1) :]
    step, cols = new_out.shape[1], raw_in.shape[2]
    own_blk, own_op = meta[0], meta[1]
    scale, theta = norm_theta(parts1[...], count)
    vv, vc, vs, ff, vf, vt, fs, ft = (parts2[:, j, :] for j in range(8))

    def mean(x):
        return jnp.sum(x, axis=0, keepdims=True) * (1.0 / count)

    along = mean(vc)
    beta = vc / jnp.maximum(vv, 1e-30) - along
    norm_sq = mean(ff + 2.0 * beta * vf + beta * beta * vv)
    unit = lax.rsqrt(jnp.maximum(norm_sq, 0.0) + EPS)
    v_s1 = unit * mean(vt + beta * vs)
    u_s0 = unit * mean(fs + beta * vs)
    u_s1 = unit * unit * mean(ft + beta * (vt + fs) + beta * beta * vs)
    cv, cu, energy = ritz_pair(theta, 0.5 * (v_s1 + u_s0), u_s1)
    energy_out[0] = jnp.max(energy)
    cu = cu * unit
    for e in range(n_op):
        there = own_op ^ e
        tile = parts2[own_blk * n_op + there]
        back = tile[1:2] / jnp.maximum(tile[0:1], 1e-30) - along
        on_vec = (cv + cu * back) * scale
        at = pl.multiple_of(there * cols, LANES)
        for d in range(n_blk):
            if e:
                blocks = got1[e - 1][0, d], got1[e - 1][1, d], got2[e - 1][0, d], got2[e - 1][1, d]
            else:
                rows = pl.ds(pl.multiple_of(own_op * step, step), step)
                blocks = raw_in[d, rows], sig_in[d, rows], f_in[d, rows], t_in[d, rows]
            raw, sigma, fld, image = (block.astype(jnp.float32) for block in blocks)
            newvec = on_vec * raw + cu * fld
            res = on_vec * sigma + cu * image - energy * newvec
            new_out[slots[d], :, pl.ds(at, cols)] = newvec.astype(jnp.bfloat16)
            res_out[slots[d], :, pl.ds(at, cols)] = res.astype(jnp.bfloat16)


def per_device(
    psi, left_ops, right_ops, term_shift, slot_sector, sector_width, diag_left, diag_right
):
    n_blk, n_op = lax.axis_size("blk"), lax.axis_size("op")
    _, rows, ncols = psi.shape
    terms = right_ops.shape[0]
    cols = diag_right.shape[0] // n_op
    step = rows // n_op
    count = float(n_blk * rows * ncols)
    n_dev = n_blk * n_op
    own_blk, own_op = lax.axis_index("blk"), lax.axis_index("op")
    meta = jnp.stack([own_blk, own_op]).astype(jnp.int32)
    bf16, f32 = jnp.bfloat16, jnp.float32

    left = gather_left(left_ops[:, 0], n_blk, n_op)
    left_ins = [(left[d, e], VMEM) for d in range(n_blk) for e in range(n_op)]

    sent = kernel(
        functools.partial(pack_body, n_blk, n_op),
        [(meta, SMEM), (term_shift, SMEM), (psi, HBM), (right_ops, VMEM), (left[0, n_op // 2], ANY)],
        [((rows, cols), bf16, VMEM)] * n_blk + [((terms * cols + 16, cols), bf16, VMEM)] * n_op,
        [pltpu.SemaphoreType.DMA((n_blk,))],
        nbytes=1 << 20,
    )
    right = [sent[n_blk]] + [swap(sent[n_blk + e], e, n_op) for e in range(1, n_op)]
    right_ins = [(block, VMEM) for block in right]
    psi_ins = [(block, VMEM) for block in by_distance(sent[0], n_blk, lambda d: sent[d])]
    dr = lax.dynamic_slice_in_dim(diag_right, own_op * cols, cols, 0)
    src, widths, slots, dmat = kernel(
        functools.partial(table_body, n_blk, n_op, terms),
        [(meta, SMEM), (slot_sector, SMEM), (sector_width, SMEM)]
        + [(diag_left, VMEM), (dr[None], VMEM)]
        + right_ins,
        [((n_blk * n_op * terms,), jnp.int32, SMEM)]
        + [((n_blk,), jnp.int32, SMEM)] * 2
        + [((n_blk, rows, cols), f32, VMEM)],
    )

    tables = [(meta, SMEM), (src, SMEM), (widths, SMEM)]
    wide = ((n_blk, rows, cols), f32, VMEM)
    narrow = ((n_blk, rows, cols), bf16, VMEM)
    dots = ((n_dev, 8, LANES), f32, VMEM)
    sends = [((2, n_blk, step, cols), bf16, VMEM)] * (n_op - 1)
    inter = pltpu.VMEM((n_blk + 1, n_op * terms, rows, cols), bf16)
    left_all = (n_blk, n_op, terms, rows, rows)
    flops = 2 * n_blk * rows * cols * terms * n_op * (rows + cols)
    cost = dict(flops=flops, nbytes=8 << 20)

    def totals(parts):
        return lax.all_to_all(parts, ("blk", "op"), 0, 0, tiled=True)

    sig, raw, dots1, kept, *out1 = kernel(
        functools.partial(first_body, n_blk, n_op),
        tables + left_ins + right_ins + psi_ins + [(dmat, VMEM)],
        [wide, narrow, dots, (left_all, bf16, HBM)] + sends,
        [inter, pltpu.SemaphoreType.DMA((n_dev,))],
        **cost,
    )
    parts1 = totals(dots1)
    got1 = [swap(block, e, n_op) for e, block in enumerate(out1, 1)]
    fld, img, dots2, *out2 = kernel(
        functools.partial(second_body, n_blk, n_op, count),
        tables + [(kept, HBM)] + right_ins + [(x, VMEM) for x in (parts1, raw, sig, dmat)],
        [narrow, wide, dots] + sends,
        [inter, pltpu.VMEM((n_blk, rows, cols), f32), pltpu.VMEM(left_all, bf16), pltpu.SemaphoreType.DMA((n_blk,))],
        **cost,
    )
    parts2 = totals(dots2)
    got2 = [swap(block, e, n_op) for e, block in enumerate(out2, 1)]
    final = ((n_blk, step, n_op * cols), bf16, VMEM)
    new, res, energy = kernel(
        functools.partial(third_body, n_blk, n_op, count),
        [(meta, SMEM), (slots, SMEM)]
        + [(x, VMEM) for x in (parts1, parts2, raw, sig, fld, img, *got1, *got2)],
        [final, final, ((1,), f32, SMEM)],
        nbytes=4 << 20,
    )
    return new, res, energy


def solution(mesh):
    placed = (
        P(("grp", "blk"), None, None),
        P("op", ("grp", "blk"), None, None),
        P("op", ("grp", "blk"), None, None),
        P("op"),
        P("grp"),
        P("grp"),
        P("grp", None),
        P(("grp", "blk")),
    )

    def body(*args):
        psi, left_ops, right_ops, diag_right = args[0], args[1], args[2], args[7]
        n_op = mesh.shape["op"]
        cols = diag_right.shape[0] // n_op
        fits = (
            psi.shape[0] == 1
            and diag_right.shape[0] % n_op == 0
            and cols % LANES == 0
            and cols % right_ops.shape[2] == 0
            and cols // right_ops.shape[2] * n_op == right_ops.shape[1]
            and psi.shape[1] % (16 * n_op) == 0
            and n_op & (n_op - 1) == 0
        )
        return (per_device if fits else per_device_general)(*args)

    return jax.shard_map(
        body,
        mesh=mesh,
        in_specs=placed,
        out_specs=(P("grp", "op", "blk"), P("grp", "op", "blk"), P("grp")),
        check_vma=False,
    )
```

```python
import functools

import jax
import jax.numpy as jnp
from jax import lax
from jax.experimental import pallas as pl
from jax.experimental.pallas import tpu as pltpu
from jax.sharding import PartitionSpec as P

EPS = 1e-06
LANES = 128
VMEM_LIMIT = 20 * 1024 * 1024


def per_device_general(
    psi, left_ops, right_ops, term_shift, slot_sector, sector_width, diag_left, diag_right
):
    sec_dev, rows, ncols = psi.shape
    nsec = slot_sector.shape[0]
    terms_dev = left_ops.shape[0]
    right_local = right_ops.shape[1]
    right_width = right_ops.shape[2]
    local_cols = diag_right.shape[0]
    count = float(nsec * rows * ncols)
    match = slot_sector[:, None] == jnp.arange(nsec)[None, :]
    widths = jnp.sum(jnp.where(match, sector_width[None, :], 0), axis=1)
    mask_all = (jnp.arange(rows)[None, :] < widths[:, None]).astype(jnp.float32)
    own_mask = lax.dynamic_slice_in_dim(mask_all, lax.axis_index("blk") * sec_dev, sec_dev, 0)
    raw = psi.astype(jnp.float32) * own_mask[:, :, None]
    squares = lax.psum(jnp.sum(raw * raw), "blk")
    v_left = (raw * lax.rsqrt(squares / count + EPS)).astype(jnp.bfloat16)
    onehots = (
        slot_sector[None, None, :] == slot_sector[None, :, None] - term_shift[:, None, None]
    ).astype(jnp.bfloat16)
    op_rows = rows // lax.axis_size("op")
    op_start = lax.axis_index("op") * op_rows
    dmat = diag_left[:, :, None] + diag_right[None, None, :]

    def left_local(field):
        return jnp.einsum(
            "ksij,sjc->ksic", left_ops, field, preferred_element_type=jnp.float32
        ).astype(jnp.bfloat16)

    def right_part(moved_in):
        flat = moved_in.reshape(terms_dev, nsec, rows * local_cols)
        shifted = jnp.einsum(
            "kts,ksx->ktx", onehots, flat, preferred_element_type=jnp.float32
        ).astype(jnp.bfloat16)
        shifted = shifted.reshape(terms_dev, nsec, rows, right_local, right_width)
        accum = jnp.einsum(
            "ktwrc,krdc->twrd", shifted, right_ops, preferred_element_type=jnp.float32
        )
        return accum.reshape(nsec, rows, local_cols) * mask_all[:, :, None]

    def op_total(partial_value):
        return lax.psum(partial_value.astype(jnp.bfloat16), "op").astype(jnp.float32)

    def final_rows(array):
        return lax.dynamic_slice_in_dim(array, op_start, op_rows, 1)

    def reduce_dots(values):
        sums = lax.psum(values, "blk")
        return tuple((item / count for item in sums))

    moved_first, v_moved = (
        lax.all_to_all(left_local(v_left), "blk", split_axis=3, concat_axis=1, tiled=True),
        lax.all_to_all(v_left[None], "blk", split_axis=3, concat_axis=1, tiled=True),
    )
    v_right = v_moved[0]
    vec32 = v_right.astype(jnp.float32)
    first_sigma = op_total(right_part(moved_first)) + dmat * vec32
    theta = reduce_dots((jnp.sum(vec32 * first_sigma),))[0]
    resid = first_sigma - theta * vec32
    den = dmat - theta
    corr = resid * den / jnp.maximum(den * den, 0.25)
    along = reduce_dots((jnp.sum(vec32 * corr),))[0]
    orth = corr - along * vec32
    norm_sq = reduce_dots((jnp.sum(orth * orth),))[0]
    update = (orth * lax.rsqrt(norm_sq + EPS)).astype(jnp.bfloat16)
    upd32 = update.astype(jnp.float32)
    upd_left = lax.all_to_all(update, "blk", split_axis=0, concat_axis=2, tiled=True)
    moved_second = lax.all_to_all(
        left_local(upd_left), "blk", split_axis=3, concat_axis=1, tiled=True
    )
    second_sigma = op_total(right_part(moved_second)) + dmat * upd32
    v_s1, u_s0, u_s1 = reduce_dots(
        (jnp.sum(vec32 * second_sigma), jnp.sum(upd32 * first_sigma), jnp.sum(upd32 * second_sigma))
    )
    h_mix = 0.5 * (v_s1 + u_s0)
    coef_v, coef_u, energy = ritz(theta, h_mix, u_s1)
    newvec = coef_v * vec32 + coef_u * upd32
    image = coef_v * first_sigma + coef_u * second_sigma
    new_out = final_rows(newvec.astype(jnp.bfloat16))
    res_out = final_rows((image - energy * newvec).astype(jnp.bfloat16))
    return (new_out, res_out, jnp.reshape(energy, (1,)))


def ritz(theta, h_mix, h_two):
    angle = 0.5 * jnp.arctan2(2.0 * h_mix, theta - h_two)
    sine = jnp.sin(angle)
    flip = jnp.where(sine > 0, -1.0, 1.0)
    coef_v = -sine * flip
    coef_u = jnp.cos(angle) * flip
    half = 0.5 * (theta - h_two)
    energy = 0.5 * (theta + h_two) - jnp.sqrt(half * half + h_mix * h_mix)
    return coef_v, coef_u, energy


VMEM, SMEM, HBM, ANY = pltpu.VMEM, pltpu.SMEM, pltpu.HBM, pl.ANY


def kernel(body, ins, outs, scratch=(), flops=0, nbytes=0):
    return pl.pallas_call(
        body,
        out_shape=[
            HBM(shape, dtype) if space == HBM else jax.ShapeDtypeStruct(shape, dtype)
            for shape, dtype, space in outs
        ],
        in_specs=[pl.BlockSpec(memory_space=space) for _, space in ins],
        out_specs=[pl.BlockSpec(memory_space=space) for _, _, space in outs],
        scratch_shapes=list(scratch),
        compiler_params=pltpu.CompilerParams(vmem_limit_bytes=VMEM_LIMIT),
        cost_estimate=pl.CostEstimate(flops=flops, bytes_accessed=nbytes, transcendentals=0),
    )(*[pltpu.with_memory_space_constraint(x, HBM) if space == HBM else x for x, space in ins])


def onward(block, d, n_blk):
    return lax.ppermute(block, "blk", [(i, (i + d) % n_blk) for i in range(n_blk)])


def swap(block, e, n_op):
    return lax.ppermute(block, "op", [(i, i ^ e) for i in range(n_op)])


def gather_left(own, n_blk, n_op):
    held = {(0, 0): own}
    for d in range(1, n_blk):
        held[d, 0] = onward(held[d - 1, 0], 1, n_blk)
    bit = n_op // 2
    while bit:
        held.update({(d, e ^ bit): swap(block, bit, n_op) for (d, e), block in held.items()})
        bit //= 2
    return held


def place_of():
    return lax.axis_index("blk"), lax.axis_index("op")


def pack_body(n_blk, n_op, shift, psi, right, _, *outs):
    psi_out, right_out, sems = outs[:n_blk], outs[n_blk : n_blk + n_op], outs[-1]
    cols = psi_out[0].shape[1]
    terms, _, width, _ = right.shape
    per = cols // width
    own_blk, own_op = place_of()
    copies = []
    for d in range(n_blk):
        there = lax.rem(own_blk + d, n_blk)
        start = pl.multiple_of((there * n_op + own_op) * cols, LANES)
        copies.append(
            pltpu.make_async_copy(psi.at[0, :, pl.ds(start, cols)], psi_out[d], sems.at[d])
        )
        copies[-1].start()
    lane = lax.broadcasted_iota(jnp.int32, (16, cols), 1)
    line = jnp.zeros((16, cols), jnp.float32)
    for k in range(terms):
        line = jnp.where(lane == k, shift[k].astype(jnp.float32), line)
    square = [lax.broadcasted_iota(jnp.int32, (width, width), axis) for axis in (0, 1)]
    unit = (square[0] == square[1]).astype(jnp.bfloat16)
    for e in range(n_op):
        there = (own_op ^ e) * per
        for k in range(terms):
            turned = [
                lax.dot_general(
                    right[k, there + r], unit, (((0,), (0,)), ((), ())),
                    preferred_element_type=jnp.float32,
                )
                for r in range(per)
            ]
            line_up = jnp.concatenate(turned, axis=1).astype(jnp.bfloat16)
            right_out[e][k * width : (k + 1) * width] = line_up
        right_out[e][terms * width :] = line.astype(jnp.bfloat16)
    for copy in copies:
        copy.wait()


def table_body(n_blk, n_op, terms, sector, width, left_diag, right_diag, *refs):
    tails, src, widths, slots, dmat = refs[:n_op], *refs[n_op:]
    rows, cols = tails[0].shape
    own_blk, own_op = place_of()
    lane = lax.broadcasted_iota(jnp.int32, (16, cols), 1)
    for d in range(n_blk):
        slot = lax.rem(own_blk - d + n_blk, n_blk)
        slots[d] = slot
        widths[d] = width[sector[slot]]
    for e in range(n_op):
        tail = tails[e][rows - 16 :].astype(jnp.float32)
        for k in range(terms):
            shift = jnp.max(jnp.where(lane == k, tail, -1e9)).astype(jnp.int32)
            for t in range(n_blk):
                want = sector[slots[t]] - shift
                found = jnp.int32(n_blk)
                for d in range(n_blk):
                    found = jnp.where(sector[slots[d]] == want, d, found)
                src[(t * n_op + e) * terms + k] = found
    on_cols = right_diag[:, pl.ds(pl.multiple_of(own_op * cols, LANES), cols)]
    for d in range(n_blk):
        row = left_diag[pl.ds(slots[d], 1), :]
        dmat[d] = jnp.transpose(jnp.broadcast_to(row, (cols, row.shape[1]))) + on_cols


def row_mask(width, shape):
    return lax.broadcasted_iota(jnp.int32, shape, 0) < width


def fold(x):
    return jnp.sum(x.reshape(-1, 8, x.shape[-1]), axis=0)


def whole(x):
    return jnp.sum(jnp.sum(x, axis=0, keepdims=True), axis=1, keepdims=True)


def spread(values, out):
    line = lax.broadcasted_iota(jnp.int32, out.shape[1:], 0)
    tile = jnp.zeros(out.shape[1:], jnp.float32)
    for j, value in enumerate(values):
        tile = jnp.where(line == j, value, tile)
    for d in range(out.shape[0]):
        out[d] = tile


def by_block(packed, terms, cols):
    width = (packed.shape[0] - 16) // terms
    lane = lax.broadcasted_iota(jnp.int32, (width, cols), 1)
    parts = []
    for k in range(terms):
        block = packed[k * width : (k + 1) * width].astype(jnp.float32)
        for r in range(cols // width):
            inside = (lane >= r * width) & (lane < (r + 1) * width)
            parts.append(jnp.where(inside, block, 0.0).astype(jnp.bfloat16))
    return jnp.concatenate(parts, axis=0)


def apply_h(src, field, left, right, inter, emit):
    n_blk, n_op = inter.shape[0] - 1, len(right)
    rows, cols = inter.shape[2], inter.shape[3]
    terms = inter.shape[1] // n_op
    inter[n_blk] = jnp.zeros_like(inter[n_blk])
    diagonal = [by_block(ref, terms, cols) for ref in right]
    for d in range(n_blk):
        block = field(d)
        for e in range(n_op):
            ops = left(d, e).reshape(terms * rows, rows)
            prod = jnp.dot(ops, block, preferred_element_type=jnp.float32)
            prod = prod.astype(jnp.bfloat16).reshape(terms, rows, cols)
            inter[d, e * terms : (e + 1) * terms] = prod
    for t in range(n_blk):
        total = None
        for e in range(n_op):
            js = range(e * terms, (e + 1) * terms)
            moved = jnp.concatenate([inter[src[t * n_op * terms + j], j] for j in js], axis=1)
            part = jnp.dot(moved, diagonal[e], preferred_element_type=jnp.float32)
            total = part if total is None else total + part
        emit(t, total)


def split_refs(refs, n_blk, n_op):
    left = [refs[d * n_op : (d + 1) * n_op] for d in range(n_blk)]
    return left, refs[n_blk * n_op :]


def send_rows(sends, j, d, ref):
    _, own_op = place_of()
    step = sends[0].shape[2]
    for e, send in enumerate(sends, 1):
        start = pl.multiple_of((own_op ^ e) * step, step)
        send[j, d] = ref[d, pl.ds(start, step)].astype(send.dtype)


def first_body(n_blk, n_op, src, widths, *refs):
    left, refs = split_refs(refs, n_blk, n_op)
    right, psi, refs = refs[:n_op], refs[n_op : n_op + n_blk], refs[n_op + n_blk :]
    dmat, sig_out, raw_out, dots_out, left_out = refs[:5]
    sends, inter, sems = refs[5:-2], refs[-2], refs[-1]
    copies = []
    for d in range(n_blk):
        for e in range(n_op):
            copies.append(
                pltpu.make_async_copy(left[d][e], left_out.at[d, e], sems.at[d * n_op + e])
            )
            copies[-1].start()

    def field(d):
        block = psi[d][...].astype(jnp.float32)
        block = jnp.where(row_mask(widths[d], block.shape), block, 0.0)
        raw_out[d] = block.astype(jnp.bfloat16)
        return raw_out[d]

    zero = jnp.zeros((8, dmat.shape[2]), jnp.float32)
    sums = [zero, zero]

    def emit(d, total):
        raw = raw_out[d].astype(jnp.float32)
        sigma = jnp.where(row_mask(widths[d], raw.shape), total, 0.0) + dmat[d] * raw
        sig_out[d] = sigma
        sums[0] = sums[0] + fold(raw * raw)
        sums[1] = sums[1] + fold(raw * sigma)
        send_rows(sends, 0, d, raw_out)
        send_rows(sends, 1, d, sig_out)

    apply_h(src, field, lambda d, e: left[d][e][...], right, inter, emit)
    spread([whole(x) for x in sums], dots_out)
    for copy in copies:
        copy.wait()


def norm_theta(parts, count):
    tot = jnp.sum(parts, axis=0) * (1.0 / count)
    scale = lax.rsqrt(tot[0:1] + EPS)
    return scale, tot[1:2] * scale * scale


def second_body(n_blk, n_op, count, src, widths, left_in, *refs):
    right, refs = refs[:n_op], refs[n_op:]
    parts, raw_in, sig_in, dmat, f_out, t_out, dots_out = refs[:7]
    sends, inter, corr, held, sems = refs[7:-4], *refs[-4:]
    copies = [pltpu.make_async_copy(left_in.at[d], held.at[d], sems.at[d]) for d in range(n_blk)]
    for copy in copies:
        copy.start()
    scale, theta = norm_theta(parts[...], count)
    zero = jnp.zeros((8, raw_in.shape[2]), jnp.float32)
    vv, vc, vs = zero, zero, zero
    for d in range(n_blk):
        vec = raw_in[d].astype(jnp.float32) * scale
        sigma = sig_in[d] * scale
        den = dmat[d] - theta
        item = (sigma - theta * vec) * den / jnp.maximum(den * den, 0.25)
        corr[d] = item
        vv, vc, vs = vv + fold(vec * vec), vc + fold(vec * item), vs + fold(vec * sigma)
    vv, vc, vs = whole(vv), whole(vc), whole(vs)
    along = vc / jnp.maximum(vv, 1e-30)

    def field(d):
        vec = raw_in[d].astype(jnp.float32) * scale
        f_out[d] = (corr[d] - along * vec).astype(jnp.bfloat16)
        copies[d].wait()
        return f_out[d]

    sums = [zero for _ in range(5)]

    def emit(d, total):
        fld = f_out[d].astype(jnp.float32)
        image = jnp.where(row_mask(widths[d], fld.shape), total, 0.0) + dmat[d] * fld
        t_out[d] = image
        vec = raw_in[d].astype(jnp.float32) * scale
        sigma = sig_in[d] * scale
        prods = (fld * fld, vec * fld, vec * image, fld * sigma, fld * image)
        sums[:] = [one + fold(prod) for one, prod in zip(sums, prods)]
        send_rows(sends, 0, d, f_out)
        send_rows(sends, 1, d, t_out)

    apply_h(src, field, lambda d, e: held[d, e], right, inter, emit)
    spread([vv, vc, vs] + [whole(x) for x in sums], dots_out)


def ritz_pair(theta, h_mix, h_two):
    diff, twice = theta - h_two, 2.0 * h_mix
    size = jnp.sqrt(diff * diff + twice * twice)
    some = size > 0.0
    safe = jnp.where(some, size, 1.0)
    big = jnp.sqrt(0.5 + 0.5 * jnp.abs(diff) / safe)
    small = 0.5 * jnp.abs(twice) / (safe * big)
    sine = jnp.where(diff >= 0.0, small, big)
    cosine = jnp.where(diff >= 0.0, big, small)
    sine = jnp.where(some, sine, 0.0)
    cosine = jnp.where(some, cosine, 1.0)
    upward = (twice > 0.0) | ((twice == 0.0) & (diff < 0.0))
    return sine, jnp.where(upward, -cosine, cosine), 0.5 * (theta + h_two) - 0.5 * size


def third_body(n_blk, n_op, count, slots, parts1, parts2, raw_in, sig_in, f_in, t_in, *refs):
    got1, got2 = refs[: n_op - 1], refs[n_op - 1 : 2 * (n_op - 1)]
    new_out, res_out, energy_out = refs[2 * (n_op - 1) :]
    step, cols = new_out.shape[1], raw_in.shape[2]
    own_blk, own_op = place_of()
    scale, theta = norm_theta(parts1[...], count)
    vv, vc, vs, ff, vf, vt, fs, ft = (parts2[:, j, :] for j in range(8))

    def mean(x):
        return jnp.sum(x, axis=0, keepdims=True) * (1.0 / count)

    along = mean(vc)
    beta = vc / jnp.maximum(vv, 1e-30) - along
    norm_sq = mean(ff + 2.0 * beta * vf + beta * beta * vv)
    unit = lax.rsqrt(jnp.maximum(norm_sq, 0.0) + EPS)
    v_s1 = unit * mean(vt + beta * vs)
    u_s0 = unit * mean(fs + beta * vs)
    u_s1 = unit * unit * mean(ft + beta * (vt + fs) + beta * beta * vs)
    cv, cu, energy = ritz_pair(theta, 0.5 * (v_s1 + u_s0), u_s1)
    energy_out[0] = jnp.max(energy)
    cu = cu * unit
    for e in range(n_op):
        there = own_op ^ e
        tile = parts2[own_blk * n_op + there]
        back = tile[1:2] / jnp.maximum(tile[0:1], 1e-30) - along
        on_vec = (cv + cu * back) * scale
        at = pl.multiple_of(there * cols, LANES)
        for d in range(n_blk):
            if e:
                blocks = got1[e - 1][0, d], got1[e - 1][1, d], got2[e - 1][0, d], got2[e - 1][1, d]
            else:
                rows = pl.ds(pl.multiple_of(own_op * step, step), step)
                blocks = raw_in[d, rows], sig_in[d, rows], f_in[d, rows], t_in[d, rows]
            raw, sigma, fld, image = (block.astype(jnp.float32) for block in blocks)
            newvec = on_vec * raw + cu * fld
            res = on_vec * sigma + cu * image - energy * newvec
            new_out[slots[d], :, pl.ds(at, cols)] = newvec.astype(jnp.bfloat16)
            res_out[slots[d], :, pl.ds(at, cols)] = res.astype(jnp.bfloat16)


def per_device(
    psi, left_ops, right_ops, term_shift, slot_sector, sector_width, diag_left, diag_right
):
    n_blk, n_op = lax.axis_size("blk"), lax.axis_size("op")
    _, rows, ncols = psi.shape
    terms, _, width, _ = right_ops.shape
    cols = diag_right.shape[0] // n_op
    step = rows // n_op
    count = float(n_blk * rows * ncols)
    n_dev = n_blk * n_op
    bf16, f32 = jnp.bfloat16, jnp.float32

    left = gather_left(left_ops[:, 0], n_blk, n_op)
    left_ins = [(left[d, e], VMEM) for d in range(n_blk) for e in range(n_op)]

    sent = kernel(
        functools.partial(pack_body, n_blk, n_op),
        [(term_shift, SMEM), (psi, ANY), (right_ops, VMEM), (left[0, 1], ANY)],
        [((rows, cols), bf16, VMEM)] * n_blk + [((terms * width + 16, cols), bf16, VMEM)] * n_op,
        [pltpu.SemaphoreType.DMA((n_blk,))],
        nbytes=1 << 20,
    )
    right = [sent[n_blk]] + [swap(sent[n_blk + e], e, n_op) for e in range(1, n_op)]
    right_ins = [(block, VMEM) for block in right]
    psi_ins = [(sent[0], VMEM)] + [(onward(sent[d], d, n_blk), VMEM) for d in range(1, n_blk)]
    src, widths, slots, dmat = kernel(
        functools.partial(table_body, n_blk, n_op, terms),
        [(slot_sector, SMEM), (sector_width, SMEM), (diag_left, VMEM), (diag_right[None], VMEM)]
        + right_ins,
        [((n_blk * n_op * terms,), jnp.int32, SMEM)]
        + [((n_blk,), jnp.int32, SMEM)] * 2
        + [((n_blk, rows, cols), f32, VMEM)],
    )

    tables = [(src, SMEM), (widths, SMEM)]
    wide = ((n_blk, rows, cols), f32, VMEM)
    narrow = ((n_blk, rows, cols), bf16, VMEM)
    dots = ((n_dev, 8, LANES), f32, VMEM)
    sends = [((2, n_blk, step, cols), bf16, VMEM)] * (n_op - 1)
    inter = pltpu.VMEM((n_blk + 1, n_op * terms, rows, cols), bf16)
    left_all = (n_blk, n_op, terms, rows, rows)
    flops = 2 * n_blk * rows * cols * terms * n_op * (rows + cols)
    cost = dict(flops=flops, nbytes=8 << 20)

    def totals(parts):
        return lax.all_to_all(parts, ("blk", "op"), 0, 0, tiled=True)

    sig, raw, dots1, kept, *out1 = kernel(
        functools.partial(first_body, n_blk, n_op),
        tables + left_ins + right_ins + psi_ins + [(dmat, VMEM)],
        [wide, narrow, dots, (left_all, bf16, HBM)] + sends,
        [inter, pltpu.SemaphoreType.DMA((n_dev,))],
        **cost,
    )
    parts1 = totals(dots1)
    got1 = [swap(block, e, n_op) for e, block in enumerate(out1, 1)]
    fld, img, dots2, *out2 = kernel(
        functools.partial(second_body, n_blk, n_op, count),
        tables + [(kept, HBM)] + right_ins + [(x, VMEM) for x in (parts1, raw, sig, dmat)],
        [narrow, wide, dots] + sends,
        [inter, pltpu.VMEM((n_blk, rows, cols), f32), pltpu.VMEM(left_all, bf16), pltpu.SemaphoreType.DMA((n_blk,))],
        **cost,
    )
    parts2 = totals(dots2)
    got2 = [swap(block, e, n_op) for e, block in enumerate(out2, 1)]
    final = ((n_blk, step, n_op * cols), bf16, VMEM)
    new, res, energy = kernel(
        functools.partial(third_body, n_blk, n_op, count),
        [(slots, SMEM)]
        + [(x, VMEM) for x in (parts1, parts2, raw, sig, fld, img, *got1, *got2)],
        [final, final, ((1,), f32, SMEM)],
        nbytes=4 << 20,
    )
    return new, res, energy


def solution(mesh):
    placed = (
        P(("grp", "blk"), None, None),
        P("op", ("grp", "blk"), None, None),
        P("op", ("grp", "blk"), None, None),
        P("op"),
        P("grp"),
        P("grp"),
        P("grp", None),
        P(("grp", "blk")),
    )

    def body(*args):
        psi, left_ops, right_ops, diag_right = args[0], args[1], args[2], args[7]
        n_op = mesh.shape["op"]
        cols = diag_right.shape[0] // n_op
        fits = (
            psi.shape[0] == 1
            and diag_right.shape[0] % n_op == 0
            and cols % LANES == 0
            and cols % right_ops.shape[2] == 0
            and cols // right_ops.shape[2] * n_op == right_ops.shape[1]
            and psi.shape[1] % (16 * n_op) == 0
            and n_op & (n_op - 1) == 0
        )
        return (per_device if fits else per_device_general)(*args)

    return jax.shard_map(
        body,
        mesh=mesh,
        in_specs=placed,
        out_specs=(P("grp", "op", "blk"), P("grp", "op", "blk"), P("grp")),
        check_vma=False,
    )
```

```python
import functools

import jax
import jax.numpy as jnp
from jax import lax
from jax.experimental import pallas as pl
from jax.experimental.pallas import tpu as pltpu
from jax.sharding import PartitionSpec as P

EPS = 1e-06
LANES = 128
VMEM_LIMIT = 20 * 1024 * 1024


def per_device_general(
    psi, left_ops, right_ops, term_shift, slot_sector, sector_width, diag_left, diag_right
):
    sec_dev, rows, ncols = psi.shape
    nsec = slot_sector.shape[0]
    terms_dev = left_ops.shape[0]
    right_local = right_ops.shape[1]
    right_width = right_ops.shape[2]
    local_cols = diag_right.shape[0]
    count = float(nsec * rows * ncols)
    match = slot_sector[:, None] == jnp.arange(nsec)[None, :]
    widths = jnp.sum(jnp.where(match, sector_width[None, :], 0), axis=1)
    mask_all = (jnp.arange(rows)[None, :] < widths[:, None]).astype(jnp.float32)
    own_mask = lax.dynamic_slice_in_dim(mask_all, lax.axis_index("blk") * sec_dev, sec_dev, 0)
    raw = psi.astype(jnp.float32) * own_mask[:, :, None]
    squares = lax.psum(jnp.sum(raw * raw), "blk")
    v_left = (raw * lax.rsqrt(squares / count + EPS)).astype(jnp.bfloat16)
    onehots = (
        slot_sector[None, None, :] == slot_sector[None, :, None] - term_shift[:, None, None]
    ).astype(jnp.bfloat16)
    op_rows = rows // lax.axis_size("op")
    op_start = lax.axis_index("op") * op_rows
    dmat = diag_left[:, :, None] + diag_right[None, None, :]

    def left_local(field):
        return jnp.einsum(
            "ksij,sjc->ksic", left_ops, field, preferred_element_type=jnp.float32
        ).astype(jnp.bfloat16)

    def right_part(moved_in):
        flat = moved_in.reshape(terms_dev, nsec, rows * local_cols)
        shifted = jnp.einsum(
            "kts,ksx->ktx", onehots, flat, preferred_element_type=jnp.float32
        ).astype(jnp.bfloat16)
        shifted = shifted.reshape(terms_dev, nsec, rows, right_local, right_width)
        accum = jnp.einsum(
            "ktwrc,krdc->twrd", shifted, right_ops, preferred_element_type=jnp.float32
        )
        return accum.reshape(nsec, rows, local_cols) * mask_all[:, :, None]

    def op_total(partial_value):
        return lax.psum(partial_value.astype(jnp.bfloat16), "op").astype(jnp.float32)

    def final_rows(array):
        return lax.dynamic_slice_in_dim(array, op_start, op_rows, 1)

    def reduce_dots(values):
        sums = lax.psum(values, "blk")
        return tuple((item / count for item in sums))

    moved_first, v_moved = (
        lax.all_to_all(left_local(v_left), "blk", split_axis=3, concat_axis=1, tiled=True),
        lax.all_to_all(v_left[None], "blk", split_axis=3, concat_axis=1, tiled=True),
    )
    v_right = v_moved[0]
    vec32 = v_right.astype(jnp.float32)
    first_sigma = op_total(right_part(moved_first)) + dmat * vec32
    theta = reduce_dots((jnp.sum(vec32 * first_sigma),))[0]
    resid = first_sigma - theta * vec32
    den = dmat - theta
    corr = resid * den / jnp.maximum(den * den, 0.25)
    along = reduce_dots((jnp.sum(vec32 * corr),))[0]
    orth = corr - along * vec32
    norm_sq = reduce_dots((jnp.sum(orth * orth),))[0]
    update = (orth * lax.rsqrt(norm_sq + EPS)).astype(jnp.bfloat16)
    upd32 = update.astype(jnp.float32)
    upd_left = lax.all_to_all(update, "blk", split_axis=0, concat_axis=2, tiled=True)
    moved_second = lax.all_to_all(
        left_local(upd_left), "blk", split_axis=3, concat_axis=1, tiled=True
    )
    second_sigma = op_total(right_part(moved_second)) + dmat * upd32
    v_s1, u_s0, u_s1 = reduce_dots(
        (jnp.sum(vec32 * second_sigma), jnp.sum(upd32 * first_sigma), jnp.sum(upd32 * second_sigma))
    )
    h_mix = 0.5 * (v_s1 + u_s0)
    coef_v, coef_u, energy = ritz(theta, h_mix, u_s1)
    newvec = coef_v * vec32 + coef_u * upd32
    image = coef_v * first_sigma + coef_u * second_sigma
    new_out = final_rows(newvec.astype(jnp.bfloat16))
    res_out = final_rows((image - energy * newvec).astype(jnp.bfloat16))
    return (new_out, res_out, jnp.reshape(energy, (1,)))


def ritz(theta, h_mix, h_two):
    angle = 0.5 * jnp.arctan2(2.0 * h_mix, theta - h_two)
    sine = jnp.sin(angle)
    flip = jnp.where(sine > 0, -1.0, 1.0)
    coef_v = -sine * flip
    coef_u = jnp.cos(angle) * flip
    half = 0.5 * (theta - h_two)
    energy = 0.5 * (theta + h_two) - jnp.sqrt(half * half + h_mix * h_mix)
    return coef_v, coef_u, energy


VMEM, SMEM, HBM, ANY = pltpu.VMEM, pltpu.SMEM, pltpu.HBM, pl.ANY


def kernel(body, ins, outs, scratch=(), flops=0, nbytes=0):
    return pl.pallas_call(
        body,
        out_shape=[
            HBM(shape, dtype) if space == HBM else jax.ShapeDtypeStruct(shape, dtype)
            for shape, dtype, space in outs
        ],
        in_specs=[pl.BlockSpec(memory_space=space) for _, space in ins],
        out_specs=[pl.BlockSpec(memory_space=space) for _, _, space in outs],
        scratch_shapes=list(scratch),
        compiler_params=pltpu.CompilerParams(vmem_limit_bytes=VMEM_LIMIT),
        cost_estimate=pl.CostEstimate(flops=flops, bytes_accessed=nbytes, transcendentals=0),
    )(*[pltpu.with_memory_space_constraint(x, HBM) if space == HBM else x for x, space in ins])


def onward(block, d, n_blk):
    return lax.ppermute(block, "blk", [(i, (i + d) % n_blk) for i in range(n_blk)])


def swap(block, e, n_op):
    return lax.ppermute(block, "op", [(i, i ^ e) for i in range(n_op)])


def gather(own, n_blk, n_op, pack, table):
    bits = [1 << b for b in reversed(range(n_op.bit_length() - 1))]
    order = sorted(range(1, n_blk), key=lambda d: min(d, n_blk - d))
    left, psi, right, tables = {(0, 0): own}, {}, {}, None
    waiting = {(0, 0): 0}
    for j in range(n_blk + len(bits)):
        new, moved = {}, {}
        for (d, e), done in waiting.items():
            if e == 0 and d + 1 < n_blk:
                new[d + 1, 0] = onward(left[d, 0], 1, n_blk), 0
            for b in range(done, len(bits)):
                new[d, e ^ bits[b]] = swap(left[d, e], bits[b], n_op), b + 1
        kept = {key: block for key, (block, _) in new.items()}
        if j == 0:
            sent = pack(kept[0, bits[-1]])
            moved["sent"] = sent
        if j == 1:
            moved["right"] = [swap(sent[1][e], e, n_op) for e in range(1, n_op)]
        if 1 <= j < n_blk:
            d = order[j - 1]
            moved["psi"] = onward(sent[0][d], d, n_blk)
        if j == 2:
            moved["tables"] = table([sent[1][0]] + right)
        if not kept and not moved:
            break
        waiting = {key: done for key, (_, done) in new.items()}
        kept, moved = lax.optimization_barrier((kept, moved))
        left.update(kept)
        sent = moved.get("sent", sent)
        right = moved.get("right", right)
        tables = moved.get("tables", tables)
        if "psi" in moved:
            psi[d] = moved["psi"]
    return left, [sent[0][0]] + [psi[d] for d in range(1, n_blk)], [sent[1][0]] + right, tables


def place_of():
    return lax.axis_index("blk"), lax.axis_index("op")


def pack_body(n_blk, n_op, shift, psi, right, *outs):
    psi_out, right_out, sems = outs[:n_blk], outs[n_blk : n_blk + n_op], outs[-1]
    cols = psi_out[0].shape[1]
    terms, _, width, _ = right.shape
    per = cols // width
    own_blk, own_op = place_of()
    copies = []
    for d in range(n_blk):
        there = lax.rem(own_blk + d, n_blk)
        start = pl.multiple_of((there * n_op + own_op) * cols, LANES)
        copies.append(
            pltpu.make_async_copy(psi.at[0, :, pl.ds(start, cols)], psi_out[d], sems.at[d])
        )
        copies[-1].start()
    lane = lax.broadcasted_iota(jnp.int32, (16, cols), 1)
    line = jnp.zeros((16, cols), jnp.float32)
    for k in range(terms):
        line = jnp.where(lane == k, shift[k].astype(jnp.float32), line)
    square = [lax.broadcasted_iota(jnp.int32, (width, width), axis) for axis in (0, 1)]
    unit = (square[0] == square[1]).astype(jnp.bfloat16)
    for e in range(n_op):
        there = (own_op ^ e) * per
        for k in range(terms):
            turned = [
                lax.dot_general(
                    right[k, there + r], unit, (((0,), (0,)), ((), ())),
                    preferred_element_type=jnp.float32,
                )
                for r in range(per)
            ]
            line_up = jnp.concatenate(turned, axis=1).astype(jnp.bfloat16)
            right_out[e][k * width : (k + 1) * width] = line_up
        right_out[e][terms * width :] = line.astype(jnp.bfloat16)
    for copy in copies:
        copy.wait()


def table_body(n_blk, n_op, terms, sector, width, left_diag, right_diag, *refs):
    tails, src, widths, slots, dmat = refs[:n_op], *refs[n_op:]
    rows, cols = tails[0].shape
    own_blk, own_op = place_of()
    lane = lax.broadcasted_iota(jnp.int32, (16, cols), 1)
    for d in range(n_blk):
        slot = lax.rem(own_blk - d + n_blk, n_blk)
        slots[d] = slot
        widths[d] = width[sector[slot]]
    for e in range(n_op):
        tail = tails[e][rows - 16 :].astype(jnp.float32)
        for k in range(terms):
            shift = jnp.max(jnp.where(lane == k, tail, -1e9)).astype(jnp.int32)
            for t in range(n_blk):
                want = sector[slots[t]] - shift
                found = jnp.int32(n_blk)
                for d in range(n_blk):
                    found = jnp.where(sector[slots[d]] == want, d, found)
                src[(t * n_op + e) * terms + k] = found
    on_cols = right_diag[:, pl.ds(pl.multiple_of(own_op * cols, LANES), cols)]
    for d in range(n_blk):
        row = left_diag[pl.ds(slots[d], 1), :]
        dmat[d] = jnp.transpose(jnp.broadcast_to(row, (cols, row.shape[1]))) + on_cols


def row_mask(width, shape):
    return lax.broadcasted_iota(jnp.int32, shape, 0) < width


def fold(x):
    return jnp.sum(x.reshape(-1, 8, x.shape[-1]), axis=0)


def whole(x):
    return jnp.sum(jnp.sum(x, axis=0, keepdims=True), axis=1, keepdims=True)


def spread(values, out):
    line = lax.broadcasted_iota(jnp.int32, out.shape[1:], 0)
    tile = jnp.zeros(out.shape[1:], jnp.float32)
    for j, value in enumerate(values):
        tile = jnp.where(line == j, value, tile)
    for d in range(out.shape[0]):
        out[d] = tile


def by_block(packed, terms, cols):
    width = (packed.shape[0] - 16) // terms
    lane = lax.broadcasted_iota(jnp.int32, (width, cols), 1)
    parts = []
    for k in range(terms):
        block = packed[k * width : (k + 1) * width].astype(jnp.float32)
        for r in range(cols // width):
            inside = (lane >= r * width) & (lane < (r + 1) * width)
            parts.append(jnp.where(inside, block, 0.0).astype(jnp.bfloat16))
    return jnp.concatenate(parts, axis=0)


def apply_h(src, field, left, right, inter, emit):
    n_blk, n_op = inter.shape[0] - 1, len(right)
    rows, cols = inter.shape[2], inter.shape[3]
    terms = inter.shape[1] // n_op
    inter[n_blk] = jnp.zeros_like(inter[n_blk])
    diagonal = [by_block(ref, terms, cols) for ref in right]
    for d in range(n_blk):
        block = field(d)
        for e in range(n_op):
            ops = left(d, e).reshape(terms * rows, rows)
            prod = jnp.dot(ops, block, preferred_element_type=jnp.float32)
            prod = prod.astype(jnp.bfloat16).reshape(terms, rows, cols)
            inter[d, e * terms : (e + 1) * terms] = prod
    for t in range(n_blk):
        total = None
        for e in range(n_op):
            js = range(e * terms, (e + 1) * terms)
            moved = jnp.concatenate([inter[src[t * n_op * terms + j], j] for j in js], axis=1)
            part = jnp.dot(moved, diagonal[e], preferred_element_type=jnp.float32)
            total = part if total is None else total + part
        emit(t, total)


def split_refs(refs, n_blk, n_op):
    left = [refs[d * n_op : (d + 1) * n_op] for d in range(n_blk)]
    return left, refs[n_blk * n_op :]


def send_rows(sends, j, d, ref):
    _, own_op = place_of()
    step = sends[0].shape[2]
    for e, send in enumerate(sends, 1):
        start = pl.multiple_of((own_op ^ e) * step, step)
        send[j, d] = ref[d, pl.ds(start, step)].astype(send.dtype)


def first_body(n_blk, n_op, src, widths, *refs):
    left, refs = split_refs(refs, n_blk, n_op)
    right, psi, refs = refs[:n_op], refs[n_op : n_op + n_blk], refs[n_op + n_blk :]
    dmat, sig_out, raw_out, dots_out, left_out = refs[:5]
    sends, inter, sems = refs[5:-2], refs[-2], refs[-1]
    copies = []
    for d in range(n_blk):
        for e in range(n_op):
            copies.append(
                pltpu.make_async_copy(left[d][e], left_out.at[d, e], sems.at[d * n_op + e])
            )
            copies[-1].start()

    def field(d):
        block = psi[d][...].astype(jnp.float32)
        block = jnp.where(row_mask(widths[d], block.shape), block, 0.0)
        raw_out[d] = block.astype(jnp.bfloat16)
        return raw_out[d]

    zero = jnp.zeros((8, dmat.shape[2]), jnp.float32)
    sums = [zero, zero]

    def emit(d, total):
        raw = raw_out[d].astype(jnp.float32)
        sigma = jnp.where(row_mask(widths[d], raw.shape), total, 0.0) + dmat[d] * raw
        sig_out[d] = sigma
        sums[0] = sums[0] + fold(raw * raw)
        sums[1] = sums[1] + fold(raw * sigma)
        send_rows(sends, 0, d, raw_out)
        send_rows(sends, 1, d, sig_out)

    apply_h(src, field, lambda d, e: left[d][e][...], right, inter, emit)
    spread([whole(x) for x in sums], dots_out)
    for copy in copies:
        copy.wait()


def norm_theta(parts, count):
    tot = jnp.sum(parts, axis=0) * (1.0 / count)
    scale = lax.rsqrt(tot[0:1] + EPS)
    return scale, tot[1:2] * scale * scale


def second_body(n_blk, n_op, count, src, widths, left_in, *refs):
    right, refs = refs[:n_op], refs[n_op:]
    parts, raw_in, sig_in, dmat, f_out, t_out, dots_out = refs[:7]
    sends, inter, corr, held, sems = refs[7:-4], *refs[-4:]
    copies = [pltpu.make_async_copy(left_in.at[d], held.at[d], sems.at[d]) for d in range(n_blk)]
    for copy in copies:
        copy.start()
    scale, theta = norm_theta(parts[...], count)
    zero = jnp.zeros((8, raw_in.shape[2]), jnp.float32)
    vv, vc, vs = zero, zero, zero
    for d in range(n_blk):
        vec = raw_in[d].astype(jnp.float32) * scale
        sigma = sig_in[d] * scale
        den = dmat[d] - theta
        item = (sigma - theta * vec) * den / jnp.maximum(den * den, 0.25)
        corr[d] = item
        vv, vc, vs = vv + fold(vec * vec), vc + fold(vec * item), vs + fold(vec * sigma)
    vv, vc, vs = whole(vv), whole(vc), whole(vs)
    along = vc / jnp.maximum(vv, 1e-30)

    def field(d):
        vec = raw_in[d].astype(jnp.float32) * scale
        f_out[d] = (corr[d] - along * vec).astype(jnp.bfloat16)
        copies[d].wait()
        return f_out[d]

    sums = [zero for _ in range(5)]

    def emit(d, total):
        fld = f_out[d].astype(jnp.float32)
        image = jnp.where(row_mask(widths[d], fld.shape), total, 0.0) + dmat[d] * fld
        t_out[d] = image
        vec = raw_in[d].astype(jnp.float32) * scale
        sigma = sig_in[d] * scale
        prods = (fld * fld, vec * fld, vec * image, fld * sigma, fld * image)
        sums[:] = [one + fold(prod) for one, prod in zip(sums, prods)]
        send_rows(sends, 0, d, f_out)
        send_rows(sends, 1, d, t_out)

    apply_h(src, field, lambda d, e: held[d, e], right, inter, emit)
    spread([vv, vc, vs] + [whole(x) for x in sums], dots_out)


def ritz_pair(theta, h_mix, h_two):
    diff, twice = theta - h_two, 2.0 * h_mix
    size = jnp.sqrt(diff * diff + twice * twice)
    some = size > 0.0
    safe = jnp.where(some, size, 1.0)
    big = jnp.sqrt(0.5 + 0.5 * jnp.abs(diff) / safe)
    small = 0.5 * jnp.abs(twice) / (safe * big)
    sine = jnp.where(diff >= 0.0, small, big)
    cosine = jnp.where(diff >= 0.0, big, small)
    sine = jnp.where(some, sine, 0.0)
    cosine = jnp.where(some, cosine, 1.0)
    upward = (twice > 0.0) | ((twice == 0.0) & (diff < 0.0))
    return sine, jnp.where(upward, -cosine, cosine), 0.5 * (theta + h_two) - 0.5 * size


def third_body(n_blk, n_op, count, slots, parts1, parts2, raw_in, sig_in, f_in, t_in, *refs):
    got1, got2 = refs[: n_op - 1], refs[n_op - 1 : 2 * (n_op - 1)]
    new_out, res_out, energy_out = refs[2 * (n_op - 1) :]
    step, cols = new_out.shape[1], raw_in.shape[2]
    own_blk, own_op = place_of()
    scale, theta = norm_theta(parts1[...], count)
    vv, vc, vs, ff, vf, vt, fs, ft = (parts2[:, j, :] for j in range(8))

    def mean(x):
        return jnp.sum(x, axis=0, keepdims=True) * (1.0 / count)

    along = mean(vc)
    beta = vc / jnp.maximum(vv, 1e-30) - along
    norm_sq = mean(ff + 2.0 * beta * vf + beta * beta * vv)
    unit = lax.rsqrt(jnp.maximum(norm_sq, 0.0) + EPS)
    v_s1 = unit * mean(vt + beta * vs)
    u_s0 = unit * mean(fs + beta * vs)
    u_s1 = unit * unit * mean(ft + beta * (vt + fs) + beta * beta * vs)
    cv, cu, energy = ritz_pair(theta, 0.5 * (v_s1 + u_s0), u_s1)
    energy_out[0] = jnp.max(energy)
    cu = cu * unit
    for e in range(n_op):
        there = own_op ^ e
        tile = parts2[own_blk * n_op + there]
        back = tile[1:2] / jnp.maximum(tile[0:1], 1e-30) - along
        on_vec = (cv + cu * back) * scale
        at = pl.multiple_of(there * cols, LANES)
        for d in range(n_blk):
            if e:
                blocks = got1[e - 1][0, d], got1[e - 1][1, d], got2[e - 1][0, d], got2[e - 1][1, d]
            else:
                rows = pl.ds(pl.multiple_of(own_op * step, step), step)
                blocks = raw_in[d, rows], sig_in[d, rows], f_in[d, rows], t_in[d, rows]
            raw, sigma, fld, image = (block.astype(jnp.float32) for block in blocks)
            newvec = on_vec * raw + cu * fld
            res = on_vec * sigma + cu * image - energy * newvec
            new_out[slots[d], :, pl.ds(at, cols)] = newvec.astype(jnp.bfloat16)
            res_out[slots[d], :, pl.ds(at, cols)] = res.astype(jnp.bfloat16)


def per_device(
    psi, left_ops, right_ops, term_shift, slot_sector, sector_width, diag_left, diag_right
):
    n_blk, n_op = lax.axis_size("blk"), lax.axis_size("op")
    _, rows, ncols = psi.shape
    terms, _, width, _ = right_ops.shape
    cols = diag_right.shape[0] // n_op
    step = rows // n_op
    count = float(n_blk * rows * ncols)
    n_dev = n_blk * n_op
    bf16, f32 = jnp.bfloat16, jnp.float32

    def pack(after):
        given = lax.optimization_barrier((term_shift, psi, right_ops, after))
        sent = kernel(
            functools.partial(pack_body, n_blk, n_op),
            list(zip(given, (SMEM, ANY, VMEM))),
            [((rows, cols), bf16, VMEM)] * n_blk + [((terms * width + 16, cols), bf16, VMEM)] * n_op,
            [pltpu.SemaphoreType.DMA((n_blk,))],
            nbytes=1 << 20,
        )
        return sent[:n_blk], sent[n_blk:]

    def table(right):
        return kernel(
            functools.partial(table_body, n_blk, n_op, terms),
            [(slot_sector, SMEM), (sector_width, SMEM), (diag_left, VMEM), (diag_right[None], VMEM)]
            + [(block, VMEM) for block in right],
            [((n_blk * n_op * terms,), jnp.int32, SMEM)]
            + [((n_blk,), jnp.int32, SMEM)] * 2
            + [((n_blk, rows, cols), f32, VMEM)],
        )

    left, psi_by, right, (src, widths, slots, dmat) = gather(left_ops[:, 0], n_blk, n_op, pack, table)
    left_ins = [(left[d, e], VMEM) for d in range(n_blk) for e in range(n_op)]
    right_ins = [(block, VMEM) for block in right]
    psi_ins = [(block, VMEM) for block in psi_by]

    tables = [(src, SMEM), (widths, SMEM)]
    wide = ((n_blk, rows, cols), f32, VMEM)
    narrow = ((n_blk, rows, cols), bf16, VMEM)
    dots = ((n_dev, 8, LANES), f32, VMEM)
    sends = [((2, n_blk, step, cols), bf16, VMEM)] * (n_op - 1)
    inter = pltpu.VMEM((n_blk + 1, n_op * terms, rows, cols), bf16)
    left_all = (n_blk, n_op, terms, rows, rows)
    flops = 2 * n_blk * rows * cols * terms * n_op * (rows + cols)
    cost = dict(flops=flops, nbytes=8 << 20)

    def totals(parts):
        return lax.all_to_all(parts, ("blk", "op"), 0, 0, tiled=True)

    sig, raw, dots1, kept, *out1 = kernel(
        functools.partial(first_body, n_blk, n_op),
        tables + left_ins + right_ins + psi_ins + [(dmat, VMEM)],
        [wide, narrow, dots, (left_all, bf16, HBM)] + sends,
        [inter, pltpu.SemaphoreType.DMA((n_dev,))],
        **cost,
    )
    parts1 = totals(dots1)
    got1 = [swap(block, e, n_op) for e, block in enumerate(out1, 1)]
    fld, img, dots2, *out2 = kernel(
        functools.partial(second_body, n_blk, n_op, count),
        tables + [(kept, HBM)] + right_ins + [(x, VMEM) for x in (parts1, raw, sig, dmat)],
        [narrow, wide, dots] + sends,
        [inter, pltpu.VMEM((n_blk, rows, cols), f32), pltpu.VMEM(left_all, bf16), pltpu.SemaphoreType.DMA((n_blk,))],
        **cost,
    )
    parts2 = totals(dots2)
    got2 = [swap(block, e, n_op) for e, block in enumerate(out2, 1)]
    final = ((n_blk, step, n_op * cols), bf16, VMEM)
    new, res, energy = kernel(
        functools.partial(third_body, n_blk, n_op, count),
        [(slots, SMEM)]
        + [(x, VMEM) for x in (parts1, parts2, raw, sig, fld, img, *got1, *got2)],
        [final, final, ((1,), f32, SMEM)],
        nbytes=4 << 20,
    )
    return new, res, energy


def solution(mesh):
    placed = (
        P(("grp", "blk"), None, None),
        P("op", ("grp", "blk"), None, None),
        P("op", ("grp", "blk"), None, None),
        P("op"),
        P("grp"),
        P("grp"),
        P("grp", None),
        P(("grp", "blk")),
    )

    def body(*args):
        psi, left_ops, right_ops, diag_right = args[0], args[1], args[2], args[7]
        n_op = mesh.shape["op"]
        cols = diag_right.shape[0] // n_op
        fits = (
            psi.shape[0] == 1
            and diag_right.shape[0] % n_op == 0
            and cols % LANES == 0
            and cols % right_ops.shape[2] == 0
            and cols // right_ops.shape[2] * n_op == right_ops.shape[1]
            and psi.shape[1] % (16 * n_op) == 0
            and n_op & (n_op - 1) == 0
        )
        return (per_device if fits else per_device_general)(*args)

    return jax.shard_map(
        body,
        mesh=mesh,
        in_specs=placed,
        out_specs=(P("grp", "op", "blk"), P("grp", "op", "blk"), P("grp")),
        check_vma=False,
    )
```

```python
import functools

import jax
import jax.numpy as jnp
from jax import lax
from jax.experimental import pallas as pl
from jax.experimental.pallas import tpu as pltpu
from jax.sharding import PartitionSpec as P

EPS = 1e-06
LANES = 128
VMEM_LIMIT = 20 * 1024 * 1024


def per_device_general(
    psi, left_ops, right_ops, term_shift, slot_sector, sector_width, diag_left, diag_right
):
    sec_dev, rows, ncols = psi.shape
    nsec = slot_sector.shape[0]
    terms_dev = left_ops.shape[0]
    right_local = right_ops.shape[1]
    right_width = right_ops.shape[2]
    local_cols = diag_right.shape[0]
    count = float(nsec * rows * ncols)
    match = slot_sector[:, None] == jnp.arange(nsec)[None, :]
    widths = jnp.sum(jnp.where(match, sector_width[None, :], 0), axis=1)
    mask_all = (jnp.arange(rows)[None, :] < widths[:, None]).astype(jnp.float32)
    own_mask = lax.dynamic_slice_in_dim(mask_all, lax.axis_index("blk") * sec_dev, sec_dev, 0)
    raw = psi.astype(jnp.float32) * own_mask[:, :, None]
    squares = lax.psum(jnp.sum(raw * raw), "blk")
    v_left = (raw * lax.rsqrt(squares / count + EPS)).astype(jnp.bfloat16)
    onehots = (
        slot_sector[None, None, :] == slot_sector[None, :, None] - term_shift[:, None, None]
    ).astype(jnp.bfloat16)
    op_rows = rows // lax.axis_size("op")
    op_start = lax.axis_index("op") * op_rows
    dmat = diag_left[:, :, None] + diag_right[None, None, :]

    def left_local(field):
        return jnp.einsum(
            "ksij,sjc->ksic", left_ops, field, preferred_element_type=jnp.float32
        ).astype(jnp.bfloat16)

    def right_part(moved_in):
        flat = moved_in.reshape(terms_dev, nsec, rows * local_cols)
        shifted = jnp.einsum(
            "kts,ksx->ktx", onehots, flat, preferred_element_type=jnp.float32
        ).astype(jnp.bfloat16)
        shifted = shifted.reshape(terms_dev, nsec, rows, right_local, right_width)
        accum = jnp.einsum(
            "ktwrc,krdc->twrd", shifted, right_ops, preferred_element_type=jnp.float32
        )
        return accum.reshape(nsec, rows, local_cols) * mask_all[:, :, None]

    def op_total(partial_value):
        return lax.psum(partial_value.astype(jnp.bfloat16), "op").astype(jnp.float32)

    def final_rows(array):
        return lax.dynamic_slice_in_dim(array, op_start, op_rows, 1)

    def reduce_dots(values):
        sums = lax.psum(values, "blk")
        return tuple((item / count for item in sums))

    moved_first, v_moved = (
        lax.all_to_all(left_local(v_left), "blk", split_axis=3, concat_axis=1, tiled=True),
        lax.all_to_all(v_left[None], "blk", split_axis=3, concat_axis=1, tiled=True),
    )
    v_right = v_moved[0]
    vec32 = v_right.astype(jnp.float32)
    first_sigma = op_total(right_part(moved_first)) + dmat * vec32
    theta = reduce_dots((jnp.sum(vec32 * first_sigma),))[0]
    resid = first_sigma - theta * vec32
    den = dmat - theta
    corr = resid * den / jnp.maximum(den * den, 0.25)
    along = reduce_dots((jnp.sum(vec32 * corr),))[0]
    orth = corr - along * vec32
    norm_sq = reduce_dots((jnp.sum(orth * orth),))[0]
    update = (orth * lax.rsqrt(norm_sq + EPS)).astype(jnp.bfloat16)
    upd32 = update.astype(jnp.float32)
    upd_left = lax.all_to_all(update, "blk", split_axis=0, concat_axis=2, tiled=True)
    moved_second = lax.all_to_all(
        left_local(upd_left), "blk", split_axis=3, concat_axis=1, tiled=True
    )
    second_sigma = op_total(right_part(moved_second)) + dmat * upd32
    v_s1, u_s0, u_s1 = reduce_dots(
        (jnp.sum(vec32 * second_sigma), jnp.sum(upd32 * first_sigma), jnp.sum(upd32 * second_sigma))
    )
    h_mix = 0.5 * (v_s1 + u_s0)
    coef_v, coef_u, energy = ritz(theta, h_mix, u_s1)
    newvec = coef_v * vec32 + coef_u * upd32
    image = coef_v * first_sigma + coef_u * second_sigma
    new_out = final_rows(newvec.astype(jnp.bfloat16))
    res_out = final_rows((image - energy * newvec).astype(jnp.bfloat16))
    return (new_out, res_out, jnp.reshape(energy, (1,)))


def ritz(theta, h_mix, h_two):
    angle = 0.5 * jnp.arctan2(2.0 * h_mix, theta - h_two)
    sine = jnp.sin(angle)
    flip = jnp.where(sine > 0, -1.0, 1.0)
    coef_v = -sine * flip
    coef_u = jnp.cos(angle) * flip
    half = 0.5 * (theta - h_two)
    energy = 0.5 * (theta + h_two) - jnp.sqrt(half * half + h_mix * h_mix)
    return coef_v, coef_u, energy


VMEM, SMEM, HBM, ANY = pltpu.VMEM, pltpu.SMEM, pltpu.HBM, pl.ANY


def kernel(body, ins, outs, scratch=(), flops=0, nbytes=0):
    return pl.pallas_call(
        body,
        out_shape=[
            HBM(shape, dtype) if space == HBM else jax.ShapeDtypeStruct(shape, dtype)
            for shape, dtype, space in outs
        ],
        in_specs=[pl.BlockSpec(memory_space=space) for _, space in ins],
        out_specs=[pl.BlockSpec(memory_space=space) for _, _, space in outs],
        scratch_shapes=list(scratch),
        compiler_params=pltpu.CompilerParams(vmem_limit_bytes=VMEM_LIMIT),
        cost_estimate=pl.CostEstimate(flops=flops, bytes_accessed=nbytes, transcendentals=0),
    )(*[pltpu.with_memory_space_constraint(x, HBM) if space == HBM else x for x, space in ins])


def onward(block, d, n_blk):
    return lax.ppermute(block, "blk", [(i, (i + d) % n_blk) for i in range(n_blk)])


def swap(block, e, n_op):
    return lax.ppermute(block, "op", [(i, i ^ e) for i in range(n_op)])


def gather(own, n_blk, n_op, pack, table, early):
    bits = [1 << b for b in reversed(range(n_op.bit_length() - 1))]
    left, psi, right, made = {(0, 0): own}, [], [], {}
    waiting = {(0, 0): 0}
    for j in range(n_blk + len(bits)):
        new, moved = {}, {}
        for (d, e), done in waiting.items():
            if e == 0 and d + 1 < n_blk:
                new[d + 1, 0] = onward(left[d, 0], 1, n_blk), 0
            for b in range(done, len(bits)):
                new[d, e ^ bits[b]] = swap(left[d, e], bits[b], n_op), b + 1
        kept = {key: block for key, (block, _) in new.items()}
        if j == 0:
            columns, packed = pack(kept[0, bits[-1]])
            moved["right"] = [packed[0]] + [swap(packed[e], e, n_op) for e in range(1, n_op)]
            moved["columns"] = columns
        elif j < n_blk:
            moved["psi"] = onward(columns[j], j, n_blk)
        if j == 1:
            moved["tables"] = table(right)
        full = j - len(bits) + 1
        if j == n_blk - 1 and full > 0:
            moved["early"] = early(left, psi, full, made["tables"])
        if not kept and not moved:
            break
        waiting = {key: done for key, (_, done) in new.items()}
        kept, moved = lax.optimization_barrier((kept, moved))
        left.update(kept)
        if j == 0:
            columns, right = moved["columns"], moved["right"]
            psi = list(columns[:1])
        elif j < n_blk:
            psi = psi + [moved["psi"]]
        made.update({key: moved[key] for key in ("tables", "early") if key in moved})
    return left, psi, right, made["tables"], made.get("early")


def place_of():
    return lax.axis_index("blk"), lax.axis_index("op")


def pack_body(n_blk, n_op, shift, psi, right_in, *outs):
    psi_out, right_out, right, sems = outs[:n_blk], outs[n_blk : n_blk + n_op], outs[-2], outs[-1]
    cols = psi_out[0].shape[1]
    terms, _, width, _ = right.shape
    per = cols // width
    own_blk, own_op = place_of()
    fetch = pltpu.make_async_copy(right_in, right, sems.at[n_blk])
    fetch.start()
    copies = []
    for d in range(n_blk):
        there = lax.rem(own_blk + d, n_blk)
        start = pl.multiple_of((there * n_op + own_op) * cols, LANES)
        copies.append(
            pltpu.make_async_copy(psi.at[0, :, pl.ds(start, cols)], psi_out[d], sems.at[d])
        )
        copies[-1].start()
    lane = lax.broadcasted_iota(jnp.int32, (16, cols), 1)
    line = jnp.zeros((16, cols), jnp.float32)
    for k in range(terms):
        line = jnp.where(lane == k, shift[k].astype(jnp.float32), line)
    square = [lax.broadcasted_iota(jnp.int32, (width, width), axis) for axis in (0, 1)]
    unit = (square[0] == square[1]).astype(jnp.bfloat16)
    fetch.wait()
    for e in range(n_op):
        there = (own_op ^ e) * per
        for k in range(terms):
            turned = [
                lax.dot_general(
                    right[k, there + r], unit, (((0,), (0,)), ((), ())),
                    preferred_element_type=jnp.float32,
                )
                for r in range(per)
            ]
            line_up = jnp.concatenate(turned, axis=1).astype(jnp.bfloat16)
            right_out[e][k * width : (k + 1) * width] = line_up
        right_out[e][terms * width :] = line.astype(jnp.bfloat16)
    for copy in copies:
        copy.wait()


def table_body(n_blk, n_op, terms, sector, width, left_diag, right_diag, *refs):
    tails, src, widths, slots, dmat = refs[:n_op], *refs[n_op:]
    rows, cols = tails[0].shape
    own_blk, own_op = place_of()
    lane = lax.broadcasted_iota(jnp.int32, (16, cols), 1)
    for d in range(n_blk):
        slot = lax.rem(own_blk - d + n_blk, n_blk)
        slots[d] = slot
        widths[d] = width[sector[slot]]
    for e in range(n_op):
        tail = tails[e][rows - 16 :].astype(jnp.float32)
        for k in range(terms):
            shift = jnp.max(jnp.where(lane == k, tail, -1e9)).astype(jnp.int32)
            for t in range(n_blk):
                want = sector[slots[t]] - shift
                found = jnp.int32(n_blk)
                for d in range(n_blk):
                    found = jnp.where(sector[slots[d]] == want, d, found)
                src[(t * n_op + e) * terms + k] = found
    on_cols = right_diag[:, pl.ds(pl.multiple_of(own_op * cols, LANES), cols)]
    for d in range(n_blk):
        row = left_diag[pl.ds(slots[d], 1), :]
        dmat[d] = jnp.transpose(jnp.broadcast_to(row, (cols, row.shape[1]))) + on_cols


def row_mask(width, shape):
    return lax.broadcasted_iota(jnp.int32, shape, 0) < width


def fold(x):
    return jnp.sum(x.reshape(-1, 8, x.shape[-1]), axis=0)


def whole(x):
    return jnp.sum(jnp.sum(x, axis=0, keepdims=True), axis=1, keepdims=True)


def spread(values, out):
    line = lax.broadcasted_iota(jnp.int32, out.shape[1:], 0)
    tile = jnp.zeros(out.shape[1:], jnp.float32)
    for j, value in enumerate(values):
        tile = jnp.where(line == j, value, tile)
    for d in range(out.shape[0]):
        out[d] = tile


def by_block(packed, terms, cols):
    width = (packed.shape[0] - 16) // terms
    lane = lax.broadcasted_iota(jnp.int32, (width, cols), 1)
    parts = []
    for k in range(terms):
        block = packed[k * width : (k + 1) * width].astype(jnp.float32)
        for r in range(cols // width):
            inside = (lane >= r * width) & (lane < (r + 1) * width)
            parts.append(jnp.where(inside, block, 0.0).astype(jnp.bfloat16))
    return jnp.concatenate(parts, axis=0)


def left_products(block, left, inter):
    n_terms, rows, cols = inter.shape
    at = 0
    while at < n_terms:
        ops = left(at)
        terms = ops.shape[0]
        prod = jnp.dot(ops.reshape(terms * rows, rows), block, preferred_element_type=jnp.float32)
        inter[at : at + terms] = prod.astype(jnp.bfloat16).reshape(terms, rows, cols)
        at += terms


def sum_terms(src, inter, right, emit):
    n_blk, n_terms, _, cols = inter.shape
    n_blk, n_op = n_blk - 1, len(right)
    terms = n_terms // n_op
    diagonal = [by_block(ref, terms, cols) for ref in right]
    for t in range(n_blk):
        total = None
        for e in range(n_op):
            js = range(e * terms, (e + 1) * terms)
            moved = jnp.concatenate([inter[src[t * n_terms + j], j] for j in js], axis=1)
            part = jnp.dot(moved, diagonal[e], preferred_element_type=jnp.float32)
            total = part if total is None else total + part
        emit(t, total)


def keep(left, left_out, sems):
    copies = []
    for d, line in enumerate(left):
        for e, ref in enumerate(line):
            copies.append(pltpu.make_async_copy(ref, left_out.at[d, e], sems.at[d * len(line) + e]))
            copies[-1].start()
    return copies


def masked(ref, width):
    block = ref[...].astype(jnp.float32)
    return jnp.where(row_mask(width, block.shape), block, 0.0).astype(jnp.bfloat16)


def early_body(n_blk, n_op, widths, *refs):
    left = [refs[d * n_op : (d + 1) * n_op] for d in range(n_blk)]
    psi, refs = refs[n_blk * n_op : n_blk * (n_op + 1)], refs[n_blk * (n_op + 1) :]
    inter_out, left_out, sems = refs
    copies = keep(left, left_out, sems)
    for d in range(n_blk):
        terms = left[d][0].shape[0]
        left_products(
            masked(psi[d], widths[d]), lambda at: left[d][at // terms][...], inter_out.at[d]
        )
    for copy in copies:
        copy.wait()


def send_rows(sends, j, d, ref):
    _, own_op = place_of()
    step = sends[0].shape[2]
    for e, send in enumerate(sends, 1):
        start = pl.multiple_of((own_op ^ e) * step, step)
        send[j, d] = ref[d, pl.ds(start, step)].astype(send.dtype)


def first_body(n_blk, n_op, n_early, src, widths, *refs):
    n_late = n_blk - n_early
    left = [refs[d * n_op : (d + 1) * n_op] for d in range(n_late)]
    refs = refs[n_late * n_op :]
    right, psi, refs = refs[:n_op], refs[n_op : n_op + n_blk], refs[n_op + n_blk :]
    dmat, inter_in, sig_out, raw_out, dots_out, left_out = refs[:6]
    sends, inter, sems = refs[6:-2], refs[-2], refs[-1]
    copies = keep(left, left_out, sems)
    ready = pltpu.make_async_copy(inter_in, inter.at[:n_early], sems.at[n_late * n_op])
    ready.start()
    inter[n_blk] = jnp.zeros_like(inter[n_blk])
    for d in range(n_blk):
        raw_out[d] = masked(psi[d], widths[d])
    for d in range(n_late):
        terms = left[d][0].shape[0]
        left_products(
            raw_out[n_early + d], lambda at: left[d][at // terms][...], inter.at[n_early + d]
        )
    ready.wait()
    zero = jnp.zeros((8, dmat.shape[2]), jnp.float32)
    sums = [zero, zero]

    def emit(d, total):
        raw = raw_out[d].astype(jnp.float32)
        sigma = jnp.where(row_mask(widths[d], raw.shape), total, 0.0) + dmat[d] * raw
        sig_out[d] = sigma
        sums[0] = sums[0] + fold(raw * raw)
        sums[1] = sums[1] + fold(raw * sigma)
        send_rows(sends, 0, d, raw_out)
        send_rows(sends, 1, d, sig_out)

    sum_terms(src, inter, right, emit)
    spread([whole(x) for x in sums], dots_out)
    for copy in copies:
        copy.wait()


def norm_theta(parts, count):
    tot = jnp.sum(parts, axis=0) * (1.0 / count)
    scale = lax.rsqrt(tot[0:1] + EPS)
    return scale, tot[1:2] * scale * scale


def second_body(n_blk, n_op, count, src, widths, left_early, left_late, *refs):
    right, refs = refs[:n_op], refs[n_op:]
    n_early = left_early.shape[0]
    parts, raw_in, sig_in, dmat, f_out, t_out, dots_out = refs[:7]
    sends, inter, corr, held, sems = refs[7:-4], *refs[-4:]
    copies = []
    for d in range(n_blk):
        kept = left_early.at[d] if d < n_early else left_late.at[d - n_early]
        copies.append(pltpu.make_async_copy(kept, held.at[d], sems.at[d]))
        copies[-1].start()
    inter[n_blk] = jnp.zeros_like(inter[n_blk])
    scale, theta = norm_theta(parts[...], count)
    zero = jnp.zeros((8, raw_in.shape[2]), jnp.float32)
    vv, vc, vs = zero, zero, zero
    for d in range(n_blk):
        vec = raw_in[d].astype(jnp.float32) * scale
        sigma = sig_in[d] * scale
        den = dmat[d] - theta
        item = (sigma - theta * vec) * den / jnp.maximum(den * den, 0.25)
        corr[d] = item
        vv, vc, vs = vv + fold(vec * vec), vc + fold(vec * item), vs + fold(vec * sigma)
    vv, vc, vs = whole(vv), whole(vc), whole(vs)
    along = vc / jnp.maximum(vv, 1e-30)

    for d in range(n_blk):
        vec = raw_in[d].astype(jnp.float32) * scale
        f_out[d] = (corr[d] - along * vec).astype(jnp.bfloat16)
        copies[d].wait()
        terms = held.shape[2]
        left_products(f_out[d], lambda at: held[d, at // terms], inter.at[d])
    sums = [zero for _ in range(5)]

    def emit(d, total):
        fld = f_out[d].astype(jnp.float32)
        image = jnp.where(row_mask(widths[d], fld.shape), total, 0.0) + dmat[d] * fld
        t_out[d] = image
        vec = raw_in[d].astype(jnp.float32) * scale
        sigma = sig_in[d] * scale
        prods = (fld * fld, vec * fld, vec * image, fld * sigma, fld * image)
        sums[:] = [one + fold(prod) for one, prod in zip(sums, prods)]
        send_rows(sends, 0, d, f_out)
        send_rows(sends, 1, d, t_out)

    sum_terms(src, inter, right, emit)
    spread([vv, vc, vs] + [whole(x) for x in sums], dots_out)


def ritz_pair(theta, h_mix, h_two):
    diff, twice = theta - h_two, 2.0 * h_mix
    size = jnp.sqrt(diff * diff + twice * twice)
    some = size > 0.0
    safe = jnp.where(some, size, 1.0)
    big = jnp.sqrt(0.5 + 0.5 * jnp.abs(diff) / safe)
    small = 0.5 * jnp.abs(twice) / (safe * big)
    sine = jnp.where(diff >= 0.0, small, big)
    cosine = jnp.where(diff >= 0.0, big, small)
    sine = jnp.where(some, sine, 0.0)
    cosine = jnp.where(some, cosine, 1.0)
    upward = (twice > 0.0) | ((twice == 0.0) & (diff < 0.0))
    return sine, jnp.where(upward, -cosine, cosine), 0.5 * (theta + h_two) - 0.5 * size


def third_body(n_blk, n_op, count, slots, parts1, parts2, raw_in, sig_in, f_in, t_in, *refs):
    got1, got2 = refs[: n_op - 1], refs[n_op - 1 : 2 * (n_op - 1)]
    new_out, res_out, energy_out = refs[2 * (n_op - 1) :]
    step, cols = new_out.shape[1], raw_in.shape[2]
    own_blk, own_op = place_of()
    scale, theta = norm_theta(parts1[...], count)
    vv, vc, vs, ff, vf, vt, fs, ft = (parts2[:, j, :] for j in range(8))

    def mean(x):
        return jnp.sum(x, axis=0, keepdims=True) * (1.0 / count)

    along = mean(vc)
    beta = vc / jnp.maximum(vv, 1e-30) - along
    norm_sq = mean(ff + 2.0 * beta * vf + beta * beta * vv)
    unit = lax.rsqrt(jnp.maximum(norm_sq, 0.0) + EPS)
    v_s1 = unit * mean(vt + beta * vs)
    u_s0 = unit * mean(fs + beta * vs)
    u_s1 = unit * unit * mean(ft + beta * (vt + fs) + beta * beta * vs)
    cv, cu, energy = ritz_pair(theta, 0.5 * (v_s1 + u_s0), u_s1)
    energy_out[0] = jnp.max(energy)
    cu = cu * unit
    for e in range(n_op):
        there = own_op ^ e
        tile = parts2[own_blk * n_op + there]
        back = tile[1:2] / jnp.maximum(tile[0:1], 1e-30) - along
        on_vec = (cv + cu * back) * scale
        at = pl.multiple_of(there * cols, LANES)
        for d in range(n_blk):
            if e:
                blocks = got1[e - 1][0, d], got1[e - 1][1, d], got2[e - 1][0, d], got2[e - 1][1, d]
            else:
                rows = pl.ds(pl.multiple_of(own_op * step, step), step)
                blocks = raw_in[d, rows], sig_in[d, rows], f_in[d, rows], t_in[d, rows]
            raw, sigma, fld, image = (block.astype(jnp.float32) for block in blocks)
            newvec = on_vec * raw + cu * fld
            res = on_vec * sigma + cu * image - energy * newvec
            new_out[slots[d], :, pl.ds(at, cols)] = newvec.astype(jnp.bfloat16)
            res_out[slots[d], :, pl.ds(at, cols)] = res.astype(jnp.bfloat16)


def per_device(
    psi, left_ops, right_ops, term_shift, slot_sector, sector_width, diag_left, diag_right
):
    n_blk, n_op = lax.axis_size("blk"), lax.axis_size("op")
    _, rows, ncols = psi.shape
    terms, _, width, _ = right_ops.shape
    cols = diag_right.shape[0] // n_op
    step = rows // n_op
    count = float(n_blk * rows * ncols)
    n_dev = n_blk * n_op
    bf16, f32 = jnp.bfloat16, jnp.float32

    def pack(after):
        given = lax.optimization_barrier((term_shift, psi, right_ops, after))
        sent = kernel(
            functools.partial(pack_body, n_blk, n_op),
            list(zip(given, (SMEM, HBM, HBM))),
            [((rows, cols), bf16, VMEM)] * n_blk + [((terms * width + 16, cols), bf16, VMEM)] * n_op,
            [pltpu.VMEM(right_ops.shape, bf16), pltpu.SemaphoreType.DMA((n_blk + 1,))],
            nbytes=1 << 20,
        )
        return sent[:n_blk], sent[n_blk:]

    def table(right):
        return kernel(
            functools.partial(table_body, n_blk, n_op, terms),
            [(slot_sector, SMEM), (sector_width, SMEM), (diag_left, VMEM), (diag_right[None], VMEM)]
            + [(block, VMEM) for block in right],
            [((n_blk * n_op * terms,), jnp.int32, SMEM)]
            + [((n_blk,), jnp.int32, SMEM)] * 2
            + [((n_blk, rows, cols), f32, VMEM)],
        )

    def early(left, psi, n_early, tables):
        outs = [
            ((n_early, n_op * terms, rows, cols), bf16, VMEM),
            ((n_early, n_op, terms, rows, rows), bf16, HBM),
        ]
        return kernel(
            functools.partial(early_body, n_early, n_op),
            [(tables[1], SMEM)]
            + [(left[d, e], VMEM) for d in range(n_early) for e in range(n_op)]
            + [(psi[d], VMEM) for d in range(n_early)],
            outs,
            [pltpu.SemaphoreType.DMA((n_early * n_op,))],
            flops=2 * n_early * rows * rows * cols * terms * n_op,
            nbytes=8 << 20,
        )

    left, psi_by, right, (src, widths, slots, dmat), (inter_early, left_early) = gather(
        left_ops[:, 0], n_blk, n_op, pack, table, early
    )
    n_early = inter_early.shape[0]
    n_late = n_blk - n_early
    left_ins = [(left[d, e], VMEM) for d in range(n_early, n_blk) for e in range(n_op)]
    right_ins = [(block, VMEM) for block in right]
    psi_ins = [(block, VMEM) for block in psi_by]

    tables = [(src, SMEM), (widths, SMEM)]
    wide = ((n_blk, rows, cols), f32, VMEM)
    narrow = ((n_blk, rows, cols), bf16, VMEM)
    dots = ((n_dev, 8, LANES), f32, VMEM)
    sends = [((2, n_blk, step, cols), bf16, VMEM)] * (n_op - 1)
    inter = pltpu.VMEM((n_blk + 1, n_op * terms, rows, cols), bf16)
    left_late = (n_late, n_op, terms, rows, rows)
    flops = 2 * n_blk * rows * cols * terms * n_op * (rows + cols)
    cost = dict(flops=flops, nbytes=8 << 20)

    def totals(parts):
        return lax.all_to_all(parts, ("blk", "op"), 0, 0, tiled=True)

    sig, raw, dots1, kept, *out1 = kernel(
        functools.partial(first_body, n_blk, n_op, n_early),
        tables + left_ins + right_ins + psi_ins + [(dmat, VMEM), (inter_early, VMEM)],
        [wide, narrow, dots, (left_late, bf16, HBM)] + sends,
        [inter, pltpu.SemaphoreType.DMA((n_late * n_op + 1,))],
        **cost,
    )
    parts1 = totals(dots1)
    got1 = [swap(block, e, n_op) for e, block in enumerate(out1, 1)]
    fld, img, dots2, *out2 = kernel(
        functools.partial(second_body, n_blk, n_op, count),
        tables + [(left_early, HBM), (kept, HBM)] + right_ins + [(x, VMEM) for x in (parts1, raw, sig, dmat)],
        [narrow, wide, dots] + sends,
        [inter, pltpu.VMEM((n_blk, rows, cols), f32), pltpu.VMEM((n_blk, *left_late[1:]), bf16), pltpu.SemaphoreType.DMA((n_blk,))],
        **cost,
    )
    parts2 = totals(dots2)
    got2 = [swap(block, e, n_op) for e, block in enumerate(out2, 1)]
    final = ((n_blk, step, n_op * cols), bf16, VMEM)
    new, res, energy = kernel(
        functools.partial(third_body, n_blk, n_op, count),
        [(slots, SMEM)]
        + [(x, VMEM) for x in (parts1, parts2, raw, sig, fld, img, *got1, *got2)],
        [final, final, ((1,), f32, SMEM)],
        nbytes=4 << 20,
    )
    return new, res, energy


def solution(mesh):
    placed = (
        P(("grp", "blk"), None, None),
        P("op", ("grp", "blk"), None, None),
        P("op", ("grp", "blk"), None, None),
        P("op"),
        P("grp"),
        P("grp"),
        P("grp", None),
        P(("grp", "blk")),
    )

    def body(*args):
        psi, left_ops, right_ops, diag_right = args[0], args[1], args[2], args[7]
        n_op = mesh.shape["op"]
        cols = diag_right.shape[0] // n_op
        fits = (
            psi.shape[0] == 1
            and diag_right.shape[0] % n_op == 0
            and cols % LANES == 0
            and cols % right_ops.shape[2] == 0
            and cols // right_ops.shape[2] * n_op == right_ops.shape[1]
            and psi.shape[1] % (16 * n_op) == 0
            and n_op & (n_op - 1) == 0
            and mesh.shape["blk"] >= n_op.bit_length()
        )
        return (per_device if fits else per_device_general)(*args)

    return jax.shard_map(
        body,
        mesh=mesh,
        in_specs=placed,
        out_specs=(P("grp", "op", "blk"), P("grp", "op", "blk"), P("grp")),
        check_vma=False,
    )
```

```python
import functools

import jax
import jax.numpy as jnp
from jax import lax
from jax.experimental import pallas as pl
from jax.experimental.pallas import tpu as pltpu
from jax.sharding import PartitionSpec as P

EPS = 1e-06
LANES = 128
VMEM_LIMIT = 20 * 1024 * 1024


def per_device_general(
    psi, left_ops, right_ops, term_shift, slot_sector, sector_width, diag_left, diag_right
):
    sec_dev, rows, ncols = psi.shape
    nsec = slot_sector.shape[0]
    terms_dev = left_ops.shape[0]
    right_local = right_ops.shape[1]
    right_width = right_ops.shape[2]
    local_cols = diag_right.shape[0]
    count = float(nsec * rows * ncols)
    match = slot_sector[:, None] == jnp.arange(nsec)[None, :]
    widths = jnp.sum(jnp.where(match, sector_width[None, :], 0), axis=1)
    mask_all = (jnp.arange(rows)[None, :] < widths[:, None]).astype(jnp.float32)
    own_mask = lax.dynamic_slice_in_dim(mask_all, lax.axis_index("blk") * sec_dev, sec_dev, 0)
    raw = psi.astype(jnp.float32) * own_mask[:, :, None]
    squares = lax.psum(jnp.sum(raw * raw), "blk")
    v_left = (raw * lax.rsqrt(squares / count + EPS)).astype(jnp.bfloat16)
    onehots = (
        slot_sector[None, None, :] == slot_sector[None, :, None] - term_shift[:, None, None]
    ).astype(jnp.bfloat16)
    op_rows = rows // lax.axis_size("op")
    op_start = lax.axis_index("op") * op_rows
    dmat = diag_left[:, :, None] + diag_right[None, None, :]

    def left_local(field):
        return jnp.einsum(
            "ksij,sjc->ksic", left_ops, field, preferred_element_type=jnp.float32
        ).astype(jnp.bfloat16)

    def right_part(moved_in):
        flat = moved_in.reshape(terms_dev, nsec, rows * local_cols)
        shifted = jnp.einsum(
            "kts,ksx->ktx", onehots, flat, preferred_element_type=jnp.float32
        ).astype(jnp.bfloat16)
        shifted = shifted.reshape(terms_dev, nsec, rows, right_local, right_width)
        accum = jnp.einsum(
            "ktwrc,krdc->twrd", shifted, right_ops, preferred_element_type=jnp.float32
        )
        return accum.reshape(nsec, rows, local_cols) * mask_all[:, :, None]

    def op_total(partial_value):
        return lax.psum(partial_value.astype(jnp.bfloat16), "op").astype(jnp.float32)

    def final_rows(array):
        return lax.dynamic_slice_in_dim(array, op_start, op_rows, 1)

    def reduce_dots(values):
        sums = lax.psum(values, "blk")
        return tuple((item / count for item in sums))

    moved_first, v_moved = (
        lax.all_to_all(left_local(v_left), "blk", split_axis=3, concat_axis=1, tiled=True),
        lax.all_to_all(v_left[None], "blk", split_axis=3, concat_axis=1, tiled=True),
    )
    v_right = v_moved[0]
    vec32 = v_right.astype(jnp.float32)
    first_sigma = op_total(right_part(moved_first)) + dmat * vec32
    theta = reduce_dots((jnp.sum(vec32 * first_sigma),))[0]
    resid = first_sigma - theta * vec32
    den = dmat - theta
    corr = resid * den / jnp.maximum(den * den, 0.25)
    along = reduce_dots((jnp.sum(vec32 * corr),))[0]
    orth = corr - along * vec32
    norm_sq = reduce_dots((jnp.sum(orth * orth),))[0]
    update = (orth * lax.rsqrt(norm_sq + EPS)).astype(jnp.bfloat16)
    upd32 = update.astype(jnp.float32)
    upd_left = lax.all_to_all(update, "blk", split_axis=0, concat_axis=2, tiled=True)
    moved_second = lax.all_to_all(
        left_local(upd_left), "blk", split_axis=3, concat_axis=1, tiled=True
    )
    second_sigma = op_total(right_part(moved_second)) + dmat * upd32
    v_s1, u_s0, u_s1 = reduce_dots(
        (jnp.sum(vec32 * second_sigma), jnp.sum(upd32 * first_sigma), jnp.sum(upd32 * second_sigma))
    )
    h_mix = 0.5 * (v_s1 + u_s0)
    coef_v, coef_u, energy = ritz(theta, h_mix, u_s1)
    newvec = coef_v * vec32 + coef_u * upd32
    image = coef_v * first_sigma + coef_u * second_sigma
    new_out = final_rows(newvec.astype(jnp.bfloat16))
    res_out = final_rows((image - energy * newvec).astype(jnp.bfloat16))
    return (new_out, res_out, jnp.reshape(energy, (1,)))


def ritz(theta, h_mix, h_two):
    angle = 0.5 * jnp.arctan2(2.0 * h_mix, theta - h_two)
    sine = jnp.sin(angle)
    flip = jnp.where(sine > 0, -1.0, 1.0)
    coef_v = -sine * flip
    coef_u = jnp.cos(angle) * flip
    half = 0.5 * (theta - h_two)
    energy = 0.5 * (theta + h_two) - jnp.sqrt(half * half + h_mix * h_mix)
    return coef_v, coef_u, energy


VMEM, SMEM, HBM, ANY = pltpu.VMEM, pltpu.SMEM, pltpu.HBM, pl.ANY


def kernel(body, ins, outs, scratch=(), flops=0, nbytes=0):
    return pl.pallas_call(
        body,
        out_shape=[
            HBM(shape, dtype) if space == HBM else jax.ShapeDtypeStruct(shape, dtype)
            for shape, dtype, space in outs
        ],
        in_specs=[pl.BlockSpec(memory_space=space) for _, space in ins],
        out_specs=[pl.BlockSpec(memory_space=space) for _, _, space in outs],
        scratch_shapes=list(scratch),
        compiler_params=pltpu.CompilerParams(vmem_limit_bytes=VMEM_LIMIT),
        cost_estimate=pl.CostEstimate(flops=flops, bytes_accessed=nbytes, transcendentals=0),
    )(*[pltpu.with_memory_space_constraint(x, HBM) if space == HBM else x for x, space in ins])


def ring_at(place, n_blk):
    place = place % n_blk if isinstance(place, int) else lax.rem(place + n_blk, n_blk)
    odd, even = 2 * place - 1, 2 * (n_blk - place)
    if isinstance(place, int):
        return 0 if place == 0 else odd if odd < n_blk else even
    return jnp.where(place == 0, 0, jnp.where(odd < n_blk, odd, even))


def ring_place(index, n_blk):
    odd, even = (index + 1) // 2, lax.rem(n_blk - index // 2, n_blk)
    return jnp.where(lax.rem(index, 2) == 1, odd, even)


def onward(block, d, n_blk):
    pairs = [(ring_at(i, n_blk), ring_at(i + d, n_blk)) for i in range(n_blk)]
    return lax.ppermute(block, "blk", pairs)


def swap(block, e, n_op):
    return lax.ppermute(block, "op", [(i, i ^ e) for i in range(n_op)])


def gather(own, n_blk, n_op, pack, table, early):
    bits = [1 << b for b in reversed(range(n_op.bit_length() - 1))]
    left, psi, right, made = {(0, 0): own}, [], [], {}
    waiting = {(0, 0): 0}
    for j in range(n_blk + len(bits)):
        new, moved = {}, {}
        for (d, e), done in waiting.items():
            if e == 0 and d + 1 < n_blk:
                new[d + 1, 0] = onward(left[d, 0], 1, n_blk), 0
            for b in range(done, len(bits)):
                new[d, e ^ bits[b]] = swap(left[d, e], bits[b], n_op), b + 1
        kept = {key: block for key, (block, _) in new.items()}
        if j == 0:
            columns, packed = pack(kept[0, bits[-1]])
            moved["right"] = [packed[0]] + [swap(packed[e], e, n_op) for e in range(1, n_op)]
            moved["columns"] = columns
        else:
            due = {1: [1], n_blk - 1: list(range(2, n_blk))}.get(j, [])
            moved["psi"] = [onward(columns[d], d, n_blk) for d in due]
        if j == 1:
            moved["tables"] = table(right)
        full = j - len(bits) + 1
        if j == n_blk - 1 and full > 0:
            moved["early"] = early(left, psi, full, made["tables"])
        if not kept:
            break
        waiting = {key: done for key, (_, done) in new.items()}
        kept, moved = lax.optimization_barrier((kept, moved))
        left.update(kept)
        if j == 0:
            columns, right = moved["columns"], moved["right"]
            psi = list(columns[:1])
        else:
            psi = psi + moved["psi"]
        made.update({key: moved[key] for key in ("tables", "early") if key in moved})
    return left, psi, right, made["tables"], made.get("early")


def place_of():
    return lax.axis_index("blk"), lax.axis_index("op")


def pack_body(n_blk, n_op, shift, psi, right_in, *outs):
    psi_out, right_out, right, sems = outs[:n_blk], outs[n_blk : n_blk + n_op], outs[-2], outs[-1]
    cols = psi_out[0].shape[1]
    terms, _, width, _ = right.shape
    per = cols // width
    own_blk, own_op = place_of()
    fetch = pltpu.make_async_copy(right_in, right, sems.at[n_blk])
    fetch.start()
    copies = []
    for d in range(n_blk):
        there = ring_at(ring_place(own_blk, n_blk) + d, n_blk)
        start = pl.multiple_of((there * n_op + own_op) * cols, LANES)
        copies.append(
            pltpu.make_async_copy(psi.at[0, :, pl.ds(start, cols)], psi_out[d], sems.at[d])
        )
        copies[-1].start()
    lane = lax.broadcasted_iota(jnp.int32, (16, cols), 1)
    line = jnp.zeros((16, cols), jnp.float32)
    for k in range(terms):
        line = jnp.where(lane == k, shift[k].astype(jnp.float32), line)
    square = [lax.broadcasted_iota(jnp.int32, (width, width), axis) for axis in (0, 1)]
    unit = (square[0] == square[1]).astype(jnp.bfloat16)
    fetch.wait()
    for e in range(n_op):
        there = (own_op ^ e) * per
        for k in range(terms):
            turned = [
                lax.dot_general(
                    right[k, there + r], unit, (((0,), (0,)), ((), ())),
                    preferred_element_type=jnp.float32,
                )
                for r in range(per)
            ]
            line_up = jnp.concatenate(turned, axis=1).astype(jnp.bfloat16)
            right_out[e][k * width : (k + 1) * width] = line_up
        right_out[e][terms * width :] = line.astype(jnp.bfloat16)
    for copy in copies:
        copy.wait()


def table_body(n_blk, n_op, terms, sector, width, left_diag, right_diag, *refs):
    tails, src, widths, slots, dmat = refs[:n_op], *refs[n_op:]
    rows, cols = tails[0].shape
    own_blk, own_op = place_of()
    lane = lax.broadcasted_iota(jnp.int32, (16, cols), 1)
    for d in range(n_blk):
        slot = ring_at(ring_place(own_blk, n_blk) - d, n_blk)
        slots[d] = slot
        widths[d] = width[sector[slot]]
    for e in range(n_op):
        tail = tails[e][rows - 16 :].astype(jnp.float32)
        for k in range(terms):
            shift = jnp.max(jnp.where(lane == k, tail, -1e9)).astype(jnp.int32)
            for t in range(n_blk):
                want = sector[slots[t]] - shift
                found = jnp.int32(n_blk)
                for d in range(n_blk):
                    found = jnp.where(sector[slots[d]] == want, d, found)
                src[(t * n_op + e) * terms + k] = found
    on_cols = right_diag[:, pl.ds(pl.multiple_of(own_op * cols, LANES), cols)]
    for d in range(n_blk):
        row = left_diag[pl.ds(slots[d], 1), :]
        dmat[d] = jnp.transpose(jnp.broadcast_to(row, (cols, row.shape[1]))) + on_cols


def row_mask(width, shape):
    return lax.broadcasted_iota(jnp.int32, shape, 0) < width


def fold(x):
    return jnp.sum(x.reshape(-1, 8, x.shape[-1]), axis=0)


def whole(x):
    return jnp.sum(jnp.sum(x, axis=0, keepdims=True), axis=1, keepdims=True)


def spread(values, out):
    line = lax.broadcasted_iota(jnp.int32, out.shape[1:], 0)
    tile = jnp.zeros(out.shape[1:], jnp.float32)
    for j, value in enumerate(values):
        tile = jnp.where(line == j, value, tile)
    for d in range(out.shape[0]):
        out[d] = tile


def by_block(packed, terms, cols):
    width = (packed.shape[0] - 16) // terms
    lane = lax.broadcasted_iota(jnp.int32, (width, cols), 1)
    parts = []
    for k in range(terms):
        block = packed[k * width : (k + 1) * width].astype(jnp.float32)
        for r in range(cols // width):
            inside = (lane >= r * width) & (lane < (r + 1) * width)
            parts.append(jnp.where(inside, block, 0.0).astype(jnp.bfloat16))
    return jnp.concatenate(parts, axis=0)


def left_products(block, left, inter):
    n_terms, rows, cols = inter.shape
    at = 0
    while at < n_terms:
        ops = left(at)
        terms = ops.shape[0]
        prod = jnp.dot(ops.reshape(terms * rows, rows), block, preferred_element_type=jnp.float32)
        inter[at : at + terms] = prod.astype(jnp.bfloat16).reshape(terms, rows, cols)
        at += terms


def sum_terms(src, inter, right, emit):
    n_blk, n_terms, _, cols = inter.shape
    n_blk, n_op = n_blk - 1, len(right)
    terms = n_terms // n_op
    diagonal = [by_block(ref, terms, cols) for ref in right]
    for t in range(n_blk):
        total = None
        for e in range(n_op):
            js = range(e * terms, (e + 1) * terms)
            moved = jnp.concatenate([inter[src[t * n_terms + j], j] for j in js], axis=1)
            part = jnp.dot(moved, diagonal[e], preferred_element_type=jnp.float32)
            total = part if total is None else total + part
        emit(t, total)


def keep(left, left_out, sems):
    copies = []
    for d, line in enumerate(left):
        for e, ref in enumerate(line):
            copies.append(pltpu.make_async_copy(ref, left_out.at[d, e], sems.at[d * len(line) + e]))
            copies[-1].start()
    return copies


def masked(ref, width):
    block = ref[...].astype(jnp.float32)
    return jnp.where(row_mask(width, block.shape), block, 0.0).astype(jnp.bfloat16)


def early_body(n_blk, n_op, widths, *refs):
    left = [refs[d * n_op : (d + 1) * n_op] for d in range(n_blk)]
    psi, refs = refs[n_blk * n_op : n_blk * (n_op + 1)], refs[n_blk * (n_op + 1) :]
    inter_out, left_out, sems = refs
    copies = keep(left, left_out, sems)
    for d in range(n_blk):
        terms = left[d][0].shape[0]
        left_products(
            masked(psi[d], widths[d]), lambda at: left[d][at // terms][...], inter_out.at[d]
        )
    for copy in copies:
        copy.wait()


def send_rows(sends, j, d, ref):
    _, own_op = place_of()
    step = sends[0].shape[2]
    for e, send in enumerate(sends, 1):
        start = pl.multiple_of((own_op ^ e) * step, step)
        send[j, d] = ref[d, pl.ds(start, step)].astype(send.dtype)


def first_body(n_blk, n_op, n_early, src, widths, *refs):
    n_late = n_blk - n_early
    left = [refs[d * n_op : (d + 1) * n_op] for d in range(n_late)]
    refs = refs[n_late * n_op :]
    right, psi, refs = refs[:n_op], refs[n_op : n_op + n_blk], refs[n_op + n_blk :]
    dmat, inter_in, sig_out, raw_out, dots_out, left_out = refs[:6]
    sends, inter, sems = refs[6:-2], refs[-2], refs[-1]
    copies = keep(left, left_out, sems)
    ready = pltpu.make_async_copy(inter_in, inter.at[:n_early], sems.at[n_late * n_op])
    ready.start()
    inter[n_blk] = jnp.zeros_like(inter[n_blk])
    for d in range(n_blk):
        raw_out[d] = masked(psi[d], widths[d])
    for d in range(n_late):
        terms = left[d][0].shape[0]
        left_products(
            raw_out[n_early + d], lambda at: left[d][at // terms][...], inter.at[n_early + d]
        )
    ready.wait()
    zero = jnp.zeros((8, dmat.shape[2]), jnp.float32)
    sums = [zero, zero]

    def emit(d, total):
        raw = raw_out[d].astype(jnp.float32)
        sigma = jnp.where(row_mask(widths[d], raw.shape), total, 0.0) + dmat[d] * raw
        sig_out[d] = sigma
        sums[0] = sums[0] + fold(raw * raw)
        sums[1] = sums[1] + fold(raw * sigma)
        send_rows(sends, 0, d, raw_out)
        send_rows(sends, 1, d, sig_out)

    sum_terms(src, inter, right, emit)
    spread([whole(x) for x in sums], dots_out)
    for copy in copies:
        copy.wait()


def norm_theta(parts, count):
    tot = jnp.sum(parts, axis=0) * (1.0 / count)
    scale = lax.rsqrt(tot[0:1] + EPS)
    return scale, tot[1:2] * scale * scale


def second_body(n_blk, n_op, count, src, widths, left_early, left_late, *refs):
    right, refs = refs[:n_op], refs[n_op:]
    n_early = left_early.shape[0]
    parts, raw_in, sig_in, dmat, f_out, t_out, dots_out = refs[:7]
    sends, inter, corr, held, sems = refs[7:-4], *refs[-4:]
    copies = []
    for d in range(n_blk):
        kept = left_early.at[d] if d < n_early else left_late.at[d - n_early]
        copies.append(pltpu.make_async_copy(kept, held.at[d], sems.at[d]))
        copies[-1].start()
    inter[n_blk] = jnp.zeros_like(inter[n_blk])
    scale, theta = norm_theta(parts[...], count)
    zero = jnp.zeros((8, raw_in.shape[2]), jnp.float32)
    vv, vc, vs = zero, zero, zero
    for d in range(n_blk):
        vec = raw_in[d].astype(jnp.float32) * scale
        sigma = sig_in[d] * scale
        den = dmat[d] - theta
        item = (sigma - theta * vec) * den / jnp.maximum(den * den, 0.25)
        corr[d] = item
        vv, vc, vs = vv + fold(vec * vec), vc + fold(vec * item), vs + fold(vec * sigma)
    vv, vc, vs = whole(vv), whole(vc), whole(vs)
    along = vc / jnp.maximum(vv, 1e-30)

    for d in range(n_blk):
        vec = raw_in[d].astype(jnp.float32) * scale
        f_out[d] = (corr[d] - along * vec).astype(jnp.bfloat16)
        copies[d].wait()
        terms = held.shape[2]
        left_products(f_out[d], lambda at: held[d, at // terms], inter.at[d])
    sums = [zero for _ in range(5)]

    def emit(d, total):
        fld = f_out[d].astype(jnp.float32)
        image = jnp.where(row_mask(widths[d], fld.shape), total, 0.0) + dmat[d] * fld
        t_out[d] = image
        vec = raw_in[d].astype(jnp.float32) * scale
        sigma = sig_in[d] * scale
        prods = (fld * fld, vec * fld, vec * image, fld * sigma, fld * image)
        sums[:] = [one + fold(prod) for one, prod in zip(sums, prods)]
        send_rows(sends, 0, d, f_out)
        send_rows(sends, 1, d, t_out)

    sum_terms(src, inter, right, emit)
    spread([vv, vc, vs] + [whole(x) for x in sums], dots_out)


def ritz_pair(theta, h_mix, h_two):
    diff, twice = theta - h_two, 2.0 * h_mix
    size = jnp.sqrt(diff * diff + twice * twice)
    some = size > 0.0
    safe = jnp.where(some, size, 1.0)
    big = jnp.sqrt(0.5 + 0.5 * jnp.abs(diff) / safe)
    small = 0.5 * jnp.abs(twice) / (safe * big)
    sine = jnp.where(diff >= 0.0, small, big)
    cosine = jnp.where(diff >= 0.0, big, small)
    sine = jnp.where(some, sine, 0.0)
    cosine = jnp.where(some, cosine, 1.0)
    upward = (twice > 0.0) | ((twice == 0.0) & (diff < 0.0))
    return sine, jnp.where(upward, -cosine, cosine), 0.5 * (theta + h_two) - 0.5 * size


def third_body(n_blk, n_op, count, slots, parts1, parts2, raw_in, sig_in, f_in, t_in, *refs):
    got1, got2 = refs[: n_op - 1], refs[n_op - 1 : 2 * (n_op - 1)]
    new_out, res_out, energy_out = refs[2 * (n_op - 1) :]
    step, cols = new_out.shape[1], raw_in.shape[2]
    own_blk, own_op = place_of()
    scale, theta = norm_theta(parts1[...], count)
    vv, vc, vs, ff, vf, vt, fs, ft = (parts2[:, j, :] for j in range(8))

    def mean(x):
        return jnp.sum(x, axis=0, keepdims=True) * (1.0 / count)

    along = mean(vc)
    beta = vc / jnp.maximum(vv, 1e-30) - along
    norm_sq = mean(ff + 2.0 * beta * vf + beta * beta * vv)
    unit = lax.rsqrt(jnp.maximum(norm_sq, 0.0) + EPS)
    v_s1 = unit * mean(vt + beta * vs)
    u_s0 = unit * mean(fs + beta * vs)
    u_s1 = unit * unit * mean(ft + beta * (vt + fs) + beta * beta * vs)
    cv, cu, energy = ritz_pair(theta, 0.5 * (v_s1 + u_s0), u_s1)
    energy_out[0] = jnp.max(energy)
    cu = cu * unit
    for e in range(n_op):
        there = own_op ^ e
        tile = parts2[own_blk * n_op + there]
        back = tile[1:2] / jnp.maximum(tile[0:1], 1e-30) - along
        on_vec = (cv + cu * back) * scale
        at = pl.multiple_of(there * cols, LANES)
        for d in range(n_blk):
            if e:
                blocks = got1[e - 1][0, d], got1[e - 1][1, d], got2[e - 1][0, d], got2[e - 1][1, d]
            else:
                rows = pl.ds(pl.multiple_of(own_op * step, step), step)
                blocks = raw_in[d, rows], sig_in[d, rows], f_in[d, rows], t_in[d, rows]
            raw, sigma, fld, image = (block.astype(jnp.float32) for block in blocks)
            newvec = on_vec * raw + cu * fld
            res = on_vec * sigma + cu * image - energy * newvec
            new_out[slots[d], :, pl.ds(at, cols)] = newvec.astype(jnp.bfloat16)
            res_out[slots[d], :, pl.ds(at, cols)] = res.astype(jnp.bfloat16)


def per_device(
    psi, left_ops, right_ops, term_shift, slot_sector, sector_width, diag_left, diag_right
):
    n_blk, n_op = lax.axis_size("blk"), lax.axis_size("op")
    _, rows, ncols = psi.shape
    terms, _, width, _ = right_ops.shape
    cols = diag_right.shape[0] // n_op
    step = rows // n_op
    count = float(n_blk * rows * ncols)
    n_dev = n_blk * n_op
    bf16, f32 = jnp.bfloat16, jnp.float32

    def pack(after):
        given = lax.optimization_barrier((term_shift, psi, right_ops, after))
        sent = kernel(
            functools.partial(pack_body, n_blk, n_op),
            list(zip(given, (SMEM, HBM, HBM))),
            [((rows, cols), bf16, VMEM)] * n_blk + [((terms * width + 16, cols), bf16, VMEM)] * n_op,
            [pltpu.VMEM(right_ops.shape, bf16), pltpu.SemaphoreType.DMA((n_blk + 1,))],
            nbytes=1 << 20,
        )
        return sent[:n_blk], sent[n_blk:]

    def table(right):
        return kernel(
            functools.partial(table_body, n_blk, n_op, terms),
            [(slot_sector, SMEM), (sector_width, SMEM), (diag_left, VMEM), (diag_right[None], VMEM)]
            + [(block, VMEM) for block in right],
            [((n_blk * n_op * terms,), jnp.int32, SMEM)]
            + [((n_blk,), jnp.int32, SMEM)] * 2
            + [((n_blk, rows, cols), f32, VMEM)],
        )

    def early(left, psi, n_early, tables):
        outs = [
            ((n_early, n_op * terms, rows, cols), bf16, VMEM),
            ((n_early, n_op, terms, rows, rows), bf16, HBM),
        ]
        return kernel(
            functools.partial(early_body, n_early, n_op),
            [(tables[1], SMEM)]
            + [(left[d, e], VMEM) for d in range(n_early) for e in range(n_op)]
            + [(psi[d], VMEM) for d in range(n_early)],
            outs,
            [pltpu.SemaphoreType.DMA((n_early * n_op,))],
            flops=2 * n_early * rows * rows * cols * terms * n_op,
            nbytes=8 << 20,
        )

    left, psi_by, right, (src, widths, slots, dmat), (inter_early, left_early) = gather(
        left_ops[:, 0], n_blk, n_op, pack, table, early
    )
    n_early = inter_early.shape[0]
    n_late = n_blk - n_early
    left_ins = [(left[d, e], VMEM) for d in range(n_early, n_blk) for e in range(n_op)]
    right_ins = [(block, VMEM) for block in right]
    psi_ins = [(block, VMEM) for block in psi_by]

    tables = [(src, SMEM), (widths, SMEM)]
    wide = ((n_blk, rows, cols), f32, VMEM)
    narrow = ((n_blk, rows, cols), bf16, VMEM)
    dots = ((n_dev, 8, LANES), f32, VMEM)
    sends = [((2, n_blk, step, cols), bf16, VMEM)] * (n_op - 1)
    inter = pltpu.VMEM((n_blk + 1, n_op * terms, rows, cols), bf16)
    left_late = (n_late, n_op, terms, rows, rows)
    flops = 2 * n_blk * rows * cols * terms * n_op * (rows + cols)
    cost = dict(flops=flops, nbytes=8 << 20)

    def totals(parts):
        return lax.all_to_all(parts, ("blk", "op"), 0, 0, tiled=True)

    sig, raw, dots1, kept, *out1 = kernel(
        functools.partial(first_body, n_blk, n_op, n_early),
        tables + left_ins + right_ins + psi_ins + [(dmat, VMEM), (inter_early, VMEM)],
        [wide, narrow, dots, (left_late, bf16, HBM)] + sends,
        [inter, pltpu.SemaphoreType.DMA((n_late * n_op + 1,))],
        **cost,
    )
    parts1 = totals(dots1)
    got1 = [swap(block, e, n_op) for e, block in enumerate(out1, 1)]
    fld, img, dots2, *out2 = kernel(
        functools.partial(second_body, n_blk, n_op, count),
        tables + [(left_early, HBM), (kept, HBM)] + right_ins + [(x, VMEM) for x in (parts1, raw, sig, dmat)],
        [narrow, wide, dots] + sends,
        [inter, pltpu.VMEM((n_blk, rows, cols), f32), pltpu.VMEM((n_blk, *left_late[1:]), bf16), pltpu.SemaphoreType.DMA((n_blk,))],
        **cost,
    )
    parts2 = totals(dots2)
    got2 = [swap(block, e, n_op) for e, block in enumerate(out2, 1)]
    final = ((n_blk, step, n_op * cols), bf16, VMEM)
    new, res, energy = kernel(
        functools.partial(third_body, n_blk, n_op, count),
        [(slots, SMEM)]
        + [(x, VMEM) for x in (parts1, parts2, raw, sig, fld, img, *got1, *got2)],
        [final, final, ((1,), f32, SMEM)],
        nbytes=4 << 20,
    )
    return new, res, energy


def solution(mesh):
    placed = (
        P(("grp", "blk"), None, None),
        P("op", ("grp", "blk"), None, None),
        P("op", ("grp", "blk"), None, None),
        P("op"),
        P("grp"),
        P("grp"),
        P("grp", None),
        P(("grp", "blk")),
    )

    def body(*args):
        psi, left_ops, right_ops, diag_right = args[0], args[1], args[2], args[7]
        n_op = mesh.shape["op"]
        cols = diag_right.shape[0] // n_op
        fits = (
            psi.shape[0] == 1
            and diag_right.shape[0] % n_op == 0
            and cols % LANES == 0
            and cols % right_ops.shape[2] == 0
            and cols // right_ops.shape[2] * n_op == right_ops.shape[1]
            and psi.shape[1] % (16 * n_op) == 0
            and n_op & (n_op - 1) == 0
            and mesh.shape["blk"] >= n_op.bit_length()
        )
        return (per_device if fits else per_device_general)(*args)

    return jax.shard_map(
        body,
        mesh=mesh,
        in_specs=placed,
        out_specs=(P("grp", "op", "blk"), P("grp", "op", "blk"), P("grp")),
        check_vma=False,
    )
```

```python
import functools

import jax
import jax.numpy as jnp
from jax import lax
from jax.experimental import pallas as pl
from jax.experimental.pallas import tpu as pltpu
from jax.sharding import PartitionSpec as P

EPS = 1e-06
LANES = 128
VMEM_LIMIT = 20 * 1024 * 1024


def per_device_general(
    psi, left_ops, right_ops, term_shift, slot_sector, sector_width, diag_left, diag_right
):
    sec_dev, rows, ncols = psi.shape
    nsec = slot_sector.shape[0]
    terms_dev = left_ops.shape[0]
    right_local = right_ops.shape[1]
    right_width = right_ops.shape[2]
    local_cols = diag_right.shape[0]
    count = float(nsec * rows * ncols)
    match = slot_sector[:, None] == jnp.arange(nsec)[None, :]
    widths = jnp.sum(jnp.where(match, sector_width[None, :], 0), axis=1)
    mask_all = (jnp.arange(rows)[None, :] < widths[:, None]).astype(jnp.float32)
    own_mask = lax.dynamic_slice_in_dim(mask_all, lax.axis_index("blk") * sec_dev, sec_dev, 0)
    raw = psi.astype(jnp.float32) * own_mask[:, :, None]
    squares = lax.psum(jnp.sum(raw * raw), "blk")
    v_left = (raw * lax.rsqrt(squares / count + EPS)).astype(jnp.bfloat16)
    onehots = (
        slot_sector[None, None, :] == slot_sector[None, :, None] - term_shift[:, None, None]
    ).astype(jnp.bfloat16)
    op_rows = rows // lax.axis_size("op")
    op_start = lax.axis_index("op") * op_rows
    dmat = diag_left[:, :, None] + diag_right[None, None, :]

    def left_local(field):
        return jnp.einsum(
            "ksij,sjc->ksic", left_ops, field, preferred_element_type=jnp.float32
        ).astype(jnp.bfloat16)

    def right_part(moved_in):
        flat = moved_in.reshape(terms_dev, nsec, rows * local_cols)
        shifted = jnp.einsum(
            "kts,ksx->ktx", onehots, flat, preferred_element_type=jnp.float32
        ).astype(jnp.bfloat16)
        shifted = shifted.reshape(terms_dev, nsec, rows, right_local, right_width)
        accum = jnp.einsum(
            "ktwrc,krdc->twrd", shifted, right_ops, preferred_element_type=jnp.float32
        )
        return accum.reshape(nsec, rows, local_cols) * mask_all[:, :, None]

    def op_total(partial_value):
        return lax.psum(partial_value.astype(jnp.bfloat16), "op").astype(jnp.float32)

    def final_rows(array):
        return lax.dynamic_slice_in_dim(array, op_start, op_rows, 1)

    def reduce_dots(values):
        sums = lax.psum(values, "blk")
        return tuple((item / count for item in sums))

    moved_first, v_moved = (
        lax.all_to_all(left_local(v_left), "blk", split_axis=3, concat_axis=1, tiled=True),
        lax.all_to_all(v_left[None], "blk", split_axis=3, concat_axis=1, tiled=True),
    )
    v_right = v_moved[0]
    vec32 = v_right.astype(jnp.float32)
    first_sigma = op_total(right_part(moved_first)) + dmat * vec32
    theta = reduce_dots((jnp.sum(vec32 * first_sigma),))[0]
    resid = first_sigma - theta * vec32
    den = dmat - theta
    corr = resid * den / jnp.maximum(den * den, 0.25)
    along = reduce_dots((jnp.sum(vec32 * corr),))[0]
    orth = corr - along * vec32
    norm_sq = reduce_dots((jnp.sum(orth * orth),))[0]
    update = (orth * lax.rsqrt(norm_sq + EPS)).astype(jnp.bfloat16)
    upd32 = update.astype(jnp.float32)
    upd_left = lax.all_to_all(update, "blk", split_axis=0, concat_axis=2, tiled=True)
    moved_second = lax.all_to_all(
        left_local(upd_left), "blk", split_axis=3, concat_axis=1, tiled=True
    )
    second_sigma = op_total(right_part(moved_second)) + dmat * upd32
    v_s1, u_s0, u_s1 = reduce_dots(
        (jnp.sum(vec32 * second_sigma), jnp.sum(upd32 * first_sigma), jnp.sum(upd32 * second_sigma))
    )
    h_mix = 0.5 * (v_s1 + u_s0)
    coef_v, coef_u, energy = ritz(theta, h_mix, u_s1)
    newvec = coef_v * vec32 + coef_u * upd32
    image = coef_v * first_sigma + coef_u * second_sigma
    new_out = final_rows(newvec.astype(jnp.bfloat16))
    res_out = final_rows((image - energy * newvec).astype(jnp.bfloat16))
    return (new_out, res_out, jnp.reshape(energy, (1,)))


def ritz(theta, h_mix, h_two):
    angle = 0.5 * jnp.arctan2(2.0 * h_mix, theta - h_two)
    sine = jnp.sin(angle)
    flip = jnp.where(sine > 0, -1.0, 1.0)
    coef_v = -sine * flip
    coef_u = jnp.cos(angle) * flip
    half = 0.5 * (theta - h_two)
    energy = 0.5 * (theta + h_two) - jnp.sqrt(half * half + h_mix * h_mix)
    return coef_v, coef_u, energy


VMEM, SMEM, HBM = pltpu.VMEM, pltpu.SMEM, pltpu.HBM


def kernel(body, ins, outs, scratch=(), flops=0, nbytes=0):
    return pl.pallas_call(
        body,
        out_shape=[
            HBM(shape, dtype) if space == HBM else jax.ShapeDtypeStruct(shape, dtype)
            for shape, dtype, space in outs
        ],
        in_specs=[pl.BlockSpec(memory_space=space) for _, space in ins],
        out_specs=[pl.BlockSpec(memory_space=space) for _, _, space in outs],
        scratch_shapes=list(scratch),
        compiler_params=pltpu.CompilerParams(vmem_limit_bytes=VMEM_LIMIT),
        cost_estimate=pl.CostEstimate(flops=flops, bytes_accessed=nbytes, transcendentals=0),
    )(*[pltpu.with_memory_space_constraint(x, HBM) if space == HBM else x for x, space in ins])


def ring_at(place, n_blk):
    place = place % n_blk if isinstance(place, int) else lax.rem(place + n_blk, n_blk)
    odd, even = 2 * place - 1, 2 * (n_blk - place)
    if isinstance(place, int):
        return 0 if place == 0 else odd if odd < n_blk else even
    return jnp.where(place == 0, 0, jnp.where(odd < n_blk, odd, even))


def ring_place(index, n_blk):
    odd, even = (index + 1) // 2, lax.rem(n_blk - index // 2, n_blk)
    return jnp.where(lax.rem(index, 2) == 1, odd, even)


def onward(block, d, n_blk):
    pairs = [(ring_at(i, n_blk), ring_at(i + d, n_blk)) for i in range(n_blk)]
    return lax.ppermute(block, "blk", pairs)


def swap(block, e, n_op):
    return lax.ppermute(block, "op", [(i, i ^ e) for i in range(n_op)])


def gather(own, n_blk, n_op, pack, table):
    bits = [1 << b for b in reversed(range(1, n_op.bit_length() - 1))]
    order = sorted(range(1, n_blk), key=lambda d: min(d, n_blk - d))
    left, psi, right, tables, columns = {(0, 0): own}, {}, None, None, None
    waiting, late = {(0, 0): 0}, None
    for j in range(n_blk + len(bits)):
        new, moved = {}, {}
        for (d, e), done in waiting.items():
            if e == 0 and d + 1 < n_blk:
                new[d + 1, 0] = onward(left[d, 0], 1, n_blk), 0
            for b in range(done, len(bits)):
                new[d, e ^ bits[b]] = swap(left[d, e], bits[b], n_op), b + 1
        kept = {key: block for key, (block, _) in new.items()}
        if late is not None:
            moved["psi"] = late
        if j == 0:
            columns, packed = pack()
            moved["right"] = [packed[0]]
            moved["right"] += [swap(part, 2 * e, n_op) for e, part in enumerate(packed[1:], 1)]
        if j == 1:
            moved["tables"] = table(right)
        if 2 <= j < n_blk:
            moved["other"] = swap(psi[order[j - 2]][0], 1, n_op)
        late = onward(columns[order[j]], order[j], n_blk) if j < n_blk - 1 else None
        if not kept and not moved:
            break
        waiting = {key: done for key, (_, done) in new.items()}
        kept, moved = lax.optimization_barrier((kept, moved))
        left.update(kept)
        right, tables = moved.get("right", right), moved.get("tables", tables)
        if "psi" in moved:
            psi[order[j - 1]] = [moved["psi"]]
        if "other" in moved:
            psi[order[j - 2]].append(moved["other"])
    psi[0] = [columns[0]]
    return left, psi, right, tables


def place_of():
    return lax.axis_index("blk"), lax.axis_index("op")


def pack_body(n_blk, n_op, shift, _, psi, right_in, *outs):
    n_pair = n_op // 2
    psi_out, right_out, right, sems = outs[:n_blk], outs[n_blk : n_blk + n_pair], outs[-2], outs[-1]
    terms, local, width, _ = right.shape
    cols = local * width // n_op
    per = cols // width
    own_blk, own_op = place_of()
    fetch = pltpu.make_async_copy(right_in, right, sems.at[2 * n_blk])
    fetch.start()
    copies = []
    for d in range(n_blk):
        there = ring_at(ring_place(own_blk, n_blk) + d, n_blk) * n_op
        for h in range(psi_out[d].shape[1] // cols):
            start = pl.multiple_of((there + (own_op ^ h)) * cols, LANES)
            copy = pltpu.make_async_copy(
                psi.at[0, :, pl.ds(start, cols)],
                psi_out[d].at[:, h * cols : (h + 1) * cols],
                sems.at[2 * d + h],
            )
            copy.start()
            copies.append(copy)
    lane = lax.broadcasted_iota(jnp.int32, (16, 2 * cols), 1)
    line = jnp.zeros((16, 2 * cols), jnp.float32)
    for k in range(terms):
        line = jnp.where(lane == k, shift[k].astype(jnp.float32), line)
    square = [lax.broadcasted_iota(jnp.int32, (width, width), axis) for axis in (0, 1)]
    unit = (square[0] == square[1]).astype(jnp.bfloat16)
    fetch.wait()
    for e in range(n_pair):
        for k in range(terms):
            turned = []
            for h in range(2):
                first = (own_op ^ (2 * e) ^ h) * per
                for r in range(per):
                    turned.append(
                        lax.dot_general(
                            right[k, first + r], unit, (((0,), (0,)), ((), ())),
                            preferred_element_type=jnp.float32,
                        )
                    )
            side_by_side = jnp.concatenate(turned, axis=1).astype(jnp.bfloat16)
            right_out[e][k * width : (k + 1) * width] = side_by_side
        right_out[e][terms * width :] = line.astype(jnp.bfloat16)
    for copy in copies:
        copy.wait()


def table_body(n_blk, terms, sector, width, left_diag, *refs):
    tails, src, widths, slots, diag = refs[:-4], *refs[-4:]
    n_pair = len(tails)
    rows, cols = tails[0].shape
    own_blk, _ = place_of()
    lane = lax.broadcasted_iota(jnp.int32, (16, cols), 1)
    for d in range(n_blk):
        slot = ring_at(ring_place(own_blk, n_blk) - d, n_blk)
        slots[d] = slot
        widths[d] = width[sector[slot]]
    for e in range(n_pair):
        tail = tails[e][rows - 16 :].astype(jnp.float32)
        for k in range(terms):
            shift = jnp.max(jnp.where(lane == k, tail, -1e9)).astype(jnp.int32)
            for t in range(n_blk):
                want = sector[slots[t]] - shift
                found = jnp.int32(n_blk)
                for d in range(n_blk):
                    found = jnp.where(sector[slots[d]] == want, d, found)
                src[(t * n_pair + e) * terms + k] = found
    for d in range(n_blk):
        row = left_diag[pl.ds(slots[d], 1), :]
        diag[d] = jnp.transpose(jnp.broadcast_to(row, (diag.shape[2], row.shape[1])))


def diagonal(diag, right_diag, d, h):
    cols = diag.shape[2]
    _, own_op = place_of()
    start = pl.multiple_of((own_op ^ h) * cols, LANES)
    return diag[d] + right_diag[:, pl.ds(start, cols)]


def row_mask(width, shape):
    return lax.broadcasted_iota(jnp.int32, shape, 0) < width


def fold(x):
    return jnp.sum(x.reshape(-1, 8, x.shape[-1]), axis=0)


def whole(x):
    return jnp.sum(jnp.sum(x, axis=0, keepdims=True), axis=1, keepdims=True)


def spread(values, out):
    line = lax.broadcasted_iota(jnp.int32, out.shape[1:], 0)
    tile = jnp.zeros(out.shape[1:], jnp.float32)
    for j, value in enumerate(values):
        tile = jnp.where(line == j, value, tile)
    for d in range(out.shape[0]):
        out[d] = tile


def by_block(packed, terms, k):
    rows, cols = packed.shape
    width = (rows - 16) // terms
    lane = lax.broadcasted_iota(jnp.int32, (width, cols), 1)
    block = packed[k * width : (k + 1) * width].astype(jnp.float32)
    parts = []
    for r in range(cols // width):
        inside = (lane >= r * width) & (lane < (r + 1) * width)
        parts.append(jnp.where(inside, block, 0.0).astype(jnp.bfloat16))
    return jnp.concatenate(parts, axis=0)


def left_products(block, left, inter):
    n_terms, rows, cols = inter.shape
    at = 0
    while at < n_terms:
        ops = left(at)
        terms = ops.shape[0]
        prod = jnp.dot(ops.reshape(terms * rows, rows), block, preferred_element_type=jnp.float32)
        inter[at : at + terms] = prod.astype(jnp.bfloat16).reshape(terms, rows, cols)
        at += terms


def sum_terms(src, widths, inter, right, out):
    n_blk, n_terms, _, _ = inter.shape
    n_blk -= 1
    terms = n_terms // len(right)
    turned = [by_block(right[j // terms], terms, j % terms) for j in range(n_terms)]
    for t in range(n_blk):
        total = None
        for j in range(n_terms):
            part = jnp.dot(
                inter[src[t * n_terms + j], j], turned[j], preferred_element_type=jnp.float32
            )
            total = part if total is None else total + part
        out[t] = jnp.where(row_mask(widths[t], total.shape), total, 0.0).astype(jnp.bfloat16)


def first_body(n_blk, n_pair, src, widths, *refs):
    left = [refs[d * n_pair : (d + 1) * n_pair] for d in range(n_blk)]
    refs = refs[n_blk * n_pair :]
    right, refs = refs[:n_pair], refs[n_pair:]
    psi, part_out, raw_out, left_out, inter, sems = refs[:-5], *refs[-5:]
    copies = []
    for d in range(n_blk):
        for e in range(n_pair):
            copies.append(
                pltpu.make_async_copy(left[d][e], left_out.at[d, e], sems.at[d * n_pair + e])
            )
            copies[-1].start()
    inter[n_blk] = jnp.zeros_like(inter[n_blk])
    cols = raw_out.shape[2] // 2
    for d in range(n_blk):
        at = 0
        while at < 2 * cols:
            block = psi[0][...].astype(jnp.float32)
            psi = psi[1:]
            block = jnp.where(row_mask(widths[d], block.shape), block, 0.0)
            raw_out[d, :, at : at + block.shape[1]] = block.astype(jnp.bfloat16)
            at += block.shape[1]
        terms = left[d][0].shape[0]
        left_products(raw_out[d], lambda at: left[d][at // terms][...], inter.at[d])
    sum_terms(src, widths, inter, right, part_out)
    for copy in copies:
        copy.wait()


def send_rows(sends, j, d, h, block):
    _, own_op = place_of()
    step, cols = sends[0].shape[2], block.shape[1]
    for e, send in enumerate(sends):
        start = pl.multiple_of((own_op ^ (2 * e)) * step, step)
        send[j, d, :, h * cols : (h + 1) * cols] = block[pl.ds(start, step)].astype(send.dtype)


def total_of(mine, other, d, h, cols):
    own = mine[d, :, h * cols : (h + 1) * cols].astype(jnp.float32)
    return own + other[d, :, (1 - h) * cols : (2 - h) * cols].astype(jnp.float32)


def sigma_body(mine, other, raw_in, diag, right_diag, sig_out, dots_out, *sends):
    n_blk, _, cols = diag.shape
    sums = [jnp.zeros((8, cols), jnp.float32) for _ in range(2)]
    for d in range(n_blk):
        for h in range(2):
            part = slice(h * cols, (h + 1) * cols)
            raw = raw_in[d, :, part].astype(jnp.float32)
            sigma = total_of(mine, other, d, h, cols) + diagonal(diag, right_diag, d, h) * raw
            sig_out[d, :, part] = sigma
            if h == 0:
                sums = [sums[0] + fold(raw * raw), sums[1] + fold(raw * sigma)]
    for d in range(n_blk):
        for h in range(2):
            send_rows(sends, 0, d, h, raw_in.at[d, :, h * cols : (h + 1) * cols])
            send_rows(sends, 1, d, h, sig_out.at[d, :, h * cols : (h + 1) * cols])
    spread([whole(x) for x in sums], dots_out)


def norm_theta(parts, count):
    tot = jnp.sum(parts, axis=0) * (1.0 / count)
    scale = lax.rsqrt(tot[0:1] + EPS)
    return scale, tot[1:2] * scale * scale


def second_body(n_blk, n_pair, count, src, widths, left_in, *refs):
    right, refs = refs[:n_pair], refs[n_pair:]
    parts, raw_in, sig_in, diag, right_diag, f_out, part_out, half_out = refs[:8]
    inter, corr, held, sems = refs[8:]
    copies = []
    for d in range(n_blk):
        copies.append(pltpu.make_async_copy(left_in.at[d], held.at[d], sems.at[d]))
        copies[-1].start()
    inter[n_blk] = jnp.zeros_like(inter[n_blk])
    scale, theta = norm_theta(parts[...], count)
    cols = diag.shape[2]
    halves = []
    for h in range(2):
        part = slice(h * cols, (h + 1) * cols)
        vv = vc = vs = jnp.zeros((8, cols), jnp.float32)
        for d in range(n_blk):
            vec = raw_in[d, :, part].astype(jnp.float32) * scale
            sigma = sig_in[d, :, part] * scale
            den = diagonal(diag, right_diag, d, h) - theta
            item = (sigma - theta * vec) * den / jnp.maximum(den * den, 0.25)
            corr[d, :, part] = item
            vv, vc, vs = vv + fold(vec * vec), vc + fold(vec * item), vs + fold(vec * sigma)
        halves.append((whole(vv), whole(vc), whole(vs)))
    along = (halves[0][1] + halves[1][1]) / jnp.maximum(halves[0][0] + halves[1][0], 1e-30)
    terms = held.shape[2]
    for d in range(n_blk):
        for h in range(2):
            part = slice(h * cols, (h + 1) * cols)
            vec = raw_in[d, :, part].astype(jnp.float32) * scale
            f_out[d, :, part] = (corr[d, :, part] - along * vec).astype(jnp.bfloat16)
        copies[d].wait()
        left_products(f_out[d], lambda at: held[d, at // terms], inter.at[d])
    sum_terms(src, widths, inter, right, part_out)
    spread(halves[0] + (along,), half_out)


def image_body(count, half, parts, mine, other, raw_in, sig_in, f_in, diag, right_diag, dots_out, *sends):
    n_blk, _, cols = diag.shape
    scale, _ = norm_theta(parts[...], count)
    sums = [jnp.zeros((8, cols), jnp.float32) for _ in range(5)]
    for d in range(n_blk):
        for h in range(2):
            part = slice(h * cols, (h + 1) * cols)
            fld = f_in[d, :, part].astype(jnp.float32)
            image = total_of(mine, other, d, h, cols) + diagonal(diag, right_diag, d, h) * fld
            sends[-1][h] = image
            send_rows(sends[:-1], 0, d, h, f_in.at[d, :, part])
            send_rows(sends[:-1], 1, d, h, sends[-1].at[h])
            if h == 0:
                vec = raw_in[d, :, part].astype(jnp.float32) * scale
                sigma = sig_in[d, :, part] * scale
                prods = (fld * fld, vec * fld, vec * image, fld * sigma, fld * image)
                sums = [one + fold(prod) for one, prod in zip(sums, prods)]
    known = [half[0, j : j + 1] for j in range(4)]
    spread(known + [whole(x) for x in sums], dots_out)


def ritz_pair(theta, h_mix, h_two):
    diff, twice = theta - h_two, 2.0 * h_mix
    size = jnp.sqrt(diff * diff + twice * twice)
    some = size > 0.0
    safe = jnp.where(some, size, 1.0)
    big = jnp.sqrt(0.5 + 0.5 * jnp.abs(diff) / safe)
    small = 0.5 * jnp.abs(twice) / (safe * big)
    sine = jnp.where(diff >= 0.0, small, big)
    cosine = jnp.where(diff >= 0.0, big, small)
    sine = jnp.where(some, sine, 0.0)
    cosine = jnp.where(some, cosine, 1.0)
    upward = (twice > 0.0) | ((twice == 0.0) & (diff < 0.0))
    return sine, jnp.where(upward, -cosine, cosine), 0.5 * (theta + h_two) - 0.5 * size


def third_body(n_blk, n_op, count, slots, parts1, parts2, *refs):
    n_pair = n_op // 2
    got1, got2 = refs[:n_pair], refs[n_pair : 2 * n_pair]
    new_out, res_out, energy_out = refs[2 * n_pair :]
    cols = new_out.shape[2] // n_op
    own_blk, own_op = place_of()
    scale, theta = norm_theta(parts1[...], count)
    vv, vc, vs, local, ff, vf, vt, fs, ft = (parts2[:, j, :] for j in range(9))

    def mean(x):
        return jnp.sum(x, axis=0, keepdims=True) * (1.0 / count)

    along = mean(vc)
    beta = local - along
    norm_sq = mean(ff + 2.0 * beta * vf + beta * beta * vv)
    unit = lax.rsqrt(jnp.maximum(norm_sq, 0.0) + EPS)
    v_s1 = unit * mean(vt + beta * vs)
    u_s0 = unit * mean(fs + beta * vs)
    u_s1 = unit * unit * mean(ft + beta * (vt + fs) + beta * beta * vs)
    cv, cu, energy = ritz_pair(theta, 0.5 * (v_s1 + u_s0), u_s1)
    energy_out[0] = jnp.max(energy)
    cu = cu * unit
    for e in range(n_pair):
        there = own_op ^ (2 * e)
        back = parts2[own_blk * n_op + there][3:4] - along
        on_vec = (cv + cu * back) * scale
        for h in range(2):
            at = pl.multiple_of((there ^ h) * cols, LANES)
            part = slice(h * cols, (h + 1) * cols)
            for d in range(n_blk):
                blocks = (got[e][j, d, :, part] for got in (got1, got2) for j in range(2))
                raw, sigma, fld, image = (block.astype(jnp.float32) for block in blocks)
                newvec = on_vec * raw + cu * fld
                res = on_vec * sigma + cu * image - energy * newvec
                new_out[slots[d], :, pl.ds(at, cols)] = newvec.astype(jnp.bfloat16)
                res_out[slots[d], :, pl.ds(at, cols)] = res.astype(jnp.bfloat16)


def per_device(
    psi, left_ops, right_ops, term_shift, slot_sector, sector_width, diag_left, diag_right
):
    n_blk, n_op = lax.axis_size("blk"), lax.axis_size("op")
    _, rows, ncols = psi.shape
    terms, _, width, _ = right_ops.shape
    n_pair = n_op // 2
    cols = diag_right.shape[0] // n_op
    step = rows // n_op
    count = float(n_blk * rows * ncols)
    n_dev = n_blk * n_op
    bf16, f32, i32 = jnp.bfloat16, jnp.float32, jnp.int32
    last = sorted(range(1, n_blk), key=lambda d: min(d, n_blk - d))[-1]

    def pack():
        first = swap(term_shift, 1, n_op)
        sent = kernel(
            functools.partial(pack_body, n_blk, n_op),
            [(term_shift, SMEM), (first, SMEM), (psi, HBM), (right_ops, HBM)],
            [((rows, 2 * cols if d in (0, last) else cols), bf16, VMEM) for d in range(n_blk)]
            + [((terms * width + 16, 2 * cols), bf16, VMEM)] * n_pair,
            [pltpu.VMEM(right_ops.shape, bf16), pltpu.SemaphoreType.DMA((2 * n_blk + 1,))],
            nbytes=1 << 20,
        )
        return sent[:n_blk], sent[n_blk:]

    def table(right):
        return kernel(
            functools.partial(table_body, n_blk, terms),
            [(slot_sector, SMEM), (sector_width, SMEM), (diag_left, VMEM)]
            + [(block, VMEM) for block in right],
            [((n_blk * n_pair * terms,), i32, SMEM)]
            + [((n_blk,), i32, SMEM)] * 2
            + [((n_blk, rows, LANES), f32, VMEM)],
        )

    left, psi_by, right, (src, widths, slots, diag) = gather(left_ops[:, 0], n_blk, n_op, pack, table)
    left_ins = [(left[d, 2 * e], VMEM) for d in range(n_blk) for e in range(n_pair)]
    right_ins = [(block, VMEM) for block in right]
    psi_ins = [(block, VMEM) for d in range(n_blk) for block in psi_by[d]]
    diags = [(diag, VMEM), (diag_right[None], VMEM)]

    tables = [(src, SMEM), (widths, SMEM)]
    narrow = ((n_blk, rows, 2 * cols), bf16, VMEM)
    wide = ((n_blk, rows, 2 * cols), f32, VMEM)
    sends = [((2, n_blk, step, 2 * cols), bf16, VMEM)] * n_pair
    inter = pltpu.VMEM((n_blk + 1, n_pair * terms, rows, 2 * cols), bf16)
    left_all = (n_blk, n_pair, terms, rows, rows)
    cost = dict(flops=2 * n_blk * rows * 2 * cols * terms * n_pair * (rows + 2 * cols), nbytes=6 << 20)

    def totals(parts):
        return lax.all_to_all(parts, ("blk", "op"), 0, 0, tiled=True)

    def exchange(out):
        return [out[0]] + [swap(block, 2 * e, n_op) for e, block in enumerate(out[1:], 1)]

    part1, raw, kept = kernel(
        functools.partial(first_body, n_blk, n_pair),
        tables + left_ins + right_ins + psi_ins,
        [narrow, narrow, (left_all, bf16, HBM)],
        [inter, pltpu.SemaphoreType.DMA((n_blk * n_pair,))],
        **cost,
    )
    sig, dots1, *out1 = kernel(
        sigma_body,
        [(x, VMEM) for x in (part1, swap(part1, 1, n_op), raw)] + diags,
        [wide, ((n_dev, 8, LANES), f32, VMEM)] + sends,
        nbytes=4 << 20,
    )
    parts1 = totals(dots1)
    got1 = exchange(out1)
    fld, part2, half = kernel(
        functools.partial(second_body, n_blk, n_pair, count),
        tables + [(kept, HBM)] + right_ins + [(x, VMEM) for x in (parts1, raw, sig)] + diags,
        [narrow, narrow, ((1, 8, LANES), f32, VMEM)],
        [
            inter,
            pltpu.VMEM((n_blk, rows, 2 * cols), f32),
            pltpu.VMEM(left_all, bf16),
            pltpu.SemaphoreType.DMA((n_blk,)),
        ],
        **cost,
    )
    dots2, *out2 = kernel(
        functools.partial(image_body, count),
        [(x, VMEM) for x in (half, parts1, part2, swap(part2, 1, n_op), raw, sig, fld)] + diags,
        [((n_dev, 16, LANES), f32, VMEM)] + sends,
        [pltpu.VMEM((2, rows, cols), f32)],
        nbytes=4 << 20,
    )
    parts2 = totals(dots2)
    got2 = exchange(out2)
    final = ((n_blk, step, n_op * cols), bf16, VMEM)
    new, res, energy = kernel(
        functools.partial(third_body, n_blk, n_op, count),
        [(slots, SMEM)] + [(x, VMEM) for x in (parts1, parts2, *got1, *got2)],
        [final, final, ((1,), f32, SMEM)],
        nbytes=4 << 20,
    )
    return new, res, energy


def solution(mesh):
    placed = (
        P(("grp", "blk"), None, None),
        P("op", ("grp", "blk"), None, None),
        P("op", ("grp", "blk"), None, None),
        P("op"),
        P("grp"),
        P("grp"),
        P("grp", None),
        P(("grp", "blk")),
    )

    def body(*args):
        psi, left_ops, right_ops, diag_right = args[0], args[1], args[2], args[7]
        n_op = mesh.shape["op"]
        cols = diag_right.shape[0] // n_op
        fits = (
            psi.shape[0] == 1
            and diag_right.shape[0] % n_op == 0
            and cols == LANES
            and n_op % 2 == 0
            and cols % right_ops.shape[2] == 0
            and cols // right_ops.shape[2] * n_op == right_ops.shape[1]
            and psi.shape[1] % (16 * n_op) == 0
            and n_op & (n_op - 1) == 0
            and mesh.shape["blk"] > 1
        )
        return (per_device if fits else per_device_general)(*args)

    return jax.shard_map(
        body,
        mesh=mesh,
        in_specs=placed,
        out_specs=(P("grp", "op", "blk"), P("grp", "op", "blk"), P("grp")),
        check_vma=False,
    )
```

```python
import functools

import jax
import jax.numpy as jnp
from jax import lax
from jax.experimental import pallas as pl
from jax.experimental.pallas import tpu as pltpu
from jax.sharding import PartitionSpec as P

EPS = 1e-06
LANES = 128
VMEM_LIMIT = 20 * 1024 * 1024


def per_device_general(
    psi, left_ops, right_ops, term_shift, slot_sector, sector_width, diag_left, diag_right
):
    sec_dev, rows, ncols = psi.shape
    nsec = slot_sector.shape[0]
    terms_dev = left_ops.shape[0]
    right_local = right_ops.shape[1]
    right_width = right_ops.shape[2]
    local_cols = diag_right.shape[0]
    count = float(nsec * rows * ncols)
    match = slot_sector[:, None] == jnp.arange(nsec)[None, :]
    widths = jnp.sum(jnp.where(match, sector_width[None, :], 0), axis=1)
    mask_all = (jnp.arange(rows)[None, :] < widths[:, None]).astype(jnp.float32)
    own_mask = lax.dynamic_slice_in_dim(mask_all, lax.axis_index("blk") * sec_dev, sec_dev, 0)
    raw = psi.astype(jnp.float32) * own_mask[:, :, None]
    squares = lax.psum(jnp.sum(raw * raw), "blk")
    v_left = (raw * lax.rsqrt(squares / count + EPS)).astype(jnp.bfloat16)
    onehots = (
        slot_sector[None, None, :] == slot_sector[None, :, None] - term_shift[:, None, None]
    ).astype(jnp.bfloat16)
    op_rows = rows // lax.axis_size("op")
    op_start = lax.axis_index("op") * op_rows
    dmat = diag_left[:, :, None] + diag_right[None, None, :]

    def left_local(field):
        return jnp.einsum(
            "ksij,sjc->ksic", left_ops, field, preferred_element_type=jnp.float32
        ).astype(jnp.bfloat16)

    def right_part(moved_in):
        flat = moved_in.reshape(terms_dev, nsec, rows * local_cols)
        shifted = jnp.einsum(
            "kts,ksx->ktx", onehots, flat, preferred_element_type=jnp.float32
        ).astype(jnp.bfloat16)
        shifted = shifted.reshape(terms_dev, nsec, rows, right_local, right_width)
        accum = jnp.einsum(
            "ktwrc,krdc->twrd", shifted, right_ops, preferred_element_type=jnp.float32
        )
        return accum.reshape(nsec, rows, local_cols) * mask_all[:, :, None]

    def op_total(partial_value):
        return lax.psum(partial_value.astype(jnp.bfloat16), "op").astype(jnp.float32)

    def final_rows(array):
        return lax.dynamic_slice_in_dim(array, op_start, op_rows, 1)

    def reduce_dots(values):
        sums = lax.psum(values, "blk")
        return tuple((item / count for item in sums))

    moved_first, v_moved = (
        lax.all_to_all(left_local(v_left), "blk", split_axis=3, concat_axis=1, tiled=True),
        lax.all_to_all(v_left[None], "blk", split_axis=3, concat_axis=1, tiled=True),
    )
    v_right = v_moved[0]
    vec32 = v_right.astype(jnp.float32)
    first_sigma = op_total(right_part(moved_first)) + dmat * vec32
    theta = reduce_dots((jnp.sum(vec32 * first_sigma),))[0]
    resid = first_sigma - theta * vec32
    den = dmat - theta
    corr = resid * den / jnp.maximum(den * den, 0.25)
    along = reduce_dots((jnp.sum(vec32 * corr),))[0]
    orth = corr - along * vec32
    norm_sq = reduce_dots((jnp.sum(orth * orth),))[0]
    update = (orth * lax.rsqrt(norm_sq + EPS)).astype(jnp.bfloat16)
    upd32 = update.astype(jnp.float32)
    upd_left = lax.all_to_all(update, "blk", split_axis=0, concat_axis=2, tiled=True)
    moved_second = lax.all_to_all(
        left_local(upd_left), "blk", split_axis=3, concat_axis=1, tiled=True
    )
    second_sigma = op_total(right_part(moved_second)) + dmat * upd32
    v_s1, u_s0, u_s1 = reduce_dots(
        (jnp.sum(vec32 * second_sigma), jnp.sum(upd32 * first_sigma), jnp.sum(upd32 * second_sigma))
    )
    h_mix = 0.5 * (v_s1 + u_s0)
    coef_v, coef_u, energy = ritz(theta, h_mix, u_s1)
    newvec = coef_v * vec32 + coef_u * upd32
    image = coef_v * first_sigma + coef_u * second_sigma
    new_out = final_rows(newvec.astype(jnp.bfloat16))
    res_out = final_rows((image - energy * newvec).astype(jnp.bfloat16))
    return (new_out, res_out, jnp.reshape(energy, (1,)))


def ritz(theta, h_mix, h_two):
    angle = 0.5 * jnp.arctan2(2.0 * h_mix, theta - h_two)
    sine = jnp.sin(angle)
    flip = jnp.where(sine > 0, -1.0, 1.0)
    coef_v = -sine * flip
    coef_u = jnp.cos(angle) * flip
    half = 0.5 * (theta - h_two)
    energy = 0.5 * (theta + h_two) - jnp.sqrt(half * half + h_mix * h_mix)
    return coef_v, coef_u, energy


VMEM, SMEM, HBM = pltpu.VMEM, pltpu.SMEM, pltpu.HBM


def kernel(body, ins, outs, scratch=(), flops=0, nbytes=0):
    return pl.pallas_call(
        body,
        out_shape=[
            HBM(shape, dtype) if space == HBM else jax.ShapeDtypeStruct(shape, dtype)
            for shape, dtype, space in outs
        ],
        in_specs=[pl.BlockSpec(memory_space=space) for _, space in ins],
        out_specs=[pl.BlockSpec(memory_space=space) for _, _, space in outs],
        scratch_shapes=list(scratch),
        compiler_params=pltpu.CompilerParams(vmem_limit_bytes=VMEM_LIMIT),
        cost_estimate=pl.CostEstimate(flops=flops, bytes_accessed=nbytes, transcendentals=0),
    )(*[pltpu.with_memory_space_constraint(x, HBM) if space == HBM else x for x, space in ins])


def ring_at(place, n_blk):
    place = place % n_blk if isinstance(place, int) else lax.rem(place + n_blk, n_blk)
    odd, even = 2 * place - 1, 2 * (n_blk - place)
    if isinstance(place, int):
        return 0 if place == 0 else odd if odd < n_blk else even
    return jnp.where(place == 0, 0, jnp.where(odd < n_blk, odd, even))


def ring_place(index, n_blk):
    odd, even = (index + 1) // 2, lax.rem(n_blk - index // 2, n_blk)
    return jnp.where(lax.rem(index, 2) == 1, odd, even)


def onward(block, d, n_blk):
    pairs = [(ring_at(i, n_blk), ring_at(i + d, n_blk)) for i in range(n_blk)]
    return lax.ppermute(block, "blk", pairs)


def swap(block, e, n_op):
    return lax.ppermute(block, "op", [(i, i ^ e) for i in range(n_op)])


def gather(own, n_blk, n_op, pack, table, early):
    bits = [1 << b for b in reversed(range(1, n_op.bit_length() - 1))]
    order = sorted(range(1, n_blk), key=lambda d: min(d, n_blk - d))
    left, psi, right, tables, columns = {(0, 0): own}, {}, None, None, None
    waiting, late, made = {(0, 0): 0}, None, None
    for j in range(n_blk + len(bits)):
        new, moved = {}, {}
        for (d, e), done in waiting.items():
            if e == 0 and d + 1 < n_blk:
                new[d + 1, 0] = onward(left[d, 0], 1, n_blk), 0
            for b in range(done, len(bits)):
                new[d, e ^ bits[b]] = swap(left[d, e], bits[b], n_op), b + 1
        kept = {key: block for key, (block, _) in new.items()}
        if late is not None:
            moved["psi"] = late
        if j == 0:
            columns, packed = pack()
            moved["right"] = [packed[0]]
            moved["right"] += [swap(part, 2 * e, n_op) for e, part in enumerate(packed[1:], 1)]
        if j == 1:
            moved["tables"] = table(right)
        if j == n_blk - 1 and j >= len(bits) + 1:
            n_early = min(2, n_blk - 1)
            psi[0] = [columns[0]]
            moved["early"] = early(left, psi, n_early, tables)
        if 2 <= j < n_blk:
            moved["other"] = swap(psi[order[j - 2]][0], 1, n_op)
        late = onward(columns[order[j]], order[j], n_blk) if j < n_blk - 1 else None
        if not kept and not moved:
            break
        waiting = {key: done for key, (_, done) in new.items()}
        kept, moved = lax.optimization_barrier((kept, moved))
        left.update(kept)
        right, tables = moved.get("right", right), moved.get("tables", tables)
        made = moved.get("early", made)
        if "psi" in moved:
            psi[order[j - 1]] = [moved["psi"]]
        if "other" in moved:
            psi[order[j - 2]].append(moved["other"])
    return left, psi, right, tables, made


def place_of():
    return lax.axis_index("blk"), lax.axis_index("op")


def pack_body(n_blk, n_op, shift, _, psi, right_in, *outs):
    n_pair = n_op // 2
    psi_out, right_out, right, sems = outs[:n_blk], outs[n_blk : n_blk + n_pair], outs[-2], outs[-1]
    terms, local, width, _ = right.shape
    cols = local * width // n_op
    per = cols // width
    own_blk, own_op = place_of()
    fetch = pltpu.make_async_copy(right_in, right, sems.at[2 * n_blk])
    fetch.start()
    copies = []
    for d in range(n_blk):
        there = ring_at(ring_place(own_blk, n_blk) + d, n_blk) * n_op
        for h in range(psi_out[d].shape[1] // cols):
            start = pl.multiple_of((there + (own_op ^ h)) * cols, LANES)
            copy = pltpu.make_async_copy(
                psi.at[0, :, pl.ds(start, cols)],
                psi_out[d].at[:, h * cols : (h + 1) * cols],
                sems.at[2 * d + h],
            )
            copy.start()
            copies.append(copy)
    lane = lax.broadcasted_iota(jnp.int32, (16, 2 * cols), 1)
    line = jnp.zeros((16, 2 * cols), jnp.float32)
    for k in range(terms):
        line = jnp.where(lane == k, shift[k].astype(jnp.float32), line)
    square = [lax.broadcasted_iota(jnp.int32, (width, width), axis) for axis in (0, 1)]
    unit = (square[0] == square[1]).astype(jnp.bfloat16)
    fetch.wait()
    for e in range(n_pair):
        for k in range(terms):
            turned = []
            for h in range(2):
                first = (own_op ^ (2 * e) ^ h) * per
                for r in range(per):
                    turned.append(
                        lax.dot_general(
                            right[k, first + r], unit, (((0,), (0,)), ((), ())),
                            preferred_element_type=jnp.float32,
                        )
                    )
            side_by_side = jnp.concatenate(turned, axis=1).astype(jnp.bfloat16)
            right_out[e][k * width : (k + 1) * width] = side_by_side
        right_out[e][terms * width :] = line.astype(jnp.bfloat16)
    for copy in copies:
        copy.wait()


def table_body(n_blk, terms, sector, width, left_diag, *refs):
    tails, src, widths, slots, diag = refs[:-4], *refs[-4:]
    n_pair = len(tails)
    rows, cols = tails[0].shape
    own_blk, _ = place_of()
    lane = lax.broadcasted_iota(jnp.int32, (16, cols), 1)
    for d in range(n_blk):
        slot = ring_at(ring_place(own_blk, n_blk) - d, n_blk)
        slots[d] = slot
        widths[d] = width[sector[slot]]
    for e in range(n_pair):
        tail = tails[e][rows - 16 :].astype(jnp.float32)
        for k in range(terms):
            shift = jnp.max(jnp.where(lane == k, tail, -1e9)).astype(jnp.int32)
            for t in range(n_blk):
                want = sector[slots[t]] - shift
                found = jnp.int32(n_blk)
                for d in range(n_blk):
                    found = jnp.where(sector[slots[d]] == want, d, found)
                src[(t * n_pair + e) * terms + k] = found
    for d in range(n_blk):
        row = left_diag[pl.ds(slots[d], 1), :]
        diag[d] = jnp.transpose(jnp.broadcast_to(row, (diag.shape[2], row.shape[1])))


def diagonal(diag, right_diag, d, h):
    cols = diag.shape[2]
    _, own_op = place_of()
    start = pl.multiple_of((own_op ^ h) * cols, LANES)
    return diag[d] + right_diag[:, pl.ds(start, cols)]


def row_mask(width, shape):
    return lax.broadcasted_iota(jnp.int32, shape, 0) < width


def fold(x):
    return jnp.sum(x.reshape(-1, 8, x.shape[-1]), axis=0)


def whole(x):
    return jnp.sum(jnp.sum(x, axis=0, keepdims=True), axis=1, keepdims=True)


def spread(values, out):
    line = lax.broadcasted_iota(jnp.int32, out.shape[1:], 0)
    tile = jnp.zeros(out.shape[1:], jnp.float32)
    for j, value in enumerate(values):
        tile = jnp.where(line == j, value, tile)
    for d in range(out.shape[0]):
        out[d] = tile


def by_block(packed, terms, k):
    rows, cols = packed.shape
    width = (rows - 16) // terms
    lane = lax.broadcasted_iota(jnp.int32, (width, cols), 1)
    block = packed[k * width : (k + 1) * width].astype(jnp.float32)
    parts = []
    for r in range(cols // width):
        inside = (lane >= r * width) & (lane < (r + 1) * width)
        parts.append(jnp.where(inside, block, 0.0).astype(jnp.bfloat16))
    return jnp.concatenate(parts, axis=0)


def left_products(block, left, inter):
    n_terms, rows, cols = inter.shape
    at = 0
    while at < n_terms:
        ops = left(at)
        terms = ops.shape[0]
        prod = jnp.dot(ops.reshape(terms * rows, rows), block, preferred_element_type=jnp.float32)
        inter[at : at + terms] = prod.astype(jnp.bfloat16).reshape(terms, rows, cols)
        at += terms


def sum_terms(src, widths, inter, right, out):
    n_blk, n_terms, _, _ = inter.shape
    n_blk -= 1
    terms = n_terms // len(right)
    turned = [by_block(right[j // terms], terms, j % terms) for j in range(n_terms)]
    for t in range(n_blk):
        total = None
        for j in range(n_terms):
            part = jnp.dot(
                inter[src[t * n_terms + j], j], turned[j], preferred_element_type=jnp.float32
            )
            total = part if total is None else total + part
        out[t] = jnp.where(row_mask(widths[t], total.shape), total, 0.0).astype(jnp.bfloat16)


def keep(left, left_out, sems):
    copies = []
    for d, line in enumerate(left):
        for e, ref in enumerate(line):
            copies.append(pltpu.make_async_copy(ref, left_out.at[d, e], sems.at[d * len(line) + e]))
            copies[-1].start()
    return copies


def masked(psi, width, out):
    at = 0
    for ref in psi:
        block = ref[...].astype(jnp.float32)
        block = jnp.where(row_mask(width, block.shape), block, 0.0)
        out[:, at : at + block.shape[1]] = block.astype(jnp.bfloat16)
        at += block.shape[1]


def take(refs, counts):
    out = []
    for count in counts:
        out.append(refs[:count])
        refs = refs[count:]
    return out, refs


def products_of(psi, left, widths, first, raw_out, inter):
    for d, line in enumerate(left):
        masked(psi[d], widths[first + d], raw_out.at[d])
        terms = line[0].shape[0]
        left_products(raw_out[d], lambda at: line[at // terms][...], inter.at[d])


def early_body(n_pair, counts, widths, *refs):
    left, refs = take(refs, [n_pair] * len(counts))
    psi, (raw_out, inter_out, left_out, sems) = take(refs, counts)
    copies = keep(left, left_out, sems)
    products_of(psi, left, widths, 0, raw_out, inter_out)
    for copy in copies:
        copy.wait()


def first_body(n_blk, n_pair, counts, src, widths, *refs):
    n_late = len(counts)
    n_early = n_blk - n_late
    left, refs = take(refs, [n_pair] * n_late)
    (right,), refs = take(refs, [n_pair])
    psi, (raw_in, inter_in, part_out, raw_out, left_out, inter, sems) = take(refs, counts)
    copies = keep(left, left_out, sems)
    for j, (given, own) in enumerate(((inter_in, inter), (raw_in, raw_out))):
        copies.append(
            pltpu.make_async_copy(given, own.at[:n_early], sems.at[n_late * n_pair + j])
        )
        copies[-1].start()
    inter[n_blk] = jnp.zeros_like(inter[n_blk])
    products_of(
        psi, left, widths, n_early, raw_out.at[n_early:], inter.at[n_early:n_blk]
    )
    for copy in copies:
        copy.wait()
    sum_terms(src, widths, inter, right, part_out)


def send_rows(sends, j, d, h, block):
    _, own_op = place_of()
    step, cols = sends[0].shape[2], block.shape[1]
    for e, send in enumerate(sends):
        start = pl.multiple_of((own_op ^ (2 * e)) * step, step)
        send[j, d, :, h * cols : (h + 1) * cols] = block[pl.ds(start, step)].astype(send.dtype)


def total_of(mine, other, d, h, cols):
    own = mine[d, :, h * cols : (h + 1) * cols].astype(jnp.float32)
    return own + other[d, :, (1 - h) * cols : (2 - h) * cols].astype(jnp.float32)


def sigma_body(mine, other, raw_in, diag, right_diag, sig_out, dots_out, *sends):
    n_blk, _, cols = diag.shape
    sums = [jnp.zeros((8, cols), jnp.float32) for _ in range(2)]
    for d in range(n_blk):
        for h in range(2):
            part = slice(h * cols, (h + 1) * cols)
            raw = raw_in[d, :, part].astype(jnp.float32)
            sigma = total_of(mine, other, d, h, cols) + diagonal(diag, right_diag, d, h) * raw
            sig_out[d, :, part] = sigma
            if h == 0:
                sums = [sums[0] + fold(raw * raw), sums[1] + fold(raw * sigma)]
    for d in range(n_blk):
        for h in range(2):
            send_rows(sends, 0, d, h, raw_in.at[d, :, h * cols : (h + 1) * cols])
            send_rows(sends, 1, d, h, sig_out.at[d, :, h * cols : (h + 1) * cols])
    spread([whole(x) for x in sums], dots_out)


def norm_theta(parts, count):
    tot = jnp.sum(parts, axis=0) * (1.0 / count)
    scale = lax.rsqrt(tot[0:1] + EPS)
    return scale, tot[1:2] * scale * scale


def second_body(n_blk, n_pair, count, src, widths, left_early, left_late, *refs):
    right, refs = refs[:n_pair], refs[n_pair:]
    parts, raw_in, sig_in, diag, right_diag, f_out, part_out, half_out = refs[:8]
    inter, corr, held, sems = refs[8:]
    copies = []
    n_early = left_early.shape[0]
    for d in range(n_blk):
        kept = left_early.at[d] if d < n_early else left_late.at[d - n_early]
        copies.append(pltpu.make_async_copy(kept, held.at[d], sems.at[d]))
        copies[-1].start()
    inter[n_blk] = jnp.zeros_like(inter[n_blk])
    scale, theta = norm_theta(parts[...], count)
    cols = diag.shape[2]
    halves = []
    for h in range(2):
        part = slice(h * cols, (h + 1) * cols)
        vv = vc = vs = jnp.zeros((8, cols), jnp.float32)
        for d in range(n_blk):
            vec = raw_in[d, :, part].astype(jnp.float32) * scale
            sigma = sig_in[d, :, part] * scale
            den = diagonal(diag, right_diag, d, h) - theta
            item = (sigma - theta * vec) * den / jnp.maximum(den * den, 0.25)
            corr[d, :, part] = item
            vv, vc, vs = vv + fold(vec * vec), vc + fold(vec * item), vs + fold(vec * sigma)
        halves.append((whole(vv), whole(vc), whole(vs)))
    along = (halves[0][1] + halves[1][1]) / jnp.maximum(halves[0][0] + halves[1][0], 1e-30)
    terms = held.shape[2]
    for d in range(n_blk):
        for h in range(2):
            part = slice(h * cols, (h + 1) * cols)
            vec = raw_in[d, :, part].astype(jnp.float32) * scale
            f_out[d, :, part] = (corr[d, :, part] - along * vec).astype(jnp.bfloat16)
        copies[d].wait()
        left_products(f_out[d], lambda at: held[d, at // terms], inter.at[d])
    sum_terms(src, widths, inter, right, part_out)
    spread(halves[0] + (along,), half_out)


def image_body(count, half, parts, mine, other, raw_in, sig_in, f_in, diag, right_diag, dots_out, *sends):
    n_blk, _, cols = diag.shape
    scale, _ = norm_theta(parts[...], count)
    sums = [jnp.zeros((8, cols), jnp.float32) for _ in range(5)]
    for d in range(n_blk):
        for h in range(2):
            part = slice(h * cols, (h + 1) * cols)
            fld = f_in[d, :, part].astype(jnp.float32)
            image = total_of(mine, other, d, h, cols) + diagonal(diag, right_diag, d, h) * fld
            sends[-1][h] = image
            send_rows(sends[:-1], 0, d, h, f_in.at[d, :, part])
            send_rows(sends[:-1], 1, d, h, sends[-1].at[h])
            if h == 0:
                vec = raw_in[d, :, part].astype(jnp.float32) * scale
                sigma = sig_in[d, :, part] * scale
                prods = (fld * fld, vec * fld, vec * image, fld * sigma, fld * image)
                sums = [one + fold(prod) for one, prod in zip(sums, prods)]
    known = [half[0, j : j + 1] for j in range(4)]
    spread(known + [whole(x) for x in sums], dots_out)


def ritz_pair(theta, h_mix, h_two):
    diff, twice = theta - h_two, 2.0 * h_mix
    size = jnp.sqrt(diff * diff + twice * twice)
    some = size > 0.0
    safe = jnp.where(some, size, 1.0)
    big = jnp.sqrt(0.5 + 0.5 * jnp.abs(diff) / safe)
    small = 0.5 * jnp.abs(twice) / (safe * big)
    sine = jnp.where(diff >= 0.0, small, big)
    cosine = jnp.where(diff >= 0.0, big, small)
    sine = jnp.where(some, sine, 0.0)
    cosine = jnp.where(some, cosine, 1.0)
    upward = (twice > 0.0) | ((twice == 0.0) & (diff < 0.0))
    return sine, jnp.where(upward, -cosine, cosine), 0.5 * (theta + h_two) - 0.5 * size


def third_body(n_blk, n_op, count, slots, parts1, parts2, *refs):
    n_pair = n_op // 2
    got1, got2 = refs[:n_pair], refs[n_pair : 2 * n_pair]
    new_out, res_out, energy_out = refs[2 * n_pair :]
    cols = new_out.shape[2] // n_op
    own_blk, own_op = place_of()
    scale, theta = norm_theta(parts1[...], count)
    vv, vc, vs, local, ff, vf, vt, fs, ft = (parts2[:, j, :] for j in range(9))

    def mean(x):
        return jnp.sum(x, axis=0, keepdims=True) * (1.0 / count)

    along = mean(vc)
    beta = local - along
    norm_sq = mean(ff + 2.0 * beta * vf + beta * beta * vv)
    unit = lax.rsqrt(jnp.maximum(norm_sq, 0.0) + EPS)
    v_s1 = unit * mean(vt + beta * vs)
    u_s0 = unit * mean(fs + beta * vs)
    u_s1 = unit * unit * mean(ft + beta * (vt + fs) + beta * beta * vs)
    cv, cu, energy = ritz_pair(theta, 0.5 * (v_s1 + u_s0), u_s1)
    energy_out[0] = jnp.max(energy)
    cu = cu * unit
    for e in range(n_pair):
        there = own_op ^ (2 * e)
        back = parts2[own_blk * n_op + there][3:4] - along
        on_vec = (cv + cu * back) * scale
        for h in range(2):
            at = pl.multiple_of((there ^ h) * cols, LANES)
            part = slice(h * cols, (h + 1) * cols)
            for d in range(n_blk):
                blocks = (got[e][j, d, :, part] for got in (got1, got2) for j in range(2))
                raw, sigma, fld, image = (block.astype(jnp.float32) for block in blocks)
                newvec = on_vec * raw + cu * fld
                res = on_vec * sigma + cu * image - energy * newvec
                new_out[slots[d], :, pl.ds(at, cols)] = newvec.astype(jnp.bfloat16)
                res_out[slots[d], :, pl.ds(at, cols)] = res.astype(jnp.bfloat16)


def per_device(
    psi, left_ops, right_ops, term_shift, slot_sector, sector_width, diag_left, diag_right
):
    n_blk, n_op = lax.axis_size("blk"), lax.axis_size("op")
    _, rows, ncols = psi.shape
    terms, _, width, _ = right_ops.shape
    n_pair = n_op // 2
    cols = diag_right.shape[0] // n_op
    step = rows // n_op
    count = float(n_blk * rows * ncols)
    n_dev = n_blk * n_op
    bf16, f32, i32 = jnp.bfloat16, jnp.float32, jnp.int32
    last = sorted(range(1, n_blk), key=lambda d: min(d, n_blk - d))[-1]

    def pack():
        first = swap(term_shift, 1, n_op)
        sent = kernel(
            functools.partial(pack_body, n_blk, n_op),
            [(term_shift, SMEM), (first, SMEM), (psi, HBM), (right_ops, HBM)],
            [((rows, 2 * cols if d in (0, last) else cols), bf16, VMEM) for d in range(n_blk)]
            + [((terms * width + 16, 2 * cols), bf16, VMEM)] * n_pair,
            [pltpu.VMEM(right_ops.shape, bf16), pltpu.SemaphoreType.DMA((2 * n_blk + 1,))],
            nbytes=1 << 20,
        )
        return sent[:n_blk], sent[n_blk:]

    def table(right):
        return kernel(
            functools.partial(table_body, n_blk, terms),
            [(slot_sector, SMEM), (sector_width, SMEM), (diag_left, VMEM)]
            + [(block, VMEM) for block in right],
            [((n_blk * n_pair * terms,), i32, SMEM)]
            + [((n_blk,), i32, SMEM)] * 2
            + [((n_blk, rows, LANES), f32, VMEM)],
        )

    def inputs(left, psi, those):
        blocks = [left[d, 2 * e] for d in those for e in range(n_pair)]
        halves = [half for d in those for half in psi[d]]
        return [(x, VMEM) for x in blocks], [(x, VMEM) for x in halves], [len(psi[d]) for d in those]

    def early(left, psi, n_early, tables):
        left_ins, psi_ins, counts = inputs(left, psi, range(n_early))
        return kernel(
            functools.partial(early_body, n_pair, counts),
            [(tables[1], SMEM)] + left_ins + psi_ins,
            [
                ((n_early, rows, 2 * cols), bf16, VMEM),
                ((n_early, n_pair * terms, rows, 2 * cols), bf16, VMEM),
                ((n_early, n_pair, terms, rows, rows), bf16, HBM),
            ],
            [pltpu.SemaphoreType.DMA((n_early * n_pair,))],
            flops=2 * n_early * rows * rows * 2 * cols * terms * n_pair,
            nbytes=4 << 20,
        )

    left, psi_by, right, (src, widths, slots, diag), (raw_early, inter_early, left_early) = gather(
        left_ops[:, 0], n_blk, n_op, pack, table, early
    )
    n_early = raw_early.shape[0]
    n_late = n_blk - n_early
    left_ins, psi_ins, counts = inputs(left, psi_by, range(n_early, n_blk))
    right_ins = [(block, VMEM) for block in right]
    diags = [(diag, VMEM), (diag_right[None], VMEM)]

    tables = [(src, SMEM), (widths, SMEM)]
    narrow = ((n_blk, rows, 2 * cols), bf16, VMEM)
    wide = ((n_blk, rows, 2 * cols), f32, VMEM)
    sends = [((2, n_blk, step, 2 * cols), bf16, VMEM)] * n_pair
    inter = pltpu.VMEM((n_blk + 1, n_pair * terms, rows, 2 * cols), bf16)
    left_late = (n_late, n_pair, terms, rows, rows)
    cost = dict(flops=2 * n_blk * rows * 2 * cols * terms * n_pair * (rows + 2 * cols), nbytes=6 << 20)

    def totals(parts):
        return lax.all_to_all(parts, ("blk", "op"), 0, 0, tiled=True)

    def exchange(out):
        return [out[0]] + [swap(block, 2 * e, n_op) for e, block in enumerate(out[1:], 1)]

    part1, raw, kept = kernel(
        functools.partial(first_body, n_blk, n_pair, counts),
        tables + left_ins + right_ins + psi_ins + [(raw_early, VMEM), (inter_early, VMEM)],
        [narrow, narrow, (left_late, bf16, HBM)],
        [inter, pltpu.SemaphoreType.DMA((n_late * n_pair + 2,))],
        **cost,
    )
    sig, dots1, *out1 = kernel(
        sigma_body,
        [(x, VMEM) for x in (part1, swap(part1, 1, n_op), raw)] + diags,
        [wide, ((n_dev, 8, LANES), f32, VMEM)] + sends,
        nbytes=4 << 20,
    )
    parts1, got1 = lax.optimization_barrier((totals(dots1), exchange(out1)))
    fld, part2, half = kernel(
        functools.partial(second_body, n_blk, n_pair, count),
        tables + [(left_early, HBM), (kept, HBM)] + right_ins + [(x, VMEM) for x in (parts1, raw, sig)] + diags,
        [narrow, narrow, ((1, 8, LANES), f32, VMEM)],
        [
            inter,
            pltpu.VMEM((n_blk, rows, 2 * cols), f32),
            pltpu.VMEM((n_blk, *left_late[1:]), bf16),
            pltpu.SemaphoreType.DMA((n_blk,)),
        ],
        **cost,
    )
    dots2, *out2 = kernel(
        functools.partial(image_body, count),
        [(x, VMEM) for x in (half, parts1, part2, swap(part2, 1, n_op), raw, sig, fld)] + diags,
        [((n_dev, 16, LANES), f32, VMEM)] + sends,
        [pltpu.VMEM((2, rows, cols), f32)],
        nbytes=4 << 20,
    )
    parts2 = totals(dots2)
    got2 = exchange(out2)
    final = ((n_blk, step, n_op * cols), bf16, VMEM)
    new, res, energy = kernel(
        functools.partial(third_body, n_blk, n_op, count),
        [(slots, SMEM)] + [(x, VMEM) for x in (parts1, parts2, *got1, *got2)],
        [final, final, ((1,), f32, SMEM)],
        nbytes=4 << 20,
    )
    return new, res, energy


def solution(mesh):
    placed = (
        P(("grp", "blk"), None, None),
        P("op", ("grp", "blk"), None, None),
        P("op", ("grp", "blk"), None, None),
        P("op"),
        P("grp"),
        P("grp"),
        P("grp", None),
        P(("grp", "blk")),
    )

    def body(*args):
        psi, left_ops, right_ops, diag_right = args[0], args[1], args[2], args[7]
        n_op = mesh.shape["op"]
        cols = diag_right.shape[0] // n_op
        fits = (
            psi.shape[0] == 1
            and diag_right.shape[0] % n_op == 0
            and cols == LANES
            and n_op % 2 == 0
            and cols % right_ops.shape[2] == 0
            and cols // right_ops.shape[2] * n_op == right_ops.shape[1]
            and psi.shape[1] % (16 * n_op) == 0
            and n_op & (n_op - 1) == 0
            and mesh.shape["blk"] > n_op.bit_length() - 1
        )
        return (per_device if fits else per_device_general)(*args)

    return jax.shard_map(
        body,
        mesh=mesh,
        in_specs=placed,
        out_specs=(P("grp", "op", "blk"), P("grp", "op", "blk"), P("grp")),
        check_vma=False,
    )
```

```python
import functools

import jax
import jax.numpy as jnp
from jax import lax
from jax.experimental import pallas as pl
from jax.experimental.pallas import tpu as pltpu
from jax.sharding import PartitionSpec as P

EPS = 1e-06
LANES = 128
VMEM_LIMIT = 20 * 1024 * 1024


def per_device_general(
    psi, left_ops, right_ops, term_shift, slot_sector, sector_width, diag_left, diag_right
):
    sec_dev, rows, ncols = psi.shape
    nsec = slot_sector.shape[0]
    terms_dev = left_ops.shape[0]
    right_local = right_ops.shape[1]
    right_width = right_ops.shape[2]
    local_cols = diag_right.shape[0]
    count = float(nsec * rows * ncols)
    match = slot_sector[:, None] == jnp.arange(nsec)[None, :]
    widths = jnp.sum(jnp.where(match, sector_width[None, :], 0), axis=1)
    mask_all = (jnp.arange(rows)[None, :] < widths[:, None]).astype(jnp.float32)
    own_mask = lax.dynamic_slice_in_dim(mask_all, lax.axis_index("blk") * sec_dev, sec_dev, 0)
    raw = psi.astype(jnp.float32) * own_mask[:, :, None]
    squares = lax.psum(jnp.sum(raw * raw), "blk")
    v_left = (raw * lax.rsqrt(squares / count + EPS)).astype(jnp.bfloat16)
    onehots = (
        slot_sector[None, None, :] == slot_sector[None, :, None] - term_shift[:, None, None]
    ).astype(jnp.bfloat16)
    op_rows = rows // lax.axis_size("op")
    op_start = lax.axis_index("op") * op_rows
    dmat = diag_left[:, :, None] + diag_right[None, None, :]

    def left_local(field):
        return jnp.einsum(
            "ksij,sjc->ksic", left_ops, field, preferred_element_type=jnp.float32
        ).astype(jnp.bfloat16)

    def right_part(moved_in):
        flat = moved_in.reshape(terms_dev, nsec, rows * local_cols)
        shifted = jnp.einsum(
            "kts,ksx->ktx", onehots, flat, preferred_element_type=jnp.float32
        ).astype(jnp.bfloat16)
        shifted = shifted.reshape(terms_dev, nsec, rows, right_local, right_width)
        accum = jnp.einsum(
            "ktwrc,krdc->twrd", shifted, right_ops, preferred_element_type=jnp.float32
        )
        return accum.reshape(nsec, rows, local_cols) * mask_all[:, :, None]

    def op_total(partial_value):
        return lax.psum(partial_value.astype(jnp.bfloat16), "op").astype(jnp.float32)

    def final_rows(array):
        return lax.dynamic_slice_in_dim(array, op_start, op_rows, 1)

    def reduce_dots(values):
        sums = lax.psum(values, "blk")
        return tuple((item / count for item in sums))

    moved_first, v_moved = (
        lax.all_to_all(left_local(v_left), "blk", split_axis=3, concat_axis=1, tiled=True),
        lax.all_to_all(v_left[None], "blk", split_axis=3, concat_axis=1, tiled=True),
    )
    v_right = v_moved[0]
    vec32 = v_right.astype(jnp.float32)
    first_sigma = op_total(right_part(moved_first)) + dmat * vec32
    theta = reduce_dots((jnp.sum(vec32 * first_sigma),))[0]
    resid = first_sigma - theta * vec32
    den = dmat - theta
    corr = resid * den / jnp.maximum(den * den, 0.25)
    along = reduce_dots((jnp.sum(vec32 * corr),))[0]
    orth = corr - along * vec32
    norm_sq = reduce_dots((jnp.sum(orth * orth),))[0]
    update = (orth * lax.rsqrt(norm_sq + EPS)).astype(jnp.bfloat16)
    upd32 = update.astype(jnp.float32)
    upd_left = lax.all_to_all(update, "blk", split_axis=0, concat_axis=2, tiled=True)
    moved_second = lax.all_to_all(
        left_local(upd_left), "blk", split_axis=3, concat_axis=1, tiled=True
    )
    second_sigma = op_total(right_part(moved_second)) + dmat * upd32
    v_s1, u_s0, u_s1 = reduce_dots(
        (jnp.sum(vec32 * second_sigma), jnp.sum(upd32 * first_sigma), jnp.sum(upd32 * second_sigma))
    )
    h_mix = 0.5 * (v_s1 + u_s0)
    coef_v, coef_u, energy = ritz(theta, h_mix, u_s1)
    newvec = coef_v * vec32 + coef_u * upd32
    image = coef_v * first_sigma + coef_u * second_sigma
    new_out = final_rows(newvec.astype(jnp.bfloat16))
    res_out = final_rows((image - energy * newvec).astype(jnp.bfloat16))
    return (new_out, res_out, jnp.reshape(energy, (1,)))


def ritz(theta, h_mix, h_two):
    angle = 0.5 * jnp.arctan2(2.0 * h_mix, theta - h_two)
    sine = jnp.sin(angle)
    flip = jnp.where(sine > 0, -1.0, 1.0)
    coef_v = -sine * flip
    coef_u = jnp.cos(angle) * flip
    half = 0.5 * (theta - h_two)
    energy = 0.5 * (theta + h_two) - jnp.sqrt(half * half + h_mix * h_mix)
    return coef_v, coef_u, energy


VMEM, SMEM, HBM = pltpu.VMEM, pltpu.SMEM, pltpu.HBM


def kernel(body, ins, outs, scratch=(), flops=0, nbytes=0):
    return pl.pallas_call(
        body,
        out_shape=[
            HBM(shape, dtype) if space == HBM else jax.ShapeDtypeStruct(shape, dtype)
            for shape, dtype, space in outs
        ],
        in_specs=[pl.BlockSpec(memory_space=space) for _, space in ins],
        out_specs=[pl.BlockSpec(memory_space=space) for _, _, space in outs],
        scratch_shapes=list(scratch),
        compiler_params=pltpu.CompilerParams(vmem_limit_bytes=VMEM_LIMIT),
        cost_estimate=pl.CostEstimate(flops=flops, bytes_accessed=nbytes, transcendentals=0),
    )(*[pltpu.with_memory_space_constraint(x, HBM) if space == HBM else x for x, space in ins])


def ring_at(place, n_blk):
    place = place % n_blk if isinstance(place, int) else lax.rem(place + n_blk, n_blk)
    odd, even = 2 * place - 1, 2 * (n_blk - place)
    if isinstance(place, int):
        return 0 if place == 0 else odd if odd < n_blk else even
    return jnp.where(place == 0, 0, jnp.where(odd < n_blk, odd, even))


def ring_place(index, n_blk):
    odd, even = (index + 1) // 2, lax.rem(n_blk - index // 2, n_blk)
    return jnp.where(lax.rem(index, 2) == 1, odd, even)


def onward(block, d, n_blk):
    pairs = [(ring_at(i, n_blk), ring_at(i + d, n_blk)) for i in range(n_blk)]
    return lax.ppermute(block, "blk", pairs)


def swap(block, e, n_op):
    return lax.ppermute(block, "op", [(i, i ^ e) for i in range(n_op)])


def gather(own, n_blk, n_op, pack, table, early):
    bits = [1 << b for b in reversed(range(1, n_op.bit_length() - 1))]
    order = sorted(range(1, n_blk), key=lambda d: min(d, n_blk - d))
    left, psi, right, tables, columns = {(0, 0): own}, {}, None, None, None
    waiting, late, made = {(0, 0): 0}, None, None
    for j in range(n_blk + len(bits)):
        new, moved = {}, {}
        for (d, e), done in waiting.items():
            if e == 0 and d + 1 < n_blk:
                new[d + 1, 0] = onward(left[d, 0], 1, n_blk), 0
            for b in range(done, len(bits)):
                new[d, e ^ bits[b]] = swap(left[d, e], bits[b], n_op), b + 1
        kept = {key: block for key, (block, _) in new.items()}
        if late is not None:
            moved["psi"] = late
        if j == 0:
            columns, packed = pack()
            moved["right"] = [packed[0]]
            moved["right"] += [swap(part, 2 * e, n_op) for e, part in enumerate(packed[1:], 1)]
        if j == 1:
            moved["tables"] = table(right)
        if j == n_blk - 1 and j >= len(bits) + 1:
            n_early = min(2, n_blk - 1)
            psi[0] = [columns[0]]
            moved["early"] = early(left, psi, n_early, tables)
        if 2 <= j < n_blk:
            moved["other"] = swap(psi[order[j - 2]][0], 1, n_op)
        late = onward(columns[order[j]], order[j], n_blk) if j < n_blk - 1 else None
        if not kept and not moved:
            break
        waiting = {key: done for key, (_, done) in new.items()}
        kept, moved = lax.optimization_barrier((kept, moved))
        left.update(kept)
        right, tables = moved.get("right", right), moved.get("tables", tables)
        made = moved.get("early", made)
        if "psi" in moved:
            psi[order[j - 1]] = [moved["psi"]]
        if "other" in moved:
            psi[order[j - 2]].append(moved["other"])
    return left, psi, right, tables, made


def place_of():
    return lax.axis_index("blk"), lax.axis_index("op")


def pack_body(n_blk, n_op, shift, _, psi, right_in, *outs):
    n_pair = n_op // 2
    psi_out, right_out, right, sems = outs[:n_blk], outs[n_blk : n_blk + n_pair], outs[-2], outs[-1]
    terms, local, width, _ = right.shape
    cols = local * width // n_op
    per = cols // width
    own_blk, own_op = place_of()
    fetch = pltpu.make_async_copy(right_in, right, sems.at[2 * n_blk])
    fetch.start()
    copies = []
    for d in range(n_blk):
        there = ring_at(ring_place(own_blk, n_blk) + d, n_blk) * n_op
        for h in range(psi_out[d].shape[1] // cols):
            start = pl.multiple_of((there + (own_op ^ h)) * cols, LANES)
            copy = pltpu.make_async_copy(
                psi.at[0, :, pl.ds(start, cols)],
                psi_out[d].at[:, h * cols : (h + 1) * cols],
                sems.at[2 * d + h],
            )
            copy.start()
            copies.append(copy)
    lane = lax.broadcasted_iota(jnp.int32, (16, 2 * cols), 1)
    line = jnp.zeros((16, 2 * cols), jnp.float32)
    for k in range(terms):
        line = jnp.where(lane == k, shift[k].astype(jnp.float32), line)
    square = [lax.broadcasted_iota(jnp.int32, (width, width), axis) for axis in (0, 1)]
    unit = (square[0] == square[1]).astype(jnp.bfloat16)
    fetch.wait()
    for e in range(n_pair):
        for k in range(terms):
            turned = []
            for h in range(2):
                first = (own_op ^ (2 * e) ^ h) * per
                for r in range(per):
                    turned.append(
                        lax.dot_general(
                            right[k, first + r], unit, (((0,), (0,)), ((), ())),
                            preferred_element_type=jnp.float32,
                        )
                    )
            side_by_side = jnp.concatenate(turned, axis=1).astype(jnp.bfloat16)
            right_out[e][k * width : (k + 1) * width] = side_by_side
        right_out[e][terms * width :] = line.astype(jnp.bfloat16)
    for copy in copies:
        copy.wait()


def table_body(n_blk, terms, sector, width, left_diag, *refs):
    tails, src, widths, slots, diag = refs[:-4], *refs[-4:]
    n_pair = len(tails)
    rows, cols = tails[0].shape
    own_blk, _ = place_of()
    lane = lax.broadcasted_iota(jnp.int32, (16, cols), 1)
    for d in range(n_blk):
        slot = ring_at(ring_place(own_blk, n_blk) - d, n_blk)
        slots[d] = slot
        widths[d] = width[sector[slot]]
    for e in range(n_pair):
        tail = tails[e][rows - 16 :].astype(jnp.float32)
        for k in range(terms):
            shift = jnp.max(jnp.where(lane == k, tail, -1e9)).astype(jnp.int32)
            for t in range(n_blk):
                want = sector[slots[t]] - shift
                found = jnp.int32(n_blk)
                for d in range(n_blk):
                    found = jnp.where(sector[slots[d]] == want, d, found)
                src[(t * n_pair + e) * terms + k] = found
    for d in range(n_blk):
        row = left_diag[pl.ds(slots[d], 1), :]
        diag[d] = jnp.transpose(jnp.broadcast_to(row, (diag.shape[2], row.shape[1])))


def diagonal(diag, right_diag, d, h):
    cols = diag.shape[2]
    _, own_op = place_of()
    start = pl.multiple_of((own_op ^ h) * cols, LANES)
    return diag[d] + right_diag[:, pl.ds(start, cols)]


def row_mask(width, shape):
    return lax.broadcasted_iota(jnp.int32, shape, 0) < width


def fold(x):
    return jnp.sum(x.reshape(-1, 8, x.shape[-1]), axis=0)


def whole(x):
    return jnp.sum(jnp.sum(x, axis=0, keepdims=True), axis=1, keepdims=True)


def spread(values, out):
    line = lax.broadcasted_iota(jnp.int32, out.shape[1:], 0)
    tile = jnp.zeros(out.shape[1:], jnp.float32)
    for j, value in enumerate(values):
        tile = jnp.where(line == j, value, tile)
    for d in range(out.shape[0]):
        out[d] = tile


def by_block(packed, terms, k):
    rows, cols = packed.shape
    width = (rows - 16) // terms
    lane = lax.broadcasted_iota(jnp.int32, (width, cols), 1)
    block = packed[k * width : (k + 1) * width].astype(jnp.float32)
    parts = []
    for r in range(cols // width):
        inside = (lane >= r * width) & (lane < (r + 1) * width)
        parts.append(jnp.where(inside, block, 0.0).astype(jnp.bfloat16))
    return jnp.concatenate(parts, axis=0)


def left_products(block, left, inter):
    n_terms, rows, cols = inter.shape
    at = 0
    while at < n_terms:
        ops = left(at)
        terms = ops.shape[0]
        prod = jnp.dot(ops.reshape(terms * rows, rows), block, preferred_element_type=jnp.float32)
        inter[at : at + terms] = prod.astype(jnp.bfloat16).reshape(terms, rows, cols)
        at += terms


def sum_terms(src, widths, inter, right, out):
    n_blk, n_terms, _, _ = inter.shape
    n_blk -= 1
    terms = n_terms // len(right)
    turned = [by_block(right[j // terms], terms, j % terms) for j in range(n_terms)]
    for t in range(n_blk):
        total = None
        for j in range(n_terms):
            part = jnp.dot(
                inter[src[t * n_terms + j], j], turned[j], preferred_element_type=jnp.float32
            )
            total = part if total is None else total + part
        out[t] = jnp.where(row_mask(widths[t], total.shape), total, 0.0).astype(jnp.bfloat16)


def keep(left, left_out, sems):
    copies = []
    for d, line in enumerate(left):
        for e, ref in enumerate(line):
            copies.append(pltpu.make_async_copy(ref, left_out.at[d, e], sems.at[d * len(line) + e]))
            copies[-1].start()
    return copies


def masked(psi, width, out):
    at = 0
    for ref in psi:
        block = ref[...].astype(jnp.float32)
        block = jnp.where(row_mask(width, block.shape), block, 0.0)
        out[:, at : at + block.shape[1]] = block.astype(jnp.bfloat16)
        at += block.shape[1]


def take(refs, counts):
    out = []
    for count in counts:
        out.append(refs[:count])
        refs = refs[count:]
    return out, refs


def products_of(psi, left, widths, first, raw_out, inter):
    for d, line in enumerate(left):
        masked(psi[d], widths[first + d], raw_out.at[d])
        terms = line[0].shape[0]
        left_products(raw_out[d], lambda at: line[at // terms][...], inter.at[d])


def early_body(n_pair, counts, widths, *refs):
    left, refs = take(refs, [n_pair] * len(counts))
    psi, (raw_out, inter_out, left_out, sems) = take(refs, counts)
    copies = keep(left, left_out, sems)
    products_of(psi, left, widths, 0, raw_out, inter_out)
    for copy in copies:
        copy.wait()


def first_body(n_blk, n_pair, counts, src, widths, *refs):
    n_late = len(counts)
    n_early = n_blk - n_late
    left, refs = take(refs, [n_pair] * n_late)
    (right,), refs = take(refs, [n_pair])
    psi, (raw_in, inter_in, part_out, raw_out, left_out, inter, sems) = take(refs, counts)
    copies = keep(left, left_out, sems)
    for j, (given, own) in enumerate(((inter_in, inter), (raw_in, raw_out))):
        copies.append(
            pltpu.make_async_copy(given, own.at[:n_early], sems.at[n_late * n_pair + j])
        )
        copies[-1].start()
    inter[n_blk] = jnp.zeros_like(inter[n_blk])
    products_of(
        psi, left, widths, n_early, raw_out.at[n_early:], inter.at[n_early:n_blk]
    )
    for copy in copies:
        copy.wait()
    sum_terms(src, widths, inter, right, part_out)


def send_rows(sends, j, d, h, block):
    _, own_op = place_of()
    step, cols = sends[0].shape[2], block.shape[1]
    for e, send in enumerate(sends):
        start = pl.multiple_of((own_op ^ (2 * e)) * step, step)
        send[j, d, :, h * cols : (h + 1) * cols] = block[pl.ds(start, step)].astype(send.dtype)


def total_of(mine, other, d, h, cols):
    own = mine[d, :, h * cols : (h + 1) * cols].astype(jnp.float32)
    return own + other[d, :, (1 - h) * cols : (2 - h) * cols].astype(jnp.float32)


def sigma_body(mine, other, raw_in, diag, right_diag, sig_out, dots_out, *sends):
    n_blk, _, cols = diag.shape
    sums = [[jnp.zeros((8, cols), jnp.float32) for _ in range(2)] for _ in range(2)]
    for d in range(n_blk):
        for h in range(2):
            part = slice(h * cols, (h + 1) * cols)
            raw = raw_in[d, :, part].astype(jnp.float32)
            sigma = total_of(mine, other, d, h, cols) + diagonal(diag, right_diag, d, h) * raw
            sig_out[d, :, part] = sigma
            sums[h] = [sums[h][0] + fold(raw * raw), sums[h][1] + fold(raw * sigma)]
    for d in range(n_blk):
        for h in range(2):
            send_rows(sends, 0, d, h, raw_in.at[d, :, h * cols : (h + 1) * cols])
            send_rows(sends, 1, d, h, sig_out.at[d, :, h * cols : (h + 1) * cols])
    spread([whole(x) + whole(y) for x, y in zip(*sums)], dots_out)


def norm_theta(parts, count):
    tot = jnp.sum(parts, axis=0) * (1.0 / count)
    scale = lax.rsqrt(tot[0:1] + EPS)
    return scale, tot[1:2] * scale * scale


def second_body(n_blk, n_pair, count, src, widths, left_early, left_late, *refs):
    right, refs = refs[:n_pair], refs[n_pair:]
    parts, raw_in, sig_in, diag, right_diag, f_out, part_out, pair_out = refs[:8]
    inter, corr, held, sems = refs[8:]
    copies = []
    n_early = left_early.shape[0]
    for d in range(n_blk):
        kept = left_early.at[d] if d < n_early else left_late.at[d - n_early]
        copies.append(pltpu.make_async_copy(kept, held.at[d], sems.at[d]))
        copies[-1].start()
    inter[n_blk] = jnp.zeros_like(inter[n_blk])
    scale, theta = norm_theta(parts[...], count)
    cols = diag.shape[2]
    halves = []
    for h in range(2):
        part = slice(h * cols, (h + 1) * cols)
        vv = vc = vs = jnp.zeros((8, cols), jnp.float32)
        for d in range(n_blk):
            vec = raw_in[d, :, part].astype(jnp.float32) * scale
            sigma = sig_in[d, :, part] * scale
            den = diagonal(diag, right_diag, d, h) - theta
            item = (sigma - theta * vec) * den / jnp.maximum(den * den, 0.25)
            corr[d, :, part] = item
            vv, vc, vs = vv + fold(vec * vec), vc + fold(vec * item), vs + fold(vec * sigma)
        halves.append((whole(vv), whole(vc), whole(vs)))
    vv, vc, vs = (x + y for x, y in zip(*halves))
    along = vc / jnp.maximum(vv, 1e-30)
    terms = held.shape[2]
    for d in range(n_blk):
        for h in range(2):
            part = slice(h * cols, (h + 1) * cols)
            vec = raw_in[d, :, part].astype(jnp.float32) * scale
            f_out[d, :, part] = (corr[d, :, part] - along * vec).astype(jnp.bfloat16)
        copies[d].wait()
        left_products(f_out[d], lambda at: held[d, at // terms], inter.at[d])
    sum_terms(src, widths, inter, right, part_out)
    spread((vv, vc, vs, along), pair_out)


def image_body(count, pair, parts, mine, other, raw_in, sig_in, f_in, diag, right_diag, dots_out, *sends):
    n_blk, _, cols = diag.shape
    scale, _ = norm_theta(parts[...], count)
    sums = [[jnp.zeros((8, cols), jnp.float32) for _ in range(5)] for _ in range(2)]
    for d in range(n_blk):
        for h in range(2):
            part = slice(h * cols, (h + 1) * cols)
            fld = f_in[d, :, part].astype(jnp.float32)
            image = total_of(mine, other, d, h, cols) + diagonal(diag, right_diag, d, h) * fld
            sends[-1][h] = image
            send_rows(sends[:-1], 0, d, h, f_in.at[d, :, part])
            send_rows(sends[:-1], 1, d, h, sends[-1].at[h])
            vec = raw_in[d, :, part].astype(jnp.float32) * scale
            sigma = sig_in[d, :, part] * scale
            prods = (fld * fld, vec * fld, vec * image, fld * sigma, fld * image)
            sums[h] = [one + fold(prod) for one, prod in zip(sums[h], prods)]
    known = [pair[0, j : j + 1] for j in range(4)]
    spread(known + [whole(x) + whole(y) for x, y in zip(*sums)], dots_out)


def ritz_pair(theta, h_mix, h_two):
    diff, twice = theta - h_two, 2.0 * h_mix
    size = jnp.sqrt(diff * diff + twice * twice)
    some = size > 0.0
    safe = jnp.where(some, size, 1.0)
    big = jnp.sqrt(0.5 + 0.5 * jnp.abs(diff) / safe)
    small = 0.5 * jnp.abs(twice) / (safe * big)
    sine = jnp.where(diff >= 0.0, small, big)
    cosine = jnp.where(diff >= 0.0, big, small)
    sine = jnp.where(some, sine, 0.0)
    cosine = jnp.where(some, cosine, 1.0)
    upward = (twice > 0.0) | ((twice == 0.0) & (diff < 0.0))
    return sine, jnp.where(upward, -cosine, cosine), 0.5 * (theta + h_two) - 0.5 * size


def third_body(n_blk, n_op, count, slots, parts1, parts2, *refs):
    n_pair = n_op // 2
    got1, got2 = refs[:n_pair], refs[n_pair : 2 * n_pair]
    new_out, res_out, energy_out = refs[2 * n_pair :]
    cols = new_out.shape[2] // n_op
    own_blk, own_op = place_of()
    scale, theta = norm_theta(parts1[...], count)
    vv, vc, vs, local, ff, vf, vt, fs, ft = (parts2[:, j, :] for j in range(9))

    def mean(x):
        return jnp.sum(x, axis=0, keepdims=True) * (1.0 / count)

    along = mean(vc)
    beta = local - along
    norm_sq = mean(ff + 2.0 * beta * vf + beta * beta * vv)
    unit = lax.rsqrt(jnp.maximum(norm_sq, 0.0) + EPS)
    v_s1 = unit * mean(vt + beta * vs)
    u_s0 = unit * mean(fs + beta * vs)
    u_s1 = unit * unit * mean(ft + beta * (vt + fs) + beta * beta * vs)
    cv, cu, energy = ritz_pair(theta, 0.5 * (v_s1 + u_s0), u_s1)
    energy_out[0] = jnp.max(energy)
    cu = cu * unit
    for e in range(n_pair):
        there = own_op ^ (2 * e)
        back = parts2[own_blk * n_pair + there // 2][3:4] - along
        on_vec = (cv + cu * back) * scale
        for h in range(2):
            at = pl.multiple_of((there ^ h) * cols, LANES)
            part = slice(h * cols, (h + 1) * cols)
            for d in range(n_blk):
                blocks = (got[e][j, d, :, part] for got in (got1, got2) for j in range(2))
                raw, sigma, fld, image = (block.astype(jnp.float32) for block in blocks)
                newvec = on_vec * raw + cu * fld
                res = on_vec * sigma + cu * image - energy * newvec
                new_out[slots[d], :, pl.ds(at, cols)] = newvec.astype(jnp.bfloat16)
                res_out[slots[d], :, pl.ds(at, cols)] = res.astype(jnp.bfloat16)


def per_device(
    psi, left_ops, right_ops, term_shift, slot_sector, sector_width, diag_left, diag_right
):
    n_blk, n_op = lax.axis_size("blk"), lax.axis_size("op")
    _, rows, ncols = psi.shape
    terms, _, width, _ = right_ops.shape
    n_pair = n_op // 2
    cols = diag_right.shape[0] // n_op
    step = rows // n_op
    count = float(n_blk * rows * ncols)
    n_sum = n_blk * n_pair
    bf16, f32, i32 = jnp.bfloat16, jnp.float32, jnp.int32
    last = sorted(range(1, n_blk), key=lambda d: min(d, n_blk - d))[-1]

    def pack():
        first = swap(term_shift, 1, n_op)
        sent = kernel(
            functools.partial(pack_body, n_blk, n_op),
            [(term_shift, SMEM), (first, SMEM), (psi, HBM), (right_ops, HBM)],
            [((rows, 2 * cols if d in (0, last) else cols), bf16, VMEM) for d in range(n_blk)]
            + [((terms * width + 16, 2 * cols), bf16, VMEM)] * n_pair,
            [pltpu.VMEM(right_ops.shape, bf16), pltpu.SemaphoreType.DMA((2 * n_blk + 1,))],
            nbytes=1 << 20,
        )
        return sent[:n_blk], sent[n_blk:]

    def table(right):
        return kernel(
            functools.partial(table_body, n_blk, terms),
            [(slot_sector, SMEM), (sector_width, SMEM), (diag_left, VMEM)]
            + [(block, VMEM) for block in right],
            [((n_blk * n_pair * terms,), i32, SMEM)]
            + [((n_blk,), i32, SMEM)] * 2
            + [((n_blk, rows, LANES), f32, VMEM)],
        )

    def inputs(left, psi, those):
        blocks = [left[d, 2 * e] for d in those for e in range(n_pair)]
        halves = [half for d in those for half in psi[d]]
        return [(x, VMEM) for x in blocks], [(x, VMEM) for x in halves], [len(psi[d]) for d in those]

    def early(left, psi, n_early, tables):
        left_ins, psi_ins, counts = inputs(left, psi, range(n_early))
        return kernel(
            functools.partial(early_body, n_pair, counts),
            [(tables[1], SMEM)] + left_ins + psi_ins,
            [
                ((n_early, rows, 2 * cols), bf16, VMEM),
                ((n_early, n_pair * terms, rows, 2 * cols), bf16, VMEM),
                ((n_early, n_pair, terms, rows, rows), bf16, HBM),
            ],
            [pltpu.SemaphoreType.DMA((n_early * n_pair,))],
            flops=2 * n_early * rows * rows * 2 * cols * terms * n_pair,
            nbytes=4 << 20,
        )

    left, psi_by, right, (src, widths, slots, diag), (raw_early, inter_early, left_early) = gather(
        left_ops[:, 0], n_blk, n_op, pack, table, early
    )
    n_early = raw_early.shape[0]
    n_late = n_blk - n_early
    left_ins, psi_ins, counts = inputs(left, psi_by, range(n_early, n_blk))
    right_ins = [(block, VMEM) for block in right]
    diags = [(diag, VMEM), (diag_right[None], VMEM)]

    tables = [(src, SMEM), (widths, SMEM)]
    narrow = ((n_blk, rows, 2 * cols), bf16, VMEM)
    wide = ((n_blk, rows, 2 * cols), f32, VMEM)
    sends = [((2, n_blk, step, 2 * cols), bf16, VMEM)] * n_pair
    inter = pltpu.VMEM((n_blk + 1, n_pair * terms, rows, 2 * cols), bf16)
    left_late = (n_late, n_pair, terms, rows, rows)
    cost = dict(flops=2 * n_blk * rows * 2 * cols * terms * n_pair * (rows + 2 * cols), nbytes=6 << 20)

    def totals(parts):
        groups = [list(range(bit, n_blk * n_op, 2)) for bit in range(2)]
        return lax.all_to_all(parts, ("blk", "op"), 0, 0, axis_index_groups=groups, tiled=True)

    def exchange(out):
        return [out[0]] + [swap(block, 2 * e, n_op) for e, block in enumerate(out[1:], 1)]

    part1, raw, kept = kernel(
        functools.partial(first_body, n_blk, n_pair, counts),
        tables + left_ins + right_ins + psi_ins + [(raw_early, VMEM), (inter_early, VMEM)],
        [narrow, narrow, (left_late, bf16, HBM)],
        [inter, pltpu.SemaphoreType.DMA((n_late * n_pair + 2,))],
        **cost,
    )
    sig, dots1, *out1 = kernel(
        sigma_body,
        [(x, VMEM) for x in (part1, swap(part1, 1, n_op), raw)] + diags,
        [wide, ((n_sum, 8, LANES), f32, VMEM)] + sends,
        nbytes=4 << 20,
    )
    parts1, got1 = lax.optimization_barrier((totals(dots1), exchange(out1)))
    fld, part2, pair = kernel(
        functools.partial(second_body, n_blk, n_pair, count),
        tables + [(left_early, HBM), (kept, HBM)] + right_ins + [(x, VMEM) for x in (parts1, raw, sig)] + diags,
        [narrow, narrow, ((1, 8, LANES), f32, VMEM)],
        [
            inter,
            pltpu.VMEM((n_blk, rows, 2 * cols), f32),
            pltpu.VMEM((n_blk, *left_late[1:]), bf16),
            pltpu.SemaphoreType.DMA((n_blk,)),
        ],
        **cost,
    )
    dots2, *out2 = kernel(
        functools.partial(image_body, count),
        [(x, VMEM) for x in (pair, parts1, part2, swap(part2, 1, n_op), raw, sig, fld)] + diags,
        [((n_sum, 16, LANES), f32, VMEM)] + sends,
        [pltpu.VMEM((2, rows, cols), f32)],
        nbytes=4 << 20,
    )
    parts2 = totals(dots2)
    got2 = exchange(out2)
    final = ((n_blk, step, n_op * cols), bf16, VMEM)
    new, res, energy = kernel(
        functools.partial(third_body, n_blk, n_op, count),
        [(slots, SMEM)] + [(x, VMEM) for x in (parts1, parts2, *got1, *got2)],
        [final, final, ((1,), f32, SMEM)],
        nbytes=4 << 20,
    )
    return new, res, energy


def solution(mesh):
    placed = (
        P(("grp", "blk"), None, None),
        P("op", ("grp", "blk"), None, None),
        P("op", ("grp", "blk"), None, None),
        P("op"),
        P("grp"),
        P("grp"),
        P("grp", None),
        P(("grp", "blk")),
    )

    def body(*args):
        psi, left_ops, right_ops, diag_right = args[0], args[1], args[2], args[7]
        n_op = mesh.shape["op"]
        cols = diag_right.shape[0] // n_op
        fits = (
            psi.shape[0] == 1
            and diag_right.shape[0] % n_op == 0
            and cols == LANES
            and n_op % 2 == 0
            and cols % right_ops.shape[2] == 0
            and cols // right_ops.shape[2] * n_op == right_ops.shape[1]
            and psi.shape[1] % (16 * n_op) == 0
            and n_op & (n_op - 1) == 0
            and mesh.shape["blk"] > n_op.bit_length() - 1
        )
        return (per_device if fits else per_device_general)(*args)

    return jax.shard_map(
        body,
        mesh=mesh,
        in_specs=placed,
        out_specs=(P("grp", "op", "blk"), P("grp", "op", "blk"), P("grp")),
        check_vma=False,
    )
```

```python
import functools

import jax
import jax.numpy as jnp
from jax import lax
from jax.experimental import pallas as pl
from jax.experimental.pallas import tpu as pltpu
from jax.sharding import PartitionSpec as P

EPS = 1e-06
LANES = 128
VMEM_LIMIT = 20 * 1024 * 1024


def per_device_general(
    psi, left_ops, right_ops, term_shift, slot_sector, sector_width, diag_left, diag_right
):
    sec_dev, rows, ncols = psi.shape
    nsec = slot_sector.shape[0]
    terms_dev = left_ops.shape[0]
    right_local = right_ops.shape[1]
    right_width = right_ops.shape[2]
    local_cols = diag_right.shape[0]
    count = float(nsec * rows * ncols)
    match = slot_sector[:, None] == jnp.arange(nsec)[None, :]
    widths = jnp.sum(jnp.where(match, sector_width[None, :], 0), axis=1)
    mask_all = (jnp.arange(rows)[None, :] < widths[:, None]).astype(jnp.float32)
    own_mask = lax.dynamic_slice_in_dim(mask_all, lax.axis_index("blk") * sec_dev, sec_dev, 0)
    raw = psi.astype(jnp.float32) * own_mask[:, :, None]
    squares = lax.psum(jnp.sum(raw * raw), "blk")
    v_left = (raw * lax.rsqrt(squares / count + EPS)).astype(jnp.bfloat16)
    onehots = (
        slot_sector[None, None, :] == slot_sector[None, :, None] - term_shift[:, None, None]
    ).astype(jnp.bfloat16)
    op_rows = rows // lax.axis_size("op")
    op_start = lax.axis_index("op") * op_rows
    dmat = diag_left[:, :, None] + diag_right[None, None, :]

    def left_local(field):
        return jnp.einsum(
            "ksij,sjc->ksic", left_ops, field, preferred_element_type=jnp.float32
        ).astype(jnp.bfloat16)

    def right_part(moved_in):
        flat = moved_in.reshape(terms_dev, nsec, rows * local_cols)
        shifted = jnp.einsum(
            "kts,ksx->ktx", onehots, flat, preferred_element_type=jnp.float32
        ).astype(jnp.bfloat16)
        shifted = shifted.reshape(terms_dev, nsec, rows, right_local, right_width)
        accum = jnp.einsum(
            "ktwrc,krdc->twrd", shifted, right_ops, preferred_element_type=jnp.float32
        )
        return accum.reshape(nsec, rows, local_cols) * mask_all[:, :, None]

    def op_total(partial_value):
        return lax.psum(partial_value.astype(jnp.bfloat16), "op").astype(jnp.float32)

    def final_rows(array):
        return lax.dynamic_slice_in_dim(array, op_start, op_rows, 1)

    def reduce_dots(values):
        sums = lax.psum(values, "blk")
        return tuple((item / count for item in sums))

    moved_first, v_moved = (
        lax.all_to_all(left_local(v_left), "blk", split_axis=3, concat_axis=1, tiled=True),
        lax.all_to_all(v_left[None], "blk", split_axis=3, concat_axis=1, tiled=True),
    )
    v_right = v_moved[0]
    vec32 = v_right.astype(jnp.float32)
    first_sigma = op_total(right_part(moved_first)) + dmat * vec32
    theta = reduce_dots((jnp.sum(vec32 * first_sigma),))[0]
    resid = first_sigma - theta * vec32
    den = dmat - theta
    corr = resid * den / jnp.maximum(den * den, 0.25)
    along = reduce_dots((jnp.sum(vec32 * corr),))[0]
    orth = corr - along * vec32
    norm_sq = reduce_dots((jnp.sum(orth * orth),))[0]
    update = (orth * lax.rsqrt(norm_sq + EPS)).astype(jnp.bfloat16)
    upd32 = update.astype(jnp.float32)
    upd_left = lax.all_to_all(update, "blk", split_axis=0, concat_axis=2, tiled=True)
    moved_second = lax.all_to_all(
        left_local(upd_left), "blk", split_axis=3, concat_axis=1, tiled=True
    )
    second_sigma = op_total(right_part(moved_second)) + dmat * upd32
    v_s1, u_s0, u_s1 = reduce_dots(
        (jnp.sum(vec32 * second_sigma), jnp.sum(upd32 * first_sigma), jnp.sum(upd32 * second_sigma))
    )
    h_mix = 0.5 * (v_s1 + u_s0)
    coef_v, coef_u, energy = ritz(theta, h_mix, u_s1)
    newvec = coef_v * vec32 + coef_u * upd32
    image = coef_v * first_sigma + coef_u * second_sigma
    new_out = final_rows(newvec.astype(jnp.bfloat16))
    res_out = final_rows((image - energy * newvec).astype(jnp.bfloat16))
    return (new_out, res_out, jnp.reshape(energy, (1,)))


def ritz(theta, h_mix, h_two):
    angle = 0.5 * jnp.arctan2(2.0 * h_mix, theta - h_two)
    sine = jnp.sin(angle)
    flip = jnp.where(sine > 0, -1.0, 1.0)
    coef_v = -sine * flip
    coef_u = jnp.cos(angle) * flip
    half = 0.5 * (theta - h_two)
    energy = 0.5 * (theta + h_two) - jnp.sqrt(half * half + h_mix * h_mix)
    return coef_v, coef_u, energy


VMEM, SMEM, HBM = pltpu.VMEM, pltpu.SMEM, pltpu.HBM


def kernel(body, ins, outs, scratch=(), flops=0, nbytes=0):
    return pl.pallas_call(
        body,
        out_shape=[
            HBM(shape, dtype) if space == HBM else jax.ShapeDtypeStruct(shape, dtype)
            for shape, dtype, space in outs
        ],
        in_specs=[pl.BlockSpec(memory_space=space) for _, space in ins],
        out_specs=[pl.BlockSpec(memory_space=space) for _, _, space in outs],
        scratch_shapes=list(scratch),
        compiler_params=pltpu.CompilerParams(vmem_limit_bytes=VMEM_LIMIT),
        cost_estimate=pl.CostEstimate(flops=flops, bytes_accessed=nbytes, transcendentals=0),
    )(*[pltpu.with_memory_space_constraint(x, HBM) if space == HBM else x for x, space in ins])


def ring_at(place, n_blk):
    place = place % n_blk if isinstance(place, int) else lax.rem(place + n_blk, n_blk)
    odd, even = 2 * place - 1, 2 * (n_blk - place)
    if isinstance(place, int):
        return 0 if place == 0 else odd if odd < n_blk else even
    return jnp.where(place == 0, 0, jnp.where(odd < n_blk, odd, even))


def ring_place(index, n_blk):
    odd, even = (index + 1) // 2, lax.rem(n_blk - index // 2, n_blk)
    return jnp.where(lax.rem(index, 2) == 1, odd, even)


def onward(block, d, n_blk):
    pairs = [(ring_at(i, n_blk), ring_at(i + d, n_blk)) for i in range(n_blk)]
    return lax.ppermute(block, "blk", pairs)


def swap(block, e, n_op):
    return lax.ppermute(block, "op", [(i, i ^ e) for i in range(n_op)])


def gather(own, n_blk, n_op, pack, table, early):
    bits = [1 << b for b in reversed(range(1, n_op.bit_length() - 1))]
    order = sorted(range(1, n_blk), key=lambda d: min(d, n_blk - d))
    left, psi, right, tables, columns = {(0, 0): own}, {}, None, None, None
    waiting, late, made = {(0, 0): 0}, None, None
    for j in range(n_blk + len(bits)):
        new, moved = {}, {}
        for (d, e), done in waiting.items():
            if e == 0 and d + 1 < n_blk:
                new[d + 1, 0] = onward(left[d, 0], 1, n_blk), 0
            for b in range(done, len(bits)):
                new[d, e ^ bits[b]] = swap(left[d, e], bits[b], n_op), b + 1
        kept = {key: block for key, (block, _) in new.items()}
        if late is not None:
            moved["psi"] = late
        if j == 0:
            columns, packed = pack()
            moved["right"] = [packed[0]]
            moved["right"] += [swap(part, 2 * e, n_op) for e, part in enumerate(packed[1:], 1)]
        if j == 1:
            moved["tables"] = table(right)
        if j == n_blk - 1 and j >= len(bits) + 1:
            n_early = min(2, n_blk - 1)
            psi[0] = [columns[0]]
            moved["early"] = early(left, psi, n_early, tables)
        if 2 <= j < n_blk:
            moved["other"] = swap(psi[order[j - 2]][0], 1, n_op)
        late = onward(columns[order[j]], order[j], n_blk) if j < n_blk - 1 else None
        if not kept and not moved:
            break
        waiting = {key: done for key, (_, done) in new.items()}
        kept, moved = lax.optimization_barrier((kept, moved))
        left.update(kept)
        right, tables = moved.get("right", right), moved.get("tables", tables)
        made = moved.get("early", made)
        if "psi" in moved:
            psi[order[j - 1]] = [moved["psi"]]
        if "other" in moved:
            psi[order[j - 2]].append(moved["other"])
    return left, psi, right, tables, made


def place_of():
    return lax.axis_index("blk"), lax.axis_index("op")


def pack_body(n_blk, n_op, shift, _, psi, right_in, *outs):
    n_pair = n_op // 2
    psi_out, right_out, right, sems = outs[:n_blk], outs[n_blk : n_blk + n_pair], outs[-2], outs[-1]
    terms, local, width, _ = right.shape
    cols = local * width // n_op
    per = cols // width
    own_blk, own_op = place_of()
    fetch = pltpu.make_async_copy(right_in, right, sems.at[2 * n_blk])
    fetch.start()
    copies = []
    for d in range(n_blk):
        there = ring_at(ring_place(own_blk, n_blk) + d, n_blk) * n_op
        for h in range(psi_out[d].shape[1] // cols):
            start = pl.multiple_of((there + (own_op ^ h)) * cols, LANES)
            copy = pltpu.make_async_copy(
                psi.at[0, :, pl.ds(start, cols)],
                psi_out[d].at[:, h * cols : (h + 1) * cols],
                sems.at[2 * d + h],
            )
            copy.start()
            copies.append(copy)
    lane = lax.broadcasted_iota(jnp.int32, (16, 2 * cols), 1)
    line = jnp.zeros((16, 2 * cols), jnp.float32)
    for k in range(terms):
        line = jnp.where(lane == k, shift[k].astype(jnp.float32), line)
    square = [lax.broadcasted_iota(jnp.int32, (width, width), axis) for axis in (0, 1)]
    unit = (square[0] == square[1]).astype(jnp.bfloat16)
    fetch.wait()
    for e in range(n_pair):
        for k in range(terms):
            turned = []
            for h in range(2):
                first = (own_op ^ (2 * e) ^ h) * per
                for r in range(per):
                    turned.append(
                        lax.dot_general(
                            right[k, first + r], unit, (((0,), (0,)), ((), ())),
                            preferred_element_type=jnp.float32,
                        )
                    )
            side_by_side = jnp.concatenate(turned, axis=1).astype(jnp.bfloat16)
            right_out[e][k * width : (k + 1) * width] = side_by_side
        right_out[e][terms * width :] = line.astype(jnp.bfloat16)
    for copy in copies:
        copy.wait()


def table_body(n_blk, terms, sector, width, left_diag, *refs):
    tails, src, widths, slots, diag = refs[:-4], *refs[-4:]
    n_pair = len(tails)
    rows, cols = tails[0].shape
    own_blk, _ = place_of()
    lane = lax.broadcasted_iota(jnp.int32, (16, cols), 1)
    for d in range(n_blk):
        slot = ring_at(ring_place(own_blk, n_blk) - d, n_blk)
        slots[d] = slot
        widths[d] = width[sector[slot]]
    for e in range(n_pair):
        tail = tails[e][rows - 16 :].astype(jnp.float32)
        for k in range(terms):
            shift = jnp.max(jnp.where(lane == k, tail, -1e9)).astype(jnp.int32)
            for t in range(n_blk):
                want = sector[slots[t]] - shift
                found = jnp.int32(n_blk)
                for d in range(n_blk):
                    found = jnp.where(sector[slots[d]] == want, d, found)
                src[(t * n_pair + e) * terms + k] = found
    for d in range(n_blk):
        row = left_diag[pl.ds(slots[d], 1), :]
        diag[d] = jnp.transpose(jnp.broadcast_to(row, (diag.shape[2], row.shape[1])))


def diagonal(diag, right_diag, d, h):
    cols = diag.shape[2]
    _, own_op = place_of()
    start = pl.multiple_of((own_op ^ h) * cols, LANES)
    return diag[d] + right_diag[:, pl.ds(start, cols)]


def row_mask(width, shape):
    return lax.broadcasted_iota(jnp.int32, shape, 0) < width


def fold(x):
    return jnp.sum(x.reshape(-1, 8, x.shape[-1]), axis=0)


def whole(x):
    return jnp.sum(jnp.sum(x, axis=0, keepdims=True), axis=1, keepdims=True)


def spread(values, out):
    line = lax.broadcasted_iota(jnp.int32, out.shape[1:], 0)
    tile = jnp.zeros(out.shape[1:], jnp.float32)
    for j, value in enumerate(values):
        tile = jnp.where(line == j, value, tile)
    for d in range(out.shape[0]):
        out[d] = tile


def by_block(packed, terms, k):
    rows, cols = packed.shape
    width = (rows - 16) // terms
    lane = lax.broadcasted_iota(jnp.int32, (width, cols), 1)
    block = packed[k * width : (k + 1) * width].astype(jnp.float32)
    parts = []
    for r in range(cols // width):
        inside = (lane >= r * width) & (lane < (r + 1) * width)
        parts.append(jnp.where(inside, block, 0.0).astype(jnp.bfloat16))
    return jnp.concatenate(parts, axis=0)


def left_products(block, left, inter):
    n_terms, rows, cols = inter.shape
    at = 0
    while at < n_terms:
        ops = left(at)
        terms = ops.shape[0]
        prod = jnp.dot(ops.reshape(terms * rows, rows), block, preferred_element_type=jnp.float32)
        inter[at : at + terms] = prod.astype(jnp.bfloat16).reshape(terms, rows, cols)
        at += terms


def sum_terms(src, widths, inter, right, out, emit):
    n_blk, n_terms, _, _ = inter.shape
    n_blk -= 1
    terms = n_terms // len(right)
    turned = [by_block(right[j // terms], terms, j % terms) for j in range(n_terms)]
    for t in range(n_blk):
        total = None
        for j in range(n_terms):
            part = jnp.dot(
                inter[src[t * n_terms + j], j], turned[j], preferred_element_type=jnp.float32
            )
            total = part if total is None else total + part
        total = jnp.where(row_mask(widths[t], total.shape), total, 0.0)
        out[t] = total.astype(jnp.bfloat16)
        emit(t, total)


def keep(left, left_out, sems):
    copies = []
    for d, line in enumerate(left):
        for e, ref in enumerate(line):
            copies.append(pltpu.make_async_copy(ref, left_out.at[d, e], sems.at[d * len(line) + e]))
            copies[-1].start()
    return copies


def masked(psi, width, out):
    at = 0
    for ref in psi:
        block = ref[...].astype(jnp.float32)
        block = jnp.where(row_mask(width, block.shape), block, 0.0)
        out[:, at : at + block.shape[1]] = block.astype(jnp.bfloat16)
        at += block.shape[1]


def take(refs, counts):
    out = []
    for count in counts:
        out.append(refs[:count])
        refs = refs[count:]
    return out, refs


def products_of(psi, left, widths, first, raw_out, inter):
    for d, line in enumerate(left):
        masked(psi[d], widths[first + d], raw_out.at[d])
        terms = line[0].shape[0]
        left_products(raw_out[d], lambda at: line[at // terms][...], inter.at[d])


def early_body(n_pair, counts, widths, *refs):
    left, refs = take(refs, [n_pair] * len(counts))
    psi, (raw_out, inter_out, left_out, sems) = take(refs, counts)
    copies = keep(left, left_out, sems)
    products_of(psi, left, widths, 0, raw_out, inter_out)
    for copy in copies:
        copy.wait()


def first_body(n_blk, n_pair, counts, src, widths, *refs):
    n_late = len(counts)
    n_early = n_blk - n_late
    left, refs = take(refs, [n_pair] * n_late)
    (right,), refs = take(refs, [n_pair])
    psi, refs = take(refs, counts)
    raw_in, inter_in, diag, right_diag, part_out, raw_out, left_out, dots_out, inter, sems = refs
    copies = keep(left, left_out, sems)
    for j, (given, own) in enumerate(((inter_in, inter), (raw_in, raw_out))):
        copies.append(
            pltpu.make_async_copy(given, own.at[:n_early], sems.at[n_late * n_pair + j])
        )
        copies[-1].start()
    inter[n_blk] = jnp.zeros_like(inter[n_blk])
    products_of(
        psi, left, widths, n_early, raw_out.at[n_early:], inter.at[n_early:n_blk]
    )
    for copy in copies:
        copy.wait()
    cols = diag.shape[2]
    zero = jnp.zeros((8, cols), jnp.float32)
    sums = [zero, zero]

    def emit(d, total):
        for h in range(2):
            part = slice(h * cols, (h + 1) * cols)
            raw = raw_out[d, :, part].astype(jnp.float32)
            image = total[:, part]
            if h == 0:
                image = image + diagonal(diag, right_diag, d, h) * raw
                sums[0] = sums[0] + fold(raw * raw)
            sums[1] = sums[1] + fold(raw * image)

    sum_terms(src, widths, inter, right, part_out, emit)
    spread([whole(x) for x in sums], dots_out)


def send_rows(sends, j, d, h, block):
    _, own_op = place_of()
    step, cols = sends[0].shape[2], block.shape[1]
    for e, send in enumerate(sends):
        start = pl.multiple_of((own_op ^ (2 * e)) * step, step)
        send[j, d, :, h * cols : (h + 1) * cols] = block[pl.ds(start, step)].astype(send.dtype)


def total_of(mine, other, d, h, cols):
    own = mine[d, :, h * cols : (h + 1) * cols].astype(jnp.float32)
    return own + other[d, :, (1 - h) * cols : (2 - h) * cols].astype(jnp.float32)


def sigma_body(mine, other, raw_in, diag, right_diag, sig_out, *sends):
    n_blk, _, cols = diag.shape
    for d in range(n_blk):
        for h in range(2):
            part = slice(h * cols, (h + 1) * cols)
            raw = raw_in[d, :, part].astype(jnp.float32)
            sigma = total_of(mine, other, d, h, cols) + diagonal(diag, right_diag, d, h) * raw
            sig_out[d, :, part] = sigma
            send_rows(sends, 0, d, h, raw_in.at[d, :, part])
            send_rows(sends, 1, d, h, sig_out.at[d, :, part])


def norm_theta(parts, count):
    tot = jnp.sum(parts, axis=0) * (1.0 / count)
    scale = lax.rsqrt(tot[0:1] + EPS)
    return scale, tot[1:2] * scale * scale


def second_body(n_blk, n_pair, count, src, widths, left_early, left_late, *refs):
    right, refs = refs[:n_pair], refs[n_pair:]
    parts, raw_in, sig_in, diag, right_diag, f_out, part_out, dots_out = refs[:8]
    inter, corr, held, sems = refs[8:]
    copies = []
    n_early = left_early.shape[0]
    for d in range(n_blk):
        kept = left_early.at[d] if d < n_early else left_late.at[d - n_early]
        copies.append(pltpu.make_async_copy(kept, held.at[d], sems.at[d]))
        copies[-1].start()
    inter[n_blk] = jnp.zeros_like(inter[n_blk])
    scale, theta = norm_theta(parts[...], count)
    cols = diag.shape[2]
    halves = []
    for h in range(2):
        part = slice(h * cols, (h + 1) * cols)
        vv = vc = vs = jnp.zeros((8, cols), jnp.float32)
        for d in range(n_blk):
            vec = raw_in[d, :, part].astype(jnp.float32) * scale
            sigma = sig_in[d, :, part] * scale
            den = diagonal(diag, right_diag, d, h) - theta
            item = (sigma - theta * vec) * den / jnp.maximum(den * den, 0.25)
            corr[d, :, part] = item
            vv, vc, vs = vv + fold(vec * vec), vc + fold(vec * item), vs + fold(vec * sigma)
        halves.append((whole(vv), whole(vc), whole(vs)))
    along = (halves[0][1] + halves[1][1]) / jnp.maximum(halves[0][0] + halves[1][0], 1e-30)
    terms = held.shape[2]
    for d in range(n_blk):
        for h in range(2):
            part = slice(h * cols, (h + 1) * cols)
            vec = raw_in[d, :, part].astype(jnp.float32) * scale
            f_out[d, :, part] = (corr[d, :, part] - along * vec).astype(jnp.bfloat16)
        copies[d].wait()
        left_products(f_out[d], lambda at: held[d, at // terms], inter.at[d])
    zero = jnp.zeros((8, cols), jnp.float32)
    sums = [zero for _ in range(5)]

    def emit(d, total):
        for h in range(2):
            part = slice(h * cols, (h + 1) * cols)
            fld = f_out[d, :, part].astype(jnp.float32)
            vec = raw_in[d, :, part].astype(jnp.float32) * scale
            image = total[:, part]
            if h == 0:
                image = image + diagonal(diag, right_diag, d, h) * fld
                for j, prod in enumerate((fld * fld, vec * fld, fld * sig_in[d, :, part] * scale)):
                    sums[j] = sums[j] + fold(prod)
            sums[3] = sums[3] + fold(vec * image)
            sums[4] = sums[4] + fold(fld * image)

    sum_terms(src, widths, inter, right, part_out, emit)
    spread(list(halves[0]) + [along] + [whole(x) for x in sums], dots_out)


def image_body(mine, other, f_in, diag, right_diag, *sends):
    n_blk, _, cols = diag.shape
    sends, image = sends[:-1], sends[-1]
    for d in range(n_blk):
        for h in range(2):
            part = slice(h * cols, (h + 1) * cols)
            fld = f_in[d, :, part].astype(jnp.float32)
            image[h] = total_of(mine, other, d, h, cols) + diagonal(diag, right_diag, d, h) * fld
            send_rows(sends, 0, d, h, f_in.at[d, :, part])
            send_rows(sends, 1, d, h, image.at[h])


def ritz_pair(theta, h_mix, h_two):
    diff, twice = theta - h_two, 2.0 * h_mix
    size = jnp.sqrt(diff * diff + twice * twice)
    some = size > 0.0
    safe = jnp.where(some, size, 1.0)
    big = jnp.sqrt(0.5 + 0.5 * jnp.abs(diff) / safe)
    small = 0.5 * jnp.abs(twice) / (safe * big)
    sine = jnp.where(diff >= 0.0, small, big)
    cosine = jnp.where(diff >= 0.0, big, small)
    sine = jnp.where(some, sine, 0.0)
    cosine = jnp.where(some, cosine, 1.0)
    upward = (twice > 0.0) | ((twice == 0.0) & (diff < 0.0))
    return sine, jnp.where(upward, -cosine, cosine), 0.5 * (theta + h_two) - 0.5 * size


def third_body(n_blk, n_op, count, slots, parts1, parts2, *refs):
    n_pair = n_op // 2
    got1, got2 = refs[:n_pair], refs[n_pair : 2 * n_pair]
    new_out, res_out, energy_out = refs[2 * n_pair :]
    cols = new_out.shape[2] // n_op
    own_blk, own_op = place_of()
    scale, theta = norm_theta(parts1[...], count)
    vv, vc, vs, local, ff, vf, fs, vt, ft = (parts2[:, j, :] for j in range(9))

    def mean(x):
        return jnp.sum(x, axis=0, keepdims=True) * (1.0 / count)

    along = mean(vc)
    beta = local - along
    norm_sq = mean(ff + 2.0 * beta * vf + beta * beta * vv)
    unit = lax.rsqrt(jnp.maximum(norm_sq, 0.0) + EPS)
    v_s1 = unit * mean(vt + beta * vs)
    u_s0 = unit * mean(fs + beta * vs)
    u_s1 = unit * unit * mean(ft + beta * (vt + fs) + beta * beta * vs)
    cv, cu, energy = ritz_pair(theta, 0.5 * (v_s1 + u_s0), u_s1)
    energy_out[0] = jnp.max(energy)
    cu = cu * unit
    for e in range(n_pair):
        there = own_op ^ (2 * e)
        back = parts2[own_blk * n_op + there][3:4] - along
        on_vec = (cv + cu * back) * scale
        for h in range(2):
            at = pl.multiple_of((there ^ h) * cols, LANES)
            part = slice(h * cols, (h + 1) * cols)
            for d in range(n_blk):
                blocks = (got[e][j, d, :, part] for got in (got1, got2) for j in range(2))
                raw, sigma, fld, image = (block.astype(jnp.float32) for block in blocks)
                newvec = on_vec * raw + cu * fld
                res = on_vec * sigma + cu * image - energy * newvec
                new_out[slots[d], :, pl.ds(at, cols)] = newvec.astype(jnp.bfloat16)
                res_out[slots[d], :, pl.ds(at, cols)] = res.astype(jnp.bfloat16)


def per_device(
    psi, left_ops, right_ops, term_shift, slot_sector, sector_width, diag_left, diag_right
):
    n_blk, n_op = lax.axis_size("blk"), lax.axis_size("op")
    _, rows, ncols = psi.shape
    terms, _, width, _ = right_ops.shape
    n_pair = n_op // 2
    cols = diag_right.shape[0] // n_op
    step = rows // n_op
    count = float(n_blk * rows * ncols)
    n_dev = n_blk * n_op
    bf16, f32, i32 = jnp.bfloat16, jnp.float32, jnp.int32
    last = sorted(range(1, n_blk), key=lambda d: min(d, n_blk - d))[-1]

    def pack():
        first = swap(term_shift, 1, n_op)
        sent = kernel(
            functools.partial(pack_body, n_blk, n_op),
            [(term_shift, SMEM), (first, SMEM), (psi, HBM), (right_ops, HBM)],
            [((rows, 2 * cols if d in (0, last) else cols), bf16, VMEM) for d in range(n_blk)]
            + [((terms * width + 16, 2 * cols), bf16, VMEM)] * n_pair,
            [pltpu.VMEM(right_ops.shape, bf16), pltpu.SemaphoreType.DMA((2 * n_blk + 1,))],
            nbytes=1 << 20,
        )
        return sent[:n_blk], sent[n_blk:]

    def table(right):
        return kernel(
            functools.partial(table_body, n_blk, terms),
            [(slot_sector, SMEM), (sector_width, SMEM), (diag_left, VMEM)]
            + [(block, VMEM) for block in right],
            [((n_blk * n_pair * terms,), i32, SMEM)]
            + [((n_blk,), i32, SMEM)] * 2
            + [((n_blk, rows, LANES), f32, VMEM)],
        )

    def inputs(left, psi, those):
        blocks = [left[d, 2 * e] for d in those for e in range(n_pair)]
        halves = [half for d in those for half in psi[d]]
        return [(x, VMEM) for x in blocks], [(x, VMEM) for x in halves], [len(psi[d]) for d in those]

    def early(left, psi, n_early, tables):
        left_ins, psi_ins, counts = inputs(left, psi, range(n_early))
        return kernel(
            functools.partial(early_body, n_pair, counts),
            [(tables[1], SMEM)] + left_ins + psi_ins,
            [
                ((n_early, rows, 2 * cols), bf16, VMEM),
                ((n_early, n_pair * terms, rows, 2 * cols), bf16, VMEM),
                ((n_early, n_pair, terms, rows, rows), bf16, HBM),
            ],
            [pltpu.SemaphoreType.DMA((n_early * n_pair,))],
            flops=2 * n_early * rows * rows * 2 * cols * terms * n_pair,
            nbytes=4 << 20,
        )

    left, psi_by, right, (src, widths, slots, diag), (raw_early, inter_early, left_early) = gather(
        left_ops[:, 0], n_blk, n_op, pack, table, early
    )
    n_early = raw_early.shape[0]
    n_late = n_blk - n_early
    left_ins, psi_ins, counts = inputs(left, psi_by, range(n_early, n_blk))
    right_ins = [(block, VMEM) for block in right]
    diags = [(diag, VMEM), (diag_right[None], VMEM)]

    tables = [(src, SMEM), (widths, SMEM)]
    narrow = ((n_blk, rows, 2 * cols), bf16, VMEM)
    wide = ((n_blk, rows, 2 * cols), f32, VMEM)
    sends = [((2, n_blk, step, 2 * cols), bf16, VMEM)] * n_pair
    inter = pltpu.VMEM((n_blk + 1, n_pair * terms, rows, 2 * cols), bf16)
    left_late = (n_late, n_pair, terms, rows, rows)
    cost = dict(flops=2 * n_blk * rows * 2 * cols * terms * n_pair * (rows + 2 * cols), nbytes=6 << 20)

    def totals(parts):
        return lax.all_to_all(parts, ("blk", "op"), 0, 0, tiled=True)

    def exchange(out):
        return [out[0]] + [swap(block, 2 * e, n_op) for e, block in enumerate(out[1:], 1)]

    part1, raw, kept, dots1 = kernel(
        functools.partial(first_body, n_blk, n_pair, counts),
        tables + left_ins + right_ins + psi_ins + [(raw_early, VMEM), (inter_early, VMEM)] + diags,
        [narrow, narrow, (left_late, bf16, HBM), ((n_dev, 8, LANES), f32, VMEM)],
        [inter, pltpu.SemaphoreType.DMA((n_late * n_pair + 2,))],
        **cost,
    )
    parts1 = totals(dots1)
    sig, *out1 = kernel(
        sigma_body,
        [(x, VMEM) for x in (part1, swap(part1, 1, n_op), raw)] + diags,
        [wide] + sends,
        nbytes=4 << 20,
    )
    parts1, sig, got1 = lax.optimization_barrier((parts1, sig, exchange(out1)))
    fld, part2, dots2 = kernel(
        functools.partial(second_body, n_blk, n_pair, count),
        tables + [(left_early, HBM), (kept, HBM)] + right_ins
        + [(x, VMEM) for x in (parts1, raw, sig)] + diags,
        [narrow, narrow, ((n_dev, 16, LANES), f32, VMEM)],
        [
            inter,
            pltpu.VMEM((n_blk, rows, 2 * cols), f32),
            pltpu.VMEM((n_blk, *left_late[1:]), bf16),
            pltpu.SemaphoreType.DMA((n_blk,)),
        ],
        **cost,
    )
    parts2 = totals(dots2)
    out2 = kernel(
        image_body,
        [(x, VMEM) for x in (part2, swap(part2, 1, n_op), fld)] + diags,
        sends,
        [pltpu.VMEM((2, rows, cols), f32)],
        nbytes=4 << 20,
    )
    got2 = exchange(out2)
    final = ((n_blk, step, n_op * cols), bf16, VMEM)
    new, res, energy = kernel(
        functools.partial(third_body, n_blk, n_op, count),
        [(slots, SMEM)] + [(x, VMEM) for x in (parts1, parts2, *got1, *got2)],
        [final, final, ((1,), f32, SMEM)],
        nbytes=4 << 20,
    )
    return new, res, energy


def solution(mesh):
    placed = (
        P(("grp", "blk"), None, None),
        P("op", ("grp", "blk"), None, None),
        P("op", ("grp", "blk"), None, None),
        P("op"),
        P("grp"),
        P("grp"),
        P("grp", None),
        P(("grp", "blk")),
    )

    def body(*args):
        psi, left_ops, right_ops, diag_right = args[0], args[1], args[2], args[7]
        n_op = mesh.shape["op"]
        cols = diag_right.shape[0] // n_op
        fits = (
            psi.shape[0] == 1
            and diag_right.shape[0] % n_op == 0
            and cols == LANES
            and n_op % 2 == 0
            and cols % right_ops.shape[2] == 0
            and cols // right_ops.shape[2] * n_op == right_ops.shape[1]
            and psi.shape[1] % (16 * n_op) == 0
            and n_op & (n_op - 1) == 0
            and mesh.shape["blk"] > n_op.bit_length() - 1
        )
        return (per_device if fits else per_device_general)(*args)

    return jax.shard_map(
        body,
        mesh=mesh,
        in_specs=placed,
        out_specs=(P("grp", "op", "blk"), P("grp", "op", "blk"), P("grp")),
        check_vma=False,
    )
```

```python
import functools

import jax
import jax.numpy as jnp
from jax import lax
from jax.experimental import pallas as pl
from jax.experimental.pallas import tpu as pltpu
from jax.sharding import PartitionSpec as P

EPS = 1e-06
LANES = 128
VMEM_LIMIT = 20 * 1024 * 1024


def per_device_general(
    psi, left_ops, right_ops, term_shift, slot_sector, sector_width, diag_left, diag_right
):
    sec_dev, rows, ncols = psi.shape
    nsec = slot_sector.shape[0]
    terms_dev = left_ops.shape[0]
    right_local = right_ops.shape[1]
    right_width = right_ops.shape[2]
    local_cols = diag_right.shape[0]
    count = float(nsec * rows * ncols)
    match = slot_sector[:, None] == jnp.arange(nsec)[None, :]
    widths = jnp.sum(jnp.where(match, sector_width[None, :], 0), axis=1)
    mask_all = (jnp.arange(rows)[None, :] < widths[:, None]).astype(jnp.float32)
    own_mask = lax.dynamic_slice_in_dim(mask_all, lax.axis_index("blk") * sec_dev, sec_dev, 0)
    raw = psi.astype(jnp.float32) * own_mask[:, :, None]
    squares = lax.psum(jnp.sum(raw * raw), "blk")
    v_left = (raw * lax.rsqrt(squares / count + EPS)).astype(jnp.bfloat16)
    onehots = (
        slot_sector[None, None, :] == slot_sector[None, :, None] - term_shift[:, None, None]
    ).astype(jnp.bfloat16)
    op_rows = rows // lax.axis_size("op")
    op_start = lax.axis_index("op") * op_rows
    dmat = diag_left[:, :, None] + diag_right[None, None, :]

    def left_local(field):
        return jnp.einsum(
            "ksij,sjc->ksic", left_ops, field, preferred_element_type=jnp.float32
        ).astype(jnp.bfloat16)

    def right_part(moved_in):
        flat = moved_in.reshape(terms_dev, nsec, rows * local_cols)
        shifted = jnp.einsum(
            "kts,ksx->ktx", onehots, flat, preferred_element_type=jnp.float32
        ).astype(jnp.bfloat16)
        shifted = shifted.reshape(terms_dev, nsec, rows, right_local, right_width)
        accum = jnp.einsum(
            "ktwrc,krdc->twrd", shifted, right_ops, preferred_element_type=jnp.float32
        )
        return accum.reshape(nsec, rows, local_cols) * mask_all[:, :, None]

    def op_total(partial_value):
        return lax.psum(partial_value.astype(jnp.bfloat16), "op").astype(jnp.float32)

    def final_rows(array):
        return lax.dynamic_slice_in_dim(array, op_start, op_rows, 1)

    def reduce_dots(values):
        sums = lax.psum(values, "blk")
        return tuple((item / count for item in sums))

    moved_first, v_moved = (
        lax.all_to_all(left_local(v_left), "blk", split_axis=3, concat_axis=1, tiled=True),
        lax.all_to_all(v_left[None], "blk", split_axis=3, concat_axis=1, tiled=True),
    )
    v_right = v_moved[0]
    vec32 = v_right.astype(jnp.float32)
    first_sigma = op_total(right_part(moved_first)) + dmat * vec32
    theta = reduce_dots((jnp.sum(vec32 * first_sigma),))[0]
    resid = first_sigma - theta * vec32
    den = dmat - theta
    corr = resid * den / jnp.maximum(den * den, 0.25)
    along = reduce_dots((jnp.sum(vec32 * corr),))[0]
    orth = corr - along * vec32
    norm_sq = reduce_dots((jnp.sum(orth * orth),))[0]
    update = (orth * lax.rsqrt(norm_sq + EPS)).astype(jnp.bfloat16)
    upd32 = update.astype(jnp.float32)
    upd_left = lax.all_to_all(update, "blk", split_axis=0, concat_axis=2, tiled=True)
    moved_second = lax.all_to_all(
        left_local(upd_left), "blk", split_axis=3, concat_axis=1, tiled=True
    )
    second_sigma = op_total(right_part(moved_second)) + dmat * upd32
    v_s1, u_s0, u_s1 = reduce_dots(
        (jnp.sum(vec32 * second_sigma), jnp.sum(upd32 * first_sigma), jnp.sum(upd32 * second_sigma))
    )
    h_mix = 0.5 * (v_s1 + u_s0)
    coef_v, coef_u, energy = ritz(theta, h_mix, u_s1)
    newvec = coef_v * vec32 + coef_u * upd32
    image = coef_v * first_sigma + coef_u * second_sigma
    new_out = final_rows(newvec.astype(jnp.bfloat16))
    res_out = final_rows((image - energy * newvec).astype(jnp.bfloat16))
    return (new_out, res_out, jnp.reshape(energy, (1,)))


def ritz(theta, h_mix, h_two):
    angle = 0.5 * jnp.arctan2(2.0 * h_mix, theta - h_two)
    sine = jnp.sin(angle)
    flip = jnp.where(sine > 0, -1.0, 1.0)
    coef_v = -sine * flip
    coef_u = jnp.cos(angle) * flip
    half = 0.5 * (theta - h_two)
    energy = 0.5 * (theta + h_two) - jnp.sqrt(half * half + h_mix * h_mix)
    return coef_v, coef_u, energy


VMEM, SMEM, HBM = pltpu.VMEM, pltpu.SMEM, pltpu.HBM


def kernel(body, ins, outs, scratch=(), flops=0, nbytes=0):
    return pl.pallas_call(
        body,
        out_shape=[
            HBM(shape, dtype) if space == HBM else jax.ShapeDtypeStruct(shape, dtype)
            for shape, dtype, space in outs
        ],
        in_specs=[pl.BlockSpec(memory_space=space) for _, space in ins],
        out_specs=[pl.BlockSpec(memory_space=space) for _, _, space in outs],
        scratch_shapes=list(scratch),
        compiler_params=pltpu.CompilerParams(vmem_limit_bytes=VMEM_LIMIT),
        cost_estimate=pl.CostEstimate(flops=flops, bytes_accessed=nbytes, transcendentals=0),
    )(*[pltpu.with_memory_space_constraint(x, HBM) if space == HBM else x for x, space in ins])


def ring_at(place, n_blk):
    place = place % n_blk if isinstance(place, int) else lax.rem(place + n_blk, n_blk)
    odd, even = 2 * place - 1, 2 * (n_blk - place)
    if isinstance(place, int):
        return 0 if place == 0 else odd if odd < n_blk else even
    return jnp.where(place == 0, 0, jnp.where(odd < n_blk, odd, even))


def ring_place(index, n_blk):
    odd, even = (index + 1) // 2, lax.rem(n_blk - index // 2, n_blk)
    return jnp.where(lax.rem(index, 2) == 1, odd, even)


def onward(block, d, n_blk):
    pairs = [(ring_at(i, n_blk), ring_at(i + d, n_blk)) for i in range(n_blk)]
    return lax.ppermute(block, "blk", pairs)


def swap(block, e, n_op):
    return lax.ppermute(block, "op", [(i, i ^ e) for i in range(n_op)])


def gather(own, n_blk, n_op, pack, table, early):
    bits = [1 << b for b in reversed(range(1, n_op.bit_length() - 1))]
    order = sorted(range(1, n_blk), key=lambda d: min(d, n_blk - d))
    left, psi, right, tables, columns = {(0, 0): own}, {}, None, None, None
    waiting, late, made = {(0, 0): 0}, None, None
    for j in range(n_blk + len(bits)):
        new, moved = {}, {}
        for (d, e), done in waiting.items():
            if e == 0 and d + 1 < n_blk:
                new[d + 1, 0] = onward(left[d, 0], 1, n_blk), 0
            for b in range(done, len(bits)):
                new[d, e ^ bits[b]] = swap(left[d, e], bits[b], n_op), b + 1
        kept = {key: block for key, (block, _) in new.items()}
        if late is not None:
            moved["psi"] = late
        if j == 0:
            columns, packed = pack()
            moved["right"] = [packed[0]]
            moved["right"] += [swap(part, 2 * e, n_op) for e, part in enumerate(packed[1:], 1)]
        if j == 1:
            moved["tables"] = table(right)
        if j == n_blk - 1 and j >= len(bits) + 1:
            n_early = min(2, n_blk - 1)
            psi[0] = [columns[0]]
            moved["early"] = early(left, psi, n_early, tables)
        if 2 <= j < n_blk:
            moved["other"] = swap(psi[order[j - 2]][0], 1, n_op)
        late = onward(columns[order[j]], order[j], n_blk) if j < n_blk - 1 else None
        if not kept and not moved:
            break
        waiting = {key: done for key, (_, done) in new.items()}
        kept, moved = lax.optimization_barrier((kept, moved))
        left.update(kept)
        right, tables = moved.get("right", right), moved.get("tables", tables)
        made = moved.get("early", made)
        if "psi" in moved:
            psi[order[j - 1]] = [moved["psi"]]
        if "other" in moved:
            psi[order[j - 2]].append(moved["other"])
    return left, psi, right, tables, made


def place_of():
    return lax.axis_index("blk"), lax.axis_index("op")


def pack_body(n_blk, n_op, shift, _, psi, right_in, *outs):
    n_pair = n_op // 2
    psi_out, right_out, right, sems = outs[:n_blk], outs[n_blk : n_blk + n_pair], outs[-2], outs[-1]
    terms, local, width, _ = right.shape
    cols = local * width // n_op
    per = cols // width
    own_blk, own_op = place_of()
    fetch = pltpu.make_async_copy(right_in, right, sems.at[2 * n_blk])
    fetch.start()
    copies = []
    for d in range(n_blk):
        there = ring_at(ring_place(own_blk, n_blk) + d, n_blk) * n_op
        for h in range(psi_out[d].shape[1] // cols):
            start = pl.multiple_of((there + (own_op ^ h)) * cols, LANES)
            copy = pltpu.make_async_copy(
                psi.at[0, :, pl.ds(start, cols)],
                psi_out[d].at[:, h * cols : (h + 1) * cols],
                sems.at[2 * d + h],
            )
            copy.start()
            copies.append(copy)
    lane = lax.broadcasted_iota(jnp.int32, (16, 2 * cols), 1)
    line = jnp.zeros((16, 2 * cols), jnp.float32)
    for k in range(terms):
        line = jnp.where(lane == k, shift[k].astype(jnp.float32), line)
    square = [lax.broadcasted_iota(jnp.int32, (width, width), axis) for axis in (0, 1)]
    unit = (square[0] == square[1]).astype(jnp.bfloat16)
    fetch.wait()
    for e in range(n_pair):
        for k in range(terms):
            turned = []
            for h in range(2):
                first = (own_op ^ (2 * e) ^ h) * per
                for r in range(per):
                    turned.append(
                        lax.dot_general(
                            right[k, first + r], unit, (((0,), (0,)), ((), ())),
                            preferred_element_type=jnp.float32,
                        )
                    )
            side_by_side = jnp.concatenate(turned, axis=1).astype(jnp.bfloat16)
            right_out[e][k * width : (k + 1) * width] = side_by_side
        right_out[e][terms * width :] = line.astype(jnp.bfloat16)
    for copy in copies:
        copy.wait()


def table_body(n_blk, terms, sector, width, left_diag, right_diag, *refs):
    tails, src, widths, slots, diag, right_out = refs[:-5], *refs[-5:]
    right_out[...] = right_diag[...]
    n_pair = len(tails)
    rows, cols = tails[0].shape
    own_blk, _ = place_of()
    lane = lax.broadcasted_iota(jnp.int32, (16, cols), 1)
    for d in range(n_blk):
        slot = ring_at(ring_place(own_blk, n_blk) - d, n_blk)
        slots[d] = slot
        widths[d] = width[sector[slot]]
    for e in range(n_pair):
        tail = tails[e][rows - 16 :].astype(jnp.float32)
        for k in range(terms):
            shift = jnp.max(jnp.where(lane == k, tail, -1e9)).astype(jnp.int32)
            for t in range(n_blk):
                want = sector[slots[t]] - shift
                found = jnp.int32(n_blk)
                for d in range(n_blk):
                    found = jnp.where(sector[slots[d]] == want, d, found)
                src[(t * n_pair + e) * terms + k] = found
    for d in range(n_blk):
        row = left_diag[pl.ds(slots[d], 1), :]
        diag[d] = jnp.transpose(jnp.broadcast_to(row, (diag.shape[2], row.shape[1])))


def diagonal(diag, right_diag, d, h):
    cols = diag.shape[2]
    _, own_op = place_of()
    start = pl.multiple_of((own_op ^ h) * cols, LANES)
    return diag[d] + right_diag[:, pl.ds(start, cols)]


def row_mask(width, shape):
    return lax.broadcasted_iota(jnp.int32, shape, 0) < width


def fold(x):
    return jnp.sum(x.reshape(-1, 8, x.shape[-1]), axis=0)


def whole(x):
    return jnp.sum(jnp.sum(x, axis=0, keepdims=True), axis=1, keepdims=True)


def spread(values, out):
    line = lax.broadcasted_iota(jnp.int32, out.shape[1:], 0)
    tile = jnp.zeros(out.shape[1:], jnp.float32)
    for j, value in enumerate(values):
        tile = jnp.where(line == j, value, tile)
    for d in range(out.shape[0]):
        out[d] = tile


def by_block(packed, terms, k):
    rows, cols = packed.shape
    width = (rows - 16) // terms
    lane = lax.broadcasted_iota(jnp.int32, (width, cols), 1)
    block = packed[k * width : (k + 1) * width].astype(jnp.float32)
    parts = []
    for r in range(cols // width):
        inside = (lane >= r * width) & (lane < (r + 1) * width)
        parts.append(jnp.where(inside, block, 0.0).astype(jnp.bfloat16))
    return jnp.concatenate(parts, axis=0)


def left_products(block, left, inter):
    n_terms, rows, cols = inter.shape
    at = 0
    while at < n_terms:
        ops = left(at)
        terms = ops.shape[0]
        prod = jnp.dot(ops.reshape(terms * rows, rows), block, preferred_element_type=jnp.float32)
        inter[at : at + terms] = prod.astype(jnp.bfloat16).reshape(terms, rows, cols)
        at += terms


def sum_terms(src, widths, inter, right, out, emit):
    n_blk, n_terms, _, _ = inter.shape
    n_blk -= 1
    terms = n_terms // len(right)
    turned = [by_block(right[j // terms], terms, j % terms) for j in range(n_terms)]
    for t in range(n_blk):
        total = None
        for j in range(n_terms):
            part = jnp.dot(
                inter[src[t * n_terms + j], j], turned[j], preferred_element_type=jnp.float32
            )
            total = part if total is None else total + part
        total = jnp.where(row_mask(widths[t], total.shape), total, 0.0)
        out[t] = total.astype(jnp.bfloat16)
        emit(t, total)


def keep(left, left_out, sems):
    copies = []
    for d, line in enumerate(left):
        for e, ref in enumerate(line):
            copies.append(pltpu.make_async_copy(ref, left_out.at[d, e], sems.at[d * len(line) + e]))
            copies[-1].start()
    return copies


def masked(psi, width, out):
    at = 0
    for ref in psi:
        block = ref[...].astype(jnp.float32)
        block = jnp.where(row_mask(width, block.shape), block, 0.0)
        out[:, at : at + block.shape[1]] = block.astype(jnp.bfloat16)
        at += block.shape[1]


def take(refs, counts):
    out = []
    for count in counts:
        out.append(refs[:count])
        refs = refs[count:]
    return out, refs


def products_of(psi, left, widths, first, raw_out, inter):
    for d, line in enumerate(left):
        masked(psi[d], widths[first + d], raw_out.at[d])
        terms = line[0].shape[0]
        left_products(raw_out[d], lambda at: line[at // terms][...], inter.at[d])


def early_body(n_pair, counts, widths, *refs):
    left, refs = take(refs, [n_pair] * len(counts))
    psi, (raw_out, inter_out, left_out, sems) = take(refs, counts)
    copies = keep(left, left_out, sems)
    products_of(psi, left, widths, 0, raw_out, inter_out)
    for copy in copies:
        copy.wait()


def first_body(n_blk, n_pair, counts, src, widths, *refs):
    n_late = len(counts)
    n_early = n_blk - n_late
    left, refs = take(refs, [n_pair] * n_late)
    (right,), refs = take(refs, [n_pair])
    psi, refs = take(refs, counts)
    raw_in, inter_in, diag, right_diag, part_out, raw_out, left_out, dots_out = refs[:8]
    sends, (inter, sems) = refs[8:-2], refs[-2:]
    copies = keep(left, left_out, sems)
    for j, (given, own) in enumerate(((inter_in, inter), (raw_in, raw_out))):
        copies.append(
            pltpu.make_async_copy(given, own.at[:n_early], sems.at[n_late * n_pair + j])
        )
        copies[-1].start()
    inter[n_blk] = jnp.zeros_like(inter[n_blk])
    products_of(
        psi, left, widths, n_early, raw_out.at[n_early:], inter.at[n_early:n_blk]
    )
    for copy in copies:
        copy.wait()
    cols = diag.shape[2]
    zero = jnp.zeros((8, cols), jnp.float32)
    sums = [zero, zero]

    def emit(d, total):
        for h in range(2):
            part = slice(h * cols, (h + 1) * cols)
            raw = raw_out[d, :, part].astype(jnp.float32)
            image = total[:, part]
            if h == 0:
                image = image + diagonal(diag, right_diag, d, h) * raw
                sums[0] = sums[0] + fold(raw * raw)
            sums[1] = sums[1] + fold(raw * image)
        for e, send in enumerate(sends, 2):
            send_rows(e, send, d, raw_out, part_out)

    sum_terms(src, widths, inter, right, part_out, emit)
    spread([whole(x) for x in sums], dots_out)


def send_rows(e, send, d, field, part):
    _, own_op = place_of()
    step = send.shape[2]
    rows = pl.ds(pl.multiple_of((own_op ^ e) * step, step), step)
    if e % 2 == 0:
        send[0, d] = field[d, rows].astype(send.dtype)
    send[send.shape[0] - 1, d] = part[d, rows]


def total_of(mine, other, d, h, cols):
    own = mine[d, :, h * cols : (h + 1) * cols].astype(jnp.float32)
    return own + other[d, :, (1 - h) * cols : (2 - h) * cols].astype(jnp.float32)


def norm_theta(parts, count):
    tot = jnp.sum(parts, axis=0) * (1.0 / count)
    scale = lax.rsqrt(tot[0:1] + EPS)
    return scale, tot[1:2] * scale * scale


def second_body(n_blk, n_pair, count, src, widths, left_early, left_late, *refs):
    right, refs = refs[:n_pair], refs[n_pair:]
    parts, raw_in, part_in, other_in, diag, right_diag, dots_out, own_out = refs[:8]
    sends, (inter, corr, sig, fld, part_out, held, sems) = refs[8:-7], refs[-7:]
    copies = []
    n_early = left_early.shape[0]
    for d in range(n_blk):
        kept = left_early.at[d] if d < n_early else left_late.at[d - n_early]
        copies.append(pltpu.make_async_copy(kept, held.at[d], sems.at[d]))
        copies[-1].start()
    inter[n_blk] = jnp.zeros_like(inter[n_blk])
    scale, theta = norm_theta(parts[...], count)
    cols = diag.shape[2]
    halves = []
    for h in range(2):
        part = slice(h * cols, (h + 1) * cols)
        vv = vc = vs = jnp.zeros((8, cols), jnp.float32)
        for d in range(n_blk):
            vec = raw_in[d, :, part].astype(jnp.float32) * scale
            sigma = total_of(part_in, other_in, d, h, cols)
            sigma = (sigma + diagonal(diag, right_diag, d, h) * raw_in[d, :, part].astype(jnp.float32)) * scale
            sig[d, :, part] = sigma
            den = diagonal(diag, right_diag, d, h) - theta
            item = (sigma - theta * vec) * den / jnp.maximum(den * den, 0.25)
            corr[d, :, part] = item
            vv, vc, vs = vv + fold(vec * vec), vc + fold(vec * item), vs + fold(vec * sigma)
        halves.append((whole(vv), whole(vc), whole(vs)))
    along = (halves[0][1] + halves[1][1]) / jnp.maximum(halves[0][0] + halves[1][0], 1e-30)
    terms = held.shape[2]
    for d in range(n_blk):
        for h in range(2):
            part = slice(h * cols, (h + 1) * cols)
            vec = raw_in[d, :, part].astype(jnp.float32) * scale
            fld[d, :, part] = (corr[d, :, part] - along * vec).astype(jnp.bfloat16)
        copies[d].wait()
        left_products(fld[d], lambda at: held[d, at // terms], inter.at[d])
    zero = jnp.zeros((8, cols), jnp.float32)
    sums = [zero for _ in range(5)]

    def emit(d, total):
        for h in range(2):
            part = slice(h * cols, (h + 1) * cols)
            field = fld[d, :, part].astype(jnp.float32)
            vec = raw_in[d, :, part].astype(jnp.float32) * scale
            image = total[:, part]
            if h == 0:
                image = image + diagonal(diag, right_diag, d, h) * field
                for j, prod in enumerate((field * field, vec * field, field * sig[d, :, part])):
                    sums[j] = sums[j] + fold(prod)
            sums[3] = sums[3] + fold(vec * image)
            sums[4] = sums[4] + fold(field * image)
        for e, send in enumerate(sends, 1):
            send_rows(e, send, d, fld, part_out)
        rows = pl.ds(pl.multiple_of(own_op * step, step), step)
        for j, ref in enumerate((raw_in, sig, fld, part_out)):
            own_out[j, d] = ref[d, rows].astype(own_out.dtype)

    _, own_op = place_of()
    step = own_out.shape[2]
    sum_terms(src, widths, inter, right, part_out, emit)
    spread(list(halves[0]) + [whole(x) for x in sums], dots_out)


def ritz_pair(theta, h_mix, h_two):
    diff, twice = theta - h_two, 2.0 * h_mix
    size = jnp.sqrt(diff * diff + twice * twice)
    some = size > 0.0
    safe = jnp.where(some, size, 1.0)
    big = jnp.sqrt(0.5 + 0.5 * jnp.abs(diff) / safe)
    small = 0.5 * jnp.abs(twice) / (safe * big)
    sine = jnp.where(diff >= 0.0, small, big)
    cosine = jnp.where(diff >= 0.0, big, small)
    sine = jnp.where(some, sine, 0.0)
    cosine = jnp.where(some, cosine, 1.0)
    upward = (twice > 0.0) | ((twice == 0.0) & (diff < 0.0))
    return sine, jnp.where(upward, -cosine, cosine), 0.5 * (theta + h_two) - 0.5 * size


def third_body(n_blk, n_op, count, slots, parts1, parts2, diag, right_diag, own, *refs):
    got1, got2 = refs[: n_op - 2], refs[n_op - 2 : 2 * n_op - 3]
    new_out, res_out, energy_out = refs[2 * n_op - 3 :]
    step, cols = new_out.shape[1], new_out.shape[2] // n_op
    own_blk, own_op = place_of()
    scale, theta = norm_theta(parts1[...], count)
    pairs = parts2[...].reshape(n_blk * n_op // 2, 2, *parts2.shape[1:])
    pairs = pairs[:, 0] + pairs[:, 1]
    vv, vc, vs, ff, vf, fs, vt, ft = (pairs[:, j, :] for j in range(8))

    def mean(x):
        return jnp.sum(x, axis=0, keepdims=True) * (1.0 / count)

    def nearest(vv, vc):
        return vc / jnp.maximum(vv, 1e-30)

    along = mean(vc)
    beta = nearest(vv, vc) - along
    norm_sq = mean(ff + 2.0 * beta * vf + beta * beta * vv)
    unit = lax.rsqrt(jnp.maximum(norm_sq, 0.0) + EPS)
    v_s1 = unit * mean(vt + beta * vs)
    u_s0 = unit * mean(fs + beta * vs)
    u_s1 = unit * unit * mean(ft + beta * (vt + fs) + beta * beta * vs)
    cv, cu, energy = ritz_pair(theta, 0.5 * (v_s1 + u_s0), u_s1)
    energy_out[0] = jnp.max(energy)
    cu = cu * unit
    mine = pl.ds(pl.multiple_of(own_op * step, step), step)
    for e in range(0, n_op, 2):
        there = own_blk * n_op + (own_op ^ e)
        pair = parts2[there] + parts2[own_blk * n_op + (own_op ^ e ^ 1)]
        on_vec = cv + cu * (nearest(pair[0:1], pair[1:2]) - along)
        for h in range(2):
            at = pl.multiple_of((own_op ^ e ^ h) * cols, LANES)
            part, crossed = slice(h * cols, (h + 1) * cols), slice((1 - h) * cols, (2 - h) * cols)
            for d in range(n_blk):
                dmat = diag[d, mine] + right_diag[:, pl.ds(at, cols)]
                if e:
                    raw, fld = got1[e - 2][0, d, :, part], got2[e - 1][0, d, :, part]
                    vec = raw.astype(jnp.float32) * scale
                    sigma = got1[e - 2][1, d, :, part].astype(jnp.float32)
                    sigma = sigma + got1[e - 1][0, d, :, crossed].astype(jnp.float32)
                    sigma = sigma * scale + dmat * vec
                    image = got2[e - 1][1, d, :, part].astype(jnp.float32)
                else:
                    raw, sigma, fld, image = (own[j, d, :, part].astype(jnp.float32) for j in range(4))
                    vec = raw * scale
                fld = fld.astype(jnp.float32)
                image = image + got2[e][0, d, :, crossed].astype(jnp.float32) + dmat * fld
                newvec = on_vec * vec + cu * fld
                res = on_vec * sigma + cu * image - energy * newvec
                new_out[slots[d], :, pl.ds(at, cols)] = newvec.astype(jnp.bfloat16)
                res_out[slots[d], :, pl.ds(at, cols)] = res.astype(jnp.bfloat16)


def per_device(
    psi, left_ops, right_ops, term_shift, slot_sector, sector_width, diag_left, diag_right
):
    n_blk, n_op = lax.axis_size("blk"), lax.axis_size("op")
    _, rows, ncols = psi.shape
    terms, _, width, _ = right_ops.shape
    n_pair = n_op // 2
    cols = diag_right.shape[0] // n_op
    step = rows // n_op
    count = float(n_blk * rows * ncols)
    n_dev = n_blk * n_op
    bf16, f32, i32 = jnp.bfloat16, jnp.float32, jnp.int32
    last = sorted(range(1, n_blk), key=lambda d: min(d, n_blk - d))[-1]

    def pack():
        first = swap(term_shift, 1, n_op)
        sent = kernel(
            functools.partial(pack_body, n_blk, n_op),
            [(term_shift, SMEM), (first, SMEM), (psi, HBM), (right_ops, HBM)],
            [((rows, 2 * cols if d in (0, last) else cols), bf16, VMEM) for d in range(n_blk)]
            + [((terms * width + 16, 2 * cols), bf16, VMEM)] * n_pair,
            [pltpu.VMEM(right_ops.shape, bf16), pltpu.SemaphoreType.DMA((2 * n_blk + 1,))],
            nbytes=1 << 20,
        )
        return sent[:n_blk], sent[n_blk:]

    def table(right):
        return kernel(
            functools.partial(table_body, n_blk, terms),
            [(slot_sector, SMEM), (sector_width, SMEM), (diag_left, VMEM), (diag_right[None], VMEM)]
            + [(block, VMEM) for block in right],
            [((n_blk * n_pair * terms,), i32, SMEM)]
            + [((n_blk,), i32, SMEM)] * 2
            + [((n_blk, rows, LANES), f32, VMEM), ((1, n_op * cols), f32, VMEM)],
        )

    def inputs(left, psi, those):
        blocks = [left[d, 2 * e] for d in those for e in range(n_pair)]
        halves = [half for d in those for half in psi[d]]
        return [(x, VMEM) for x in blocks], [(x, VMEM) for x in halves], [len(psi[d]) for d in those]

    def early(left, psi, n_early, tables):
        left_ins, psi_ins, counts = inputs(left, psi, range(n_early))
        return kernel(
            functools.partial(early_body, n_pair, counts),
            [(tables[1], SMEM)] + left_ins + psi_ins,
            [
                ((n_early, rows, 2 * cols), bf16, VMEM),
                ((n_early, n_pair * terms, rows, 2 * cols), bf16, VMEM),
                ((n_early, n_pair, terms, rows, rows), bf16, HBM),
            ],
            [pltpu.SemaphoreType.DMA((n_early * n_pair,))],
            flops=2 * n_early * rows * rows * 2 * cols * terms * n_pair,
            nbytes=4 << 20,
        )

    left, psi_by, right, (src, widths, slots, *both), (raw_early, inter_early, left_early) = gather(
        left_ops[:, 0], n_blk, n_op, pack, table, early
    )
    n_early = raw_early.shape[0]
    n_late = n_blk - n_early
    left_ins, psi_ins, counts = inputs(left, psi_by, range(n_early, n_blk))
    right_ins = [(block, VMEM) for block in right]
    diags = [(x, VMEM) for x in both]

    tables = [(src, SMEM), (widths, SMEM)]
    narrow = ((n_blk, rows, 2 * cols), bf16, VMEM)
    dots = ((n_dev, 8, LANES), f32, VMEM)
    sends = [((2 - e % 2, n_blk, step, 2 * cols), bf16, VMEM) for e in range(1, n_op)]
    inter = pltpu.VMEM((n_blk + 1, n_pair * terms, rows, 2 * cols), bf16)
    left_late = (n_late, n_pair, terms, rows, rows)
    cost = dict(flops=2 * n_blk * rows * 2 * cols * terms * n_pair * (rows + 2 * cols), nbytes=6 << 20)

    def totals(parts):
        return lax.all_to_all(parts, ("blk", "op"), 0, 0, tiled=True)

    part1, raw, kept, dots1, *out1 = kernel(
        functools.partial(first_body, n_blk, n_pair, counts),
        tables + left_ins + right_ins + psi_ins + [(raw_early, VMEM), (inter_early, VMEM)] + diags,
        [narrow, narrow, (left_late, bf16, HBM), dots] + sends[1:],
        [inter, pltpu.SemaphoreType.DMA((n_late * n_pair + 2,))],
        **cost,
    )
    parts1, other1, got1 = lax.optimization_barrier(
        (
            totals(dots1),
            swap(part1, 1, n_op),
            [swap(block, e, n_op) for e, block in enumerate(out1, 2)],
        )
    )
    dots2, own, *out2 = kernel(
        functools.partial(second_body, n_blk, n_pair, count),
        tables + [(left_early, HBM), (kept, HBM)] + right_ins
        + [(x, VMEM) for x in (parts1, raw, part1, other1)] + diags,
        [dots, ((4, n_blk, step, 2 * cols), bf16, VMEM)] + sends,
        [
            inter,
            pltpu.VMEM((n_blk, rows, 2 * cols), f32),
            pltpu.VMEM((n_blk, rows, 2 * cols), f32),
            pltpu.VMEM((n_blk, rows, 2 * cols), bf16),
            pltpu.VMEM((n_blk, rows, 2 * cols), bf16),
            pltpu.VMEM((n_blk, *left_late[1:]), bf16),
            pltpu.SemaphoreType.DMA((n_blk,)),
        ],
        **cost,
    )
    parts2 = totals(dots2)
    got2 = [swap(block, e, n_op) for e, block in enumerate(out2, 1)]
    final = ((n_blk, step, n_op * cols), bf16, VMEM)
    new, res, energy = kernel(
        functools.partial(third_body, n_blk, n_op, count),
        [(slots, SMEM)] + [(x, VMEM) for x in (parts1, parts2)] + diags
        + [(x, VMEM) for x in (own, *got1, *got2)],
        [final, final, ((1,), f32, SMEM)],
        nbytes=4 << 20,
    )
    return new, res, energy


def solution(mesh):
    placed = (
        P(("grp", "blk"), None, None),
        P("op", ("grp", "blk"), None, None),
        P("op", ("grp", "blk"), None, None),
        P("op"),
        P("grp"),
        P("grp"),
        P("grp", None),
        P(("grp", "blk")),
    )

    def body(*args):
        psi, left_ops, right_ops, diag_right = args[0], args[1], args[2], args[7]
        n_op = mesh.shape["op"]
        cols = diag_right.shape[0] // n_op
        fits = (
            psi.shape[0] == 1
            and diag_right.shape[0] % n_op == 0
            and cols == LANES
            and n_op % 2 == 0
            and cols % right_ops.shape[2] == 0
            and cols // right_ops.shape[2] * n_op == right_ops.shape[1]
            and psi.shape[1] % (16 * n_op) == 0
            and n_op & (n_op - 1) == 0
            and mesh.shape["blk"] > n_op.bit_length() - 1
        )
        return (per_device if fits else per_device_general)(*args)

    return jax.shard_map(
        body,
        mesh=mesh,
        in_specs=placed,
        out_specs=(P("grp", "op", "blk"), P("grp", "op", "blk"), P("grp")),
        check_vma=False,
    )
```

```python
import functools

import jax
import jax.numpy as jnp
from jax import lax
from jax.experimental import pallas as pl
from jax.experimental.pallas import tpu as pltpu
from jax.sharding import PartitionSpec as P

EPS = 1e-06
LANES = 128
VMEM_LIMIT = 20 * 1024 * 1024


def per_device_general(
    psi, left_ops, right_ops, term_shift, slot_sector, sector_width, diag_left, diag_right
):
    sec_dev, rows, ncols = psi.shape
    nsec = slot_sector.shape[0]
    terms_dev = left_ops.shape[0]
    right_local = right_ops.shape[1]
    right_width = right_ops.shape[2]
    local_cols = diag_right.shape[0]
    count = float(nsec * rows * ncols)
    match = slot_sector[:, None] == jnp.arange(nsec)[None, :]
    widths = jnp.sum(jnp.where(match, sector_width[None, :], 0), axis=1)
    mask_all = (jnp.arange(rows)[None, :] < widths[:, None]).astype(jnp.float32)
    own_mask = lax.dynamic_slice_in_dim(mask_all, lax.axis_index("blk") * sec_dev, sec_dev, 0)
    raw = psi.astype(jnp.float32) * own_mask[:, :, None]
    squares = lax.psum(jnp.sum(raw * raw), "blk")
    v_left = (raw * lax.rsqrt(squares / count + EPS)).astype(jnp.bfloat16)
    onehots = (
        slot_sector[None, None, :] == slot_sector[None, :, None] - term_shift[:, None, None]
    ).astype(jnp.bfloat16)
    op_rows = rows // lax.axis_size("op")
    op_start = lax.axis_index("op") * op_rows
    dmat = diag_left[:, :, None] + diag_right[None, None, :]

    def left_local(field):
        return jnp.einsum(
            "ksij,sjc->ksic", left_ops, field, preferred_element_type=jnp.float32
        ).astype(jnp.bfloat16)

    def right_part(moved_in):
        flat = moved_in.reshape(terms_dev, nsec, rows * local_cols)
        shifted = jnp.einsum(
            "kts,ksx->ktx", onehots, flat, preferred_element_type=jnp.float32
        ).astype(jnp.bfloat16)
        shifted = shifted.reshape(terms_dev, nsec, rows, right_local, right_width)
        accum = jnp.einsum(
            "ktwrc,krdc->twrd", shifted, right_ops, preferred_element_type=jnp.float32
        )
        return accum.reshape(nsec, rows, local_cols) * mask_all[:, :, None]

    def op_total(partial_value):
        return lax.psum(partial_value.astype(jnp.bfloat16), "op").astype(jnp.float32)

    def final_rows(array):
        return lax.dynamic_slice_in_dim(array, op_start, op_rows, 1)

    def reduce_dots(values):
        sums = lax.psum(values, "blk")
        return tuple((item / count for item in sums))

    moved_first, v_moved = (
        lax.all_to_all(left_local(v_left), "blk", split_axis=3, concat_axis=1, tiled=True),
        lax.all_to_all(v_left[None], "blk", split_axis=3, concat_axis=1, tiled=True),
    )
    v_right = v_moved[0]
    vec32 = v_right.astype(jnp.float32)
    first_sigma = op_total(right_part(moved_first)) + dmat * vec32
    theta = reduce_dots((jnp.sum(vec32 * first_sigma),))[0]
    resid = first_sigma - theta * vec32
    den = dmat - theta
    corr = resid * den / jnp.maximum(den * den, 0.25)
    along = reduce_dots((jnp.sum(vec32 * corr),))[0]
    orth = corr - along * vec32
    norm_sq = reduce_dots((jnp.sum(orth * orth),))[0]
    update = (orth * lax.rsqrt(norm_sq + EPS)).astype(jnp.bfloat16)
    upd32 = update.astype(jnp.float32)
    upd_left = lax.all_to_all(update, "blk", split_axis=0, concat_axis=2, tiled=True)
    moved_second = lax.all_to_all(
        left_local(upd_left), "blk", split_axis=3, concat_axis=1, tiled=True
    )
    second_sigma = op_total(right_part(moved_second)) + dmat * upd32
    v_s1, u_s0, u_s1 = reduce_dots(
        (jnp.sum(vec32 * second_sigma), jnp.sum(upd32 * first_sigma), jnp.sum(upd32 * second_sigma))
    )
    h_mix = 0.5 * (v_s1 + u_s0)
    coef_v, coef_u, energy = ritz(theta, h_mix, u_s1)
    newvec = coef_v * vec32 + coef_u * upd32
    image = coef_v * first_sigma + coef_u * second_sigma
    new_out = final_rows(newvec.astype(jnp.bfloat16))
    res_out = final_rows((image - energy * newvec).astype(jnp.bfloat16))
    return (new_out, res_out, jnp.reshape(energy, (1,)))


def ritz(theta, h_mix, h_two):
    angle = 0.5 * jnp.arctan2(2.0 * h_mix, theta - h_two)
    sine = jnp.sin(angle)
    flip = jnp.where(sine > 0, -1.0, 1.0)
    coef_v = -sine * flip
    coef_u = jnp.cos(angle) * flip
    half = 0.5 * (theta - h_two)
    energy = 0.5 * (theta + h_two) - jnp.sqrt(half * half + h_mix * h_mix)
    return coef_v, coef_u, energy


VMEM, SMEM, HBM = pltpu.VMEM, pltpu.SMEM, pltpu.HBM


def kernel(body, ins, outs, scratch=(), flops=0, nbytes=0):
    return pl.pallas_call(
        body,
        out_shape=[
            HBM(shape, dtype) if space == HBM else jax.ShapeDtypeStruct(shape, dtype)
            for shape, dtype, space in outs
        ],
        in_specs=[pl.BlockSpec(memory_space=space) for _, space in ins],
        out_specs=[pl.BlockSpec(memory_space=space) for _, _, space in outs],
        scratch_shapes=list(scratch),
        compiler_params=pltpu.CompilerParams(vmem_limit_bytes=VMEM_LIMIT),
        cost_estimate=pl.CostEstimate(flops=flops, bytes_accessed=nbytes, transcendentals=0),
    )(*[pltpu.with_memory_space_constraint(x, HBM) if space == HBM else x for x, space in ins])


def ring_at(place, n_blk):
    place = place % n_blk if isinstance(place, int) else lax.rem(place + n_blk, n_blk)
    odd, even = 2 * place - 1, 2 * (n_blk - place)
    if isinstance(place, int):
        return 0 if place == 0 else odd if odd < n_blk else even
    return jnp.where(place == 0, 0, jnp.where(odd < n_blk, odd, even))


def ring_place(index, n_blk):
    odd, even = (index + 1) // 2, lax.rem(n_blk - index // 2, n_blk)
    return jnp.where(lax.rem(index, 2) == 1, odd, even)


def onward(block, d, n_blk):
    pairs = [(ring_at(i, n_blk), ring_at(i + d, n_blk)) for i in range(n_blk)]
    return lax.ppermute(block, "blk", pairs)


def swap(block, e, n_op):
    return lax.ppermute(block, "op", [(i, i ^ e) for i in range(n_op)])


def gather(own, n_blk, n_op, pack, table, early):
    bits = [1 << b for b in reversed(range(1, n_op.bit_length() - 1))]
    order = sorted(range(1, n_blk), key=lambda d: min(d, n_blk - d))
    columns, packed = pack()
    (came, swapped), columns, right = lax.optimization_barrier(
        (
            (onward(own, 1, n_blk), [swap(own, bit, n_op) for bit in bits[:1]]),
            columns,
            [packed[0]] + [swap(part, 2 * e, n_op) for e, part in enumerate(packed[1:], 1)],
        )
    )
    left, psi = {(0, 0): [own], (1, 0): [came]}, {0: columns[0]}
    for bit in bits[:1]:
        left[0, bit] = swapped
    half = max(own.shape[0] // 2, 1)
    parts = [came[at : at + half] for at in range(0, own.shape[0], half)]
    tables = made = None
    for j in range(1, n_blk):
        kept, extra = [], {}
        for c, part in enumerate(parts):
            ring = [onward(part, 1, n_blk)] if j < n_blk - 1 else []
            new = (ring, [swap(part, bit, n_op) for bit in bits[:1]])
            if c == len(parts) - 1:
                extra["psi"] = onward(columns[order[j - 1]], order[j - 1], n_blk)
                if j == n_blk - 1:
                    extra["tables"] = table(right)
                    extra["made"] = early(left, psi, extra["tables"])
            new, extra, _ = lax.optimization_barrier((new, extra, kept))
            kept.append(new)
        psi[order[j - 1]] = extra["psi"]
        for bit in bits[:1]:
            left[j, bit] = [swaps[0] for _, swaps in kept]
        if j < n_blk - 1:
            parts = [ring[0] for ring, _ in kept]
            left[j + 1, 0] = parts
        tables, made = extra.get("tables", tables), extra.get("made", made)
    for bit in bits[1:]:
        more = {(d, e ^ bit): [swap(x, bit, n_op) for x in parts] for (d, e), parts in left.items()}
        left.update(more)
    return left, psi, right, tables, made


def place_of():
    return lax.axis_index("blk"), lax.axis_index("op")


def pack_body(n_blk, n_op, shift, _, psi, right_in, *outs):
    n_pair = n_op // 2
    psi_out, right_out, right, sems = outs[:n_blk], outs[n_blk : n_blk + n_pair], outs[-2], outs[-1]
    terms, local, width, _ = right.shape
    cols = local * width // n_op
    per = cols // width
    own_blk, own_op = place_of()
    fetch = pltpu.make_async_copy(right_in, right, sems.at[2 * n_blk])
    fetch.start()
    copies = []
    for d in range(n_blk):
        there = ring_at(ring_place(own_blk, n_blk) + d, n_blk) * n_op
        for h in range(2):
            start = pl.multiple_of((there + (own_op ^ h)) * cols, LANES)
            copy = pltpu.make_async_copy(
                psi.at[0, :, pl.ds(start, cols)],
                psi_out[d].at[:, h * cols : (h + 1) * cols],
                sems.at[2 * d + h],
            )
            copy.start()
            copies.append(copy)
    lane = lax.broadcasted_iota(jnp.int32, (16, 2 * cols), 1)
    line = jnp.zeros((16, 2 * cols), jnp.float32)
    for k in range(terms):
        line = jnp.where(lane == k, shift[k].astype(jnp.float32), line)
    square = [lax.broadcasted_iota(jnp.int32, (width, width), axis) for axis in (0, 1)]
    unit = (square[0] == square[1]).astype(jnp.bfloat16)
    fetch.wait()
    for e in range(n_pair):
        for k in range(terms):
            turned = []
            for h in range(2):
                first = (own_op ^ (2 * e) ^ h) * per
                for r in range(per):
                    turned.append(
                        lax.dot_general(
                            right[k, first + r], unit, (((0,), (0,)), ((), ())),
                            preferred_element_type=jnp.float32,
                        )
                    )
            side_by_side = jnp.concatenate(turned, axis=1).astype(jnp.bfloat16)
            right_out[e][k * width : (k + 1) * width] = side_by_side
        right_out[e][terms * width :] = line.astype(jnp.bfloat16)
    for copy in copies:
        copy.wait()


def table_body(n_blk, terms, sector, width, left_diag, right_diag, *refs):
    tails, src, widths, slots, diag, right_out = refs[:-5], *refs[-5:]
    right_out[...] = right_diag[...]
    n_pair = len(tails)
    rows, cols = tails[0].shape
    own_blk, _ = place_of()
    lane = lax.broadcasted_iota(jnp.int32, (16, cols), 1)
    for d in range(n_blk):
        slot = ring_at(ring_place(own_blk, n_blk) - d, n_blk)
        slots[d] = slot
        widths[d] = width[sector[slot]]
    for e in range(n_pair):
        tail = tails[e][rows - 16 :].astype(jnp.float32)
        for k in range(terms):
            shift = jnp.max(jnp.where(lane == k, tail, -1e9)).astype(jnp.int32)
            for t in range(n_blk):
                want = sector[slots[t]] - shift
                found = jnp.int32(n_blk)
                for d in range(n_blk):
                    found = jnp.where(sector[slots[d]] == want, d, found)
                src[(t * n_pair + e) * terms + k] = found
    for d in range(n_blk):
        row = left_diag[pl.ds(slots[d], 1), :]
        diag[d] = jnp.transpose(jnp.broadcast_to(row, (diag.shape[2], row.shape[1])))


def diagonal(diag, right_diag, d, h):
    cols = diag.shape[2]
    _, own_op = place_of()
    start = pl.multiple_of((own_op ^ h) * cols, LANES)
    return diag[d] + right_diag[:, pl.ds(start, cols)]


def row_mask(width, shape):
    return lax.broadcasted_iota(jnp.int32, shape, 0) < width


def fold(x):
    return jnp.sum(x.reshape(-1, 8, x.shape[-1]), axis=0)


def whole(x):
    return jnp.sum(jnp.sum(x, axis=0, keepdims=True), axis=1, keepdims=True)


def spread(values, out):
    line = lax.broadcasted_iota(jnp.int32, out.shape[1:], 0)
    tile = jnp.zeros(out.shape[1:], jnp.float32)
    for j, value in enumerate(values):
        tile = jnp.where(line == j, value, tile)
    for d in range(out.shape[0]):
        out[d] = tile


def by_block(packed, terms, k):
    rows, cols = packed.shape
    width = (rows - 16) // terms
    lane = lax.broadcasted_iota(jnp.int32, (width, cols), 1)
    block = packed[k * width : (k + 1) * width].astype(jnp.float32)
    parts = []
    for r in range(cols // width):
        inside = (lane >= r * width) & (lane < (r + 1) * width)
        parts.append(jnp.where(inside, block, 0.0).astype(jnp.bfloat16))
    return jnp.concatenate(parts, axis=0)


def left_products(block, left, inter):
    _, rows, cols = inter.shape
    at = 0
    for ref in left:
        terms = ref.shape[0]
        ops = ref[...].reshape(terms * rows, rows)
        prod = jnp.dot(ops, block, preferred_element_type=jnp.float32)
        inter[at : at + terms] = prod.astype(jnp.bfloat16).reshape(terms, rows, cols)
        at += terms


def sum_terms(src, widths, inter, right, out, emit):
    n_blk, n_terms, _, _ = inter.shape
    n_blk -= 1
    terms = n_terms // len(right)
    turned = [by_block(right[j // terms], terms, j % terms) for j in range(n_terms)]
    for t in range(n_blk):
        total = None
        for j in range(n_terms):
            part = jnp.dot(
                inter[src[t * n_terms + j], j], turned[j], preferred_element_type=jnp.float32
            )
            total = part if total is None else total + part
        total = jnp.where(row_mask(widths[t], total.shape), total, 0.0)
        out[t] = total.astype(jnp.bfloat16)
        emit(t, total)


def keep(left, left_out, sems):
    copies = []
    for d, line in enumerate(left):
        at = 0
        for ref in line:
            there = left_out.at[d, at : at + ref.shape[0]]
            copies.append(pltpu.make_async_copy(ref, there, sems.at[len(copies)]))
            copies[-1].start()
            at += ref.shape[0]
    return copies


def take(refs, counts):
    out = []
    for count in counts:
        out.append(refs[:count])
        refs = refs[count:]
    return out, refs


def products_of(psi, left, widths, first, raw_out, inter):
    for d, line in enumerate(left):
        block = psi[d][...].astype(jnp.float32)
        block = jnp.where(row_mask(widths[first + d], block.shape), block, 0.0)
        raw_out[d] = block.astype(jnp.bfloat16)
        left_products(raw_out[d], line, inter.at[d])


def early_body(counts, widths, *refs):
    left, refs = take(refs, counts)
    (psi,), (raw_out, inter_out, left_out, sems) = take(refs, [len(counts)])
    copies = keep(left, left_out, sems)
    products_of(psi, left, widths, 0, raw_out, inter_out)
    for copy in copies:
        copy.wait()


def first_body(n_blk, n_pair, counts, src, widths, *refs):
    n_late = len(counts)
    n_early = n_blk - n_late
    left, refs = take(refs, counts)
    (right, psi), refs = take(refs, [n_pair, n_late])
    raw_in, inter_in, diag, right_diag, part_out, raw_out, left_out, dots_out = refs[:8]
    sends, (inter, sems) = refs[8:-2], refs[-2:]
    copies = keep(left, left_out, sems)
    for given, own in ((inter_in, inter), (raw_in, raw_out)):
        copies.append(
            pltpu.make_async_copy(given, own.at[:n_early], sems.at[len(copies)])
        )
        copies[-1].start()
    inter[n_blk] = jnp.zeros_like(inter[n_blk])
    products_of(psi, left, widths, n_early, raw_out.at[n_early:], inter.at[n_early:n_blk])
    for copy in copies:
        copy.wait()
    cols = diag.shape[2]
    zero = jnp.zeros((8, cols), jnp.float32)
    sums = [zero, zero]

    def emit(d, total):
        for h in range(2):
            part = slice(h * cols, (h + 1) * cols)
            raw = raw_out[d, :, part].astype(jnp.float32)
            image = total[:, part]
            if h == 0:
                image = image + diagonal(diag, right_diag, d, h) * raw
                sums[0] = sums[0] + fold(raw * raw)
            sums[1] = sums[1] + fold(raw * image)
        for e, send in enumerate(sends, 2):
            send_rows(e, send, d, raw_out, part_out)

    sum_terms(src, widths, inter, right, part_out, emit)
    spread([whole(x) for x in sums], dots_out)


def send_rows(e, send, d, field, part):
    _, own_op = place_of()
    step = send.shape[2]
    rows = pl.ds(pl.multiple_of((own_op ^ e) * step, step), step)
    if e % 2 == 0:
        send[0, d] = field[d, rows].astype(send.dtype)
    send[send.shape[0] - 1, d] = part[d, rows]


def total_of(mine, other, d, h, cols):
    own = mine[d, :, h * cols : (h + 1) * cols].astype(jnp.float32)
    return own + other[d, :, (1 - h) * cols : (2 - h) * cols].astype(jnp.float32)


def norm_theta(parts, count):
    tot = jnp.sum(parts, axis=0) * (1.0 / count)
    scale = lax.rsqrt(tot[0:1] + EPS)
    return scale, tot[1:2] * scale * scale


def second_body(n_blk, n_pair, count, src, widths, left_early, left_late, *refs):
    right, refs = refs[:n_pair], refs[n_pair:]
    parts, raw_in, part_in, other_in, diag, right_diag, dots_out, own_out = refs[:8]
    sends, (inter, corr, sig, fld, part_out, held, sems) = refs[8:-7], refs[-7:]
    copies = []
    n_early = left_early.shape[0]
    for d in range(n_blk):
        kept = left_early.at[d] if d < n_early else left_late.at[d - n_early]
        copies.append(pltpu.make_async_copy(kept, held.at[d], sems.at[d]))
        copies[-1].start()
    inter[n_blk] = jnp.zeros_like(inter[n_blk])
    scale, theta = norm_theta(parts[...], count)
    cols = diag.shape[2]
    halves = []
    for h in range(2):
        part = slice(h * cols, (h + 1) * cols)
        vv = vc = vs = jnp.zeros((8, cols), jnp.float32)
        for d in range(n_blk):
            vec = raw_in[d, :, part].astype(jnp.float32) * scale
            sigma = total_of(part_in, other_in, d, h, cols)
            sigma = (sigma + diagonal(diag, right_diag, d, h) * raw_in[d, :, part].astype(jnp.float32)) * scale
            sig[d, :, part] = sigma
            den = diagonal(diag, right_diag, d, h) - theta
            item = (sigma - theta * vec) * den / jnp.maximum(den * den, 0.25)
            corr[d, :, part] = item
            vv, vc, vs = vv + fold(vec * vec), vc + fold(vec * item), vs + fold(vec * sigma)
        halves.append((whole(vv), whole(vc), whole(vs)))
    along = (halves[0][1] + halves[1][1]) / jnp.maximum(halves[0][0] + halves[1][0], 1e-30)
    for copy in copies:
        copy.wait()
    for d in range(n_blk):
        for h in range(2):
            part = slice(h * cols, (h + 1) * cols)
            vec = raw_in[d, :, part].astype(jnp.float32) * scale
            fld[d, :, part] = (corr[d, :, part] - along * vec).astype(jnp.bfloat16)
        left_products(fld[d], [held.at[d]], inter.at[d])
    zero = jnp.zeros((8, cols), jnp.float32)
    sums = [zero for _ in range(5)]

    def emit(d, total):
        for h in range(2):
            part = slice(h * cols, (h + 1) * cols)
            field = fld[d, :, part].astype(jnp.float32)
            vec = raw_in[d, :, part].astype(jnp.float32) * scale
            image = total[:, part]
            if h == 0:
                image = image + diagonal(diag, right_diag, d, h) * field
                for j, prod in enumerate((field * field, vec * field, field * sig[d, :, part])):
                    sums[j] = sums[j] + fold(prod)
            sums[3] = sums[3] + fold(vec * image)
            sums[4] = sums[4] + fold(field * image)
        for e, send in enumerate(sends, 1):
            send_rows(e, send, d, fld, part_out)
        rows = pl.ds(pl.multiple_of(own_op * step, step), step)
        for j, ref in enumerate((raw_in, sig, fld, part_out)):
            own_out[j, d] = ref[d, rows].astype(own_out.dtype)

    _, own_op = place_of()
    step = own_out.shape[2]
    sum_terms(src, widths, inter, right, part_out, emit)
    spread(list(halves[0]) + [whole(x) for x in sums], dots_out)


def ritz_pair(theta, h_mix, h_two):
    diff, twice = theta - h_two, 2.0 * h_mix
    size = jnp.sqrt(diff * diff + twice * twice)
    some = size > 0.0
    safe = jnp.where(some, size, 1.0)
    big = jnp.sqrt(0.5 + 0.5 * jnp.abs(diff) / safe)
    small = 0.5 * jnp.abs(twice) / (safe * big)
    sine = jnp.where(diff >= 0.0, small, big)
    cosine = jnp.where(diff >= 0.0, big, small)
    sine = jnp.where(some, sine, 0.0)
    cosine = jnp.where(some, cosine, 1.0)
    upward = (twice > 0.0) | ((twice == 0.0) & (diff < 0.0))
    return sine, jnp.where(upward, -cosine, cosine), 0.5 * (theta + h_two) - 0.5 * size


def third_body(n_blk, n_op, count, slots, parts1, parts2, diag, right_diag, own, *refs):
    got1, got2 = refs[: n_op - 2], refs[n_op - 2 : 2 * n_op - 3]
    new_out, res_out, energy_out = refs[2 * n_op - 3 :]
    step, cols = new_out.shape[1], new_out.shape[2] // n_op
    own_blk, own_op = place_of()
    scale, theta = norm_theta(parts1[...], count)
    pairs = parts2[...].reshape(n_blk * n_op // 2, 2, *parts2.shape[1:])
    pairs = pairs[:, 0] + pairs[:, 1]
    vv, vc, vs, ff, vf, fs, vt, ft = (pairs[:, j, :] for j in range(8))

    def mean(x):
        return jnp.sum(x, axis=0, keepdims=True) * (1.0 / count)

    def nearest(vv, vc):
        return vc / jnp.maximum(vv, 1e-30)

    along = mean(vc)
    beta = nearest(vv, vc) - along
    norm_sq = mean(ff + 2.0 * beta * vf + beta * beta * vv)
    unit = lax.rsqrt(jnp.maximum(norm_sq, 0.0) + EPS)
    v_s1 = unit * mean(vt + beta * vs)
    u_s0 = unit * mean(fs + beta * vs)
    u_s1 = unit * unit * mean(ft + beta * (vt + fs) + beta * beta * vs)
    cv, cu, energy = ritz_pair(theta, 0.5 * (v_s1 + u_s0), u_s1)
    energy_out[0] = jnp.max(energy)
    cu = cu * unit
    mine = pl.ds(pl.multiple_of(own_op * step, step), step)
    for e in range(0, n_op, 2):
        there = own_blk * n_op + (own_op ^ e)
        pair = parts2[there] + parts2[own_blk * n_op + (own_op ^ e ^ 1)]
        on_vec = cv + cu * (nearest(pair[0:1], pair[1:2]) - along)
        for h in range(2):
            at = pl.multiple_of((own_op ^ e ^ h) * cols, LANES)
            part, crossed = slice(h * cols, (h + 1) * cols), slice((1 - h) * cols, (2 - h) * cols)
            for d in range(n_blk):
                dmat = diag[d, mine] + right_diag[:, pl.ds(at, cols)]
                if e:
                    raw, fld = got1[e - 2][0, d, :, part], got2[e - 1][0, d, :, part]
                    vec = raw.astype(jnp.float32) * scale
                    sigma = got1[e - 2][1, d, :, part].astype(jnp.float32)
                    sigma = sigma + got1[e - 1][0, d, :, crossed].astype(jnp.float32)
                    sigma = sigma * scale + dmat * vec
                    image = got2[e - 1][1, d, :, part].astype(jnp.float32)
                else:
                    raw, sigma, fld, image = (own[j, d, :, part].astype(jnp.float32) for j in range(4))
                    vec = raw * scale
                fld = fld.astype(jnp.float32)
                image = image + got2[e][0, d, :, crossed].astype(jnp.float32) + dmat * fld
                newvec = on_vec * vec + cu * fld
                res = on_vec * sigma + cu * image - energy * newvec
                new_out[slots[d], :, pl.ds(at, cols)] = newvec.astype(jnp.bfloat16)
                res_out[slots[d], :, pl.ds(at, cols)] = res.astype(jnp.bfloat16)


def per_device(
    psi, left_ops, right_ops, term_shift, slot_sector, sector_width, diag_left, diag_right
):
    n_blk, n_op = lax.axis_size("blk"), lax.axis_size("op")
    _, rows, ncols = psi.shape
    terms, _, width, _ = right_ops.shape
    n_pair = n_op // 2
    cols = diag_right.shape[0] // n_op
    step = rows // n_op
    count = float(n_blk * rows * ncols)
    n_dev = n_blk * n_op
    bf16, f32, i32 = jnp.bfloat16, jnp.float32, jnp.int32

    def pack():
        first = swap(term_shift, 1, n_op)
        sent = kernel(
            functools.partial(pack_body, n_blk, n_op),
            [(term_shift, SMEM), (first, SMEM), (psi, HBM), (right_ops, HBM)],
            [((rows, 2 * cols), bf16, VMEM)] * n_blk
            + [((terms * width + 16, 2 * cols), bf16, VMEM)] * n_pair,
            [pltpu.VMEM(right_ops.shape, bf16), pltpu.SemaphoreType.DMA((2 * n_blk + 1,))],
            nbytes=1 << 20,
        )
        return sent[:n_blk], sent[n_blk:]

    def table(right):
        return kernel(
            functools.partial(table_body, n_blk, terms),
            [(slot_sector, SMEM), (sector_width, SMEM), (diag_left, VMEM), (diag_right[None], VMEM)]
            + [(block, VMEM) for block in right],
            [((n_blk * n_pair * terms,), i32, SMEM)]
            + [((n_blk,), i32, SMEM)] * 2
            + [((n_blk, rows, LANES), f32, VMEM), ((1, n_op * cols), f32, VMEM)],
        )

    n_early = min(2, n_blk - 1)

    def inputs(left, psi, those):
        lines = [[x for e in range(n_pair) for x in left[d, 2 * e]] for d in those]
        blocks = [x for line in lines for x in line] + [psi[d] for d in those]
        return [(x, VMEM) for x in blocks], [len(line) for line in lines]

    def early(left, psi, tables):
        ins, counts = inputs(left, psi, range(n_early))
        return kernel(
            functools.partial(early_body, counts),
            [(tables[1], SMEM)] + ins,
            [
                ((n_early, rows, 2 * cols), bf16, VMEM),
                ((n_early, n_pair * terms, rows, 2 * cols), bf16, VMEM),
                ((n_early, n_pair * terms, rows, rows), bf16, HBM),
            ],
            [pltpu.SemaphoreType.DMA((sum(counts),))],
            flops=2 * n_early * rows * rows * 2 * cols * terms * n_pair,
            nbytes=4 << 20,
        )

    left, psi_by, right, (src, widths, slots, *both), (raw_early, inter_early, left_early) = gather(
        left_ops[:, 0], n_blk, n_op, pack, table, early
    )
    n_late = n_blk - n_early
    late_ins, counts = inputs(left, psi_by, range(n_early, n_blk))
    left_ins, psi_ins = late_ins[: sum(counts)], late_ins[sum(counts) :]
    right_ins = [(block, VMEM) for block in right]
    diags = [(x, VMEM) for x in both]

    tables = [(src, SMEM), (widths, SMEM)]
    narrow = ((n_blk, rows, 2 * cols), bf16, VMEM)
    dots = ((n_dev, 8, LANES), f32, VMEM)
    sends = [((2 - e % 2, n_blk, step, 2 * cols), bf16, VMEM) for e in range(1, n_op)]
    inter = pltpu.VMEM((n_blk + 1, n_pair * terms, rows, 2 * cols), bf16)
    left_late = (n_late, n_pair * terms, rows, rows)
    cost = dict(flops=2 * n_blk * rows * 2 * cols * terms * n_pair * (rows + 2 * cols), nbytes=6 << 20)

    def totals(parts):
        return lax.all_to_all(parts, ("blk", "op"), 0, 0, tiled=True)

    part1, raw, kept, dots1, *out1 = kernel(
        functools.partial(first_body, n_blk, n_pair, counts),
        tables + left_ins + right_ins + psi_ins + [(raw_early, VMEM), (inter_early, VMEM)] + diags,
        [narrow, narrow, (left_late, bf16, HBM), dots] + sends[1:],
        [inter, pltpu.SemaphoreType.DMA((sum(counts) + 2,))],
        **cost,
    )
    parts1, other1, got1 = lax.optimization_barrier(
        (
            totals(dots1),
            swap(part1, 1, n_op),
            [swap(block, e, n_op) for e, block in enumerate(out1, 2)],
        )
    )
    dots2, own, *out2 = kernel(
        functools.partial(second_body, n_blk, n_pair, count),
        tables + [(left_early, HBM), (kept, HBM)] + right_ins
        + [(x, VMEM) for x in (parts1, raw, part1, other1)] + diags,
        [dots, ((4, n_blk, step, 2 * cols), bf16, VMEM)] + sends,
        [
            inter,
            pltpu.VMEM((n_blk, rows, 2 * cols), f32),
            pltpu.VMEM((n_blk, rows, 2 * cols), f32),
            pltpu.VMEM((n_blk, rows, 2 * cols), bf16),
            pltpu.VMEM((n_blk, rows, 2 * cols), bf16),
            pltpu.VMEM((n_blk, *left_late[1:]), bf16),
            pltpu.SemaphoreType.DMA((n_blk,)),
        ],
        **cost,
    )
    parts2 = totals(dots2)
    got2 = [swap(block, e, n_op) for e, block in enumerate(out2, 1)]
    final = ((n_blk, step, n_op * cols), bf16, VMEM)
    new, res, energy = kernel(
        functools.partial(third_body, n_blk, n_op, count),
        [(slots, SMEM)] + [(x, VMEM) for x in (parts1, parts2)] + diags
        + [(x, VMEM) for x in (own, *got1, *got2)],
        [final, final, ((1,), f32, SMEM)],
        nbytes=4 << 20,
    )
    return new, res, energy


def solution(mesh):
    placed = (
        P(("grp", "blk"), None, None),
        P("op", ("grp", "blk"), None, None),
        P("op", ("grp", "blk"), None, None),
        P("op"),
        P("grp"),
        P("grp"),
        P("grp", None),
        P(("grp", "blk")),
    )

    def body(*args):
        psi, left_ops, right_ops, diag_right = args[0], args[1], args[2], args[7]
        n_op = mesh.shape["op"]
        cols = diag_right.shape[0] // n_op
        fits = (
            psi.shape[0] == 1
            and diag_right.shape[0] % n_op == 0
            and cols == LANES
            and n_op % 2 == 0
            and cols % right_ops.shape[2] == 0
            and cols // right_ops.shape[2] * n_op == right_ops.shape[1]
            and psi.shape[1] % (16 * n_op) == 0
            and n_op & (n_op - 1) == 0
            and n_op <= 4
            and mesh.shape["blk"] > 2
        )
        return (per_device if fits else per_device_general)(*args)

    return jax.shard_map(
        body,
        mesh=mesh,
        in_specs=placed,
        out_specs=(P("grp", "op", "blk"), P("grp", "op", "blk"), P("grp")),
        check_vma=False,
    )
```

```python
import functools

import jax
import jax.numpy as jnp
from jax import lax
from jax.experimental import pallas as pl
from jax.experimental.pallas import tpu as pltpu
from jax.sharding import PartitionSpec as P

EPS = 1e-06
LANES = 128
VMEM_LIMIT = 20 * 1024 * 1024


def per_device_general(
    psi, left_ops, right_ops, term_shift, slot_sector, sector_width, diag_left, diag_right
):
    sec_dev, rows, ncols = psi.shape
    nsec = slot_sector.shape[0]
    terms_dev = left_ops.shape[0]
    right_local = right_ops.shape[1]
    right_width = right_ops.shape[2]
    local_cols = diag_right.shape[0]
    count = float(nsec * rows * ncols)
    match = slot_sector[:, None] == jnp.arange(nsec)[None, :]
    widths = jnp.sum(jnp.where(match, sector_width[None, :], 0), axis=1)
    mask_all = (jnp.arange(rows)[None, :] < widths[:, None]).astype(jnp.float32)
    own_mask = lax.dynamic_slice_in_dim(mask_all, lax.axis_index("blk") * sec_dev, sec_dev, 0)
    raw = psi.astype(jnp.float32) * own_mask[:, :, None]
    squares = lax.psum(jnp.sum(raw * raw), "blk")
    v_left = (raw * lax.rsqrt(squares / count + EPS)).astype(jnp.bfloat16)
    onehots = (
        slot_sector[None, None, :] == slot_sector[None, :, None] - term_shift[:, None, None]
    ).astype(jnp.bfloat16)
    op_rows = rows // lax.axis_size("op")
    op_start = lax.axis_index("op") * op_rows
    dmat = diag_left[:, :, None] + diag_right[None, None, :]

    def left_local(field):
        return jnp.einsum(
            "ksij,sjc->ksic", left_ops, field, preferred_element_type=jnp.float32
        ).astype(jnp.bfloat16)

    def right_part(moved_in):
        flat = moved_in.reshape(terms_dev, nsec, rows * local_cols)
        shifted = jnp.einsum(
            "kts,ksx->ktx", onehots, flat, preferred_element_type=jnp.float32
        ).astype(jnp.bfloat16)
        shifted = shifted.reshape(terms_dev, nsec, rows, right_local, right_width)
        accum = jnp.einsum(
            "ktwrc,krdc->twrd", shifted, right_ops, preferred_element_type=jnp.float32
        )
        return accum.reshape(nsec, rows, local_cols) * mask_all[:, :, None]

    def op_total(partial_value):
        return lax.psum(partial_value.astype(jnp.bfloat16), "op").astype(jnp.float32)

    def final_rows(array):
        return lax.dynamic_slice_in_dim(array, op_start, op_rows, 1)

    def reduce_dots(values):
        sums = lax.psum(values, "blk")
        return tuple((item / count for item in sums))

    moved_first, v_moved = (
        lax.all_to_all(left_local(v_left), "blk", split_axis=3, concat_axis=1, tiled=True),
        lax.all_to_all(v_left[None], "blk", split_axis=3, concat_axis=1, tiled=True),
    )
    v_right = v_moved[0]
    vec32 = v_right.astype(jnp.float32)
    first_sigma = op_total(right_part(moved_first)) + dmat * vec32
    theta = reduce_dots((jnp.sum(vec32 * first_sigma),))[0]
    resid = first_sigma - theta * vec32
    den = dmat - theta
    corr = resid * den / jnp.maximum(den * den, 0.25)
    along = reduce_dots((jnp.sum(vec32 * corr),))[0]
    orth = corr - along * vec32
    norm_sq = reduce_dots((jnp.sum(orth * orth),))[0]
    update = (orth * lax.rsqrt(norm_sq + EPS)).astype(jnp.bfloat16)
    upd32 = update.astype(jnp.float32)
    upd_left = lax.all_to_all(update, "blk", split_axis=0, concat_axis=2, tiled=True)
    moved_second = lax.all_to_all(
        left_local(upd_left), "blk", split_axis=3, concat_axis=1, tiled=True
    )
    second_sigma = op_total(right_part(moved_second)) + dmat * upd32
    v_s1, u_s0, u_s1 = reduce_dots(
        (jnp.sum(vec32 * second_sigma), jnp.sum(upd32 * first_sigma), jnp.sum(upd32 * second_sigma))
    )
    h_mix = 0.5 * (v_s1 + u_s0)
    coef_v, coef_u, energy = ritz(theta, h_mix, u_s1)
    newvec = coef_v * vec32 + coef_u * upd32
    image = coef_v * first_sigma + coef_u * second_sigma
    new_out = final_rows(newvec.astype(jnp.bfloat16))
    res_out = final_rows((image - energy * newvec).astype(jnp.bfloat16))
    return (new_out, res_out, jnp.reshape(energy, (1,)))


def ritz(theta, h_mix, h_two):
    angle = 0.5 * jnp.arctan2(2.0 * h_mix, theta - h_two)
    sine = jnp.sin(angle)
    flip = jnp.where(sine > 0, -1.0, 1.0)
    coef_v = -sine * flip
    coef_u = jnp.cos(angle) * flip
    half = 0.5 * (theta - h_two)
    energy = 0.5 * (theta + h_two) - jnp.sqrt(half * half + h_mix * h_mix)
    return coef_v, coef_u, energy


VMEM, SMEM, HBM = pltpu.VMEM, pltpu.SMEM, pltpu.HBM


def kernel(body, ins, outs, scratch=(), flops=0, nbytes=0):
    return pl.pallas_call(
        body,
        out_shape=[
            HBM(shape, dtype) if space == HBM else jax.ShapeDtypeStruct(shape, dtype)
            for shape, dtype, space in outs
        ],
        in_specs=[pl.BlockSpec(memory_space=space) for _, space in ins],
        out_specs=[pl.BlockSpec(memory_space=space) for _, _, space in outs],
        scratch_shapes=list(scratch),
        compiler_params=pltpu.CompilerParams(vmem_limit_bytes=VMEM_LIMIT),
        cost_estimate=pl.CostEstimate(flops=flops, bytes_accessed=nbytes, transcendentals=0),
    )(*[pltpu.with_memory_space_constraint(x, HBM) if space == HBM else x for x, space in ins])


def ring_at(place, n_blk):
    place = place % n_blk if isinstance(place, int) else lax.rem(place + n_blk, n_blk)
    odd, even = 2 * place - 1, 2 * (n_blk - place)
    if isinstance(place, int):
        return 0 if place == 0 else odd if odd < n_blk else even
    return jnp.where(place == 0, 0, jnp.where(odd < n_blk, odd, even))


def ring_place(index, n_blk):
    odd, even = (index + 1) // 2, lax.rem(n_blk - index // 2, n_blk)
    return jnp.where(lax.rem(index, 2) == 1, odd, even)


def onward(block, d, n_blk):
    pairs = [(ring_at(i, n_blk), ring_at(i + d, n_blk)) for i in range(n_blk)]
    return lax.ppermute(block, "blk", pairs)


def swap(block, e, n_op):
    return lax.ppermute(block, "op", [(i, i ^ e) for i in range(n_op)])


def gather(own, n_blk, n_op, pack, table, early):
    bits = [1 << b for b in reversed(range(1, n_op.bit_length() - 1))]
    order = sorted(range(1, n_blk), key=lambda d: min(d, n_blk - d))
    columns, packed = pack()
    (came, swapped), columns, right, near = lax.optimization_barrier(
        (
            (onward(own, 1, n_blk), [swap(own, bit, n_op) for bit in bits[:1]]),
            columns,
            [packed[0]] + [swap(part, 2 * e, n_op) for e, part in enumerate(packed[1:], 1)],
            [onward(columns[d], d, n_blk) for d in order[:2]],
        )
    )
    left, psi = {(0, 0): [own], (1, 0): [came]}, {0: [columns[0]]}
    for d, block in zip(order[:2], near):
        psi[d] = [block]
    for bit in bits[:1]:
        left[0, bit] = swapped
    half = max(own.shape[0] // 2, 1)
    parts = [came[at : at + half] for at in range(0, own.shape[0], half)]
    tables = made = None
    for j in range(1, n_blk):
        kept, extra = [], {}
        for c, part in enumerate(parts):
            ring = [onward(part, 1, n_blk)] if j < n_blk - 1 else []
            new = (ring, [swap(part, bit, n_op) for bit in bits[:1]])
            if c == len(parts) - 1:
                if j == 1:
                    extra["tables"] = table(right)
                    extra["psi"] = {d: onward(columns[d], d, n_blk) for d in order[2:]}
                due = order[:1] if j == 2 else order[1:] if j == n_blk - 1 else []
                extra["other"] = {d: swap(psi[d][0], 1, n_op) for d in due}
                if j == n_blk - 1:
                    extra["made"] = early(left, psi, tables)
            new, extra, _ = lax.optimization_barrier((new, extra, kept))
            kept.append(new)
        for bit in bits[:1]:
            left[j, bit] = [swaps[0] for _, swaps in kept]
        if j < n_blk - 1:
            parts = [ring[0] for ring, _ in kept]
            left[j + 1, 0] = parts
        tables, made = extra.get("tables", tables), extra.get("made", made)
        psi.update({d: [block] for d, block in extra.get("psi", {}).items()})
        for d, block in extra["other"].items():
            psi[d].append(block)
    for bit in bits[1:]:
        more = {(d, e ^ bit): [swap(x, bit, n_op) for x in parts] for (d, e), parts in left.items()}
        left.update(more)
    return left, psi, right, tables, made


def place_of():
    return lax.axis_index("blk"), lax.axis_index("op")


def pack_body(n_blk, n_op, shift, _, psi, right_in, *outs):
    n_pair = n_op // 2
    psi_out, right_out, right, sems = outs[:n_blk], outs[n_blk : n_blk + n_pair], outs[-2], outs[-1]
    terms, local, width, _ = right.shape
    cols = local * width // n_op
    per = cols // width
    own_blk, own_op = place_of()
    fetch = pltpu.make_async_copy(right_in, right, sems.at[2 * n_blk])
    fetch.start()
    copies = []
    for d in range(n_blk):
        there = ring_at(ring_place(own_blk, n_blk) + d, n_blk) * n_op
        for h in range(psi_out[d].shape[1] // cols):
            start = pl.multiple_of((there + (own_op ^ h)) * cols, LANES)
            copy = pltpu.make_async_copy(
                psi.at[0, :, pl.ds(start, cols)],
                psi_out[d].at[:, h * cols : (h + 1) * cols],
                sems.at[2 * d + h],
            )
            copy.start()
            copies.append(copy)
    lane = lax.broadcasted_iota(jnp.int32, (16, 2 * cols), 1)
    line = jnp.zeros((16, 2 * cols), jnp.float32)
    for k in range(terms):
        line = jnp.where(lane == k, shift[k].astype(jnp.float32), line)
    square = [lax.broadcasted_iota(jnp.int32, (width, width), axis) for axis in (0, 1)]
    unit = (square[0] == square[1]).astype(jnp.bfloat16)
    fetch.wait()
    for e in range(n_pair):
        for k in range(terms):
            turned = []
            for h in range(2):
                first = (own_op ^ (2 * e) ^ h) * per
                for r in range(per):
                    turned.append(
                        lax.dot_general(
                            right[k, first + r], unit, (((0,), (0,)), ((), ())),
                            preferred_element_type=jnp.float32,
                        )
                    )
            side_by_side = jnp.concatenate(turned, axis=1).astype(jnp.bfloat16)
            right_out[e][k * width : (k + 1) * width] = side_by_side
        right_out[e][terms * width :] = line.astype(jnp.bfloat16)
    for copy in copies:
        copy.wait()


def table_body(n_blk, terms, sector, width, left_diag, right_diag, *refs):
    tails, src, widths, slots, diag, right_out = refs[:-5], *refs[-5:]
    right_out[...] = right_diag[...]
    n_pair = len(tails)
    rows, cols = tails[0].shape
    own_blk, _ = place_of()
    lane = lax.broadcasted_iota(jnp.int32, (16, cols), 1)
    for d in range(n_blk):
        slot = ring_at(ring_place(own_blk, n_blk) - d, n_blk)
        slots[d] = slot
        widths[d] = width[sector[slot]]
    for e in range(n_pair):
        tail = tails[e][rows - 16 :].astype(jnp.float32)
        for k in range(terms):
            shift = jnp.max(jnp.where(lane == k, tail, -1e9)).astype(jnp.int32)
            for t in range(n_blk):
                want = sector[slots[t]] - shift
                found = jnp.int32(n_blk)
                for d in range(n_blk):
                    found = jnp.where(sector[slots[d]] == want, d, found)
                src[(t * n_pair + e) * terms + k] = found
    for d in range(n_blk):
        row = left_diag[pl.ds(slots[d], 1), :]
        diag[d] = jnp.transpose(jnp.broadcast_to(row, (diag.shape[2], row.shape[1])))


def diagonal(diag, right_diag, d, h):
    cols = diag.shape[2]
    _, own_op = place_of()
    start = pl.multiple_of((own_op ^ h) * cols, LANES)
    return diag[d] + right_diag[:, pl.ds(start, cols)]


def row_mask(width, shape):
    return lax.broadcasted_iota(jnp.int32, shape, 0) < width


def fold(x):
    return jnp.sum(x.reshape(-1, 8, x.shape[-1]), axis=0)


def whole(x):
    return jnp.sum(jnp.sum(x, axis=0, keepdims=True), axis=1, keepdims=True)


def spread(values, out):
    line = lax.broadcasted_iota(jnp.int32, out.shape[1:], 0)
    tile = jnp.zeros(out.shape[1:], jnp.float32)
    for j, value in enumerate(values):
        tile = jnp.where(line == j, value, tile)
    for d in range(out.shape[0]):
        out[d] = tile


def by_block(packed, terms, k):
    rows, cols = packed.shape
    width = (rows - 16) // terms
    lane = lax.broadcasted_iota(jnp.int32, (width, cols), 1)
    block = packed[k * width : (k + 1) * width].astype(jnp.float32)
    parts = []
    for r in range(cols // width):
        inside = (lane >= r * width) & (lane < (r + 1) * width)
        parts.append(jnp.where(inside, block, 0.0).astype(jnp.bfloat16))
    return jnp.concatenate(parts, axis=0)


def left_products(block, left, inter):
    _, rows, cols = inter.shape
    at = 0
    for ref in left:
        terms = ref.shape[0]
        ops = ref[...].reshape(terms * rows, rows)
        prod = jnp.dot(ops, block, preferred_element_type=jnp.float32)
        inter[at : at + terms] = prod.astype(jnp.bfloat16).reshape(terms, rows, cols)
        at += terms


def sum_terms(src, widths, inter, right, out, emit):
    n_blk, n_terms, _, _ = inter.shape
    n_blk -= 1
    terms = n_terms // len(right)
    turned = [by_block(right[j // terms], terms, j % terms) for j in range(n_terms)]
    for t in range(n_blk):
        total = None
        for j in range(n_terms):
            part = jnp.dot(
                inter[src[t * n_terms + j], j], turned[j], preferred_element_type=jnp.float32
            )
            total = part if total is None else total + part
        total = jnp.where(row_mask(widths[t], total.shape), total, 0.0)
        out[t] = total.astype(jnp.bfloat16)
        emit(t, total)


def keep(left, left_out, sems):
    copies = []
    for d, line in enumerate(left):
        at = 0
        for ref in line:
            there = left_out.at[d, at : at + ref.shape[0]]
            copies.append(pltpu.make_async_copy(ref, there, sems.at[len(copies)]))
            copies[-1].start()
            at += ref.shape[0]
    return copies


def take(refs, counts):
    out = []
    for count in counts:
        out.append(refs[:count])
        refs = refs[count:]
    return out, refs


def products_of(psi, left, widths, first, raw_out, inter):
    for d, line in enumerate(left):
        at = 0
        for ref in psi[d]:
            block = ref[...].astype(jnp.float32)
            block = jnp.where(row_mask(widths[first + d], block.shape), block, 0.0)
            raw_out[d, :, at : at + block.shape[1]] = block.astype(jnp.bfloat16)
            at += block.shape[1]
        left_products(raw_out[d], line, inter.at[d])


def early_body(counts, halves, widths, *refs):
    left, refs = take(refs, counts)
    psi, (raw_out, inter_out, left_out, sems) = take(refs, halves)
    copies = keep(left, left_out, sems)
    products_of(psi, left, widths, 0, raw_out, inter_out)
    for copy in copies:
        copy.wait()


def first_body(n_blk, n_pair, counts, halves, src, widths, *refs):
    n_late = len(counts)
    n_early = n_blk - n_late
    left, refs = take(refs, counts)
    (right,), refs = take(refs, [n_pair])
    psi, refs = take(refs, halves)
    raw_in, inter_in, diag, right_diag, part_out, raw_out, left_out, dots_out = refs[:8]
    sends, (inter, sems) = refs[8:-2], refs[-2:]
    copies = keep(left, left_out, sems)
    for given, own in ((inter_in, inter), (raw_in, raw_out)):
        copies.append(
            pltpu.make_async_copy(given, own.at[:n_early], sems.at[len(copies)])
        )
        copies[-1].start()
    inter[n_blk] = jnp.zeros_like(inter[n_blk])
    products_of(psi, left, widths, n_early, raw_out.at[n_early:], inter.at[n_early:n_blk])
    for copy in copies:
        copy.wait()
    cols = diag.shape[2]
    zero = jnp.zeros((8, cols), jnp.float32)
    sums = [zero, zero]

    def emit(d, total):
        for h in range(2):
            part = slice(h * cols, (h + 1) * cols)
            raw = raw_out[d, :, part].astype(jnp.float32)
            image = total[:, part]
            if h == 0:
                image = image + diagonal(diag, right_diag, d, h) * raw
                sums[0] = sums[0] + fold(raw * raw)
            sums[1] = sums[1] + fold(raw * image)
        for e, send in enumerate(sends, 2):
            send_rows(e, send, d, raw_out, part_out)

    sum_terms(src, widths, inter, right, part_out, emit)
    spread([whole(x) for x in sums], dots_out)


def send_rows(e, send, d, field, part):
    _, own_op = place_of()
    step = send.shape[2]
    rows = pl.ds(pl.multiple_of((own_op ^ e) * step, step), step)
    if e % 2 == 0:
        send[0, d] = field[d, rows].astype(send.dtype)
    send[send.shape[0] - 1, d] = part[d, rows]


def total_of(mine, other, d, h, cols):
    own = mine[d, :, h * cols : (h + 1) * cols].astype(jnp.float32)
    return own + other[d, :, (1 - h) * cols : (2 - h) * cols].astype(jnp.float32)


def norm_theta(parts, count):
    tot = jnp.sum(parts, axis=0) * (1.0 / count)
    scale = lax.rsqrt(tot[0:1] + EPS)
    return scale, tot[1:2] * scale * scale


def second_body(n_blk, n_pair, count, src, widths, left_early, left_late, *refs):
    right, refs = refs[:n_pair], refs[n_pair:]
    parts, raw_in, part_in, other_in, diag, right_diag, dots_out, own_out = refs[:8]
    sends, (inter, corr, sig, fld, part_out, held, sems) = refs[8:-7], refs[-7:]
    copies = []
    n_early = left_early.shape[0]
    for d in range(n_blk):
        kept = left_early.at[d] if d < n_early else left_late.at[d - n_early]
        copies.append(pltpu.make_async_copy(kept, held.at[d], sems.at[d]))
        copies[-1].start()
    inter[n_blk] = jnp.zeros_like(inter[n_blk])
    scale, theta = norm_theta(parts[...], count)
    cols = diag.shape[2]
    halves = []
    for h in range(2):
        part = slice(h * cols, (h + 1) * cols)
        vv = vc = vs = jnp.zeros((8, cols), jnp.float32)
        for d in range(n_blk):
            vec = raw_in[d, :, part].astype(jnp.float32) * scale
            sigma = total_of(part_in, other_in, d, h, cols)
            sigma = (sigma + diagonal(diag, right_diag, d, h) * raw_in[d, :, part].astype(jnp.float32)) * scale
            sig[d, :, part] = sigma
            den = diagonal(diag, right_diag, d, h) - theta
            item = (sigma - theta * vec) * den / jnp.maximum(den * den, 0.25)
            corr[d, :, part] = item
            vv, vc, vs = vv + fold(vec * vec), vc + fold(vec * item), vs + fold(vec * sigma)
        halves.append((whole(vv), whole(vc), whole(vs)))
    along = (halves[0][1] + halves[1][1]) / jnp.maximum(halves[0][0] + halves[1][0], 1e-30)
    for copy in copies:
        copy.wait()
    for d in range(n_blk):
        for h in range(2):
            part = slice(h * cols, (h + 1) * cols)
            vec = raw_in[d, :, part].astype(jnp.float32) * scale
            fld[d, :, part] = (corr[d, :, part] - along * vec).astype(jnp.bfloat16)
        left_products(fld[d], [held.at[d]], inter.at[d])
    zero = jnp.zeros((8, cols), jnp.float32)
    sums = [zero for _ in range(5)]

    def emit(d, total):
        for h in range(2):
            part = slice(h * cols, (h + 1) * cols)
            field = fld[d, :, part].astype(jnp.float32)
            vec = raw_in[d, :, part].astype(jnp.float32) * scale
            image = total[:, part]
            if h == 0:
                image = image + diagonal(diag, right_diag, d, h) * field
                for j, prod in enumerate((field * field, vec * field, field * sig[d, :, part])):
                    sums[j] = sums[j] + fold(prod)
            sums[3] = sums[3] + fold(vec * image)
            sums[4] = sums[4] + fold(field * image)
        for e, send in enumerate(sends, 1):
            send_rows(e, send, d, fld, part_out)
        rows = pl.ds(pl.multiple_of(own_op * step, step), step)
        for j, ref in enumerate((raw_in, sig, fld, part_out)):
            own_out[j, d] = ref[d, rows].astype(own_out.dtype)

    _, own_op = place_of()
    step = own_out.shape[2]
    sum_terms(src, widths, inter, right, part_out, emit)
    spread(list(halves[0]) + [whole(x) for x in sums], dots_out)


def ritz_pair(theta, h_mix, h_two):
    diff, twice = theta - h_two, 2.0 * h_mix
    size = jnp.sqrt(diff * diff + twice * twice)
    some = size > 0.0
    safe = jnp.where(some, size, 1.0)
    big = jnp.sqrt(0.5 + 0.5 * jnp.abs(diff) / safe)
    small = 0.5 * jnp.abs(twice) / (safe * big)
    sine = jnp.where(diff >= 0.0, small, big)
    cosine = jnp.where(diff >= 0.0, big, small)
    sine = jnp.where(some, sine, 0.0)
    cosine = jnp.where(some, cosine, 1.0)
    upward = (twice > 0.0) | ((twice == 0.0) & (diff < 0.0))
    return sine, jnp.where(upward, -cosine, cosine), 0.5 * (theta + h_two) - 0.5 * size


def third_body(n_blk, n_op, count, slots, parts1, parts2, diag, right_diag, own, *refs):
    got1, got2 = refs[: n_op - 2], refs[n_op - 2 : 2 * n_op - 3]
    new_out, res_out, energy_out = refs[2 * n_op - 3 :]
    step, cols = new_out.shape[1], new_out.shape[2] // n_op
    own_blk, own_op = place_of()
    scale, theta = norm_theta(parts1[...], count)
    pairs = parts2[...].reshape(n_blk * n_op // 2, 2, *parts2.shape[1:])
    pairs = pairs[:, 0] + pairs[:, 1]
    vv, vc, vs, ff, vf, fs, vt, ft = (pairs[:, j, :] for j in range(8))

    def mean(x):
        return jnp.sum(x, axis=0, keepdims=True) * (1.0 / count)

    def nearest(vv, vc):
        return vc / jnp.maximum(vv, 1e-30)

    along = mean(vc)
    beta = nearest(vv, vc) - along
    norm_sq = mean(ff + 2.0 * beta * vf + beta * beta * vv)
    unit = lax.rsqrt(jnp.maximum(norm_sq, 0.0) + EPS)
    v_s1 = unit * mean(vt + beta * vs)
    u_s0 = unit * mean(fs + beta * vs)
    u_s1 = unit * unit * mean(ft + beta * (vt + fs) + beta * beta * vs)
    cv, cu, energy = ritz_pair(theta, 0.5 * (v_s1 + u_s0), u_s1)
    energy_out[0] = jnp.max(energy)
    cu = cu * unit
    mine = pl.ds(pl.multiple_of(own_op * step, step), step)
    for e in range(0, n_op, 2):
        there = own_blk * n_op + (own_op ^ e)
        pair = parts2[there] + parts2[own_blk * n_op + (own_op ^ e ^ 1)]
        on_vec = cv + cu * (nearest(pair[0:1], pair[1:2]) - along)
        for h in range(2):
            at = pl.multiple_of((own_op ^ e ^ h) * cols, LANES)
            part, crossed = slice(h * cols, (h + 1) * cols), slice((1 - h) * cols, (2 - h) * cols)
            for d in range(n_blk):
                dmat = diag[d, mine] + right_diag[:, pl.ds(at, cols)]
                if e:
                    raw, fld = got1[e - 2][0, d, :, part], got2[e - 1][0, d, :, part]
                    vec = raw.astype(jnp.float32) * scale
                    sigma = got1[e - 2][1, d, :, part].astype(jnp.float32)
                    sigma = sigma + got1[e - 1][0, d, :, crossed].astype(jnp.float32)
                    sigma = sigma * scale + dmat * vec
                    image = got2[e - 1][1, d, :, part].astype(jnp.float32)
                else:
                    raw, sigma, fld, image = (own[j, d, :, part].astype(jnp.float32) for j in range(4))
                    vec = raw * scale
                fld = fld.astype(jnp.float32)
                image = image + got2[e][0, d, :, crossed].astype(jnp.float32) + dmat * fld
                newvec = on_vec * vec + cu * fld
                res = on_vec * sigma + cu * image - energy * newvec
                new_out[slots[d], :, pl.ds(at, cols)] = newvec.astype(jnp.bfloat16)
                res_out[slots[d], :, pl.ds(at, cols)] = res.astype(jnp.bfloat16)


def per_device(
    psi, left_ops, right_ops, term_shift, slot_sector, sector_width, diag_left, diag_right
):
    n_blk, n_op = lax.axis_size("blk"), lax.axis_size("op")
    _, rows, ncols = psi.shape
    terms, _, width, _ = right_ops.shape
    n_pair = n_op // 2
    cols = diag_right.shape[0] // n_op
    step = rows // n_op
    count = float(n_blk * rows * ncols)
    n_dev = n_blk * n_op
    bf16, f32, i32 = jnp.bfloat16, jnp.float32, jnp.int32

    def pack():
        first = swap(term_shift, 1, n_op)
        sent = kernel(
            functools.partial(pack_body, n_blk, n_op),
            [(term_shift, SMEM), (first, SMEM), (psi, HBM), (right_ops, HBM)],
            [((rows, 2 * cols if d == 0 else cols), bf16, VMEM) for d in range(n_blk)]
            + [((terms * width + 16, 2 * cols), bf16, VMEM)] * n_pair,
            [pltpu.VMEM(right_ops.shape, bf16), pltpu.SemaphoreType.DMA((2 * n_blk + 1,))],
            nbytes=1 << 20,
        )
        return sent[:n_blk], sent[n_blk:]

    def table(right):
        return kernel(
            functools.partial(table_body, n_blk, terms),
            [(slot_sector, SMEM), (sector_width, SMEM), (diag_left, VMEM), (diag_right[None], VMEM)]
            + [(block, VMEM) for block in right],
            [((n_blk * n_pair * terms,), i32, SMEM)]
            + [((n_blk,), i32, SMEM)] * 2
            + [((n_blk, rows, LANES), f32, VMEM), ((1, n_op * cols), f32, VMEM)],
        )

    n_early = min(2, n_blk - 1)

    def inputs(left, psi, those):
        lines = [[x for e in range(n_pair) for x in left[d, 2 * e]] for d in those]
        blocks = [x for line in lines for x in line] + [x for d in those for x in psi[d]]
        return [(x, VMEM) for x in blocks], [len(line) for line in lines], [len(psi[d]) for d in those]

    def early(left, psi, tables):
        ins, counts, halves = inputs(left, psi, range(n_early))
        return kernel(
            functools.partial(early_body, counts, halves),
            [(tables[1], SMEM)] + ins,
            [
                ((n_early, rows, 2 * cols), bf16, VMEM),
                ((n_early, n_pair * terms, rows, 2 * cols), bf16, VMEM),
                ((n_early, n_pair * terms, rows, rows), bf16, HBM),
            ],
            [pltpu.SemaphoreType.DMA((sum(counts),))],
            flops=2 * n_early * rows * rows * 2 * cols * terms * n_pair,
            nbytes=4 << 20,
        )

    left, psi_by, right, (src, widths, slots, *both), (raw_early, inter_early, left_early) = gather(
        left_ops[:, 0], n_blk, n_op, pack, table, early
    )
    n_late = n_blk - n_early
    late_ins, counts, halves = inputs(left, psi_by, range(n_early, n_blk))
    left_ins, psi_ins = late_ins[: sum(counts)], late_ins[sum(counts) :]
    right_ins = [(block, VMEM) for block in right]
    diags = [(x, VMEM) for x in both]

    tables = [(src, SMEM), (widths, SMEM)]
    narrow = ((n_blk, rows, 2 * cols), bf16, VMEM)
    dots = ((n_dev, 8, LANES), f32, VMEM)
    sends = [((2 - e % 2, n_blk, step, 2 * cols), bf16, VMEM) for e in range(1, n_op)]
    inter = pltpu.VMEM((n_blk + 1, n_pair * terms, rows, 2 * cols), bf16)
    left_late = (n_late, n_pair * terms, rows, rows)
    cost = dict(flops=2 * n_blk * rows * 2 * cols * terms * n_pair * (rows + 2 * cols), nbytes=6 << 20)

    def totals(parts):
        return lax.all_to_all(parts, ("blk", "op"), 0, 0, tiled=True)

    part1, raw, kept, dots1, *out1 = kernel(
        functools.partial(first_body, n_blk, n_pair, counts, halves),
        tables + left_ins + right_ins + psi_ins + [(raw_early, VMEM), (inter_early, VMEM)] + diags,
        [narrow, narrow, (left_late, bf16, HBM), dots] + sends[1:],
        [inter, pltpu.SemaphoreType.DMA((sum(counts) + 2,))],
        **cost,
    )
    parts1, other1, got1 = lax.optimization_barrier(
        (
            totals(dots1),
            swap(part1, 1, n_op),
            [swap(block, e, n_op) for e, block in enumerate(out1, 2)],
        )
    )
    dots2, own, *out2 = kernel(
        functools.partial(second_body, n_blk, n_pair, count),
        tables + [(left_early, HBM), (kept, HBM)] + right_ins
        + [(x, VMEM) for x in (parts1, raw, part1, other1)] + diags,
        [dots, ((4, n_blk, step, 2 * cols), bf16, VMEM)] + sends,
        [
            inter,
            pltpu.VMEM((n_blk, rows, 2 * cols), f32),
            pltpu.VMEM((n_blk, rows, 2 * cols), f32),
            pltpu.VMEM((n_blk, rows, 2 * cols), bf16),
            pltpu.VMEM((n_blk, rows, 2 * cols), bf16),
            pltpu.VMEM((n_blk, *left_late[1:]), bf16),
            pltpu.SemaphoreType.DMA((n_blk,)),
        ],
        **cost,
    )
    parts2 = totals(dots2)
    got2 = [swap(block, e, n_op) for e, block in enumerate(out2, 1)]
    final = ((n_blk, step, n_op * cols), bf16, VMEM)
    new, res, energy = kernel(
        functools.partial(third_body, n_blk, n_op, count),
        [(slots, SMEM)] + [(x, VMEM) for x in (parts1, parts2)] + diags
        + [(x, VMEM) for x in (own, *got1, *got2)],
        [final, final, ((1,), f32, SMEM)],
        nbytes=4 << 20,
    )
    return new, res, energy


def solution(mesh):
    placed = (
        P(("grp", "blk"), None, None),
        P("op", ("grp", "blk"), None, None),
        P("op", ("grp", "blk"), None, None),
        P("op"),
        P("grp"),
        P("grp"),
        P("grp", None),
        P(("grp", "blk")),
    )

    def body(*args):
        psi, left_ops, right_ops, diag_right = args[0], args[1], args[2], args[7]
        n_op = mesh.shape["op"]
        cols = diag_right.shape[0] // n_op
        fits = (
            psi.shape[0] == 1
            and diag_right.shape[0] % n_op == 0
            and cols == LANES
            and n_op % 2 == 0
            and cols % right_ops.shape[2] == 0
            and cols // right_ops.shape[2] * n_op == right_ops.shape[1]
            and psi.shape[1] % (16 * n_op) == 0
            and n_op & (n_op - 1) == 0
            and n_op <= 4
            and mesh.shape["blk"] > 3
        )
        return (per_device if fits else per_device_general)(*args)

    return jax.shard_map(
        body,
        mesh=mesh,
        in_specs=placed,
        out_specs=(P("grp", "op", "blk"), P("grp", "op", "blk"), P("grp")),
        check_vma=False,
    )
```

```python
import functools

import jax
import jax.numpy as jnp
from jax import lax
from jax.experimental import pallas as pl
from jax.experimental.pallas import tpu as pltpu
from jax.sharding import PartitionSpec as P

EPS = 1e-06
LANES = 128
VMEM_LIMIT = 20 * 1024 * 1024


def per_device_general(
    psi, left_ops, right_ops, term_shift, slot_sector, sector_width, diag_left, diag_right
):
    sec_dev, rows, ncols = psi.shape
    nsec = slot_sector.shape[0]
    terms_dev = left_ops.shape[0]
    right_local = right_ops.shape[1]
    right_width = right_ops.shape[2]
    local_cols = diag_right.shape[0]
    count = float(nsec * rows * ncols)
    match = slot_sector[:, None] == jnp.arange(nsec)[None, :]
    widths = jnp.sum(jnp.where(match, sector_width[None, :], 0), axis=1)
    mask_all = (jnp.arange(rows)[None, :] < widths[:, None]).astype(jnp.float32)
    own_mask = lax.dynamic_slice_in_dim(mask_all, lax.axis_index("blk") * sec_dev, sec_dev, 0)
    raw = psi.astype(jnp.float32) * own_mask[:, :, None]
    squares = lax.psum(jnp.sum(raw * raw), "blk")
    v_left = (raw * lax.rsqrt(squares / count + EPS)).astype(jnp.bfloat16)
    onehots = (
        slot_sector[None, None, :] == slot_sector[None, :, None] - term_shift[:, None, None]
    ).astype(jnp.bfloat16)
    op_rows = rows // lax.axis_size("op")
    op_start = lax.axis_index("op") * op_rows
    dmat = diag_left[:, :, None] + diag_right[None, None, :]

    def left_local(field):
        return jnp.einsum(
            "ksij,sjc->ksic", left_ops, field, preferred_element_type=jnp.float32
        ).astype(jnp.bfloat16)

    def right_part(moved_in):
        flat = moved_in.reshape(terms_dev, nsec, rows * local_cols)
        shifted = jnp.einsum(
            "kts,ksx->ktx", onehots, flat, preferred_element_type=jnp.float32
        ).astype(jnp.bfloat16)
        shifted = shifted.reshape(terms_dev, nsec, rows, right_local, right_width)
        accum = jnp.einsum(
            "ktwrc,krdc->twrd", shifted, right_ops, preferred_element_type=jnp.float32
        )
        return accum.reshape(nsec, rows, local_cols) * mask_all[:, :, None]

    def op_total(partial_value):
        return lax.psum(partial_value.astype(jnp.bfloat16), "op").astype(jnp.float32)

    def final_rows(array):
        return lax.dynamic_slice_in_dim(array, op_start, op_rows, 1)

    def reduce_dots(values):
        sums = lax.psum(values, "blk")
        return tuple((item / count for item in sums))

    moved_first, v_moved = (
        lax.all_to_all(left_local(v_left), "blk", split_axis=3, concat_axis=1, tiled=True),
        lax.all_to_all(v_left[None], "blk", split_axis=3, concat_axis=1, tiled=True),
    )
    v_right = v_moved[0]
    vec32 = v_right.astype(jnp.float32)
    first_sigma = op_total(right_part(moved_first)) + dmat * vec32
    theta = reduce_dots((jnp.sum(vec32 * first_sigma),))[0]
    resid = first_sigma - theta * vec32
    den = dmat - theta
    corr = resid * den / jnp.maximum(den * den, 0.25)
    along = reduce_dots((jnp.sum(vec32 * corr),))[0]
    orth = corr - along * vec32
    norm_sq = reduce_dots((jnp.sum(orth * orth),))[0]
    update = (orth * lax.rsqrt(norm_sq + EPS)).astype(jnp.bfloat16)
    upd32 = update.astype(jnp.float32)
    upd_left = lax.all_to_all(update, "blk", split_axis=0, concat_axis=2, tiled=True)
    moved_second = lax.all_to_all(
        left_local(upd_left), "blk", split_axis=3, concat_axis=1, tiled=True
    )
    second_sigma = op_total(right_part(moved_second)) + dmat * upd32
    v_s1, u_s0, u_s1 = reduce_dots(
        (jnp.sum(vec32 * second_sigma), jnp.sum(upd32 * first_sigma), jnp.sum(upd32 * second_sigma))
    )
    h_mix = 0.5 * (v_s1 + u_s0)
    coef_v, coef_u, energy = ritz(theta, h_mix, u_s1)
    newvec = coef_v * vec32 + coef_u * upd32
    image = coef_v * first_sigma + coef_u * second_sigma
    new_out = final_rows(newvec.astype(jnp.bfloat16))
    res_out = final_rows((image - energy * newvec).astype(jnp.bfloat16))
    return (new_out, res_out, jnp.reshape(energy, (1,)))


def ritz(theta, h_mix, h_two):
    angle = 0.5 * jnp.arctan2(2.0 * h_mix, theta - h_two)
    sine = jnp.sin(angle)
    flip = jnp.where(sine > 0, -1.0, 1.0)
    coef_v = -sine * flip
    coef_u = jnp.cos(angle) * flip
    half = 0.5 * (theta - h_two)
    energy = 0.5 * (theta + h_two) - jnp.sqrt(half * half + h_mix * h_mix)
    return coef_v, coef_u, energy


VMEM, SMEM, HBM = pltpu.VMEM, pltpu.SMEM, pltpu.HBM


def kernel(body, ins, outs, scratch=(), flops=0, nbytes=0):
    return pl.pallas_call(
        body,
        out_shape=[
            HBM(shape, dtype) if space == HBM else jax.ShapeDtypeStruct(shape, dtype)
            for shape, dtype, space in outs
        ],
        in_specs=[pl.BlockSpec(memory_space=space) for _, space in ins],
        out_specs=[pl.BlockSpec(memory_space=space) for _, _, space in outs],
        scratch_shapes=list(scratch),
        compiler_params=pltpu.CompilerParams(vmem_limit_bytes=VMEM_LIMIT),
        cost_estimate=pl.CostEstimate(flops=flops, bytes_accessed=nbytes, transcendentals=0),
    )(*[pltpu.with_memory_space_constraint(x, HBM) if space == HBM else x for x, space in ins])


def ring_at(place, n_blk):
    place = place % n_blk if isinstance(place, int) else lax.rem(place + n_blk, n_blk)
    odd, even = 2 * place - 1, 2 * (n_blk - place)
    if isinstance(place, int):
        return 0 if place == 0 else odd if odd < n_blk else even
    return jnp.where(place == 0, 0, jnp.where(odd < n_blk, odd, even))


def ring_place(index, n_blk):
    odd, even = (index + 1) // 2, lax.rem(n_blk - index // 2, n_blk)
    return jnp.where(lax.rem(index, 2) == 1, odd, even)


def onward(block, d, n_blk):
    pairs = [(ring_at(i, n_blk), ring_at(i + d, n_blk)) for i in range(n_blk)]
    return lax.ppermute(block, "blk", pairs)


def swap(block, e, n_op):
    return lax.ppermute(block, "op", [(i, i ^ e) for i in range(n_op)])


def gather(own, n_blk, n_op, pack, table, early):
    bits = [1 << b for b in reversed(range(1, n_op.bit_length() - 1))]
    order = sorted(range(1, n_blk), key=lambda d: min(d, n_blk - d))
    left, psi, right, tables, columns = {(0, 0): own}, {}, None, None, None
    waiting, late, made = {(0, 0): 0}, None, None
    for j in range(n_blk + len(bits)):
        new, moved = {}, {}
        for (d, e), done in waiting.items():
            if e == 0 and d + 1 < n_blk:
                new[d + 1, 0] = onward(left[d, 0], 1, n_blk), 0
            for b in range(done, len(bits)):
                new[d, e ^ bits[b]] = swap(left[d, e], bits[b], n_op), b + 1
        kept = {key: block for key, (block, _) in new.items()}
        if late is not None:
            moved["psi"] = late
        if j == 0:
            columns, packed = pack()
            moved["right"] = [packed[0]]
            moved["right"] += [swap(part, 2 * e, n_op) for e, part in enumerate(packed[1:], 1)]
        if j == 1:
            moved["tables"] = table(right)
        if j == n_blk - 1 and j >= len(bits) + 1:
            n_early = min(2, n_blk - 1)
            psi[0] = [columns[0]]
            moved["early"] = early(left, psi, n_early, tables)
        if 2 <= j < n_blk:
            moved["other"] = swap(psi[order[j - 2]][0], 1, n_op)
        late = onward(columns[order[j]], order[j], n_blk) if j < n_blk - 1 else None
        if not kept and not moved:
            break
        waiting = {key: done for key, (_, done) in new.items()}
        kept, moved = lax.optimization_barrier((kept, moved))
        left.update(kept)
        right, tables = moved.get("right", right), moved.get("tables", tables)
        made = moved.get("early", made)
        if "psi" in moved:
            psi[order[j - 1]] = [moved["psi"]]
        if "other" in moved:
            psi[order[j - 2]].append(moved["other"])
    return left, psi, right, tables, made


def place_of():
    return lax.axis_index("blk"), lax.axis_index("op")


def pack_body(n_blk, n_op, shift, _, psi, right_in, *outs):
    n_pair = n_op // 2
    psi_out, right_out, right, sems = outs[:n_blk], outs[n_blk : n_blk + n_pair], outs[-2], outs[-1]
    terms, local, width, _ = right.shape
    cols = local * width // n_op
    per = cols // width
    own_blk, own_op = place_of()
    fetch = pltpu.make_async_copy(right_in, right, sems.at[2 * n_blk])
    fetch.start()
    copies = []
    for d in range(n_blk):
        there = ring_at(ring_place(own_blk, n_blk) + d, n_blk) * n_op
        for h in range(psi_out[d].shape[1] // cols):
            start = pl.multiple_of((there + (own_op ^ h)) * cols, LANES)
            copy = pltpu.make_async_copy(
                psi.at[0, :, pl.ds(start, cols)],
                psi_out[d].at[:, h * cols : (h + 1) * cols],
                sems.at[2 * d + h],
            )
            copy.start()
            copies.append(copy)
    lane = lax.broadcasted_iota(jnp.int32, (16, 2 * cols), 1)
    line = jnp.zeros((16, 2 * cols), jnp.float32)
    for k in range(terms):
        line = jnp.where(lane == k, shift[k].astype(jnp.float32), line)
    square = [lax.broadcasted_iota(jnp.int32, (width, width), axis) for axis in (0, 1)]
    unit = (square[0] == square[1]).astype(jnp.bfloat16)
    fetch.wait()
    for e in range(n_pair):
        for k in range(terms):
            turned = []
            for h in range(2):
                first = (own_op ^ (2 * e) ^ h) * per
                for r in range(per):
                    turned.append(
                        lax.dot_general(
                            right[k, first + r], unit, (((0,), (0,)), ((), ())),
                            preferred_element_type=jnp.float32,
                        )
                    )
            side_by_side = jnp.concatenate(turned, axis=1).astype(jnp.bfloat16)
            right_out[e][k * width : (k + 1) * width] = side_by_side
        right_out[e][terms * width :] = line.astype(jnp.bfloat16)
    for copy in copies:
        copy.wait()


def table_body(n_blk, terms, sector, width, left_diag, right_diag, *refs):
    tails, src, widths, slots, diag, right_out = refs[:-5], *refs[-5:]
    right_out[...] = right_diag[...]
    n_pair = len(tails)
    rows, cols = tails[0].shape
    own_blk, _ = place_of()
    lane = lax.broadcasted_iota(jnp.int32, (16, cols), 1)
    for d in range(n_blk):
        slot = ring_at(ring_place(own_blk, n_blk) - d, n_blk)
        slots[d] = slot
        widths[d] = width[sector[slot]]
    for e in range(n_pair):
        tail = tails[e][rows - 16 :].astype(jnp.float32)
        for k in range(terms):
            shift = jnp.max(jnp.where(lane == k, tail, -1e9)).astype(jnp.int32)
            for t in range(n_blk):
                want = sector[slots[t]] - shift
                found = jnp.int32(n_blk)
                for d in range(n_blk):
                    found = jnp.where(sector[slots[d]] == want, d, found)
                src[(t * n_pair + e) * terms + k] = found
    for d in range(n_blk):
        row = left_diag[pl.ds(slots[d], 1), :]
        diag[d] = jnp.transpose(jnp.broadcast_to(row, (diag.shape[2], row.shape[1])))


def diagonal(diag, right_diag, d, h):
    cols = diag.shape[2]
    _, own_op = place_of()
    start = pl.multiple_of((own_op ^ h) * cols, LANES)
    return diag[d] + right_diag[:, pl.ds(start, cols)]


def row_mask(width, shape):
    return lax.broadcasted_iota(jnp.int32, shape, 0) < width


def fold(x):
    return jnp.sum(x.reshape(-1, 8, x.shape[-1]), axis=0)


def whole(x):
    return jnp.sum(jnp.sum(x, axis=0, keepdims=True), axis=1, keepdims=True)


def spread(values, out):
    lane = lax.broadcasted_iota(jnp.int32, out.shape[1:], 1)
    row = jnp.zeros(out.shape[1:], jnp.float32)
    for j, value in enumerate(values):
        row = jnp.where(lane == j, value, row)
    for d in range(out.shape[0]):
        out[d] = row


def by_block(packed, terms, k):
    rows, cols = packed.shape
    width = (rows - 16) // terms
    lane = lax.broadcasted_iota(jnp.int32, (width, cols), 1)
    block = packed[k * width : (k + 1) * width].astype(jnp.float32)
    parts = []
    for r in range(cols // width):
        inside = (lane >= r * width) & (lane < (r + 1) * width)
        parts.append(jnp.where(inside, block, 0.0).astype(jnp.bfloat16))
    return jnp.concatenate(parts, axis=0)


def left_products(block, left, inter):
    n_terms, rows, cols = inter.shape
    at = 0
    while at < n_terms:
        ops = left(at)
        terms = ops.shape[0]
        prod = jnp.dot(ops.reshape(terms * rows, rows), block, preferred_element_type=jnp.float32)
        inter[at : at + terms] = prod.astype(jnp.bfloat16).reshape(terms, rows, cols)
        at += terms


def sum_terms(src, widths, inter, right, out, emit):
    n_blk, n_terms, _, _ = inter.shape
    n_blk -= 1
    terms = n_terms // len(right)
    turned = [by_block(right[j // terms], terms, j % terms) for j in range(n_terms)]
    for t in range(n_blk):
        total = None
        for j in range(n_terms):
            part = jnp.dot(
                inter[src[t * n_terms + j], j], turned[j], preferred_element_type=jnp.float32
            )
            total = part if total is None else total + part
        total = jnp.where(row_mask(widths[t], total.shape), total, 0.0)
        out[t] = total.astype(jnp.bfloat16)
        emit(t, total)


def keep(left, left_out, sems):
    copies = []
    for d, line in enumerate(left):
        for e, ref in enumerate(line):
            copies.append(pltpu.make_async_copy(ref, left_out.at[d, e], sems.at[d * len(line) + e]))
            copies[-1].start()
    return copies


def masked(psi, width, out):
    at = 0
    for ref in psi:
        block = ref[...].astype(jnp.float32)
        block = jnp.where(row_mask(width, block.shape), block, 0.0)
        out[:, at : at + block.shape[1]] = block.astype(jnp.bfloat16)
        at += block.shape[1]


def take(refs, counts):
    out = []
    for count in counts:
        out.append(refs[:count])
        refs = refs[count:]
    return out, refs


def products_of(psi, left, widths, first, raw_out, inter):
    for d, line in enumerate(left):
        masked(psi[d], widths[first + d], raw_out.at[d])
        terms = line[0].shape[0]
        left_products(raw_out[d], lambda at: line[at // terms][...], inter.at[d])


def early_body(n_pair, counts, widths, *refs):
    left, refs = take(refs, [n_pair] * len(counts))
    psi, (raw_out, inter_out, left_out, sems) = take(refs, counts)
    copies = keep(left, left_out, sems)
    products_of(psi, left, widths, 0, raw_out, inter_out)
    for copy in copies:
        copy.wait()


def first_body(n_blk, n_pair, counts, src, widths, *refs):
    n_late = len(counts)
    n_early = n_blk - n_late
    left, refs = take(refs, [n_pair] * n_late)
    (right,), refs = take(refs, [n_pair])
    psi, refs = take(refs, counts)
    raw_in, inter_in, diag, right_diag, part_out, raw_out, left_out, dots_out = refs[:8]
    sends, (inter, sems) = refs[8:-2], refs[-2:]
    copies = keep(left, left_out, sems)
    for j, (given, own) in enumerate(((inter_in, inter), (raw_in, raw_out))):
        copies.append(
            pltpu.make_async_copy(given, own.at[:n_early], sems.at[n_late * n_pair + j])
        )
        copies[-1].start()
    inter[n_blk] = jnp.zeros_like(inter[n_blk])
    products_of(
        psi, left, widths, n_early, raw_out.at[n_early:], inter.at[n_early:n_blk]
    )
    for copy in copies:
        copy.wait()
    cols = diag.shape[2]
    zero = jnp.zeros((8, cols), jnp.float32)
    sums = [zero, zero]

    def emit(d, total):
        for h in range(2):
            part = slice(h * cols, (h + 1) * cols)
            raw = raw_out[d, :, part].astype(jnp.float32)
            image = total[:, part]
            if h == 0:
                image = image + diagonal(diag, right_diag, d, h) * raw
                sums[0] = sums[0] + fold(raw * raw)
            sums[1] = sums[1] + fold(raw * image)
        for e, send in enumerate(sends, 2):
            send_rows(e, send, d, raw_out, part_out)

    sum_terms(src, widths, inter, right, part_out, emit)
    spread([whole(x) for x in sums], dots_out)


def send_rows(e, send, d, field, part):
    _, own_op = place_of()
    step = send.shape[2]
    rows = pl.ds(pl.multiple_of((own_op ^ e) * step, step), step)
    if e % 2 == 0:
        send[0, d] = field[d, rows].astype(send.dtype)
    send[send.shape[0] - 1, d] = part[d, rows]


def total_of(mine, other, d, h, cols):
    own = mine[d, :, h * cols : (h + 1) * cols].astype(jnp.float32)
    return own + other[d, :, (1 - h) * cols : (2 - h) * cols].astype(jnp.float32)


def norm_theta(parts, count):
    tot = jnp.sum(parts, axis=0) * (1.0 / count)
    scale = lax.rsqrt(tot[:, 0:1] + EPS)
    return scale, tot[:, 1:2] * scale * scale


def second_body(n_blk, n_pair, count, src, widths, left_early, left_late, *refs):
    right, refs = refs[:n_pair], refs[n_pair:]
    parts, raw_in, part_in, other_in, diag, right_diag, dots_out, own_out = refs[:8]
    sends, (inter, corr, sig, fld, part_out, held, sems) = refs[8:-7], refs[-7:]
    copies = []
    n_early = left_early.shape[0]
    for d in range(n_blk):
        kept = left_early.at[d] if d < n_early else left_late.at[d - n_early]
        copies.append(pltpu.make_async_copy(kept, held.at[d], sems.at[d]))
        copies[-1].start()
    inter[n_blk] = jnp.zeros_like(inter[n_blk])
    scale, theta = norm_theta(parts[...], count)
    cols = diag.shape[2]
    halves = []
    for h in range(2):
        part = slice(h * cols, (h + 1) * cols)
        vv = vc = vs = jnp.zeros((8, cols), jnp.float32)
        for d in range(n_blk):
            vec = raw_in[d, :, part].astype(jnp.float32) * scale
            sigma = total_of(part_in, other_in, d, h, cols)
            sigma = (sigma + diagonal(diag, right_diag, d, h) * raw_in[d, :, part].astype(jnp.float32)) * scale
            sig[d, :, part] = sigma
            den = diagonal(diag, right_diag, d, h) - theta
            item = (sigma - theta * vec) * den / jnp.maximum(den * den, 0.25)
            corr[d, :, part] = item
            vv, vc, vs = vv + fold(vec * vec), vc + fold(vec * item), vs + fold(vec * sigma)
        halves.append((whole(vv), whole(vc), whole(vs)))
    along = (halves[0][1] + halves[1][1]) / jnp.maximum(halves[0][0] + halves[1][0], 1e-30)
    terms = held.shape[2]
    for copy in copies:
        copy.wait()
    for d in range(n_blk):
        for h in range(2):
            part = slice(h * cols, (h + 1) * cols)
            vec = raw_in[d, :, part].astype(jnp.float32) * scale
            fld[d, :, part] = (corr[d, :, part] - along * vec).astype(jnp.bfloat16)
        left_products(fld[d], lambda at: held[d, at // terms], inter.at[d])
    zero = jnp.zeros((8, cols), jnp.float32)
    sums = [zero for _ in range(5)]

    def emit(d, total):
        for h in range(2):
            part = slice(h * cols, (h + 1) * cols)
            field = fld[d, :, part].astype(jnp.float32)
            vec = raw_in[d, :, part].astype(jnp.float32) * scale
            image = total[:, part]
            if h == 0:
                image = image + diagonal(diag, right_diag, d, h) * field
                for j, prod in enumerate((field * field, vec * field, field * sig[d, :, part])):
                    sums[j] = sums[j] + fold(prod)
            sums[3] = sums[3] + fold(vec * image)
            sums[4] = sums[4] + fold(field * image)
        for e, send in enumerate(sends, 1):
            send_rows(e, send, d, fld, part_out)
        rows = pl.ds(pl.multiple_of(own_op * step, step), step)
        for j, ref in enumerate((raw_in, sig, fld, part_out)):
            own_out[j, d] = ref[d, rows].astype(own_out.dtype)

    _, own_op = place_of()
    step = own_out.shape[2]
    sum_terms(src, widths, inter, right, part_out, emit)
    spread(list(halves[0]) + [whole(x) for x in sums], dots_out)


def ritz_pair(theta, h_mix, h_two):
    diff, twice = theta - h_two, 2.0 * h_mix
    size = jnp.sqrt(diff * diff + twice * twice)
    some = size > 0.0
    safe = jnp.where(some, size, 1.0)
    big = jnp.sqrt(0.5 + 0.5 * jnp.abs(diff) / safe)
    small = 0.5 * jnp.abs(twice) / (safe * big)
    sine = jnp.where(diff >= 0.0, small, big)
    cosine = jnp.where(diff >= 0.0, big, small)
    sine = jnp.where(some, sine, 0.0)
    cosine = jnp.where(some, cosine, 1.0)
    upward = (twice > 0.0) | ((twice == 0.0) & (diff < 0.0))
    return sine, jnp.where(upward, -cosine, cosine), 0.5 * (theta + h_two) - 0.5 * size


def third_body(n_blk, n_op, count, slots, parts1, parts2, diag, right_diag, own, *refs):
    got1, got2 = refs[: n_op - 2], refs[n_op - 2 : 2 * n_op - 3]
    new_out, res_out, energy_out = refs[2 * n_op - 3 :]
    step, cols = new_out.shape[1], new_out.shape[2] // n_op
    own_blk, own_op = place_of()
    scale, theta = norm_theta(parts1[...], count)
    pairs = parts2[...].reshape(n_blk * n_op // 2, 2, *parts2.shape[1:])
    pairs = pairs[:, 0] + pairs[:, 1]
    vv, vc, vs, ff, vf, fs, vt, ft = (pairs[:, 0, j : j + 1] for j in range(8))

    def mean(x):
        return jnp.sum(x, axis=0, keepdims=True) * (1.0 / count)

    def nearest(vv, vc):
        return vc / jnp.maximum(vv, 1e-30)

    along = mean(vc)
    beta = nearest(vv, vc) - along
    norm_sq = mean(ff + 2.0 * beta * vf + beta * beta * vv)
    unit = lax.rsqrt(jnp.maximum(norm_sq, 0.0) + EPS)
    v_s1 = unit * mean(vt + beta * vs)
    u_s0 = unit * mean(fs + beta * vs)
    u_s1 = unit * unit * mean(ft + beta * (vt + fs) + beta * beta * vs)
    cv, cu, energy = ritz_pair(theta, 0.5 * (v_s1 + u_s0), u_s1)
    energy_out[0] = jnp.max(energy)
    cu = cu * unit
    mine = pl.ds(pl.multiple_of(own_op * step, step), step)
    for e in range(0, n_op, 2):
        there = own_blk * n_op + (own_op ^ e)
        pair = parts2[there] + parts2[own_blk * n_op + (own_op ^ e ^ 1)]
        on_vec = cv + cu * (nearest(pair[:, 0:1], pair[:, 1:2]) - along)
        for h in range(2):
            at = pl.multiple_of((own_op ^ e ^ h) * cols, LANES)
            part, crossed = slice(h * cols, (h + 1) * cols), slice((1 - h) * cols, (2 - h) * cols)
            for d in range(n_blk):
                dmat = diag[d, mine] + right_diag[:, pl.ds(at, cols)]
                if e:
                    raw, fld = got1[e - 2][0, d, :, part], got2[e - 1][0, d, :, part]
                    vec = raw.astype(jnp.float32) * scale
                    sigma = got1[e - 2][1, d, :, part].astype(jnp.float32)
                    sigma = sigma + got1[e - 1][0, d, :, crossed].astype(jnp.float32)
                    sigma = sigma * scale + dmat * vec
                    image = got2[e - 1][1, d, :, part].astype(jnp.float32)
                else:
                    raw, sigma, fld, image = (own[j, d, :, part].astype(jnp.float32) for j in range(4))
                    vec = raw * scale
                fld = fld.astype(jnp.float32)
                image = image + got2[e][0, d, :, crossed].astype(jnp.float32) + dmat * fld
                newvec = on_vec * vec + cu * fld
                res = on_vec * sigma + cu * image - energy * newvec
                new_out[slots[d], :, pl.ds(at, cols)] = newvec.astype(jnp.bfloat16)
                res_out[slots[d], :, pl.ds(at, cols)] = res.astype(jnp.bfloat16)


def per_device(
    psi, left_ops, right_ops, term_shift, slot_sector, sector_width, diag_left, diag_right
):
    n_blk, n_op = lax.axis_size("blk"), lax.axis_size("op")
    _, rows, ncols = psi.shape
    terms, _, width, _ = right_ops.shape
    n_pair = n_op // 2
    cols = diag_right.shape[0] // n_op
    step = rows // n_op
    count = float(n_blk * rows * ncols)
    n_dev = n_blk * n_op
    bf16, f32, i32 = jnp.bfloat16, jnp.float32, jnp.int32
    last = sorted(range(1, n_blk), key=lambda d: min(d, n_blk - d))[-1]

    def pack():
        first = swap(term_shift, 1, n_op)
        sent = kernel(
            functools.partial(pack_body, n_blk, n_op),
            [(term_shift, SMEM), (first, SMEM), (psi, HBM), (right_ops, HBM)],
            [((rows, 2 * cols if d in (0, last) else cols), bf16, VMEM) for d in range(n_blk)]
            + [((terms * width + 16, 2 * cols), bf16, VMEM)] * n_pair,
            [pltpu.VMEM(right_ops.shape, bf16), pltpu.SemaphoreType.DMA((2 * n_blk + 1,))],
            nbytes=1 << 20,
        )
        return sent[:n_blk], sent[n_blk:]

    def table(right):
        return kernel(
            functools.partial(table_body, n_blk, terms),
            [(slot_sector, SMEM), (sector_width, SMEM), (diag_left, VMEM), (diag_right[None], VMEM)]
            + [(block, VMEM) for block in right],
            [((n_blk * n_pair * terms,), i32, SMEM)]
            + [((n_blk,), i32, SMEM)] * 2
            + [((n_blk, rows, LANES), f32, VMEM), ((1, n_op * cols), f32, VMEM)],
        )

    def inputs(left, psi, those):
        blocks = [left[d, 2 * e] for d in those for e in range(n_pair)]
        halves = [half for d in those for half in psi[d]]
        return [(x, VMEM) for x in blocks], [(x, VMEM) for x in halves], [len(psi[d]) for d in those]

    def early(left, psi, n_early, tables):
        left_ins, psi_ins, counts = inputs(left, psi, range(n_early))
        return kernel(
            functools.partial(early_body, n_pair, counts),
            [(tables[1], SMEM)] + left_ins + psi_ins,
            [
                ((n_early, rows, 2 * cols), bf16, VMEM),
                ((n_early, n_pair * terms, rows, 2 * cols), bf16, VMEM),
                ((n_early, n_pair, terms, rows, rows), bf16, HBM),
            ],
            [pltpu.SemaphoreType.DMA((n_early * n_pair,))],
            flops=2 * n_early * rows * rows * 2 * cols * terms * n_pair,
            nbytes=4 << 20,
        )

    left, psi_by, right, (src, widths, slots, *both), (raw_early, inter_early, left_early) = gather(
        left_ops[:, 0], n_blk, n_op, pack, table, early
    )
    n_early = raw_early.shape[0]
    n_late = n_blk - n_early
    left_ins, psi_ins, counts = inputs(left, psi_by, range(n_early, n_blk))
    right_ins = [(block, VMEM) for block in right]
    diags = [(x, VMEM) for x in both]

    tables = [(src, SMEM), (widths, SMEM)]
    narrow = ((n_blk, rows, 2 * cols), bf16, VMEM)
    dots = ((n_dev, 1, LANES), f32, VMEM)
    sends = [((2 - e % 2, n_blk, step, 2 * cols), bf16, VMEM) for e in range(1, n_op)]
    inter = pltpu.VMEM((n_blk + 1, n_pair * terms, rows, 2 * cols), bf16)
    left_late = (n_late, n_pair, terms, rows, rows)
    cost = dict(flops=2 * n_blk * rows * 2 * cols * terms * n_pair * (rows + 2 * cols), nbytes=6 << 20)

    def totals(parts):
        return lax.all_to_all(parts, ("blk", "op"), 0, 0, tiled=True)

    part1, raw, kept, dots1, *out1 = kernel(
        functools.partial(first_body, n_blk, n_pair, counts),
        tables + left_ins + right_ins + psi_ins + [(raw_early, VMEM), (inter_early, VMEM)] + diags,
        [narrow, narrow, (left_late, bf16, HBM), dots] + sends[1:],
        [inter, pltpu.SemaphoreType.DMA((n_late * n_pair + 2,))],
        **cost,
    )
    parts1, other1, got1 = lax.optimization_barrier(
        (
            totals(dots1),
            swap(part1, 1, n_op),
            [swap(block, e, n_op) for e, block in enumerate(out1, 2)],
        )
    )
    dots2, own, *out2 = kernel(
        functools.partial(second_body, n_blk, n_pair, count),
        tables + [(left_early, HBM), (kept, HBM)] + right_ins
        + [(x, VMEM) for x in (parts1, raw, part1, other1)] + diags,
        [dots, ((4, n_blk, step, 2 * cols), bf16, VMEM)] + sends,
        [
            inter,
            pltpu.VMEM((n_blk, rows, 2 * cols), f32),
            pltpu.VMEM((n_blk, rows, 2 * cols), f32),
            pltpu.VMEM((n_blk, rows, 2 * cols), bf16),
            pltpu.VMEM((n_blk, rows, 2 * cols), bf16),
            pltpu.VMEM((n_blk, *left_late[1:]), bf16),
            pltpu.SemaphoreType.DMA((n_blk,)),
        ],
        **cost,
    )
    parts2 = totals(dots2)
    got2 = [swap(block, e, n_op) for e, block in enumerate(out2, 1)]
    final = ((n_blk, step, n_op * cols), bf16, VMEM)
    new, res, energy = kernel(
        functools.partial(third_body, n_blk, n_op, count),
        [(slots, SMEM)] + [(x, VMEM) for x in (parts1, parts2)] + diags
        + [(x, VMEM) for x in (own, *got1, *got2)],
        [final, final, ((1,), f32, SMEM)],
        nbytes=4 << 20,
    )
    return new, res, energy


def solution(mesh):
    placed = (
        P(("grp", "blk"), None, None),
        P("op", ("grp", "blk"), None, None),
        P("op", ("grp", "blk"), None, None),
        P("op"),
        P("grp"),
        P("grp"),
        P("grp", None),
        P(("grp", "blk")),
    )

    def body(*args):
        psi, left_ops, right_ops, diag_right = args[0], args[1], args[2], args[7]
        n_op = mesh.shape["op"]
        cols = diag_right.shape[0] // n_op
        fits = (
            psi.shape[0] == 1
            and diag_right.shape[0] % n_op == 0
            and cols == LANES
            and n_op % 2 == 0
            and cols % right_ops.shape[2] == 0
            and cols // right_ops.shape[2] * n_op == right_ops.shape[1]
            and psi.shape[1] % (16 * n_op) == 0
            and n_op & (n_op - 1) == 0
            and mesh.shape["blk"] > n_op.bit_length() - 1
        )
        return (per_device if fits else per_device_general)(*args)

    return jax.shard_map(
        body,
        mesh=mesh,
        in_specs=placed,
        out_specs=(P("grp", "op", "blk"), P("grp", "op", "blk"), P("grp")),
        check_vma=False,
    )
```

```python
import functools

import jax
import jax.numpy as jnp
from jax import lax
from jax.experimental import pallas as pl
from jax.experimental.pallas import tpu as pltpu
from jax.sharding import PartitionSpec as P

EPS = 1e-06
LANES = 128
VMEM_LIMIT = 20 * 1024 * 1024


def per_device_general(
    psi, left_ops, right_ops, term_shift, slot_sector, sector_width, diag_left, diag_right
):
    sec_dev, rows, ncols = psi.shape
    nsec = slot_sector.shape[0]
    terms_dev = left_ops.shape[0]
    right_local = right_ops.shape[1]
    right_width = right_ops.shape[2]
    local_cols = diag_right.shape[0]
    count = float(nsec * rows * ncols)
    match = slot_sector[:, None] == jnp.arange(nsec)[None, :]
    widths = jnp.sum(jnp.where(match, sector_width[None, :], 0), axis=1)
    mask_all = (jnp.arange(rows)[None, :] < widths[:, None]).astype(jnp.float32)
    own_mask = lax.dynamic_slice_in_dim(mask_all, lax.axis_index("blk") * sec_dev, sec_dev, 0)
    raw = psi.astype(jnp.float32) * own_mask[:, :, None]
    squares = lax.psum(jnp.sum(raw * raw), "blk")
    v_left = (raw * lax.rsqrt(squares / count + EPS)).astype(jnp.bfloat16)
    onehots = (
        slot_sector[None, None, :] == slot_sector[None, :, None] - term_shift[:, None, None]
    ).astype(jnp.bfloat16)
    op_rows = rows // lax.axis_size("op")
    op_start = lax.axis_index("op") * op_rows
    dmat = diag_left[:, :, None] + diag_right[None, None, :]

    def left_local(field):
        return jnp.einsum(
            "ksij,sjc->ksic", left_ops, field, preferred_element_type=jnp.float32
        ).astype(jnp.bfloat16)

    def right_part(moved_in):
        flat = moved_in.reshape(terms_dev, nsec, rows * local_cols)
        shifted = jnp.einsum(
            "kts,ksx->ktx", onehots, flat, preferred_element_type=jnp.float32
        ).astype(jnp.bfloat16)
        shifted = shifted.reshape(terms_dev, nsec, rows, right_local, right_width)
        accum = jnp.einsum(
            "ktwrc,krdc->twrd", shifted, right_ops, preferred_element_type=jnp.float32
        )
        return accum.reshape(nsec, rows, local_cols) * mask_all[:, :, None]

    def op_total(partial_value):
        return lax.psum(partial_value.astype(jnp.bfloat16), "op").astype(jnp.float32)

    def final_rows(array):
        return lax.dynamic_slice_in_dim(array, op_start, op_rows, 1)

    def reduce_dots(values):
        sums = lax.psum(values, "blk")
        return tuple((item / count for item in sums))

    moved_first, v_moved = (
        lax.all_to_all(left_local(v_left), "blk", split_axis=3, concat_axis=1, tiled=True),
        lax.all_to_all(v_left[None], "blk", split_axis=3, concat_axis=1, tiled=True),
    )
    v_right = v_moved[0]
    vec32 = v_right.astype(jnp.float32)
    first_sigma = op_total(right_part(moved_first)) + dmat * vec32
    theta = reduce_dots((jnp.sum(vec32 * first_sigma),))[0]
    resid = first_sigma - theta * vec32
    den = dmat - theta
    corr = resid * den / jnp.maximum(den * den, 0.25)
    along = reduce_dots((jnp.sum(vec32 * corr),))[0]
    orth = corr - along * vec32
    norm_sq = reduce_dots((jnp.sum(orth * orth),))[0]
    update = (orth * lax.rsqrt(norm_sq + EPS)).astype(jnp.bfloat16)
    upd32 = update.astype(jnp.float32)
    upd_left = lax.all_to_all(update, "blk", split_axis=0, concat_axis=2, tiled=True)
    moved_second = lax.all_to_all(
        left_local(upd_left), "blk", split_axis=3, concat_axis=1, tiled=True
    )
    second_sigma = op_total(right_part(moved_second)) + dmat * upd32
    v_s1, u_s0, u_s1 = reduce_dots(
        (jnp.sum(vec32 * second_sigma), jnp.sum(upd32 * first_sigma), jnp.sum(upd32 * second_sigma))
    )
    h_mix = 0.5 * (v_s1 + u_s0)
    coef_v, coef_u, energy = ritz(theta, h_mix, u_s1)
    newvec = coef_v * vec32 + coef_u * upd32
    image = coef_v * first_sigma + coef_u * second_sigma
    new_out = final_rows(newvec.astype(jnp.bfloat16))
    res_out = final_rows((image - energy * newvec).astype(jnp.bfloat16))
    return (new_out, res_out, jnp.reshape(energy, (1,)))


def ritz(theta, h_mix, h_two):
    angle = 0.5 * jnp.arctan2(2.0 * h_mix, theta - h_two)
    sine = jnp.sin(angle)
    flip = jnp.where(sine > 0, -1.0, 1.0)
    coef_v = -sine * flip
    coef_u = jnp.cos(angle) * flip
    half = 0.5 * (theta - h_two)
    energy = 0.5 * (theta + h_two) - jnp.sqrt(half * half + h_mix * h_mix)
    return coef_v, coef_u, energy


VMEM, SMEM, HBM = pltpu.VMEM, pltpu.SMEM, pltpu.HBM


def kernel(body, ins, outs, scratch=(), flops=0, nbytes=0, in_place=None):
    return pl.pallas_call(
        body,
        out_shape=[
            HBM(shape, dtype) if space == HBM else jax.ShapeDtypeStruct(shape, dtype)
            for shape, dtype, space in outs
        ],
        in_specs=[pl.BlockSpec(memory_space=space) for _, space in ins],
        out_specs=[pl.BlockSpec(memory_space=space) for _, _, space in outs],
        scratch_shapes=list(scratch),
        input_output_aliases=in_place or {},
        compiler_params=pltpu.CompilerParams(vmem_limit_bytes=VMEM_LIMIT),
        cost_estimate=pl.CostEstimate(flops=flops, bytes_accessed=nbytes, transcendentals=0),
    )(*[pltpu.with_memory_space_constraint(x, HBM) if space == HBM else x for x, space in ins])


def ring_at(place, n_blk):
    place = place % n_blk if isinstance(place, int) else lax.rem(place + n_blk, n_blk)
    odd, even = 2 * place - 1, 2 * (n_blk - place)
    if isinstance(place, int):
        return 0 if place == 0 else odd if odd < n_blk else even
    return jnp.where(place == 0, 0, jnp.where(odd < n_blk, odd, even))


def ring_place(index, n_blk):
    odd, even = (index + 1) // 2, lax.rem(n_blk - index // 2, n_blk)
    return jnp.where(lax.rem(index, 2) == 1, odd, even)


def onward(block, d, n_blk):
    pairs = [(ring_at(i, n_blk), ring_at(i + d, n_blk)) for i in range(n_blk)]
    return lax.ppermute(block, "blk", pairs)


def swap(block, e, n_op):
    return lax.ppermute(block, "op", [(i, i ^ e) for i in range(n_op)])


def gather(own, n_blk, n_op, pack, table, early):
    bits = [1 << b for b in reversed(range(1, n_op.bit_length() - 1))]
    order = sorted(range(1, n_blk), key=lambda d: min(d, n_blk - d))
    left, psi, right, tables, columns = {(0, 0): own}, {}, None, None, None
    waiting, late, made = {(0, 0): 0}, None, None
    for j in range(n_blk + len(bits)):
        new, moved = {}, {}
        for (d, e), done in waiting.items():
            if e == 0 and d + 1 < n_blk:
                new[d + 1, 0] = onward(left[d, 0], 1, n_blk), 0
            for b in range(done, len(bits)):
                new[d, e ^ bits[b]] = swap(left[d, e], bits[b], n_op), b + 1
        kept = {key: block for key, (block, _) in new.items()}
        if late is not None:
            moved["psi"] = late
        if j == 0:
            columns, packed = pack()
            moved["right"] = [packed[0]]
            moved["right"] += [swap(part, 2 * e, n_op) for e, part in enumerate(packed[1:], 1)]
        if j == 1:
            moved["tables"] = table(right)
        if j == n_blk - 1 and j >= len(bits) + 1:
            n_early = min(2, n_blk - 1)
            psi[0] = [columns[0]]
            moved["early"] = early(left, psi, n_early, tables)
        if 2 <= j < n_blk:
            moved["other"] = swap(psi[order[j - 2]][0], 1, n_op)
        late = onward(columns[order[j]], order[j], n_blk) if j < n_blk - 1 else None
        if not kept and not moved:
            break
        waiting = {key: done for key, (_, done) in new.items()}
        kept, moved = lax.optimization_barrier((kept, moved))
        left.update(kept)
        right, tables = moved.get("right", right), moved.get("tables", tables)
        made = moved.get("early", made)
        if "psi" in moved:
            psi[order[j - 1]] = [moved["psi"]]
        if "other" in moved:
            psi[order[j - 2]].append(moved["other"])
    return left, psi, right, tables, made


def place_of():
    return lax.axis_index("blk"), lax.axis_index("op")


def pack_body(n_blk, n_op, shift, _, psi, right_in, *outs):
    n_pair = n_op // 2
    psi_out, right_out, right, sems = outs[:n_blk], outs[n_blk : n_blk + n_pair], outs[-2], outs[-1]
    terms, local, width, _ = right.shape
    cols = local * width // n_op
    per = cols // width
    own_blk, own_op = place_of()
    fetch = pltpu.make_async_copy(right_in, right, sems.at[2 * n_blk])
    fetch.start()
    copies = []
    for d in range(n_blk):
        there = ring_at(ring_place(own_blk, n_blk) + d, n_blk) * n_op
        for h in range(psi_out[d].shape[1] // cols):
            start = pl.multiple_of((there + (own_op ^ h)) * cols, LANES)
            copy = pltpu.make_async_copy(
                psi.at[0, :, pl.ds(start, cols)],
                psi_out[d].at[:, h * cols : (h + 1) * cols],
                sems.at[2 * d + h],
            )
            copy.start()
            copies.append(copy)
    lane = lax.broadcasted_iota(jnp.int32, (16, 2 * cols), 1)
    line = jnp.zeros((16, 2 * cols), jnp.float32)
    for k in range(terms):
        line = jnp.where(lane == k, shift[k].astype(jnp.float32), line)
    square = [lax.broadcasted_iota(jnp.int32, (width, width), axis) for axis in (0, 1)]
    unit = (square[0] == square[1]).astype(jnp.bfloat16)
    fetch.wait()
    for e in range(n_pair):
        for k in range(terms):
            turned = []
            for h in range(2):
                first = (own_op ^ (2 * e) ^ h) * per
                for r in range(per):
                    turned.append(
                        lax.dot_general(
                            right[k, first + r], unit, (((0,), (0,)), ((), ())),
                            preferred_element_type=jnp.float32,
                        )
                    )
            side_by_side = jnp.concatenate(turned, axis=1).astype(jnp.bfloat16)
            right_out[e][k * width : (k + 1) * width] = side_by_side
        right_out[e][terms * width :] = line.astype(jnp.bfloat16)
    for copy in copies:
        copy.wait()


def table_body(n_blk, terms, sector, width, left_diag, right_diag, *refs):
    tails, src, widths, slots, diag, right_out = refs[:-5], *refs[-5:]
    right_out[...] = right_diag[...]
    n_pair = len(tails)
    rows, cols = tails[0].shape
    own_blk, _ = place_of()
    lane = lax.broadcasted_iota(jnp.int32, (16, cols), 1)
    for d in range(n_blk):
        slot = ring_at(ring_place(own_blk, n_blk) - d, n_blk)
        slots[d] = slot
        widths[d] = width[sector[slot]]
    for e in range(n_pair):
        tail = tails[e][rows - 16 :].astype(jnp.float32)
        for k in range(terms):
            shift = jnp.max(jnp.where(lane == k, tail, -1e9)).astype(jnp.int32)
            for t in range(n_blk):
                want = sector[slots[t]] - shift
                found = jnp.int32(n_blk)
                for d in range(n_blk):
                    found = jnp.where(sector[slots[d]] == want, d, found)
                src[(t * n_pair + e) * terms + k] = found
    for d in range(n_blk):
        row = left_diag[pl.ds(slots[d], 1), :]
        diag[d] = jnp.transpose(jnp.broadcast_to(row, (diag.shape[2], row.shape[1])))


def diagonal(diag, right_diag, d, h):
    cols = diag.shape[2]
    _, own_op = place_of()
    start = pl.multiple_of((own_op ^ h) * cols, LANES)
    return diag[d] + right_diag[:, pl.ds(start, cols)]


def row_mask(width, shape):
    return lax.broadcasted_iota(jnp.int32, shape, 0) < width


def fold(x):
    return jnp.sum(x.reshape(-1, 8, x.shape[-1]), axis=0)


def whole(x):
    return jnp.sum(jnp.sum(x, axis=0, keepdims=True), axis=1, keepdims=True)


def spread(values, out):
    lane = lax.broadcasted_iota(jnp.int32, out.shape[1:], 1)
    row = jnp.zeros(out.shape[1:], jnp.float32)
    for j, value in enumerate(values):
        row = jnp.where(lane == j, value, row)
    for d in range(out.shape[0]):
        out[d] = row


def by_block(packed, terms, k):
    rows, cols = packed.shape
    width = (rows - 16) // terms
    lane = lax.broadcasted_iota(jnp.int32, (width, cols), 1)
    block = packed[k * width : (k + 1) * width].astype(jnp.float32)
    parts = []
    for r in range(cols // width):
        inside = (lane >= r * width) & (lane < (r + 1) * width)
        parts.append(jnp.where(inside, block, 0.0).astype(jnp.bfloat16))
    return jnp.concatenate(parts, axis=0)


def left_products(block, left, inter):
    n_terms, rows, cols = inter.shape
    at = 0
    while at < n_terms:
        ops = left(at)
        terms = ops.shape[0]
        prod = jnp.dot(ops.reshape(terms * rows, rows), block, preferred_element_type=jnp.float32)
        inter[at : at + terms] = prod.astype(jnp.bfloat16).reshape(terms, rows, cols)
        at += terms


def sum_terms(src, widths, inter, right, out, emit):
    n_blk, n_terms, _, _ = inter.shape
    n_blk -= 1
    terms = n_terms // len(right)
    turned = [by_block(right[j // terms], terms, j % terms) for j in range(n_terms)]
    for t in range(n_blk):
        total = None
        for j in range(n_terms):
            part = jnp.dot(
                inter[src[t * n_terms + j], j], turned[j], preferred_element_type=jnp.float32
            )
            total = part if total is None else total + part
        total = jnp.where(row_mask(widths[t], total.shape), total, 0.0)
        out[t] = total.astype(jnp.bfloat16)
        emit(t, total)


def keep(left, left_out, sems):
    copies = []
    for d, line in enumerate(left):
        for e, ref in enumerate(line):
            copies.append(pltpu.make_async_copy(ref, left_out.at[d, e], sems.at[d * len(line) + e]))
            copies[-1].start()
    return copies


def masked(psi, width, out):
    at = 0
    for ref in psi:
        block = ref[...].astype(jnp.float32)
        block = jnp.where(row_mask(width, block.shape), block, 0.0)
        out[:, at : at + block.shape[1]] = block.astype(jnp.bfloat16)
        at += block.shape[1]


def take(refs, counts):
    out = []
    for count in counts:
        out.append(refs[:count])
        refs = refs[count:]
    return out, refs


def products_of(psi, left, widths, first, raw_out, inter):
    for d, line in enumerate(left):
        masked(psi[d], widths[first + d], raw_out.at[d])
        terms = line[0].shape[0]
        left_products(raw_out[d], lambda at: line[at // terms][...], inter.at[d])


def early_body(n_pair, counts, widths, *refs):
    left, refs = take(refs, [n_pair] * len(counts))
    psi, (raw_out, inter_out, left_out, sems) = take(refs, counts)
    copies = keep(left, left_out, sems)
    inter_out[inter_out.shape[0] - 1] = jnp.zeros_like(inter_out[0])
    products_of(psi, left, widths, 0, raw_out, inter_out)
    for copy in copies:
        copy.wait()


def first_body(n_blk, n_pair, counts, src, widths, *refs):
    n_late = len(counts)
    n_early = n_blk - n_late
    left, refs = take(refs, [n_pair] * n_late)
    (right,), refs = take(refs, [n_pair])
    psi, refs = take(refs, counts)
    diag, right_diag, _, _, raw_out, inter, part_out, left_out, dots_out = refs[:9]
    sends, sems = refs[9:-1], refs[-1]
    copies = keep(left, left_out, sems)
    products_of(
        psi, left, widths, n_early, raw_out.at[n_early:], inter.at[n_early:n_blk]
    )
    cols = diag.shape[2]
    zero = jnp.zeros((8, cols), jnp.float32)
    sums = [zero, zero]

    def emit(d, total):
        for h in range(2):
            part = slice(h * cols, (h + 1) * cols)
            raw = raw_out[d, :, part].astype(jnp.float32)
            image = total[:, part]
            if h == 0:
                image = image + diagonal(diag, right_diag, d, h) * raw
                sums[0] = sums[0] + fold(raw * raw)
            sums[1] = sums[1] + fold(raw * image)
        for e, send in enumerate(sends, 1):
            send_rows(2 * e, send, d, raw_out, part_out, part_out)

    sum_terms(src, widths, inter, right, part_out, emit)
    spread([whole(x) for x in sums], dots_out)
    for copy in copies:
        copy.wait()


def send_rows(e, send, d, *refs):
    _, own_op = place_of()
    step = send.shape[2]
    for j, ref in enumerate(refs):
        other = e ^ 1 if j == 2 else e
        rows = pl.ds(pl.multiple_of((own_op ^ other) * step, step), step)
        send[j, d] = ref[d, rows].astype(send.dtype)


def total_of(mine, other, d, h, cols):
    own = mine[d, :, h * cols : (h + 1) * cols].astype(jnp.float32)
    return own + other[d, :, (1 - h) * cols : (2 - h) * cols].astype(jnp.float32)


def norm_theta(parts, count):
    tot = jnp.sum(parts, axis=0) * (1.0 / count)
    scale = lax.rsqrt(tot[:, 0:1] + EPS)
    return scale, tot[:, 1:2] * scale * scale


def second_body(n_blk, n_pair, count, src, widths, left_early, left_late, *refs):
    right, refs = refs[:n_pair], refs[n_pair:]
    parts, raw_in, part_in, other_in, diag, right_diag, dots_out, own_out = refs[:8]
    sends, (inter, corr, sig, fld, part_out, held, sems) = refs[8:-7], refs[-7:]
    copies = []
    n_early = left_early.shape[0]
    for d in range(n_blk):
        kept = left_early.at[d] if d < n_early else left_late.at[d - n_early]
        copies.append(pltpu.make_async_copy(kept, held.at[d], sems.at[d]))
        copies[-1].start()
    inter[n_blk] = jnp.zeros_like(inter[n_blk])
    scale, theta = norm_theta(parts[...], count)
    cols = diag.shape[2]
    halves = []
    for h in range(2):
        part = slice(h * cols, (h + 1) * cols)
        vv = vc = vs = jnp.zeros((8, cols), jnp.float32)
        for d in range(n_blk):
            vec = raw_in[d, :, part].astype(jnp.float32) * scale
            sigma = total_of(part_in, other_in, d, h, cols)
            sigma = (sigma + diagonal(diag, right_diag, d, h) * raw_in[d, :, part].astype(jnp.float32)) * scale
            sig[d, :, part] = sigma
            den = diagonal(diag, right_diag, d, h) - theta
            item = (sigma - theta * vec) * den / jnp.maximum(den * den, 0.25)
            corr[d, :, part] = item
            vv, vc, vs = vv + fold(vec * vec), vc + fold(vec * item), vs + fold(vec * sigma)
        halves.append((whole(vv), whole(vc), whole(vs)))
    along = (halves[0][1] + halves[1][1]) / jnp.maximum(halves[0][0] + halves[1][0], 1e-30)
    terms = held.shape[2]
    for copy in copies:
        copy.wait()
    for d in range(n_blk):
        for h in range(2):
            part = slice(h * cols, (h + 1) * cols)
            vec = raw_in[d, :, part].astype(jnp.float32) * scale
            fld[d, :, part] = (corr[d, :, part] - along * vec).astype(jnp.bfloat16)
        left_products(fld[d], lambda at: held[d, at // terms], inter.at[d])
    zero = jnp.zeros((8, cols), jnp.float32)
    sums = [zero for _ in range(5)]

    def emit(d, total):
        for h in range(2):
            part = slice(h * cols, (h + 1) * cols)
            field = fld[d, :, part].astype(jnp.float32)
            raw = raw_in[d, :, part].astype(jnp.float32)
            image = total[:, part]
            if h == 0:
                image = image + diagonal(diag, right_diag, d, h) * field
                for j, prod in enumerate((field * field, raw * field, field * sig[d, :, part])):
                    sums[j] = sums[j] + fold(prod)
            sums[3] = sums[3] + fold(raw * image)
            sums[4] = sums[4] + fold(field * image)
        for e, send in enumerate(sends, 1):
            send_rows(e, send, d, *((part_out,) if e % 2 else (fld, part_out)))
        rows = pl.ds(pl.multiple_of(own_op * step, step), step)
        for j, ref in enumerate((raw_in, sig, fld, part_out)):
            own_out[j, d] = ref[d, rows].astype(own_out.dtype)

    _, own_op = place_of()
    step = own_out.shape[2]
    sum_terms(src, widths, inter, right, part_out, emit)
    ff, vf, fs, vt, ft = (whole(x) for x in sums)
    spread(list(halves[0]) + [ff, vf * scale, fs, vt * scale, ft], dots_out)


def ritz_pair(theta, h_mix, h_two):
    diff, twice = theta - h_two, 2.0 * h_mix
    size = jnp.sqrt(diff * diff + twice * twice)
    some = size > 0.0
    safe = jnp.where(some, size, 1.0)
    big = jnp.sqrt(0.5 + 0.5 * jnp.abs(diff) / safe)
    small = 0.5 * jnp.abs(twice) / (safe * big)
    sine = jnp.where(diff >= 0.0, small, big)
    cosine = jnp.where(diff >= 0.0, big, small)
    sine = jnp.where(some, sine, 0.0)
    cosine = jnp.where(some, cosine, 1.0)
    upward = (twice > 0.0) | ((twice == 0.0) & (diff < 0.0))
    return sine, jnp.where(upward, -cosine, cosine), 0.5 * (theta + h_two) - 0.5 * size


def third_body(n_blk, n_op, count, slots, parts1, parts2, diag, right_diag, own, *refs):
    n_far = n_op - 2
    got1, got2 = refs[:n_far], refs[n_far : n_far + n_op - 1]
    new_out, res_out, energy_out = refs[n_far + n_op - 1 :]
    step, cols = new_out.shape[1], new_out.shape[2] // n_op
    own_blk, own_op = place_of()
    scale, theta = norm_theta(parts1[...], count)
    pairs = parts2[...].reshape(n_blk * n_op // 2, 2, *parts2.shape[1:])
    pairs = pairs[:, 0] + pairs[:, 1]
    vv, vc, vs, ff, vf, fs, vt, ft = (pairs[:, 0, j : j + 1] for j in range(8))

    def mean(x):
        return jnp.sum(x, axis=0, keepdims=True) * (1.0 / count)

    def nearest(vv, vc):
        return vc / jnp.maximum(vv, 1e-30)

    along = mean(vc)
    beta = nearest(vv, vc) - along
    norm_sq = mean(ff + 2.0 * beta * vf + beta * beta * vv)
    unit = lax.rsqrt(jnp.maximum(norm_sq, 0.0) + EPS)
    v_s1 = unit * mean(vt + beta * vs)
    u_s0 = unit * mean(fs + beta * vs)
    u_s1 = unit * unit * mean(ft + beta * (vt + fs) + beta * beta * vs)
    cv, cu, energy = ritz_pair(theta, 0.5 * (v_s1 + u_s0), u_s1)
    energy_out[0] = jnp.max(energy)
    cu = cu * unit
    mine = pl.ds(pl.multiple_of(own_op * step, step), step)
    for e in range(0, n_op, 2):
        there = own_blk * n_op + (own_op ^ e)
        pair = parts2[there] + parts2[own_blk * n_op + (own_op ^ e ^ 1)]
        on_vec = cv + cu * (nearest(pair[:, 0:1], pair[:, 1:2]) - along)
        for h in range(2):
            at = pl.multiple_of((own_op ^ e ^ h) * cols, LANES)
            part, crossed = slice(h * cols, (h + 1) * cols), slice((1 - h) * cols, (2 - h) * cols)
            for d in range(n_blk):
                dmat = diag[d, mine] + right_diag[:, pl.ds(at, cols)]
                if e:
                    raw, fld = got1[e - 2][0, d, :, part], got2[e - 1][0, d, :, part]
                    vec = raw.astype(jnp.float32) * scale
                    sigma = got1[e - 2][1, d, :, part].astype(jnp.float32)
                    sigma = sigma + got1[e - 1][0, d, :, crossed].astype(jnp.float32)
                    sigma = sigma * scale + dmat * vec
                    image = got2[e - 1][1, d, :, part].astype(jnp.float32)
                else:
                    raw, sigma, fld, image = (own[j, d, :, part].astype(jnp.float32) for j in range(4))
                    vec = raw * scale
                fld = fld.astype(jnp.float32)
                image = image + got2[e][0, d, :, crossed].astype(jnp.float32) + dmat * fld
                newvec = on_vec * vec + cu * fld
                res = on_vec * sigma + cu * image - energy * newvec
                new_out[slots[d], :, pl.ds(at, cols)] = newvec.astype(jnp.bfloat16)
                res_out[slots[d], :, pl.ds(at, cols)] = res.astype(jnp.bfloat16)


def per_device(
    psi, left_ops, right_ops, term_shift, slot_sector, sector_width, diag_left, diag_right
):
    n_blk, n_op = lax.axis_size("blk"), lax.axis_size("op")
    _, rows, ncols = psi.shape
    terms, _, width, _ = right_ops.shape
    n_pair = n_op // 2
    cols = diag_right.shape[0] // n_op
    step = rows // n_op
    count = float(n_blk * rows * ncols)
    n_dev = n_blk * n_op
    bf16, f32, i32 = jnp.bfloat16, jnp.float32, jnp.int32
    last = sorted(range(1, n_blk), key=lambda d: min(d, n_blk - d))[-1]

    def pack():
        first = swap(term_shift, 1, n_op)
        sent = kernel(
            functools.partial(pack_body, n_blk, n_op),
            [(term_shift, SMEM), (first, SMEM), (psi, HBM), (right_ops, HBM)],
            [((rows, 2 * cols if d in (0, last) else cols), bf16, VMEM) for d in range(n_blk)]
            + [((terms * width + 16, 2 * cols), bf16, VMEM)] * n_pair,
            [pltpu.VMEM(right_ops.shape, bf16), pltpu.SemaphoreType.DMA((2 * n_blk + 1,))],
            nbytes=1 << 20,
        )
        return sent[:n_blk], sent[n_blk:]

    def table(right):
        return kernel(
            functools.partial(table_body, n_blk, terms),
            [(slot_sector, SMEM), (sector_width, SMEM), (diag_left, VMEM), (diag_right[None], VMEM)]
            + [(block, VMEM) for block in right],
            [((n_blk * n_pair * terms,), i32, SMEM)]
            + [((n_blk,), i32, SMEM)] * 2
            + [((n_blk, rows, LANES), f32, VMEM), ((1, n_op * cols), f32, VMEM)],
        )

    narrow = ((n_blk, rows, 2 * cols), bf16, VMEM)

    def inputs(left, psi, those):
        blocks = [left[d, 2 * e] for d in those for e in range(n_pair)]
        halves = [half for d in those for half in psi[d]]
        return [(x, VMEM) for x in blocks], [(x, VMEM) for x in halves], [len(psi[d]) for d in those]

    def early(left, psi, n_early, tables):
        left_ins, psi_ins, counts = inputs(left, psi, range(n_early))
        return kernel(
            functools.partial(early_body, n_pair, counts),
            [(tables[1], SMEM)] + left_ins + psi_ins,
            [
                narrow,
                ((n_blk + 1, n_pair * terms, rows, 2 * cols), bf16, VMEM),
                ((n_early, n_pair, terms, rows, rows), bf16, HBM),
            ],
            [pltpu.SemaphoreType.DMA((n_early * n_pair,))],
            flops=2 * n_early * rows * rows * 2 * cols * terms * n_pair,
            nbytes=4 << 20,
        )

    left, psi_by, right, (src, widths, slots, *both), (raw_early, inter_early, left_early) = gather(
        left_ops[:, 0], n_blk, n_op, pack, table, early
    )
    n_early = left_early.shape[0]
    n_late = n_blk - n_early
    left_ins, psi_ins, counts = inputs(left, psi_by, range(n_early, n_blk))
    right_ins = [(block, VMEM) for block in right]
    diags = [(x, VMEM) for x in both]

    tables = [(src, SMEM), (widths, SMEM)]
    dots = ((n_dev, 1, LANES), f32, VMEM)
    sends1 = [((3, n_blk, step, 2 * cols), bf16, VMEM)] * (n_pair - 1)
    sends2 = [((2 - e % 2, n_blk, step, 2 * cols), bf16, VMEM) for e in range(1, n_op)]
    inter = pltpu.VMEM((n_blk + 1, n_pair * terms, rows, 2 * cols), bf16)
    left_late = (n_late, n_pair, terms, rows, rows)
    cost = dict(flops=2 * n_blk * rows * 2 * cols * terms * n_pair * (rows + 2 * cols), nbytes=6 << 20)

    def totals(parts):
        return lax.all_to_all(parts, ("blk", "op"), 0, 0, tiled=True)

    first_ins = tables + left_ins + right_ins + psi_ins + diags
    raw, _, part1, kept, dots1, *out1 = kernel(
        functools.partial(first_body, n_blk, n_pair, counts),
        first_ins + [(raw_early, VMEM), (inter_early, VMEM)],
        [narrow, (inter_early.shape, bf16, VMEM), narrow, (left_late, bf16, HBM), dots] + sends1,
        [pltpu.SemaphoreType.DMA((n_late * n_pair,))],
        in_place={len(first_ins): 0, len(first_ins) + 1: 1},
        **cost,
    )
    parts1, other1, far = lax.optimization_barrier(
        (
            totals(dots1),
            swap(part1, 1, n_op),
            [swap(block, 2 * e, n_op) for e, block in enumerate(out1, 1)],
        )
    )
    got1 = [x for block in far for x in (block, swap(block[2:], 1, n_op))]
    dots2, own, *out2 = kernel(
        functools.partial(second_body, n_blk, n_pair, count),
        tables + [(left_early, HBM), (kept, HBM)] + right_ins
        + [(x, VMEM) for x in (parts1, raw, part1, other1)] + diags,
        [dots, ((4, n_blk, step, 2 * cols), bf16, VMEM)] + sends2,
        [
            inter,
            pltpu.VMEM((n_blk, rows, 2 * cols), f32),
            pltpu.VMEM((n_blk, rows, 2 * cols), f32),
            pltpu.VMEM((n_blk, rows, 2 * cols), bf16),
            pltpu.VMEM((n_blk, rows, 2 * cols), bf16),
            pltpu.VMEM((n_blk, *left_late[1:]), bf16),
            pltpu.SemaphoreType.DMA((n_blk,)),
        ],
        **cost,
    )
    parts2 = totals(dots2)
    got2 = [swap(block, e, n_op) for e, block in enumerate(out2, 1)]
    final = ((n_blk, step, n_op * cols), bf16, VMEM)
    new, res, energy = kernel(
        functools.partial(third_body, n_blk, n_op, count),
        [(slots, SMEM)] + [(x, VMEM) for x in (parts1, parts2)] + diags
        + [(x, VMEM) for x in (own, *got1, *got2)],
        [final, final, ((1,), f32, SMEM)],
        nbytes=4 << 20,
    )
    return new, res, energy


def solution(mesh):
    placed = (
        P(("grp", "blk"), None, None),
        P("op", ("grp", "blk"), None, None),
        P("op", ("grp", "blk"), None, None),
        P("op"),
        P("grp"),
        P("grp"),
        P("grp", None),
        P(("grp", "blk")),
    )

    def body(*args):
        psi, left_ops, right_ops, diag_right = args[0], args[1], args[2], args[7]
        n_op = mesh.shape["op"]
        cols = diag_right.shape[0] // n_op
        fits = (
            psi.shape[0] == 1
            and diag_right.shape[0] % n_op == 0
            and cols == LANES
            and n_op % 2 == 0
            and cols % right_ops.shape[2] == 0
            and cols // right_ops.shape[2] * n_op == right_ops.shape[1]
            and psi.shape[1] % (16 * n_op) == 0
            and n_op & (n_op - 1) == 0
            and mesh.shape["blk"] > n_op.bit_length() - 1
        )
        return (per_device if fits else per_device_general)(*args)

    return jax.shard_map(
        body,
        mesh=mesh,
        in_specs=placed,
        out_specs=(P("grp", "op", "blk"), P("grp", "op", "blk"), P("grp")),
        check_vma=False,
    )
```

```python
import functools

import jax
import jax.numpy as jnp
from jax import lax
from jax.experimental import pallas as pl
from jax.experimental.pallas import tpu as pltpu
from jax.sharding import PartitionSpec as P

EPS = 1e-06
LANES = 128
VMEM_LIMIT = 20 * 1024 * 1024


def per_device_general(
    psi, left_ops, right_ops, term_shift, slot_sector, sector_width, diag_left, diag_right
):
    sec_dev, rows, ncols = psi.shape
    nsec = slot_sector.shape[0]
    terms_dev = left_ops.shape[0]
    right_local = right_ops.shape[1]
    right_width = right_ops.shape[2]
    local_cols = diag_right.shape[0]
    count = float(nsec * rows * ncols)
    match = slot_sector[:, None] == jnp.arange(nsec)[None, :]
    widths = jnp.sum(jnp.where(match, sector_width[None, :], 0), axis=1)
    mask_all = (jnp.arange(rows)[None, :] < widths[:, None]).astype(jnp.float32)
    own_mask = lax.dynamic_slice_in_dim(mask_all, lax.axis_index("blk") * sec_dev, sec_dev, 0)
    raw = psi.astype(jnp.float32) * own_mask[:, :, None]
    squares = lax.psum(jnp.sum(raw * raw), "blk")
    v_left = (raw * lax.rsqrt(squares / count + EPS)).astype(jnp.bfloat16)
    onehots = (
        slot_sector[None, None, :] == slot_sector[None, :, None] - term_shift[:, None, None]
    ).astype(jnp.bfloat16)
    op_rows = rows // lax.axis_size("op")
    op_start = lax.axis_index("op") * op_rows
    dmat = diag_left[:, :, None] + diag_right[None, None, :]

    def left_local(field):
        return jnp.einsum(
            "ksij,sjc->ksic", left_ops, field, preferred_element_type=jnp.float32
        ).astype(jnp.bfloat16)

    def right_part(moved_in):
        flat = moved_in.reshape(terms_dev, nsec, rows * local_cols)
        shifted = jnp.einsum(
            "kts,ksx->ktx", onehots, flat, preferred_element_type=jnp.float32
        ).astype(jnp.bfloat16)
        shifted = shifted.reshape(terms_dev, nsec, rows, right_local, right_width)
        accum = jnp.einsum(
            "ktwrc,krdc->twrd", shifted, right_ops, preferred_element_type=jnp.float32
        )
        return accum.reshape(nsec, rows, local_cols) * mask_all[:, :, None]

    def op_total(partial_value):
        return lax.psum(partial_value.astype(jnp.bfloat16), "op").astype(jnp.float32)

    def final_rows(array):
        return lax.dynamic_slice_in_dim(array, op_start, op_rows, 1)

    def reduce_dots(values):
        sums = lax.psum(values, "blk")
        return tuple((item / count for item in sums))

    moved_first, v_moved = (
        lax.all_to_all(left_local(v_left), "blk", split_axis=3, concat_axis=1, tiled=True),
        lax.all_to_all(v_left[None], "blk", split_axis=3, concat_axis=1, tiled=True),
    )
    v_right = v_moved[0]
    vec32 = v_right.astype(jnp.float32)
    first_sigma = op_total(right_part(moved_first)) + dmat * vec32
    theta = reduce_dots((jnp.sum(vec32 * first_sigma),))[0]
    resid = first_sigma - theta * vec32
    den = dmat - theta
    corr = resid * den / jnp.maximum(den * den, 0.25)
    along = reduce_dots((jnp.sum(vec32 * corr),))[0]
    orth = corr - along * vec32
    norm_sq = reduce_dots((jnp.sum(orth * orth),))[0]
    update = (orth * lax.rsqrt(norm_sq + EPS)).astype(jnp.bfloat16)
    upd32 = update.astype(jnp.float32)
    upd_left = lax.all_to_all(update, "blk", split_axis=0, concat_axis=2, tiled=True)
    moved_second = lax.all_to_all(
        left_local(upd_left), "blk", split_axis=3, concat_axis=1, tiled=True
    )
    second_sigma = op_total(right_part(moved_second)) + dmat * upd32
    v_s1, u_s0, u_s1 = reduce_dots(
        (jnp.sum(vec32 * second_sigma), jnp.sum(upd32 * first_sigma), jnp.sum(upd32 * second_sigma))
    )
    h_mix = 0.5 * (v_s1 + u_s0)
    coef_v, coef_u, energy = ritz(theta, h_mix, u_s1)
    newvec = coef_v * vec32 + coef_u * upd32
    image = coef_v * first_sigma + coef_u * second_sigma
    new_out = final_rows(newvec.astype(jnp.bfloat16))
    res_out = final_rows((image - energy * newvec).astype(jnp.bfloat16))
    return (new_out, res_out, jnp.reshape(energy, (1,)))


def ritz(theta, h_mix, h_two):
    angle = 0.5 * jnp.arctan2(2.0 * h_mix, theta - h_two)
    sine = jnp.sin(angle)
    flip = jnp.where(sine > 0, -1.0, 1.0)
    coef_v = -sine * flip
    coef_u = jnp.cos(angle) * flip
    half = 0.5 * (theta - h_two)
    energy = 0.5 * (theta + h_two) - jnp.sqrt(half * half + h_mix * h_mix)
    return coef_v, coef_u, energy


VMEM, SMEM, HBM = pltpu.VMEM, pltpu.SMEM, pltpu.HBM


def kernel(body, ins, outs, scratch=(), flops=0, nbytes=0):
    return pl.pallas_call(
        body,
        out_shape=[
            HBM(shape, dtype) if space == HBM else jax.ShapeDtypeStruct(shape, dtype)
            for shape, dtype, space in outs
        ],
        in_specs=[pl.BlockSpec(memory_space=space) for _, space in ins],
        out_specs=[pl.BlockSpec(memory_space=space) for _, _, space in outs],
        scratch_shapes=list(scratch),
        compiler_params=pltpu.CompilerParams(vmem_limit_bytes=VMEM_LIMIT),
        cost_estimate=pl.CostEstimate(flops=flops, bytes_accessed=nbytes, transcendentals=0),
    )(*[pltpu.with_memory_space_constraint(x, HBM) if space == HBM else x for x, space in ins])


def ring_at(place, n_blk):
    place = place % n_blk if isinstance(place, int) else lax.rem(place + n_blk, n_blk)
    odd, even = 2 * place - 1, 2 * (n_blk - place)
    if isinstance(place, int):
        return 0 if place == 0 else odd if odd < n_blk else even
    return jnp.where(place == 0, 0, jnp.where(odd < n_blk, odd, even))


def ring_place(index, n_blk):
    odd, even = (index + 1) // 2, lax.rem(n_blk - index // 2, n_blk)
    return jnp.where(lax.rem(index, 2) == 1, odd, even)


def onward(block, d, n_blk):
    pairs = [(ring_at(i, n_blk), ring_at(i + d, n_blk)) for i in range(n_blk)]
    return lax.ppermute(block, "blk", pairs)


def swap(block, e, n_op):
    return lax.ppermute(block, "op", [(i, i ^ e) for i in range(n_op)])


def gather(own, n_blk, n_op, pack, table, early):
    bits = [1 << b for b in reversed(range(1, n_op.bit_length() - 1))]
    order = sorted(range(1, n_blk), key=lambda d: min(d, n_blk - d))
    left, psi, right, tables, columns = {(0, 0): own}, {}, None, None, None
    waiting, late, made = {(0, 0): 0}, None, None
    for j in range(n_blk + len(bits)):
        new, moved = {}, {}
        for (d, e), done in waiting.items():
            if e == 0 and d + 1 < n_blk:
                new[d + 1, 0] = onward(left[d, 0], 1, n_blk), 0
            for b in range(done, len(bits)):
                new[d, e ^ bits[b]] = swap(left[d, e], bits[b], n_op), b + 1
        kept = {key: block for key, (block, _) in new.items()}
        if late is not None:
            moved["psi"] = late
        if j == 0:
            columns, packed = pack()
            moved["right"] = [packed[0]]
            moved["right"] += [swap(part, 2 * e, n_op) for e, part in enumerate(packed[1:], 1)]
        if j == 1:
            moved["tables"] = table(right)
        if j == n_blk - 1 and j >= len(bits) + 1:
            n_early = min(2, n_blk - 1)
            psi[0] = [columns[0]]
            moved["early"] = early(left, psi, n_early, tables)
        if 2 <= j < n_blk:
            moved["other"] = swap(psi[order[j - 2]][0], 1, n_op)
        late = onward(columns[order[j]], order[j], n_blk) if j < n_blk - 1 else None
        if not kept and not moved:
            break
        waiting = {key: done for key, (_, done) in new.items()}
        kept, moved = lax.optimization_barrier((kept, moved))
        left.update(kept)
        right, tables = moved.get("right", right), moved.get("tables", tables)
        made = moved.get("early", made)
        if "psi" in moved:
            psi[order[j - 1]] = [moved["psi"]]
        if "other" in moved:
            psi[order[j - 2]].append(moved["other"])
    return left, psi, right, tables, made


def place_of():
    return lax.axis_index("blk"), lax.axis_index("op")


def pack_body(n_blk, n_op, shift, _, psi, right_in, *outs):
    n_pair = n_op // 2
    psi_out, right_out, right, sems = outs[:n_blk], outs[n_blk : n_blk + n_pair], outs[-2], outs[-1]
    terms, local, width, _ = right.shape
    cols = local * width // n_op
    per = cols // width
    own_blk, own_op = place_of()
    fetch = pltpu.make_async_copy(right_in, right, sems.at[2 * n_blk])
    fetch.start()
    copies = []
    for d in range(n_blk):
        there = ring_at(ring_place(own_blk, n_blk) + d, n_blk) * n_op
        for h in range(psi_out[d].shape[1] // cols):
            start = pl.multiple_of((there + (own_op ^ h)) * cols, LANES)
            copy = pltpu.make_async_copy(
                psi.at[0, :, pl.ds(start, cols)],
                psi_out[d].at[:, h * cols : (h + 1) * cols],
                sems.at[2 * d + h],
            )
            copy.start()
            copies.append(copy)
    lane = lax.broadcasted_iota(jnp.int32, (16, 2 * cols), 1)
    line = jnp.zeros((16, 2 * cols), jnp.float32)
    for k in range(terms):
        line = jnp.where(lane == k, shift[k].astype(jnp.float32), line)
    square = [lax.broadcasted_iota(jnp.int32, (width, width), axis) for axis in (0, 1)]
    unit = (square[0] == square[1]).astype(jnp.bfloat16)
    fetch.wait()
    for e in range(n_pair):
        for k in range(terms):
            turned = []
            for h in range(2):
                first = (own_op ^ (2 * e) ^ h) * per
                for r in range(per):
                    turned.append(
                        lax.dot_general(
                            right[k, first + r], unit, (((0,), (0,)), ((), ())),
                            preferred_element_type=jnp.float32,
                        )
                    )
            side_by_side = jnp.concatenate(turned, axis=1).astype(jnp.bfloat16)
            right_out[e][k * width : (k + 1) * width] = side_by_side
        right_out[e][terms * width :] = line.astype(jnp.bfloat16)
    for copy in copies:
        copy.wait()


def table_body(n_blk, terms, sector, width, left_diag, right_diag, *refs):
    tails, src, widths, slots, diag, right_out = refs[:-5], *refs[-5:]
    right_out[...] = right_diag[...]
    n_pair = len(tails)
    rows, cols = tails[0].shape
    own_blk, _ = place_of()
    lane = lax.broadcasted_iota(jnp.int32, (16, cols), 1)
    for d in range(n_blk):
        slot = ring_at(ring_place(own_blk, n_blk) - d, n_blk)
        slots[d] = slot
        widths[d] = width[sector[slot]]
    for e in range(n_pair):
        tail = tails[e][rows - 16 :].astype(jnp.float32)
        for k in range(terms):
            shift = jnp.max(jnp.where(lane == k, tail, -1e9)).astype(jnp.int32)
            for t in range(n_blk):
                want = sector[slots[t]] - shift
                found = jnp.int32(n_blk)
                for d in range(n_blk):
                    found = jnp.where(sector[slots[d]] == want, d, found)
                src[(t * n_pair + e) * terms + k] = found
    for d in range(n_blk):
        row = left_diag[pl.ds(slots[d], 1), :]
        diag[d] = jnp.transpose(jnp.broadcast_to(row, (diag.shape[2], row.shape[1])))


def diagonal(diag, right_diag, d, h):
    cols = diag.shape[2]
    _, own_op = place_of()
    start = pl.multiple_of((own_op ^ h) * cols, LANES)
    return diag[d] + right_diag[:, pl.ds(start, cols)]


def row_mask(width, shape):
    return lax.broadcasted_iota(jnp.int32, shape, 0) < width


def fold(x):
    return jnp.sum(x.reshape(-1, 8, x.shape[-1]), axis=0)


def whole(x):
    return jnp.sum(jnp.sum(x, axis=0, keepdims=True), axis=1, keepdims=True)


def spread(values, out):
    lane = lax.broadcasted_iota(jnp.int32, out.shape[1:], 1)
    row = jnp.zeros(out.shape[1:], jnp.float32)
    for j, value in enumerate(values):
        row = jnp.where(lane == j, value, row)
    for d in range(out.shape[0]):
        out[d] = row


def by_block(packed, terms, k):
    rows, cols = packed.shape
    width = (rows - 16) // terms
    lane = lax.broadcasted_iota(jnp.int32, (width, cols), 1)
    block = packed[k * width : (k + 1) * width].astype(jnp.float32)
    parts = []
    for r in range(cols // width):
        inside = (lane >= r * width) & (lane < (r + 1) * width)
        parts.append(jnp.where(inside, block, 0.0).astype(jnp.bfloat16))
    return jnp.concatenate(parts, axis=0)


def left_products(block, left, inter):
    n_terms, rows, cols = inter.shape
    at = 0
    while at < n_terms:
        ops = left(at)
        terms = ops.shape[0]
        prod = jnp.dot(ops.reshape(terms * rows, rows), block, preferred_element_type=jnp.float32)
        inter[at : at + terms] = prod.astype(jnp.bfloat16).reshape(terms, rows, cols)
        at += terms


def sum_terms(src, widths, inter, right, out, emit):
    n_blk, n_terms, _, _ = inter.shape
    n_blk -= 1
    terms = n_terms // len(right)
    turned = [by_block(right[j // terms], terms, j % terms) for j in range(n_terms)]
    for t in range(n_blk):
        total = None
        for j in range(n_terms):
            part = jnp.dot(
                inter[src[t * n_terms + j], j], turned[j], preferred_element_type=jnp.float32
            )
            total = part if total is None else total + part
        total = jnp.where(row_mask(widths[t], total.shape), total, 0.0)
        out[t] = total.astype(jnp.bfloat16)
        emit(t, total)


def keep(left, left_out, sems):
    copies = []
    for d, line in enumerate(left):
        for e, ref in enumerate(line):
            copies.append(pltpu.make_async_copy(ref, left_out.at[d, e], sems.at[d * len(line) + e]))
            copies[-1].start()
    return copies


def masked(psi, width, out):
    at = 0
    for ref in psi:
        block = ref[...].astype(jnp.float32)
        block = jnp.where(row_mask(width, block.shape), block, 0.0)
        out[:, at : at + block.shape[1]] = block.astype(jnp.bfloat16)
        at += block.shape[1]


def take(refs, counts):
    out = []
    for count in counts:
        out.append(refs[:count])
        refs = refs[count:]
    return out, refs


def products_of(psi, left, widths, first, raw_out, inter):
    for d, line in enumerate(left):
        masked(psi[d], widths[first + d], raw_out.at[d])
        terms = line[0].shape[0]
        left_products(raw_out[d], lambda at: line[at // terms][...], inter.at[d])


def early_body(n_pair, counts, widths, *refs):
    left, refs = take(refs, [n_pair] * len(counts))
    psi, (raw_out, inter_out, left_out, sems) = take(refs, counts)
    copies = keep(left, left_out, sems)
    products_of(psi, left, widths, 0, raw_out, inter_out)
    for copy in copies:
        copy.wait()


def first_body(n_blk, n_pair, counts, src, widths, *refs):
    n_late = len(counts)
    n_early = n_blk - n_late
    left, refs = take(refs, [n_pair] * n_late)
    (right,), refs = take(refs, [n_pair])
    psi, refs = take(refs, counts)
    raw_in, inter_in, diag, right_diag, part_out, raw_out, left_out, dots_out = refs[:8]
    sends, (inter, sems) = refs[8:-2], refs[-2:]
    copies = keep(left, left_out, sems)
    for j, (given, own) in enumerate(((inter_in, inter), (raw_in, raw_out))):
        copies.append(
            pltpu.make_async_copy(given, own.at[:n_early], sems.at[n_late * n_pair + j])
        )
        copies[-1].start()
    inter[n_blk] = jnp.zeros_like(inter[n_blk])
    products_of(
        psi, left, widths, n_early, raw_out.at[n_early:], inter.at[n_early:n_blk]
    )
    for copy in copies:
        copy.wait()
    cols = diag.shape[2]
    zero = jnp.zeros((8, cols), jnp.float32)
    sums = [zero, zero]

    def emit(d, total):
        for h in range(2):
            part = slice(h * cols, (h + 1) * cols)
            raw = raw_out[d, :, part].astype(jnp.float32)
            image = total[:, part]
            if h == 0:
                image = image + diagonal(diag, right_diag, d, h) * raw
                sums[0] = sums[0] + fold(raw * raw)
            sums[1] = sums[1] + fold(raw * image)
        for e, send in enumerate(sends, 2):
            send_rows(e, send, d, raw_out, part_out)

    sum_terms(src, widths, inter, right, part_out, emit)
    spread([whole(x) for x in sums], dots_out)


def send_rows(e, send, d, field, part):
    _, own_op = place_of()
    step = send.shape[2]
    rows = pl.ds(pl.multiple_of((own_op ^ e) * step, step), step)
    if e % 2 == 0:
        send[0, d] = field[d, rows].astype(send.dtype)
    send[send.shape[0] - 1, d] = part[d, rows]


def total_of(mine, other, d, h, cols):
    own = mine[d, :, h * cols : (h + 1) * cols].astype(jnp.float32)
    return own + other[d, :, (1 - h) * cols : (2 - h) * cols].astype(jnp.float32)


def norm_theta(parts, count):
    tot = jnp.sum(parts, axis=0) * (1.0 / count)
    scale = lax.rsqrt(tot[:, 0:1] + EPS)
    return scale, tot[:, 1:2] * scale * scale


def second_body(n_blk, n_pair, count, src, widths, left_early, left_late, *refs):
    right, refs = refs[:n_pair], refs[n_pair:]
    parts, raw_in, part_in, other_in, diag, right_diag, dots_out, own_out = refs[:8]
    sends, (inter, corr, sig, fld, part_out, held, sems) = refs[8:-7], refs[-7:]
    copies = []
    n_early = left_early.shape[0]
    for d in range(n_blk):
        kept = left_early.at[d] if d < n_early else left_late.at[d - n_early]
        copies.append(pltpu.make_async_copy(kept, held.at[d], sems.at[d]))
        copies[-1].start()
    inter[n_blk] = jnp.zeros_like(inter[n_blk])
    scale, theta = norm_theta(parts[...], count)
    cols = diag.shape[2]
    halves = []
    for h in range(2):
        part = slice(h * cols, (h + 1) * cols)
        vv = vc = vs = jnp.zeros((8, cols), jnp.float32)
        for d in range(n_blk):
            vec = raw_in[d, :, part].astype(jnp.float32) * scale
            sigma = total_of(part_in, other_in, d, h, cols)
            sigma = (sigma + diagonal(diag, right_diag, d, h) * raw_in[d, :, part].astype(jnp.float32)) * scale
            sig[d, :, part] = sigma
            den = diagonal(diag, right_diag, d, h) - theta
            item = (sigma - theta * vec) * den / jnp.maximum(den * den, 0.25)
            corr[d, :, part] = item
            vv, vc, vs = vv + fold(vec * vec), vc + fold(vec * item), vs + fold(vec * sigma)
        halves.append((whole(vv), whole(vc), whole(vs)))
    along = (halves[0][1] + halves[1][1]) / jnp.maximum(halves[0][0] + halves[1][0], 1e-30)
    terms = held.shape[2]
    for copy in copies:
        copy.wait()
    for d in range(n_blk):
        for h in range(2):
            part = slice(h * cols, (h + 1) * cols)
            vec = raw_in[d, :, part].astype(jnp.float32) * scale
            fld[d, :, part] = (corr[d, :, part] - along * vec).astype(jnp.bfloat16)
        left_products(fld[d], lambda at: held[d, at // terms], inter.at[d])
    zero = jnp.zeros((8, cols), jnp.float32)
    sums = [zero for _ in range(5)]

    def emit(d, total):
        for h in range(2):
            part = slice(h * cols, (h + 1) * cols)
            field = fld[d, :, part].astype(jnp.float32)
            vec = raw_in[d, :, part].astype(jnp.float32) * scale
            image = total[:, part]
            if h == 0:
                image = image + diagonal(diag, right_diag, d, h) * field
                for j, prod in enumerate((field * field, vec * field, field * sig[d, :, part])):
                    sums[j] = sums[j] + fold(prod)
            sums[3] = sums[3] + fold(vec * image)
            sums[4] = sums[4] + fold(field * image)
        for e, send in enumerate(sends, 1):
            send_rows(e, send, d, fld, part_out)
        rows = pl.ds(pl.multiple_of(own_op * step, step), step)
        for j, ref in enumerate((raw_in, sig, fld, part_out)):
            own_out[j, d] = ref[d, rows].astype(own_out.dtype)

    _, own_op = place_of()
    step = own_out.shape[2]
    sum_terms(src, widths, inter, right, part_out, emit)
    spread(list(halves[0]) + [whole(x) for x in sums], dots_out)


def ritz_pair(theta, h_mix, h_two):
    diff, twice = theta - h_two, 2.0 * h_mix
    size = jnp.sqrt(diff * diff + twice * twice)
    some = size > 0.0
    safe = jnp.where(some, size, 1.0)
    big = jnp.sqrt(0.5 + 0.5 * jnp.abs(diff) / safe)
    small = 0.5 * jnp.abs(twice) / (safe * big)
    sine = jnp.where(diff >= 0.0, small, big)
    cosine = jnp.where(diff >= 0.0, big, small)
    sine = jnp.where(some, sine, 0.0)
    cosine = jnp.where(some, cosine, 1.0)
    upward = (twice > 0.0) | ((twice == 0.0) & (diff < 0.0))
    return sine, jnp.where(upward, -cosine, cosine), 0.5 * (theta + h_two) - 0.5 * size


def third_body(n_blk, n_op, count, slots, parts1, parts2, diag, right_diag, own, *refs):
    got1, got2 = refs[: n_op - 2], refs[n_op - 2 : 2 * n_op - 3]
    new_out, res_out, energy_out = refs[2 * n_op - 3 :]
    step, cols = new_out.shape[1], new_out.shape[2] // n_op
    own_blk, own_op = place_of()
    scale, theta = norm_theta(parts1[...], count)
    pairs = parts2[...].reshape(n_blk * n_op // 2, 2, *parts2.shape[1:])
    pairs = pairs[:, 0] + pairs[:, 1]
    vv, vc, vs, ff, vf, fs, vt, ft = (pairs[:, 0, j : j + 1] for j in range(8))

    def mean(x):
        return jnp.sum(x, axis=0, keepdims=True) * (1.0 / count)

    def nearest(vv, vc):
        return vc / jnp.maximum(vv, 1e-30)

    along = mean(vc)
    beta = nearest(vv, vc) - along
    norm_sq = mean(ff + 2.0 * beta * vf + beta * beta * vv)
    unit = lax.rsqrt(jnp.maximum(norm_sq, 0.0) + EPS)
    v_s1 = unit * mean(vt + beta * vs)
    u_s0 = unit * mean(fs + beta * vs)
    u_s1 = unit * unit * mean(ft + beta * (vt + fs) + beta * beta * vs)
    cv, cu, energy = ritz_pair(theta, 0.5 * (v_s1 + u_s0), u_s1)
    energy_out[0] = jnp.max(energy)
    cu = cu * unit
    mine = pl.ds(pl.multiple_of(own_op * step, step), step)
    for e in range(0, n_op, 2):
        there = own_blk * n_op + (own_op ^ e)
        pair = parts2[there] + parts2[own_blk * n_op + (own_op ^ e ^ 1)]
        on_vec = cv + cu * (nearest(pair[:, 0:1], pair[:, 1:2]) - along)
        for h in range(2):
            at = pl.multiple_of((own_op ^ e ^ h) * cols, LANES)
            part, crossed = slice(h * cols, (h + 1) * cols), slice((1 - h) * cols, (2 - h) * cols)
            for d in range(n_blk):
                dmat = diag[d, mine] + right_diag[:, pl.ds(at, cols)]
                if e:
                    raw, fld = got1[e - 2][0, d, :, part], got2[e - 1][0, d, :, part]
                    vec = raw.astype(jnp.float32) * scale
                    sigma = got1[e - 2][1, d, :, part].astype(jnp.float32)
                    sigma = sigma + got1[e - 1][0, d, :, crossed].astype(jnp.float32)
                    sigma = sigma * scale + dmat * vec
                    image = got2[e - 1][1, d, :, part].astype(jnp.float32)
                else:
                    raw, sigma, fld, image = (own[j, d, :, part].astype(jnp.float32) for j in range(4))
                    vec = raw * scale
                fld = fld.astype(jnp.float32)
                image = image + got2[e][0, d, :, crossed].astype(jnp.float32) + dmat * fld
                newvec = on_vec * vec + cu * fld
                res = on_vec * sigma + cu * image - energy * newvec
                new_out[slots[d], :, pl.ds(at, cols)] = newvec.astype(jnp.bfloat16)
                res_out[slots[d], :, pl.ds(at, cols)] = res.astype(jnp.bfloat16)


def per_device(
    psi, left_ops, right_ops, term_shift, slot_sector, sector_width, diag_left, diag_right
):
    n_blk, n_op = lax.axis_size("blk"), lax.axis_size("op")
    _, rows, ncols = psi.shape
    terms, _, width, _ = right_ops.shape
    n_pair = n_op // 2
    cols = diag_right.shape[0] // n_op
    step = rows // n_op
    count = float(n_blk * rows * ncols)
    n_dev = n_blk * n_op
    bf16, f32, i32 = jnp.bfloat16, jnp.float32, jnp.int32
    last = sorted(range(1, n_blk), key=lambda d: min(d, n_blk - d))[-1]

    def pack():
        first = swap(term_shift, 1, n_op)
        sent = kernel(
            functools.partial(pack_body, n_blk, n_op),
            [(term_shift, SMEM), (first, SMEM), (psi, HBM), (right_ops, HBM)],
            [((rows, 2 * cols if d in (0, last) else cols), bf16, VMEM) for d in range(n_blk)]
            + [((terms * width + 16, 2 * cols), bf16, VMEM)] * n_pair,
            [pltpu.VMEM(right_ops.shape, bf16), pltpu.SemaphoreType.DMA((2 * n_blk + 1,))],
            nbytes=1 << 20,
        )
        return sent[:n_blk], sent[n_blk:]

    def table(right):
        return kernel(
            functools.partial(table_body, n_blk, terms),
            [(slot_sector, SMEM), (sector_width, SMEM), (diag_left, VMEM), (diag_right[None], VMEM)]
            + [(block, VMEM) for block in right],
            [((n_blk * n_pair * terms,), i32, SMEM)]
            + [((n_blk,), i32, SMEM)] * 2
            + [((n_blk, rows, LANES), f32, VMEM), ((1, n_op * cols), f32, VMEM)],
        )

    def inputs(left, psi, those):
        blocks = [left[d, 2 * e] for d in those for e in range(n_pair)]
        halves = [half for d in those for half in psi[d]]
        return [(x, VMEM) for x in blocks], [(x, VMEM) for x in halves], [len(psi[d]) for d in those]

    def early(left, psi, n_early, tables):
        left_ins, psi_ins, counts = inputs(left, psi, range(n_early))
        return kernel(
            functools.partial(early_body, n_pair, counts),
            [(tables[1], SMEM)] + left_ins + psi_ins,
            [
                ((n_early, rows, 2 * cols), bf16, VMEM),
                ((n_early, n_pair * terms, rows, 2 * cols), bf16, VMEM),
                ((n_early, n_pair, terms, rows, rows), bf16, HBM),
            ],
            [pltpu.SemaphoreType.DMA((n_early * n_pair,))],
            flops=2 * n_early * rows * rows * 2 * cols * terms * n_pair,
            nbytes=4 << 20,
        )

    left, psi_by, right, (src, widths, slots, *both), (raw_early, inter_early, left_early) = gather(
        left_ops[:, 0], n_blk, n_op, pack, table, early
    )
    n_early = raw_early.shape[0]
    n_late = n_blk - n_early
    left_ins, psi_ins, counts = inputs(left, psi_by, range(n_early, n_blk))
    right_ins = [(block, VMEM) for block in right]
    diags = [(x, VMEM) for x in both]

    tables = [(src, SMEM), (widths, SMEM)]
    narrow = ((n_blk, rows, 2 * cols), bf16, VMEM)
    dots = ((n_dev, 1, LANES), f32, VMEM)
    sends = [((2 - e % 2, n_blk, step, 2 * cols), bf16, VMEM) for e in range(1, n_op)]
    inter = pltpu.VMEM((n_blk + 1, n_pair * terms, rows, 2 * cols), bf16)
    left_late = (n_late, n_pair, terms, rows, rows)
    cost = dict(flops=2 * n_blk * rows * 2 * cols * terms * n_pair * (rows + 2 * cols), nbytes=6 << 20)

    def totals(parts):
        return lax.all_to_all(parts, ("blk", "op"), 0, 0, tiled=True)

    part1, raw, kept, dots1, *out1 = kernel(
        functools.partial(first_body, n_blk, n_pair, counts),
        tables + left_ins + right_ins + psi_ins + [(raw_early, VMEM), (inter_early, VMEM)] + diags,
        [narrow, narrow, (left_late, bf16, HBM), dots] + sends[1:],
        [inter, pltpu.SemaphoreType.DMA((n_late * n_pair + 2,))],
        **cost,
    )
    parts1, other1 = lax.optimization_barrier((totals(dots1), swap(part1, 1, n_op)))
    got1 = [swap(block, e, n_op) for e, block in enumerate(out1, 2)]
    dots2, own, *out2 = kernel(
        functools.partial(second_body, n_blk, n_pair, count),
        tables + [(left_early, HBM), (kept, HBM)] + right_ins
        + [(x, VMEM) for x in (parts1, raw, part1, other1)] + diags,
        [dots, ((4, n_blk, step, 2 * cols), bf16, VMEM)] + sends,
        [
            inter,
            pltpu.VMEM((n_blk, rows, 2 * cols), f32),
            pltpu.VMEM((n_blk, rows, 2 * cols), f32),
            pltpu.VMEM((n_blk, rows, 2 * cols), bf16),
            pltpu.VMEM((n_blk, rows, 2 * cols), bf16),
            pltpu.VMEM((n_blk, *left_late[1:]), bf16),
            pltpu.SemaphoreType.DMA((n_blk,)),
        ],
        **cost,
    )
    dots2, out2, got1 = lax.optimization_barrier((dots2, out2, got1))
    parts2 = totals(dots2)
    got2 = [swap(block, e, n_op) for e, block in enumerate(out2, 1)]
    final = ((n_blk, step, n_op * cols), bf16, VMEM)
    new, res, energy = kernel(
        functools.partial(third_body, n_blk, n_op, count),
        [(slots, SMEM)] + [(x, VMEM) for x in (parts1, parts2)] + diags
        + [(x, VMEM) for x in (own, *got1, *got2)],
        [final, final, ((1,), f32, SMEM)],
        nbytes=4 << 20,
    )
    return new, res, energy


def solution(mesh):
    placed = (
        P(("grp", "blk"), None, None),
        P("op", ("grp", "blk"), None, None),
        P("op", ("grp", "blk"), None, None),
        P("op"),
        P("grp"),
        P("grp"),
        P("grp", None),
        P(("grp", "blk")),
    )

    def body(*args):
        psi, left_ops, right_ops, diag_right = args[0], args[1], args[2], args[7]
        n_op = mesh.shape["op"]
        cols = diag_right.shape[0] // n_op
        fits = (
            psi.shape[0] == 1
            and diag_right.shape[0] % n_op == 0
            and cols == LANES
            and n_op % 2 == 0
            and cols % right_ops.shape[2] == 0
            and cols // right_ops.shape[2] * n_op == right_ops.shape[1]
            and psi.shape[1] % (16 * n_op) == 0
            and n_op & (n_op - 1) == 0
            and mesh.shape["blk"] > n_op.bit_length() - 1
        )
        return (per_device if fits else per_device_general)(*args)

    return jax.shard_map(
        body,
        mesh=mesh,
        in_specs=placed,
        out_specs=(P("grp", "op", "blk"), P("grp", "op", "blk"), P("grp")),
        check_vma=False,
    )
```

```python
import functools

import jax
import jax.numpy as jnp
from jax import lax
from jax.experimental import pallas as pl
from jax.experimental.pallas import tpu as pltpu
from jax.sharding import PartitionSpec as P

EPS = 1e-06
LANES = 128
VMEM_LIMIT = 20 * 1024 * 1024


def per_device_general(
    psi, left_ops, right_ops, term_shift, slot_sector, sector_width, diag_left, diag_right
):
    sec_dev, rows, ncols = psi.shape
    nsec = slot_sector.shape[0]
    terms_dev = left_ops.shape[0]
    right_local = right_ops.shape[1]
    right_width = right_ops.shape[2]
    local_cols = diag_right.shape[0]
    count = float(nsec * rows * ncols)
    match = slot_sector[:, None] == jnp.arange(nsec)[None, :]
    widths = jnp.sum(jnp.where(match, sector_width[None, :], 0), axis=1)
    mask_all = (jnp.arange(rows)[None, :] < widths[:, None]).astype(jnp.float32)
    own_mask = lax.dynamic_slice_in_dim(mask_all, lax.axis_index("blk") * sec_dev, sec_dev, 0)
    raw = psi.astype(jnp.float32) * own_mask[:, :, None]
    squares = lax.psum(jnp.sum(raw * raw), "blk")
    v_left = (raw * lax.rsqrt(squares / count + EPS)).astype(jnp.bfloat16)
    onehots = (
        slot_sector[None, None, :] == slot_sector[None, :, None] - term_shift[:, None, None]
    ).astype(jnp.bfloat16)
    op_rows = rows // lax.axis_size("op")
    op_start = lax.axis_index("op") * op_rows
    dmat = diag_left[:, :, None] + diag_right[None, None, :]

    def left_local(field):
        return jnp.einsum(
            "ksij,sjc->ksic", left_ops, field, preferred_element_type=jnp.float32
        ).astype(jnp.bfloat16)

    def right_part(moved_in):
        flat = moved_in.reshape(terms_dev, nsec, rows * local_cols)
        shifted = jnp.einsum(
            "kts,ksx->ktx", onehots, flat, preferred_element_type=jnp.float32
        ).astype(jnp.bfloat16)
        shifted = shifted.reshape(terms_dev, nsec, rows, right_local, right_width)
        accum = jnp.einsum(
            "ktwrc,krdc->twrd", shifted, right_ops, preferred_element_type=jnp.float32
        )
        return accum.reshape(nsec, rows, local_cols) * mask_all[:, :, None]

    def op_total(partial_value):
        return lax.psum(partial_value.astype(jnp.bfloat16), "op").astype(jnp.float32)

    def final_rows(array):
        return lax.dynamic_slice_in_dim(array, op_start, op_rows, 1)

    def reduce_dots(values):
        sums = lax.psum(values, "blk")
        return tuple((item / count for item in sums))

    moved_first, v_moved = (
        lax.all_to_all(left_local(v_left), "blk", split_axis=3, concat_axis=1, tiled=True),
        lax.all_to_all(v_left[None], "blk", split_axis=3, concat_axis=1, tiled=True),
    )
    v_right = v_moved[0]
    vec32 = v_right.astype(jnp.float32)
    first_sigma = op_total(right_part(moved_first)) + dmat * vec32
    theta = reduce_dots((jnp.sum(vec32 * first_sigma),))[0]
    resid = first_sigma - theta * vec32
    den = dmat - theta
    corr = resid * den / jnp.maximum(den * den, 0.25)
    along = reduce_dots((jnp.sum(vec32 * corr),))[0]
    orth = corr - along * vec32
    norm_sq = reduce_dots((jnp.sum(orth * orth),))[0]
    update = (orth * lax.rsqrt(norm_sq + EPS)).astype(jnp.bfloat16)
    upd32 = update.astype(jnp.float32)
    upd_left = lax.all_to_all(update, "blk", split_axis=0, concat_axis=2, tiled=True)
    moved_second = lax.all_to_all(
        left_local(upd_left), "blk", split_axis=3, concat_axis=1, tiled=True
    )
    second_sigma = op_total(right_part(moved_second)) + dmat * upd32
    v_s1, u_s0, u_s1 = reduce_dots(
        (jnp.sum(vec32 * second_sigma), jnp.sum(upd32 * first_sigma), jnp.sum(upd32 * second_sigma))
    )
    h_mix = 0.5 * (v_s1 + u_s0)
    coef_v, coef_u, energy = ritz(theta, h_mix, u_s1)
    newvec = coef_v * vec32 + coef_u * upd32
    image = coef_v * first_sigma + coef_u * second_sigma
    new_out = final_rows(newvec.astype(jnp.bfloat16))
    res_out = final_rows((image - energy * newvec).astype(jnp.bfloat16))
    return (new_out, res_out, jnp.reshape(energy, (1,)))


def ritz(theta, h_mix, h_two):
    angle = 0.5 * jnp.arctan2(2.0 * h_mix, theta - h_two)
    sine = jnp.sin(angle)
    flip = jnp.where(sine > 0, -1.0, 1.0)
    coef_v = -sine * flip
    coef_u = jnp.cos(angle) * flip
    half = 0.5 * (theta - h_two)
    energy = 0.5 * (theta + h_two) - jnp.sqrt(half * half + h_mix * h_mix)
    return coef_v, coef_u, energy


VMEM, SMEM, HBM = pltpu.VMEM, pltpu.SMEM, pltpu.HBM


def kernel(body, ins, outs, scratch=(), flops=0, nbytes=0):
    return pl.pallas_call(
        body,
        out_shape=[
            HBM(shape, dtype) if space == HBM else jax.ShapeDtypeStruct(shape, dtype)
            for shape, dtype, space in outs
        ],
        in_specs=[pl.BlockSpec(memory_space=space) for _, space in ins],
        out_specs=[pl.BlockSpec(memory_space=space) for _, _, space in outs],
        scratch_shapes=list(scratch),
        compiler_params=pltpu.CompilerParams(vmem_limit_bytes=VMEM_LIMIT),
        cost_estimate=pl.CostEstimate(flops=flops, bytes_accessed=nbytes, transcendentals=0),
    )(*[pltpu.with_memory_space_constraint(x, HBM) if space == HBM else x for x, space in ins])


def ring_at(place, n_blk):
    place = place % n_blk if isinstance(place, int) else lax.rem(place + n_blk, n_blk)
    odd, even = 2 * place - 1, 2 * (n_blk - place)
    if isinstance(place, int):
        return 0 if place == 0 else odd if odd < n_blk else even
    return jnp.where(place == 0, 0, jnp.where(odd < n_blk, odd, even))


def ring_place(index, n_blk):
    odd, even = (index + 1) // 2, lax.rem(n_blk - index // 2, n_blk)
    return jnp.where(lax.rem(index, 2) == 1, odd, even)


def onward(block, d, n_blk):
    pairs = [(ring_at(i, n_blk), ring_at(i + d, n_blk)) for i in range(n_blk)]
    return lax.ppermute(block, "blk", pairs)


def swap(block, e, n_op):
    return lax.ppermute(block, "op", [(i, i ^ e) for i in range(n_op)])


def gather(own, n_blk, n_op, pack, table, early):
    bits = [1 << b for b in reversed(range(1, n_op.bit_length() - 1))]
    order = sorted(range(1, n_blk), key=lambda d: min(d, n_blk - d))
    left, psi, right, tables, columns = {(0, 0): own}, {}, None, None, None
    waiting, late, made = {(0, 0): 0}, None, None
    for j in range(n_blk + len(bits)):
        new, moved = {}, {}
        for (d, e), done in waiting.items():
            if e == 0 and d + 1 < n_blk:
                new[d + 1, 0] = onward(left[d, 0], 1, n_blk), 0
            for b in range(done, len(bits)):
                new[d, e ^ bits[b]] = swap(left[d, e], bits[b], n_op), b + 1
        kept = {key: block for key, (block, _) in new.items()}
        if late is not None:
            moved["psi"] = late
        if j == 0:
            columns, packed = pack()
            moved["right"] = [packed[0]]
            moved["right"] += [swap(part, 2 * e, n_op) for e, part in enumerate(packed[1:], 1)]
        if j == 1:
            moved["tables"] = table(right)
        if j == n_blk - 1 and j >= len(bits) + 1:
            n_early = min(2, n_blk - 1)
            psi[0] = [columns[0]]
            moved["early"] = early(left, psi, n_early, tables)
        if 2 <= j < n_blk:
            moved["other"] = swap(psi[order[j - 2]][0], 1, n_op)
        late = onward(columns[order[j]], order[j], n_blk) if j < n_blk - 1 else None
        if not kept and not moved:
            break
        waiting = {key: done for key, (_, done) in new.items()}
        kept, moved = lax.optimization_barrier((kept, moved))
        left.update(kept)
        right, tables = moved.get("right", right), moved.get("tables", tables)
        made = moved.get("early", made)
        if "psi" in moved:
            psi[order[j - 1]] = [moved["psi"]]
        if "other" in moved:
            psi[order[j - 2]].append(moved["other"])
    return left, psi, right, tables, made


def place_of():
    return lax.axis_index("blk"), lax.axis_index("op")


def pack_body(n_blk, n_op, shift, _, psi, right_in, *outs):
    n_pair = n_op // 2
    psi_out, right_out, right, sems = outs[:n_blk], outs[n_blk : n_blk + n_pair], outs[-2], outs[-1]
    terms, local, width, _ = right.shape
    cols = local * width // n_op
    per = cols // width
    own_blk, own_op = place_of()
    fetch = pltpu.make_async_copy(right_in, right, sems.at[2 * n_blk])
    fetch.start()
    copies = []
    for d in range(n_blk):
        there = ring_at(ring_place(own_blk, n_blk) + d, n_blk) * n_op
        for h in range(psi_out[d].shape[1] // cols):
            start = pl.multiple_of((there + (own_op ^ h)) * cols, LANES)
            copy = pltpu.make_async_copy(
                psi.at[0, :, pl.ds(start, cols)],
                psi_out[d].at[:, h * cols : (h + 1) * cols],
                sems.at[2 * d + h],
            )
            copy.start()
            copies.append(copy)
    lane = lax.broadcasted_iota(jnp.int32, (16, 2 * cols), 1)
    line = jnp.zeros((16, 2 * cols), jnp.float32)
    for k in range(terms):
        line = jnp.where(lane == k, shift[k].astype(jnp.float32), line)
    square = [lax.broadcasted_iota(jnp.int32, (width, width), axis) for axis in (0, 1)]
    unit = (square[0] == square[1]).astype(jnp.bfloat16)
    fetch.wait()
    for e in range(n_pair):
        for k in range(terms):
            turned = []
            for h in range(2):
                first = (own_op ^ (2 * e) ^ h) * per
                for r in range(per):
                    turned.append(
                        lax.dot_general(
                            right[k, first + r], unit, (((0,), (0,)), ((), ())),
                            preferred_element_type=jnp.float32,
                        )
                    )
            side_by_side = jnp.concatenate(turned, axis=1).astype(jnp.bfloat16)
            right_out[e][k * width : (k + 1) * width] = side_by_side
        right_out[e][terms * width :] = line.astype(jnp.bfloat16)
    for copy in copies:
        copy.wait()


def table_body(n_blk, terms, sector, width, left_diag, right_diag, *refs):
    tails, src, widths, slots, diag, right_out = refs[:-5], *refs[-5:]
    right_out[...] = right_diag[...]
    n_pair = len(tails)
    rows, cols = tails[0].shape
    own_blk, _ = place_of()
    lane = lax.broadcasted_iota(jnp.int32, (16, cols), 1)
    for d in range(n_blk):
        slot = ring_at(ring_place(own_blk, n_blk) - d, n_blk)
        slots[d] = slot
        widths[d] = width[sector[slot]]
    for e in range(n_pair):
        tail = tails[e][rows - 16 :].astype(jnp.float32)
        for k in range(terms):
            shift = jnp.max(jnp.where(lane == k, tail, -1e9)).astype(jnp.int32)
            for t in range(n_blk):
                want = sector[slots[t]] - shift
                found = jnp.int32(n_blk)
                for d in range(n_blk):
                    found = jnp.where(sector[slots[d]] == want, d, found)
                src[(t * n_pair + e) * terms + k] = found
    for d in range(n_blk):
        row = left_diag[pl.ds(slots[d], 1), :]
        diag[d] = jnp.transpose(jnp.broadcast_to(row, (diag.shape[2], row.shape[1])))


def diagonal(diag, right_diag, d, h):
    cols = diag.shape[2]
    _, own_op = place_of()
    start = pl.multiple_of((own_op ^ h) * cols, LANES)
    return diag[d] + right_diag[:, pl.ds(start, cols)]


def row_mask(width, shape):
    return lax.broadcasted_iota(jnp.int32, shape, 0) < width


def fold(x):
    return jnp.sum(x.reshape(-1, 8, x.shape[-1]), axis=0)


def whole(x):
    return jnp.sum(jnp.sum(x, axis=0, keepdims=True), axis=1, keepdims=True)


def spread(values, out):
    lane = lax.broadcasted_iota(jnp.int32, out.shape[1:], 1)
    row = jnp.zeros(out.shape[1:], jnp.float32)
    for j, value in enumerate(values):
        row = jnp.where(lane == j, value, row)
    for d in range(out.shape[0]):
        out[d] = row


def by_block(packed, terms, k):
    rows, cols = packed.shape
    width = (rows - 16) // terms
    lane = lax.broadcasted_iota(jnp.int32, (width, cols), 1)
    block = packed[k * width : (k + 1) * width].astype(jnp.float32)
    parts = []
    for r in range(cols // width):
        inside = (lane >= r * width) & (lane < (r + 1) * width)
        parts.append(jnp.where(inside, block, 0.0).astype(jnp.bfloat16))
    return jnp.concatenate(parts, axis=0)


def left_products(block, left, inter):
    n_terms, rows, cols = inter.shape
    at = 0
    while at < n_terms:
        ops = left(at)
        terms = ops.shape[0]
        prod = jnp.dot(ops.reshape(terms * rows, rows), block, preferred_element_type=jnp.float32)
        inter[at : at + terms] = prod.astype(jnp.bfloat16).reshape(terms, rows, cols)
        at += terms


def sum_terms(src, widths, inter, right, out, emit):
    n_blk, n_terms, _, _ = inter.shape
    n_blk -= 1
    terms = n_terms // len(right)
    turned = [by_block(right[j // terms], terms, j % terms) for j in range(n_terms)]
    turned = jnp.concatenate(turned, axis=0)
    for t in range(n_blk):
        moved = [inter[src[t * n_terms + j], j] for j in range(n_terms)]
        moved = jnp.concatenate(moved, axis=1)
        total = jnp.dot(moved, turned, preferred_element_type=jnp.float32)
        total = jnp.where(row_mask(widths[t], total.shape), total, 0.0)
        out[t] = total.astype(jnp.bfloat16)
        emit(t, total)


def keep(left, left_out, sems):
    copies = []
    for d, line in enumerate(left):
        for e, ref in enumerate(line):
            copies.append(pltpu.make_async_copy(ref, left_out.at[d, e], sems.at[d * len(line) + e]))
            copies[-1].start()
    return copies


def masked(psi, width, out):
    at = 0
    for ref in psi:
        block = ref[...].astype(jnp.float32)
        block = jnp.where(row_mask(width, block.shape), block, 0.0)
        out[:, at : at + block.shape[1]] = block.astype(jnp.bfloat16)
        at += block.shape[1]


def take(refs, counts):
    out = []
    for count in counts:
        out.append(refs[:count])
        refs = refs[count:]
    return out, refs


def products_of(psi, left, widths, first, raw_out, inter):
    for d, line in enumerate(left):
        masked(psi[d], widths[first + d], raw_out.at[d])
        terms = line[0].shape[0]
        left_products(raw_out[d], lambda at: line[at // terms][...], inter.at[d])


def early_body(n_pair, counts, widths, *refs):
    left, refs = take(refs, [n_pair] * len(counts))
    psi, (raw_out, inter_out, left_out, sems) = take(refs, counts)
    copies = keep(left, left_out, sems)
    products_of(psi, left, widths, 0, raw_out, inter_out)
    for copy in copies:
        copy.wait()


def first_body(n_blk, n_pair, counts, src, widths, *refs):
    n_late = len(counts)
    n_early = n_blk - n_late
    left, refs = take(refs, [n_pair] * n_late)
    (right,), refs = take(refs, [n_pair])
    psi, refs = take(refs, counts)
    raw_in, inter_in, diag, right_diag, part_out, raw_out, left_out, dots_out = refs[:8]
    sends, (inter, sems) = refs[8:-2], refs[-2:]
    copies = keep(left, left_out, sems)
    for j, (given, own) in enumerate(((inter_in, inter), (raw_in, raw_out))):
        copies.append(
            pltpu.make_async_copy(given, own.at[:n_early], sems.at[n_late * n_pair + j])
        )
        copies[-1].start()
    inter[n_blk] = jnp.zeros_like(inter[n_blk])
    products_of(
        psi, left, widths, n_early, raw_out.at[n_early:], inter.at[n_early:n_blk]
    )
    for copy in copies:
        copy.wait()
    cols = diag.shape[2]
    zero = jnp.zeros((8, cols), jnp.float32)
    sums = [zero, zero]

    def emit(d, total):
        for h in range(2):
            part = slice(h * cols, (h + 1) * cols)
            raw = raw_out[d, :, part].astype(jnp.float32)
            image = total[:, part]
            if h == 0:
                image = image + diagonal(diag, right_diag, d, h) * raw
                sums[0] = sums[0] + fold(raw * raw)
            sums[1] = sums[1] + fold(raw * image)
        for e, send in enumerate(sends, 2):
            send_rows(e, send, d, raw_out, part_out)

    sum_terms(src, widths, inter, right, part_out, emit)
    spread([whole(x) for x in sums], dots_out)


def send_rows(e, send, d, field, part):
    _, own_op = place_of()
    step = send.shape[2]
    rows = pl.ds(pl.multiple_of((own_op ^ e) * step, step), step)
    if e % 2 == 0:
        send[0, d] = field[d, rows].astype(send.dtype)
    send[send.shape[0] - 1, d] = part[d, rows]


def total_of(mine, other, d, h, cols):
    own = mine[d, :, h * cols : (h + 1) * cols].astype(jnp.float32)
    return own + other[d, :, (1 - h) * cols : (2 - h) * cols].astype(jnp.float32)


def norm_theta(parts, count):
    tot = jnp.sum(parts, axis=0) * (1.0 / count)
    scale = lax.rsqrt(tot[:, 0:1] + EPS)
    return scale, tot[:, 1:2] * scale * scale


def second_body(n_blk, n_pair, count, src, widths, left_early, left_late, *refs):
    right, refs = refs[:n_pair], refs[n_pair:]
    parts, raw_in, part_in, other_in, diag, right_diag, dots_out, own_out = refs[:8]
    sends, (inter, corr, sig, fld, part_out, held, sems) = refs[8:-7], refs[-7:]
    copies = []
    n_early = left_early.shape[0]
    for d in range(n_blk):
        kept = left_early.at[d] if d < n_early else left_late.at[d - n_early]
        copies.append(pltpu.make_async_copy(kept, held.at[d], sems.at[d]))
        copies[-1].start()
    inter[n_blk] = jnp.zeros_like(inter[n_blk])
    scale, theta = norm_theta(parts[...], count)
    cols = diag.shape[2]
    halves = []
    for h in range(2):
        part = slice(h * cols, (h + 1) * cols)
        vv = vc = vs = jnp.zeros((8, cols), jnp.float32)
        for d in range(n_blk):
            vec = raw_in[d, :, part].astype(jnp.float32) * scale
            sigma = total_of(part_in, other_in, d, h, cols)
            sigma = (sigma + diagonal(diag, right_diag, d, h) * raw_in[d, :, part].astype(jnp.float32)) * scale
            sig[d, :, part] = sigma
            den = diagonal(diag, right_diag, d, h) - theta
            item = (sigma - theta * vec) * den / jnp.maximum(den * den, 0.25)
            corr[d, :, part] = item
            vv, vc = vv + fold(vec * vec), vc + fold(vec * item)
            if h == 0:
                vs = vs + fold(vec * sigma)
        halves.append((whole(vv), whole(vc), vs))
    along = (halves[0][1] + halves[1][1]) / jnp.maximum(halves[0][0] + halves[1][0], 1e-30)
    terms = held.shape[2]
    for copy in copies:
        copy.wait()
    for d in range(n_blk):
        for h in range(2):
            part = slice(h * cols, (h + 1) * cols)
            vec = raw_in[d, :, part].astype(jnp.float32) * scale
            fld[d, :, part] = (corr[d, :, part] - along * vec).astype(jnp.bfloat16)
        left_products(fld[d], lambda at: held[d, at // terms], inter.at[d])
    zero = jnp.zeros((8, cols), jnp.float32)
    sums = [zero for _ in range(5)]

    def emit(d, total):
        for h in range(2):
            part = slice(h * cols, (h + 1) * cols)
            field = fld[d, :, part].astype(jnp.float32)
            vec = raw_in[d, :, part].astype(jnp.float32) * scale
            image = total[:, part]
            if h == 0:
                image = image + diagonal(diag, right_diag, d, h) * field
                for j, prod in enumerate((field * field, vec * field, field * sig[d, :, part])):
                    sums[j] = sums[j] + fold(prod)
            sums[3] = sums[3] + fold(vec * image)
            sums[4] = sums[4] + fold(field * image)
        for e, send in enumerate(sends, 1):
            send_rows(e, send, d, fld, part_out)
        rows = pl.ds(pl.multiple_of(own_op * step, step), step)
        for j, ref in enumerate((raw_in, sig, fld, part_out)):
            own_out[j, d] = ref[d, rows].astype(own_out.dtype)

    _, own_op = place_of()
    step = own_out.shape[2]
    sum_terms(src, widths, inter, right, part_out, emit)
    vv, vc, vs = halves[0]
    spread([vv, vc] + [whole(x) for x in [vs] + sums], dots_out)


def ritz_pair(theta, h_mix, h_two):
    diff, twice = theta - h_two, 2.0 * h_mix
    size = jnp.sqrt(diff * diff + twice * twice)
    some = size > 0.0
    safe = jnp.where(some, size, 1.0)
    big = jnp.sqrt(0.5 + 0.5 * jnp.abs(diff) / safe)
    small = 0.5 * jnp.abs(twice) / (safe * big)
    sine = jnp.where(diff >= 0.0, small, big)
    cosine = jnp.where(diff >= 0.0, big, small)
    sine = jnp.where(some, sine, 0.0)
    cosine = jnp.where(some, cosine, 1.0)
    upward = (twice > 0.0) | ((twice == 0.0) & (diff < 0.0))
    return sine, jnp.where(upward, -cosine, cosine), 0.5 * (theta + h_two) - 0.5 * size


def third_body(n_blk, n_op, count, slots, parts1, parts2, diag, right_diag, own, *refs):
    got1, got2 = refs[: n_op - 2], refs[n_op - 2 : 2 * n_op - 3]
    new_out, res_out, energy_out = refs[2 * n_op - 3 :]
    step, cols = new_out.shape[1], new_out.shape[2] // n_op
    own_blk, own_op = place_of()
    scale, theta = norm_theta(parts1[...], count)
    pairs = parts2[...].reshape(n_blk * n_op // 2, 2, *parts2.shape[1:])
    pairs = pairs[:, 0] + pairs[:, 1]
    vv, vc, vs, ff, vf, fs, vt, ft = (pairs[:, 0, j : j + 1] for j in range(8))

    def mean(x):
        return jnp.sum(x, axis=0, keepdims=True) * (1.0 / count)

    def nearest(vv, vc):
        return vc / jnp.maximum(vv, 1e-30)

    along = mean(vc)
    beta = nearest(vv, vc) - along
    norm_sq = mean(ff + 2.0 * beta * vf + beta * beta * vv)
    unit = lax.rsqrt(jnp.maximum(norm_sq, 0.0) + EPS)
    v_s1 = unit * mean(vt + beta * vs)
    u_s0 = unit * mean(fs + beta * vs)
    u_s1 = unit * unit * mean(ft + beta * (vt + fs) + beta * beta * vs)
    cv, cu, energy = ritz_pair(theta, 0.5 * (v_s1 + u_s0), u_s1)
    energy_out[0] = jnp.max(energy)
    cu = cu * unit
    mine = pl.ds(pl.multiple_of(own_op * step, step), step)
    for e in range(0, n_op, 2):
        there = own_blk * n_op + (own_op ^ e)
        pair = parts2[there] + parts2[own_blk * n_op + (own_op ^ e ^ 1)]
        on_vec = cv + cu * (nearest(pair[:, 0:1], pair[:, 1:2]) - along)
        for h in range(2):
            at = pl.multiple_of((own_op ^ e ^ h) * cols, LANES)
            part, crossed = slice(h * cols, (h + 1) * cols), slice((1 - h) * cols, (2 - h) * cols)
            for d in range(n_blk):
                dmat = diag[d, mine] + right_diag[:, pl.ds(at, cols)]
                if e:
                    raw, fld = got1[e - 2][0, d, :, part], got2[e - 1][0, d, :, part]
                    vec = raw.astype(jnp.float32) * scale
                    sigma = got1[e - 2][1, d, :, part].astype(jnp.float32)
                    sigma = sigma + got1[e - 1][0, d, :, crossed].astype(jnp.float32)
                    sigma = sigma * scale + dmat * vec
                    image = got2[e - 1][1, d, :, part].astype(jnp.float32)
                else:
                    raw, sigma, fld, image = (own[j, d, :, part].astype(jnp.float32) for j in range(4))
                    vec = raw * scale
                fld = fld.astype(jnp.float32)
                image = image + got2[e][0, d, :, crossed].astype(jnp.float32) + dmat * fld
                newvec = on_vec * vec + cu * fld
                res = on_vec * sigma + cu * image - energy * newvec
                new_out[slots[d], :, pl.ds(at, cols)] = newvec.astype(jnp.bfloat16)
                res_out[slots[d], :, pl.ds(at, cols)] = res.astype(jnp.bfloat16)


def per_device(
    psi, left_ops, right_ops, term_shift, slot_sector, sector_width, diag_left, diag_right
):
    n_blk, n_op = lax.axis_size("blk"), lax.axis_size("op")
    _, rows, ncols = psi.shape
    terms, _, width, _ = right_ops.shape
    n_pair = n_op // 2
    cols = diag_right.shape[0] // n_op
    step = rows // n_op
    count = float(n_blk * rows * ncols)
    n_dev = n_blk * n_op
    bf16, f32, i32 = jnp.bfloat16, jnp.float32, jnp.int32
    last = sorted(range(1, n_blk), key=lambda d: min(d, n_blk - d))[-1]

    def pack():
        first = swap(term_shift, 1, n_op)
        sent = kernel(
            functools.partial(pack_body, n_blk, n_op),
            [(term_shift, SMEM), (first, SMEM), (psi, HBM), (right_ops, HBM)],
            [((rows, 2 * cols if d in (0, last) else cols), bf16, VMEM) for d in range(n_blk)]
            + [((terms * width + 16, 2 * cols), bf16, VMEM)] * n_pair,
            [pltpu.VMEM(right_ops.shape, bf16), pltpu.SemaphoreType.DMA((2 * n_blk + 1,))],
            nbytes=1 << 20,
        )
        return sent[:n_blk], sent[n_blk:]

    def table(right):
        return kernel(
            functools.partial(table_body, n_blk, terms),
            [(slot_sector, SMEM), (sector_width, SMEM), (diag_left, VMEM), (diag_right[None], VMEM)]
            + [(block, VMEM) for block in right],
            [((n_blk * n_pair * terms,), i32, SMEM)]
            + [((n_blk,), i32, SMEM)] * 2
            + [((n_blk, rows, LANES), f32, VMEM), ((1, n_op * cols), f32, VMEM)],
        )

    def inputs(left, psi, those):
        blocks = [left[d, 2 * e] for d in those for e in range(n_pair)]
        halves = [half for d in those for half in psi[d]]
        return [(x, VMEM) for x in blocks], [(x, VMEM) for x in halves], [len(psi[d]) for d in those]

    def early(left, psi, n_early, tables):
        left_ins, psi_ins, counts = inputs(left, psi, range(n_early))
        return kernel(
            functools.partial(early_body, n_pair, counts),
            [(tables[1], SMEM)] + left_ins + psi_ins,
            [
                ((n_early, rows, 2 * cols), bf16, VMEM),
                ((n_early, n_pair * terms, rows, 2 * cols), bf16, VMEM),
                ((n_early, n_pair, terms, rows, rows), bf16, HBM),
            ],
            [pltpu.SemaphoreType.DMA((n_early * n_pair,))],
            flops=2 * n_early * rows * rows * 2 * cols * terms * n_pair,
            nbytes=4 << 20,
        )

    left, psi_by, right, (src, widths, slots, *both), (raw_early, inter_early, left_early) = gather(
        left_ops[:, 0], n_blk, n_op, pack, table, early
    )
    n_early = raw_early.shape[0]
    n_late = n_blk - n_early
    left_ins, psi_ins, counts = inputs(left, psi_by, range(n_early, n_blk))
    right_ins = [(block, VMEM) for block in right]
    diags = [(x, VMEM) for x in both]

    tables = [(src, SMEM), (widths, SMEM)]
    narrow = ((n_blk, rows, 2 * cols), bf16, VMEM)
    dots = ((n_dev, 1, LANES), f32, VMEM)
    sends = [((2 - e % 2, n_blk, step, 2 * cols), bf16, VMEM) for e in range(1, n_op)]
    inter = pltpu.VMEM((n_blk + 1, n_pair * terms, rows, 2 * cols), bf16)
    left_late = (n_late, n_pair, terms, rows, rows)
    cost = dict(flops=2 * n_blk * rows * 2 * cols * terms * n_pair * (rows + 2 * cols), nbytes=6 << 20)

    def totals(parts):
        return lax.all_to_all(parts, ("blk", "op"), 0, 0, tiled=True)

    part1, raw, kept, dots1, *out1 = kernel(
        functools.partial(first_body, n_blk, n_pair, counts),
        tables + left_ins + right_ins + psi_ins + [(raw_early, VMEM), (inter_early, VMEM)] + diags,
        [narrow, narrow, (left_late, bf16, HBM), dots] + sends[1:],
        [inter, pltpu.SemaphoreType.DMA((n_late * n_pair + 2,))],
        **cost,
    )
    parts1, other1 = lax.optimization_barrier((totals(dots1), swap(part1, 1, n_op)))
    got1 = [swap(block, e, n_op) for e, block in enumerate(out1, 2)]
    dots2, own, *out2 = kernel(
        functools.partial(second_body, n_blk, n_pair, count),
        tables + [(left_early, HBM), (kept, HBM)] + right_ins
        + [(x, VMEM) for x in (parts1, raw, part1, other1)] + diags,
        [dots, ((4, n_blk, step, 2 * cols), bf16, VMEM)] + sends,
        [
            inter,
            pltpu.VMEM((n_blk, rows, 2 * cols), f32),
            pltpu.VMEM((n_blk, rows, 2 * cols), f32),
            pltpu.VMEM((n_blk, rows, 2 * cols), bf16),
            pltpu.VMEM((n_blk, rows, 2 * cols), bf16),
            pltpu.VMEM((n_blk, *left_late[1:]), bf16),
            pltpu.SemaphoreType.DMA((n_blk,)),
        ],
        flops=4 * cost["flops"],
        nbytes=24 << 20,
    )
    dots2, out2, got1 = lax.optimization_barrier((dots2, out2, got1))
    parts2 = totals(dots2)
    got2 = [swap(block, e, n_op) for e, block in enumerate(out2, 1)]
    final = ((n_blk, step, n_op * cols), bf16, VMEM)
    new, res, energy = kernel(
        functools.partial(third_body, n_blk, n_op, count),
        [(slots, SMEM)] + [(x, VMEM) for x in (parts1, parts2)] + diags
        + [(x, VMEM) for x in (own, *got1, *got2)],
        [final, final, ((1,), f32, SMEM)],
        nbytes=4 << 20,
    )
    return new, res, energy


def solution(mesh):
    placed = (
        P(("grp", "blk"), None, None),
        P("op", ("grp", "blk"), None, None),
        P("op", ("grp", "blk"), None, None),
        P("op"),
        P("grp"),
        P("grp"),
        P("grp", None),
        P(("grp", "blk")),
    )

    def body(*args):
        psi, left_ops, right_ops, diag_right = args[0], args[1], args[2], args[7]
        n_op = mesh.shape["op"]
        cols = diag_right.shape[0] // n_op
        fits = (
            psi.shape[0] == 1
            and diag_right.shape[0] % n_op == 0
            and cols == LANES
            and n_op % 2 == 0
            and cols % right_ops.shape[2] == 0
            and cols // right_ops.shape[2] * n_op == right_ops.shape[1]
            and psi.shape[1] % (16 * n_op) == 0
            and n_op & (n_op - 1) == 0
            and mesh.shape["blk"] > n_op.bit_length() - 1
        )
        return (per_device if fits else per_device_general)(*args)

    return jax.shard_map(
        body,
        mesh=mesh,
        in_specs=placed,
        out_specs=(P("grp", "op", "blk"), P("grp", "op", "blk"), P("grp")),
        check_vma=False,
    )
```

```python
import functools

import jax
import jax.numpy as jnp
from jax import lax
from jax.experimental import pallas as pl
from jax.experimental.pallas import tpu as pltpu
from jax.sharding import PartitionSpec as P

EPS = 1e-06
LANES = 128
VMEM_LIMIT = 20 * 1024 * 1024


def per_device_general(
    psi, left_ops, right_ops, term_shift, slot_sector, sector_width, diag_left, diag_right
):
    sec_dev, rows, ncols = psi.shape
    nsec = slot_sector.shape[0]
    terms_dev = left_ops.shape[0]
    right_local = right_ops.shape[1]
    right_width = right_ops.shape[2]
    local_cols = diag_right.shape[0]
    count = float(nsec * rows * ncols)
    match = slot_sector[:, None] == jnp.arange(nsec)[None, :]
    widths = jnp.sum(jnp.where(match, sector_width[None, :], 0), axis=1)
    mask_all = (jnp.arange(rows)[None, :] < widths[:, None]).astype(jnp.float32)
    own_mask = lax.dynamic_slice_in_dim(mask_all, lax.axis_index("blk") * sec_dev, sec_dev, 0)
    raw = psi.astype(jnp.float32) * own_mask[:, :, None]
    squares = lax.psum(jnp.sum(raw * raw), "blk")
    v_left = (raw * lax.rsqrt(squares / count + EPS)).astype(jnp.bfloat16)
    onehots = (
        slot_sector[None, None, :] == slot_sector[None, :, None] - term_shift[:, None, None]
    ).astype(jnp.bfloat16)
    op_rows = rows // lax.axis_size("op")
    op_start = lax.axis_index("op") * op_rows
    dmat = diag_left[:, :, None] + diag_right[None, None, :]

    def left_local(field):
        return jnp.einsum(
            "ksij,sjc->ksic", left_ops, field, preferred_element_type=jnp.float32
        ).astype(jnp.bfloat16)

    def right_part(moved_in):
        flat = moved_in.reshape(terms_dev, nsec, rows * local_cols)
        shifted = jnp.einsum(
            "kts,ksx->ktx", onehots, flat, preferred_element_type=jnp.float32
        ).astype(jnp.bfloat16)
        shifted = shifted.reshape(terms_dev, nsec, rows, right_local, right_width)
        accum = jnp.einsum(
            "ktwrc,krdc->twrd", shifted, right_ops, preferred_element_type=jnp.float32
        )
        return accum.reshape(nsec, rows, local_cols) * mask_all[:, :, None]

    def op_total(partial_value):
        return lax.psum(partial_value.astype(jnp.bfloat16), "op").astype(jnp.float32)

    def final_rows(array):
        return lax.dynamic_slice_in_dim(array, op_start, op_rows, 1)

    def reduce_dots(values):
        sums = lax.psum(values, "blk")
        return tuple((item / count for item in sums))

    moved_first, v_moved = (
        lax.all_to_all(left_local(v_left), "blk", split_axis=3, concat_axis=1, tiled=True),
        lax.all_to_all(v_left[None], "blk", split_axis=3, concat_axis=1, tiled=True),
    )
    v_right = v_moved[0]
    vec32 = v_right.astype(jnp.float32)
    first_sigma = op_total(right_part(moved_first)) + dmat * vec32
    theta = reduce_dots((jnp.sum(vec32 * first_sigma),))[0]
    resid = first_sigma - theta * vec32
    den = dmat - theta
    corr = resid * den / jnp.maximum(den * den, 0.25)
    along = reduce_dots((jnp.sum(vec32 * corr),))[0]
    orth = corr - along * vec32
    norm_sq = reduce_dots((jnp.sum(orth * orth),))[0]
    update = (orth * lax.rsqrt(norm_sq + EPS)).astype(jnp.bfloat16)
    upd32 = update.astype(jnp.float32)
    upd_left = lax.all_to_all(update, "blk", split_axis=0, concat_axis=2, tiled=True)
    moved_second = lax.all_to_all(
        left_local(upd_left), "blk", split_axis=3, concat_axis=1, tiled=True
    )
    second_sigma = op_total(right_part(moved_second)) + dmat * upd32
    v_s1, u_s0, u_s1 = reduce_dots(
        (jnp.sum(vec32 * second_sigma), jnp.sum(upd32 * first_sigma), jnp.sum(upd32 * second_sigma))
    )
    h_mix = 0.5 * (v_s1 + u_s0)
    coef_v, coef_u, energy = ritz(theta, h_mix, u_s1)
    newvec = coef_v * vec32 + coef_u * upd32
    image = coef_v * first_sigma + coef_u * second_sigma
    new_out = final_rows(newvec.astype(jnp.bfloat16))
    res_out = final_rows((image - energy * newvec).astype(jnp.bfloat16))
    return (new_out, res_out, jnp.reshape(energy, (1,)))


def ritz(theta, h_mix, h_two):
    angle = 0.5 * jnp.arctan2(2.0 * h_mix, theta - h_two)
    sine = jnp.sin(angle)
    flip = jnp.where(sine > 0, -1.0, 1.0)
    coef_v = -sine * flip
    coef_u = jnp.cos(angle) * flip
    half = 0.5 * (theta - h_two)
    energy = 0.5 * (theta + h_two) - jnp.sqrt(half * half + h_mix * h_mix)
    return coef_v, coef_u, energy


VMEM, SMEM, HBM = pltpu.VMEM, pltpu.SMEM, pltpu.HBM


def kernel(body, ins, outs, scratch=(), flops=0, nbytes=0):
    return pl.pallas_call(
        body,
        out_shape=[
            HBM(shape, dtype) if space == HBM else jax.ShapeDtypeStruct(shape, dtype)
            for shape, dtype, space in outs
        ],
        in_specs=[pl.BlockSpec(memory_space=space) for _, space in ins],
        out_specs=[pl.BlockSpec(memory_space=space) for _, _, space in outs],
        scratch_shapes=list(scratch),
        compiler_params=pltpu.CompilerParams(vmem_limit_bytes=VMEM_LIMIT),
        cost_estimate=pl.CostEstimate(flops=flops, bytes_accessed=nbytes, transcendentals=0),
    )(*[pltpu.with_memory_space_constraint(x, HBM) if space == HBM else x for x, space in ins])


def ring_at(place, n_blk):
    place = place % n_blk if isinstance(place, int) else lax.rem(place + n_blk, n_blk)
    odd, even = 2 * place - 1, 2 * (n_blk - place)
    if isinstance(place, int):
        return 0 if place == 0 else odd if odd < n_blk else even
    return jnp.where(place == 0, 0, jnp.where(odd < n_blk, odd, even))


def ring_place(index, n_blk):
    odd, even = (index + 1) // 2, lax.rem(n_blk - index // 2, n_blk)
    return jnp.where(lax.rem(index, 2) == 1, odd, even)


def onward(block, d, n_blk):
    pairs = [(ring_at(i, n_blk), ring_at(i + d, n_blk)) for i in range(n_blk)]
    return lax.ppermute(block, "blk", pairs)


def swap(block, e, n_op):
    return lax.ppermute(block, "op", [(i, i ^ e) for i in range(n_op)])


def gather(own, n_blk, n_op, pack, table, early):
    bits = [1 << b for b in reversed(range(1, n_op.bit_length() - 1))]
    order = sorted(range(1, n_blk), key=lambda d: min(d, n_blk - d))
    left, psi, right, tables, columns = {(0, 0): own}, {}, None, None, None
    waiting, late, made = {(0, 0): 0}, None, None
    for j in range(n_blk + len(bits)):
        new, moved = {}, {}
        for (d, e), done in waiting.items():
            if e == 0 and d + 1 < n_blk:
                new[d + 1, 0] = onward(left[d, 0], 1, n_blk), 0
            for b in range(done, len(bits)):
                new[d, e ^ bits[b]] = swap(left[d, e], bits[b], n_op), b + 1
        kept = {key: block for key, (block, _) in new.items()}
        if late is not None:
            moved["psi"] = late
        if j == 0:
            columns, packed = pack()
            moved["right"] = [packed[0]]
            moved["right"] += [swap(part, 2 * e, n_op) for e, part in enumerate(packed[1:], 1)]
        if j == 1:
            moved["tables"] = table(right)
        if j == n_blk - 1 and j >= len(bits) + 1:
            n_early = min(2, n_blk - 1)
            psi[0] = [columns[0]]
            moved["early"] = early(left, psi, n_early, tables)
        if 2 <= j < n_blk:
            moved["other"] = swap(psi[order[j - 2]][0], 1, n_op)
        late = onward(columns[order[j]], order[j], n_blk) if j < n_blk - 1 else None
        if not kept and not moved:
            break
        waiting = {key: done for key, (_, done) in new.items()}
        kept, moved = lax.optimization_barrier((kept, moved))
        left.update(kept)
        right, tables = moved.get("right", right), moved.get("tables", tables)
        made = moved.get("early", made)
        if "psi" in moved:
            psi[order[j - 1]] = [moved["psi"]]
        if "other" in moved:
            psi[order[j - 2]].append(moved["other"])
    return left, psi, right, tables, made


def place_of():
    return lax.axis_index("blk"), lax.axis_index("op")


def pack_body(n_blk, n_op, shift, _, psi, right_in, *outs):
    n_pair = n_op // 2
    psi_out, right_out, right, sems = outs[:n_blk], outs[n_blk : n_blk + n_pair], outs[-2], outs[-1]
    terms, local, width, _ = right.shape
    cols = local * width // n_op
    per = cols // width
    own_blk, own_op = place_of()
    fetch = pltpu.make_async_copy(right_in, right, sems.at[2 * n_blk])
    fetch.start()
    copies = []
    for d in range(n_blk):
        there = ring_at(ring_place(own_blk, n_blk) + d, n_blk) * n_op
        for h in range(psi_out[d].shape[1] // cols):
            start = pl.multiple_of((there + (own_op ^ h)) * cols, LANES)
            copy = pltpu.make_async_copy(
                psi.at[0, :, pl.ds(start, cols)],
                psi_out[d].at[:, h * cols : (h + 1) * cols],
                sems.at[2 * d + h],
            )
            copy.start()
            copies.append(copy)
    lane = lax.broadcasted_iota(jnp.int32, (16, 2 * cols), 1)
    line = jnp.zeros((16, 2 * cols), jnp.float32)
    for k in range(terms):
        line = jnp.where(lane == k, shift[k].astype(jnp.float32), line)
    square = [lax.broadcasted_iota(jnp.int32, (width, width), axis) for axis in (0, 1)]
    unit = (square[0] == square[1]).astype(jnp.bfloat16)
    fetch.wait()
    for e in range(n_pair):
        for k in range(terms):
            turned = []
            for h in range(2):
                first = (own_op ^ (2 * e) ^ h) * per
                for r in range(per):
                    turned.append(
                        lax.dot_general(
                            right[k, first + r], unit, (((0,), (0,)), ((), ())),
                            preferred_element_type=jnp.float32,
                        )
                    )
            side_by_side = jnp.concatenate(turned, axis=1).astype(jnp.bfloat16)
            right_out[e][k * width : (k + 1) * width] = side_by_side
        right_out[e][terms * width :] = line.astype(jnp.bfloat16)
    for copy in copies:
        copy.wait()


def table_body(n_blk, terms, sector, width, left_diag, right_diag, *refs):
    tails, src, widths, slots, diag, right_out = refs[:-5], *refs[-5:]
    right_out[...] = right_diag[...]
    n_pair = len(tails)
    rows, cols = tails[0].shape
    own_blk, _ = place_of()
    lane = lax.broadcasted_iota(jnp.int32, (16, cols), 1)
    for d in range(n_blk):
        slot = ring_at(ring_place(own_blk, n_blk) - d, n_blk)
        slots[d] = slot
        widths[d] = width[sector[slot]]
    for e in range(n_pair):
        tail = tails[e][rows - 16 :].astype(jnp.float32)
        for k in range(terms):
            shift = jnp.max(jnp.where(lane == k, tail, -1e9)).astype(jnp.int32)
            for t in range(n_blk):
                want = sector[slots[t]] - shift
                found = jnp.int32(n_blk)
                for d in range(n_blk):
                    found = jnp.where(sector[slots[d]] == want, d, found)
                src[(t * n_pair + e) * terms + k] = found
    for d in range(n_blk):
        row = left_diag[pl.ds(slots[d], 1), :]
        diag[d] = jnp.transpose(jnp.broadcast_to(row, (diag.shape[2], row.shape[1])))


def diagonal(diag, right_diag, d, h):
    cols = diag.shape[2]
    _, own_op = place_of()
    start = pl.multiple_of((own_op ^ h) * cols, LANES)
    return diag[d] + right_diag[:, pl.ds(start, cols)]


def row_mask(width, shape):
    return lax.broadcasted_iota(jnp.int32, shape, 0) < width


def fold(x):
    return jnp.sum(x.reshape(-1, 8, x.shape[-1]), axis=0)


def whole(x):
    return jnp.sum(jnp.sum(x, axis=0, keepdims=True), axis=1, keepdims=True)


def spread(values, out):
    lane = lax.broadcasted_iota(jnp.int32, out.shape[1:], 1)
    row = jnp.zeros(out.shape[1:], jnp.float32)
    for j, value in enumerate(values):
        row = jnp.where(lane == j, value, row)
    for d in range(out.shape[0]):
        out[d] = row


def by_block(packed, terms, k):
    rows, cols = packed.shape
    width = (rows - 16) // terms
    lane = lax.broadcasted_iota(jnp.int32, (width, cols), 1)
    block = packed[k * width : (k + 1) * width].astype(jnp.float32)
    parts = []
    for r in range(cols // width):
        inside = (lane >= r * width) & (lane < (r + 1) * width)
        parts.append(jnp.where(inside, block, 0.0).astype(jnp.bfloat16))
    return jnp.concatenate(parts, axis=0)


def left_products(block, left, inter):
    n_terms, rows, cols = inter.shape
    at = 0
    while at < n_terms:
        ops = left(at)
        terms = ops.shape[0]
        prod = jnp.dot(ops.reshape(terms * rows, rows), block, preferred_element_type=jnp.float32)
        inter[at : at + terms] = prod.astype(jnp.bfloat16).reshape(terms, rows, cols)
        at += terms


def sum_terms(src, widths, inter, right, out, emit):
    n_blk, n_terms, _, _ = inter.shape
    n_blk -= 1
    terms = n_terms // len(right)
    turned = [by_block(right[j // terms], terms, j % terms) for j in range(n_terms)]
    for t in range(n_blk):
        total = None
        for j in range(n_terms):
            part = jnp.dot(
                inter[src[t * n_terms + j], j], turned[j], preferred_element_type=jnp.float32
            )
            total = part if total is None else total + part
        total = jnp.where(row_mask(widths[t], total.shape), total, 0.0)
        out[t] = total.astype(jnp.bfloat16)
        emit(t, total)


def keep(left, left_out, sems):
    copies = []
    for d, line in enumerate(left):
        for e, ref in enumerate(line):
            copies.append(pltpu.make_async_copy(ref, left_out.at[d, e], sems.at[d * len(line) + e]))
            copies[-1].start()
    return copies


def masked(psi, width, out):
    at = 0
    for ref in psi:
        block = ref[...].astype(jnp.float32)
        block = jnp.where(row_mask(width, block.shape), block, 0.0)
        out[:, at : at + block.shape[1]] = block.astype(jnp.bfloat16)
        at += block.shape[1]


def take(refs, counts):
    out = []
    for count in counts:
        out.append(refs[:count])
        refs = refs[count:]
    return out, refs


def products_of(psi, left, widths, first, raw_out, inter):
    for d, line in enumerate(left):
        masked(psi[d], widths[first + d], raw_out.at[d])
        terms = line[0].shape[0]
        left_products(raw_out[d], lambda at: line[at // terms][...], inter.at[d])


def early_body(n_pair, counts, widths, *refs):
    left, refs = take(refs, [n_pair] * len(counts))
    psi, (raw_out, inter_out, left_out, sems) = take(refs, counts)
    copies = keep(left, left_out, sems)
    products_of(psi, left, widths, 0, raw_out, inter_out)
    for copy in copies:
        copy.wait()


def first_body(n_blk, n_pair, counts, src, widths, *refs):
    n_late = len(counts)
    n_early = n_blk - n_late
    left, refs = take(refs, [n_pair] * n_late)
    (right,), refs = take(refs, [n_pair])
    psi, refs = take(refs, counts)
    raw_in, inter_in, diag, right_diag, part_out, raw_out, left_out, dots_out = refs[:8]
    sends, (inter, sems) = refs[8:-2], refs[-2:]
    copies = keep(left, left_out, sems)
    for j, (given, own) in enumerate(((inter_in, inter), (raw_in, raw_out))):
        copies.append(
            pltpu.make_async_copy(given, own.at[:n_early], sems.at[n_late * n_pair + j])
        )
        copies[-1].start()
    inter[n_blk] = jnp.zeros_like(inter[n_blk])
    products_of(
        psi, left, widths, n_early, raw_out.at[n_early:], inter.at[n_early:n_blk]
    )
    for copy in copies:
        copy.wait()
    cols = diag.shape[2]
    zero = jnp.zeros((8, cols), jnp.float32)
    sums = [zero, zero]

    def emit(d, total):
        for h in range(2):
            part = slice(h * cols, (h + 1) * cols)
            raw = raw_out[d, :, part].astype(jnp.float32)
            image = total[:, part]
            if h == 0:
                image = image + diagonal(diag, right_diag, d, h) * raw
                sums[0] = sums[0] + fold(raw * raw)
            sums[1] = sums[1] + fold(raw * image)
        for e, send in enumerate(sends, 2):
            send_rows(e, send, d, raw_out, part_out)

    sum_terms(src, widths, inter, right, part_out, emit)
    spread([whole(x) for x in sums], dots_out)


def send_rows(e, send, d, field, part):
    _, own_op = place_of()
    step = send.shape[2]
    rows = pl.ds(pl.multiple_of((own_op ^ e) * step, step), step)
    if e % 2 == 0:
        send[0, d] = field[d, rows].astype(send.dtype)
    send[send.shape[0] - 1, d] = part[d, rows]


def total_of(mine, other, d, h, cols):
    own = mine[d, :, h * cols : (h + 1) * cols].astype(jnp.float32)
    return own + other[d, :, (1 - h) * cols : (2 - h) * cols].astype(jnp.float32)


def norm_theta(parts, count):
    tot = jnp.sum(parts, axis=0) * (1.0 / count)
    scale = lax.rsqrt(tot[:, 0:1] + EPS)
    return scale, tot[:, 1:2] * scale * scale


def second_body(n_blk, n_pair, count, src, widths, left_early, left_late, *refs):
    right, refs = refs[:n_pair], refs[n_pair:]
    parts, raw_in, part_in, other_in, diag, right_diag, dots_out, own_out = refs[:8]
    sends, (inter, corr, sig, fld, part_out, held, sems) = refs[8:-7], refs[-7:]
    copies = []
    n_early = left_early.shape[0]
    for d in range(n_blk):
        kept = left_early.at[d] if d < n_early else left_late.at[d - n_early]
        copies.append(pltpu.make_async_copy(kept, held.at[d], sems.at[d]))
        copies[-1].start()
    inter[n_blk] = jnp.zeros_like(inter[n_blk])
    scale, theta = norm_theta(parts[...], count)
    cols = diag.shape[2]
    halves = []
    for h in range(2):
        part = slice(h * cols, (h + 1) * cols)
        vv = vc = vs = jnp.zeros((8, cols), jnp.float32)
        for d in range(n_blk):
            vec = raw_in[d, :, part].astype(jnp.float32) * scale
            sigma = total_of(part_in, other_in, d, h, cols)
            sigma = (sigma + diagonal(diag, right_diag, d, h) * raw_in[d, :, part].astype(jnp.float32)) * scale
            sig[d, :, part] = sigma
            den = diagonal(diag, right_diag, d, h) - theta
            item = (sigma - theta * vec) * den / jnp.maximum(den * den, 0.25)
            corr[d, :, part] = item
            vv, vc = vv + fold(vec * vec), vc + fold(vec * item)
            if h == 0:
                vs = vs + fold(vec * sigma)
        halves.append((whole(vv), whole(vc), vs))
    along = (halves[0][1] + halves[1][1]) / jnp.maximum(halves[0][0] + halves[1][0], 1e-30)
    terms = held.shape[2]
    for copy in copies:
        copy.wait()
    for d in range(n_blk):
        for h in range(2):
            part = slice(h * cols, (h + 1) * cols)
            vec = raw_in[d, :, part].astype(jnp.float32) * scale
            fld[d, :, part] = (corr[d, :, part] - along * vec).astype(jnp.bfloat16)
        left_products(fld[d], lambda at: held[d, at // terms], inter.at[d])
    zero = jnp.zeros((8, cols), jnp.float32)
    sums = [zero for _ in range(5)]

    def emit(d, total):
        for h in range(2):
            part = slice(h * cols, (h + 1) * cols)
            field = fld[d, :, part].astype(jnp.float32)
            vec = raw_in[d, :, part].astype(jnp.float32) * scale
            image = total[:, part]
            if h == 0:
                image = image + diagonal(diag, right_diag, d, h) * field
                for j, prod in enumerate((field * field, vec * field, field * sig[d, :, part])):
                    sums[j] = sums[j] + fold(prod)
            sums[3] = sums[3] + fold(vec * image)
            sums[4] = sums[4] + fold(field * image)
        for e, send in enumerate(sends, 1):
            send_rows(e, send, d, fld, part_out)
        rows = pl.ds(pl.multiple_of(own_op * step, step), step)
        for j, ref in enumerate((raw_in, sig, fld, part_out)):
            own_out[j, d] = ref[d, rows].astype(own_out.dtype)

    _, own_op = place_of()
    step = own_out.shape[2]
    sum_terms(src, widths, inter, right, part_out, emit)
    vv, vc, vs = halves[0]
    spread([vv, vc] + [whole(x) for x in [vs] + sums], dots_out)


def ritz_pair(theta, h_mix, h_two):
    diff, twice = theta - h_two, 2.0 * h_mix
    size = jnp.sqrt(diff * diff + twice * twice)
    some = size > 0.0
    safe = jnp.where(some, size, 1.0)
    big = jnp.sqrt(0.5 + 0.5 * jnp.abs(diff) / safe)
    small = 0.5 * jnp.abs(twice) / (safe * big)
    sine = jnp.where(diff >= 0.0, small, big)
    cosine = jnp.where(diff >= 0.0, big, small)
    sine = jnp.where(some, sine, 0.0)
    cosine = jnp.where(some, cosine, 1.0)
    upward = (twice > 0.0) | ((twice == 0.0) & (diff < 0.0))
    return sine, jnp.where(upward, -cosine, cosine), 0.5 * (theta + h_two) - 0.5 * size


def third_body(n_blk, n_op, count, slots, parts1, parts2, diag, right_diag, own, *refs):
    got1, got2 = refs[: n_op - 2], refs[n_op - 2 : 2 * n_op - 3]
    new_out, res_out, energy_out = refs[2 * n_op - 3 :]
    step, cols = new_out.shape[1], new_out.shape[2] // n_op
    own_blk, own_op = place_of()
    scale, theta = norm_theta(parts1[...], count)
    pairs = parts2[...].reshape(n_blk * n_op // 2, 2, *parts2.shape[1:])
    pairs = pairs[:, 0] + pairs[:, 1]
    vv, vc, vs, ff, vf, fs, vt, ft = (pairs[:, 0, j : j + 1] for j in range(8))

    def mean(x):
        return jnp.sum(x, axis=0, keepdims=True) * (1.0 / count)

    def nearest(vv, vc):
        return vc / jnp.maximum(vv, 1e-30)

    along = mean(vc)
    beta = nearest(vv, vc) - along
    norm_sq = mean(ff + 2.0 * beta * vf + beta * beta * vv)
    unit = lax.rsqrt(jnp.maximum(norm_sq, 0.0) + EPS)
    v_s1 = unit * mean(vt + beta * vs)
    u_s0 = unit * mean(fs + beta * vs)
    u_s1 = unit * unit * mean(ft + beta * (vt + fs) + beta * beta * vs)
    cv, cu, energy = ritz_pair(theta, 0.5 * (v_s1 + u_s0), u_s1)
    energy_out[0] = jnp.max(energy)
    cu = cu * unit
    mine = pl.ds(pl.multiple_of(own_op * step, step), step)
    for e in range(0, n_op, 2):
        there = own_blk * n_op + (own_op ^ e)
        pair = parts2[there] + parts2[own_blk * n_op + (own_op ^ e ^ 1)]
        on_vec = cv + cu * (nearest(pair[:, 0:1], pair[:, 1:2]) - along)
        for h in range(2):
            at = pl.multiple_of((own_op ^ e ^ h) * cols, LANES)
            part, crossed = slice(h * cols, (h + 1) * cols), slice((1 - h) * cols, (2 - h) * cols)
            for d in range(n_blk):
                dmat = diag[d, mine] + right_diag[:, pl.ds(at, cols)]
                if e:
                    raw, fld = got1[e - 2][0, d, :, part], got2[e - 1][0, d, :, part]
                    vec = raw.astype(jnp.float32) * scale
                    sigma = got1[e - 2][1, d, :, part].astype(jnp.float32)
                    sigma = sigma + got1[e - 1][0, d, :, crossed].astype(jnp.float32)
                    sigma = sigma * scale + dmat * vec
                    image = got2[e - 1][1, d, :, part].astype(jnp.float32)
                else:
                    raw, sigma, fld, image = (own[j, d, :, part].astype(jnp.float32) for j in range(4))
                    vec = raw * scale
                fld = fld.astype(jnp.float32)
                image = image + got2[e][0, d, :, crossed].astype(jnp.float32) + dmat * fld
                newvec = on_vec * vec + cu * fld
                res = on_vec * sigma + cu * image - energy * newvec
                new_out[slots[d], :, pl.ds(at, cols)] = newvec.astype(jnp.bfloat16)
                res_out[slots[d], :, pl.ds(at, cols)] = res.astype(jnp.bfloat16)


def per_device(
    psi, left_ops, right_ops, term_shift, slot_sector, sector_width, diag_left, diag_right
):
    n_blk, n_op = lax.axis_size("blk"), lax.axis_size("op")
    _, rows, ncols = psi.shape
    terms, _, width, _ = right_ops.shape
    n_pair = n_op // 2
    cols = diag_right.shape[0] // n_op
    step = rows // n_op
    count = float(n_blk * rows * ncols)
    n_dev = n_blk * n_op
    bf16, f32, i32 = jnp.bfloat16, jnp.float32, jnp.int32
    last = sorted(range(1, n_blk), key=lambda d: min(d, n_blk - d))[-1]

    def pack():
        first = swap(term_shift, 1, n_op)
        sent = kernel(
            functools.partial(pack_body, n_blk, n_op),
            [(term_shift, SMEM), (first, SMEM), (psi, HBM), (right_ops, HBM)],
            [((rows, 2 * cols if d in (0, last) else cols), bf16, VMEM) for d in range(n_blk)]
            + [((terms * width + 16, 2 * cols), bf16, VMEM)] * n_pair,
            [pltpu.VMEM(right_ops.shape, bf16), pltpu.SemaphoreType.DMA((2 * n_blk + 1,))],
            nbytes=1 << 20,
        )
        return sent[:n_blk], sent[n_blk:]

    def table(right):
        return kernel(
            functools.partial(table_body, n_blk, terms),
            [(slot_sector, SMEM), (sector_width, SMEM), (diag_left, VMEM), (diag_right[None], VMEM)]
            + [(block, VMEM) for block in right],
            [((n_blk * n_pair * terms,), i32, SMEM)]
            + [((n_blk,), i32, SMEM)] * 2
            + [((n_blk, rows, LANES), f32, VMEM), ((1, n_op * cols), f32, VMEM)],
        )

    def inputs(left, psi, those):
        blocks = [left[d, 2 * e] for d in those for e in range(n_pair)]
        halves = [half for d in those for half in psi[d]]
        return [(x, VMEM) for x in blocks], [(x, VMEM) for x in halves], [len(psi[d]) for d in those]

    def early(left, psi, n_early, tables):
        left_ins, psi_ins, counts = inputs(left, psi, range(n_early))
        return kernel(
            functools.partial(early_body, n_pair, counts),
            [(tables[1], SMEM)] + left_ins + psi_ins,
            [
                ((n_early, rows, 2 * cols), bf16, VMEM),
                ((n_early, n_pair * terms, rows, 2 * cols), bf16, VMEM),
                ((n_early, n_pair, terms, rows, rows), bf16, HBM),
            ],
            [pltpu.SemaphoreType.DMA((n_early * n_pair,))],
            flops=2 * n_early * rows * rows * 2 * cols * terms * n_pair,
            nbytes=4 << 20,
        )

    left, psi_by, right, (src, widths, slots, *both), (raw_early, inter_early, left_early) = gather(
        left_ops[:, 0], n_blk, n_op, pack, table, early
    )
    n_early = raw_early.shape[0]
    n_late = n_blk - n_early
    left_ins, psi_ins, counts = inputs(left, psi_by, range(n_early, n_blk))
    right_ins = [(block, VMEM) for block in right]
    diags = [(x, VMEM) for x in both]

    tables = [(src, SMEM), (widths, SMEM)]
    narrow = ((n_blk, rows, 2 * cols), bf16, VMEM)
    dots = ((n_dev, 1, LANES), f32, VMEM)
    sends = [((2 - e % 2, n_blk, step, 2 * cols), bf16, VMEM) for e in range(1, n_op)]
    inter = pltpu.VMEM((n_blk + 1, n_pair * terms, rows, 2 * cols), bf16)
    left_late = (n_late, n_pair, terms, rows, rows)
    cost = dict(flops=2 * n_blk * rows * 2 * cols * terms * n_pair * (rows + 2 * cols), nbytes=6 << 20)

    def totals(parts):
        return lax.all_to_all(parts, ("blk", "op"), 0, 0, tiled=True)

    part1, raw, kept, dots1, *out1 = kernel(
        functools.partial(first_body, n_blk, n_pair, counts),
        tables + left_ins + right_ins + psi_ins + [(raw_early, VMEM), (inter_early, VMEM)] + diags,
        [narrow, narrow, (left_late, bf16, HBM), dots] + sends[1:],
        [inter, pltpu.SemaphoreType.DMA((n_late * n_pair + 2,))],
        **cost,
    )
    parts1, other1 = lax.optimization_barrier((totals(dots1), swap(part1, 1, n_op)))
    got1 = [swap(block, e, n_op) for e, block in enumerate(out1, 2)]
    dots2, own, *out2 = kernel(
        functools.partial(second_body, n_blk, n_pair, count),
        tables + [(left_early, HBM), (kept, HBM)] + right_ins
        + [(x, VMEM) for x in (parts1, raw, part1, other1)] + diags,
        [dots, ((4, n_blk, step, 2 * cols), bf16, VMEM)] + sends,
        [
            inter,
            pltpu.VMEM((n_blk, rows, 2 * cols), f32),
            pltpu.VMEM((n_blk, rows, 2 * cols), f32),
            pltpu.VMEM((n_blk, rows, 2 * cols), bf16),
            pltpu.VMEM((n_blk, rows, 2 * cols), bf16),
            pltpu.VMEM((n_blk, *left_late[1:]), bf16),
            pltpu.SemaphoreType.DMA((n_blk,)),
        ],
        flops=4 * cost["flops"],
        nbytes=24 << 20,
    )
    dots2, got1 = lax.optimization_barrier((dots2, got1))
    parts2 = totals(dots2)
    got2 = [swap(block, e, n_op) for e, block in enumerate(out2, 1)]
    final = ((n_blk, step, n_op * cols), bf16, VMEM)
    new, res, energy = kernel(
        functools.partial(third_body, n_blk, n_op, count),
        [(slots, SMEM)] + [(x, VMEM) for x in (parts1, parts2)] + diags
        + [(x, VMEM) for x in (own, *got1, *got2)],
        [final, final, ((1,), f32, SMEM)],
        nbytes=4 << 20,
    )
    return new, res, energy


def solution(mesh):
    placed = (
        P(("grp", "blk"), None, None),
        P("op", ("grp", "blk"), None, None),
        P("op", ("grp", "blk"), None, None),
        P("op"),
        P("grp"),
        P("grp"),
        P("grp", None),
        P(("grp", "blk")),
    )

    def body(*args):
        psi, left_ops, right_ops, diag_right = args[0], args[1], args[2], args[7]
        n_op = mesh.shape["op"]
        cols = diag_right.shape[0] // n_op
        fits = (
            psi.shape[0] == 1
            and diag_right.shape[0] % n_op == 0
            and cols == LANES
            and n_op % 2 == 0
            and cols % right_ops.shape[2] == 0
            and cols // right_ops.shape[2] * n_op == right_ops.shape[1]
            and psi.shape[1] % (16 * n_op) == 0
            and n_op & (n_op - 1) == 0
            and mesh.shape["blk"] > n_op.bit_length() - 1
        )
        return (per_device if fits else per_device_general)(*args)

    return jax.shard_map(
        body,
        mesh=mesh,
        in_specs=placed,
        out_specs=(P("grp", "op", "blk"), P("grp", "op", "blk"), P("grp")),
        check_vma=False,
    )
```

```python
import functools

import jax
import jax.numpy as jnp
from jax import lax
from jax.experimental import pallas as pl
from jax.experimental.pallas import tpu as pltpu
from jax.sharding import PartitionSpec as P

EPS = 1e-06
LANES = 128
VMEM_LIMIT = 20 * 1024 * 1024


def per_device_general(
    psi, left_ops, right_ops, term_shift, slot_sector, sector_width, diag_left, diag_right
):
    sec_dev, rows, ncols = psi.shape
    nsec = slot_sector.shape[0]
    terms_dev = left_ops.shape[0]
    right_local = right_ops.shape[1]
    right_width = right_ops.shape[2]
    local_cols = diag_right.shape[0]
    count = float(nsec * rows * ncols)
    match = slot_sector[:, None] == jnp.arange(nsec)[None, :]
    widths = jnp.sum(jnp.where(match, sector_width[None, :], 0), axis=1)
    mask_all = (jnp.arange(rows)[None, :] < widths[:, None]).astype(jnp.float32)
    own_mask = lax.dynamic_slice_in_dim(mask_all, lax.axis_index("blk") * sec_dev, sec_dev, 0)
    raw = psi.astype(jnp.float32) * own_mask[:, :, None]
    squares = lax.psum(jnp.sum(raw * raw), "blk")
    v_left = (raw * lax.rsqrt(squares / count + EPS)).astype(jnp.bfloat16)
    onehots = (
        slot_sector[None, None, :] == slot_sector[None, :, None] - term_shift[:, None, None]
    ).astype(jnp.bfloat16)
    op_rows = rows // lax.axis_size("op")
    op_start = lax.axis_index("op") * op_rows
    dmat = diag_left[:, :, None] + diag_right[None, None, :]

    def left_local(field):
        return jnp.einsum(
            "ksij,sjc->ksic", left_ops, field, preferred_element_type=jnp.float32
        ).astype(jnp.bfloat16)

    def right_part(moved_in):
        flat = moved_in.reshape(terms_dev, nsec, rows * local_cols)
        shifted = jnp.einsum(
            "kts,ksx->ktx", onehots, flat, preferred_element_type=jnp.float32
        ).astype(jnp.bfloat16)
        shifted = shifted.reshape(terms_dev, nsec, rows, right_local, right_width)
        accum = jnp.einsum(
            "ktwrc,krdc->twrd", shifted, right_ops, preferred_element_type=jnp.float32
        )
        return accum.reshape(nsec, rows, local_cols) * mask_all[:, :, None]

    def op_total(partial_value):
        return lax.psum(partial_value.astype(jnp.bfloat16), "op").astype(jnp.float32)

    def final_rows(array):
        return lax.dynamic_slice_in_dim(array, op_start, op_rows, 1)

    def reduce_dots(values):
        sums = lax.psum(values, "blk")
        return tuple((item / count for item in sums))

    moved_first, v_moved = (
        lax.all_to_all(left_local(v_left), "blk", split_axis=3, concat_axis=1, tiled=True),
        lax.all_to_all(v_left[None], "blk", split_axis=3, concat_axis=1, tiled=True),
    )
    v_right = v_moved[0]
    vec32 = v_right.astype(jnp.float32)
    first_sigma = op_total(right_part(moved_first)) + dmat * vec32
    theta = reduce_dots((jnp.sum(vec32 * first_sigma),))[0]
    resid = first_sigma - theta * vec32
    den = dmat - theta
    corr = resid * den / jnp.maximum(den * den, 0.25)
    along = reduce_dots((jnp.sum(vec32 * corr),))[0]
    orth = corr - along * vec32
    norm_sq = reduce_dots((jnp.sum(orth * orth),))[0]
    update = (orth * lax.rsqrt(norm_sq + EPS)).astype(jnp.bfloat16)
    upd32 = update.astype(jnp.float32)
    upd_left = lax.all_to_all(update, "blk", split_axis=0, concat_axis=2, tiled=True)
    moved_second = lax.all_to_all(
        left_local(upd_left), "blk", split_axis=3, concat_axis=1, tiled=True
    )
    second_sigma = op_total(right_part(moved_second)) + dmat * upd32
    v_s1, u_s0, u_s1 = reduce_dots(
        (jnp.sum(vec32 * second_sigma), jnp.sum(upd32 * first_sigma), jnp.sum(upd32 * second_sigma))
    )
    h_mix = 0.5 * (v_s1 + u_s0)
    coef_v, coef_u, energy = ritz(theta, h_mix, u_s1)
    newvec = coef_v * vec32 + coef_u * upd32
    image = coef_v * first_sigma + coef_u * second_sigma
    new_out = final_rows(newvec.astype(jnp.bfloat16))
    res_out = final_rows((image - energy * newvec).astype(jnp.bfloat16))
    return (new_out, res_out, jnp.reshape(energy, (1,)))


def ritz(theta, h_mix, h_two):
    angle = 0.5 * jnp.arctan2(2.0 * h_mix, theta - h_two)
    sine = jnp.sin(angle)
    flip = jnp.where(sine > 0, -1.0, 1.0)
    coef_v = -sine * flip
    coef_u = jnp.cos(angle) * flip
    half = 0.5 * (theta - h_two)
    energy = 0.5 * (theta + h_two) - jnp.sqrt(half * half + h_mix * h_mix)
    return coef_v, coef_u, energy


VMEM, SMEM, HBM = pltpu.VMEM, pltpu.SMEM, pltpu.HBM


def kernel(body, ins, outs, scratch=(), flops=0, nbytes=0):
    return pl.pallas_call(
        body,
        out_shape=[
            HBM(shape, dtype) if space == HBM else jax.ShapeDtypeStruct(shape, dtype)
            for shape, dtype, space in outs
        ],
        in_specs=[pl.BlockSpec(memory_space=space) for _, space in ins],
        out_specs=[pl.BlockSpec(memory_space=space) for _, _, space in outs],
        scratch_shapes=list(scratch),
        compiler_params=pltpu.CompilerParams(vmem_limit_bytes=VMEM_LIMIT),
        cost_estimate=pl.CostEstimate(flops=flops, bytes_accessed=nbytes, transcendentals=0),
    )(*[pltpu.with_memory_space_constraint(x, HBM) if space == HBM else x for x, space in ins])


def ring_at(place, n_blk):
    place = place % n_blk if isinstance(place, int) else lax.rem(place + n_blk, n_blk)
    odd, even = 2 * place - 1, 2 * (n_blk - place)
    if isinstance(place, int):
        return 0 if place == 0 else odd if odd < n_blk else even
    return jnp.where(place == 0, 0, jnp.where(odd < n_blk, odd, even))


def ring_place(index, n_blk):
    odd, even = (index + 1) // 2, lax.rem(n_blk - index // 2, n_blk)
    return jnp.where(lax.rem(index, 2) == 1, odd, even)


def onward(block, d, n_blk):
    pairs = [(ring_at(i, n_blk), ring_at(i + d, n_blk)) for i in range(n_blk)]
    return lax.ppermute(block, "blk", pairs)


def swap(block, e, n_op):
    return lax.ppermute(block, "op", [(i, i ^ e) for i in range(n_op)])


def gather(own, n_blk, n_op, pack, table, early):
    bits = [1 << b for b in reversed(range(1, n_op.bit_length() - 1))]
    order = sorted(range(1, n_blk), key=lambda d: min(d, n_blk - d))
    left, psi, right, tables, columns = {(0, 0): own}, {}, None, None, None
    waiting, late, made = {(0, 0): 0}, None, None
    for j in range(n_blk + len(bits)):
        new, moved = {}, {}
        for (d, e), done in waiting.items():
            if e == 0 and d + 1 < n_blk:
                new[d + 1, 0] = onward(left[d, 0], 1, n_blk), 0
            for b in range(done, len(bits)):
                new[d, e ^ bits[b]] = swap(left[d, e], bits[b], n_op), b + 1
        kept = {key: block for key, (block, _) in new.items()}
        if late is not None:
            moved["psi"] = late
        if j == 0:
            columns, packed = pack()
            moved["right"] = [packed[0]]
            moved["right"] += [swap(part, 2 * e, n_op) for e, part in enumerate(packed[1:], 1)]
        if j == 1:
            moved["tables"] = table(right)
        if j == n_blk - 1 and j >= len(bits) + 1:
            n_early = min(2, n_blk - 1)
            psi[0] = [columns[0]]
            moved["early"] = early(left, psi, n_early, tables)
        if 2 <= j < n_blk:
            moved["other"] = swap(psi[order[j - 2]][0], 1, n_op)
        late = onward(columns[order[j]], order[j], n_blk) if j < n_blk - 1 else None
        if not kept and not moved:
            break
        waiting = {key: done for key, (_, done) in new.items()}
        kept, moved = lax.optimization_barrier((kept, moved))
        left.update(kept)
        right, tables = moved.get("right", right), moved.get("tables", tables)
        made = moved.get("early", made)
        if "psi" in moved:
            psi[order[j - 1]] = [moved["psi"]]
        if "other" in moved:
            psi[order[j - 2]].append(moved["other"])
    return left, psi, right, tables, made


def place_of():
    return lax.axis_index("blk"), lax.axis_index("op")


def pack_body(n_blk, n_op, shift, _, psi, right_in, *outs):
    n_pair = n_op // 2
    psi_out, right_out, right, sems = outs[:n_blk], outs[n_blk : n_blk + n_pair], outs[-2], outs[-1]
    terms, local, width, _ = right.shape
    cols = local * width // n_op
    per = cols // width
    own_blk, own_op = place_of()
    fetch = pltpu.make_async_copy(right_in, right, sems.at[2 * n_blk])
    fetch.start()
    copies = []
    for d in range(n_blk):
        there = ring_at(ring_place(own_blk, n_blk) + d, n_blk) * n_op
        for h in range(psi_out[d].shape[1] // cols):
            start = pl.multiple_of((there + (own_op ^ h)) * cols, LANES)
            copy = pltpu.make_async_copy(
                psi.at[0, :, pl.ds(start, cols)],
                psi_out[d].at[:, h * cols : (h + 1) * cols],
                sems.at[2 * d + h],
            )
            copy.start()
            copies.append(copy)
    lane = lax.broadcasted_iota(jnp.int32, (16, 2 * cols), 1)
    line = jnp.zeros((16, 2 * cols), jnp.float32)
    for k in range(terms):
        line = jnp.where(lane == k, shift[k].astype(jnp.float32), line)
    square = [lax.broadcasted_iota(jnp.int32, (width, width), axis) for axis in (0, 1)]
    unit = (square[0] == square[1]).astype(jnp.bfloat16)
    fetch.wait()
    for e in range(n_pair):
        for k in range(terms):
            turned = []
            for h in range(2):
                first = (own_op ^ (2 * e) ^ h) * per
                for r in range(per):
                    turned.append(
                        lax.dot_general(
                            right[k, first + r], unit, (((0,), (0,)), ((), ())),
                            preferred_element_type=jnp.float32,
                        )
                    )
            side_by_side = jnp.concatenate(turned, axis=1).astype(jnp.bfloat16)
            right_out[e][k * width : (k + 1) * width] = side_by_side
        right_out[e][terms * width :] = line.astype(jnp.bfloat16)
    for copy in copies:
        copy.wait()


def table_body(n_blk, terms, sector, width, left_diag, right_diag, *refs):
    tails, src, widths, slots, diag, right_out = refs[:-5], *refs[-5:]
    right_out[...] = right_diag[...]
    n_pair = len(tails)
    rows, cols = tails[0].shape
    own_blk, _ = place_of()
    lane = lax.broadcasted_iota(jnp.int32, (16, cols), 1)
    for d in range(n_blk):
        slot = ring_at(ring_place(own_blk, n_blk) - d, n_blk)
        slots[d] = slot
        widths[d] = width[sector[slot]]
    for e in range(n_pair):
        tail = tails[e][rows - 16 :].astype(jnp.float32)
        for k in range(terms):
            shift = jnp.max(jnp.where(lane == k, tail, -1e9)).astype(jnp.int32)
            for t in range(n_blk):
                want = sector[slots[t]] - shift
                found = jnp.int32(n_blk)
                for d in range(n_blk):
                    found = jnp.where(sector[slots[d]] == want, d, found)
                src[(t * n_pair + e) * terms + k] = found
    for d in range(n_blk):
        row = left_diag[pl.ds(slots[d], 1), :]
        diag[d] = jnp.transpose(jnp.broadcast_to(row, (diag.shape[2], row.shape[1])))


def diagonal(diag, right_diag, d, h):
    cols = diag.shape[2]
    _, own_op = place_of()
    start = pl.multiple_of((own_op ^ h) * cols, LANES)
    return diag[d] + right_diag[:, pl.ds(start, cols)]


def row_mask(width, shape):
    return lax.broadcasted_iota(jnp.int32, shape, 0) < width


def fold(x):
    return jnp.sum(x.reshape(-1, 8, x.shape[-1]), axis=0)


def whole(x):
    return jnp.sum(jnp.sum(x, axis=0, keepdims=True), axis=1, keepdims=True)


def spread(values, out):
    lane = lax.broadcasted_iota(jnp.int32, out.shape[1:], 1)
    row = jnp.zeros(out.shape[1:], jnp.float32)
    for j, value in enumerate(values):
        row = jnp.where(lane == j, value, row)
    for d in range(out.shape[0]):
        out[d] = row


def by_block(packed, terms, k):
    rows, cols = packed.shape
    width = (rows - 16) // terms
    lane = lax.broadcasted_iota(jnp.int32, (width, cols), 1)
    block = packed[k * width : (k + 1) * width].astype(jnp.float32)
    parts = []
    for r in range(cols // width):
        inside = (lane >= r * width) & (lane < (r + 1) * width)
        parts.append(jnp.where(inside, block, 0.0).astype(jnp.bfloat16))
    return jnp.concatenate(parts, axis=0)


def left_products(block, left, inter):
    n_terms, rows, cols = inter.shape
    at = 0
    while at < n_terms:
        ops = left(at)
        terms = ops.shape[0]
        prod = jnp.dot(ops.reshape(terms * rows, rows), block, preferred_element_type=jnp.float32)
        inter[at : at + terms] = prod.astype(jnp.bfloat16).reshape(terms, rows, cols)
        at += terms


def sum_terms(src, widths, inter, right, out, emit):
    n_blk, n_terms, _, _ = inter.shape
    n_blk -= 1
    terms = n_terms // len(right)
    turned = [by_block(right[j // terms], terms, j % terms) for j in range(n_terms)]
    for t in range(n_blk):
        total = None
        for j in range(n_terms):
            part = jnp.dot(
                inter[src[t * n_terms + j], j], turned[j], preferred_element_type=jnp.float32
            )
            total = part if total is None else total + part
        total = jnp.where(row_mask(widths[t], total.shape), total, 0.0)
        out[t] = total.astype(jnp.bfloat16)
        emit(t, total)


def keep(left, left_out, sems):
    copies = []
    for d, line in enumerate(left):
        for e, ref in enumerate(line):
            copies.append(pltpu.make_async_copy(ref, left_out.at[d, e], sems.at[d * len(line) + e]))
            copies[-1].start()
    return copies


def masked(psi, width, out):
    at = 0
    for ref in psi:
        block = ref[...].astype(jnp.float32)
        block = jnp.where(row_mask(width, block.shape), block, 0.0)
        out[:, at : at + block.shape[1]] = block.astype(jnp.bfloat16)
        at += block.shape[1]


def take(refs, counts):
    out = []
    for count in counts:
        out.append(refs[:count])
        refs = refs[count:]
    return out, refs


def products_of(psi, left, widths, first, raw_out, inter):
    for d, line in enumerate(left):
        masked(psi[d], widths[first + d], raw_out.at[d])
        terms = line[0].shape[0]
        left_products(raw_out[d], lambda at: line[at // terms][...], inter.at[d])


def early_body(n_pair, counts, widths, *refs):
    left, refs = take(refs, [n_pair] * len(counts))
    psi, (raw_out, inter_out, left_out, sems) = take(refs, counts)
    copies = keep(left, left_out, sems)
    products_of(psi, left, widths, 0, raw_out, inter_out)
    for copy in copies:
        copy.wait()


def first_body(n_blk, n_pair, counts, src, widths, *refs):
    n_late = len(counts)
    n_early = n_blk - n_late
    left, refs = take(refs, [n_pair] * n_late)
    (right,), refs = take(refs, [n_pair])
    psi, refs = take(refs, counts)
    raw_in, inter_in, diag, right_diag, part_out, raw_out, left_out, dots_out, inter, sems = refs
    copies = keep(left, left_out, sems)
    for j, (given, own) in enumerate(((inter_in, inter), (raw_in, raw_out))):
        copies.append(
            pltpu.make_async_copy(given, own.at[:n_early], sems.at[n_late * n_pair + j])
        )
        copies[-1].start()
    inter[n_blk] = jnp.zeros_like(inter[n_blk])
    products_of(
        psi, left, widths, n_early, raw_out.at[n_early:], inter.at[n_early:n_blk]
    )
    for copy in copies:
        copy.wait()
    cols = diag.shape[2]
    zero = jnp.zeros((8, cols), jnp.float32)
    sums = [zero, zero]

    def emit(d, total):
        for h in range(2):
            part = slice(h * cols, (h + 1) * cols)
            raw = raw_out[d, :, part].astype(jnp.float32)
            image = total[:, part]
            if h == 0:
                image = image + diagonal(diag, right_diag, d, h) * raw
                sums[0] = sums[0] + fold(raw * raw)
            sums[1] = sums[1] + fold(raw * image)

    sum_terms(src, widths, inter, right, part_out, emit)
    spread([whole(x) for x in sums], dots_out)


def send_rows(e, send, d, *refs):
    _, own_op = place_of()
    step = send.shape[2]
    rows = pl.ds(pl.multiple_of((own_op ^ e) * step, step), step)
    for j, ref in enumerate(refs):
        send[j, d] = ref[d, rows].astype(send.dtype)


def total_of(mine, other, d, h, cols):
    own = mine[d, :, h * cols : (h + 1) * cols].astype(jnp.float32)
    return own + other[d, :, (1 - h) * cols : (2 - h) * cols].astype(jnp.float32)


def sigma_body(mine, other, raw_in, diag, right_diag, sig_out, *sends):
    n_blk, _, cols = diag.shape
    for d in range(n_blk):
        for h in range(2):
            part = slice(h * cols, (h + 1) * cols)
            raw = raw_in[d, :, part].astype(jnp.float32)
            sigma = total_of(mine, other, d, h, cols) + diagonal(diag, right_diag, d, h) * raw
            sig_out[d, :, part] = sigma
        for e, send in enumerate(sends, 1):
            send_rows(2 * e, send, d, raw_in, sig_out)


def norm_theta(parts, count):
    tot = jnp.sum(parts, axis=0) * (1.0 / count)
    scale = lax.rsqrt(tot[:, 0:1] + EPS)
    return scale, tot[:, 1:2] * scale * scale


def second_body(n_blk, n_pair, count, src, widths, left_early, left_late, *refs):
    right, refs = refs[:n_pair], refs[n_pair:]
    parts, raw_in, sig, diag, right_diag, dots_out, own_out = refs[:7]
    sends, (inter, corr, fld, part_out, held, sems) = refs[7:-6], refs[-6:]
    copies = []
    n_early = left_early.shape[0]
    for d in range(n_blk):
        kept = left_early.at[d] if d < n_early else left_late.at[d - n_early]
        copies.append(pltpu.make_async_copy(kept, held.at[d], sems.at[d]))
        copies[-1].start()
    inter[n_blk] = jnp.zeros_like(inter[n_blk])
    scale, theta = norm_theta(parts[...], count)
    cols = diag.shape[2]
    halves = []
    for h in range(2):
        part = slice(h * cols, (h + 1) * cols)
        vv = vc = vs = jnp.zeros((8, cols), jnp.float32)
        for d in range(n_blk):
            vec = raw_in[d, :, part].astype(jnp.float32) * scale
            sigma = sig[d, :, part] * scale
            den = diagonal(diag, right_diag, d, h) - theta
            item = (sigma - theta * vec) * den / jnp.maximum(den * den, 0.25)
            corr[d, :, part] = item
            vv, vc = vv + fold(vec * vec), vc + fold(vec * item)
            if h == 0:
                vs = vs + fold(vec * sigma)
        halves.append((whole(vv), whole(vc), vs))
    along = (halves[0][1] + halves[1][1]) / jnp.maximum(halves[0][0] + halves[1][0], 1e-30)
    terms = held.shape[2]
    for copy in copies:
        copy.wait()
    for d in range(n_blk):
        for h in range(2):
            part = slice(h * cols, (h + 1) * cols)
            vec = raw_in[d, :, part].astype(jnp.float32) * scale
            fld[d, :, part] = (corr[d, :, part] - along * vec).astype(jnp.bfloat16)
        left_products(fld[d], lambda at: held[d, at // terms], inter.at[d])
    zero = jnp.zeros((8, cols), jnp.float32)
    sums = [zero for _ in range(5)]

    def emit(d, total):
        for h in range(2):
            part = slice(h * cols, (h + 1) * cols)
            field = fld[d, :, part].astype(jnp.float32)
            raw = raw_in[d, :, part].astype(jnp.float32)
            image = total[:, part]
            if h == 0:
                image = image + diagonal(diag, right_diag, d, h) * field
                for j, prod in enumerate((field * field, raw * field, field * sig[d, :, part])):
                    sums[j] = sums[j] + fold(prod)
            sums[3] = sums[3] + fold(raw * image)
            sums[4] = sums[4] + fold(field * image)
        for e, send in enumerate(sends, 1):
            send_rows(e, send, d, *((part_out,) if e % 2 else (fld, part_out)))
        rows = pl.ds(pl.multiple_of(own_op * step, step), step)
        for j, ref in enumerate((raw_in, sig, fld, part_out)):
            own_out[j, d] = ref[d, rows].astype(own_out.dtype)

    _, own_op = place_of()
    step = own_out.shape[2]
    sum_terms(src, widths, inter, right, part_out, emit)
    vv, vc, vs = halves[0]
    ff, vf, fs, vt, ft = (whole(x) for x in sums)
    spread([vv, vc, whole(vs), ff, vf * scale, fs * scale, vt * scale, ft], dots_out)


def ritz_pair(theta, h_mix, h_two):
    diff, twice = theta - h_two, 2.0 * h_mix
    size = jnp.sqrt(diff * diff + twice * twice)
    some = size > 0.0
    safe = jnp.where(some, size, 1.0)
    big = jnp.sqrt(0.5 + 0.5 * jnp.abs(diff) / safe)
    small = 0.5 * jnp.abs(twice) / (safe * big)
    sine = jnp.where(diff >= 0.0, small, big)
    cosine = jnp.where(diff >= 0.0, big, small)
    sine = jnp.where(some, sine, 0.0)
    cosine = jnp.where(some, cosine, 1.0)
    upward = (twice > 0.0) | ((twice == 0.0) & (diff < 0.0))
    return sine, jnp.where(upward, -cosine, cosine), 0.5 * (theta + h_two) - 0.5 * size


def third_body(n_blk, n_op, count, slots, parts1, parts2, diag, right_diag, own, *refs):
    n_far = n_op // 2 - 1
    got1, got2 = refs[:n_far], refs[n_far : n_far + n_op - 1]
    new_out, res_out, energy_out = refs[n_far + n_op - 1 :]
    step, cols = new_out.shape[1], new_out.shape[2] // n_op
    own_blk, own_op = place_of()
    scale, theta = norm_theta(parts1[...], count)
    pairs = parts2[...].reshape(n_blk * n_op // 2, 2, *parts2.shape[1:])
    pairs = pairs[:, 0] + pairs[:, 1]
    vv, vc, vs, ff, vf, fs, vt, ft = (pairs[:, 0, j : j + 1] for j in range(8))

    def mean(x):
        return jnp.sum(x, axis=0, keepdims=True) * (1.0 / count)

    def nearest(vv, vc):
        return vc / jnp.maximum(vv, 1e-30)

    along = mean(vc)
    beta = nearest(vv, vc) - along
    norm_sq = mean(ff + 2.0 * beta * vf + beta * beta * vv)
    unit = lax.rsqrt(jnp.maximum(norm_sq, 0.0) + EPS)
    v_s1 = unit * mean(vt + beta * vs)
    u_s0 = unit * mean(fs + beta * vs)
    u_s1 = unit * unit * mean(ft + beta * (vt + fs) + beta * beta * vs)
    cv, cu, energy = ritz_pair(theta, 0.5 * (v_s1 + u_s0), u_s1)
    energy_out[0] = jnp.max(energy)
    cu = cu * unit
    mine = pl.ds(pl.multiple_of(own_op * step, step), step)
    for e in range(0, n_op, 2):
        there = own_blk * n_op + (own_op ^ e)
        pair = parts2[there] + parts2[own_blk * n_op + (own_op ^ e ^ 1)]
        on_vec = cv + cu * (nearest(pair[:, 0:1], pair[:, 1:2]) - along)
        for h in range(2):
            at = pl.multiple_of((own_op ^ e ^ h) * cols, LANES)
            part, crossed = slice(h * cols, (h + 1) * cols), slice((1 - h) * cols, (2 - h) * cols)
            for d in range(n_blk):
                dmat = diag[d, mine] + right_diag[:, pl.ds(at, cols)]
                blocks = [own.at[j] for j in range(4)]
                if e:
                    far, near = got1[e // 2 - 1], got2[e - 1]
                    blocks = far.at[0], far.at[1], near.at[0], near.at[1]
                raw, sigma, fld, image = (x[d, :, part].astype(jnp.float32) for x in blocks)
                vec, sigma = raw * scale, sigma * scale
                image = image + got2[e][0, d, :, crossed].astype(jnp.float32) + dmat * fld
                newvec = on_vec * vec + cu * fld
                res = on_vec * sigma + cu * image - energy * newvec
                new_out[slots[d], :, pl.ds(at, cols)] = newvec.astype(jnp.bfloat16)
                res_out[slots[d], :, pl.ds(at, cols)] = res.astype(jnp.bfloat16)


def per_device(
    psi, left_ops, right_ops, term_shift, slot_sector, sector_width, diag_left, diag_right
):
    n_blk, n_op = lax.axis_size("blk"), lax.axis_size("op")
    _, rows, ncols = psi.shape
    terms, _, width, _ = right_ops.shape
    n_pair = n_op // 2
    cols = diag_right.shape[0] // n_op
    step = rows // n_op
    count = float(n_blk * rows * ncols)
    n_dev = n_blk * n_op
    bf16, f32, i32 = jnp.bfloat16, jnp.float32, jnp.int32
    last = sorted(range(1, n_blk), key=lambda d: min(d, n_blk - d))[-1]

    def pack():
        first = swap(term_shift, 1, n_op)
        sent = kernel(
            functools.partial(pack_body, n_blk, n_op),
            [(term_shift, SMEM), (first, SMEM), (psi, HBM), (right_ops, HBM)],
            [((rows, 2 * cols if d in (0, last) else cols), bf16, VMEM) for d in range(n_blk)]
            + [((terms * width + 16, 2 * cols), bf16, VMEM)] * n_pair,
            [pltpu.VMEM(right_ops.shape, bf16), pltpu.SemaphoreType.DMA((2 * n_blk + 1,))],
            nbytes=1 << 20,
        )
        return sent[:n_blk], sent[n_blk:]

    def table(right):
        return kernel(
            functools.partial(table_body, n_blk, terms),
            [(slot_sector, SMEM), (sector_width, SMEM), (diag_left, VMEM), (diag_right[None], VMEM)]
            + [(block, VMEM) for block in right],
            [((n_blk * n_pair * terms,), i32, SMEM)]
            + [((n_blk,), i32, SMEM)] * 2
            + [((n_blk, rows, LANES), f32, VMEM), ((1, n_op * cols), f32, VMEM)],
        )

    def inputs(left, psi, those):
        blocks = [left[d, 2 * e] for d in those for e in range(n_pair)]
        halves = [half for d in those for half in psi[d]]
        return [(x, VMEM) for x in blocks], [(x, VMEM) for x in halves], [len(psi[d]) for d in those]

    def early(left, psi, n_early, tables):
        left_ins, psi_ins, counts = inputs(left, psi, range(n_early))
        return kernel(
            functools.partial(early_body, n_pair, counts),
            [(tables[1], SMEM)] + left_ins + psi_ins,
            [
                ((n_early, rows, 2 * cols), bf16, VMEM),
                ((n_early, n_pair * terms, rows, 2 * cols), bf16, VMEM),
                ((n_early, n_pair, terms, rows, rows), bf16, HBM),
            ],
            [pltpu.SemaphoreType.DMA((n_early * n_pair,))],
            flops=2 * n_early * rows * rows * 2 * cols * terms * n_pair,
            nbytes=4 << 20,
        )

    left, psi_by, right, (src, widths, slots, *both), (raw_early, inter_early, left_early) = gather(
        left_ops[:, 0], n_blk, n_op, pack, table, early
    )
    n_early = raw_early.shape[0]
    n_late = n_blk - n_early
    left_ins, psi_ins, counts = inputs(left, psi_by, range(n_early, n_blk))
    right_ins = [(block, VMEM) for block in right]
    diags = [(x, VMEM) for x in both]

    tables = [(src, SMEM), (widths, SMEM)]
    narrow = ((n_blk, rows, 2 * cols), bf16, VMEM)
    dots = ((n_dev, 1, LANES), f32, VMEM)
    wide = ((n_blk, rows, 2 * cols), f32, VMEM)
    sends = [((2 - e % 2, n_blk, step, 2 * cols), bf16, VMEM) for e in range(1, n_op)]
    inter = pltpu.VMEM((n_blk + 1, n_pair * terms, rows, 2 * cols), bf16)
    left_late = (n_late, n_pair, terms, rows, rows)
    cost = dict(flops=2 * n_blk * rows * 2 * cols * terms * n_pair * (rows + 2 * cols), nbytes=6 << 20)

    def totals(parts):
        return lax.all_to_all(parts, ("blk", "op"), 0, 0, tiled=True)

    part1, raw, kept, dots1 = kernel(
        functools.partial(first_body, n_blk, n_pair, counts),
        tables + left_ins + right_ins + psi_ins + [(raw_early, VMEM), (inter_early, VMEM)] + diags,
        [narrow, narrow, (left_late, bf16, HBM), dots],
        [inter, pltpu.SemaphoreType.DMA((n_late * n_pair + 2,))],
        **cost,
    )
    parts1 = totals(dots1)
    sig, *out1 = kernel(
        sigma_body,
        [(x, VMEM) for x in (part1, swap(part1, 1, n_op), raw)] + diags,
        [wide] + sends[1::2],
        nbytes=4 << 20,
    )
    got1 = [swap(block, 2 * e, n_op) for e, block in enumerate(out1, 1)]
    dots2, own, *out2 = kernel(
        functools.partial(second_body, n_blk, n_pair, count),
        tables + [(left_early, HBM), (kept, HBM)] + right_ins
        + [(x, VMEM) for x in (parts1, raw, sig)] + diags,
        [dots, ((4, n_blk, step, 2 * cols), bf16, VMEM)] + sends,
        [
            inter,
            pltpu.VMEM((n_blk, rows, 2 * cols), f32),
            pltpu.VMEM((n_blk, rows, 2 * cols), bf16),
            pltpu.VMEM((n_blk, rows, 2 * cols), bf16),
            pltpu.VMEM((n_blk, *left_late[1:]), bf16),
            pltpu.SemaphoreType.DMA((n_blk,)),
        ],
        flops=4 * cost["flops"],
        nbytes=24 << 20,
    )
    dots2, out2, got1 = lax.optimization_barrier((dots2, out2, got1))
    parts2 = totals(dots2)
    got2 = [swap(block, e, n_op) for e, block in enumerate(out2, 1)]
    final = ((n_blk, step, n_op * cols), bf16, VMEM)
    new, res, energy = kernel(
        functools.partial(third_body, n_blk, n_op, count),
        [(slots, SMEM)] + [(x, VMEM) for x in (parts1, parts2)] + diags
        + [(x, VMEM) for x in (own, *got1, *got2)],
        [final, final, ((1,), f32, SMEM)],
        nbytes=4 << 20,
    )
    return new, res, energy


def solution(mesh):
    placed = (
        P(("grp", "blk"), None, None),
        P("op", ("grp", "blk"), None, None),
        P("op", ("grp", "blk"), None, None),
        P("op"),
        P("grp"),
        P("grp"),
        P("grp", None),
        P(("grp", "blk")),
    )

    def body(*args):
        psi, left_ops, right_ops, diag_right = args[0], args[1], args[2], args[7]
        n_op = mesh.shape["op"]
        cols = diag_right.shape[0] // n_op
        fits = (
            psi.shape[0] == 1
            and diag_right.shape[0] % n_op == 0
            and cols == LANES
            and n_op % 2 == 0
            and cols % right_ops.shape[2] == 0
            and cols // right_ops.shape[2] * n_op == right_ops.shape[1]
            and psi.shape[1] % (16 * n_op) == 0
            and n_op & (n_op - 1) == 0
            and mesh.shape["blk"] > n_op.bit_length() - 1
        )
        return (per_device if fits else per_device_general)(*args)

    return jax.shard_map(
        body,
        mesh=mesh,
        in_specs=placed,
        out_specs=(P("grp", "op", "blk"), P("grp", "op", "blk"), P("grp")),
        check_vma=False,
    )
```

```python
import functools

import jax
import jax.numpy as jnp
from jax import lax
from jax.experimental import pallas as pl
from jax.experimental.pallas import tpu as pltpu
from jax.sharding import PartitionSpec as P

EPS = 1e-06
LANES = 128
VMEM_LIMIT = 20 * 1024 * 1024


def per_device_general(
    psi, left_ops, right_ops, term_shift, slot_sector, sector_width, diag_left, diag_right
):
    sec_dev, rows, ncols = psi.shape
    nsec = slot_sector.shape[0]
    terms_dev = left_ops.shape[0]
    right_local = right_ops.shape[1]
    right_width = right_ops.shape[2]
    local_cols = diag_right.shape[0]
    count = float(nsec * rows * ncols)
    match = slot_sector[:, None] == jnp.arange(nsec)[None, :]
    widths = jnp.sum(jnp.where(match, sector_width[None, :], 0), axis=1)
    mask_all = (jnp.arange(rows)[None, :] < widths[:, None]).astype(jnp.float32)
    own_mask = lax.dynamic_slice_in_dim(mask_all, lax.axis_index("blk") * sec_dev, sec_dev, 0)
    raw = psi.astype(jnp.float32) * own_mask[:, :, None]
    squares = lax.psum(jnp.sum(raw * raw), "blk")
    v_left = (raw * lax.rsqrt(squares / count + EPS)).astype(jnp.bfloat16)
    onehots = (
        slot_sector[None, None, :] == slot_sector[None, :, None] - term_shift[:, None, None]
    ).astype(jnp.bfloat16)
    op_rows = rows // lax.axis_size("op")
    op_start = lax.axis_index("op") * op_rows
    dmat = diag_left[:, :, None] + diag_right[None, None, :]

    def left_local(field):
        return jnp.einsum(
            "ksij,sjc->ksic", left_ops, field, preferred_element_type=jnp.float32
        ).astype(jnp.bfloat16)

    def right_part(moved_in):
        flat = moved_in.reshape(terms_dev, nsec, rows * local_cols)
        shifted = jnp.einsum(
            "kts,ksx->ktx", onehots, flat, preferred_element_type=jnp.float32
        ).astype(jnp.bfloat16)
        shifted = shifted.reshape(terms_dev, nsec, rows, right_local, right_width)
        accum = jnp.einsum(
            "ktwrc,krdc->twrd", shifted, right_ops, preferred_element_type=jnp.float32
        )
        return accum.reshape(nsec, rows, local_cols) * mask_all[:, :, None]

    def op_total(partial_value):
        return lax.psum(partial_value.astype(jnp.bfloat16), "op").astype(jnp.float32)

    def final_rows(array):
        return lax.dynamic_slice_in_dim(array, op_start, op_rows, 1)

    def reduce_dots(values):
        sums = lax.psum(values, "blk")
        return tuple((item / count for item in sums))

    moved_first, v_moved = (
        lax.all_to_all(left_local(v_left), "blk", split_axis=3, concat_axis=1, tiled=True),
        lax.all_to_all(v_left[None], "blk", split_axis=3, concat_axis=1, tiled=True),
    )
    v_right = v_moved[0]
    vec32 = v_right.astype(jnp.float32)
    first_sigma = op_total(right_part(moved_first)) + dmat * vec32
    theta = reduce_dots((jnp.sum(vec32 * first_sigma),))[0]
    resid = first_sigma - theta * vec32
    den = dmat - theta
    corr = resid * den / jnp.maximum(den * den, 0.25)
    along = reduce_dots((jnp.sum(vec32 * corr),))[0]
    orth = corr - along * vec32
    norm_sq = reduce_dots((jnp.sum(orth * orth),))[0]
    update = (orth * lax.rsqrt(norm_sq + EPS)).astype(jnp.bfloat16)
    upd32 = update.astype(jnp.float32)
    upd_left = lax.all_to_all(update, "blk", split_axis=0, concat_axis=2, tiled=True)
    moved_second = lax.all_to_all(
        left_local(upd_left), "blk", split_axis=3, concat_axis=1, tiled=True
    )
    second_sigma = op_total(right_part(moved_second)) + dmat * upd32
    v_s1, u_s0, u_s1 = reduce_dots(
        (jnp.sum(vec32 * second_sigma), jnp.sum(upd32 * first_sigma), jnp.sum(upd32 * second_sigma))
    )
    h_mix = 0.5 * (v_s1 + u_s0)
    coef_v, coef_u, energy = ritz(theta, h_mix, u_s1)
    newvec = coef_v * vec32 + coef_u * upd32
    image = coef_v * first_sigma + coef_u * second_sigma
    new_out = final_rows(newvec.astype(jnp.bfloat16))
    res_out = final_rows((image - energy * newvec).astype(jnp.bfloat16))
    return (new_out, res_out, jnp.reshape(energy, (1,)))


def ritz(theta, h_mix, h_two):
    angle = 0.5 * jnp.arctan2(2.0 * h_mix, theta - h_two)
    sine = jnp.sin(angle)
    flip = jnp.where(sine > 0, -1.0, 1.0)
    coef_v = -sine * flip
    coef_u = jnp.cos(angle) * flip
    half = 0.5 * (theta - h_two)
    energy = 0.5 * (theta + h_two) - jnp.sqrt(half * half + h_mix * h_mix)
    return coef_v, coef_u, energy


VMEM, SMEM, HBM = pltpu.VMEM, pltpu.SMEM, pltpu.HBM


def kernel(body, ins, outs, scratch=(), flops=0, nbytes=0):
    return pl.pallas_call(
        body,
        out_shape=[
            HBM(shape, dtype) if space == HBM else jax.ShapeDtypeStruct(shape, dtype)
            for shape, dtype, space in outs
        ],
        in_specs=[pl.BlockSpec(memory_space=space) for _, space in ins],
        out_specs=[pl.BlockSpec(memory_space=space) for _, _, space in outs],
        scratch_shapes=list(scratch),
        compiler_params=pltpu.CompilerParams(vmem_limit_bytes=VMEM_LIMIT),
        cost_estimate=pl.CostEstimate(flops=flops, bytes_accessed=nbytes, transcendentals=0),
    )(*[pltpu.with_memory_space_constraint(x, HBM) if space == HBM else x for x, space in ins])


def ring_at(place, n_blk):
    place = place % n_blk if isinstance(place, int) else lax.rem(place + n_blk, n_blk)
    odd, even = 2 * place - 1, 2 * (n_blk - place)
    if isinstance(place, int):
        return 0 if place == 0 else odd if odd < n_blk else even
    return jnp.where(place == 0, 0, jnp.where(odd < n_blk, odd, even))


def ring_place(index, n_blk):
    odd, even = (index + 1) // 2, lax.rem(n_blk - index // 2, n_blk)
    return jnp.where(lax.rem(index, 2) == 1, odd, even)


def onward(block, d, n_blk):
    pairs = [(ring_at(i, n_blk), ring_at(i + d, n_blk)) for i in range(n_blk)]
    return lax.ppermute(block, "blk", pairs)


def swap(block, e, n_op):
    return lax.ppermute(block, "op", [(i, i ^ e) for i in range(n_op)])


def gather(own, n_blk, n_op, pack, table, early):
    bits = [1 << b for b in reversed(range(1, n_op.bit_length() - 1))]
    order = sorted(range(1, n_blk), key=lambda d: min(d, n_blk - d))
    left, psi, right, tables, columns = {(0, 0): own}, {}, None, None, None
    waiting, late, made = {(0, 0): 0}, None, None
    for j in range(n_blk + len(bits)):
        new, moved = {}, {}
        for (d, e), done in waiting.items():
            if e == 0 and d + 1 < n_blk:
                new[d + 1, 0] = onward(left[d, 0], 1, n_blk), 0
            for b in range(done, len(bits)):
                new[d, e ^ bits[b]] = swap(left[d, e], bits[b], n_op), b + 1
        kept = {key: block for key, (block, _) in new.items()}
        if late is not None:
            moved["psi"] = late
        if j == 0:
            columns, packed = pack()
            moved["right"] = [packed[0]]
            moved["right"] += [swap(part, 2 * e, n_op) for e, part in enumerate(packed[1:], 1)]
        if j == 1:
            moved["tables"] = table(right)
        if j == n_blk - 1 and j >= len(bits) + 1:
            n_early = min(2, n_blk - 1)
            psi[0] = [columns[0]]
            moved["early"] = early(left, psi, n_early, tables)
        if 2 <= j < n_blk:
            moved["other"] = swap(psi[order[j - 2]][0], 1, n_op)
        late = onward(columns[order[j]], order[j], n_blk) if j < n_blk - 1 else None
        if not kept and not moved:
            break
        waiting = {key: done for key, (_, done) in new.items()}
        kept, moved = lax.optimization_barrier((kept, moved))
        left.update(kept)
        right, tables = moved.get("right", right), moved.get("tables", tables)
        made = moved.get("early", made)
        if "psi" in moved:
            psi[order[j - 1]] = [moved["psi"]]
        if "other" in moved:
            psi[order[j - 2]].append(moved["other"])
    return left, psi, right, tables, made


def place_of():
    return lax.axis_index("blk"), lax.axis_index("op")


def pack_body(n_blk, n_op, shift, _, psi, right_in, *outs):
    n_pair = n_op // 2
    psi_out, right_out, right, sems = outs[:n_blk], outs[n_blk : n_blk + n_pair], outs[-2], outs[-1]
    terms, local, width, _ = right.shape
    cols = local * width // n_op
    per = cols // width
    own_blk, own_op = place_of()
    fetch = pltpu.make_async_copy(right_in, right, sems.at[2 * n_blk])
    fetch.start()
    copies = []
    for d in range(n_blk):
        there = ring_at(ring_place(own_blk, n_blk) + d, n_blk) * n_op
        for h in range(psi_out[d].shape[1] // cols):
            start = pl.multiple_of((there + (own_op ^ h)) * cols, LANES)
            copy = pltpu.make_async_copy(
                psi.at[0, :, pl.ds(start, cols)],
                psi_out[d].at[:, h * cols : (h + 1) * cols],
                sems.at[2 * d + h],
            )
            copy.start()
            copies.append(copy)
    lane = lax.broadcasted_iota(jnp.int32, (16, 2 * cols), 1)
    line = jnp.zeros((16, 2 * cols), jnp.float32)
    for k in range(terms):
        line = jnp.where(lane == k, shift[k].astype(jnp.float32), line)
    square = [lax.broadcasted_iota(jnp.int32, (width, width), axis) for axis in (0, 1)]
    unit = (square[0] == square[1]).astype(jnp.bfloat16)
    fetch.wait()
    for e in range(n_pair):
        for k in range(terms):
            turned = []
            for h in range(2):
                first = (own_op ^ (2 * e) ^ h) * per
                for r in range(per):
                    turned.append(
                        lax.dot_general(
                            right[k, first + r], unit, (((0,), (0,)), ((), ())),
                            preferred_element_type=jnp.float32,
                        )
                    )
            side_by_side = jnp.concatenate(turned, axis=1).astype(jnp.bfloat16)
            right_out[e][k * width : (k + 1) * width] = side_by_side
        right_out[e][terms * width :] = line.astype(jnp.bfloat16)
    for copy in copies:
        copy.wait()


def table_body(n_blk, terms, sector, width, left_diag, right_diag, *refs):
    tails, src, widths, slots, diag, right_out = refs[:-5], *refs[-5:]
    right_out[...] = right_diag[...]
    n_pair = len(tails)
    rows, cols = tails[0].shape
    own_blk, _ = place_of()
    lane = lax.broadcasted_iota(jnp.int32, (16, cols), 1)
    for d in range(n_blk):
        slot = ring_at(ring_place(own_blk, n_blk) - d, n_blk)
        slots[d] = slot
        widths[d] = width[sector[slot]]
    for e in range(n_pair):
        tail = tails[e][rows - 16 :].astype(jnp.float32)
        for k in range(terms):
            shift = jnp.max(jnp.where(lane == k, tail, -1e9)).astype(jnp.int32)
            for t in range(n_blk):
                want = sector[slots[t]] - shift
                found = jnp.int32(n_blk)
                for d in range(n_blk):
                    found = jnp.where(sector[slots[d]] == want, d, found)
                src[(t * n_pair + e) * terms + k] = found
    for d in range(n_blk):
        row = left_diag[pl.ds(slots[d], 1), :]
        diag[d] = jnp.transpose(jnp.broadcast_to(row, (diag.shape[2], row.shape[1])))


def diagonal(diag, right_diag, d, h):
    cols = diag.shape[2]
    _, own_op = place_of()
    start = pl.multiple_of((own_op ^ h) * cols, LANES)
    return diag[d] + right_diag[:, pl.ds(start, cols)]


def row_mask(width, shape):
    return lax.broadcasted_iota(jnp.int32, shape, 0) < width


def fold(x):
    return jnp.sum(x.reshape(-1, 8, x.shape[-1]), axis=0)


def whole(x):
    return jnp.sum(jnp.sum(x, axis=0, keepdims=True), axis=1, keepdims=True)


def spread(values, out):
    lane = lax.broadcasted_iota(jnp.int32, out.shape[1:], 1)
    row = jnp.zeros(out.shape[1:], jnp.float32)
    for j, value in enumerate(values):
        row = jnp.where(lane == j, value, row)
    for d in range(out.shape[0]):
        out[d] = row


def by_block(packed, terms, k):
    rows, cols = packed.shape
    width = (rows - 16) // terms
    lane = lax.broadcasted_iota(jnp.int32, (width, cols), 1)
    block = packed[k * width : (k + 1) * width].astype(jnp.float32)
    parts = []
    for r in range(cols // width):
        inside = (lane >= r * width) & (lane < (r + 1) * width)
        parts.append(jnp.where(inside, block, 0.0).astype(jnp.bfloat16))
    return jnp.concatenate(parts, axis=0)


def left_products(block, left, inter):
    n_terms, rows, cols = inter.shape
    at = 0
    while at < n_terms:
        ops = left(at)
        terms = ops.shape[0]
        prod = jnp.dot(ops.reshape(terms * rows, rows), block, preferred_element_type=jnp.float32)
        inter[at : at + terms] = prod.astype(jnp.bfloat16).reshape(terms, rows, cols)
        at += terms


def sum_terms(src, widths, inter, right, out, emit):
    n_blk, n_terms, _, _ = inter.shape
    n_blk -= 1
    terms = n_terms // len(right)
    turned = [by_block(right[j // terms], terms, j % terms) for j in range(n_terms)]
    for t in range(n_blk):
        total = None
        for j in range(n_terms):
            part = jnp.dot(
                inter[src[t * n_terms + j], j], turned[j], preferred_element_type=jnp.float32
            )
            total = part if total is None else total + part
        total = jnp.where(row_mask(widths[t], total.shape), total, 0.0)
        out[t] = total.astype(jnp.bfloat16)
        emit(t, total)


def keep(left, left_out, sems):
    copies = []
    for d, line in enumerate(left):
        for e, ref in enumerate(line):
            copies.append(pltpu.make_async_copy(ref, left_out.at[d, e], sems.at[d * len(line) + e]))
            copies[-1].start()
    return copies


def masked(psi, width, out):
    at = 0
    for ref in psi:
        block = ref[...].astype(jnp.float32)
        block = jnp.where(row_mask(width, block.shape), block, 0.0)
        out[:, at : at + block.shape[1]] = block.astype(jnp.bfloat16)
        at += block.shape[1]


def take(refs, counts):
    out = []
    for count in counts:
        out.append(refs[:count])
        refs = refs[count:]
    return out, refs


def products_of(psi, left, widths, first, raw_out, inter):
    for d, line in enumerate(left):
        masked(psi[d], widths[first + d], raw_out.at[d])
        terms = line[0].shape[0]
        left_products(raw_out[d], lambda at: line[at // terms][...], inter.at[d])


def early_body(n_pair, counts, widths, *refs):
    left, refs = take(refs, [n_pair] * len(counts))
    psi, (raw_out, inter_out, left_out, sems) = take(refs, counts)
    copies = keep(left, left_out, sems)
    products_of(psi, left, widths, 0, raw_out, inter_out)
    for copy in copies:
        copy.wait()


def first_body(n_blk, n_pair, counts, src, widths, *refs):
    n_late = len(counts)
    n_early = n_blk - n_late
    left, refs = take(refs, [n_pair] * n_late)
    (right,), refs = take(refs, [n_pair])
    psi, refs = take(refs, counts)
    raw_in, inter_in, diag, right_diag, part_out, raw_out, left_out, dots_out, inter, sems = refs
    copies = keep(left, left_out, sems)
    for j, (given, own) in enumerate(((inter_in, inter), (raw_in, raw_out))):
        copies.append(
            pltpu.make_async_copy(given, own.at[:n_early], sems.at[n_late * n_pair + j])
        )
        copies[-1].start()
    inter[n_blk] = jnp.zeros_like(inter[n_blk])
    products_of(
        psi, left, widths, n_early, raw_out.at[n_early:], inter.at[n_early:n_blk]
    )
    for copy in copies:
        copy.wait()
    cols = diag.shape[2]
    zero = jnp.zeros((8, cols), jnp.float32)
    sums = [zero, zero]

    def emit(d, total):
        for h in range(2):
            part = slice(h * cols, (h + 1) * cols)
            raw = raw_out[d, :, part].astype(jnp.float32)
            image = total[:, part]
            if h == 0:
                image = image + diagonal(diag, right_diag, d, h) * raw
                sums[0] = sums[0] + fold(raw * raw)
            sums[1] = sums[1] + fold(raw * image)

    sum_terms(src, widths, inter, right, part_out, emit)
    spread([whole(x) for x in sums], dots_out)


def send_rows(e, send, d, *refs):
    _, own_op = place_of()
    step = send.shape[2]
    rows = pl.ds(pl.multiple_of((own_op ^ e) * step, step), step)
    for j, ref in enumerate(refs):
        send[j, d] = ref[d, rows].astype(send.dtype)


def total_of(mine, other, d, h, cols):
    own = mine[d, :, h * cols : (h + 1) * cols].astype(jnp.float32)
    return own + other[d, :, (1 - h) * cols : (2 - h) * cols].astype(jnp.float32)


def sigma_body(mine, other, raw_in, diag, right_diag, sig_out, *sends):
    n_blk, _, cols = diag.shape
    for d in range(n_blk):
        for h in range(2):
            part = slice(h * cols, (h + 1) * cols)
            raw = raw_in[d, :, part].astype(jnp.float32)
            sigma = total_of(mine, other, d, h, cols) + diagonal(diag, right_diag, d, h) * raw
            sig_out[d, :, part] = sigma
        for e, send in enumerate(sends, 1):
            send_rows(2 * e, send, d, raw_in, sig_out)


def norm_theta(parts, count):
    tot = jnp.sum(parts, axis=0) * (1.0 / count)
    scale = lax.rsqrt(tot[:, 0:1] + EPS)
    return scale, tot[:, 1:2] * scale * scale


def second_body(n_blk, n_pair, count, src, widths, left_early, left_late, *refs):
    right, refs = refs[:n_pair], refs[n_pair:]
    parts, raw_in, sig, diag, right_diag, dots_out, own_out = refs[:7]
    sends, (inter, corr, fld, part_out, held, sems) = refs[7:-6], refs[-6:]
    copies = []
    n_early = left_early.shape[0]
    for d in range(n_blk):
        kept = left_early.at[d] if d < n_early else left_late.at[d - n_early]
        copies.append(pltpu.make_async_copy(kept, held.at[d], sems.at[d]))
        copies[-1].start()
    inter[n_blk] = jnp.zeros_like(inter[n_blk])
    scale, theta = norm_theta(parts[...], count)
    cols = diag.shape[2]
    halves = []
    for h in range(2):
        part = slice(h * cols, (h + 1) * cols)
        vv = vc = vs = jnp.zeros((8, cols), jnp.float32)
        for d in range(n_blk):
            vec = raw_in[d, :, part].astype(jnp.float32) * scale
            sigma = sig[d, :, part] * scale
            den = diagonal(diag, right_diag, d, h) - theta
            item = (sigma - theta * vec) * den / jnp.maximum(den * den, 0.25)
            corr[d, :, part] = item
            vv, vc = vv + fold(vec * vec), vc + fold(vec * item)
            if h == 0:
                vs = vs + fold(vec * sigma)
        halves.append((whole(vv), whole(vc), vs))
    along = (halves[0][1] + halves[1][1]) / jnp.maximum(halves[0][0] + halves[1][0], 1e-30)
    terms = held.shape[2]
    for copy in copies:
        copy.wait()
    for d in range(n_blk):
        for h in range(2):
            part = slice(h * cols, (h + 1) * cols)
            vec = raw_in[d, :, part].astype(jnp.float32) * scale
            fld[d, :, part] = (corr[d, :, part] - along * vec).astype(jnp.bfloat16)
        left_products(fld[d], lambda at: held[d, at // terms], inter.at[d])
    zero = jnp.zeros((8, cols), jnp.float32)
    sums = [zero for _ in range(5)]

    def emit(d, total):
        for h in range(2):
            part = slice(h * cols, (h + 1) * cols)
            field = fld[d, :, part].astype(jnp.float32)
            raw = raw_in[d, :, part].astype(jnp.float32)
            image = total[:, part]
            if h == 0:
                image = image + diagonal(diag, right_diag, d, h) * field
                for j, prod in enumerate((field * field, raw * field, field * sig[d, :, part])):
                    sums[j] = sums[j] + fold(prod)
            sums[3] = sums[3] + fold(raw * image)
            sums[4] = sums[4] + fold(field * image)
        for e, send in enumerate(sends, 1):
            send_rows(e, send, d, *((part_out,) if e % 2 else (fld, part_out)))
        rows = pl.ds(pl.multiple_of(own_op * step, step), step)
        for j, ref in enumerate((raw_in, sig, fld, part_out)):
            own_out[j, d] = ref[d, rows].astype(own_out.dtype)

    _, own_op = place_of()
    step = own_out.shape[2]
    sum_terms(src, widths, inter, right, part_out, emit)
    vv, vc, vs = halves[0]
    ff, vf, fs, vt, ft = (whole(x) for x in sums)
    spread([vv, vc, whole(vs), ff, vf * scale, fs * scale, vt * scale, ft], dots_out)


def ritz_pair(theta, h_mix, h_two):
    diff, twice = theta - h_two, 2.0 * h_mix
    size = jnp.sqrt(diff * diff + twice * twice)
    some = size > 0.0
    safe = jnp.where(some, size, 1.0)
    big = jnp.sqrt(0.5 + 0.5 * jnp.abs(diff) / safe)
    small = 0.5 * jnp.abs(twice) / (safe * big)
    sine = jnp.where(diff >= 0.0, small, big)
    cosine = jnp.where(diff >= 0.0, big, small)
    sine = jnp.where(some, sine, 0.0)
    cosine = jnp.where(some, cosine, 1.0)
    upward = (twice > 0.0) | ((twice == 0.0) & (diff < 0.0))
    return sine, jnp.where(upward, -cosine, cosine), 0.5 * (theta + h_two) - 0.5 * size


def third_body(n_blk, n_op, count, slots, parts1, parts2, diag, right_diag, own, *refs):
    n_far = n_op // 2 - 1
    got1, got2 = refs[:n_far], refs[n_far : n_far + n_op - 1]
    new_out, res_out, energy_out = refs[n_far + n_op - 1 :]
    step, cols = new_out.shape[1], new_out.shape[2] // n_op
    own_blk, own_op = place_of()
    scale, theta = norm_theta(parts1[...], count)
    pairs = parts2[...].reshape(n_blk * n_op // 2, 2, *parts2.shape[1:])
    pairs = pairs[:, 0] + pairs[:, 1]
    vv, vc, vs, ff, vf, fs, vt, ft = (pairs[:, 0, j : j + 1] for j in range(8))

    def mean(x):
        return jnp.sum(x, axis=0, keepdims=True) * (1.0 / count)

    def nearest(vv, vc):
        return vc / jnp.maximum(vv, 1e-30)

    along = mean(vc)
    beta = nearest(vv, vc) - along
    norm_sq = mean(ff + 2.0 * beta * vf + beta * beta * vv)
    unit = lax.rsqrt(jnp.maximum(norm_sq, 0.0) + EPS)
    v_s1 = unit * mean(vt + beta * vs)
    u_s0 = unit * mean(fs + beta * vs)
    u_s1 = unit * unit * mean(ft + beta * (vt + fs) + beta * beta * vs)
    cv, cu, energy = ritz_pair(theta, 0.5 * (v_s1 + u_s0), u_s1)
    energy_out[0] = jnp.max(energy)
    cu = cu * unit
    mine = pl.ds(pl.multiple_of(own_op * step, step), step)
    for e in range(0, n_op, 2):
        there = own_blk * n_op + (own_op ^ e)
        pair = parts2[there] + parts2[own_blk * n_op + (own_op ^ e ^ 1)]
        on_vec = cv + cu * (nearest(pair[:, 0:1], pair[:, 1:2]) - along)
        for h in range(2):
            at = pl.multiple_of((own_op ^ e ^ h) * cols, LANES)
            part, crossed = slice(h * cols, (h + 1) * cols), slice((1 - h) * cols, (2 - h) * cols)
            for d in range(n_blk):
                dmat = diag[d, mine] + right_diag[:, pl.ds(at, cols)]
                blocks = [own.at[j] for j in range(4)]
                if e:
                    far, near = got1[e // 2 - 1], got2[e - 1]
                    blocks = far.at[0], far.at[1], near.at[0], near.at[1]
                raw, sigma, fld, image = (x[d, :, part].astype(jnp.float32) for x in blocks)
                vec, sigma = raw * scale, sigma * scale
                image = image + got2[e][0, d, :, crossed].astype(jnp.float32) + dmat * fld
                newvec = on_vec * vec + cu * fld
                res = on_vec * sigma + cu * image - energy * newvec
                new_out[slots[d], :, pl.ds(at, cols)] = newvec.astype(jnp.bfloat16)
                res_out[slots[d], :, pl.ds(at, cols)] = res.astype(jnp.bfloat16)


def per_device(
    psi, left_ops, right_ops, term_shift, slot_sector, sector_width, diag_left, diag_right
):
    n_blk, n_op = lax.axis_size("blk"), lax.axis_size("op")
    _, rows, ncols = psi.shape
    terms, _, width, _ = right_ops.shape
    n_pair = n_op // 2
    cols = diag_right.shape[0] // n_op
    step = rows // n_op
    count = float(n_blk * rows * ncols)
    n_dev = n_blk * n_op
    bf16, f32, i32 = jnp.bfloat16, jnp.float32, jnp.int32
    last = sorted(range(1, n_blk), key=lambda d: min(d, n_blk - d))[-1]

    def pack():
        first = swap(term_shift, 1, n_op)
        sent = kernel(
            functools.partial(pack_body, n_blk, n_op),
            [(term_shift, SMEM), (first, SMEM), (psi, HBM), (right_ops, HBM)],
            [((rows, 2 * cols if d in (0, last) else cols), bf16, VMEM) for d in range(n_blk)]
            + [((terms * width + 16, 2 * cols), bf16, VMEM)] * n_pair,
            [pltpu.VMEM(right_ops.shape, bf16), pltpu.SemaphoreType.DMA((2 * n_blk + 1,))],
            nbytes=1 << 20,
        )
        return sent[:n_blk], sent[n_blk:]

    def table(right):
        return kernel(
            functools.partial(table_body, n_blk, terms),
            [(slot_sector, SMEM), (sector_width, SMEM), (diag_left, VMEM), (diag_right[None], VMEM)]
            + [(block, VMEM) for block in right],
            [((n_blk * n_pair * terms,), i32, SMEM)]
            + [((n_blk,), i32, SMEM)] * 2
            + [((n_blk, rows, LANES), f32, VMEM), ((1, n_op * cols), f32, VMEM)],
        )

    def inputs(left, psi, those):
        blocks = [left[d, 2 * e] for d in those for e in range(n_pair)]
        halves = [half for d in those for half in psi[d]]
        return [(x, VMEM) for x in blocks], [(x, VMEM) for x in halves], [len(psi[d]) for d in those]

    def early(left, psi, n_early, tables):
        left_ins, psi_ins, counts = inputs(left, psi, range(n_early))
        return kernel(
            functools.partial(early_body, n_pair, counts),
            [(tables[1], SMEM)] + left_ins + psi_ins,
            [
                ((n_early, rows, 2 * cols), bf16, VMEM),
                ((n_early, n_pair * terms, rows, 2 * cols), bf16, VMEM),
                ((n_early, n_pair, terms, rows, rows), bf16, HBM),
            ],
            [pltpu.SemaphoreType.DMA((n_early * n_pair,))],
            flops=2 * n_early * rows * rows * 2 * cols * terms * n_pair,
            nbytes=4 << 20,
        )

    left, psi_by, right, (src, widths, slots, *both), (raw_early, inter_early, left_early) = gather(
        left_ops[:, 0], n_blk, n_op, pack, table, early
    )
    n_early = raw_early.shape[0]
    n_late = n_blk - n_early
    left_ins, psi_ins, counts = inputs(left, psi_by, range(n_early, n_blk))
    right_ins = [(block, VMEM) for block in right]
    diags = [(x, VMEM) for x in both]

    tables = [(src, SMEM), (widths, SMEM)]
    narrow = ((n_blk, rows, 2 * cols), bf16, VMEM)
    dots = ((n_dev, 1, LANES), f32, VMEM)
    wide = ((n_blk, rows, 2 * cols), f32, VMEM)
    sends = [((2 - e % 2, n_blk, step, 2 * cols), bf16, VMEM) for e in range(1, n_op)]
    inter = pltpu.VMEM((n_blk + 1, n_pair * terms, rows, 2 * cols), bf16)
    left_late = (n_late, n_pair, terms, rows, rows)
    cost = dict(flops=2 * n_blk * rows * 2 * cols * terms * n_pair * (rows + 2 * cols), nbytes=6 << 20)

    def totals(parts):
        return lax.all_to_all(parts, ("blk", "op"), 0, 0, tiled=True)

    part1, raw, kept, dots1 = kernel(
        functools.partial(first_body, n_blk, n_pair, counts),
        tables + left_ins + right_ins + psi_ins + [(raw_early, VMEM), (inter_early, VMEM)] + diags,
        [narrow, narrow, (left_late, bf16, HBM), dots],
        [inter, pltpu.SemaphoreType.DMA((n_late * n_pair + 2,))],
        **cost,
    )
    parts1 = totals(dots1)
    sig, *out1 = kernel(
        sigma_body,
        [(x, VMEM) for x in (part1, swap(part1, 1, n_op), raw)] + diags,
        [wide] + sends[1::2],
        nbytes=4 << 20,
    )
    got1 = [swap(block, 2 * e, n_op) for e, block in enumerate(out1, 1)]
    dots2, own, *out2 = kernel(
        functools.partial(second_body, n_blk, n_pair, count),
        tables + [(left_early, HBM), (kept, HBM)] + right_ins
        + [(x, VMEM) for x in (parts1, raw, sig)] + diags,
        [dots, ((4, n_blk, step, 2 * cols), bf16, VMEM)] + sends,
        [
            inter,
            pltpu.VMEM((n_blk, rows, 2 * cols), f32),
            pltpu.VMEM((n_blk, rows, 2 * cols), bf16),
            pltpu.VMEM((n_blk, rows, 2 * cols), bf16),
            pltpu.VMEM((n_blk, *left_late[1:]), bf16),
            pltpu.SemaphoreType.DMA((n_blk,)),
        ],
        flops=4 * cost["flops"],
        nbytes=24 << 20,
    )
    near, got1 = lax.optimization_barrier((out2[0], got1))
    parts2 = totals(dots2)
    got2 = [swap(near, 1, n_op)] + [swap(block, e, n_op) for e, block in enumerate(out2[1:], 2)]
    final = ((n_blk, step, n_op * cols), bf16, VMEM)
    new, res, energy = kernel(
        functools.partial(third_body, n_blk, n_op, count),
        [(slots, SMEM)] + [(x, VMEM) for x in (parts1, parts2)] + diags
        + [(x, VMEM) for x in (own, *got1, *got2)],
        [final, final, ((1,), f32, SMEM)],
        nbytes=4 << 20,
    )
    return new, res, energy


def solution(mesh):
    placed = (
        P(("grp", "blk"), None, None),
        P("op", ("grp", "blk"), None, None),
        P("op", ("grp", "blk"), None, None),
        P("op"),
        P("grp"),
        P("grp"),
        P("grp", None),
        P(("grp", "blk")),
    )

    def body(*args):
        psi, left_ops, right_ops, diag_right = args[0], args[1], args[2], args[7]
        n_op = mesh.shape["op"]
        cols = diag_right.shape[0] // n_op
        fits = (
            psi.shape[0] == 1
            and diag_right.shape[0] % n_op == 0
            and cols == LANES
            and n_op % 2 == 0
            and cols % right_ops.shape[2] == 0
            and cols // right_ops.shape[2] * n_op == right_ops.shape[1]
            and psi.shape[1] % (16 * n_op) == 0
            and n_op & (n_op - 1) == 0
            and mesh.shape["blk"] > n_op.bit_length() - 1
        )
        return (per_device if fits else per_device_general)(*args)

    return jax.shard_map(
        body,
        mesh=mesh,
        in_specs=placed,
        out_specs=(P("grp", "op", "blk"), P("grp", "op", "blk"), P("grp")),
        check_vma=False,
    )
```

```python
import functools

import jax
import jax.numpy as jnp
from jax import lax
from jax.experimental import pallas as pl
from jax.experimental.pallas import tpu as pltpu
from jax.sharding import PartitionSpec as P

EPS = 1e-06
LANES = 128
VMEM_LIMIT = 20 * 1024 * 1024


def per_device_general(
    psi, left_ops, right_ops, term_shift, slot_sector, sector_width, diag_left, diag_right
):
    sec_dev, rows, ncols = psi.shape
    nsec = slot_sector.shape[0]
    terms_dev = left_ops.shape[0]
    right_local = right_ops.shape[1]
    right_width = right_ops.shape[2]
    local_cols = diag_right.shape[0]
    count = float(nsec * rows * ncols)
    match = slot_sector[:, None] == jnp.arange(nsec)[None, :]
    widths = jnp.sum(jnp.where(match, sector_width[None, :], 0), axis=1)
    mask_all = (jnp.arange(rows)[None, :] < widths[:, None]).astype(jnp.float32)
    own_mask = lax.dynamic_slice_in_dim(mask_all, lax.axis_index("blk") * sec_dev, sec_dev, 0)
    raw = psi.astype(jnp.float32) * own_mask[:, :, None]
    squares = lax.psum(jnp.sum(raw * raw), "blk")
    v_left = (raw * lax.rsqrt(squares / count + EPS)).astype(jnp.bfloat16)
    onehots = (
        slot_sector[None, None, :] == slot_sector[None, :, None] - term_shift[:, None, None]
    ).astype(jnp.bfloat16)
    op_rows = rows // lax.axis_size("op")
    op_start = lax.axis_index("op") * op_rows
    dmat = diag_left[:, :, None] + diag_right[None, None, :]

    def left_local(field):
        return jnp.einsum(
            "ksij,sjc->ksic", left_ops, field, preferred_element_type=jnp.float32
        ).astype(jnp.bfloat16)

    def right_part(moved_in):
        flat = moved_in.reshape(terms_dev, nsec, rows * local_cols)
        shifted = jnp.einsum(
            "kts,ksx->ktx", onehots, flat, preferred_element_type=jnp.float32
        ).astype(jnp.bfloat16)
        shifted = shifted.reshape(terms_dev, nsec, rows, right_local, right_width)
        accum = jnp.einsum(
            "ktwrc,krdc->twrd", shifted, right_ops, preferred_element_type=jnp.float32
        )
        return accum.reshape(nsec, rows, local_cols) * mask_all[:, :, None]

    def op_total(partial_value):
        return lax.psum(partial_value.astype(jnp.bfloat16), "op").astype(jnp.float32)

    def final_rows(array):
        return lax.dynamic_slice_in_dim(array, op_start, op_rows, 1)

    def reduce_dots(values):
        sums = lax.psum(values, "blk")
        return tuple((item / count for item in sums))

    moved_first, v_moved = (
        lax.all_to_all(left_local(v_left), "blk", split_axis=3, concat_axis=1, tiled=True),
        lax.all_to_all(v_left[None], "blk", split_axis=3, concat_axis=1, tiled=True),
    )
    v_right = v_moved[0]
    vec32 = v_right.astype(jnp.float32)
    first_sigma = op_total(right_part(moved_first)) + dmat * vec32
    theta = reduce_dots((jnp.sum(vec32 * first_sigma),))[0]
    resid = first_sigma - theta * vec32
    den = dmat - theta
    corr = resid * den / jnp.maximum(den * den, 0.25)
    along = reduce_dots((jnp.sum(vec32 * corr),))[0]
    orth = corr - along * vec32
    norm_sq = reduce_dots((jnp.sum(orth * orth),))[0]
    update = (orth * lax.rsqrt(norm_sq + EPS)).astype(jnp.bfloat16)
    upd32 = update.astype(jnp.float32)
    upd_left = lax.all_to_all(update, "blk", split_axis=0, concat_axis=2, tiled=True)
    moved_second = lax.all_to_all(
        left_local(upd_left), "blk", split_axis=3, concat_axis=1, tiled=True
    )
    second_sigma = op_total(right_part(moved_second)) + dmat * upd32
    v_s1, u_s0, u_s1 = reduce_dots(
        (jnp.sum(vec32 * second_sigma), jnp.sum(upd32 * first_sigma), jnp.sum(upd32 * second_sigma))
    )
    h_mix = 0.5 * (v_s1 + u_s0)
    coef_v, coef_u, energy = ritz(theta, h_mix, u_s1)
    newvec = coef_v * vec32 + coef_u * upd32
    image = coef_v * first_sigma + coef_u * second_sigma
    new_out = final_rows(newvec.astype(jnp.bfloat16))
    res_out = final_rows((image - energy * newvec).astype(jnp.bfloat16))
    return (new_out, res_out, jnp.reshape(energy, (1,)))


def ritz(theta, h_mix, h_two):
    angle = 0.5 * jnp.arctan2(2.0 * h_mix, theta - h_two)
    sine = jnp.sin(angle)
    flip = jnp.where(sine > 0, -1.0, 1.0)
    coef_v = -sine * flip
    coef_u = jnp.cos(angle) * flip
    half = 0.5 * (theta - h_two)
    energy = 0.5 * (theta + h_two) - jnp.sqrt(half * half + h_mix * h_mix)
    return coef_v, coef_u, energy


VMEM, SMEM, HBM = pltpu.VMEM, pltpu.SMEM, pltpu.HBM


def kernel(body, ins, outs, scratch=(), flops=0, nbytes=0):
    return pl.pallas_call(
        body,
        out_shape=[
            HBM(shape, dtype) if space == HBM else jax.ShapeDtypeStruct(shape, dtype)
            for shape, dtype, space in outs
        ],
        in_specs=[pl.BlockSpec(memory_space=space) for _, space in ins],
        out_specs=[pl.BlockSpec(memory_space=space) for _, _, space in outs],
        scratch_shapes=list(scratch),
        compiler_params=pltpu.CompilerParams(vmem_limit_bytes=VMEM_LIMIT),
        cost_estimate=pl.CostEstimate(flops=flops, bytes_accessed=nbytes, transcendentals=0),
    )(*[pltpu.with_memory_space_constraint(x, HBM) if space == HBM else x for x, space in ins])


def ring_at(place, n_blk):
    place = place % n_blk if isinstance(place, int) else lax.rem(place + n_blk, n_blk)
    odd, even = 2 * place - 1, 2 * (n_blk - place)
    if isinstance(place, int):
        return 0 if place == 0 else odd if odd < n_blk else even
    return jnp.where(place == 0, 0, jnp.where(odd < n_blk, odd, even))


def ring_place(index, n_blk):
    odd, even = (index + 1) // 2, lax.rem(n_blk - index // 2, n_blk)
    return jnp.where(lax.rem(index, 2) == 1, odd, even)


def onward(block, d, n_blk):
    pairs = [(ring_at(i, n_blk), ring_at(i + d, n_blk)) for i in range(n_blk)]
    return lax.ppermute(block, "blk", pairs)


def swap(block, e, n_op):
    return lax.ppermute(block, "op", [(i, i ^ e) for i in range(n_op)])


def gather(own, n_blk, n_op, pack, table, early):
    bits = [1 << b for b in reversed(range(1, n_op.bit_length() - 1))]
    order = sorted(range(1, n_blk), key=lambda d: min(d, n_blk - d))
    left, psi, right, tables, columns = {(0, 0): own}, {}, None, None, None
    waiting, across, late, made = {(0, 0): 0}, {}, None, None
    for j in range(n_blk + len(bits)):
        new, moved = {}, {}
        for (d, e), done in waiting.items():
            if e == 0 and d + 1 < n_blk:
                new[d + 1, 0] = onward(left[d, 0], 1, n_blk), 0
            for b in range(done, len(bits)):
                new[d, e ^ bits[b]] = swap(left[d, e], bits[b], n_op), b + 1
        left.update({key: block for key, (block, _) in new.items()})
        kept = {key: block for key, (block, _) in new.items() if key[1] == 0}
        kept.update(across)
        across = {key: block for key, (block, _) in new.items() if key[1] != 0}
        if late is not None:
            moved["psi"] = late
        if j == 0:
            columns, packed = pack()
            right = [packed[0]]
            right += [swap(part, 2 * e, n_op) for e, part in enumerate(packed[1:], 1)]
            moved["columns"] = columns
        if j == 0:
            moved["right"] = right
        if j == 1:
            moved["tables"] = table(right)
        if j == n_blk - 1 and j >= len(bits) + 1:
            n_early = min(2, n_blk - 1)
            psi[0] = [columns[0]]
            moved["early"] = early(left, psi, n_early, tables)
        if 2 <= j < n_blk:
            moved["other"] = swap(psi[order[j - 2]][0], 1, n_op)
        late = onward(columns[order[j]], order[j], n_blk) if j < n_blk - 1 else None
        if not kept:
            break
        waiting = {key: done for key, (_, done) in new.items()}
        kept, moved = lax.optimization_barrier((kept, moved))
        left.update(kept)
        right, tables = moved.get("right", right), moved.get("tables", tables)
        columns = moved.get("columns", columns)
        made = moved.get("early", made)
        if "psi" in moved:
            psi[order[j - 1]] = [moved["psi"]]
        if "other" in moved:
            psi[order[j - 2]].append(moved["other"])
    return left, psi, right, tables, made


def place_of():
    return lax.axis_index("blk"), lax.axis_index("op")


def pack_body(n_blk, n_op, shift, _, psi, right_in, *outs):
    n_pair = n_op // 2
    psi_out, right_out, right, sems = outs[:n_blk], outs[n_blk : n_blk + n_pair], outs[-2], outs[-1]
    terms, local, width, _ = right.shape
    cols = local * width // n_op
    per = cols // width
    own_blk, own_op = place_of()
    fetch = pltpu.make_async_copy(right_in, right, sems.at[2 * n_blk])
    fetch.start()
    copies = []
    for d in range(n_blk):
        there = ring_at(ring_place(own_blk, n_blk) + d, n_blk) * n_op
        for h in range(psi_out[d].shape[1] // cols):
            start = pl.multiple_of((there + (own_op ^ h)) * cols, LANES)
            copy = pltpu.make_async_copy(
                psi.at[0, :, pl.ds(start, cols)],
                psi_out[d].at[:, h * cols : (h + 1) * cols],
                sems.at[2 * d + h],
            )
            copy.start()
            copies.append(copy)
    lane = lax.broadcasted_iota(jnp.int32, (16, 2 * cols), 1)
    line = jnp.zeros((16, 2 * cols), jnp.float32)
    for k in range(terms):
        line = jnp.where(lane == k, shift[k].astype(jnp.float32), line)
    square = [lax.broadcasted_iota(jnp.int32, (width, width), axis) for axis in (0, 1)]
    unit = (square[0] == square[1]).astype(jnp.bfloat16)
    fetch.wait()
    for e in range(n_pair):
        for k in range(terms):
            turned = []
            for h in range(2):
                first = (own_op ^ (2 * e) ^ h) * per
                for r in range(per):
                    turned.append(
                        lax.dot_general(
                            right[k, first + r], unit, (((0,), (0,)), ((), ())),
                            preferred_element_type=jnp.float32,
                        )
                    )
            side_by_side = jnp.concatenate(turned, axis=1).astype(jnp.bfloat16)
            right_out[e][k * width : (k + 1) * width] = side_by_side
        right_out[e][terms * width :] = line.astype(jnp.bfloat16)
    for copy in copies:
        copy.wait()


def table_body(n_blk, terms, sector, width, left_diag, right_diag, *refs):
    tails, src, widths, slots, diag, right_out = refs[:-5], *refs[-5:]
    right_out[...] = right_diag[...]
    n_pair = len(tails)
    rows, cols = tails[0].shape
    own_blk, _ = place_of()
    lane = lax.broadcasted_iota(jnp.int32, (16, cols), 1)
    for d in range(n_blk):
        slot = ring_at(ring_place(own_blk, n_blk) - d, n_blk)
        slots[d] = slot
        widths[d] = width[sector[slot]]
    for e in range(n_pair):
        tail = tails[e][rows - 16 :].astype(jnp.float32)
        for k in range(terms):
            shift = jnp.max(jnp.where(lane == k, tail, -1e9)).astype(jnp.int32)
            for t in range(n_blk):
                want = sector[slots[t]] - shift
                found = jnp.int32(n_blk)
                for d in range(n_blk):
                    found = jnp.where(sector[slots[d]] == want, d, found)
                src[(t * n_pair + e) * terms + k] = found
    for d in range(n_blk):
        row = left_diag[pl.ds(slots[d], 1), :]
        diag[d] = jnp.transpose(jnp.broadcast_to(row, (diag.shape[2], row.shape[1])))


def diagonal(diag, right_diag, d, h):
    cols = diag.shape[2]
    _, own_op = place_of()
    start = pl.multiple_of((own_op ^ h) * cols, LANES)
    return diag[d] + right_diag[:, pl.ds(start, cols)]


def row_mask(width, shape):
    return lax.broadcasted_iota(jnp.int32, shape, 0) < width


def fold(x):
    return jnp.sum(x.reshape(-1, 8, x.shape[-1]), axis=0)


def whole(x):
    return jnp.sum(jnp.sum(x, axis=0, keepdims=True), axis=1, keepdims=True)


def spread(values, out):
    lane = lax.broadcasted_iota(jnp.int32, out.shape[1:], 1)
    row = jnp.zeros(out.shape[1:], jnp.float32)
    for j, value in enumerate(values):
        row = jnp.where(lane == j, value, row)
    for d in range(out.shape[0]):
        out[d] = row


def by_block(packed, terms, k):
    rows, cols = packed.shape
    width = (rows - 16) // terms
    lane = lax.broadcasted_iota(jnp.int32, (width, cols), 1)
    block = packed[k * width : (k + 1) * width].astype(jnp.float32)
    parts = []
    for r in range(cols // width):
        inside = (lane >= r * width) & (lane < (r + 1) * width)
        parts.append(jnp.where(inside, block, 0.0).astype(jnp.bfloat16))
    return jnp.concatenate(parts, axis=0)


def left_products(block, left, inter):
    n_terms, rows, cols = inter.shape
    at = 0
    while at < n_terms:
        ops = left(at)
        terms = ops.shape[0]
        prod = jnp.dot(ops.reshape(terms * rows, rows), block, preferred_element_type=jnp.float32)
        inter[at : at + terms] = prod.astype(jnp.bfloat16).reshape(terms, rows, cols)
        at += terms


def sum_terms(src, widths, inter, right, out, emit):
    n_blk, n_terms, _, _ = inter.shape
    n_blk -= 1
    terms = n_terms // len(right)
    turned = [by_block(right[j // terms], terms, j % terms) for j in range(n_terms)]
    for t in range(n_blk):
        total = None
        for j in range(n_terms):
            part = jnp.dot(
                inter[src[t * n_terms + j], j], turned[j], preferred_element_type=jnp.float32
            )
            total = part if total is None else total + part
        total = jnp.where(row_mask(widths[t], total.shape), total, 0.0)
        out[t] = total.astype(jnp.bfloat16)
        emit(t, total)


def keep(left, left_out, sems):
    copies = []
    for d, line in enumerate(left):
        for e, ref in enumerate(line):
            copies.append(pltpu.make_async_copy(ref, left_out.at[d, e], sems.at[d * len(line) + e]))
            copies[-1].start()
    return copies


def masked(psi, width, out):
    at = 0
    for ref in psi:
        block = ref[...].astype(jnp.float32)
        block = jnp.where(row_mask(width, block.shape), block, 0.0)
        out[:, at : at + block.shape[1]] = block.astype(jnp.bfloat16)
        at += block.shape[1]


def take(refs, counts):
    out = []
    for count in counts:
        out.append(refs[:count])
        refs = refs[count:]
    return out, refs


def products_of(psi, left, widths, first, raw_out, inter):
    for d, line in enumerate(left):
        masked(psi[d], widths[first + d], raw_out.at[d])
        terms = line[0].shape[0]
        left_products(raw_out[d], lambda at: line[at // terms][...], inter.at[d])


def early_body(n_pair, counts, widths, *refs):
    left, refs = take(refs, [n_pair] * len(counts))
    psi, (raw_out, inter_out, left_out, sems) = take(refs, counts)
    copies = keep(left, left_out, sems)
    products_of(psi, left, widths, 0, raw_out, inter_out)
    for copy in copies:
        copy.wait()


def first_body(n_blk, n_pair, counts, src, widths, *refs):
    n_late = len(counts)
    n_early = n_blk - n_late
    left, refs = take(refs, [n_pair] * n_late)
    (right,), refs = take(refs, [n_pair])
    psi, refs = take(refs, counts)
    raw_in, inter_in, diag, right_diag, part_out, raw_out, left_out, dots_out, inter, sems = refs
    copies = keep(left, left_out, sems)
    for j, (given, own) in enumerate(((inter_in, inter), (raw_in, raw_out))):
        copies.append(
            pltpu.make_async_copy(given, own.at[:n_early], sems.at[n_late * n_pair + j])
        )
        copies[-1].start()
    inter[n_blk] = jnp.zeros_like(inter[n_blk])
    products_of(
        psi, left, widths, n_early, raw_out.at[n_early:], inter.at[n_early:n_blk]
    )
    for copy in copies:
        copy.wait()
    cols = diag.shape[2]
    zero = jnp.zeros((8, cols), jnp.float32)
    sums = [zero, zero]

    def emit(d, total):
        for h in range(2):
            part = slice(h * cols, (h + 1) * cols)
            raw = raw_out[d, :, part].astype(jnp.float32)
            image = total[:, part]
            if h == 0:
                image = image + diagonal(diag, right_diag, d, h) * raw
                sums[0] = sums[0] + fold(raw * raw)
            sums[1] = sums[1] + fold(raw * image)

    sum_terms(src, widths, inter, right, part_out, emit)
    spread([whole(x) for x in sums], dots_out)


def send_rows(e, send, d, *refs):
    _, own_op = place_of()
    step = send.shape[2]
    rows = pl.ds(pl.multiple_of((own_op ^ e) * step, step), step)
    for j, ref in enumerate(refs):
        send[j, d] = ref[d, rows].astype(send.dtype)


def total_of(mine, other, d, h, cols):
    own = mine[d, :, h * cols : (h + 1) * cols].astype(jnp.float32)
    return own + other[d, :, (1 - h) * cols : (2 - h) * cols].astype(jnp.float32)


def sigma_body(mine, other, raw_in, diag, right_diag, sig_out, *sends):
    n_blk, _, cols = diag.shape
    for d in range(n_blk):
        for h in range(2):
            part = slice(h * cols, (h + 1) * cols)
            raw = raw_in[d, :, part].astype(jnp.float32)
            sigma = total_of(mine, other, d, h, cols) + diagonal(diag, right_diag, d, h) * raw
            sig_out[d, :, part] = sigma
        for e, send in enumerate(sends, 1):
            send_rows(2 * e, send, d, raw_in, sig_out)


def norm_theta(parts, count):
    tot = jnp.sum(parts, axis=0) * (1.0 / count)
    scale = lax.rsqrt(tot[:, 0:1] + EPS)
    return scale, tot[:, 1:2] * scale * scale


def second_body(n_blk, n_pair, count, src, widths, left_early, left_late, *refs):
    right, refs = refs[:n_pair], refs[n_pair:]
    parts, raw_in, sig, diag, right_diag, dots_out, own_out = refs[:7]
    sends, (inter, corr, fld, part_out, held, sems) = refs[7:-6], refs[-6:]
    copies = []
    n_early = left_early.shape[0]
    for d in range(n_blk):
        kept = left_early.at[d] if d < n_early else left_late.at[d - n_early]
        copies.append(pltpu.make_async_copy(kept, held.at[d], sems.at[d]))
        copies[-1].start()
    inter[n_blk] = jnp.zeros_like(inter[n_blk])
    scale, theta = norm_theta(parts[...], count)
    cols = diag.shape[2]
    halves = []
    for h in range(2):
        part = slice(h * cols, (h + 1) * cols)
        vv = vc = vs = jnp.zeros((8, cols), jnp.float32)
        for d in range(n_blk):
            vec = raw_in[d, :, part].astype(jnp.float32) * scale
            sigma = sig[d, :, part] * scale
            den = diagonal(diag, right_diag, d, h) - theta
            item = (sigma - theta * vec) * den / jnp.maximum(den * den, 0.25)
            corr[d, :, part] = item
            vv, vc = vv + fold(vec * vec), vc + fold(vec * item)
            if h == 0:
                vs = vs + fold(vec * sigma)
        halves.append((whole(vv), whole(vc), vs))
    along = (halves[0][1] + halves[1][1]) / jnp.maximum(halves[0][0] + halves[1][0], 1e-30)
    terms = held.shape[2]
    for copy in copies:
        copy.wait()
    for d in range(n_blk):
        for h in range(2):
            part = slice(h * cols, (h + 1) * cols)
            vec = raw_in[d, :, part].astype(jnp.float32) * scale
            fld[d, :, part] = (corr[d, :, part] - along * vec).astype(jnp.bfloat16)
        left_products(fld[d], lambda at: held[d, at // terms], inter.at[d])
    zero = jnp.zeros((8, cols), jnp.float32)
    sums = [zero for _ in range(5)]

    def emit(d, total):
        for h in range(2):
            part = slice(h * cols, (h + 1) * cols)
            field = fld[d, :, part].astype(jnp.float32)
            raw = raw_in[d, :, part].astype(jnp.float32)
            image = total[:, part]
            if h == 0:
                image = image + diagonal(diag, right_diag, d, h) * field
                for j, prod in enumerate((field * field, raw * field, field * sig[d, :, part])):
                    sums[j] = sums[j] + fold(prod)
            sums[3] = sums[3] + fold(raw * image)
            sums[4] = sums[4] + fold(field * image)
        for e, send in enumerate(sends, 1):
            send_rows(e, send, d, *((part_out,) if e % 2 else (fld, part_out)))
        rows = pl.ds(pl.multiple_of(own_op * step, step), step)
        for j, ref in enumerate((raw_in, sig, fld, part_out)):
            own_out[j, d] = ref[d, rows].astype(own_out.dtype)

    _, own_op = place_of()
    step = own_out.shape[2]
    sum_terms(src, widths, inter, right, part_out, emit)
    vv, vc, vs = halves[0]
    ff, vf, fs, vt, ft = (whole(x) for x in sums)
    spread([vv, vc, whole(vs), ff, vf * scale, fs * scale, vt * scale, ft], dots_out)


def ritz_pair(theta, h_mix, h_two):
    diff, twice = theta - h_two, 2.0 * h_mix
    size = jnp.sqrt(diff * diff + twice * twice)
    some = size > 0.0
    safe = jnp.where(some, size, 1.0)
    big = jnp.sqrt(0.5 + 0.5 * jnp.abs(diff) / safe)
    small = 0.5 * jnp.abs(twice) / (safe * big)
    sine = jnp.where(diff >= 0.0, small, big)
    cosine = jnp.where(diff >= 0.0, big, small)
    sine = jnp.where(some, sine, 0.0)
    cosine = jnp.where(some, cosine, 1.0)
    upward = (twice > 0.0) | ((twice == 0.0) & (diff < 0.0))
    return sine, jnp.where(upward, -cosine, cosine), 0.5 * (theta + h_two) - 0.5 * size


def third_body(n_blk, n_op, count, slots, parts1, parts2, diag, right_diag, own, *refs):
    n_far = n_op // 2 - 1
    got1, got2 = refs[:n_far], refs[n_far : n_far + n_op - 1]
    new_out, res_out, energy_out = refs[n_far + n_op - 1 :]
    step, cols = new_out.shape[1], new_out.shape[2] // n_op
    own_blk, own_op = place_of()
    scale, theta = norm_theta(parts1[...], count)
    pairs = parts2[...].reshape(n_blk * n_op // 2, 2, *parts2.shape[1:])
    pairs = pairs[:, 0] + pairs[:, 1]
    vv, vc, vs, ff, vf, fs, vt, ft = (pairs[:, 0, j : j + 1] for j in range(8))

    def mean(x):
        return jnp.sum(x, axis=0, keepdims=True) * (1.0 / count)

    def nearest(vv, vc):
        return vc / jnp.maximum(vv, 1e-30)

    along = mean(vc)
    beta = nearest(vv, vc) - along
    norm_sq = mean(ff + 2.0 * beta * vf + beta * beta * vv)
    unit = lax.rsqrt(jnp.maximum(norm_sq, 0.0) + EPS)
    v_s1 = unit * mean(vt + beta * vs)
    u_s0 = unit * mean(fs + beta * vs)
    u_s1 = unit * unit * mean(ft + beta * (vt + fs) + beta * beta * vs)
    cv, cu, energy = ritz_pair(theta, 0.5 * (v_s1 + u_s0), u_s1)
    energy_out[0] = jnp.max(energy)
    cu = cu * unit
    mine = pl.ds(pl.multiple_of(own_op * step, step), step)
    for e in range(0, n_op, 2):
        there = own_blk * n_op + (own_op ^ e)
        pair = parts2[there] + parts2[own_blk * n_op + (own_op ^ e ^ 1)]
        on_vec = cv + cu * (nearest(pair[:, 0:1], pair[:, 1:2]) - along)
        for h in range(2):
            at = pl.multiple_of((own_op ^ e ^ h) * cols, LANES)
            part, crossed = slice(h * cols, (h + 1) * cols), slice((1 - h) * cols, (2 - h) * cols)
            for d in range(n_blk):
                dmat = diag[d, mine] + right_diag[:, pl.ds(at, cols)]
                blocks = [own.at[j] for j in range(4)]
                if e:
                    far, near = got1[e // 2 - 1], got2[e - 1]
                    blocks = far.at[0], far.at[1], near.at[0], near.at[1]
                raw, sigma, fld, image = (x[d, :, part].astype(jnp.float32) for x in blocks)
                vec, sigma = raw * scale, sigma * scale
                image = image + got2[e][0, d, :, crossed].astype(jnp.float32) + dmat * fld
                newvec = on_vec * vec + cu * fld
                res = on_vec * sigma + cu * image - energy * newvec
                new_out[slots[d], :, pl.ds(at, cols)] = newvec.astype(jnp.bfloat16)
                res_out[slots[d], :, pl.ds(at, cols)] = res.astype(jnp.bfloat16)


def per_device(
    psi, left_ops, right_ops, term_shift, slot_sector, sector_width, diag_left, diag_right
):
    n_blk, n_op = lax.axis_size("blk"), lax.axis_size("op")
    _, rows, ncols = psi.shape
    terms, _, width, _ = right_ops.shape
    n_pair = n_op // 2
    cols = diag_right.shape[0] // n_op
    step = rows // n_op
    count = float(n_blk * rows * ncols)
    n_dev = n_blk * n_op
    bf16, f32, i32 = jnp.bfloat16, jnp.float32, jnp.int32
    last = sorted(range(1, n_blk), key=lambda d: min(d, n_blk - d))[-1]

    def pack():
        first = swap(term_shift, 1, n_op)
        sent = kernel(
            functools.partial(pack_body, n_blk, n_op),
            [(term_shift, SMEM), (first, SMEM), (psi, HBM), (right_ops, HBM)],
            [((rows, 2 * cols if d in (0, last) else cols), bf16, VMEM) for d in range(n_blk)]
            + [((terms * width + 16, 2 * cols), bf16, VMEM)] * n_pair,
            [pltpu.VMEM(right_ops.shape, bf16), pltpu.SemaphoreType.DMA((2 * n_blk + 1,))],
            nbytes=1 << 20,
        )
        return sent[:n_blk], sent[n_blk:]

    def table(right):
        return kernel(
            functools.partial(table_body, n_blk, terms),
            [(slot_sector, SMEM), (sector_width, SMEM), (diag_left, VMEM), (diag_right[None], VMEM)]
            + [(block, VMEM) for block in right],
            [((n_blk * n_pair * terms,), i32, SMEM)]
            + [((n_blk,), i32, SMEM)] * 2
            + [((n_blk, rows, LANES), f32, VMEM), ((1, n_op * cols), f32, VMEM)],
        )

    def inputs(left, psi, those):
        blocks = [left[d, 2 * e] for d in those for e in range(n_pair)]
        halves = [half for d in those for half in psi[d]]
        return [(x, VMEM) for x in blocks], [(x, VMEM) for x in halves], [len(psi[d]) for d in those]

    def early(left, psi, n_early, tables):
        left_ins, psi_ins, counts = inputs(left, psi, range(n_early))
        return kernel(
            functools.partial(early_body, n_pair, counts),
            [(tables[1], SMEM)] + left_ins + psi_ins,
            [
                ((n_early, rows, 2 * cols), bf16, VMEM),
                ((n_early, n_pair * terms, rows, 2 * cols), bf16, VMEM),
                ((n_early, n_pair, terms, rows, rows), bf16, HBM),
            ],
            [pltpu.SemaphoreType.DMA((n_early * n_pair,))],
            flops=2 * n_early * rows * rows * 2 * cols * terms * n_pair,
            nbytes=4 << 20,
        )

    left, psi_by, right, (src, widths, slots, *both), (raw_early, inter_early, left_early) = gather(
        left_ops[:, 0], n_blk, n_op, pack, table, early
    )
    n_early = raw_early.shape[0]
    n_late = n_blk - n_early
    left_ins, psi_ins, counts = inputs(left, psi_by, range(n_early, n_blk))
    right_ins = [(block, VMEM) for block in right]
    diags = [(x, VMEM) for x in both]

    tables = [(src, SMEM), (widths, SMEM)]
    narrow = ((n_blk, rows, 2 * cols), bf16, VMEM)
    dots = ((n_dev, 1, LANES), f32, VMEM)
    wide = ((n_blk, rows, 2 * cols), f32, VMEM)
    sends = [((2 - e % 2, n_blk, step, 2 * cols), bf16, VMEM) for e in range(1, n_op)]
    inter = pltpu.VMEM((n_blk + 1, n_pair * terms, rows, 2 * cols), bf16)
    left_late = (n_late, n_pair, terms, rows, rows)
    cost = dict(flops=2 * n_blk * rows * 2 * cols * terms * n_pair * (rows + 2 * cols), nbytes=6 << 20)

    def totals(parts):
        return lax.all_to_all(parts, ("blk", "op"), 0, 0, tiled=True)

    part1, raw, kept, dots1 = kernel(
        functools.partial(first_body, n_blk, n_pair, counts),
        tables + left_ins + right_ins + psi_ins + [(raw_early, VMEM), (inter_early, VMEM)] + diags,
        [narrow, narrow, (left_late, bf16, HBM), dots],
        [inter, pltpu.SemaphoreType.DMA((n_late * n_pair + 2,))],
        **cost,
    )
    parts1 = totals(dots1)
    sig, *out1 = kernel(
        sigma_body,
        [(x, VMEM) for x in (part1, swap(part1, 1, n_op), raw)] + diags,
        [wide] + sends[1::2],
        nbytes=4 << 20,
    )
    got1 = [swap(block, 2 * e, n_op) for e, block in enumerate(out1, 1)]
    dots2, own, *out2 = kernel(
        functools.partial(second_body, n_blk, n_pair, count),
        tables + [(left_early, HBM), (kept, HBM)] + right_ins
        + [(x, VMEM) for x in (parts1, raw, sig)] + diags,
        [dots, ((4, n_blk, step, 2 * cols), bf16, VMEM)] + sends,
        [
            inter,
            pltpu.VMEM((n_blk, rows, 2 * cols), f32),
            pltpu.VMEM((n_blk, rows, 2 * cols), bf16),
            pltpu.VMEM((n_blk, rows, 2 * cols), bf16),
            pltpu.VMEM((n_blk, *left_late[1:]), bf16),
            pltpu.SemaphoreType.DMA((n_blk,)),
        ],
        flops=4 * cost["flops"],
        nbytes=24 << 20,
    )
    near, got1 = lax.optimization_barrier((out2[0], got1))
    parts2 = totals(dots2)
    got2 = [swap(near, 1, n_op)] + [swap(block, e, n_op) for e, block in enumerate(out2[1:], 2)]
    final = ((n_blk, step, n_op * cols), bf16, VMEM)
    new, res, energy = kernel(
        functools.partial(third_body, n_blk, n_op, count),
        [(slots, SMEM)] + [(x, VMEM) for x in (parts1, parts2)] + diags
        + [(x, VMEM) for x in (own, *got1, *got2)],
        [final, final, ((1,), f32, SMEM)],
        nbytes=4 << 20,
    )
    return new, res, energy


def solution(mesh):
    placed = (
        P(("grp", "blk"), None, None),
        P("op", ("grp", "blk"), None, None),
        P("op", ("grp", "blk"), None, None),
        P("op"),
        P("grp"),
        P("grp"),
        P("grp", None),
        P(("grp", "blk")),
    )

    def body(*args):
        psi, left_ops, right_ops, diag_right = args[0], args[1], args[2], args[7]
        n_op = mesh.shape["op"]
        cols = diag_right.shape[0] // n_op
        fits = (
            psi.shape[0] == 1
            and diag_right.shape[0] % n_op == 0
            and cols == LANES
            and n_op % 2 == 0
            and cols % right_ops.shape[2] == 0
            and cols // right_ops.shape[2] * n_op == right_ops.shape[1]
            and psi.shape[1] % (16 * n_op) == 0
            and n_op & (n_op - 1) == 0
            and mesh.shape["blk"] > n_op.bit_length() - 1
        )
        return (per_device if fits else per_device_general)(*args)

    return jax.shard_map(
        body,
        mesh=mesh,
        in_specs=placed,
        out_specs=(P("grp", "op", "blk"), P("grp", "op", "blk"), P("grp")),
        check_vma=False,
    )
```

```python
import functools

import jax
import jax.numpy as jnp
from jax import lax
from jax.experimental import pallas as pl
from jax.experimental.pallas import tpu as pltpu
from jax.sharding import PartitionSpec as P

EPS = 1e-06
LANES = 128
VMEM_LIMIT = 20 * 1024 * 1024


def per_device_general(
    psi, left_ops, right_ops, term_shift, slot_sector, sector_width, diag_left, diag_right
):
    sec_dev, rows, ncols = psi.shape
    nsec = slot_sector.shape[0]
    terms_dev = left_ops.shape[0]
    right_local = right_ops.shape[1]
    right_width = right_ops.shape[2]
    local_cols = diag_right.shape[0]
    count = float(nsec * rows * ncols)
    match = slot_sector[:, None] == jnp.arange(nsec)[None, :]
    widths = jnp.sum(jnp.where(match, sector_width[None, :], 0), axis=1)
    mask_all = (jnp.arange(rows)[None, :] < widths[:, None]).astype(jnp.float32)
    own_mask = lax.dynamic_slice_in_dim(mask_all, lax.axis_index("blk") * sec_dev, sec_dev, 0)
    raw = psi.astype(jnp.float32) * own_mask[:, :, None]
    squares = lax.psum(jnp.sum(raw * raw), "blk")
    v_left = (raw * lax.rsqrt(squares / count + EPS)).astype(jnp.bfloat16)
    onehots = (
        slot_sector[None, None, :] == slot_sector[None, :, None] - term_shift[:, None, None]
    ).astype(jnp.bfloat16)
    op_rows = rows // lax.axis_size("op")
    op_start = lax.axis_index("op") * op_rows
    dmat = diag_left[:, :, None] + diag_right[None, None, :]

    def left_local(field):
        return jnp.einsum(
            "ksij,sjc->ksic", left_ops, field, preferred_element_type=jnp.float32
        ).astype(jnp.bfloat16)

    def right_part(moved_in):
        flat = moved_in.reshape(terms_dev, nsec, rows * local_cols)
        shifted = jnp.einsum(
            "kts,ksx->ktx", onehots, flat, preferred_element_type=jnp.float32
        ).astype(jnp.bfloat16)
        shifted = shifted.reshape(terms_dev, nsec, rows, right_local, right_width)
        accum = jnp.einsum(
            "ktwrc,krdc->twrd", shifted, right_ops, preferred_element_type=jnp.float32
        )
        return accum.reshape(nsec, rows, local_cols) * mask_all[:, :, None]

    def op_total(partial_value):
        return lax.psum(partial_value.astype(jnp.bfloat16), "op").astype(jnp.float32)

    def final_rows(array):
        return lax.dynamic_slice_in_dim(array, op_start, op_rows, 1)

    def reduce_dots(values):
        sums = lax.psum(values, "blk")
        return tuple((item / count for item in sums))

    moved_first, v_moved = (
        lax.all_to_all(left_local(v_left), "blk", split_axis=3, concat_axis=1, tiled=True),
        lax.all_to_all(v_left[None], "blk", split_axis=3, concat_axis=1, tiled=True),
    )
    v_right = v_moved[0]
    vec32 = v_right.astype(jnp.float32)
    first_sigma = op_total(right_part(moved_first)) + dmat * vec32
    theta = reduce_dots((jnp.sum(vec32 * first_sigma),))[0]
    resid = first_sigma - theta * vec32
    den = dmat - theta
    corr = resid * den / jnp.maximum(den * den, 0.25)
    along = reduce_dots((jnp.sum(vec32 * corr),))[0]
    orth = corr - along * vec32
    norm_sq = reduce_dots((jnp.sum(orth * orth),))[0]
    update = (orth * lax.rsqrt(norm_sq + EPS)).astype(jnp.bfloat16)
    upd32 = update.astype(jnp.float32)
    upd_left = lax.all_to_all(update, "blk", split_axis=0, concat_axis=2, tiled=True)
    moved_second = lax.all_to_all(
        left_local(upd_left), "blk", split_axis=3, concat_axis=1, tiled=True
    )
    second_sigma = op_total(right_part(moved_second)) + dmat * upd32
    v_s1, u_s0, u_s1 = reduce_dots(
        (jnp.sum(vec32 * second_sigma), jnp.sum(upd32 * first_sigma), jnp.sum(upd32 * second_sigma))
    )
    h_mix = 0.5 * (v_s1 + u_s0)
    coef_v, coef_u, energy = ritz(theta, h_mix, u_s1)
    newvec = coef_v * vec32 + coef_u * upd32
    image = coef_v * first_sigma + coef_u * second_sigma
    new_out = final_rows(newvec.astype(jnp.bfloat16))
    res_out = final_rows((image - energy * newvec).astype(jnp.bfloat16))
    return (new_out, res_out, jnp.reshape(energy, (1,)))


def ritz(theta, h_mix, h_two):
    angle = 0.5 * jnp.arctan2(2.0 * h_mix, theta - h_two)
    sine = jnp.sin(angle)
    flip = jnp.where(sine > 0, -1.0, 1.0)
    coef_v = -sine * flip
    coef_u = jnp.cos(angle) * flip
    half = 0.5 * (theta - h_two)
    energy = 0.5 * (theta + h_two) - jnp.sqrt(half * half + h_mix * h_mix)
    return coef_v, coef_u, energy


VMEM, SMEM, HBM = pltpu.VMEM, pltpu.SMEM, pltpu.HBM


def kernel(body, ins, outs, scratch=(), flops=0, nbytes=0, in_place=None):
    return pl.pallas_call(
        body,
        out_shape=[
            HBM(shape, dtype) if space == HBM else jax.ShapeDtypeStruct(shape, dtype)
            for shape, dtype, space in outs
        ],
        in_specs=[pl.BlockSpec(memory_space=space) for _, space in ins],
        out_specs=[pl.BlockSpec(memory_space=space) for _, _, space in outs],
        scratch_shapes=list(scratch),
        input_output_aliases=in_place or {},
        compiler_params=pltpu.CompilerParams(vmem_limit_bytes=VMEM_LIMIT),
        cost_estimate=pl.CostEstimate(flops=flops, bytes_accessed=nbytes, transcendentals=0),
    )(*[pltpu.with_memory_space_constraint(x, HBM) if space == HBM else x for x, space in ins])


def ring_at(place, n_blk):
    place = place % n_blk if isinstance(place, int) else lax.rem(place + n_blk, n_blk)
    odd, even = 2 * place - 1, 2 * (n_blk - place)
    if isinstance(place, int):
        return 0 if place == 0 else odd if odd < n_blk else even
    return jnp.where(place == 0, 0, jnp.where(odd < n_blk, odd, even))


def ring_place(index, n_blk):
    odd, even = (index + 1) // 2, lax.rem(n_blk - index // 2, n_blk)
    return jnp.where(lax.rem(index, 2) == 1, odd, even)


def onward(block, d, n_blk):
    pairs = [(ring_at(i, n_blk), ring_at(i + d, n_blk)) for i in range(n_blk)]
    return lax.ppermute(block, "blk", pairs)


def swap(block, e, n_op):
    return lax.ppermute(block, "op", [(i, i ^ e) for i in range(n_op)])


def gather(own, n_blk, n_op, pack, table, early):
    bits = [1 << b for b in reversed(range(1, n_op.bit_length() - 1))]
    order = sorted(range(1, n_blk), key=lambda d: min(d, n_blk - d))
    left, psi, right, tables, columns = {(0, 0): own}, {}, None, None, None
    waiting, late, made = {(0, 0): 0}, None, None
    for j in range(n_blk + len(bits)):
        new, moved = {}, {}
        for (d, e), done in waiting.items():
            if e == 0 and d + 1 < n_blk:
                new[d + 1, 0] = onward(left[d, 0], 1, n_blk), 0
            for b in range(done, len(bits)):
                new[d, e ^ bits[b]] = swap(left[d, e], bits[b], n_op), b + 1
        kept = {key: block for key, (block, _) in new.items()}
        if late is not None:
            moved["psi"] = late
        if j == 0:
            columns, packed = pack()
            moved["right"] = [packed[0]]
            moved["right"] += [swap(part, 2 * e, n_op) for e, part in enumerate(packed[1:], 1)]
        if j == 1:
            moved["tables"] = table(right)
        if j == n_blk - 1 and j >= len(bits) + 1:
            n_early = min(2, n_blk - 1)
            psi[0] = [columns[0]]
            moved["early"] = early(left, psi, right, n_early, tables)
        if 2 <= j < n_blk:
            moved["other"] = swap(psi[order[j - 2]][0], 1, n_op)
        late = onward(columns[order[j]], order[j], n_blk) if j < n_blk - 1 else None
        if not kept and not moved:
            break
        waiting = {key: done for key, (_, done) in new.items()}
        kept, moved = lax.optimization_barrier((kept, moved))
        left.update(kept)
        right, tables = moved.get("right", right), moved.get("tables", tables)
        made = moved.get("early", made)
        if "psi" in moved:
            psi[order[j - 1]] = [moved["psi"]]
        if "other" in moved:
            psi[order[j - 2]].append(moved["other"])
    return left, psi, right, tables, made


def place_of():
    return lax.axis_index("blk"), lax.axis_index("op")


def pack_body(n_blk, n_op, shift, _, psi, right_in, *outs):
    n_pair = n_op // 2
    psi_out, right_out, right, sems = outs[:n_blk], outs[n_blk : n_blk + n_pair], outs[-2], outs[-1]
    terms, local, width, _ = right.shape
    cols = local * width // n_op
    per = cols // width
    own_blk, own_op = place_of()
    fetch = pltpu.make_async_copy(right_in, right, sems.at[2 * n_blk])
    fetch.start()
    copies = []
    for d in range(n_blk):
        there = ring_at(ring_place(own_blk, n_blk) + d, n_blk) * n_op
        for h in range(psi_out[d].shape[1] // cols):
            start = pl.multiple_of((there + (own_op ^ h)) * cols, LANES)
            copy = pltpu.make_async_copy(
                psi.at[0, :, pl.ds(start, cols)],
                psi_out[d].at[:, h * cols : (h + 1) * cols],
                sems.at[2 * d + h],
            )
            copy.start()
            copies.append(copy)
    lane = lax.broadcasted_iota(jnp.int32, (16, 2 * cols), 1)
    line = jnp.zeros((16, 2 * cols), jnp.float32)
    for k in range(terms):
        line = jnp.where(lane == k, shift[k].astype(jnp.float32), line)
    square = [lax.broadcasted_iota(jnp.int32, (width, width), axis) for axis in (0, 1)]
    unit = (square[0] == square[1]).astype(jnp.bfloat16)
    fetch.wait()
    for e in range(n_pair):
        for k in range(terms):
            turned = []
            for h in range(2):
                first = (own_op ^ (2 * e) ^ h) * per
                for r in range(per):
                    turned.append(
                        lax.dot_general(
                            right[k, first + r], unit, (((0,), (0,)), ((), ())),
                            preferred_element_type=jnp.float32,
                        )
                    )
            side_by_side = jnp.concatenate(turned, axis=1).astype(jnp.bfloat16)
            right_out[e][k * width : (k + 1) * width] = side_by_side
        right_out[e][terms * width :] = line.astype(jnp.bfloat16)
    for copy in copies:
        copy.wait()


def table_body(n_blk, terms, sector, width, left_diag, right_diag, *refs):
    tails, src, widths, slots, diag, right_out = refs[:-5], *refs[-5:]
    right_out[...] = right_diag[...]
    n_pair = len(tails)
    rows, cols = tails[0].shape
    own_blk, _ = place_of()
    lane = lax.broadcasted_iota(jnp.int32, (16, cols), 1)
    for d in range(n_blk):
        slot = ring_at(ring_place(own_blk, n_blk) - d, n_blk)
        slots[d] = slot
        widths[d] = width[sector[slot]]
    for e in range(n_pair):
        tail = tails[e][rows - 16 :].astype(jnp.float32)
        for k in range(terms):
            shift = jnp.max(jnp.where(lane == k, tail, -1e9)).astype(jnp.int32)
            for t in range(n_blk):
                want = sector[slots[t]] - shift
                found = jnp.int32(n_blk)
                for d in range(n_blk):
                    found = jnp.where(sector[slots[d]] == want, d, found)
                src[(t * n_pair + e) * terms + k] = found
    for d in range(n_blk):
        row = left_diag[pl.ds(slots[d], 1), :]
        diag[d] = jnp.transpose(jnp.broadcast_to(row, (diag.shape[2], row.shape[1])))


def diagonal(diag, right_diag, d, h):
    cols = diag.shape[2]
    _, own_op = place_of()
    start = pl.multiple_of((own_op ^ h) * cols, LANES)
    return diag[d] + right_diag[:, pl.ds(start, cols)]


def row_mask(width, shape):
    return lax.broadcasted_iota(jnp.int32, shape, 0) < width


def fold(x):
    return jnp.sum(x.reshape(-1, 8, x.shape[-1]), axis=0)


def whole(x):
    return jnp.sum(jnp.sum(x, axis=0, keepdims=True), axis=1, keepdims=True)


def spread(values, out):
    lane = lax.broadcasted_iota(jnp.int32, out.shape[1:], 1)
    row = jnp.zeros(out.shape[1:], jnp.float32)
    for j, value in enumerate(values):
        row = jnp.where(lane == j, value, row)
    for d in range(out.shape[0]):
        out[d] = row


def by_block(packed, terms, k):
    rows, cols = packed.shape
    width = (rows - 16) // terms
    lane = lax.broadcasted_iota(jnp.int32, (width, cols), 1)
    block = packed[k * width : (k + 1) * width].astype(jnp.float32)
    parts = []
    for r in range(cols // width):
        inside = (lane >= r * width) & (lane < (r + 1) * width)
        parts.append(jnp.where(inside, block, 0.0).astype(jnp.bfloat16))
    return jnp.concatenate(parts, axis=0)


def left_products(block, left, inter):
    n_terms, rows, cols = inter.shape
    at = 0
    while at < n_terms:
        ops = left(at)
        terms = ops.shape[0]
        prod = jnp.dot(ops.reshape(terms * rows, rows), block, preferred_element_type=jnp.float32)
        inter[at : at + terms] = prod.astype(jnp.bfloat16).reshape(terms, rows, cols)
        at += terms


def sum_terms(src, widths, inter, blocks, out, emit):
    n_blk, n_terms, _, _ = inter.shape
    n_blk -= 1
    for t in range(n_blk):
        total = None
        for j in range(n_terms):
            part = jnp.dot(
                inter[src[t * n_terms + j], j], blocks[j], preferred_element_type=jnp.float32
            )
            total = part if total is None else total + part
        total = jnp.where(row_mask(widths[t], total.shape), total, 0.0)
        out[t] = total.astype(jnp.bfloat16)
        emit(t, total)


def keep(left, left_out, sems):
    copies = []
    for d, line in enumerate(left):
        for e, ref in enumerate(line):
            copies.append(pltpu.make_async_copy(ref, left_out.at[d, e], sems.at[d * len(line) + e]))
            copies[-1].start()
    return copies


def masked(psi, width, out):
    at = 0
    for ref in psi:
        block = ref[...].astype(jnp.float32)
        block = jnp.where(row_mask(width, block.shape), block, 0.0)
        out[:, at : at + block.shape[1]] = block.astype(jnp.bfloat16)
        at += block.shape[1]


def take(refs, counts):
    out = []
    for count in counts:
        out.append(refs[:count])
        refs = refs[count:]
    return out, refs


def products_of(psi, left, widths, first, raw_out, inter):
    for d, line in enumerate(left):
        masked(psi[d], widths[first + d], raw_out.at[d])
        terms = line[0].shape[0]
        left_products(raw_out[d], lambda at: line[at // terms][...], inter.at[d])


def right_products(inter, blocks, sums, d):
    for j in range(blocks.shape[0]):
        prod = jnp.dot(inter[d, j], blocks[j], preferred_element_type=jnp.float32)
        sums[d, j] = prod.astype(sums.dtype)


def early_body(n_pair, counts, widths, *refs):
    left, refs = take(refs, [n_pair] * len(counts))
    (right,), refs = take(refs, [n_pair])
    psi, (raw_out, sums_out, blocks_out, left_out, inter, sems) = take(refs, counts)
    copies = keep(left, left_out, sems)
    n_terms = blocks_out.shape[0]
    terms = n_terms // n_pair
    for j in range(n_terms):
        blocks_out[j] = by_block(right[j // terms], terms, j % terms)
    sums_out[sums_out.shape[0] - 1] = jnp.zeros_like(sums_out[0])
    products_of(psi, left, widths, 0, raw_out, inter)
    for d in range(len(counts)):
        right_products(inter, blocks_out, sums_out, d)
    for copy in copies:
        copy.wait()


def first_body(n_blk, n_pair, counts, src, widths, *refs):
    n_late = len(counts)
    n_early = n_blk - n_late
    left, refs = take(refs, [n_pair] * n_late)
    psi, refs = take(refs, counts)
    blocks, diag, right_diag, _, _, raw_out, held, part_out, left_out, dots_out, inter, sems = refs
    n_terms = blocks.shape[0]
    copies = keep(left, left_out, sems)
    products_of(psi, left, widths, n_early, raw_out.at[n_early:], inter)
    for d in range(n_late):
        right_products(inter, blocks, held.at[n_early:], d)
    cols = diag.shape[2]
    zero = jnp.zeros((8, cols), jnp.float32)
    sums = [zero, zero]

    def emit(d, total):
        for h in range(2):
            part = slice(h * cols, (h + 1) * cols)
            raw = raw_out[d, :, part].astype(jnp.float32)
            image = total[:, part]
            if h == 0:
                image = image + diagonal(diag, right_diag, d, h) * raw
                sums[0] = sums[0] + fold(raw * raw)
            sums[1] = sums[1] + fold(raw * image)

    for t in range(n_blk):
        total = None
        for j in range(n_terms):
            part = held[src[t * n_terms + j], j].astype(jnp.float32)
            total = part if total is None else total + part
        total = jnp.where(row_mask(widths[t], total.shape), total, 0.0)
        part_out[t] = total.astype(jnp.bfloat16)
        emit(t, total)
    spread([whole(x) for x in sums], dots_out)
    for copy in copies:
        copy.wait()


def send_rows(e, send, d, *refs):
    _, own_op = place_of()
    step = send.shape[2]
    rows = pl.ds(pl.multiple_of((own_op ^ e) * step, step), step)
    for j, ref in enumerate(refs):
        send[j, d] = ref[d, rows].astype(send.dtype)


def total_of(mine, other, d, h, cols):
    own = mine[d, :, h * cols : (h + 1) * cols].astype(jnp.float32)
    return own + other[d, :, (1 - h) * cols : (2 - h) * cols].astype(jnp.float32)


def sigma_body(mine, other, raw_in, diag, right_diag, sig_out, *sends):
    n_blk, _, cols = diag.shape
    for d in range(n_blk):
        for h in range(2):
            part = slice(h * cols, (h + 1) * cols)
            raw = raw_in[d, :, part].astype(jnp.float32)
            sigma = total_of(mine, other, d, h, cols) + diagonal(diag, right_diag, d, h) * raw
            sig_out[d, :, part] = sigma
        for e, send in enumerate(sends, 1):
            send_rows(2 * e, send, d, raw_in, sig_out)


def norm_theta(parts, count):
    tot = jnp.sum(parts, axis=0) * (1.0 / count)
    scale = lax.rsqrt(tot[:, 0:1] + EPS)
    return scale, tot[:, 1:2] * scale * scale


def second_body(n_blk, count, src, widths, left_early, left_late, *refs):
    blocks, refs = refs[0], refs[1:]
    parts, raw_in, sig, diag, right_diag, dots_out, own_out = refs[:7]
    sends, (inter, corr, fld, part_out, held, sems) = refs[7:-6], refs[-6:]
    copies = []
    n_early = left_early.shape[0]
    for d in range(n_blk):
        kept = left_early.at[d] if d < n_early else left_late.at[d - n_early]
        copies.append(pltpu.make_async_copy(kept, held.at[d], sems.at[d]))
        copies[-1].start()
    inter[n_blk] = jnp.zeros_like(inter[n_blk])
    scale, theta = norm_theta(parts[...], count)
    cols = diag.shape[2]
    halves = []
    for h in range(2):
        part = slice(h * cols, (h + 1) * cols)
        vv = vc = vs = jnp.zeros((8, cols), jnp.float32)
        for d in range(n_blk):
            vec = raw_in[d, :, part].astype(jnp.float32) * scale
            sigma = sig[d, :, part] * scale
            den = diagonal(diag, right_diag, d, h) - theta
            item = (sigma - theta * vec) * den / jnp.maximum(den * den, 0.25)
            corr[d, :, part] = item
            vv, vc = vv + fold(vec * vec), vc + fold(vec * item)
            if h == 0:
                vs = vs + fold(vec * sigma)
        halves.append((whole(vv), whole(vc), vs))
    along = (halves[0][1] + halves[1][1]) / jnp.maximum(halves[0][0] + halves[1][0], 1e-30)
    terms = held.shape[2]
    for copy in copies:
        copy.wait()
    for d in range(n_blk):
        for h in range(2):
            part = slice(h * cols, (h + 1) * cols)
            vec = raw_in[d, :, part].astype(jnp.float32) * scale
            fld[d, :, part] = (corr[d, :, part] - along * vec).astype(jnp.bfloat16)
        left_products(fld[d], lambda at: held[d, at // terms], inter.at[d])
    zero = jnp.zeros((8, cols), jnp.float32)
    sums = [zero for _ in range(5)]

    def emit(d, total):
        for h in range(2):
            part = slice(h * cols, (h + 1) * cols)
            field = fld[d, :, part].astype(jnp.float32)
            raw = raw_in[d, :, part].astype(jnp.float32)
            image = total[:, part]
            if h == 0:
                image = image + diagonal(diag, right_diag, d, h) * field
                for j, prod in enumerate((field * field, raw * field, field * sig[d, :, part])):
                    sums[j] = sums[j] + fold(prod)
            sums[3] = sums[3] + fold(raw * image)
            sums[4] = sums[4] + fold(field * image)
        for e, send in enumerate(sends, 1):
            send_rows(e, send, d, *((part_out,) if e % 2 else (fld, part_out)))
        rows = pl.ds(pl.multiple_of(own_op * step, step), step)
        for j, ref in enumerate((raw_in, sig, fld, part_out)):
            own_out[j, d] = ref[d, rows].astype(own_out.dtype)

    _, own_op = place_of()
    step = own_out.shape[2]
    sum_terms(src, widths, inter, blocks, part_out, emit)
    vv, vc, vs = halves[0]
    ff, vf, fs, vt, ft = (whole(x) for x in sums)
    spread([vv, vc, whole(vs), ff, vf * scale, fs * scale, vt * scale, ft], dots_out)


def ritz_pair(theta, h_mix, h_two):
    diff, twice = theta - h_two, 2.0 * h_mix
    size = jnp.sqrt(diff * diff + twice * twice)
    some = size > 0.0
    safe = jnp.where(some, size, 1.0)
    big = jnp.sqrt(0.5 + 0.5 * jnp.abs(diff) / safe)
    small = 0.5 * jnp.abs(twice) / (safe * big)
    sine = jnp.where(diff >= 0.0, small, big)
    cosine = jnp.where(diff >= 0.0, big, small)
    sine = jnp.where(some, sine, 0.0)
    cosine = jnp.where(some, cosine, 1.0)
    upward = (twice > 0.0) | ((twice == 0.0) & (diff < 0.0))
    return sine, jnp.where(upward, -cosine, cosine), 0.5 * (theta + h_two) - 0.5 * size


def third_body(n_blk, n_op, count, slots, parts1, parts2, diag, right_diag, own, *refs):
    n_far = n_op // 2 - 1
    got1, got2 = refs[:n_far], refs[n_far : n_far + n_op - 1]
    new_out, res_out, energy_out, new, res, sems = refs[n_far + n_op - 1 :]
    step, cols = new.shape[1], new.shape[2] // n_op
    own_blk, own_op = place_of()
    scale, theta = norm_theta(parts1[...], count)
    pairs = parts2[...].reshape(n_blk * n_op // 2, 2, *parts2.shape[1:])
    pairs = pairs[:, 0] + pairs[:, 1]
    vv, vc, vs, ff, vf, fs, vt, ft = (pairs[:, 0, j : j + 1] for j in range(8))

    def mean(x):
        return jnp.sum(x, axis=0, keepdims=True) * (1.0 / count)

    def nearest(vv, vc):
        return vc / jnp.maximum(vv, 1e-30)

    along = mean(vc)
    beta = nearest(vv, vc) - along
    norm_sq = mean(ff + 2.0 * beta * vf + beta * beta * vv)
    unit = lax.rsqrt(jnp.maximum(norm_sq, 0.0) + EPS)
    v_s1 = unit * mean(vt + beta * vs)
    u_s0 = unit * mean(fs + beta * vs)
    u_s1 = unit * unit * mean(ft + beta * (vt + fs) + beta * beta * vs)
    cv, cu, energy = ritz_pair(theta, 0.5 * (v_s1 + u_s0), u_s1)
    energy_out[0] = jnp.max(energy)
    cu = cu * unit
    mine = pl.ds(pl.multiple_of(own_op * step, step), step)
    on_vec = []
    for e in range(0, n_op, 2):
        there = own_blk * n_op + (own_op ^ e)
        pair = parts2[there] + parts2[own_blk * n_op + (own_op ^ e ^ 1)]
        on_vec.append(cv + cu * (nearest(pair[:, 0:1], pair[:, 1:2]) - along))
    copies = []
    for d in range(n_blk):
        for e in range(0, n_op, 2):
            blocks = [own.at[j] for j in range(4)]
            if e:
                far, near = got1[e // 2 - 1], got2[e - 1]
                blocks = far.at[0], far.at[1], near.at[0], near.at[1]
            for h in range(2):
                at = pl.multiple_of((own_op ^ e ^ h) * cols, LANES)
                part, crossed = slice(h * cols, (h + 1) * cols), slice((1 - h) * cols, (2 - h) * cols)
                dmat = diag[d, mine] + right_diag[:, pl.ds(at, cols)]
                raw, sigma, fld, image = (x[d, :, part].astype(jnp.float32) for x in blocks)
                image = image + got2[e][0, d, :, crossed].astype(jnp.float32) + dmat * fld
                newvec = on_vec[e // 2] * (raw * scale) + cu * fld
                rest = on_vec[e // 2] * (sigma * scale) + cu * image - energy * newvec
                new[d, :, pl.ds(at, cols)] = newvec.astype(jnp.bfloat16)
                res[d, :, pl.ds(at, cols)] = rest.astype(jnp.bfloat16)
        for j, (held, out) in enumerate(((new, new_out), (res, res_out))):
            copies.append(pltpu.make_async_copy(held.at[d], out.at[slots[d]], sems.at[2 * d + j]))
            copies[-1].start()
    for copy in copies:
        copy.wait()


def per_device(
    psi, left_ops, right_ops, term_shift, slot_sector, sector_width, diag_left, diag_right
):
    n_blk, n_op = lax.axis_size("blk"), lax.axis_size("op")
    _, rows, ncols = psi.shape
    terms, _, width, _ = right_ops.shape
    n_pair = n_op // 2
    cols = diag_right.shape[0] // n_op
    step = rows // n_op
    count = float(n_blk * rows * ncols)
    n_dev = n_blk * n_op
    bf16, f32, i32 = jnp.bfloat16, jnp.float32, jnp.int32
    last = sorted(range(1, n_blk), key=lambda d: min(d, n_blk - d))[-1]

    def pack():
        first = swap(term_shift, 1, n_op)
        sent = kernel(
            functools.partial(pack_body, n_blk, n_op),
            [(term_shift, SMEM), (first, SMEM), (psi, HBM), (right_ops, HBM)],
            [((rows, 2 * cols if d in (0, last) else cols), bf16, VMEM) for d in range(n_blk)]
            + [((terms * width + 16, 2 * cols), bf16, VMEM)] * n_pair,
            [pltpu.VMEM(right_ops.shape, bf16), pltpu.SemaphoreType.DMA((2 * n_blk + 1,))],
            nbytes=1 << 20,
        )
        return sent[:n_blk], sent[n_blk:]

    def table(right):
        return kernel(
            functools.partial(table_body, n_blk, terms),
            [(slot_sector, SMEM), (sector_width, SMEM), (diag_left, VMEM), (diag_right[None], VMEM)]
            + [(block, VMEM) for block in right],
            [((n_blk * n_pair * terms,), i32, SMEM)]
            + [((n_blk,), i32, SMEM)] * 2
            + [((n_blk, rows, LANES), f32, VMEM), ((1, n_op * cols), f32, VMEM)],
        )

    def inputs(left, psi, those):
        blocks = [left[d, 2 * e] for d in those for e in range(n_pair)]
        halves = [half for d in those for half in psi[d]]
        return [(x, VMEM) for x in blocks], [(x, VMEM) for x in halves], [len(psi[d]) for d in those]

    narrow = ((n_blk, rows, 2 * cols), bf16, VMEM)

    def early(left, psi, right, n_early, tables):
        left_ins, psi_ins, counts = inputs(left, psi, range(n_early))
        return kernel(
            functools.partial(early_body, n_pair, counts),
            [(tables[1], SMEM)] + left_ins + [(x, VMEM) for x in right] + psi_ins,
            [
                narrow,
                ((n_blk + 1, n_pair * terms, rows, 2 * cols), bf16, VMEM),
                ((n_pair * terms, 2 * cols, 2 * cols), bf16, VMEM),
                ((n_early, n_pair, terms, rows, rows), bf16, HBM),
            ],
            [
                pltpu.VMEM((n_early, n_pair * terms, rows, 2 * cols), bf16),
                pltpu.SemaphoreType.DMA((n_early * n_pair,)),
            ],
            flops=2 * n_early * rows * rows * 2 * cols * terms * n_pair,
            nbytes=4 << 20,
        )

    left, psi_by, right, (src, widths, slots, *both), (raw_early, products, blocks, left_early) = gather(
        left_ops[:, 0], n_blk, n_op, pack, table, early
    )
    n_early = left_early.shape[0]
    n_late = n_blk - n_early
    left_ins, psi_ins, counts = inputs(left, psi_by, range(n_early, n_blk))
    diags = [(x, VMEM) for x in both]

    tables = [(src, SMEM), (widths, SMEM)]
    dots = ((n_dev, 1, LANES), f32, VMEM)
    wide = ((n_blk, rows, 2 * cols), f32, VMEM)
    sends = [((2 - e % 2, n_blk, step, 2 * cols), bf16, VMEM) for e in range(1, n_op)]
    inter = pltpu.VMEM((n_blk + 1, n_pair * terms, rows, 2 * cols), bf16)
    left_late = (n_late, n_pair, terms, rows, rows)
    cost = dict(flops=2 * n_blk * rows * 2 * cols * terms * n_pair * (rows + 2 * cols), nbytes=6 << 20)

    def totals(parts):
        return lax.all_to_all(parts, ("blk", "op"), 0, 0, tiled=True)

    first_ins = tables + left_ins + psi_ins + [(blocks, VMEM)] + diags
    raw, _, part1, kept, dots1 = kernel(
        functools.partial(first_body, n_blk, n_pair, counts),
        first_ins + [(raw_early, VMEM), (products, VMEM)],
        [narrow, (products.shape, bf16, VMEM), narrow, (left_late, bf16, HBM), dots],
        [
            pltpu.VMEM((n_late, n_pair * terms, rows, 2 * cols), bf16),
            pltpu.SemaphoreType.DMA((n_late * n_pair,)),
        ],
        in_place={len(first_ins): 0, len(first_ins) + 1: 1},
        **cost,
    )
    parts1 = totals(dots1)
    sig, *out1 = kernel(
        sigma_body,
        [(x, VMEM) for x in (part1, swap(part1, 1, n_op), raw)] + diags,
        [wide] + sends[1::2],
        nbytes=4 << 20,
    )
    got1 = [swap(block, 2 * e, n_op) for e, block in enumerate(out1, 1)]
    dots2, own, *out2 = kernel(
        functools.partial(second_body, n_blk, count),
        tables + [(left_early, HBM), (kept, HBM), (blocks, VMEM)]
        + [(x, VMEM) for x in (parts1, raw, sig)] + diags,
        [dots, ((4, n_blk, step, 2 * cols), bf16, VMEM)] + sends,
        [
            inter,
            pltpu.VMEM((n_blk, rows, 2 * cols), f32),
            pltpu.VMEM((n_blk, rows, 2 * cols), bf16),
            pltpu.VMEM((n_blk, rows, 2 * cols), bf16),
            pltpu.VMEM((n_blk, *left_late[1:]), bf16),
            pltpu.SemaphoreType.DMA((n_blk,)),
        ],
        flops=4 * cost["flops"],
        nbytes=24 << 20,
    )
    near, got1 = lax.optimization_barrier((out2[0], got1))
    parts2 = totals(dots2)
    got2 = [swap(near, 1, n_op)] + [swap(block, e, n_op) for e, block in enumerate(out2[1:], 2)]
    final = ((n_blk, step, n_op * cols), bf16, HBM)
    new, res, energy = kernel(
        functools.partial(third_body, n_blk, n_op, count),
        [(slots, SMEM)] + [(x, VMEM) for x in (parts1, parts2)] + diags
        + [(x, VMEM) for x in (own, *got1, *got2)],
        [final, final, ((1,), f32, SMEM)],
        [pltpu.VMEM(final[0], bf16)] * 2 + [pltpu.SemaphoreType.DMA((2 * n_blk,))],
        nbytes=4 << 20,
    )
    return new, res, energy


def solution(mesh):
    placed = (
        P(("grp", "blk"), None, None),
        P("op", ("grp", "blk"), None, None),
        P("op", ("grp", "blk"), None, None),
        P("op"),
        P("grp"),
        P("grp"),
        P("grp", None),
        P(("grp", "blk")),
    )

    def body(*args):
        psi, left_ops, right_ops, diag_right = args[0], args[1], args[2], args[7]
        n_op = mesh.shape["op"]
        cols = diag_right.shape[0] // n_op
        fits = (
            psi.shape[0] == 1
            and diag_right.shape[0] % n_op == 0
            and cols == LANES
            and n_op % 2 == 0
            and cols % right_ops.shape[2] == 0
            and cols // right_ops.shape[2] * n_op == right_ops.shape[1]
            and psi.shape[1] % (16 * n_op) == 0
            and n_op & (n_op - 1) == 0
            and mesh.shape["blk"] > n_op.bit_length() - 1
        )
        return (per_device if fits else per_device_general)(*args)

    return jax.shard_map(
        body,
        mesh=mesh,
        in_specs=placed,
        out_specs=(P("grp", "op", "blk"), P("grp", "op", "blk"), P("grp")),
        check_vma=False,
    )
```

```python
import functools

import jax
import jax.numpy as jnp
from jax import lax
from jax.experimental import pallas as pl
from jax.experimental.pallas import tpu as pltpu
from jax.sharding import PartitionSpec as P

EPS = 1e-06
LANES = 128
VMEM_LIMIT = 20 * 1024 * 1024


def per_device_general(
    psi, left_ops, right_ops, term_shift, slot_sector, sector_width, diag_left, diag_right
):
    sec_dev, rows, ncols = psi.shape
    nsec = slot_sector.shape[0]
    terms_dev = left_ops.shape[0]
    right_local = right_ops.shape[1]
    right_width = right_ops.shape[2]
    local_cols = diag_right.shape[0]
    count = float(nsec * rows * ncols)
    match = slot_sector[:, None] == jnp.arange(nsec)[None, :]
    widths = jnp.sum(jnp.where(match, sector_width[None, :], 0), axis=1)
    mask_all = (jnp.arange(rows)[None, :] < widths[:, None]).astype(jnp.float32)
    own_mask = lax.dynamic_slice_in_dim(mask_all, lax.axis_index("blk") * sec_dev, sec_dev, 0)
    raw = psi.astype(jnp.float32) * own_mask[:, :, None]
    squares = lax.psum(jnp.sum(raw * raw), "blk")
    v_left = (raw * lax.rsqrt(squares / count + EPS)).astype(jnp.bfloat16)
    onehots = (
        slot_sector[None, None, :] == slot_sector[None, :, None] - term_shift[:, None, None]
    ).astype(jnp.bfloat16)
    op_rows = rows // lax.axis_size("op")
    op_start = lax.axis_index("op") * op_rows
    dmat = diag_left[:, :, None] + diag_right[None, None, :]

    def left_local(field):
        return jnp.einsum(
            "ksij,sjc->ksic", left_ops, field, preferred_element_type=jnp.float32
        ).astype(jnp.bfloat16)

    def right_part(moved_in):
        flat = moved_in.reshape(terms_dev, nsec, rows * local_cols)
        shifted = jnp.einsum(
            "kts,ksx->ktx", onehots, flat, preferred_element_type=jnp.float32
        ).astype(jnp.bfloat16)
        shifted = shifted.reshape(terms_dev, nsec, rows, right_local, right_width)
        accum = jnp.einsum(
            "ktwrc,krdc->twrd", shifted, right_ops, preferred_element_type=jnp.float32
        )
        return accum.reshape(nsec, rows, local_cols) * mask_all[:, :, None]

    def op_total(partial_value):
        return lax.psum(partial_value.astype(jnp.bfloat16), "op").astype(jnp.float32)

    def final_rows(array):
        return lax.dynamic_slice_in_dim(array, op_start, op_rows, 1)

    def reduce_dots(values):
        sums = lax.psum(values, "blk")
        return tuple((item / count for item in sums))

    moved_first, v_moved = (
        lax.all_to_all(left_local(v_left), "blk", split_axis=3, concat_axis=1, tiled=True),
        lax.all_to_all(v_left[None], "blk", split_axis=3, concat_axis=1, tiled=True),
    )
    v_right = v_moved[0]
    vec32 = v_right.astype(jnp.float32)
    first_sigma = op_total(right_part(moved_first)) + dmat * vec32
    theta = reduce_dots((jnp.sum(vec32 * first_sigma),))[0]
    resid = first_sigma - theta * vec32
    den = dmat - theta
    corr = resid * den / jnp.maximum(den * den, 0.25)
    along = reduce_dots((jnp.sum(vec32 * corr),))[0]
    orth = corr - along * vec32
    norm_sq = reduce_dots((jnp.sum(orth * orth),))[0]
    update = (orth * lax.rsqrt(norm_sq + EPS)).astype(jnp.bfloat16)
    upd32 = update.astype(jnp.float32)
    upd_left = lax.all_to_all(update, "blk", split_axis=0, concat_axis=2, tiled=True)
    moved_second = lax.all_to_all(
        left_local(upd_left), "blk", split_axis=3, concat_axis=1, tiled=True
    )
    second_sigma = op_total(right_part(moved_second)) + dmat * upd32
    v_s1, u_s0, u_s1 = reduce_dots(
        (jnp.sum(vec32 * second_sigma), jnp.sum(upd32 * first_sigma), jnp.sum(upd32 * second_sigma))
    )
    h_mix = 0.5 * (v_s1 + u_s0)
    coef_v, coef_u, energy = ritz(theta, h_mix, u_s1)
    newvec = coef_v * vec32 + coef_u * upd32
    image = coef_v * first_sigma + coef_u * second_sigma
    new_out = final_rows(newvec.astype(jnp.bfloat16))
    res_out = final_rows((image - energy * newvec).astype(jnp.bfloat16))
    return (new_out, res_out, jnp.reshape(energy, (1,)))


def ritz(theta, h_mix, h_two):
    angle = 0.5 * jnp.arctan2(2.0 * h_mix, theta - h_two)
    sine = jnp.sin(angle)
    flip = jnp.where(sine > 0, -1.0, 1.0)
    coef_v = -sine * flip
    coef_u = jnp.cos(angle) * flip
    half = 0.5 * (theta - h_two)
    energy = 0.5 * (theta + h_two) - jnp.sqrt(half * half + h_mix * h_mix)
    return coef_v, coef_u, energy


VMEM, SMEM, HBM = pltpu.VMEM, pltpu.SMEM, pltpu.HBM


def kernel(body, ins, outs, scratch=(), flops=0, nbytes=0):
    return pl.pallas_call(
        body,
        out_shape=[
            HBM(shape, dtype) if space == HBM else jax.ShapeDtypeStruct(shape, dtype)
            for shape, dtype, space in outs
        ],
        in_specs=[pl.BlockSpec(memory_space=space) for _, space in ins],
        out_specs=[pl.BlockSpec(memory_space=space) for _, _, space in outs],
        scratch_shapes=list(scratch),
        compiler_params=pltpu.CompilerParams(vmem_limit_bytes=VMEM_LIMIT),
        cost_estimate=pl.CostEstimate(flops=flops, bytes_accessed=nbytes, transcendentals=0),
    )(*[pltpu.with_memory_space_constraint(x, HBM) if space == HBM else x for x, space in ins])


def ring_at(place, n_blk):
    place = place % n_blk if isinstance(place, int) else lax.rem(place + n_blk, n_blk)
    even, odd = 2 * place, 2 * (n_blk - place) - 1
    if isinstance(place, int):
        return even if even < n_blk else odd
    return jnp.where(even < n_blk, even, odd)


def ring_place(index, n_blk):
    return jnp.where(lax.rem(index, 2) == 1, n_blk - (index + 1) // 2, index // 2)


def onward(block, d, n_blk):
    pairs = [(ring_at(i, n_blk), ring_at(i + d, n_blk)) for i in range(n_blk)]
    return lax.ppermute(block, "blk", pairs)


def swap(block, e, n_op):
    return lax.ppermute(block, "op", [(i, i ^ e) for i in range(n_op)])


def gather(own, n_blk, n_op, pack, table, early):
    bits = [1 << b for b in reversed(range(1, n_op.bit_length() - 1))]
    order = sorted(range(1, n_blk), key=lambda d: (min(d, n_blk - d), -d))
    left, psi, right, tables, columns = {(0, 0): own}, {}, None, None, None
    waiting, across, late, made = {(0, 0): 0}, {}, None, None
    for j in range(n_blk + len(bits)):
        new, moved = {}, {}
        for (d, e), done in waiting.items():
            if e == 0 and d + 1 < n_blk:
                new[d + 1, 0] = onward(left[d, 0], 1, n_blk), 0
            for b in range(done, len(bits)):
                new[d, e ^ bits[b]] = swap(left[d, e], bits[b], n_op), b + 1
        left.update({key: block for key, (block, _) in new.items()})
        kept = {key: block for key, (block, _) in new.items() if key[1] == 0}
        kept.update(across)
        across = {key: block for key, (block, _) in new.items() if key[1] != 0}
        if late is not None:
            moved["psi"] = late
        if j == 0:
            columns, packed = pack()
            right = [packed[0]]
            right += [swap(part, 2 * e, n_op) for e, part in enumerate(packed[1:], 1)]
            moved["columns"] = columns
        if j == 0:
            moved["right"] = right
        if j == 1:
            moved["tables"] = table(right)
        if j == n_blk - 1 and j >= len(bits) + 1:
            n_early = min(2, n_blk - 1)
            psi[0] = [columns[0]]
            moved["other"] = swap(psi[order[j - 2]][0], 1, n_op)
            at_hand = {**psi, order[j - 2]: psi[order[j - 2]] + [moved["other"]]}
            moved["early"] = early(left, at_hand, n_early, tables)
        elif 2 <= j < n_blk:
            moved["other"] = swap(psi[order[j - 2]][0], 1, n_op)
        late = onward(columns[order[j]], order[j], n_blk) if j < n_blk - 1 else None
        if not kept:
            break
        waiting = {key: done for key, (_, done) in new.items()}
        kept, moved = lax.optimization_barrier((kept, moved))
        left.update(kept)
        right, tables = moved.get("right", right), moved.get("tables", tables)
        columns = moved.get("columns", columns)
        made = moved.get("early", made)
        if "psi" in moved:
            psi[order[j - 1]] = [moved["psi"]]
        if "other" in moved:
            psi[order[j - 2]].append(moved["other"])
    return left, psi, right, tables, made


def place_of():
    return lax.axis_index("blk"), lax.axis_index("op")


def pack_body(n_blk, n_op, shift, _, psi, right_in, *outs):
    n_pair = n_op // 2
    psi_out, right_out, right, sems = outs[:n_blk], outs[n_blk : n_blk + n_pair], outs[-2], outs[-1]
    terms, local, width, _ = right.shape
    cols = local * width // n_op
    per = cols // width
    own_blk, own_op = place_of()
    fetch = pltpu.make_async_copy(right_in, right, sems.at[2 * n_blk])
    fetch.start()
    copies = []
    for d in range(n_blk):
        there = ring_at(ring_place(own_blk, n_blk) + d, n_blk) * n_op
        for h in range(psi_out[d].shape[1] // cols):
            start = pl.multiple_of((there + (own_op ^ h)) * cols, LANES)
            copy = pltpu.make_async_copy(
                psi.at[0, :, pl.ds(start, cols)],
                psi_out[d].at[:, h * cols : (h + 1) * cols],
                sems.at[2 * d + h],
            )
            copy.start()
            copies.append(copy)
    lane = lax.broadcasted_iota(jnp.int32, (16, 2 * cols), 1)
    line = jnp.zeros((16, 2 * cols), jnp.float32)
    for k in range(terms):
        line = jnp.where(lane == k, shift[k].astype(jnp.float32), line)
    square = [lax.broadcasted_iota(jnp.int32, (width, width), axis) for axis in (0, 1)]
    unit = (square[0] == square[1]).astype(jnp.bfloat16)
    fetch.wait()
    for e in range(n_pair):
        for k in range(terms):
            turned = []
            for h in range(2):
                first = (own_op ^ (2 * e) ^ h) * per
                for r in range(per):
                    turned.append(
                        lax.dot_general(
                            right[k, first + r], unit, (((0,), (0,)), ((), ())),
                            preferred_element_type=jnp.float32,
                        )
                    )
            side_by_side = jnp.concatenate(turned, axis=1).astype(jnp.bfloat16)
            right_out[e][k * width : (k + 1) * width] = side_by_side
        right_out[e][terms * width :] = line.astype(jnp.bfloat16)
    for copy in copies:
        copy.wait()


def table_body(n_blk, terms, sector, width, left_diag, right_diag, *refs):
    tails, src, widths, slots, diag, right_out = refs[:-5], *refs[-5:]
    right_out[...] = right_diag[...]
    n_pair = len(tails)
    rows, cols = tails[0].shape
    own_blk, _ = place_of()
    lane = lax.broadcasted_iota(jnp.int32, (16, cols), 1)
    for d in range(n_blk):
        slot = ring_at(ring_place(own_blk, n_blk) - d, n_blk)
        slots[d] = slot
        widths[d] = width[sector[slot]]
    for e in range(n_pair):
        tail = tails[e][rows - 16 :].astype(jnp.float32)
        for k in range(terms):
            shift = jnp.max(jnp.where(lane == k, tail, -1e9)).astype(jnp.int32)
            for t in range(n_blk):
                want = sector[slots[t]] - shift
                found = jnp.int32(n_blk)
                for d in range(n_blk):
                    found = jnp.where(sector[slots[d]] == want, d, found)
                src[(t * n_pair + e) * terms + k] = found
    for d in range(n_blk):
        row = left_diag[pl.ds(slots[d], 1), :]
        diag[d] = jnp.transpose(jnp.broadcast_to(row, (diag.shape[2], row.shape[1])))


def diagonal(diag, right_diag, d, h):
    cols = diag.shape[2]
    _, own_op = place_of()
    start = pl.multiple_of((own_op ^ h) * cols, LANES)
    return diag[d] + right_diag[:, pl.ds(start, cols)]


def row_mask(width, shape):
    return lax.broadcasted_iota(jnp.int32, shape, 0) < width


def fold(x):
    return jnp.sum(x.reshape(-1, 8, x.shape[-1]), axis=0)


def whole(x):
    return jnp.sum(jnp.sum(x, axis=0, keepdims=True), axis=1, keepdims=True)


def spread(values, out):
    lane = lax.broadcasted_iota(jnp.int32, out.shape[1:], 1)
    row = jnp.zeros(out.shape[1:], jnp.float32)
    for j, value in enumerate(values):
        row = jnp.where(lane == j, value, row)
    for d in range(out.shape[0]):
        out[d] = row


def by_block(packed, terms, k):
    rows, cols = packed.shape
    width = (rows - 16) // terms
    lane = lax.broadcasted_iota(jnp.int32, (width, cols), 1)
    block = packed[k * width : (k + 1) * width].astype(jnp.float32)
    parts = []
    for r in range(cols // width):
        inside = (lane >= r * width) & (lane < (r + 1) * width)
        parts.append(jnp.where(inside, block, 0.0).astype(jnp.bfloat16))
    return jnp.concatenate(parts, axis=0)


def left_products(block, left, inter):
    n_terms, rows, cols = inter.shape
    at = 0
    while at < n_terms:
        ops = left(at)
        terms = ops.shape[0]
        prod = jnp.dot(ops.reshape(terms * rows, rows), block, preferred_element_type=jnp.float32)
        inter[at : at + terms] = prod.astype(jnp.bfloat16).reshape(terms, rows, cols)
        at += terms


def sum_terms(src, widths, inter, right, out, emit):
    n_blk, n_terms, _, _ = inter.shape
    n_blk -= 1
    terms = n_terms // len(right)
    turned = [by_block(right[j // terms], terms, j % terms) for j in range(n_terms)]
    for t in range(n_blk):
        total = None
        for j in range(n_terms):
            part = jnp.dot(
                inter[src[t * n_terms + j], j], turned[j], preferred_element_type=jnp.float32
            )
            total = part if total is None else total + part
        total = jnp.where(row_mask(widths[t], total.shape), total, 0.0)
        out[t] = total.astype(jnp.bfloat16)
        emit(t, total)


def keep(left, left_out, sems):
    copies = []
    for d, line in enumerate(left):
        for e, ref in enumerate(line):
            copies.append(pltpu.make_async_copy(ref, left_out.at[d, e], sems.at[d * len(line) + e]))
            copies[-1].start()
    return copies


def masked(psi, width, out):
    at = 0
    for ref in psi:
        block = ref[...].astype(jnp.float32)
        block = jnp.where(row_mask(width, block.shape), block, 0.0)
        out[:, at : at + block.shape[1]] = block.astype(jnp.bfloat16)
        at += block.shape[1]


def take(refs, counts):
    out = []
    for count in counts:
        out.append(refs[:count])
        refs = refs[count:]
    return out, refs


def products_of(psi, left, widths, first, raw_out, inter):
    for d, line in enumerate(left):
        masked(psi[d], widths[first + d], raw_out.at[d])
        terms = line[0].shape[0]
        left_products(raw_out[d], lambda at: line[at // terms][...], inter.at[d])


def early_body(n_pair, counts, widths, *refs):
    left, refs = take(refs, [n_pair] * len(counts))
    psi, (raw_out, inter_out, left_out, sems) = take(refs, counts)
    copies = keep(left, left_out, sems)
    products_of(psi, left, widths, 0, raw_out, inter_out)
    for copy in copies:
        copy.wait()


def first_body(n_blk, n_pair, counts, src, widths, *refs):
    n_late = len(counts)
    n_early = n_blk - n_late
    left, refs = take(refs, [n_pair] * n_late)
    (right,), refs = take(refs, [n_pair])
    psi, refs = take(refs, counts)
    raw_in, inter_in, diag, right_diag, part_out, raw_out, left_out, dots_out, inter, sems = refs
    copies = keep(left, left_out, sems)
    for j, (given, own) in enumerate(((inter_in, inter), (raw_in, raw_out))):
        copies.append(
            pltpu.make_async_copy(given, own.at[:n_early], sems.at[n_late * n_pair + j])
        )
        copies[-1].start()
    inter[n_blk] = jnp.zeros_like(inter[n_blk])
    products_of(
        psi, left, widths, n_early, raw_out.at[n_early:], inter.at[n_early:n_blk]
    )
    for copy in copies:
        copy.wait()
    cols = diag.shape[2]
    zero = jnp.zeros((8, cols), jnp.float32)
    sums = [zero, zero]

    def emit(d, total):
        for h in range(2):
            part = slice(h * cols, (h + 1) * cols)
            raw = raw_out[d, :, part].astype(jnp.float32)
            image = total[:, part]
            if h == 0:
                image = image + diagonal(diag, right_diag, d, h) * raw
                sums[0] = sums[0] + fold(raw * raw)
            sums[1] = sums[1] + fold(raw * image)

    sum_terms(src, widths, inter, right, part_out, emit)
    spread([whole(x) for x in sums], dots_out)


def send_rows(e, send, d, *refs):
    _, own_op = place_of()
    step = send.shape[2]
    rows = pl.ds(pl.multiple_of((own_op ^ e) * step, step), step)
    for j, ref in enumerate(refs):
        send[j, d] = ref[d, rows].astype(send.dtype)


def total_of(mine, other, d, h, cols):
    own = mine[d, :, h * cols : (h + 1) * cols].astype(jnp.float32)
    return own + other[d, :, (1 - h) * cols : (2 - h) * cols].astype(jnp.float32)


def sigma_body(mine, other, raw_in, diag, right_diag, sig_out, *sends):
    n_blk, _, cols = diag.shape
    for d in range(n_blk):
        for h in range(2):
            part = slice(h * cols, (h + 1) * cols)
            raw = raw_in[d, :, part].astype(jnp.float32)
            sigma = total_of(mine, other, d, h, cols) + diagonal(diag, right_diag, d, h) * raw
            sig_out[d, :, part] = sigma
        for e, send in enumerate(sends, 1):
            send_rows(2 * e, send, d, raw_in, sig_out)


def norm_theta(parts, count):
    tot = jnp.sum(parts, axis=0) * (1.0 / count)
    scale = lax.rsqrt(tot[:, 0:1] + EPS)
    return scale, tot[:, 1:2] * scale * scale


def second_body(n_blk, n_pair, count, src, widths, left_early, left_late, *refs):
    right, refs = refs[:n_pair], refs[n_pair:]
    parts, raw_in, sig, diag, right_diag, dots_out, own_out = refs[:7]
    sends, (inter, corr, fld, part_out, held, sems) = refs[7:-6], refs[-6:]
    copies = []
    n_early = left_early.shape[0]
    for d in range(n_blk):
        kept = left_early.at[d] if d < n_early else left_late.at[d - n_early]
        copies.append(pltpu.make_async_copy(kept, held.at[d], sems.at[d]))
        copies[-1].start()
    inter[n_blk] = jnp.zeros_like(inter[n_blk])
    scale, theta = norm_theta(parts[...], count)
    cols = diag.shape[2]
    halves = []
    for h in range(2):
        part = slice(h * cols, (h + 1) * cols)
        vv = vc = vs = jnp.zeros((8, cols), jnp.float32)
        for d in range(n_blk):
            vec = raw_in[d, :, part].astype(jnp.float32) * scale
            sigma = sig[d, :, part] * scale
            den = diagonal(diag, right_diag, d, h) - theta
            item = (sigma - theta * vec) * den / jnp.maximum(den * den, 0.25)
            corr[d, :, part] = item
            vv, vc = vv + fold(vec * vec), vc + fold(vec * item)
            if h == 0:
                vs = vs + fold(vec * sigma)
        halves.append((whole(vv), whole(vc), vs))
    along = (halves[0][1] + halves[1][1]) / jnp.maximum(halves[0][0] + halves[1][0], 1e-30)
    terms = held.shape[2]
    for copy in copies:
        copy.wait()
    for d in range(n_blk):
        for h in range(2):
            part = slice(h * cols, (h + 1) * cols)
            vec = raw_in[d, :, part].astype(jnp.float32) * scale
            fld[d, :, part] = (corr[d, :, part] - along * vec).astype(jnp.bfloat16)
        left_products(fld[d], lambda at: held[d, at // terms], inter.at[d])
    zero = jnp.zeros((8, cols), jnp.float32)
    sums = [zero for _ in range(5)]

    def emit(d, total):
        for h in range(2):
            part = slice(h * cols, (h + 1) * cols)
            field = fld[d, :, part].astype(jnp.float32)
            raw = raw_in[d, :, part].astype(jnp.float32)
            image = total[:, part]
            if h == 0:
                image = image + diagonal(diag, right_diag, d, h) * field
                for j, prod in enumerate((field * field, raw * field, field * sig[d, :, part])):
                    sums[j] = sums[j] + fold(prod)
            sums[3] = sums[3] + fold(raw * image)
            sums[4] = sums[4] + fold(field * image)
        for e, send in enumerate(sends, 1):
            send_rows(e, send, d, *((part_out,) if e % 2 else (fld, part_out)))
        rows = pl.ds(pl.multiple_of(own_op * step, step), step)
        for j, ref in enumerate((raw_in, sig, fld, part_out)):
            own_out[j, d] = ref[d, rows].astype(own_out.dtype)

    _, own_op = place_of()
    step = own_out.shape[2]
    sum_terms(src, widths, inter, right, part_out, emit)
    vv, vc, vs = halves[0]
    ff, vf, fs, vt, ft = (whole(x) for x in sums)
    spread([vv, vc, whole(vs), ff, vf * scale, fs * scale, vt * scale, ft], dots_out)


def ritz_pair(theta, h_mix, h_two):
    diff, twice = theta - h_two, 2.0 * h_mix
    size = jnp.sqrt(diff * diff + twice * twice)
    some = size > 0.0
    safe = jnp.where(some, size, 1.0)
    big = jnp.sqrt(0.5 + 0.5 * jnp.abs(diff) / safe)
    small = 0.5 * jnp.abs(twice) / (safe * big)
    sine = jnp.where(diff >= 0.0, small, big)
    cosine = jnp.where(diff >= 0.0, big, small)
    sine = jnp.where(some, sine, 0.0)
    cosine = jnp.where(some, cosine, 1.0)
    upward = (twice > 0.0) | ((twice == 0.0) & (diff < 0.0))
    return sine, jnp.where(upward, -cosine, cosine), 0.5 * (theta + h_two) - 0.5 * size


def third_body(n_blk, n_op, count, slots, parts1, parts2, diag, right_diag, own, *refs):
    n_far = n_op // 2 - 1
    got1, got2 = refs[:n_far], refs[n_far : n_far + n_op - 1]
    new_out, res_out, energy_out = refs[n_far + n_op - 1 :]
    step, cols = new_out.shape[1], new_out.shape[2] // n_op
    own_blk, own_op = place_of()
    scale, theta = norm_theta(parts1[...], count)
    pairs = parts2[...].reshape(n_blk * n_op // 2, 2, *parts2.shape[1:])
    pairs = pairs[:, 0] + pairs[:, 1]
    vv, vc, vs, ff, vf, fs, vt, ft = (pairs[:, 0, j : j + 1] for j in range(8))

    def mean(x):
        return jnp.sum(x, axis=0, keepdims=True) * (1.0 / count)

    def nearest(vv, vc):
        return vc / jnp.maximum(vv, 1e-30)

    along = mean(vc)
    beta = nearest(vv, vc) - along
    norm_sq = mean(ff + 2.0 * beta * vf + beta * beta * vv)
    unit = lax.rsqrt(jnp.maximum(norm_sq, 0.0) + EPS)
    v_s1 = unit * mean(vt + beta * vs)
    u_s0 = unit * mean(fs + beta * vs)
    u_s1 = unit * unit * mean(ft + beta * (vt + fs) + beta * beta * vs)
    cv, cu, energy = ritz_pair(theta, 0.5 * (v_s1 + u_s0), u_s1)
    energy_out[0] = jnp.max(energy)
    cu = cu * unit
    mine = pl.ds(pl.multiple_of(own_op * step, step), step)
    for e in range(0, n_op, 2):
        there = own_blk * n_op + (own_op ^ e)
        pair = parts2[there] + parts2[own_blk * n_op + (own_op ^ e ^ 1)]
        on_vec = cv + cu * (nearest(pair[:, 0:1], pair[:, 1:2]) - along)
        for h in range(2):
            at = pl.multiple_of((own_op ^ e ^ h) * cols, LANES)
            part, crossed = slice(h * cols, (h + 1) * cols), slice((1 - h) * cols, (2 - h) * cols)
            for d in range(n_blk):
                dmat = diag[d, mine] + right_diag[:, pl.ds(at, cols)]
                blocks = [own.at[j] for j in range(4)]
                if e:
                    far, near = got1[e // 2 - 1], got2[e - 1]
                    blocks = far.at[0], far.at[1], near.at[0], near.at[1]
                raw, sigma, fld, image = (x[d, :, part].astype(jnp.float32) for x in blocks)
                vec, sigma = raw * scale, sigma * scale
                image = image + got2[e][0, d, :, crossed].astype(jnp.float32) + dmat * fld
                newvec = on_vec * vec + cu * fld
                res = on_vec * sigma + cu * image - energy * newvec
                new_out[slots[d], :, pl.ds(at, cols)] = newvec.astype(jnp.bfloat16)
                res_out[slots[d], :, pl.ds(at, cols)] = res.astype(jnp.bfloat16)


def per_device(
    psi, left_ops, right_ops, term_shift, slot_sector, sector_width, diag_left, diag_right
):
    n_blk, n_op = lax.axis_size("blk"), lax.axis_size("op")
    _, rows, ncols = psi.shape
    terms, _, width, _ = right_ops.shape
    n_pair = n_op // 2
    cols = diag_right.shape[0] // n_op
    step = rows // n_op
    count = float(n_blk * rows * ncols)
    n_dev = n_blk * n_op
    bf16, f32, i32 = jnp.bfloat16, jnp.float32, jnp.int32
    last = sorted(range(1, n_blk), key=lambda d: (min(d, n_blk - d), -d))[-1]

    def pack():
        first = swap(term_shift, 1, n_op)
        sent = kernel(
            functools.partial(pack_body, n_blk, n_op),
            [(term_shift, SMEM), (first, SMEM), (psi, HBM), (right_ops, HBM)],
            [((rows, 2 * cols if d in (0, last) else cols), bf16, VMEM) for d in range(n_blk)]
            + [((terms * width + 16, 2 * cols), bf16, VMEM)] * n_pair,
            [pltpu.VMEM(right_ops.shape, bf16), pltpu.SemaphoreType.DMA((2 * n_blk + 1,))],
            nbytes=1 << 20,
        )
        return sent[:n_blk], sent[n_blk:]

    def table(right):
        return kernel(
            functools.partial(table_body, n_blk, terms),
            [(slot_sector, SMEM), (sector_width, SMEM), (diag_left, VMEM), (diag_right[None], VMEM)]
            + [(block, VMEM) for block in right],
            [((n_blk * n_pair * terms,), i32, SMEM)]
            + [((n_blk,), i32, SMEM)] * 2
            + [((n_blk, rows, LANES), f32, VMEM), ((1, n_op * cols), f32, VMEM)],
        )

    def inputs(left, psi, those):
        blocks = [left[d, 2 * e] for d in those for e in range(n_pair)]
        halves = [half for d in those for half in psi[d]]
        return [(x, VMEM) for x in blocks], [(x, VMEM) for x in halves], [len(psi[d]) for d in those]

    def early(left, psi, n_early, tables):
        left_ins, psi_ins, counts = inputs(left, psi, range(n_early))
        return kernel(
            functools.partial(early_body, n_pair, counts),
            [(tables[1], SMEM)] + left_ins + psi_ins,
            [
                ((n_early, rows, 2 * cols), bf16, VMEM),
                ((n_early, n_pair * terms, rows, 2 * cols), bf16, VMEM),
                ((n_early, n_pair, terms, rows, rows), bf16, HBM),
            ],
            [pltpu.SemaphoreType.DMA((n_early * n_pair,))],
            flops=2 * n_early * rows * rows * 2 * cols * terms * n_pair,
            nbytes=4 << 20,
        )

    left, psi_by, right, (src, widths, slots, *both), (raw_early, inter_early, left_early) = gather(
        left_ops[:, 0], n_blk, n_op, pack, table, early
    )
    n_early = raw_early.shape[0]
    n_late = n_blk - n_early
    left_ins, psi_ins, counts = inputs(left, psi_by, range(n_early, n_blk))
    right_ins = [(block, VMEM) for block in right]
    diags = [(x, VMEM) for x in both]

    tables = [(src, SMEM), (widths, SMEM)]
    narrow = ((n_blk, rows, 2 * cols), bf16, VMEM)
    dots = ((n_dev, 1, LANES), f32, VMEM)
    wide = ((n_blk, rows, 2 * cols), f32, VMEM)
    sends = [((2 - e % 2, n_blk, step, 2 * cols), bf16, VMEM) for e in range(1, n_op)]
    inter = pltpu.VMEM((n_blk + 1, n_pair * terms, rows, 2 * cols), bf16)
    left_late = (n_late, n_pair, terms, rows, rows)
    cost = dict(flops=2 * n_blk * rows * 2 * cols * terms * n_pair * (rows + 2 * cols), nbytes=6 << 20)

    def totals(parts):
        return lax.all_to_all(parts, ("blk", "op"), 0, 0, tiled=True)

    part1, raw, kept, dots1 = kernel(
        functools.partial(first_body, n_blk, n_pair, counts),
        tables + left_ins + right_ins + psi_ins + [(raw_early, VMEM), (inter_early, VMEM)] + diags,
        [narrow, narrow, (left_late, bf16, HBM), dots],
        [inter, pltpu.SemaphoreType.DMA((n_late * n_pair + 2,))],
        **cost,
    )
    parts1 = totals(dots1)
    sig, *out1 = kernel(
        sigma_body,
        [(x, VMEM) for x in (part1, swap(part1, 1, n_op), raw)] + diags,
        [wide] + sends[1::2],
        nbytes=4 << 20,
    )
    got1 = [swap(block, 2 * e, n_op) for e, block in enumerate(out1, 1)]
    dots2, own, *out2 = kernel(
        functools.partial(second_body, n_blk, n_pair, count),
        tables + [(left_early, HBM), (kept, HBM)] + right_ins
        + [(x, VMEM) for x in (parts1, raw, sig)] + diags,
        [dots, ((4, n_blk, step, 2 * cols), bf16, VMEM)] + sends,
        [
            inter,
            pltpu.VMEM((n_blk, rows, 2 * cols), f32),
            pltpu.VMEM((n_blk, rows, 2 * cols), bf16),
            pltpu.VMEM((n_blk, rows, 2 * cols), bf16),
            pltpu.VMEM((n_blk, *left_late[1:]), bf16),
            pltpu.SemaphoreType.DMA((n_blk,)),
        ],
        flops=4 * cost["flops"],
        nbytes=24 << 20,
    )
    near, got1 = lax.optimization_barrier((out2[0], got1))
    parts2 = totals(dots2)
    got2 = [swap(near, 1, n_op)] + [swap(block, e, n_op) for e, block in enumerate(out2[1:], 2)]
    final = ((n_blk, step, n_op * cols), bf16, VMEM)
    new, res, energy = kernel(
        functools.partial(third_body, n_blk, n_op, count),
        [(slots, SMEM)] + [(x, VMEM) for x in (parts1, parts2)] + diags
        + [(x, VMEM) for x in (own, *got1, *got2)],
        [final, final, ((1,), f32, SMEM)],
        nbytes=4 << 20,
    )
    return new, res, energy


def solution(mesh):
    placed = (
        P(("grp", "blk"), None, None),
        P("op", ("grp", "blk"), None, None),
        P("op", ("grp", "blk"), None, None),
        P("op"),
        P("grp"),
        P("grp"),
        P("grp", None),
        P(("grp", "blk")),
    )

    def body(*args):
        psi, left_ops, right_ops, diag_right = args[0], args[1], args[2], args[7]
        n_op = mesh.shape["op"]
        cols = diag_right.shape[0] // n_op
        fits = (
            psi.shape[0] == 1
            and diag_right.shape[0] % n_op == 0
            and cols == LANES
            and n_op % 2 == 0
            and cols % right_ops.shape[2] == 0
            and cols // right_ops.shape[2] * n_op == right_ops.shape[1]
            and psi.shape[1] % (16 * n_op) == 0
            and n_op & (n_op - 1) == 0
            and mesh.shape["blk"] > n_op.bit_length() - 1
        )
        return (per_device if fits else per_device_general)(*args)

    return jax.shard_map(
        body,
        mesh=mesh,
        in_specs=placed,
        out_specs=(P("grp", "op", "blk"), P("grp", "op", "blk"), P("grp")),
        check_vma=False,
    )
```

```python
import functools

import jax
import jax.numpy as jnp
from jax import lax
from jax.experimental import pallas as pl
from jax.experimental.pallas import tpu as pltpu
from jax.sharding import PartitionSpec as P

EPS = 1e-06
LANES = 128
VMEM_LIMIT = 20 * 1024 * 1024


def per_device_general(
    psi, left_ops, right_ops, term_shift, slot_sector, sector_width, diag_left, diag_right
):
    sec_dev, rows, ncols = psi.shape
    nsec = slot_sector.shape[0]
    terms_dev = left_ops.shape[0]
    right_local = right_ops.shape[1]
    right_width = right_ops.shape[2]
    local_cols = diag_right.shape[0]
    count = float(nsec * rows * ncols)
    match = slot_sector[:, None] == jnp.arange(nsec)[None, :]
    widths = jnp.sum(jnp.where(match, sector_width[None, :], 0), axis=1)
    mask_all = (jnp.arange(rows)[None, :] < widths[:, None]).astype(jnp.float32)
    own_mask = lax.dynamic_slice_in_dim(mask_all, lax.axis_index("blk") * sec_dev, sec_dev, 0)
    raw = psi.astype(jnp.float32) * own_mask[:, :, None]
    squares = lax.psum(jnp.sum(raw * raw), "blk")
    v_left = (raw * lax.rsqrt(squares / count + EPS)).astype(jnp.bfloat16)
    onehots = (
        slot_sector[None, None, :] == slot_sector[None, :, None] - term_shift[:, None, None]
    ).astype(jnp.bfloat16)
    op_rows = rows // lax.axis_size("op")
    op_start = lax.axis_index("op") * op_rows
    dmat = diag_left[:, :, None] + diag_right[None, None, :]

    def left_local(field):
        return jnp.einsum(
            "ksij,sjc->ksic", left_ops, field, preferred_element_type=jnp.float32
        ).astype(jnp.bfloat16)

    def right_part(moved_in):
        flat = moved_in.reshape(terms_dev, nsec, rows * local_cols)
        shifted = jnp.einsum(
            "kts,ksx->ktx", onehots, flat, preferred_element_type=jnp.float32
        ).astype(jnp.bfloat16)
        shifted = shifted.reshape(terms_dev, nsec, rows, right_local, right_width)
        accum = jnp.einsum(
            "ktwrc,krdc->twrd", shifted, right_ops, preferred_element_type=jnp.float32
        )
        return accum.reshape(nsec, rows, local_cols) * mask_all[:, :, None]

    def op_total(partial_value):
        return lax.psum(partial_value.astype(jnp.bfloat16), "op").astype(jnp.float32)

    def final_rows(array):
        return lax.dynamic_slice_in_dim(array, op_start, op_rows, 1)

    def reduce_dots(values):
        sums = lax.psum(values, "blk")
        return tuple((item / count for item in sums))

    moved_first, v_moved = (
        lax.all_to_all(left_local(v_left), "blk", split_axis=3, concat_axis=1, tiled=True),
        lax.all_to_all(v_left[None], "blk", split_axis=3, concat_axis=1, tiled=True),
    )
    v_right = v_moved[0]
    vec32 = v_right.astype(jnp.float32)
    first_sigma = op_total(right_part(moved_first)) + dmat * vec32
    theta = reduce_dots((jnp.sum(vec32 * first_sigma),))[0]
    resid = first_sigma - theta * vec32
    den = dmat - theta
    corr = resid * den / jnp.maximum(den * den, 0.25)
    along = reduce_dots((jnp.sum(vec32 * corr),))[0]
    orth = corr - along * vec32
    norm_sq = reduce_dots((jnp.sum(orth * orth),))[0]
    update = (orth * lax.rsqrt(norm_sq + EPS)).astype(jnp.bfloat16)
    upd32 = update.astype(jnp.float32)
    upd_left = lax.all_to_all(update, "blk", split_axis=0, concat_axis=2, tiled=True)
    moved_second = lax.all_to_all(
        left_local(upd_left), "blk", split_axis=3, concat_axis=1, tiled=True
    )
    second_sigma = op_total(right_part(moved_second)) + dmat * upd32
    v_s1, u_s0, u_s1 = reduce_dots(
        (jnp.sum(vec32 * second_sigma), jnp.sum(upd32 * first_sigma), jnp.sum(upd32 * second_sigma))
    )
    h_mix = 0.5 * (v_s1 + u_s0)
    coef_v, coef_u, energy = ritz(theta, h_mix, u_s1)
    newvec = coef_v * vec32 + coef_u * upd32
    image = coef_v * first_sigma + coef_u * second_sigma
    new_out = final_rows(newvec.astype(jnp.bfloat16))
    res_out = final_rows((image - energy * newvec).astype(jnp.bfloat16))
    return (new_out, res_out, jnp.reshape(energy, (1,)))


def ritz(theta, h_mix, h_two):
    angle = 0.5 * jnp.arctan2(2.0 * h_mix, theta - h_two)
    sine = jnp.sin(angle)
    flip = jnp.where(sine > 0, -1.0, 1.0)
    coef_v = -sine * flip
    coef_u = jnp.cos(angle) * flip
    half = 0.5 * (theta - h_two)
    energy = 0.5 * (theta + h_two) - jnp.sqrt(half * half + h_mix * h_mix)
    return coef_v, coef_u, energy


VMEM, SMEM, HBM = pltpu.VMEM, pltpu.SMEM, pltpu.HBM


def kernel(body, ins, outs, scratch=(), flops=0, nbytes=0):
    return pl.pallas_call(
        body,
        out_shape=[
            HBM(shape, dtype) if space == HBM else jax.ShapeDtypeStruct(shape, dtype)
            for shape, dtype, space in outs
        ],
        in_specs=[pl.BlockSpec(memory_space=space) for _, space in ins],
        out_specs=[pl.BlockSpec(memory_space=space) for _, _, space in outs],
        scratch_shapes=list(scratch),
        compiler_params=pltpu.CompilerParams(vmem_limit_bytes=VMEM_LIMIT),
        cost_estimate=pl.CostEstimate(flops=flops, bytes_accessed=nbytes, transcendentals=0),
    )(*[pltpu.with_memory_space_constraint(x, HBM) if space == HBM else x for x, space in ins])


def ring_at(place, n_blk):
    place = place % n_blk if isinstance(place, int) else lax.rem(place + n_blk, n_blk)
    even, odd = 2 * place, 2 * (n_blk - place) - 1
    if isinstance(place, int):
        return even if even < n_blk else odd
    return jnp.where(even < n_blk, even, odd)


def ring_place(index, n_blk):
    return jnp.where(lax.rem(index, 2) == 1, n_blk - (index + 1) // 2, index // 2)


def onward(block, d, n_blk):
    pairs = [(ring_at(i, n_blk), ring_at(i + d, n_blk)) for i in range(n_blk)]
    return lax.ppermute(block, "blk", pairs)


def swap(block, e, n_op):
    return lax.ppermute(block, "op", [(i, i ^ e) for i in range(n_op)])


def gather(own, n_blk, n_op, pack, table, early):
    bits = [1 << b for b in reversed(range(1, n_op.bit_length() - 1))]
    order = sorted(range(1, n_blk), key=lambda d: min(d, n_blk - d))
    left, psi, right, tables, columns = {(0, 0): own}, {}, None, None, None
    waiting, across, late, made = {(0, 0): 0}, {}, None, None
    for j in range(n_blk + len(bits)):
        new, moved = {}, {}
        for (d, e), done in waiting.items():
            if e == 0 and d + 1 < n_blk:
                new[d + 1, 0] = onward(left[d, 0], 1, n_blk), 0
            for b in range(done, len(bits)):
                new[d, e ^ bits[b]] = swap(left[d, e], bits[b], n_op), b + 1
        left.update({key: block for key, (block, _) in new.items()})
        kept = {key: block for key, (block, _) in new.items() if key[1] == 0}
        kept.update(across)
        across = {key: block for key, (block, _) in new.items() if key[1] != 0}
        if late is not None:
            moved["psi"] = late
        if j == 0:
            columns, packed = pack()
            right = [packed[0]]
            right += [swap(part, 2 * e, n_op) for e, part in enumerate(packed[1:], 1)]
            moved["columns"] = columns
        if j == 1:
            moved["right"] = right
        if j == 2:
            moved["tables"] = table(right)
        if j == n_blk - 1 and j >= len(bits) + 1:
            n_early = min(2, n_blk - 1)
            psi[0] = [columns[0]]
            moved["early"] = early(left, psi, n_early, tables)
        if 2 <= j < n_blk:
            moved["other"] = swap(psi[order[j - 2]][0], 1, n_op)
        late = onward(columns[order[j]], order[j], n_blk) if j < n_blk - 1 else None
        if not kept:
            break
        waiting = {key: done for key, (_, done) in new.items()}
        kept, moved = lax.optimization_barrier((kept, moved))
        left.update(kept)
        right, tables = moved.get("right", right), moved.get("tables", tables)
        columns = moved.get("columns", columns)
        made = moved.get("early", made)
        if "psi" in moved:
            psi[order[j - 1]] = [moved["psi"]]
        if "other" in moved:
            psi[order[j - 2]].append(moved["other"])
    return left, psi, right, tables, made


def place_of():
    return lax.axis_index("blk"), lax.axis_index("op")


def pack_body(n_blk, n_op, shift, _, psi, right_in, *outs):
    n_pair = n_op // 2
    psi_out, right_out, right, sems = outs[:n_blk], outs[n_blk : n_blk + n_pair], outs[-2], outs[-1]
    terms, local, width, _ = right.shape
    cols = local * width // n_op
    per = cols // width
    own_blk, own_op = place_of()
    fetch = pltpu.make_async_copy(right_in, right, sems.at[2 * n_blk])
    fetch.start()
    copies = []
    for d in range(n_blk):
        there = ring_at(ring_place(own_blk, n_blk) + d, n_blk) * n_op
        for h in range(psi_out[d].shape[1] // cols):
            start = pl.multiple_of((there + (own_op ^ h)) * cols, LANES)
            copy = pltpu.make_async_copy(
                psi.at[0, :, pl.ds(start, cols)],
                psi_out[d].at[:, h * cols : (h + 1) * cols],
                sems.at[2 * d + h],
            )
            copy.start()
            copies.append(copy)
    lane = lax.broadcasted_iota(jnp.int32, (16, 2 * cols), 1)
    line = jnp.zeros((16, 2 * cols), jnp.float32)
    for k in range(terms):
        line = jnp.where(lane == k, shift[k].astype(jnp.float32), line)
    square = [lax.broadcasted_iota(jnp.int32, (width, width), axis) for axis in (0, 1)]
    unit = (square[0] == square[1]).astype(jnp.bfloat16)
    fetch.wait()
    for e in range(n_pair):
        for k in range(terms):
            turned = []
            for h in range(2):
                first = (own_op ^ (2 * e) ^ h) * per
                for r in range(per):
                    turned.append(
                        lax.dot_general(
                            right[k, first + r], unit, (((0,), (0,)), ((), ())),
                            preferred_element_type=jnp.float32,
                        )
                    )
            side_by_side = jnp.concatenate(turned, axis=1).astype(jnp.bfloat16)
            right_out[e][k * width : (k + 1) * width] = side_by_side
        right_out[e][terms * width :] = line.astype(jnp.bfloat16)
    for copy in copies:
        copy.wait()


def table_body(n_blk, terms, sector, width, left_diag, right_diag, *refs):
    tails, src, widths, slots, diag, right_out = refs[:-5], *refs[-5:]
    right_out[...] = right_diag[...]
    n_pair = len(tails)
    rows, cols = tails[0].shape
    own_blk, _ = place_of()
    lane = lax.broadcasted_iota(jnp.int32, (16, cols), 1)
    for d in range(n_blk):
        slot = ring_at(ring_place(own_blk, n_blk) - d, n_blk)
        slots[d] = slot
        widths[d] = width[sector[slot]]
    for e in range(n_pair):
        tail = tails[e][rows - 16 :].astype(jnp.float32)
        for k in range(terms):
            shift = jnp.max(jnp.where(lane == k, tail, -1e9)).astype(jnp.int32)
            for t in range(n_blk):
                want = sector[slots[t]] - shift
                found = jnp.int32(n_blk)
                for d in range(n_blk):
                    found = jnp.where(sector[slots[d]] == want, d, found)
                src[(t * n_pair + e) * terms + k] = found
    for d in range(n_blk):
        row = left_diag[pl.ds(slots[d], 1), :]
        diag[d] = jnp.transpose(jnp.broadcast_to(row, (diag.shape[2], row.shape[1])))


def diagonal(diag, right_diag, d, h):
    cols = diag.shape[2]
    _, own_op = place_of()
    start = pl.multiple_of((own_op ^ h) * cols, LANES)
    return diag[d] + right_diag[:, pl.ds(start, cols)]


def row_mask(width, shape):
    return lax.broadcasted_iota(jnp.int32, shape, 0) < width


def fold(x):
    return jnp.sum(x.reshape(-1, 8, x.shape[-1]), axis=0)


def whole(x):
    return jnp.sum(jnp.sum(x, axis=0, keepdims=True), axis=1, keepdims=True)


def spread(values, out):
    lane = lax.broadcasted_iota(jnp.int32, out.shape[1:], 1)
    row = jnp.zeros(out.shape[1:], jnp.float32)
    for j, value in enumerate(values):
        row = jnp.where(lane == j, value, row)
    for d in range(out.shape[0]):
        out[d] = row


def by_block(packed, terms, k):
    rows, cols = packed.shape
    width = (rows - 16) // terms
    lane = lax.broadcasted_iota(jnp.int32, (width, cols), 1)
    block = packed[k * width : (k + 1) * width].astype(jnp.float32)
    parts = []
    for r in range(cols // width):
        inside = (lane >= r * width) & (lane < (r + 1) * width)
        parts.append(jnp.where(inside, block, 0.0).astype(jnp.bfloat16))
    return jnp.concatenate(parts, axis=0)


def left_products(block, left, inter):
    n_terms, rows, cols = inter.shape
    at = 0
    while at < n_terms:
        ops = left(at)
        terms = ops.shape[0]
        prod = jnp.dot(ops.reshape(terms * rows, rows), block, preferred_element_type=jnp.float32)
        inter[at : at + terms] = prod.astype(jnp.bfloat16).reshape(terms, rows, cols)
        at += terms


def sum_terms(src, widths, inter, right, out, emit):
    n_blk, n_terms, _, _ = inter.shape
    n_blk -= 1
    terms = n_terms // len(right)
    turned = [by_block(right[j // terms], terms, j % terms) for j in range(n_terms)]
    for t in range(n_blk):
        total = None
        for j in range(n_terms):
            part = jnp.dot(
                inter[src[t * n_terms + j], j], turned[j], preferred_element_type=jnp.float32
            )
            total = part if total is None else total + part
        total = jnp.where(row_mask(widths[t], total.shape), total, 0.0)
        out[t] = total.astype(jnp.bfloat16)
        emit(t, total)


def keep(left, left_out, sems):
    copies = []
    for d, line in enumerate(left):
        for e, ref in enumerate(line):
            copies.append(pltpu.make_async_copy(ref, left_out.at[d, e], sems.at[d * len(line) + e]))
            copies[-1].start()
    return copies


def masked(psi, width, out):
    at = 0
    for ref in psi:
        block = ref[...].astype(jnp.float32)
        block = jnp.where(row_mask(width, block.shape), block, 0.0)
        out[:, at : at + block.shape[1]] = block.astype(jnp.bfloat16)
        at += block.shape[1]


def take(refs, counts):
    out = []
    for count in counts:
        out.append(refs[:count])
        refs = refs[count:]
    return out, refs


def products_of(psi, left, widths, first, raw_out, inter):
    for d, line in enumerate(left):
        masked(psi[d], widths[first + d], raw_out.at[d])
        terms = line[0].shape[0]
        left_products(raw_out[d], lambda at: line[at // terms][...], inter.at[d])


def early_body(n_pair, counts, widths, *refs):
    left, refs = take(refs, [n_pair] * len(counts))
    psi, (raw_out, inter_out, left_out, sems) = take(refs, counts)
    copies = keep(left, left_out, sems)
    products_of(psi, left, widths, 0, raw_out, inter_out)
    for copy in copies:
        copy.wait()


def first_body(n_blk, n_pair, counts, src, widths, *refs):
    n_late = len(counts)
    n_early = n_blk - n_late
    left, refs = take(refs, [n_pair] * n_late)
    (right,), refs = take(refs, [n_pair])
    psi, refs = take(refs, counts)
    raw_in, inter_in, diag, right_diag, part_out, raw_out, left_out, dots_out, inter, sems = refs
    copies = keep(left, left_out, sems)
    for j, (given, own) in enumerate(((inter_in, inter), (raw_in, raw_out))):
        copies.append(
            pltpu.make_async_copy(given, own.at[:n_early], sems.at[n_late * n_pair + j])
        )
        copies[-1].start()
    inter[n_blk] = jnp.zeros_like(inter[n_blk])
    products_of(
        psi, left, widths, n_early, raw_out.at[n_early:], inter.at[n_early:n_blk]
    )
    for copy in copies:
        copy.wait()
    cols = diag.shape[2]
    zero = jnp.zeros((8, cols), jnp.float32)
    sums = [zero, zero]

    def emit(d, total):
        for h in range(2):
            part = slice(h * cols, (h + 1) * cols)
            raw = raw_out[d, :, part].astype(jnp.float32)
            image = total[:, part]
            if h == 0:
                image = image + diagonal(diag, right_diag, d, h) * raw
                sums[0] = sums[0] + fold(raw * raw)
            sums[1] = sums[1] + fold(raw * image)

    sum_terms(src, widths, inter, right, part_out, emit)
    spread([whole(x) for x in sums], dots_out)


def send_rows(e, send, d, *refs):
    _, own_op = place_of()
    step = send.shape[2]
    rows = pl.ds(pl.multiple_of((own_op ^ e) * step, step), step)
    for j, ref in enumerate(refs):
        send[j, d] = ref[d, rows].astype(send.dtype)


def total_of(mine, other, d, h, cols):
    own = mine[d, :, h * cols : (h + 1) * cols].astype(jnp.float32)
    return own + other[d, :, (1 - h) * cols : (2 - h) * cols].astype(jnp.float32)


def sigma_body(mine, other, raw_in, diag, right_diag, sig_out, *sends):
    n_blk, _, cols = diag.shape
    for d in range(n_blk):
        for h in range(2):
            part = slice(h * cols, (h + 1) * cols)
            raw = raw_in[d, :, part].astype(jnp.float32)
            sigma = total_of(mine, other, d, h, cols) + diagonal(diag, right_diag, d, h) * raw
            sig_out[d, :, part] = sigma
        for e, send in enumerate(sends):
            send_rows(2 * e, send, d, raw_in, sig_out)


def norm_theta(parts, count):
    tot = jnp.sum(parts, axis=0) * (1.0 / count)
    scale = lax.rsqrt(tot[:, 0:1] + EPS)
    return scale, tot[:, 1:2] * scale * scale


def second_body(n_blk, n_pair, count, src, widths, left_early, left_late, *refs):
    right, refs = refs[:n_pair], refs[n_pair:]
    parts, raw_in, sig, diag, right_diag, dots_out, own_out = refs[:7]
    sends, (inter, corr, fld, part_out, held, sems) = refs[7:-6], refs[-6:]
    copies = []
    n_early = left_early.shape[0]
    for d in range(n_blk):
        kept = left_early.at[d] if d < n_early else left_late.at[d - n_early]
        copies.append(pltpu.make_async_copy(kept, held.at[d], sems.at[d]))
        copies[-1].start()
    inter[n_blk] = jnp.zeros_like(inter[n_blk])
    scale, theta = norm_theta(parts[...], count)
    cols = diag.shape[2]
    halves = []
    for h in range(2):
        part = slice(h * cols, (h + 1) * cols)
        vv = vc = vs = jnp.zeros((8, cols), jnp.float32)
        for d in range(n_blk):
            vec = raw_in[d, :, part].astype(jnp.float32) * scale
            sigma = sig[d, :, part] * scale
            den = diagonal(diag, right_diag, d, h) - theta
            item = (sigma - theta * vec) * den / jnp.maximum(den * den, 0.25)
            corr[d, :, part] = item
            vv, vc = vv + fold(vec * vec), vc + fold(vec * item)
            if h == 0:
                vs = vs + fold(vec * sigma)
        halves.append((whole(vv), whole(vc), vs))
    along = (halves[0][1] + halves[1][1]) / jnp.maximum(halves[0][0] + halves[1][0], 1e-30)
    terms = held.shape[2]
    for copy in copies:
        copy.wait()
    for d in range(n_blk):
        for h in range(2):
            part = slice(h * cols, (h + 1) * cols)
            vec = raw_in[d, :, part].astype(jnp.float32) * scale
            fld[d, :, part] = (corr[d, :, part] - along * vec).astype(jnp.bfloat16)
        left_products(fld[d], lambda at: held[d, at // terms], inter.at[d])
    zero = jnp.zeros((8, cols), jnp.float32)
    sums = [zero for _ in range(5)]

    def emit(d, total):
        for h in range(2):
            part = slice(h * cols, (h + 1) * cols)
            field = fld[d, :, part].astype(jnp.float32)
            raw = raw_in[d, :, part].astype(jnp.float32)
            image = total[:, part]
            if h == 0:
                image = image + diagonal(diag, right_diag, d, h) * field
                for j, prod in enumerate((field * field, raw * field, field * sig[d, :, part])):
                    sums[j] = sums[j] + fold(prod)
            sums[3] = sums[3] + fold(raw * image)
            sums[4] = sums[4] + fold(field * image)
        for e, send in enumerate(sends, 1):
            send_rows(e, send, d, *((part_out,) if e % 2 else (fld, part_out)))
        send_rows(0, own_out, d, fld, part_out)

    sum_terms(src, widths, inter, right, part_out, emit)
    vv, vc, vs = halves[0]
    ff, vf, fs, vt, ft = (whole(x) for x in sums)
    spread([vv, vc, whole(vs), ff, vf * scale, fs * scale, vt * scale, ft], dots_out)


def ritz_pair(theta, h_mix, h_two):
    diff, twice = theta - h_two, 2.0 * h_mix
    size = jnp.sqrt(diff * diff + twice * twice)
    some = size > 0.0
    safe = jnp.where(some, size, 1.0)
    big = jnp.sqrt(0.5 + 0.5 * jnp.abs(diff) / safe)
    small = 0.5 * jnp.abs(twice) / (safe * big)
    sine = jnp.where(diff >= 0.0, small, big)
    cosine = jnp.where(diff >= 0.0, big, small)
    sine = jnp.where(some, sine, 0.0)
    cosine = jnp.where(some, cosine, 1.0)
    upward = (twice > 0.0) | ((twice == 0.0) & (diff < 0.0))
    return sine, jnp.where(upward, -cosine, cosine), 0.5 * (theta + h_two) - 0.5 * size


def third_body(n_blk, n_op, count, slots, parts1, parts2, diag, right_diag, *refs):
    n_far = n_op // 2
    got1, got2 = refs[:n_far], refs[n_far : n_far + n_op]
    new_out, res_out, energy_out = refs[n_far + n_op :]
    step, cols = new_out.shape[1], new_out.shape[2] // n_op
    own_blk, own_op = place_of()
    scale, theta = norm_theta(parts1[...], count)
    pairs = parts2[...].reshape(n_blk * n_op // 2, 2, *parts2.shape[1:])
    pairs = pairs[:, 0] + pairs[:, 1]
    vv, vc, vs, ff, vf, fs, vt, ft = (pairs[:, 0, j : j + 1] for j in range(8))

    def mean(x):
        return jnp.sum(x, axis=0, keepdims=True) * (1.0 / count)

    def nearest(vv, vc):
        return vc / jnp.maximum(vv, 1e-30)

    along = mean(vc)
    beta = nearest(vv, vc) - along
    norm_sq = mean(ff + 2.0 * beta * vf + beta * beta * vv)
    unit = lax.rsqrt(jnp.maximum(norm_sq, 0.0) + EPS)
    v_s1 = unit * mean(vt + beta * vs)
    u_s0 = unit * mean(fs + beta * vs)
    u_s1 = unit * unit * mean(ft + beta * (vt + fs) + beta * beta * vs)
    cv, cu, energy = ritz_pair(theta, 0.5 * (v_s1 + u_s0), u_s1)
    energy_out[0] = jnp.max(energy)
    cu = cu * unit
    mine = pl.ds(pl.multiple_of(own_op * step, step), step)
    for e in range(0, n_op, 2):
        there = own_blk * n_op + (own_op ^ e)
        pair = parts2[there] + parts2[own_blk * n_op + (own_op ^ e ^ 1)]
        on_vec = cv + cu * (nearest(pair[:, 0:1], pair[:, 1:2]) - along)
        for h in range(2):
            at = pl.multiple_of((own_op ^ e ^ h) * cols, LANES)
            part, crossed = slice(h * cols, (h + 1) * cols), slice((1 - h) * cols, (2 - h) * cols)
            for d in range(n_blk):
                dmat = diag[d, mine] + right_diag[:, pl.ds(at, cols)]
                far, near = got1[e // 2], got2[e]
                blocks = far.at[0], far.at[1], near.at[0], near.at[1]
                raw, sigma, fld, image = (x[d, :, part].astype(jnp.float32) for x in blocks)
                vec, sigma = raw * scale, sigma * scale
                image = image + got2[e + 1][0, d, :, crossed].astype(jnp.float32) + dmat * fld
                newvec = on_vec * vec + cu * fld
                res = on_vec * sigma + cu * image - energy * newvec
                new_out[slots[d], :, pl.ds(at, cols)] = newvec.astype(jnp.bfloat16)
                res_out[slots[d], :, pl.ds(at, cols)] = res.astype(jnp.bfloat16)


def per_device(
    psi, left_ops, right_ops, term_shift, slot_sector, sector_width, diag_left, diag_right
):
    n_blk, n_op = lax.axis_size("blk"), lax.axis_size("op")
    _, rows, ncols = psi.shape
    terms, _, width, _ = right_ops.shape
    n_pair = n_op // 2
    cols = diag_right.shape[0] // n_op
    step = rows // n_op
    count = float(n_blk * rows * ncols)
    n_dev = n_blk * n_op
    bf16, f32, i32 = jnp.bfloat16, jnp.float32, jnp.int32
    last = sorted(range(1, n_blk), key=lambda d: min(d, n_blk - d))[-1]

    def pack():
        first = swap(term_shift, 1, n_op)
        sent = kernel(
            functools.partial(pack_body, n_blk, n_op),
            [(term_shift, SMEM), (first, SMEM), (psi, HBM), (right_ops, HBM)],
            [((rows, 2 * cols if d in (0, last) else cols), bf16, VMEM) for d in range(n_blk)]
            + [((terms * width + 16, 2 * cols), bf16, VMEM)] * n_pair,
            [pltpu.VMEM(right_ops.shape, bf16), pltpu.SemaphoreType.DMA((2 * n_blk + 1,))],
            nbytes=1 << 20,
        )
        return sent[:n_blk], sent[n_blk:]

    def table(right):
        return kernel(
            functools.partial(table_body, n_blk, terms),
            [(slot_sector, SMEM), (sector_width, SMEM), (diag_left, VMEM), (diag_right[None], VMEM)]
            + [(block, VMEM) for block in right],
            [((n_blk * n_pair * terms,), i32, SMEM)]
            + [((n_blk,), i32, SMEM)] * 2
            + [((n_blk, rows, LANES), f32, VMEM), ((1, n_op * cols), f32, VMEM)],
        )

    def inputs(left, psi, those):
        blocks = [left[d, 2 * e] for d in those for e in range(n_pair)]
        halves = [half for d in those for half in psi[d]]
        return [(x, VMEM) for x in blocks], [(x, VMEM) for x in halves], [len(psi[d]) for d in those]

    def early(left, psi, n_early, tables):
        left_ins, psi_ins, counts = inputs(left, psi, range(n_early))
        return kernel(
            functools.partial(early_body, n_pair, counts),
            [(tables[1], SMEM)] + left_ins + psi_ins,
            [
                ((n_early, rows, 2 * cols), bf16, VMEM),
                ((n_early, n_pair * terms, rows, 2 * cols), bf16, VMEM),
                ((n_early, n_pair, terms, rows, rows), bf16, HBM),
            ],
            [pltpu.SemaphoreType.DMA((n_early * n_pair,))],
            flops=2 * n_early * rows * rows * 2 * cols * terms * n_pair,
            nbytes=4 << 20,
        )

    left, psi_by, right, (src, widths, slots, *both), (raw_early, inter_early, left_early) = gather(
        left_ops[:, 0], n_blk, n_op, pack, table, early
    )
    n_early = raw_early.shape[0]
    n_late = n_blk - n_early
    left_ins, psi_ins, counts = inputs(left, psi_by, range(n_early, n_blk))
    right_ins = [(block, VMEM) for block in right]
    diags = [(x, VMEM) for x in both]

    tables = [(src, SMEM), (widths, SMEM)]
    narrow = ((n_blk, rows, 2 * cols), bf16, VMEM)
    dots = ((n_dev, 1, LANES), f32, VMEM)
    wide = ((n_blk, rows, 2 * cols), f32, VMEM)
    sends = [((2 - e % 2, n_blk, step, 2 * cols), bf16, VMEM) for e in range(1, n_op)]
    inter = pltpu.VMEM((n_blk + 1, n_pair * terms, rows, 2 * cols), bf16)
    left_late = (n_late, n_pair, terms, rows, rows)
    cost = dict(flops=2 * n_blk * rows * 2 * cols * terms * n_pair * (rows + 2 * cols), nbytes=6 << 20)

    def totals(parts):
        return lax.all_to_all(parts, ("blk", "op"), 0, 0, tiled=True)

    part1, raw, kept, dots1 = kernel(
        functools.partial(first_body, n_blk, n_pair, counts),
        tables + left_ins + right_ins + psi_ins + [(raw_early, VMEM), (inter_early, VMEM)] + diags,
        [narrow, narrow, (left_late, bf16, HBM), dots],
        [inter, pltpu.SemaphoreType.DMA((n_late * n_pair + 2,))],
        **cost,
    )
    parts1 = totals(dots1)
    sig, *out1 = kernel(
        sigma_body,
        [(x, VMEM) for x in (part1, swap(part1, 1, n_op), raw)] + diags,
        [wide] + sends[1:2] * n_pair,
        nbytes=4 << 20,
    )
    got1 = [swap(block, 2 * e, n_op) for e, block in enumerate(out1[1:], 1)]
    dots2, own, *out2 = kernel(
        functools.partial(second_body, n_blk, n_pair, count),
        tables + [(left_early, HBM), (kept, HBM)] + right_ins
        + [(x, VMEM) for x in (parts1, raw, sig)] + diags,
        [dots, sends[1]] + sends,
        [
            inter,
            pltpu.VMEM((n_blk, rows, 2 * cols), f32),
            pltpu.VMEM((n_blk, rows, 2 * cols), bf16),
            pltpu.VMEM((n_blk, rows, 2 * cols), bf16),
            pltpu.VMEM((n_blk, *left_late[1:]), bf16),
            pltpu.SemaphoreType.DMA((n_blk,)),
        ],
        flops=4 * cost["flops"],
        nbytes=24 << 20,
    )
    near, got1 = lax.optimization_barrier((out2[0], got1))
    parts2 = totals(dots2)
    got2 = [swap(near, 1, n_op)] + [swap(block, e, n_op) for e, block in enumerate(out2[1:], 2)]
    final = ((n_blk, step, n_op * cols), bf16, VMEM)
    new, res, energy = kernel(
        functools.partial(third_body, n_blk, n_op, count),
        [(slots, SMEM)] + [(x, VMEM) for x in (parts1, parts2)] + diags
        + [(x, VMEM) for x in (out1[0], *got1, own, *got2)],
        [final, final, ((1,), f32, SMEM)],
        nbytes=4 << 20,
    )
    return new, res, energy


def solution(mesh):
    placed = (
        P(("grp", "blk"), None, None),
        P("op", ("grp", "blk"), None, None),
        P("op", ("grp", "blk"), None, None),
        P("op"),
        P("grp"),
        P("grp"),
        P("grp", None),
        P(("grp", "blk")),
    )

    def body(*args):
        psi, left_ops, right_ops, diag_right = args[0], args[1], args[2], args[7]
        n_op = mesh.shape["op"]
        cols = diag_right.shape[0] // n_op
        fits = (
            psi.shape[0] == 1
            and diag_right.shape[0] % n_op == 0
            and cols == LANES
            and n_op % 2 == 0
            and cols % right_ops.shape[2] == 0
            and cols // right_ops.shape[2] * n_op == right_ops.shape[1]
            and psi.shape[1] % (16 * n_op) == 0
            and n_op & (n_op - 1) == 0
            and mesh.shape["blk"] > n_op.bit_length() - 1
        )
        return (per_device if fits else per_device_general)(*args)

    return jax.shard_map(
        body,
        mesh=mesh,
        in_specs=placed,
        out_specs=(P("grp", "op", "blk"), P("grp", "op", "blk"), P("grp")),
        check_vma=False,
    )
```

```python
import functools

import jax
import jax.numpy as jnp
from jax import lax
from jax.experimental import pallas as pl
from jax.experimental.pallas import tpu as pltpu
from jax.sharding import PartitionSpec as P

EPS = 1e-06
LANES = 128
VMEM_LIMIT = 20 * 1024 * 1024


def per_device_general(
    psi, left_ops, right_ops, term_shift, slot_sector, sector_width, diag_left, diag_right
):
    sec_dev, rows, ncols = psi.shape
    nsec = slot_sector.shape[0]
    terms_dev = left_ops.shape[0]
    right_local = right_ops.shape[1]
    right_width = right_ops.shape[2]
    local_cols = diag_right.shape[0]
    count = float(nsec * rows * ncols)
    match = slot_sector[:, None] == jnp.arange(nsec)[None, :]
    widths = jnp.sum(jnp.where(match, sector_width[None, :], 0), axis=1)
    mask_all = (jnp.arange(rows)[None, :] < widths[:, None]).astype(jnp.float32)
    own_mask = lax.dynamic_slice_in_dim(mask_all, lax.axis_index("blk") * sec_dev, sec_dev, 0)
    raw = psi.astype(jnp.float32) * own_mask[:, :, None]
    squares = lax.psum(jnp.sum(raw * raw), "blk")
    v_left = (raw * lax.rsqrt(squares / count + EPS)).astype(jnp.bfloat16)
    onehots = (
        slot_sector[None, None, :] == slot_sector[None, :, None] - term_shift[:, None, None]
    ).astype(jnp.bfloat16)
    op_rows = rows // lax.axis_size("op")
    op_start = lax.axis_index("op") * op_rows
    dmat = diag_left[:, :, None] + diag_right[None, None, :]

    def left_local(field):
        return jnp.einsum(
            "ksij,sjc->ksic", left_ops, field, preferred_element_type=jnp.float32
        ).astype(jnp.bfloat16)

    def right_part(moved_in):
        flat = moved_in.reshape(terms_dev, nsec, rows * local_cols)
        shifted = jnp.einsum(
            "kts,ksx->ktx", onehots, flat, preferred_element_type=jnp.float32
        ).astype(jnp.bfloat16)
        shifted = shifted.reshape(terms_dev, nsec, rows, right_local, right_width)
        accum = jnp.einsum(
            "ktwrc,krdc->twrd", shifted, right_ops, preferred_element_type=jnp.float32
        )
        return accum.reshape(nsec, rows, local_cols) * mask_all[:, :, None]

    def op_total(partial_value):
        return lax.psum(partial_value.astype(jnp.bfloat16), "op").astype(jnp.float32)

    def final_rows(array):
        return lax.dynamic_slice_in_dim(array, op_start, op_rows, 1)

    def reduce_dots(values):
        sums = lax.psum(values, "blk")
        return tuple((item / count for item in sums))

    moved_first, v_moved = (
        lax.all_to_all(left_local(v_left), "blk", split_axis=3, concat_axis=1, tiled=True),
        lax.all_to_all(v_left[None], "blk", split_axis=3, concat_axis=1, tiled=True),
    )
    v_right = v_moved[0]
    vec32 = v_right.astype(jnp.float32)
    first_sigma = op_total(right_part(moved_first)) + dmat * vec32
    theta = reduce_dots((jnp.sum(vec32 * first_sigma),))[0]
    resid = first_sigma - theta * vec32
    den = dmat - theta
    corr = resid * den / jnp.maximum(den * den, 0.25)
    along = reduce_dots((jnp.sum(vec32 * corr),))[0]
    orth = corr - along * vec32
    norm_sq = reduce_dots((jnp.sum(orth * orth),))[0]
    update = (orth * lax.rsqrt(norm_sq + EPS)).astype(jnp.bfloat16)
    upd32 = update.astype(jnp.float32)
    upd_left = lax.all_to_all(update, "blk", split_axis=0, concat_axis=2, tiled=True)
    moved_second = lax.all_to_all(
        left_local(upd_left), "blk", split_axis=3, concat_axis=1, tiled=True
    )
    second_sigma = op_total(right_part(moved_second)) + dmat * upd32
    v_s1, u_s0, u_s1 = reduce_dots(
        (jnp.sum(vec32 * second_sigma), jnp.sum(upd32 * first_sigma), jnp.sum(upd32 * second_sigma))
    )
    h_mix = 0.5 * (v_s1 + u_s0)
    coef_v, coef_u, energy = ritz(theta, h_mix, u_s1)
    newvec = coef_v * vec32 + coef_u * upd32
    image = coef_v * first_sigma + coef_u * second_sigma
    new_out = final_rows(newvec.astype(jnp.bfloat16))
    res_out = final_rows((image - energy * newvec).astype(jnp.bfloat16))
    return (new_out, res_out, jnp.reshape(energy, (1,)))


def ritz(theta, h_mix, h_two):
    angle = 0.5 * jnp.arctan2(2.0 * h_mix, theta - h_two)
    sine = jnp.sin(angle)
    flip = jnp.where(sine > 0, -1.0, 1.0)
    coef_v = -sine * flip
    coef_u = jnp.cos(angle) * flip
    half = 0.5 * (theta - h_two)
    energy = 0.5 * (theta + h_two) - jnp.sqrt(half * half + h_mix * h_mix)
    return coef_v, coef_u, energy


VMEM, SMEM, HBM = pltpu.VMEM, pltpu.SMEM, pltpu.HBM


def kernel(body, ins, outs, scratch=(), flops=0, nbytes=0):
    return pl.pallas_call(
        body,
        out_shape=[
            HBM(shape, dtype) if space == HBM else jax.ShapeDtypeStruct(shape, dtype)
            for shape, dtype, space in outs
        ],
        in_specs=[pl.BlockSpec(memory_space=space) for _, space in ins],
        out_specs=[pl.BlockSpec(memory_space=space) for _, _, space in outs],
        scratch_shapes=list(scratch),
        compiler_params=pltpu.CompilerParams(vmem_limit_bytes=VMEM_LIMIT),
        cost_estimate=pl.CostEstimate(flops=flops, bytes_accessed=nbytes, transcendentals=0),
    )(*[pltpu.with_memory_space_constraint(x, HBM) if space == HBM else x for x, space in ins])


def ring_at(place, n_blk):
    place = place % n_blk if isinstance(place, int) else lax.rem(place + n_blk, n_blk)
    even, odd = 2 * place, 2 * (n_blk - place) - 1
    if isinstance(place, int):
        return even if even < n_blk else odd
    return jnp.where(even < n_blk, even, odd)


def ring_place(index, n_blk):
    return jnp.where(lax.rem(index, 2) == 1, n_blk - (index + 1) // 2, index // 2)


def onward(block, d, n_blk):
    pairs = [(ring_at(i, n_blk), ring_at(i + d, n_blk)) for i in range(n_blk)]
    return lax.ppermute(block, "blk", pairs)


def swap(block, e, n_op):
    return lax.ppermute(block, "op", [(i, i ^ e) for i in range(n_op)])


def gather(own, n_blk, n_op, pack, table, early):
    bits = [1 << b for b in reversed(range(1, n_op.bit_length() - 1))]
    order = sorted(range(1, n_blk), key=lambda d: min(d, n_blk - d))
    left, psi, right, tables, columns = {(0, 0): own}, {}, None, None, None
    waiting, across, late, made = {(0, 0): 0}, {}, None, None
    for j in range(n_blk + len(bits)):
        new, moved = {}, {}
        for (d, e), done in waiting.items():
            if e == 0 and d + 1 < n_blk:
                new[d + 1, 0] = onward(left[d, 0], 1, n_blk), 0
            for b in range(done, len(bits)):
                new[d, e ^ bits[b]] = swap(left[d, e], bits[b], n_op), b + 1
        left.update({key: block for key, (block, _) in new.items()})
        kept = {key: block for key, (block, _) in new.items() if key[1] == 0}
        kept.update(across)
        across = {key: block for key, (block, _) in new.items() if key[1] != 0}
        if late is not None:
            moved["psi"] = late
        if j == 0:
            columns, packed = pack()
            right = [packed[0]]
            right += [swap(part, 2 * e, n_op) for e, part in enumerate(packed[1:], 1)]
            moved["columns"] = columns
        if j == 0:
            moved["right"] = right
        if j == 1:
            moved["tables"] = table(right)
        if j == n_blk - 1 and j >= len(bits) + 1:
            n_early = min(2, n_blk - 1)
            psi[0] = [columns[0]]
            moved["early"] = early(left, psi, n_early, tables)
        if 2 <= j < n_blk:
            moved["other"] = swap(psi[order[j - 2]][0], 1, n_op)
        late = onward(columns[order[j]], order[j], n_blk) if j < n_blk - 1 else None
        if not kept:
            break
        waiting = {key: done for key, (_, done) in new.items()}
        kept, moved = lax.optimization_barrier((kept, moved))
        left.update(kept)
        right, tables = moved.get("right", right), moved.get("tables", tables)
        columns = moved.get("columns", columns)
        made = moved.get("early", made)
        if "psi" in moved:
            psi[order[j - 1]] = [moved["psi"]]
        if "other" in moved:
            psi[order[j - 2]].append(moved["other"])
    return left, psi, right, tables, made


def place_of():
    return lax.axis_index("blk"), lax.axis_index("op")


def pack_body(n_blk, n_op, shift, _, psi, right_in, *outs):
    n_pair = n_op // 2
    psi_out, right_out, right, sems = outs[:n_blk], outs[n_blk : n_blk + n_pair], outs[-2], outs[-1]
    terms, local, width, _ = right.shape
    cols = local * width // n_op
    per = cols // width
    own_blk, own_op = place_of()
    fetch = pltpu.make_async_copy(right_in, right, sems.at[2 * n_blk])
    fetch.start()
    copies = []
    for d in range(n_blk):
        there = ring_at(ring_place(own_blk, n_blk) + d, n_blk) * n_op
        for h in range(psi_out[d].shape[1] // cols):
            start = pl.multiple_of((there + (own_op ^ h)) * cols, LANES)
            copy = pltpu.make_async_copy(
                psi.at[0, :, pl.ds(start, cols)],
                psi_out[d].at[:, h * cols : (h + 1) * cols],
                sems.at[2 * d + h],
            )
            copy.start()
            copies.append(copy)
    lane = lax.broadcasted_iota(jnp.int32, (16, 2 * cols), 1)
    line = jnp.zeros((16, 2 * cols), jnp.float32)
    for k in range(terms):
        line = jnp.where(lane == k, shift[k].astype(jnp.float32), line)
    square = [lax.broadcasted_iota(jnp.int32, (width, width), axis) for axis in (0, 1)]
    unit = (square[0] == square[1]).astype(jnp.bfloat16)
    fetch.wait()
    for e in range(n_pair):
        for k in range(terms):
            turned = []
            for h in range(2):
                first = (own_op ^ (2 * e) ^ h) * per
                for r in range(per):
                    turned.append(
                        lax.dot_general(
                            right[k, first + r], unit, (((0,), (0,)), ((), ())),
                            preferred_element_type=jnp.float32,
                        )
                    )
            side_by_side = jnp.concatenate(turned, axis=1).astype(jnp.bfloat16)
            right_out[e][k * width : (k + 1) * width] = side_by_side
        right_out[e][terms * width :] = line.astype(jnp.bfloat16)
    for copy in copies:
        copy.wait()


def table_body(n_blk, terms, sector, width, left_diag, right_diag, *refs):
    tails, src, widths, slots, diag, right_out = refs[:-5], *refs[-5:]
    right_out[...] = right_diag[...]
    n_pair = len(tails)
    rows, cols = tails[0].shape
    own_blk, _ = place_of()
    lane = lax.broadcasted_iota(jnp.int32, (16, cols), 1)
    for d in range(n_blk):
        slot = ring_at(ring_place(own_blk, n_blk) - d, n_blk)
        slots[d] = slot
        widths[d] = width[sector[slot]]
    for e in range(n_pair):
        tail = tails[e][rows - 16 :].astype(jnp.float32)
        for k in range(terms):
            shift = jnp.max(jnp.where(lane == k, tail, -1e9)).astype(jnp.int32)
            for t in range(n_blk):
                want = sector[slots[t]] - shift
                found = jnp.int32(n_blk)
                for d in range(n_blk):
                    found = jnp.where(sector[slots[d]] == want, d, found)
                src[(t * n_pair + e) * terms + k] = found
    for d in range(n_blk):
        row = left_diag[pl.ds(slots[d], 1), :]
        diag[d] = jnp.transpose(jnp.broadcast_to(row, (diag.shape[2], row.shape[1])))


def diagonal(diag, right_diag, d, h):
    cols = diag.shape[2]
    _, own_op = place_of()
    start = pl.multiple_of((own_op ^ h) * cols, LANES)
    return diag[d] + right_diag[:, pl.ds(start, cols)]


def row_mask(width, shape):
    return lax.broadcasted_iota(jnp.int32, shape, 0) < width


def fold(x):
    return jnp.sum(x.reshape(-1, 8, x.shape[-1]), axis=0)


def whole(x):
    return jnp.sum(jnp.sum(x, axis=0, keepdims=True), axis=1, keepdims=True)


def spread(values, out):
    lane = lax.broadcasted_iota(jnp.int32, out.shape[1:], 1)
    row = jnp.zeros(out.shape[1:], jnp.float32)
    for j, value in enumerate(values):
        row = jnp.where(lane == j, value, row)
    for d in range(out.shape[0]):
        out[d] = row


def by_block(packed, terms, k):
    rows, cols = packed.shape
    width = (rows - 16) // terms
    lane = lax.broadcasted_iota(jnp.int32, (width, cols), 1)
    block = packed[k * width : (k + 1) * width].astype(jnp.float32)
    parts = []
    for r in range(cols // width):
        inside = (lane >= r * width) & (lane < (r + 1) * width)
        parts.append(jnp.where(inside, block, 0.0).astype(jnp.bfloat16))
    return jnp.concatenate(parts, axis=0)


def left_products(block, left, inter):
    n_terms, rows, cols = inter.shape
    at = 0
    while at < n_terms:
        ops = left(at)
        terms = ops.shape[0]
        prod = jnp.dot(ops.reshape(terms * rows, rows), block, preferred_element_type=jnp.float32)
        inter[at : at + terms] = prod.astype(jnp.bfloat16).reshape(terms, rows, cols)
        at += terms


def sum_terms(src, widths, inter, right, out, emit):
    n_blk, n_terms, _, _ = inter.shape
    n_blk -= 1
    terms = n_terms // len(right)
    turned = [by_block(right[j // terms], terms, j % terms) for j in range(n_terms)]
    for t in range(n_blk):
        total = None
        for j in range(n_terms):
            part = jnp.dot(
                inter[src[t * n_terms + j], j], turned[j], preferred_element_type=jnp.float32
            )
            total = part if total is None else total + part
        total = jnp.where(row_mask(widths[t], total.shape), total, 0.0)
        out[t] = total.astype(jnp.bfloat16)
        emit(t, total)


def keep(left, left_out, sems):
    copies = []
    for d, line in enumerate(left):
        for e, ref in enumerate(line):
            copies.append(pltpu.make_async_copy(ref, left_out.at[d, e], sems.at[d * len(line) + e]))
            copies[-1].start()
    return copies


def masked(psi, width, out):
    at = 0
    for ref in psi:
        block = ref[...].astype(jnp.float32)
        block = jnp.where(row_mask(width, block.shape), block, 0.0)
        out[:, at : at + block.shape[1]] = block.astype(jnp.bfloat16)
        at += block.shape[1]


def take(refs, counts):
    out = []
    for count in counts:
        out.append(refs[:count])
        refs = refs[count:]
    return out, refs


def products_of(psi, left, widths, first, raw_out, inter):
    for d, line in enumerate(left):
        masked(psi[d], widths[first + d], raw_out.at[d])
        terms = line[0].shape[0]
        left_products(raw_out[d], lambda at: line[at // terms][...], inter.at[d])


def early_body(n_pair, counts, widths, *refs):
    left, refs = take(refs, [n_pair] * len(counts))
    psi, (raw_out, inter_out, left_out, sems) = take(refs, counts)
    copies = keep(left, left_out, sems)
    products_of(psi, left, widths, 0, raw_out, inter_out)
    for copy in copies:
        copy.wait()


def first_body(n_blk, n_pair, counts, src, widths, *refs):
    n_late = len(counts)
    n_early = n_blk - n_late
    left, refs = take(refs, [n_pair] * n_late)
    (right,), refs = take(refs, [n_pair])
    psi, refs = take(refs, counts)
    raw_in, inter_in, diag, right_diag, part_out, raw_out, left_out, dots_out, inter, sems = refs
    ready = []
    for j, (given, own) in enumerate(((inter_in, inter), (raw_in, raw_out))):
        ready.append(
            pltpu.make_async_copy(given, own.at[:n_early], sems.at[n_late * n_pair + j])
        )
        ready[-1].start()
    copies = keep(left, left_out, sems)
    inter[n_blk] = jnp.zeros_like(inter[n_blk])
    products_of(
        psi, left, widths, n_early, raw_out.at[n_early:], inter.at[n_early:n_blk]
    )
    for copy in ready:
        copy.wait()
    cols = diag.shape[2]
    zero = jnp.zeros((8, cols), jnp.float32)
    sums = [zero, zero]

    def emit(d, total):
        for h in range(2):
            part = slice(h * cols, (h + 1) * cols)
            raw = raw_out[d, :, part].astype(jnp.float32)
            image = total[:, part]
            if h == 0:
                image = image + diagonal(diag, right_diag, d, h) * raw
                sums[0] = sums[0] + fold(raw * raw)
            sums[1] = sums[1] + fold(raw * image)

    sum_terms(src, widths, inter, right, part_out, emit)
    spread([whole(x) for x in sums], dots_out)
    for copy in copies:
        copy.wait()


def send_rows(e, send, d, *refs):
    _, own_op = place_of()
    step = send.shape[2]
    rows = pl.ds(pl.multiple_of((own_op ^ e) * step, step), step)
    for j, ref in enumerate(refs):
        send[j, d] = ref[d, rows].astype(send.dtype)


def total_of(mine, other, d, h, cols):
    own = mine[d, :, h * cols : (h + 1) * cols].astype(jnp.float32)
    return own + other[d, :, (1 - h) * cols : (2 - h) * cols].astype(jnp.float32)


def sigma_body(mine, other, raw_in, diag, right_diag, sig_out, *sends):
    n_blk, _, cols = diag.shape
    for d in range(n_blk):
        for h in range(2):
            part = slice(h * cols, (h + 1) * cols)
            raw = raw_in[d, :, part].astype(jnp.float32)
            sigma = total_of(mine, other, d, h, cols) + diagonal(diag, right_diag, d, h) * raw
            sig_out[d, :, part] = sigma
        for e, send in enumerate(sends, 1):
            send_rows(2 * e, send, d, raw_in, sig_out)


def norm_theta(parts, count):
    tot = jnp.sum(parts, axis=0) * (1.0 / count)
    scale = lax.rsqrt(tot[:, 0:1] + EPS)
    return scale, tot[:, 1:2] * scale * scale


def second_body(n_blk, n_pair, count, src, widths, left_early, left_late, *refs):
    right, refs = refs[:n_pair], refs[n_pair:]
    parts, raw_in, sig, diag, right_diag, dots_out, own_out = refs[:7]
    sends, (inter, corr, fld, part_out, held, sems) = refs[7:-6], refs[-6:]
    copies = []
    n_early = left_early.shape[0]
    for d in range(n_blk):
        kept = left_early.at[d] if d < n_early else left_late.at[d - n_early]
        copies.append(pltpu.make_async_copy(kept, held.at[d], sems.at[d]))
        copies[-1].start()
    inter[n_blk] = jnp.zeros_like(inter[n_blk])
    scale, theta = norm_theta(parts[...], count)
    cols = diag.shape[2]
    halves = []
    for h in range(2):
        part = slice(h * cols, (h + 1) * cols)
        vv = vc = vs = jnp.zeros((8, cols), jnp.float32)
        for d in range(n_blk):
            vec = raw_in[d, :, part].astype(jnp.float32) * scale
            sigma = sig[d, :, part] * scale
            den = diagonal(diag, right_diag, d, h) - theta
            item = (sigma - theta * vec) * den / jnp.maximum(den * den, 0.25)
            corr[d, :, part] = item
            vv, vc = vv + fold(vec * vec), vc + fold(vec * item)
            if h == 0:
                vs = vs + fold(vec * sigma)
        halves.append((whole(vv), whole(vc), vs))
    along = (halves[0][1] + halves[1][1]) / jnp.maximum(halves[0][0] + halves[1][0], 1e-30)
    terms = held.shape[2]
    for copy in copies:
        copy.wait()
    for d in range(n_blk):
        for h in range(2):
            part = slice(h * cols, (h + 1) * cols)
            vec = raw_in[d, :, part].astype(jnp.float32) * scale
            fld[d, :, part] = (corr[d, :, part] - along * vec).astype(jnp.bfloat16)
        left_products(fld[d], lambda at: held[d, at // terms], inter.at[d])
    zero = jnp.zeros((8, cols), jnp.float32)
    sums = [zero for _ in range(5)]

    def emit(d, total):
        for h in range(2):
            part = slice(h * cols, (h + 1) * cols)
            field = fld[d, :, part].astype(jnp.float32)
            raw = raw_in[d, :, part].astype(jnp.float32)
            image = total[:, part]
            if h == 0:
                image = image + diagonal(diag, right_diag, d, h) * field
                for j, prod in enumerate((field * field, raw * field, field * sig[d, :, part])):
                    sums[j] = sums[j] + fold(prod)
            sums[3] = sums[3] + fold(raw * image)
            sums[4] = sums[4] + fold(field * image)
        for e, send in enumerate(sends, 1):
            send_rows(e, send, d, *((part_out,) if e % 2 else (fld, part_out)))
        rows = pl.ds(pl.multiple_of(own_op * step, step), step)
        for j, ref in enumerate((raw_in, sig, fld, part_out)):
            own_out[j, d] = ref[d, rows].astype(own_out.dtype)

    _, own_op = place_of()
    step = own_out.shape[2]
    sum_terms(src, widths, inter, right, part_out, emit)
    vv, vc, vs = halves[0]
    ff, vf, fs, vt, ft = (whole(x) for x in sums)
    spread([vv, vc, whole(vs), ff, vf * scale, fs * scale, vt * scale, ft], dots_out)


def ritz_pair(theta, h_mix, h_two):
    diff, twice = theta - h_two, 2.0 * h_mix
    size = jnp.sqrt(diff * diff + twice * twice)
    some = size > 0.0
    safe = jnp.where(some, size, 1.0)
    big = jnp.sqrt(0.5 + 0.5 * jnp.abs(diff) / safe)
    small = 0.5 * jnp.abs(twice) / (safe * big)
    sine = jnp.where(diff >= 0.0, small, big)
    cosine = jnp.where(diff >= 0.0, big, small)
    sine = jnp.where(some, sine, 0.0)
    cosine = jnp.where(some, cosine, 1.0)
    upward = (twice > 0.0) | ((twice == 0.0) & (diff < 0.0))
    return sine, jnp.where(upward, -cosine, cosine), 0.5 * (theta + h_two) - 0.5 * size


def third_body(n_blk, n_op, count, slots, parts1, parts2, diag, right_diag, own, *refs):
    n_far = n_op // 2 - 1
    got1, got2 = refs[:n_far], refs[n_far : n_far + n_op - 1]
    new_out, res_out, energy_out = refs[n_far + n_op - 1 :]
    step, cols = new_out.shape[1], new_out.shape[2] // n_op
    own_blk, own_op = place_of()
    scale, theta = norm_theta(parts1[...], count)
    pairs = parts2[...].reshape(n_blk * n_op // 2, 2, *parts2.shape[1:])
    pairs = pairs[:, 0] + pairs[:, 1]
    vv, vc, vs, ff, vf, fs, vt, ft = (pairs[:, 0, j : j + 1] for j in range(8))

    def mean(x):
        return jnp.sum(x, axis=0, keepdims=True) * (1.0 / count)

    def nearest(vv, vc):
        return vc / jnp.maximum(vv, 1e-30)

    along = mean(vc)
    beta = nearest(vv, vc) - along
    norm_sq = mean(ff + 2.0 * beta * vf + beta * beta * vv)
    unit = lax.rsqrt(jnp.maximum(norm_sq, 0.0) + EPS)
    v_s1 = unit * mean(vt + beta * vs)
    u_s0 = unit * mean(fs + beta * vs)
    u_s1 = unit * unit * mean(ft + beta * (vt + fs) + beta * beta * vs)
    cv, cu, energy = ritz_pair(theta, 0.5 * (v_s1 + u_s0), u_s1)
    energy_out[0] = jnp.max(energy)
    cu = cu * unit
    mine = pl.ds(pl.multiple_of(own_op * step, step), step)
    for e in range(0, n_op, 2):
        there = own_blk * n_op + (own_op ^ e)
        pair = parts2[there] + parts2[own_blk * n_op + (own_op ^ e ^ 1)]
        on_vec = cv + cu * (nearest(pair[:, 0:1], pair[:, 1:2]) - along)
        for h in range(2):
            at = pl.multiple_of((own_op ^ e ^ h) * cols, LANES)
            part, crossed = slice(h * cols, (h + 1) * cols), slice((1 - h) * cols, (2 - h) * cols)
            for d in range(n_blk):
                dmat = diag[d, mine] + right_diag[:, pl.ds(at, cols)]
                blocks = [own.at[j] for j in range(4)]
                if e:
                    far, near = got1[e // 2 - 1], got2[e - 1]
                    blocks = far.at[0], far.at[1], near.at[0], near.at[1]
                raw, sigma, fld, image = (x[d, :, part].astype(jnp.float32) for x in blocks)
                vec, sigma = raw * scale, sigma * scale
                image = image + got2[e][0, d, :, crossed].astype(jnp.float32) + dmat * fld
                newvec = on_vec * vec + cu * fld
                res = on_vec * sigma + cu * image - energy * newvec
                new_out[slots[d], :, pl.ds(at, cols)] = newvec.astype(jnp.bfloat16)
                res_out[slots[d], :, pl.ds(at, cols)] = res.astype(jnp.bfloat16)


def per_device(
    psi, left_ops, right_ops, term_shift, slot_sector, sector_width, diag_left, diag_right
):
    n_blk, n_op = lax.axis_size("blk"), lax.axis_size("op")
    _, rows, ncols = psi.shape
    terms, _, width, _ = right_ops.shape
    n_pair = n_op // 2
    cols = diag_right.shape[0] // n_op
    step = rows // n_op
    count = float(n_blk * rows * ncols)
    n_dev = n_blk * n_op
    bf16, f32, i32 = jnp.bfloat16, jnp.float32, jnp.int32
    last = sorted(range(1, n_blk), key=lambda d: min(d, n_blk - d))[-1]

    def pack():
        first = swap(term_shift, 1, n_op)
        sent = kernel(
            functools.partial(pack_body, n_blk, n_op),
            [(term_shift, SMEM), (first, SMEM), (psi, HBM), (right_ops, HBM)],
            [((rows, 2 * cols if d in (0, last) else cols), bf16, VMEM) for d in range(n_blk)]
            + [((terms * width + 16, 2 * cols), bf16, VMEM)] * n_pair,
            [pltpu.VMEM(right_ops.shape, bf16), pltpu.SemaphoreType.DMA((2 * n_blk + 1,))],
            nbytes=1 << 20,
        )
        return sent[:n_blk], sent[n_blk:]

    def table(right):
        return kernel(
            functools.partial(table_body, n_blk, terms),
            [(slot_sector, SMEM), (sector_width, SMEM), (diag_left, VMEM), (diag_right[None], VMEM)]
            + [(block, VMEM) for block in right],
            [((n_blk * n_pair * terms,), i32, SMEM)]
            + [((n_blk,), i32, SMEM)] * 2
            + [((n_blk, rows, LANES), f32, VMEM), ((1, n_op * cols), f32, VMEM)],
        )

    def inputs(left, psi, those):
        blocks = [left[d, 2 * e] for d in those for e in range(n_pair)]
        halves = [half for d in those for half in psi[d]]
        return [(x, VMEM) for x in blocks], [(x, VMEM) for x in halves], [len(psi[d]) for d in those]

    def early(left, psi, n_early, tables):
        left_ins, psi_ins, counts = inputs(left, psi, range(n_early))
        return kernel(
            functools.partial(early_body, n_pair, counts),
            [(tables[1], SMEM)] + left_ins + psi_ins,
            [
                ((n_early, rows, 2 * cols), bf16, VMEM),
                ((n_early, n_pair * terms, rows, 2 * cols), bf16, VMEM),
                ((n_early, n_pair, terms, rows, rows), bf16, HBM),
            ],
            [pltpu.SemaphoreType.DMA((n_early * n_pair,))],
            flops=2 * n_early * rows * rows * 2 * cols * terms * n_pair,
            nbytes=4 << 20,
        )

    left, psi_by, right, (src, widths, slots, *both), (raw_early, inter_early, left_early) = gather(
        left_ops[:, 0], n_blk, n_op, pack, table, early
    )
    n_early = raw_early.shape[0]
    n_late = n_blk - n_early
    left_ins, psi_ins, counts = inputs(left, psi_by, range(n_early, n_blk))
    right_ins = [(block, VMEM) for block in right]
    diags = [(x, VMEM) for x in both]

    tables = [(src, SMEM), (widths, SMEM)]
    narrow = ((n_blk, rows, 2 * cols), bf16, VMEM)
    dots = ((n_dev, 1, LANES), f32, VMEM)
    wide = ((n_blk, rows, 2 * cols), f32, VMEM)
    sends = [((2 - e % 2, n_blk, step, 2 * cols), bf16, VMEM) for e in range(1, n_op)]
    inter = pltpu.VMEM((n_blk + 1, n_pair * terms, rows, 2 * cols), bf16)
    left_late = (n_late, n_pair, terms, rows, rows)
    cost = dict(flops=2 * n_blk * rows * 2 * cols * terms * n_pair * (rows + 2 * cols), nbytes=6 << 20)

    def totals(parts):
        return lax.all_to_all(parts, ("blk", "op"), 0, 0, tiled=True)

    part1, raw, kept, dots1 = kernel(
        functools.partial(first_body, n_blk, n_pair, counts),
        tables + left_ins + right_ins + psi_ins + [(raw_early, VMEM), (inter_early, VMEM)] + diags,
        [narrow, narrow, (left_late, bf16, HBM), dots],
        [inter, pltpu.SemaphoreType.DMA((n_late * n_pair + 2,))],
        **cost,
    )
    parts1 = totals(dots1)
    sig, *out1 = kernel(
        sigma_body,
        [(x, VMEM) for x in (part1, swap(part1, 1, n_op), raw)] + diags,
        [wide] + sends[1::2],
        nbytes=4 << 20,
    )
    got1 = [swap(block, 2 * e, n_op) for e, block in enumerate(out1, 1)]
    dots2, own, *out2 = kernel(
        functools.partial(second_body, n_blk, n_pair, count),
        tables + [(left_early, HBM), (kept, HBM)] + right_ins
        + [(x, VMEM) for x in (parts1, raw, sig)] + diags,
        [dots, ((4, n_blk, step, 2 * cols), bf16, VMEM)] + sends,
        [
            inter,
            pltpu.VMEM((n_blk, rows, 2 * cols), f32),
            pltpu.VMEM((n_blk, rows, 2 * cols), bf16),
            pltpu.VMEM((n_blk, rows, 2 * cols), bf16),
            pltpu.VMEM((n_blk, *left_late[1:]), bf16),
            pltpu.SemaphoreType.DMA((n_blk,)),
        ],
        flops=4 * cost["flops"],
        nbytes=24 << 20,
    )
    near, got1 = lax.optimization_barrier((out2[0], got1))
    parts2 = totals(dots2)
    got2 = [swap(near, 1, n_op)] + [swap(block, e, n_op) for e, block in enumerate(out2[1:], 2)]
    final = ((n_blk, step, n_op * cols), bf16, VMEM)
    new, res, energy = kernel(
        functools.partial(third_body, n_blk, n_op, count),
        [(slots, SMEM)] + [(x, VMEM) for x in (parts1, parts2)] + diags
        + [(x, VMEM) for x in (own, *got1, *got2)],
        [final, final, ((1,), f32, SMEM)],
        nbytes=4 << 20,
    )
    return new, res, energy


def solution(mesh):
    placed = (
        P(("grp", "blk"), None, None),
        P("op", ("grp", "blk"), None, None),
        P("op", ("grp", "blk"), None, None),
        P("op"),
        P("grp"),
        P("grp"),
        P("grp", None),
        P(("grp", "blk")),
    )

    def body(*args):
        psi, left_ops, right_ops, diag_right = args[0], args[1], args[2], args[7]
        n_op = mesh.shape["op"]
        cols = diag_right.shape[0] // n_op
        fits = (
            psi.shape[0] == 1
            and diag_right.shape[0] % n_op == 0
            and cols == LANES
            and n_op % 2 == 0
            and cols % right_ops.shape[2] == 0
            and cols // right_ops.shape[2] * n_op == right_ops.shape[1]
            and psi.shape[1] % (16 * n_op) == 0
            and n_op & (n_op - 1) == 0
            and mesh.shape["blk"] > n_op.bit_length() - 1
        )
        return (per_device if fits else per_device_general)(*args)

    return jax.shard_map(
        body,
        mesh=mesh,
        in_specs=placed,
        out_specs=(P("grp", "op", "blk"), P("grp", "op", "blk"), P("grp")),
        check_vma=False,
    )
```

```python
import functools

import jax
import jax.numpy as jnp
from jax import lax
from jax.experimental import pallas as pl
from jax.experimental.pallas import tpu as pltpu
from jax.sharding import PartitionSpec as P

EPS = 1e-06
LANES = 128
VMEM_LIMIT = 20 * 1024 * 1024


def per_device_general(
    psi, left_ops, right_ops, term_shift, slot_sector, sector_width, diag_left, diag_right
):
    sec_dev, rows, ncols = psi.shape
    nsec = slot_sector.shape[0]
    terms_dev = left_ops.shape[0]
    right_local = right_ops.shape[1]
    right_width = right_ops.shape[2]
    local_cols = diag_right.shape[0]
    count = float(nsec * rows * ncols)
    match = slot_sector[:, None] == jnp.arange(nsec)[None, :]
    widths = jnp.sum(jnp.where(match, sector_width[None, :], 0), axis=1)
    mask_all = (jnp.arange(rows)[None, :] < widths[:, None]).astype(jnp.float32)
    own_mask = lax.dynamic_slice_in_dim(mask_all, lax.axis_index("blk") * sec_dev, sec_dev, 0)
    raw = psi.astype(jnp.float32) * own_mask[:, :, None]
    squares = lax.psum(jnp.sum(raw * raw), "blk")
    v_left = (raw * lax.rsqrt(squares / count + EPS)).astype(jnp.bfloat16)
    onehots = (
        slot_sector[None, None, :] == slot_sector[None, :, None] - term_shift[:, None, None]
    ).astype(jnp.bfloat16)
    op_rows = rows // lax.axis_size("op")
    op_start = lax.axis_index("op") * op_rows
    dmat = diag_left[:, :, None] + diag_right[None, None, :]

    def left_local(field):
        return jnp.einsum(
            "ksij,sjc->ksic", left_ops, field, preferred_element_type=jnp.float32
        ).astype(jnp.bfloat16)

    def right_part(moved_in):
        flat = moved_in.reshape(terms_dev, nsec, rows * local_cols)
        shifted = jnp.einsum(
            "kts,ksx->ktx", onehots, flat, preferred_element_type=jnp.float32
        ).astype(jnp.bfloat16)
        shifted = shifted.reshape(terms_dev, nsec, rows, right_local, right_width)
        accum = jnp.einsum(
            "ktwrc,krdc->twrd", shifted, right_ops, preferred_element_type=jnp.float32
        )
        return accum.reshape(nsec, rows, local_cols) * mask_all[:, :, None]

    def op_total(partial_value):
        return lax.psum(partial_value.astype(jnp.bfloat16), "op").astype(jnp.float32)

    def final_rows(array):
        return lax.dynamic_slice_in_dim(array, op_start, op_rows, 1)

    def reduce_dots(values):
        sums = lax.psum(values, "blk")
        return tuple((item / count for item in sums))

    moved_first, v_moved = (
        lax.all_to_all(left_local(v_left), "blk", split_axis=3, concat_axis=1, tiled=True),
        lax.all_to_all(v_left[None], "blk", split_axis=3, concat_axis=1, tiled=True),
    )
    v_right = v_moved[0]
    vec32 = v_right.astype(jnp.float32)
    first_sigma = op_total(right_part(moved_first)) + dmat * vec32
    theta = reduce_dots((jnp.sum(vec32 * first_sigma),))[0]
    resid = first_sigma - theta * vec32
    den = dmat - theta
    corr = resid * den / jnp.maximum(den * den, 0.25)
    along = reduce_dots((jnp.sum(vec32 * corr),))[0]
    orth = corr - along * vec32
    norm_sq = reduce_dots((jnp.sum(orth * orth),))[0]
    update = (orth * lax.rsqrt(norm_sq + EPS)).astype(jnp.bfloat16)
    upd32 = update.astype(jnp.float32)
    upd_left = lax.all_to_all(update, "blk", split_axis=0, concat_axis=2, tiled=True)
    moved_second = lax.all_to_all(
        left_local(upd_left), "blk", split_axis=3, concat_axis=1, tiled=True
    )
    second_sigma = op_total(right_part(moved_second)) + dmat * upd32
    v_s1, u_s0, u_s1 = reduce_dots(
        (jnp.sum(vec32 * second_sigma), jnp.sum(upd32 * first_sigma), jnp.sum(upd32 * second_sigma))
    )
    h_mix = 0.5 * (v_s1 + u_s0)
    coef_v, coef_u, energy = ritz(theta, h_mix, u_s1)
    newvec = coef_v * vec32 + coef_u * upd32
    image = coef_v * first_sigma + coef_u * second_sigma
    new_out = final_rows(newvec.astype(jnp.bfloat16))
    res_out = final_rows((image - energy * newvec).astype(jnp.bfloat16))
    return (new_out, res_out, jnp.reshape(energy, (1,)))


def ritz(theta, h_mix, h_two):
    angle = 0.5 * jnp.arctan2(2.0 * h_mix, theta - h_two)
    sine = jnp.sin(angle)
    flip = jnp.where(sine > 0, -1.0, 1.0)
    coef_v = -sine * flip
    coef_u = jnp.cos(angle) * flip
    half = 0.5 * (theta - h_two)
    energy = 0.5 * (theta + h_two) - jnp.sqrt(half * half + h_mix * h_mix)
    return coef_v, coef_u, energy


VMEM, SMEM, HBM = pltpu.VMEM, pltpu.SMEM, pltpu.HBM


def kernel(body, ins, outs, scratch=(), flops=0, nbytes=0, in_place=None):
    return pl.pallas_call(
        body,
        out_shape=[
            HBM(shape, dtype) if space == HBM else jax.ShapeDtypeStruct(shape, dtype)
            for shape, dtype, space in outs
        ],
        in_specs=[pl.BlockSpec(memory_space=space) for _, space in ins],
        out_specs=[pl.BlockSpec(memory_space=space) for _, _, space in outs],
        scratch_shapes=list(scratch),
        input_output_aliases=in_place or {},
        compiler_params=pltpu.CompilerParams(vmem_limit_bytes=VMEM_LIMIT),
        cost_estimate=pl.CostEstimate(flops=flops, bytes_accessed=nbytes, transcendentals=0),
    )(*[pltpu.with_memory_space_constraint(x, HBM) if space == HBM else x for x, space in ins])


def ring_at(place, n_blk):
    place = place % n_blk if isinstance(place, int) else lax.rem(place + n_blk, n_blk)
    even, odd = 2 * place, 2 * (n_blk - place) - 1
    if isinstance(place, int):
        return even if even < n_blk else odd
    return jnp.where(even < n_blk, even, odd)


def ring_place(index, n_blk):
    return jnp.where(lax.rem(index, 2) == 1, n_blk - (index + 1) // 2, index // 2)


def onward(block, d, n_blk):
    pairs = [(ring_at(i, n_blk), ring_at(i + d, n_blk)) for i in range(n_blk)]
    return lax.ppermute(block, "blk", pairs)


def swap(block, e, n_op):
    return lax.ppermute(block, "op", [(i, i ^ e) for i in range(n_op)])


def gather(own, n_blk, n_op, pack, table, early):
    bits = [1 << b for b in reversed(range(1, n_op.bit_length() - 1))]
    order = sorted(range(1, n_blk), key=lambda d: min(d, n_blk - d))
    left, psi, right, tables, columns = {(0, 0): own}, {}, None, None, None
    waiting, across, late, made = {(0, 0): 0}, {}, None, None
    for j in range(n_blk + len(bits)):
        new, moved = {}, {}
        for (d, e), done in waiting.items():
            if e == 0 and d + 1 < n_blk:
                new[d + 1, 0] = onward(left[d, 0], 1, n_blk), 0
            for b in range(done, len(bits)):
                new[d, e ^ bits[b]] = swap(left[d, e], bits[b], n_op), b + 1
        left.update({key: block for key, (block, _) in new.items()})
        kept = {key: block for key, (block, _) in new.items() if key[1] == 0}
        kept.update(across)
        across = {key: block for key, (block, _) in new.items() if key[1] != 0}
        if late is not None:
            moved["psi"] = late
        if j == 0:
            columns, packed = pack()
            right = [packed[0]]
            right += [swap(part, 2 * e, n_op) for e, part in enumerate(packed[1:], 1)]
            moved["columns"] = columns
        if j == 0:
            moved["right"] = right
        if j == 1:
            moved["tables"] = table(right)
        if j == n_blk - 1 and j >= len(bits) + 1:
            n_early = min(2, n_blk - 1)
            psi[0] = [columns[0]]
            moved["early"] = early(left, psi, n_early, tables)
        if 2 <= j < n_blk:
            moved["other"] = swap(psi[order[j - 2]][0], 1, n_op)
        late = onward(columns[order[j]], order[j], n_blk) if j < n_blk - 1 else None
        if not kept:
            break
        waiting = {key: done for key, (_, done) in new.items()}
        kept, moved = lax.optimization_barrier((kept, moved))
        left.update(kept)
        right, tables = moved.get("right", right), moved.get("tables", tables)
        columns = moved.get("columns", columns)
        made = moved.get("early", made)
        if "psi" in moved:
            psi[order[j - 1]] = [moved["psi"]]
        if "other" in moved:
            psi[order[j - 2]].append(moved["other"])
    return left, psi, right, tables, made


def place_of():
    return lax.axis_index("blk"), lax.axis_index("op")


def pack_body(n_blk, n_op, shift, _, psi, right_in, *outs):
    n_pair = n_op // 2
    psi_out, right_out, right, sems = outs[:n_blk], outs[n_blk : n_blk + n_pair], outs[-2], outs[-1]
    terms, local, width, _ = right.shape
    cols = local * width // n_op
    per = cols // width
    own_blk, own_op = place_of()
    fetch = pltpu.make_async_copy(right_in, right, sems.at[2 * n_blk])
    fetch.start()
    copies = []
    for d in range(n_blk):
        there = ring_at(ring_place(own_blk, n_blk) + d, n_blk) * n_op
        for h in range(psi_out[d].shape[1] // cols):
            start = pl.multiple_of((there + (own_op ^ h)) * cols, LANES)
            copy = pltpu.make_async_copy(
                psi.at[0, :, pl.ds(start, cols)],
                psi_out[d].at[:, h * cols : (h + 1) * cols],
                sems.at[2 * d + h],
            )
            copy.start()
            copies.append(copy)
    lane = lax.broadcasted_iota(jnp.int32, (16, 2 * cols), 1)
    line = jnp.zeros((16, 2 * cols), jnp.float32)
    for k in range(terms):
        line = jnp.where(lane == k, shift[k].astype(jnp.float32), line)
    square = [lax.broadcasted_iota(jnp.int32, (width, width), axis) for axis in (0, 1)]
    unit = (square[0] == square[1]).astype(jnp.bfloat16)
    fetch.wait()
    for e in range(n_pair):
        for k in range(terms):
            turned = []
            for h in range(2):
                first = (own_op ^ (2 * e) ^ h) * per
                for r in range(per):
                    turned.append(
                        lax.dot_general(
                            right[k, first + r], unit, (((0,), (0,)), ((), ())),
                            preferred_element_type=jnp.float32,
                        )
                    )
            side_by_side = jnp.concatenate(turned, axis=1).astype(jnp.bfloat16)
            right_out[e][k * width : (k + 1) * width] = side_by_side
        right_out[e][terms * width :] = line.astype(jnp.bfloat16)
    for copy in copies:
        copy.wait()


def table_body(n_blk, terms, sector, width, left_diag, right_diag, *refs):
    tails, src, widths, slots, diag, right_out = refs[:-5], *refs[-5:]
    right_out[...] = right_diag[...]
    n_pair = len(tails)
    rows, cols = tails[0].shape
    own_blk, _ = place_of()
    lane = lax.broadcasted_iota(jnp.int32, (16, cols), 1)
    for d in range(n_blk):
        slot = ring_at(ring_place(own_blk, n_blk) - d, n_blk)
        slots[d] = slot
        widths[d] = width[sector[slot]]
    for e in range(n_pair):
        tail = tails[e][rows - 16 :].astype(jnp.float32)
        for k in range(terms):
            shift = jnp.max(jnp.where(lane == k, tail, -1e9)).astype(jnp.int32)
            for t in range(n_blk):
                want = sector[slots[t]] - shift
                found = jnp.int32(n_blk)
                for d in range(n_blk):
                    found = jnp.where(sector[slots[d]] == want, d, found)
                src[(t * n_pair + e) * terms + k] = found
    for d in range(n_blk):
        row = left_diag[pl.ds(slots[d], 1), :]
        diag[d] = jnp.transpose(jnp.broadcast_to(row, (diag.shape[2], row.shape[1])))


def diagonal(diag, right_diag, d, h):
    cols = diag.shape[2]
    _, own_op = place_of()
    start = pl.multiple_of((own_op ^ h) * cols, LANES)
    return diag[d] + right_diag[:, pl.ds(start, cols)]


def row_mask(width, shape):
    return lax.broadcasted_iota(jnp.int32, shape, 0) < width


def fold(x):
    return jnp.sum(x.reshape(-1, 8, x.shape[-1]), axis=0)


def whole(x):
    return jnp.sum(jnp.sum(x, axis=0, keepdims=True), axis=1, keepdims=True)


def spread(values, out):
    lane = lax.broadcasted_iota(jnp.int32, out.shape[1:], 1)
    row = jnp.zeros(out.shape[1:], jnp.float32)
    for j, value in enumerate(values):
        row = jnp.where(lane == j, value, row)
    for d in range(out.shape[0]):
        out[d] = row


def by_block(packed, terms, k):
    rows, cols = packed.shape
    width = (rows - 16) // terms
    lane = lax.broadcasted_iota(jnp.int32, (width, cols), 1)
    block = packed[k * width : (k + 1) * width].astype(jnp.float32)
    parts = []
    for r in range(cols // width):
        inside = (lane >= r * width) & (lane < (r + 1) * width)
        parts.append(jnp.where(inside, block, 0.0).astype(jnp.bfloat16))
    return jnp.concatenate(parts, axis=0)


def left_products(block, left, inter):
    n_terms, rows, cols = inter.shape
    at = 0
    while at < n_terms:
        ops = left(at)
        terms = ops.shape[0]
        prod = jnp.dot(ops.reshape(terms * rows, rows), block, preferred_element_type=jnp.float32)
        inter[at : at + terms] = prod.astype(jnp.bfloat16).reshape(terms, rows, cols)
        at += terms


def sum_terms(src, widths, inter, right, out, emit):
    n_blk, n_terms, _, _ = inter.shape
    n_blk -= 1
    terms = n_terms // len(right)
    turned = [by_block(right[j // terms], terms, j % terms) for j in range(n_terms)]
    for t in range(n_blk):
        total = None
        for j in range(n_terms):
            part = jnp.dot(
                inter[src[t * n_terms + j], j], turned[j], preferred_element_type=jnp.float32
            )
            total = part if total is None else total + part
        total = jnp.where(row_mask(widths[t], total.shape), total, 0.0)
        out[t] = total.astype(jnp.bfloat16)
        emit(t, total)


def keep(left, left_out, sems):
    copies = []
    for d, line in enumerate(left):
        for e, ref in enumerate(line):
            copies.append(pltpu.make_async_copy(ref, left_out.at[d, e], sems.at[d * len(line) + e]))
            copies[-1].start()
    return copies


def masked(psi, width, out):
    at = 0
    for ref in psi:
        block = ref[...].astype(jnp.float32)
        block = jnp.where(row_mask(width, block.shape), block, 0.0)
        out[:, at : at + block.shape[1]] = block.astype(jnp.bfloat16)
        at += block.shape[1]


def take(refs, counts):
    out = []
    for count in counts:
        out.append(refs[:count])
        refs = refs[count:]
    return out, refs


def products_of(psi, left, widths, first, raw_out, inter):
    for d, line in enumerate(left):
        masked(psi[d], widths[first + d], raw_out.at[d])
        terms = line[0].shape[0]
        left_products(raw_out[d], lambda at: line[at // terms][...], inter.at[d])


def early_body(n_pair, counts, widths, *refs):
    left, refs = take(refs, [n_pair] * len(counts))
    psi, (raw_out, inter_out, left_out, sems) = take(refs, counts)
    copies = keep(left, left_out, sems)
    inter_out[inter_out.shape[0] - 1] = jnp.zeros_like(inter_out[0])
    products_of(psi, left, widths, 0, raw_out, inter_out)
    for copy in copies:
        copy.wait()


def first_body(n_blk, n_pair, counts, src, widths, *refs):
    n_late = len(counts)
    n_early = n_blk - n_late
    left, refs = take(refs, [n_pair] * n_late)
    (right,), refs = take(refs, [n_pair])
    psi, refs = take(refs, counts)
    diag, right_diag, _, _, raw_out, inter, part_out, left_out, dots_out, sems = refs
    copies = keep(left, left_out, sems)
    products_of(
        psi, left, widths, n_early, raw_out.at[n_early:], inter.at[n_early:n_blk]
    )
    cols = diag.shape[2]
    zero = jnp.zeros((8, cols), jnp.float32)
    sums = [zero, zero]

    def emit(d, total):
        for h in range(2):
            part = slice(h * cols, (h + 1) * cols)
            raw = raw_out[d, :, part].astype(jnp.float32)
            image = total[:, part]
            if h == 0:
                image = image + diagonal(diag, right_diag, d, h) * raw
                sums[0] = sums[0] + fold(raw * raw)
            sums[1] = sums[1] + fold(raw * image)

    sum_terms(src, widths, inter, right, part_out, emit)
    spread([whole(x) for x in sums], dots_out)
    for copy in copies:
        copy.wait()


def send_rows(e, send, d, *refs):
    _, own_op = place_of()
    step = send.shape[2]
    rows = pl.ds(pl.multiple_of((own_op ^ e) * step, step), step)
    for j, ref in enumerate(refs):
        send[j, d] = ref[d, rows].astype(send.dtype)


def total_of(mine, other, d, h, cols):
    own = mine[d, :, h * cols : (h + 1) * cols].astype(jnp.float32)
    return own + other[d, :, (1 - h) * cols : (2 - h) * cols].astype(jnp.float32)


def sigma_body(mine, other, raw_in, diag, right_diag, sig_out, *sends):
    n_blk, _, cols = diag.shape
    for d in range(n_blk):
        for h in range(2):
            part = slice(h * cols, (h + 1) * cols)
            raw = raw_in[d, :, part].astype(jnp.float32)
            sigma = total_of(mine, other, d, h, cols) + diagonal(diag, right_diag, d, h) * raw
            sig_out[d, :, part] = sigma
        for e, send in enumerate(sends, 1):
            send_rows(2 * e, send, d, raw_in, sig_out)


def norm_theta(parts, count):
    tot = jnp.sum(parts, axis=0) * (1.0 / count)
    scale = lax.rsqrt(tot[:, 0:1] + EPS)
    return scale, tot[:, 1:2] * scale * scale


def second_body(n_blk, n_pair, count, src, widths, left_early, left_late, *refs):
    right, refs = refs[:n_pair], refs[n_pair:]
    parts, raw_in, sig, diag, right_diag, dots_out, own_out = refs[:7]
    sends, (inter, corr, fld, part_out, held, sems) = refs[7:-6], refs[-6:]
    copies = []
    n_early = left_early.shape[0]
    for d in range(n_blk):
        kept = left_early.at[d] if d < n_early else left_late.at[d - n_early]
        copies.append(pltpu.make_async_copy(kept, held.at[d], sems.at[d]))
        copies[-1].start()
    inter[n_blk] = jnp.zeros_like(inter[n_blk])
    scale, theta = norm_theta(parts[...], count)
    cols = diag.shape[2]
    halves = []
    for h in range(2):
        part = slice(h * cols, (h + 1) * cols)
        vv = vc = vs = jnp.zeros((8, cols), jnp.float32)
        for d in range(n_blk):
            vec = raw_in[d, :, part].astype(jnp.float32) * scale
            sigma = sig[d, :, part] * scale
            den = diagonal(diag, right_diag, d, h) - theta
            item = (sigma - theta * vec) * den / jnp.maximum(den * den, 0.25)
            corr[d, :, part] = item
            vv, vc = vv + fold(vec * vec), vc + fold(vec * item)
            if h == 0:
                vs = vs + fold(vec * sigma)
        halves.append((whole(vv), whole(vc), vs))
    along = (halves[0][1] + halves[1][1]) / jnp.maximum(halves[0][0] + halves[1][0], 1e-30)
    terms = held.shape[2]
    for copy in copies:
        copy.wait()
    for d in range(n_blk):
        for h in range(2):
            part = slice(h * cols, (h + 1) * cols)
            vec = raw_in[d, :, part].astype(jnp.float32) * scale
            fld[d, :, part] = (corr[d, :, part] - along * vec).astype(jnp.bfloat16)
        left_products(fld[d], lambda at: held[d, at // terms], inter.at[d])
    zero = jnp.zeros((8, cols), jnp.float32)
    sums = [zero for _ in range(5)]

    def emit(d, total):
        for h in range(2):
            part = slice(h * cols, (h + 1) * cols)
            field = fld[d, :, part].astype(jnp.float32)
            raw = raw_in[d, :, part].astype(jnp.float32)
            image = total[:, part]
            if h == 0:
                image = image + diagonal(diag, right_diag, d, h) * field
                for j, prod in enumerate((field * field, raw * field, field * sig[d, :, part])):
                    sums[j] = sums[j] + fold(prod)
            sums[3] = sums[3] + fold(raw * image)
            sums[4] = sums[4] + fold(field * image)
        for e, send in enumerate(sends, 1):
            send_rows(e, send, d, *((part_out,) if e % 2 else (fld, part_out)))
        rows = pl.ds(pl.multiple_of(own_op * step, step), step)
        for j, ref in enumerate((raw_in, sig, fld, part_out)):
            own_out[j, d] = ref[d, rows].astype(own_out.dtype)

    _, own_op = place_of()
    step = own_out.shape[2]
    sum_terms(src, widths, inter, right, part_out, emit)
    vv, vc, vs = halves[0]
    ff, vf, fs, vt, ft = (whole(x) for x in sums)
    spread([vv, vc, whole(vs), ff, vf * scale, fs * scale, vt * scale, ft], dots_out)


def ritz_pair(theta, h_mix, h_two):
    diff, twice = theta - h_two, 2.0 * h_mix
    size = jnp.sqrt(diff * diff + twice * twice)
    some = size > 0.0
    safe = jnp.where(some, size, 1.0)
    big = jnp.sqrt(0.5 + 0.5 * jnp.abs(diff) / safe)
    small = 0.5 * jnp.abs(twice) / (safe * big)
    sine = jnp.where(diff >= 0.0, small, big)
    cosine = jnp.where(diff >= 0.0, big, small)
    sine = jnp.where(some, sine, 0.0)
    cosine = jnp.where(some, cosine, 1.0)
    upward = (twice > 0.0) | ((twice == 0.0) & (diff < 0.0))
    return sine, jnp.where(upward, -cosine, cosine), 0.5 * (theta + h_two) - 0.5 * size


def third_body(n_blk, n_op, count, slots, parts1, parts2, diag, right_diag, own, *refs):
    n_far = n_op // 2 - 1
    got1, got2 = refs[:n_far], refs[n_far : n_far + n_op - 1]
    new_out, res_out, energy_out = refs[n_far + n_op - 1 :]
    step, cols = new_out.shape[1], new_out.shape[2] // n_op
    own_blk, own_op = place_of()
    scale, theta = norm_theta(parts1[...], count)
    pairs = parts2[...].reshape(n_blk * n_op // 2, 2, *parts2.shape[1:])
    pairs = pairs[:, 0] + pairs[:, 1]
    vv, vc, vs, ff, vf, fs, vt, ft = (pairs[:, 0, j : j + 1] for j in range(8))

    def mean(x):
        return jnp.sum(x, axis=0, keepdims=True) * (1.0 / count)

    def nearest(vv, vc):
        return vc / jnp.maximum(vv, 1e-30)

    along = mean(vc)
    beta = nearest(vv, vc) - along
    norm_sq = mean(ff + 2.0 * beta * vf + beta * beta * vv)
    unit = lax.rsqrt(jnp.maximum(norm_sq, 0.0) + EPS)
    v_s1 = unit * mean(vt + beta * vs)
    u_s0 = unit * mean(fs + beta * vs)
    u_s1 = unit * unit * mean(ft + beta * (vt + fs) + beta * beta * vs)
    cv, cu, energy = ritz_pair(theta, 0.5 * (v_s1 + u_s0), u_s1)
    energy_out[0] = jnp.max(energy)
    cu = cu * unit
    mine = pl.ds(pl.multiple_of(own_op * step, step), step)
    for e in range(0, n_op, 2):
        there = own_blk * n_op + (own_op ^ e)
        pair = parts2[there] + parts2[own_blk * n_op + (own_op ^ e ^ 1)]
        on_vec = cv + cu * (nearest(pair[:, 0:1], pair[:, 1:2]) - along)
        for h in range(2):
            at = pl.multiple_of((own_op ^ e ^ h) * cols, LANES)
            part, crossed = slice(h * cols, (h + 1) * cols), slice((1 - h) * cols, (2 - h) * cols)
            for d in range(n_blk):
                dmat = diag[d, mine] + right_diag[:, pl.ds(at, cols)]
                blocks = [own.at[j] for j in range(4)]
                if e:
                    far, near = got1[e // 2 - 1], got2[e - 1]
                    blocks = far.at[0], far.at[1], near.at[0], near.at[1]
                raw, sigma, fld, image = (x[d, :, part].astype(jnp.float32) for x in blocks)
                vec, sigma = raw * scale, sigma * scale
                image = image + got2[e][0, d, :, crossed].astype(jnp.float32) + dmat * fld
                newvec = on_vec * vec + cu * fld
                res = on_vec * sigma + cu * image - energy * newvec
                new_out[slots[d], :, pl.ds(at, cols)] = newvec.astype(jnp.bfloat16)
                res_out[slots[d], :, pl.ds(at, cols)] = res.astype(jnp.bfloat16)


def per_device(
    psi, left_ops, right_ops, term_shift, slot_sector, sector_width, diag_left, diag_right
):
    n_blk, n_op = lax.axis_size("blk"), lax.axis_size("op")
    _, rows, ncols = psi.shape
    terms, _, width, _ = right_ops.shape
    n_pair = n_op // 2
    cols = diag_right.shape[0] // n_op
    step = rows // n_op
    count = float(n_blk * rows * ncols)
    n_dev = n_blk * n_op
    bf16, f32, i32 = jnp.bfloat16, jnp.float32, jnp.int32
    last = sorted(range(1, n_blk), key=lambda d: min(d, n_blk - d))[-1]

    def pack():
        first = swap(term_shift, 1, n_op)
        sent = kernel(
            functools.partial(pack_body, n_blk, n_op),
            [(term_shift, SMEM), (first, SMEM), (psi, HBM), (right_ops, HBM)],
            [((rows, 2 * cols if d in (0, last) else cols), bf16, VMEM) for d in range(n_blk)]
            + [((terms * width + 16, 2 * cols), bf16, VMEM)] * n_pair,
            [pltpu.VMEM(right_ops.shape, bf16), pltpu.SemaphoreType.DMA((2 * n_blk + 1,))],
            nbytes=1 << 20,
        )
        return sent[:n_blk], sent[n_blk:]

    def table(right):
        return kernel(
            functools.partial(table_body, n_blk, terms),
            [(slot_sector, SMEM), (sector_width, SMEM), (diag_left, VMEM), (diag_right[None], VMEM)]
            + [(block, VMEM) for block in right],
            [((n_blk * n_pair * terms,), i32, SMEM)]
            + [((n_blk,), i32, SMEM)] * 2
            + [((n_blk, rows, LANES), f32, VMEM), ((1, n_op * cols), f32, VMEM)],
        )

    def inputs(left, psi, those):
        blocks = [left[d, 2 * e] for d in those for e in range(n_pair)]
        halves = [half for d in those for half in psi[d]]
        return [(x, VMEM) for x in blocks], [(x, VMEM) for x in halves], [len(psi[d]) for d in those]

    def early(left, psi, n_early, tables):
        left_ins, psi_ins, counts = inputs(left, psi, range(n_early))
        return kernel(
            functools.partial(early_body, n_pair, counts),
            [(tables[1], SMEM)] + left_ins + psi_ins,
            [
                ((n_blk, rows, 2 * cols), bf16, VMEM),
                ((n_blk + 1, n_pair * terms, rows, 2 * cols), bf16, VMEM),
                ((n_early, n_pair, terms, rows, rows), bf16, HBM),
            ],
            [pltpu.SemaphoreType.DMA((n_early * n_pair,))],
            flops=2 * n_early * rows * rows * 2 * cols * terms * n_pair,
            nbytes=4 << 20,
        )

    left, psi_by, right, (src, widths, slots, *both), (raw_early, inter_early, left_early) = gather(
        left_ops[:, 0], n_blk, n_op, pack, table, early
    )
    n_early = left_early.shape[0]
    n_late = n_blk - n_early
    left_ins, psi_ins, counts = inputs(left, psi_by, range(n_early, n_blk))
    right_ins = [(block, VMEM) for block in right]
    diags = [(x, VMEM) for x in both]

    tables = [(src, SMEM), (widths, SMEM)]
    narrow = ((n_blk, rows, 2 * cols), bf16, VMEM)
    dots = ((n_dev, 1, LANES), f32, VMEM)
    wide = ((n_blk, rows, 2 * cols), f32, VMEM)
    sends = [((2 - e % 2, n_blk, step, 2 * cols), bf16, VMEM) for e in range(1, n_op)]
    inter = pltpu.VMEM((n_blk + 1, n_pair * terms, rows, 2 * cols), bf16)
    left_late = (n_late, n_pair, terms, rows, rows)
    cost = dict(flops=2 * n_blk * rows * 2 * cols * terms * n_pair * (rows + 2 * cols), nbytes=6 << 20)

    def totals(parts):
        return lax.all_to_all(parts, ("blk", "op"), 0, 0, tiled=True)

    first_ins = tables + left_ins + right_ins + psi_ins + diags
    raw, _, part1, kept, dots1 = kernel(
        functools.partial(first_body, n_blk, n_pair, counts),
        first_ins + [(raw_early, VMEM), (inter_early, VMEM)],
        [narrow, (inter_early.shape, bf16, VMEM), narrow, (left_late, bf16, HBM), dots],
        [pltpu.SemaphoreType.DMA((n_late * n_pair,))],
        in_place={len(first_ins): 0, len(first_ins) + 1: 1},
        **cost,
    )
    parts1 = totals(dots1)
    sig, *out1 = kernel(
        sigma_body,
        [(x, VMEM) for x in (part1, swap(part1, 1, n_op), raw)] + diags,
        [wide] + sends[1::2],
        nbytes=4 << 20,
    )
    got1 = [swap(block, 2 * e, n_op) for e, block in enumerate(out1, 1)]
    dots2, own, *out2 = kernel(
        functools.partial(second_body, n_blk, n_pair, count),
        tables + [(left_early, HBM), (kept, HBM)] + right_ins
        + [(x, VMEM) for x in (parts1, raw, sig)] + diags,
        [dots, ((4, n_blk, step, 2 * cols), bf16, VMEM)] + sends,
        [
            inter,
            pltpu.VMEM((n_blk, rows, 2 * cols), f32),
            pltpu.VMEM((n_blk, rows, 2 * cols), bf16),
            pltpu.VMEM((n_blk, rows, 2 * cols), bf16),
            pltpu.VMEM((n_blk, *left_late[1:]), bf16),
            pltpu.SemaphoreType.DMA((n_blk,)),
        ],
        flops=4 * cost["flops"],
        nbytes=24 << 20,
    )
    near, got1 = lax.optimization_barrier((out2[0], got1))
    parts2 = totals(dots2)
    got2 = [swap(near, 1, n_op)] + [swap(block, e, n_op) for e, block in enumerate(out2[1:], 2)]
    final = ((n_blk, step, n_op * cols), bf16, VMEM)
    new, res, energy = kernel(
        functools.partial(third_body, n_blk, n_op, count),
        [(slots, SMEM)] + [(x, VMEM) for x in (parts1, parts2)] + diags
        + [(x, VMEM) for x in (own, *got1, *got2)],
        [final, final, ((1,), f32, SMEM)],
        nbytes=4 << 20,
    )
    return new, res, energy


def solution(mesh):
    placed = (
        P(("grp", "blk"), None, None),
        P("op", ("grp", "blk"), None, None),
        P("op", ("grp", "blk"), None, None),
        P("op"),
        P("grp"),
        P("grp"),
        P("grp", None),
        P(("grp", "blk")),
    )

    def body(*args):
        psi, left_ops, right_ops, diag_right = args[0], args[1], args[2], args[7]
        n_op = mesh.shape["op"]
        cols = diag_right.shape[0] // n_op
        fits = (
            psi.shape[0] == 1
            and diag_right.shape[0] % n_op == 0
            and cols == LANES
            and n_op % 2 == 0
            and cols % right_ops.shape[2] == 0
            and cols // right_ops.shape[2] * n_op == right_ops.shape[1]
            and psi.shape[1] % (16 * n_op) == 0
            and n_op & (n_op - 1) == 0
            and mesh.shape["blk"] > n_op.bit_length() - 1
        )
        return (per_device if fits else per_device_general)(*args)

    return jax.shard_map(
        body,
        mesh=mesh,
        in_specs=placed,
        out_specs=(P("grp", "op", "blk"), P("grp", "op", "blk"), P("grp")),
        check_vma=False,
    )
```

```python
import functools

import jax
import jax.numpy as jnp
from jax import lax
from jax.experimental import pallas as pl
from jax.experimental.pallas import tpu as pltpu
from jax.sharding import PartitionSpec as P

EPS = 1e-06
LANES = 128
VMEM_LIMIT = 20 * 1024 * 1024


def per_device_general(
    psi, left_ops, right_ops, term_shift, slot_sector, sector_width, diag_left, diag_right
):
    sec_dev, rows, ncols = psi.shape
    nsec = slot_sector.shape[0]
    terms_dev = left_ops.shape[0]
    right_local = right_ops.shape[1]
    right_width = right_ops.shape[2]
    local_cols = diag_right.shape[0]
    count = float(nsec * rows * ncols)
    match = slot_sector[:, None] == jnp.arange(nsec)[None, :]
    widths = jnp.sum(jnp.where(match, sector_width[None, :], 0), axis=1)
    mask_all = (jnp.arange(rows)[None, :] < widths[:, None]).astype(jnp.float32)
    own_mask = lax.dynamic_slice_in_dim(mask_all, lax.axis_index("blk") * sec_dev, sec_dev, 0)
    raw = psi.astype(jnp.float32) * own_mask[:, :, None]
    squares = lax.psum(jnp.sum(raw * raw), "blk")
    v_left = (raw * lax.rsqrt(squares / count + EPS)).astype(jnp.bfloat16)
    onehots = (
        slot_sector[None, None, :] == slot_sector[None, :, None] - term_shift[:, None, None]
    ).astype(jnp.bfloat16)
    op_rows = rows // lax.axis_size("op")
    op_start = lax.axis_index("op") * op_rows
    dmat = diag_left[:, :, None] + diag_right[None, None, :]

    def left_local(field):
        return jnp.einsum(
            "ksij,sjc->ksic", left_ops, field, preferred_element_type=jnp.float32
        ).astype(jnp.bfloat16)

    def right_part(moved_in):
        flat = moved_in.reshape(terms_dev, nsec, rows * local_cols)
        shifted = jnp.einsum(
            "kts,ksx->ktx", onehots, flat, preferred_element_type=jnp.float32
        ).astype(jnp.bfloat16)
        shifted = shifted.reshape(terms_dev, nsec, rows, right_local, right_width)
        accum = jnp.einsum(
            "ktwrc,krdc->twrd", shifted, right_ops, preferred_element_type=jnp.float32
        )
        return accum.reshape(nsec, rows, local_cols) * mask_all[:, :, None]

    def op_total(partial_value):
        return lax.psum(partial_value.astype(jnp.bfloat16), "op").astype(jnp.float32)

    def final_rows(array):
        return lax.dynamic_slice_in_dim(array, op_start, op_rows, 1)

    def reduce_dots(values):
        sums = lax.psum(values, "blk")
        return tuple((item / count for item in sums))

    moved_first, v_moved = (
        lax.all_to_all(left_local(v_left), "blk", split_axis=3, concat_axis=1, tiled=True),
        lax.all_to_all(v_left[None], "blk", split_axis=3, concat_axis=1, tiled=True),
    )
    v_right = v_moved[0]
    vec32 = v_right.astype(jnp.float32)
    first_sigma = op_total(right_part(moved_first)) + dmat * vec32
    theta = reduce_dots((jnp.sum(vec32 * first_sigma),))[0]
    resid = first_sigma - theta * vec32
    den = dmat - theta
    corr = resid * den / jnp.maximum(den * den, 0.25)
    along = reduce_dots((jnp.sum(vec32 * corr),))[0]
    orth = corr - along * vec32
    norm_sq = reduce_dots((jnp.sum(orth * orth),))[0]
    update = (orth * lax.rsqrt(norm_sq + EPS)).astype(jnp.bfloat16)
    upd32 = update.astype(jnp.float32)
    upd_left = lax.all_to_all(update, "blk", split_axis=0, concat_axis=2, tiled=True)
    moved_second = lax.all_to_all(
        left_local(upd_left), "blk", split_axis=3, concat_axis=1, tiled=True
    )
    second_sigma = op_total(right_part(moved_second)) + dmat * upd32
    v_s1, u_s0, u_s1 = reduce_dots(
        (jnp.sum(vec32 * second_sigma), jnp.sum(upd32 * first_sigma), jnp.sum(upd32 * second_sigma))
    )
    h_mix = 0.5 * (v_s1 + u_s0)
    coef_v, coef_u, energy = ritz(theta, h_mix, u_s1)
    newvec = coef_v * vec32 + coef_u * upd32
    image = coef_v * first_sigma + coef_u * second_sigma
    new_out = final_rows(newvec.astype(jnp.bfloat16))
    res_out = final_rows((image - energy * newvec).astype(jnp.bfloat16))
    return (new_out, res_out, jnp.reshape(energy, (1,)))


def ritz(theta, h_mix, h_two):
    angle = 0.5 * jnp.arctan2(2.0 * h_mix, theta - h_two)
    sine = jnp.sin(angle)
    flip = jnp.where(sine > 0, -1.0, 1.0)
    coef_v = -sine * flip
    coef_u = jnp.cos(angle) * flip
    half = 0.5 * (theta - h_two)
    energy = 0.5 * (theta + h_two) - jnp.sqrt(half * half + h_mix * h_mix)
    return coef_v, coef_u, energy


VMEM, SMEM, HBM = pltpu.VMEM, pltpu.SMEM, pltpu.HBM


def kernel(body, ins, outs, scratch=(), flops=0, nbytes=0):
    return pl.pallas_call(
        body,
        out_shape=[
            HBM(shape, dtype) if space == HBM else jax.ShapeDtypeStruct(shape, dtype)
            for shape, dtype, space in outs
        ],
        in_specs=[pl.BlockSpec(memory_space=space) for _, space in ins],
        out_specs=[pl.BlockSpec(memory_space=space) for _, _, space in outs],
        scratch_shapes=list(scratch),
        compiler_params=pltpu.CompilerParams(vmem_limit_bytes=VMEM_LIMIT),
        cost_estimate=pl.CostEstimate(flops=flops, bytes_accessed=nbytes, transcendentals=0),
    )(*[pltpu.with_memory_space_constraint(x, HBM) if space == HBM else x for x, space in ins])


def ring_at(place, n_blk):
    place = place % n_blk if isinstance(place, int) else lax.rem(place + n_blk, n_blk)
    even, odd = 2 * place, 2 * (n_blk - place) - 1
    if isinstance(place, int):
        return even if even < n_blk else odd
    return jnp.where(even < n_blk, even, odd)


def ring_place(index, n_blk):
    return jnp.where(lax.rem(index, 2) == 1, n_blk - (index + 1) // 2, index // 2)


def onward(block, d, n_blk):
    pairs = [(ring_at(i, n_blk), ring_at(i + d, n_blk)) for i in range(n_blk)]
    return lax.ppermute(block, "blk", pairs)


def swap(block, e, n_op):
    return lax.ppermute(block, "op", [(i, i ^ e) for i in range(n_op)])


def gather(own, n_blk, n_op, pack, table, early):
    bits = [1 << b for b in reversed(range(1, n_op.bit_length() - 1))]
    order = sorted(range(1, n_blk), key=lambda d: min(d, n_blk - d))
    left, psi, right, tables, columns = {(0, 0): own}, {}, None, None, None
    waiting, across, late, made = {(0, 0): 0}, {}, None, None
    for j in range(n_blk + len(bits)):
        new, moved = {}, {}
        for (d, e), done in waiting.items():
            if e == 0 and d + 1 < n_blk:
                new[d + 1, 0] = onward(left[d, 0], 1, n_blk), 0
            for b in range(done, len(bits)):
                new[d, e ^ bits[b]] = swap(left[d, e], bits[b], n_op), b + 1
        left.update({key: block for key, (block, _) in new.items()})
        kept = {key: block for key, (block, _) in new.items() if key[1] == 0}
        kept.update(across)
        across = {key: block for key, (block, _) in new.items() if key[1] != 0}
        if late is not None:
            moved["psi"] = late
        if j == 0:
            columns, packed = pack()
            right = [packed[0]]
            right += [swap(part, 2 * e, n_op) for e, part in enumerate(packed[1:], 1)]
            moved["columns"] = columns
        if j == 0:
            moved["right"] = right
        if j == 1:
            moved["tables"] = table(right)
        if j == n_blk - 1 and j >= len(bits) + 1:
            n_early = min(2, n_blk - 1)
            psi[0] = [columns[0]]
            moved["early"] = early(left, psi, n_early, tables)
        if 2 <= j < n_blk:
            moved["other"] = swap(psi[order[j - 2]][0], 1, n_op)
        late = onward(columns[order[j]], order[j], n_blk) if j < n_blk - 1 else None
        if not kept:
            break
        waiting = {key: done for key, (_, done) in new.items()}
        kept, moved = lax.optimization_barrier((kept, moved))
        left.update(kept)
        right, tables = moved.get("right", right), moved.get("tables", tables)
        columns = moved.get("columns", columns)
        made = moved.get("early", made)
        if "psi" in moved:
            psi[order[j - 1]] = [moved["psi"]]
        if "other" in moved:
            psi[order[j - 2]].append(moved["other"])
    return left, psi, right, tables, made


def place_of():
    return lax.axis_index("blk"), lax.axis_index("op")


def pack_body(n_blk, n_op, shift, _, psi, right_in, *outs):
    n_pair = n_op // 2
    psi_out, right_out, right, sems = outs[:n_blk], outs[n_blk : n_blk + n_pair], outs[-2], outs[-1]
    terms, local, width, _ = right.shape
    cols = local * width // n_op
    per = cols // width
    own_blk, own_op = place_of()
    fetch = pltpu.make_async_copy(right_in, right, sems.at[2 * n_blk])
    fetch.start()
    copies = []
    for d in range(n_blk):
        there = ring_at(ring_place(own_blk, n_blk) + d, n_blk) * n_op
        for h in range(psi_out[d].shape[1] // cols):
            start = pl.multiple_of((there + (own_op ^ h)) * cols, LANES)
            copy = pltpu.make_async_copy(
                psi.at[0, :, pl.ds(start, cols)],
                psi_out[d].at[:, h * cols : (h + 1) * cols],
                sems.at[2 * d + h],
            )
            copy.start()
            copies.append(copy)
    lane = lax.broadcasted_iota(jnp.int32, (16, 2 * cols), 1)
    line = jnp.zeros((16, 2 * cols), jnp.float32)
    for k in range(terms):
        line = jnp.where(lane == k, shift[k].astype(jnp.float32), line)
    square = [lax.broadcasted_iota(jnp.int32, (width, width), axis) for axis in (0, 1)]
    unit = (square[0] == square[1]).astype(jnp.bfloat16)
    fetch.wait()
    for e in range(n_pair):
        for k in range(terms):
            turned = []
            for h in range(2):
                first = (own_op ^ (2 * e) ^ h) * per
                for r in range(per):
                    turned.append(
                        lax.dot_general(
                            right[k, first + r], unit, (((0,), (0,)), ((), ())),
                            preferred_element_type=jnp.float32,
                        )
                    )
            side_by_side = jnp.concatenate(turned, axis=1).astype(jnp.bfloat16)
            right_out[e][k * width : (k + 1) * width] = side_by_side
        right_out[e][terms * width :] = line.astype(jnp.bfloat16)
    for copy in copies:
        copy.wait()


def table_body(n_blk, terms, sector, width, left_diag, right_diag, *refs):
    tails, src, widths, slots, diag, right_out = refs[:-5], *refs[-5:]
    right_out[...] = right_diag[...]
    n_pair = len(tails)
    rows, cols = tails[0].shape
    own_blk, _ = place_of()
    lane = lax.broadcasted_iota(jnp.int32, (16, cols), 1)
    for d in range(n_blk):
        slot = ring_at(ring_place(own_blk, n_blk) - d, n_blk)
        slots[d] = slot
        widths[d] = width[sector[slot]]
    for e in range(n_pair):
        tail = tails[e][rows - 16 :].astype(jnp.float32)
        for k in range(terms):
            shift = jnp.max(jnp.where(lane == k, tail, -1e9)).astype(jnp.int32)
            for t in range(n_blk):
                want = sector[slots[t]] - shift
                found = jnp.int32(n_blk)
                for d in range(n_blk):
                    found = jnp.where(sector[slots[d]] == want, d, found)
                src[(t * n_pair + e) * terms + k] = found
    for d in range(n_blk):
        row = left_diag[pl.ds(slots[d], 1), :]
        diag[d] = jnp.transpose(jnp.broadcast_to(row, (diag.shape[2], row.shape[1])))


def diagonal(diag, right_diag, d, h):
    cols = diag.shape[2]
    _, own_op = place_of()
    start = pl.multiple_of((own_op ^ h) * cols, LANES)
    return diag[d] + right_diag[:, pl.ds(start, cols)]


def row_mask(width, shape):
    return lax.broadcasted_iota(jnp.int32, shape, 0) < width


def fold(x):
    return jnp.sum(x.reshape(-1, 8, x.shape[-1]), axis=0)


def whole(x):
    return jnp.sum(jnp.sum(x, axis=0, keepdims=True), axis=1, keepdims=True)


def spread(values, out):
    lane = lax.broadcasted_iota(jnp.int32, out.shape[1:], 1)
    row = jnp.zeros(out.shape[1:], jnp.float32)
    for j, value in enumerate(values):
        row = jnp.where(lane == j, value, row)
    for d in range(out.shape[0]):
        out[d] = row


def by_block(packed, terms, k):
    rows, cols = packed.shape
    width = (rows - 16) // terms
    lane = lax.broadcasted_iota(jnp.int32, (width, cols), 1)
    block = packed[k * width : (k + 1) * width].astype(jnp.float32)
    parts = []
    for r in range(cols // width):
        inside = (lane >= r * width) & (lane < (r + 1) * width)
        parts.append(jnp.where(inside, block, 0.0).astype(jnp.bfloat16))
    return jnp.concatenate(parts, axis=0)


def left_products(block, left, inter):
    n_terms, rows, cols = inter.shape
    at = 0
    while at < n_terms:
        ops = left(at)
        terms = ops.shape[0]
        prod = jnp.dot(ops.reshape(terms * rows, rows), block, preferred_element_type=jnp.float32)
        inter[at : at + terms] = prod.astype(jnp.bfloat16).reshape(terms, rows, cols)
        at += terms


def sum_terms(src, widths, inter, right, out, emit):
    n_blk, n_terms, _, _ = inter.shape
    n_blk -= 1
    terms = n_terms // len(right)
    turned = [by_block(right[j // terms], terms, j % terms) for j in range(n_terms)]
    for t in range(n_blk):
        total = None
        for j in range(n_terms):
            part = jnp.dot(
                inter[src[t * n_terms + j], j], turned[j], preferred_element_type=jnp.float32
            )
            total = part if total is None else total + part
        total = jnp.where(row_mask(widths[t], total.shape), total, 0.0)
        out[t] = total.astype(jnp.bfloat16)
        emit(t, total)


def keep(left, left_out, sems):
    copies = []
    for d, line in enumerate(left):
        for e, ref in enumerate(line):
            copies.append(pltpu.make_async_copy(ref, left_out.at[d, e], sems.at[d * len(line) + e]))
            copies[-1].start()
    return copies


def masked(psi, width, out):
    at = 0
    for ref in psi:
        block = ref[...].astype(jnp.float32)
        block = jnp.where(row_mask(width, block.shape), block, 0.0)
        out[:, at : at + block.shape[1]] = block.astype(jnp.bfloat16)
        at += block.shape[1]


def take(refs, counts):
    out = []
    for count in counts:
        out.append(refs[:count])
        refs = refs[count:]
    return out, refs


def products_of(psi, left, widths, first, raw_out, inter):
    for d, line in enumerate(left):
        masked(psi[d], widths[first + d], raw_out.at[d])
        terms = line[0].shape[0]
        left_products(raw_out[d], lambda at: line[at // terms][...], inter.at[d])


def early_body(n_pair, counts, widths, *refs):
    left, refs = take(refs, [n_pair] * len(counts))
    psi, (raw_out, inter_out, left_out, sems) = take(refs, counts)
    copies = keep(left, left_out, sems)
    products_of(psi, left, widths, 0, raw_out, inter_out)
    for copy in copies:
        copy.wait()


def first_body(n_blk, n_pair, counts, src, widths, *refs):
    n_late = len(counts)
    n_early = n_blk - n_late
    left, refs = take(refs, [n_pair] * n_late)
    (right,), refs = take(refs, [n_pair])
    psi, refs = take(refs, counts)
    raw_in, inter_in, diag, right_diag, part_out, raw_out, left_out, dots_out, inter, sems = refs
    ready = []
    for j, (given, own) in enumerate(((inter_in, inter), (raw_in, raw_out))):
        ready.append(
            pltpu.make_async_copy(given, own.at[:n_early], sems.at[n_late * n_pair + j])
        )
        ready[-1].start()
    inter[n_blk] = jnp.zeros_like(inter[n_blk])
    products_of(
        psi, left, widths, n_early, raw_out.at[n_early:], inter.at[n_early:n_blk]
    )
    copies = keep(left, left_out, sems)
    for copy in ready:
        copy.wait()
    cols = diag.shape[2]
    zero = jnp.zeros((8, cols), jnp.float32)
    sums = [zero, zero]

    def emit(d, total):
        for h in range(2):
            part = slice(h * cols, (h + 1) * cols)
            raw = raw_out[d, :, part].astype(jnp.float32)
            image = total[:, part]
            if h == 0:
                image = image + diagonal(diag, right_diag, d, h) * raw
                sums[0] = sums[0] + fold(raw * raw)
            sums[1] = sums[1] + fold(raw * image)

    sum_terms(src, widths, inter, right, part_out, emit)
    spread([whole(x) for x in sums], dots_out)
    for copy in copies:
        copy.wait()


def send_rows(e, send, d, *refs):
    _, own_op = place_of()
    step = send.shape[2]
    rows = pl.ds(pl.multiple_of((own_op ^ e) * step, step), step)
    for j, ref in enumerate(refs):
        send[j, d] = ref[d, rows].astype(send.dtype)


def total_of(mine, other, d, h, cols):
    own = mine[d, :, h * cols : (h + 1) * cols].astype(jnp.float32)
    return own + other[d, :, (1 - h) * cols : (2 - h) * cols].astype(jnp.float32)


def sigma_body(mine, other, raw_in, diag, right_diag, sig_out, *sends):
    n_blk, _, cols = diag.shape
    for d in range(n_blk):
        for h in range(2):
            part = slice(h * cols, (h + 1) * cols)
            raw = raw_in[d, :, part].astype(jnp.float32)
            sigma = total_of(mine, other, d, h, cols) + diagonal(diag, right_diag, d, h) * raw
            sig_out[d, :, part] = sigma
        for e, send in enumerate(sends, 1):
            send_rows(2 * e, send, d, raw_in, sig_out)


def norm_theta(parts, count):
    tot = jnp.sum(parts, axis=0) * (1.0 / count)
    scale = lax.rsqrt(tot[:, 0:1] + EPS)
    return scale, tot[:, 1:2] * scale * scale


def second_body(n_blk, n_pair, count, src, widths, left_early, left_late, *refs):
    right, refs = refs[:n_pair], refs[n_pair:]
    parts, raw_in, sig, diag, right_diag, dots_out, own_out = refs[:7]
    sends, (inter, corr, fld, part_out, held, sems) = refs[7:-6], refs[-6:]
    copies = []
    n_early = left_early.shape[0]
    for d in range(n_blk):
        kept = left_early.at[d] if d < n_early else left_late.at[d - n_early]
        copies.append(pltpu.make_async_copy(kept, held.at[d], sems.at[d]))
        copies[-1].start()
    inter[n_blk] = jnp.zeros_like(inter[n_blk])
    scale, theta = norm_theta(parts[...], count)
    cols = diag.shape[2]
    halves = []
    for h in range(2):
        part = slice(h * cols, (h + 1) * cols)
        vv = vc = vs = jnp.zeros((8, cols), jnp.float32)
        for d in range(n_blk):
            vec = raw_in[d, :, part].astype(jnp.float32) * scale
            sigma = sig[d, :, part] * scale
            den = diagonal(diag, right_diag, d, h) - theta
            item = (sigma - theta * vec) * den / jnp.maximum(den * den, 0.25)
            corr[d, :, part] = item
            vv, vc = vv + fold(vec * vec), vc + fold(vec * item)
            if h == 0:
                vs = vs + fold(vec * sigma)
        halves.append((whole(vv), whole(vc), vs))
    along = (halves[0][1] + halves[1][1]) / jnp.maximum(halves[0][0] + halves[1][0], 1e-30)
    terms = held.shape[2]
    for copy in copies:
        copy.wait()
    for d in range(n_blk):
        for h in range(2):
            part = slice(h * cols, (h + 1) * cols)
            vec = raw_in[d, :, part].astype(jnp.float32) * scale
            fld[d, :, part] = (corr[d, :, part] - along * vec).astype(jnp.bfloat16)
        left_products(fld[d], lambda at: held[d, at // terms], inter.at[d])
    zero = jnp.zeros((8, cols), jnp.float32)
    sums = [zero for _ in range(5)]

    def emit(d, total):
        for h in range(2):
            part = slice(h * cols, (h + 1) * cols)
            field = fld[d, :, part].astype(jnp.float32)
            raw = raw_in[d, :, part].astype(jnp.float32)
            image = total[:, part]
            if h == 0:
                image = image + diagonal(diag, right_diag, d, h) * field
                for j, prod in enumerate((field * field, raw * field, field * sig[d, :, part])):
                    sums[j] = sums[j] + fold(prod)
            sums[3] = sums[3] + fold(raw * image)
            sums[4] = sums[4] + fold(field * image)
        for e, send in enumerate(sends, 1):
            send_rows(e, send, d, *((part_out,) if e % 2 else (fld, part_out)))
        rows = pl.ds(pl.multiple_of(own_op * step, step), step)
        for j, ref in enumerate((raw_in, sig, fld, part_out)):
            own_out[j, d] = ref[d, rows].astype(own_out.dtype)

    _, own_op = place_of()
    step = own_out.shape[2]
    sum_terms(src, widths, inter, right, part_out, emit)
    vv, vc, vs = halves[0]
    ff, vf, fs, vt, ft = (whole(x) for x in sums)
    spread([vv, vc, whole(vs), ff, vf * scale, fs * scale, vt * scale, ft], dots_out)


def ritz_pair(theta, h_mix, h_two):
    diff, twice = theta - h_two, 2.0 * h_mix
    size = jnp.sqrt(diff * diff + twice * twice)
    some = size > 0.0
    safe = jnp.where(some, size, 1.0)
    big = jnp.sqrt(0.5 + 0.5 * jnp.abs(diff) / safe)
    small = 0.5 * jnp.abs(twice) / (safe * big)
    sine = jnp.where(diff >= 0.0, small, big)
    cosine = jnp.where(diff >= 0.0, big, small)
    sine = jnp.where(some, sine, 0.0)
    cosine = jnp.where(some, cosine, 1.0)
    upward = (twice > 0.0) | ((twice == 0.0) & (diff < 0.0))
    return sine, jnp.where(upward, -cosine, cosine), 0.5 * (theta + h_two) - 0.5 * size


def third_body(n_blk, n_op, count, slots, parts1, parts2, diag, right_diag, own, *refs):
    n_far = n_op // 2 - 1
    got1, got2 = refs[:n_far], refs[n_far : n_far + n_op - 1]
    new_out, res_out, energy_out = refs[n_far + n_op - 1 :]
    step, cols = new_out.shape[1], new_out.shape[2] // n_op
    own_blk, own_op = place_of()
    scale, theta = norm_theta(parts1[...], count)
    pairs = parts2[...].reshape(n_blk * n_op // 2, 2, *parts2.shape[1:])
    pairs = pairs[:, 0] + pairs[:, 1]
    vv, vc, vs, ff, vf, fs, vt, ft = (pairs[:, 0, j : j + 1] for j in range(8))

    def mean(x):
        return jnp.sum(x, axis=0, keepdims=True) * (1.0 / count)

    def nearest(vv, vc):
        return vc / jnp.maximum(vv, 1e-30)

    along = mean(vc)
    beta = nearest(vv, vc) - along
    norm_sq = mean(ff + 2.0 * beta * vf + beta * beta * vv)
    unit = lax.rsqrt(jnp.maximum(norm_sq, 0.0) + EPS)
    v_s1 = unit * mean(vt + beta * vs)
    u_s0 = unit * mean(fs + beta * vs)
    u_s1 = unit * unit * mean(ft + beta * (vt + fs) + beta * beta * vs)
    cv, cu, energy = ritz_pair(theta, 0.5 * (v_s1 + u_s0), u_s1)
    energy_out[0] = jnp.max(energy)
    cu = cu * unit
    mine = pl.ds(pl.multiple_of(own_op * step, step), step)
    for e in range(0, n_op, 2):
        there = own_blk * n_op + (own_op ^ e)
        pair = parts2[there] + parts2[own_blk * n_op + (own_op ^ e ^ 1)]
        on_vec = cv + cu * (nearest(pair[:, 0:1], pair[:, 1:2]) - along)
        for h in range(2):
            at = pl.multiple_of((own_op ^ e ^ h) * cols, LANES)
            part, crossed = slice(h * cols, (h + 1) * cols), slice((1 - h) * cols, (2 - h) * cols)
            for d in range(n_blk):
                dmat = diag[d, mine] + right_diag[:, pl.ds(at, cols)]
                blocks = [own.at[j] for j in range(4)]
                if e:
                    far, near = got1[e // 2 - 1], got2[e - 1]
                    blocks = far.at[0], far.at[1], near.at[0], near.at[1]
                raw, sigma, fld, image = (x[d, :, part].astype(jnp.float32) for x in blocks)
                vec, sigma = raw * scale, sigma * scale
                image = image + got2[e][0, d, :, crossed].astype(jnp.float32) + dmat * fld
                newvec = on_vec * vec + cu * fld
                res = on_vec * sigma + cu * image - energy * newvec
                new_out[slots[d], :, pl.ds(at, cols)] = newvec.astype(jnp.bfloat16)
                res_out[slots[d], :, pl.ds(at, cols)] = res.astype(jnp.bfloat16)


def per_device(
    psi, left_ops, right_ops, term_shift, slot_sector, sector_width, diag_left, diag_right
):
    n_blk, n_op = lax.axis_size("blk"), lax.axis_size("op")
    _, rows, ncols = psi.shape
    terms, _, width, _ = right_ops.shape
    n_pair = n_op // 2
    cols = diag_right.shape[0] // n_op
    step = rows // n_op
    count = float(n_blk * rows * ncols)
    n_dev = n_blk * n_op
    bf16, f32, i32 = jnp.bfloat16, jnp.float32, jnp.int32
    last = sorted(range(1, n_blk), key=lambda d: min(d, n_blk - d))[-1]

    def pack():
        first = swap(term_shift, 1, n_op)
        sent = kernel(
            functools.partial(pack_body, n_blk, n_op),
            [(term_shift, SMEM), (first, SMEM), (psi, HBM), (right_ops, HBM)],
            [((rows, 2 * cols if d in (0, last) else cols), bf16, VMEM) for d in range(n_blk)]
            + [((terms * width + 16, 2 * cols), bf16, VMEM)] * n_pair,
            [pltpu.VMEM(right_ops.shape, bf16), pltpu.SemaphoreType.DMA((2 * n_blk + 1,))],
            nbytes=1 << 20,
        )
        return sent[:n_blk], sent[n_blk:]

    def table(right):
        return kernel(
            functools.partial(table_body, n_blk, terms),
            [(slot_sector, SMEM), (sector_width, SMEM), (diag_left, VMEM), (diag_right[None], VMEM)]
            + [(block, VMEM) for block in right],
            [((n_blk * n_pair * terms,), i32, SMEM)]
            + [((n_blk,), i32, SMEM)] * 2
            + [((n_blk, rows, LANES), f32, VMEM), ((1, n_op * cols), f32, VMEM)],
        )

    def inputs(left, psi, those):
        blocks = [left[d, 2 * e] for d in those for e in range(n_pair)]
        halves = [half for d in those for half in psi[d]]
        return [(x, VMEM) for x in blocks], [(x, VMEM) for x in halves], [len(psi[d]) for d in those]

    def early(left, psi, n_early, tables):
        left_ins, psi_ins, counts = inputs(left, psi, range(n_early))
        return kernel(
            functools.partial(early_body, n_pair, counts),
            [(tables[1], SMEM)] + left_ins + psi_ins,
            [
                ((n_early, rows, 2 * cols), bf16, VMEM),
                ((n_early, n_pair * terms, rows, 2 * cols), bf16, VMEM),
                ((n_early, n_pair, terms, rows, rows), bf16, HBM),
            ],
            [pltpu.SemaphoreType.DMA((n_early * n_pair,))],
            flops=2 * n_early * rows * rows * 2 * cols * terms * n_pair,
            nbytes=4 << 20,
        )

    left, psi_by, right, (src, widths, slots, *both), (raw_early, inter_early, left_early) = gather(
        left_ops[:, 0], n_blk, n_op, pack, table, early
    )
    n_early = raw_early.shape[0]
    n_late = n_blk - n_early
    left_ins, psi_ins, counts = inputs(left, psi_by, range(n_early, n_blk))
    right_ins = [(block, VMEM) for block in right]
    diags = [(x, VMEM) for x in both]

    tables = [(src, SMEM), (widths, SMEM)]
    narrow = ((n_blk, rows, 2 * cols), bf16, VMEM)
    dots = ((n_dev, 1, LANES), f32, VMEM)
    wide = ((n_blk, rows, 2 * cols), f32, VMEM)
    sends = [((2 - e % 2, n_blk, step, 2 * cols), bf16, VMEM) for e in range(1, n_op)]
    inter = pltpu.VMEM((n_blk + 1, n_pair * terms, rows, 2 * cols), bf16)
    left_late = (n_late, n_pair, terms, rows, rows)
    cost = dict(flops=2 * n_blk * rows * 2 * cols * terms * n_pair * (rows + 2 * cols), nbytes=6 << 20)

    def totals(parts):
        return lax.all_to_all(parts, ("blk", "op"), 0, 0, tiled=True)

    part1, raw, kept, dots1 = kernel(
        functools.partial(first_body, n_blk, n_pair, counts),
        tables + left_ins + right_ins + psi_ins + [(raw_early, VMEM), (inter_early, VMEM)] + diags,
        [narrow, narrow, (left_late, bf16, HBM), dots],
        [inter, pltpu.SemaphoreType.DMA((n_late * n_pair + 2,))],
        **cost,
    )
    parts1 = totals(dots1)
    sig, *out1 = kernel(
        sigma_body,
        [(x, VMEM) for x in (part1, swap(part1, 1, n_op), raw)] + diags,
        [wide] + sends[1::2],
        nbytes=4 << 20,
    )
    got1 = [swap(block, 2 * e, n_op) for e, block in enumerate(out1, 1)]
    dots2, own, *out2 = kernel(
        functools.partial(second_body, n_blk, n_pair, count),
        tables + [(left_early, HBM), (kept, HBM)] + right_ins
        + [(x, VMEM) for x in (parts1, raw, sig)] + diags,
        [dots, ((4, n_blk, step, 2 * cols), bf16, VMEM)] + sends,
        [
            inter,
            pltpu.VMEM((n_blk, rows, 2 * cols), f32),
            pltpu.VMEM((n_blk, rows, 2 * cols), bf16),
            pltpu.VMEM((n_blk, rows, 2 * cols), bf16),
            pltpu.VMEM((n_blk, *left_late[1:]), bf16),
            pltpu.SemaphoreType.DMA((n_blk,)),
        ],
        flops=4 * cost["flops"],
        nbytes=24 << 20,
    )
    near, got1 = lax.optimization_barrier((out2[0], got1))
    parts2 = totals(dots2)
    got2 = [swap(near, 1, n_op)] + [swap(block, e, n_op) for e, block in enumerate(out2[1:], 2)]
    final = ((n_blk, step, n_op * cols), bf16, VMEM)
    new, res, energy = kernel(
        functools.partial(third_body, n_blk, n_op, count),
        [(slots, SMEM)] + [(x, VMEM) for x in (parts1, parts2)] + diags
        + [(x, VMEM) for x in (own, *got1, *got2)],
        [final, final, ((1,), f32, SMEM)],
        nbytes=4 << 20,
    )
    return new, res, energy


def solution(mesh):
    placed = (
        P(("grp", "blk"), None, None),
        P("op", ("grp", "blk"), None, None),
        P("op", ("grp", "blk"), None, None),
        P("op"),
        P("grp"),
        P("grp"),
        P("grp", None),
        P(("grp", "blk")),
    )

    def body(*args):
        psi, left_ops, right_ops, diag_right = args[0], args[1], args[2], args[7]
        n_op = mesh.shape["op"]
        cols = diag_right.shape[0] // n_op
        fits = (
            psi.shape[0] == 1
            and diag_right.shape[0] % n_op == 0
            and cols == LANES
            and n_op % 2 == 0
            and cols % right_ops.shape[2] == 0
            and cols // right_ops.shape[2] * n_op == right_ops.shape[1]
            and psi.shape[1] % (16 * n_op) == 0
            and n_op & (n_op - 1) == 0
            and mesh.shape["blk"] > n_op.bit_length() - 1
        )
        return (per_device if fits else per_device_general)(*args)

    return jax.shard_map(
        body,
        mesh=mesh,
        in_specs=placed,
        out_specs=(P("grp", "op", "blk"), P("grp", "op", "blk"), P("grp")),
        check_vma=False,
    )
```

```python
import functools

import jax
import jax.numpy as jnp
from jax import lax
from jax.experimental import pallas as pl
from jax.experimental.pallas import tpu as pltpu
from jax.sharding import PartitionSpec as P

EPS = 1e-06
LANES = 128
VMEM_LIMIT = 20 * 1024 * 1024


def per_device_general(
    psi, left_ops, right_ops, term_shift, slot_sector, sector_width, diag_left, diag_right
):
    sec_dev, rows, ncols = psi.shape
    nsec = slot_sector.shape[0]
    terms_dev = left_ops.shape[0]
    right_local = right_ops.shape[1]
    right_width = right_ops.shape[2]
    local_cols = diag_right.shape[0]
    count = float(nsec * rows * ncols)
    match = slot_sector[:, None] == jnp.arange(nsec)[None, :]
    widths = jnp.sum(jnp.where(match, sector_width[None, :], 0), axis=1)
    mask_all = (jnp.arange(rows)[None, :] < widths[:, None]).astype(jnp.float32)
    own_mask = lax.dynamic_slice_in_dim(mask_all, lax.axis_index("blk") * sec_dev, sec_dev, 0)
    raw = psi.astype(jnp.float32) * own_mask[:, :, None]
    squares = lax.psum(jnp.sum(raw * raw), "blk")
    v_left = (raw * lax.rsqrt(squares / count + EPS)).astype(jnp.bfloat16)
    onehots = (
        slot_sector[None, None, :] == slot_sector[None, :, None] - term_shift[:, None, None]
    ).astype(jnp.bfloat16)
    op_rows = rows // lax.axis_size("op")
    op_start = lax.axis_index("op") * op_rows
    dmat = diag_left[:, :, None] + diag_right[None, None, :]

    def left_local(field):
        return jnp.einsum(
            "ksij,sjc->ksic", left_ops, field, preferred_element_type=jnp.float32
        ).astype(jnp.bfloat16)

    def right_part(moved_in):
        flat = moved_in.reshape(terms_dev, nsec, rows * local_cols)
        shifted = jnp.einsum(
            "kts,ksx->ktx", onehots, flat, preferred_element_type=jnp.float32
        ).astype(jnp.bfloat16)
        shifted = shifted.reshape(terms_dev, nsec, rows, right_local, right_width)
        accum = jnp.einsum(
            "ktwrc,krdc->twrd", shifted, right_ops, preferred_element_type=jnp.float32
        )
        return accum.reshape(nsec, rows, local_cols) * mask_all[:, :, None]

    def op_total(partial_value):
        return lax.psum(partial_value.astype(jnp.bfloat16), "op").astype(jnp.float32)

    def final_rows(array):
        return lax.dynamic_slice_in_dim(array, op_start, op_rows, 1)

    def reduce_dots(values):
        sums = lax.psum(values, "blk")
        return tuple((item / count for item in sums))

    moved_first, v_moved = (
        lax.all_to_all(left_local(v_left), "blk", split_axis=3, concat_axis=1, tiled=True),
        lax.all_to_all(v_left[None], "blk", split_axis=3, concat_axis=1, tiled=True),
    )
    v_right = v_moved[0]
    vec32 = v_right.astype(jnp.float32)
    first_sigma = op_total(right_part(moved_first)) + dmat * vec32
    theta = reduce_dots((jnp.sum(vec32 * first_sigma),))[0]
    resid = first_sigma - theta * vec32
    den = dmat - theta
    corr = resid * den / jnp.maximum(den * den, 0.25)
    along = reduce_dots((jnp.sum(vec32 * corr),))[0]
    orth = corr - along * vec32
    norm_sq = reduce_dots((jnp.sum(orth * orth),))[0]
    update = (orth * lax.rsqrt(norm_sq + EPS)).astype(jnp.bfloat16)
    upd32 = update.astype(jnp.float32)
    upd_left = lax.all_to_all(update, "blk", split_axis=0, concat_axis=2, tiled=True)
    moved_second = lax.all_to_all(
        left_local(upd_left), "blk", split_axis=3, concat_axis=1, tiled=True
    )
    second_sigma = op_total(right_part(moved_second)) + dmat * upd32
    v_s1, u_s0, u_s1 = reduce_dots(
        (jnp.sum(vec32 * second_sigma), jnp.sum(upd32 * first_sigma), jnp.sum(upd32 * second_sigma))
    )
    h_mix = 0.5 * (v_s1 + u_s0)
    coef_v, coef_u, energy = ritz(theta, h_mix, u_s1)
    newvec = coef_v * vec32 + coef_u * upd32
    image = coef_v * first_sigma + coef_u * second_sigma
    new_out = final_rows(newvec.astype(jnp.bfloat16))
    res_out = final_rows((image - energy * newvec).astype(jnp.bfloat16))
    return (new_out, res_out, jnp.reshape(energy, (1,)))


def ritz(theta, h_mix, h_two):
    angle = 0.5 * jnp.arctan2(2.0 * h_mix, theta - h_two)
    sine = jnp.sin(angle)
    flip = jnp.where(sine > 0, -1.0, 1.0)
    coef_v = -sine * flip
    coef_u = jnp.cos(angle) * flip
    half = 0.5 * (theta - h_two)
    energy = 0.5 * (theta + h_two) - jnp.sqrt(half * half + h_mix * h_mix)
    return coef_v, coef_u, energy


VMEM, SMEM, HBM = pltpu.VMEM, pltpu.SMEM, pltpu.HBM


def kernel(body, ins, outs, scratch=(), flops=0, nbytes=0):
    return pl.pallas_call(
        body,
        out_shape=[
            HBM(shape, dtype) if space == HBM else jax.ShapeDtypeStruct(shape, dtype)
            for shape, dtype, space in outs
        ],
        in_specs=[pl.BlockSpec(memory_space=space) for _, space in ins],
        out_specs=[pl.BlockSpec(memory_space=space) for _, _, space in outs],
        scratch_shapes=list(scratch),
        compiler_params=pltpu.CompilerParams(vmem_limit_bytes=VMEM_LIMIT),
        cost_estimate=pl.CostEstimate(flops=flops, bytes_accessed=nbytes, transcendentals=0),
    )(*[pltpu.with_memory_space_constraint(x, HBM) if space == HBM else x for x, space in ins])


def ring_at(place, n_blk):
    place = place % n_blk if isinstance(place, int) else lax.rem(place + n_blk, n_blk)
    even, odd = 2 * place, 2 * (n_blk - place) - 1
    if isinstance(place, int):
        return even if even < n_blk else odd
    return jnp.where(even < n_blk, even, odd)


def ring_place(index, n_blk):
    return jnp.where(lax.rem(index, 2) == 1, n_blk - (index + 1) // 2, index // 2)


def onward(block, d, n_blk):
    pairs = [(ring_at(i, n_blk), ring_at(i + d, n_blk)) for i in range(n_blk)]
    return lax.ppermute(block, "blk", pairs)


def swap(block, e, n_op):
    return lax.ppermute(block, "op", [(i, i ^ e) for i in range(n_op)])


def gather(own, n_blk, n_op, pack, table, early):
    bits = [1 << b for b in reversed(range(1, n_op.bit_length() - 1))]
    order = sorted(range(1, n_blk), key=lambda d: min(d, n_blk - d))
    left, psi, right, tables, columns = {(0, 0): own}, {}, None, None, None
    waiting, across, made = {(0, 0): 0}, {}, None
    for j in range(n_blk + len(bits)):
        new, moved = {}, {}
        for (d, e), done in waiting.items():
            if e == 0 and d + 1 < n_blk:
                new[d + 1, 0] = onward(left[d, 0], 1, n_blk), 0
            for b in range(done, len(bits)):
                new[d, e ^ bits[b]] = swap(left[d, e], bits[b], n_op), b + 1
        left.update({key: block for key, (block, _) in new.items()})
        kept = {key: block for key, (block, _) in new.items() if key[1] == 0}
        kept.update(across)
        across = {key: block for key, (block, _) in new.items() if key[1] != 0}
        due = order[:2] if j == 1 else order[2:] if j == n_blk - 1 else []
        moved["psi"] = {d: onward(columns[d], d, n_blk) for d in due}
        if j == 0:
            columns, packed = pack()
            right = [packed[0]]
            right += [swap(part, 2 * e, n_op) for e, part in enumerate(packed[1:], 1)]
            moved["columns"] = columns
        if j == 0:
            moved["right"] = right
        if j == 1:
            moved["tables"] = table(right)
        if j == n_blk - 1 and j >= len(bits) + 1:
            n_early = min(2, n_blk - 1)
            psi[0] = [columns[0]]
            moved["early"] = early(left, psi, n_early, tables)
        if j == 2:
            moved["other"] = {d: swap(psi[d][0], 1, n_op) for d in order[:2]}
        if not kept:
            break
        waiting = {key: done for key, (_, done) in new.items()}
        kept, moved = lax.optimization_barrier((kept, moved))
        left.update(kept)
        right, tables = moved.get("right", right), moved.get("tables", tables)
        columns = moved.get("columns", columns)
        made = moved.get("early", made)
        psi.update({d: [block] for d, block in moved["psi"].items()})
        for d, block in moved.get("other", {}).items():
            psi[d].append(block)
    return left, psi, right, tables, made


def place_of():
    return lax.axis_index("blk"), lax.axis_index("op")


def pack_body(n_blk, n_op, shift, _, psi, right_in, *outs):
    n_pair = n_op // 2
    psi_out, right_out, right, sems = outs[:n_blk], outs[n_blk : n_blk + n_pair], outs[-2], outs[-1]
    terms, local, width, _ = right.shape
    cols = local * width // n_op
    per = cols // width
    own_blk, own_op = place_of()
    fetch = pltpu.make_async_copy(right_in, right, sems.at[2 * n_blk])
    fetch.start()
    copies = []
    for d in range(n_blk):
        there = ring_at(ring_place(own_blk, n_blk) + d, n_blk) * n_op
        for h in range(psi_out[d].shape[1] // cols):
            start = pl.multiple_of((there + (own_op ^ h)) * cols, LANES)
            copy = pltpu.make_async_copy(
                psi.at[0, :, pl.ds(start, cols)],
                psi_out[d].at[:, h * cols : (h + 1) * cols],
                sems.at[2 * d + h],
            )
            copy.start()
            copies.append(copy)
    lane = lax.broadcasted_iota(jnp.int32, (16, 2 * cols), 1)
    line = jnp.zeros((16, 2 * cols), jnp.float32)
    for k in range(terms):
        line = jnp.where(lane == k, shift[k].astype(jnp.float32), line)
    square = [lax.broadcasted_iota(jnp.int32, (width, width), axis) for axis in (0, 1)]
    unit = (square[0] == square[1]).astype(jnp.bfloat16)
    fetch.wait()
    for e in range(n_pair):
        for k in range(terms):
            turned = []
            for h in range(2):
                first = (own_op ^ (2 * e) ^ h) * per
                for r in range(per):
                    turned.append(
                        lax.dot_general(
                            right[k, first + r], unit, (((0,), (0,)), ((), ())),
                            preferred_element_type=jnp.float32,
                        )
                    )
            side_by_side = jnp.concatenate(turned, axis=1).astype(jnp.bfloat16)
            right_out[e][k * width : (k + 1) * width] = side_by_side
        right_out[e][terms * width :] = line.astype(jnp.bfloat16)
    for copy in copies:
        copy.wait()


def table_body(n_blk, terms, sector, width, left_diag, right_diag, *refs):
    tails, src, widths, slots, diag, right_out = refs[:-5], *refs[-5:]
    right_out[...] = right_diag[...]
    n_pair = len(tails)
    rows, cols = tails[0].shape
    own_blk, _ = place_of()
    lane = lax.broadcasted_iota(jnp.int32, (16, cols), 1)
    for d in range(n_blk):
        slot = ring_at(ring_place(own_blk, n_blk) - d, n_blk)
        slots[d] = slot
        widths[d] = width[sector[slot]]
    for e in range(n_pair):
        tail = tails[e][rows - 16 :].astype(jnp.float32)
        for k in range(terms):
            shift = jnp.max(jnp.where(lane == k, tail, -1e9)).astype(jnp.int32)
            for t in range(n_blk):
                want = sector[slots[t]] - shift
                found = jnp.int32(n_blk)
                for d in range(n_blk):
                    found = jnp.where(sector[slots[d]] == want, d, found)
                src[(t * n_pair + e) * terms + k] = found
    for d in range(n_blk):
        row = left_diag[pl.ds(slots[d], 1), :]
        diag[d] = jnp.transpose(jnp.broadcast_to(row, (diag.shape[2], row.shape[1])))


def diagonal(diag, right_diag, d, h):
    cols = diag.shape[2]
    _, own_op = place_of()
    start = pl.multiple_of((own_op ^ h) * cols, LANES)
    return diag[d] + right_diag[:, pl.ds(start, cols)]


def row_mask(width, shape):
    return lax.broadcasted_iota(jnp.int32, shape, 0) < width


def fold(x):
    return jnp.sum(x.reshape(-1, 8, x.shape[-1]), axis=0)


def whole(x):
    return jnp.sum(jnp.sum(x, axis=0, keepdims=True), axis=1, keepdims=True)


def spread(values, out):
    lane = lax.broadcasted_iota(jnp.int32, out.shape[1:], 1)
    row = jnp.zeros(out.shape[1:], jnp.float32)
    for j, value in enumerate(values):
        row = jnp.where(lane == j, value, row)
    for d in range(out.shape[0]):
        out[d] = row


def by_block(packed, terms, k):
    rows, cols = packed.shape
    width = (rows - 16) // terms
    lane = lax.broadcasted_iota(jnp.int32, (width, cols), 1)
    block = packed[k * width : (k + 1) * width].astype(jnp.float32)
    parts = []
    for r in range(cols // width):
        inside = (lane >= r * width) & (lane < (r + 1) * width)
        parts.append(jnp.where(inside, block, 0.0).astype(jnp.bfloat16))
    return jnp.concatenate(parts, axis=0)


def left_products(block, left, inter):
    n_terms, rows, cols = inter.shape
    at = 0
    while at < n_terms:
        ops = left(at)
        terms = ops.shape[0]
        prod = jnp.dot(ops.reshape(terms * rows, rows), block, preferred_element_type=jnp.float32)
        inter[at : at + terms] = prod.astype(jnp.bfloat16).reshape(terms, rows, cols)
        at += terms


def sum_terms(src, widths, inter, right, out, emit):
    n_blk, n_terms, _, _ = inter.shape
    n_blk -= 1
    terms = n_terms // len(right)
    turned = [by_block(right[j // terms], terms, j % terms) for j in range(n_terms)]
    for t in range(n_blk):
        total = None
        for j in range(n_terms):
            part = jnp.dot(
                inter[src[t * n_terms + j], j], turned[j], preferred_element_type=jnp.float32
            )
            total = part if total is None else total + part
        total = jnp.where(row_mask(widths[t], total.shape), total, 0.0)
        out[t] = total.astype(jnp.bfloat16)
        emit(t, total)


def keep(left, left_out, sems):
    copies = []
    for d, line in enumerate(left):
        for e, ref in enumerate(line):
            copies.append(pltpu.make_async_copy(ref, left_out.at[d, e], sems.at[d * len(line) + e]))
            copies[-1].start()
    return copies


def masked(psi, width, out):
    at = 0
    for ref in psi:
        block = ref[...].astype(jnp.float32)
        block = jnp.where(row_mask(width, block.shape), block, 0.0)
        out[:, at : at + block.shape[1]] = block.astype(jnp.bfloat16)
        at += block.shape[1]


def take(refs, counts):
    out = []
    for count in counts:
        out.append(refs[:count])
        refs = refs[count:]
    return out, refs


def products_of(psi, left, widths, first, raw_out, inter):
    for d, line in enumerate(left):
        masked(psi[d], widths[first + d], raw_out.at[d])
        terms = line[0].shape[0]
        left_products(raw_out[d], lambda at: line[at // terms][...], inter.at[d])


def early_body(n_pair, counts, widths, *refs):
    left, refs = take(refs, [n_pair] * len(counts))
    psi, (raw_out, inter_out, left_out, sems) = take(refs, counts)
    copies = keep(left, left_out, sems)
    products_of(psi, left, widths, 0, raw_out, inter_out)
    for copy in copies:
        copy.wait()


def first_body(n_blk, n_pair, counts, src, widths, *refs):
    n_late = len(counts)
    n_early = n_blk - n_late
    left, refs = take(refs, [n_pair] * n_late)
    (right,), refs = take(refs, [n_pair])
    psi, refs = take(refs, counts)
    raw_in, inter_in, diag, right_diag, part_out, raw_out, left_out, dots_out, inter, sems = refs
    ready = []
    for j, (given, own) in enumerate(((inter_in, inter), (raw_in, raw_out))):
        ready.append(
            pltpu.make_async_copy(given, own.at[:n_early], sems.at[n_late * n_pair + j])
        )
        ready[-1].start()
    copies = keep(left, left_out, sems)
    inter[n_blk] = jnp.zeros_like(inter[n_blk])
    products_of(
        psi, left, widths, n_early, raw_out.at[n_early:], inter.at[n_early:n_blk]
    )
    for copy in ready:
        copy.wait()
    cols = diag.shape[2]
    zero = jnp.zeros((8, cols), jnp.float32)
    sums = [zero, zero]

    def emit(d, total):
        for h in range(2):
            part = slice(h * cols, (h + 1) * cols)
            raw = raw_out[d, :, part].astype(jnp.float32)
            image = total[:, part]
            if h == 0:
                image = image + diagonal(diag, right_diag, d, h) * raw
                sums[0] = sums[0] + fold(raw * raw)
            sums[1] = sums[1] + fold(raw * image)

    sum_terms(src, widths, inter, right, part_out, emit)
    spread([whole(x) for x in sums], dots_out)
    for copy in copies:
        copy.wait()


def send_rows(e, send, d, *refs):
    _, own_op = place_of()
    step = send.shape[2]
    rows = pl.ds(pl.multiple_of((own_op ^ e) * step, step), step)
    for j, ref in enumerate(refs):
        send[j, d] = ref[d, rows].astype(send.dtype)


def total_of(mine, other, d, h, cols):
    own = mine[d, :, h * cols : (h + 1) * cols].astype(jnp.float32)
    return own + other[d, :, (1 - h) * cols : (2 - h) * cols].astype(jnp.float32)


def sigma_body(mine, other, raw_in, diag, right_diag, sig_out, *sends):
    n_blk, _, cols = diag.shape
    for d in range(n_blk):
        for h in range(2):
            part = slice(h * cols, (h + 1) * cols)
            raw = raw_in[d, :, part].astype(jnp.float32)
            sigma = total_of(mine, other, d, h, cols) + diagonal(diag, right_diag, d, h) * raw
            sig_out[d, :, part] = sigma
        for e, send in enumerate(sends, 1):
            send_rows(2 * e, send, d, raw_in, sig_out)


def norm_theta(parts, count):
    tot = jnp.sum(parts, axis=0) * (1.0 / count)
    scale = lax.rsqrt(tot[:, 0:1] + EPS)
    return scale, tot[:, 1:2] * scale * scale


def second_body(n_blk, n_pair, count, src, widths, left_early, left_late, *refs):
    right, refs = refs[:n_pair], refs[n_pair:]
    parts, raw_in, sig, diag, right_diag, dots_out, own_out = refs[:7]
    sends, (inter, corr, fld, part_out, held, sems) = refs[7:-6], refs[-6:]
    copies = []
    n_early = left_early.shape[0]
    for d in range(n_blk):
        kept = left_early.at[d] if d < n_early else left_late.at[d - n_early]
        copies.append(pltpu.make_async_copy(kept, held.at[d], sems.at[d]))
        copies[-1].start()
    inter[n_blk] = jnp.zeros_like(inter[n_blk])
    scale, theta = norm_theta(parts[...], count)
    cols = diag.shape[2]
    halves = []
    for h in range(2):
        part = slice(h * cols, (h + 1) * cols)
        vv = vc = vs = jnp.zeros((8, cols), jnp.float32)
        for d in range(n_blk):
            vec = raw_in[d, :, part].astype(jnp.float32) * scale
            sigma = sig[d, :, part] * scale
            den = diagonal(diag, right_diag, d, h) - theta
            item = (sigma - theta * vec) * den / jnp.maximum(den * den, 0.25)
            corr[d, :, part] = item
            vv, vc = vv + fold(vec * vec), vc + fold(vec * item)
            if h == 0:
                vs = vs + fold(vec * sigma)
        halves.append((whole(vv), whole(vc), vs))
    along = (halves[0][1] + halves[1][1]) / jnp.maximum(halves[0][0] + halves[1][0], 1e-30)
    terms = held.shape[2]
    for copy in copies:
        copy.wait()
    for d in range(n_blk):
        for h in range(2):
            part = slice(h * cols, (h + 1) * cols)
            vec = raw_in[d, :, part].astype(jnp.float32) * scale
            fld[d, :, part] = (corr[d, :, part] - along * vec).astype(jnp.bfloat16)
        left_products(fld[d], lambda at: held[d, at // terms], inter.at[d])
    zero = jnp.zeros((8, cols), jnp.float32)
    sums = [zero for _ in range(5)]

    def emit(d, total):
        for h in range(2):
            part = slice(h * cols, (h + 1) * cols)
            field = fld[d, :, part].astype(jnp.float32)
            raw = raw_in[d, :, part].astype(jnp.float32)
            image = total[:, part]
            if h == 0:
                image = image + diagonal(diag, right_diag, d, h) * field
                for j, prod in enumerate((field * field, raw * field, field * sig[d, :, part])):
                    sums[j] = sums[j] + fold(prod)
            sums[3] = sums[3] + fold(raw * image)
            sums[4] = sums[4] + fold(field * image)
        for e, send in enumerate(sends, 1):
            send_rows(e, send, d, *((part_out,) if e % 2 else (fld, part_out)))
        rows = pl.ds(pl.multiple_of(own_op * step, step), step)
        for j, ref in enumerate((raw_in, sig, fld, part_out)):
            own_out[j, d] = ref[d, rows].astype(own_out.dtype)

    _, own_op = place_of()
    step = own_out.shape[2]
    sum_terms(src, widths, inter, right, part_out, emit)
    vv, vc, vs = halves[0]
    ff, vf, fs, vt, ft = (whole(x) for x in sums)
    spread([vv, vc, whole(vs), ff, vf * scale, fs * scale, vt * scale, ft], dots_out)


def ritz_pair(theta, h_mix, h_two):
    diff, twice = theta - h_two, 2.0 * h_mix
    size = jnp.sqrt(diff * diff + twice * twice)
    some = size > 0.0
    safe = jnp.where(some, size, 1.0)
    big = jnp.sqrt(0.5 + 0.5 * jnp.abs(diff) / safe)
    small = 0.5 * jnp.abs(twice) / (safe * big)
    sine = jnp.where(diff >= 0.0, small, big)
    cosine = jnp.where(diff >= 0.0, big, small)
    sine = jnp.where(some, sine, 0.0)
    cosine = jnp.where(some, cosine, 1.0)
    upward = (twice > 0.0) | ((twice == 0.0) & (diff < 0.0))
    return sine, jnp.where(upward, -cosine, cosine), 0.5 * (theta + h_two) - 0.5 * size


def third_body(n_blk, n_op, count, slots, parts1, parts2, diag, right_diag, own, *refs):
    n_far = n_op // 2 - 1
    got1, got2 = refs[:n_far], refs[n_far : n_far + n_op - 1]
    new_out, res_out, energy_out = refs[n_far + n_op - 1 :]
    step, cols = new_out.shape[1], new_out.shape[2] // n_op
    own_blk, own_op = place_of()
    scale, theta = norm_theta(parts1[...], count)
    pairs = parts2[...].reshape(n_blk * n_op // 2, 2, *parts2.shape[1:])
    pairs = pairs[:, 0] + pairs[:, 1]
    vv, vc, vs, ff, vf, fs, vt, ft = (pairs[:, 0, j : j + 1] for j in range(8))

    def mean(x):
        return jnp.sum(x, axis=0, keepdims=True) * (1.0 / count)

    def nearest(vv, vc):
        return vc / jnp.maximum(vv, 1e-30)

    along = mean(vc)
    beta = nearest(vv, vc) - along
    norm_sq = mean(ff + 2.0 * beta * vf + beta * beta * vv)
    unit = lax.rsqrt(jnp.maximum(norm_sq, 0.0) + EPS)
    v_s1 = unit * mean(vt + beta * vs)
    u_s0 = unit * mean(fs + beta * vs)
    u_s1 = unit * unit * mean(ft + beta * (vt + fs) + beta * beta * vs)
    cv, cu, energy = ritz_pair(theta, 0.5 * (v_s1 + u_s0), u_s1)
    energy_out[0] = jnp.max(energy)
    cu = cu * unit
    mine = pl.ds(pl.multiple_of(own_op * step, step), step)
    for e in range(0, n_op, 2):
        there = own_blk * n_op + (own_op ^ e)
        pair = parts2[there] + parts2[own_blk * n_op + (own_op ^ e ^ 1)]
        on_vec = cv + cu * (nearest(pair[:, 0:1], pair[:, 1:2]) - along)
        for h in range(2):
            at = pl.multiple_of((own_op ^ e ^ h) * cols, LANES)
            part, crossed = slice(h * cols, (h + 1) * cols), slice((1 - h) * cols, (2 - h) * cols)
            for d in range(n_blk):
                dmat = diag[d, mine] + right_diag[:, pl.ds(at, cols)]
                blocks = [own.at[j] for j in range(4)]
                if e:
                    far, near = got1[e // 2 - 1], got2[e - 1]
                    blocks = far.at[0], far.at[1], near.at[0], near.at[1]
                raw, sigma, fld, image = (x[d, :, part].astype(jnp.float32) for x in blocks)
                vec, sigma = raw * scale, sigma * scale
                image = image + got2[e][0, d, :, crossed].astype(jnp.float32) + dmat * fld
                newvec = on_vec * vec + cu * fld
                res = on_vec * sigma + cu * image - energy * newvec
                new_out[slots[d], :, pl.ds(at, cols)] = newvec.astype(jnp.bfloat16)
                res_out[slots[d], :, pl.ds(at, cols)] = res.astype(jnp.bfloat16)


def per_device(
    psi, left_ops, right_ops, term_shift, slot_sector, sector_width, diag_left, diag_right
):
    n_blk, n_op = lax.axis_size("blk"), lax.axis_size("op")
    _, rows, ncols = psi.shape
    terms, _, width, _ = right_ops.shape
    n_pair = n_op // 2
    cols = diag_right.shape[0] // n_op
    step = rows // n_op
    count = float(n_blk * rows * ncols)
    n_dev = n_blk * n_op
    bf16, f32, i32 = jnp.bfloat16, jnp.float32, jnp.int32
    far = sorted(range(1, n_blk), key=lambda d: min(d, n_blk - d))[2:]

    def pack():
        first = swap(term_shift, 1, n_op)
        sent = kernel(
            functools.partial(pack_body, n_blk, n_op),
            [(term_shift, SMEM), (first, SMEM), (psi, HBM), (right_ops, HBM)],
            [((rows, 2 * cols if d in (0, *far) else cols), bf16, VMEM) for d in range(n_blk)]
            + [((terms * width + 16, 2 * cols), bf16, VMEM)] * n_pair,
            [pltpu.VMEM(right_ops.shape, bf16), pltpu.SemaphoreType.DMA((2 * n_blk + 1,))],
            nbytes=1 << 20,
        )
        return sent[:n_blk], sent[n_blk:]

    def table(right):
        return kernel(
            functools.partial(table_body, n_blk, terms),
            [(slot_sector, SMEM), (sector_width, SMEM), (diag_left, VMEM), (diag_right[None], VMEM)]
            + [(block, VMEM) for block in right],
            [((n_blk * n_pair * terms,), i32, SMEM)]
            + [((n_blk,), i32, SMEM)] * 2
            + [((n_blk, rows, LANES), f32, VMEM), ((1, n_op * cols), f32, VMEM)],
        )

    def inputs(left, psi, those):
        blocks = [left[d, 2 * e] for d in those for e in range(n_pair)]
        halves = [half for d in those for half in psi[d]]
        return [(x, VMEM) for x in blocks], [(x, VMEM) for x in halves], [len(psi[d]) for d in those]

    def early(left, psi, n_early, tables):
        left_ins, psi_ins, counts = inputs(left, psi, range(n_early))
        return kernel(
            functools.partial(early_body, n_pair, counts),
            [(tables[1], SMEM)] + left_ins + psi_ins,
            [
                ((n_early, rows, 2 * cols), bf16, VMEM),
                ((n_early, n_pair * terms, rows, 2 * cols), bf16, VMEM),
                ((n_early, n_pair, terms, rows, rows), bf16, HBM),
            ],
            [pltpu.SemaphoreType.DMA((n_early * n_pair,))],
            flops=2 * n_early * rows * rows * 2 * cols * terms * n_pair,
            nbytes=4 << 20,
        )

    left, psi_by, right, (src, widths, slots, *both), (raw_early, inter_early, left_early) = gather(
        left_ops[:, 0], n_blk, n_op, pack, table, early
    )
    n_early = raw_early.shape[0]
    n_late = n_blk - n_early
    left_ins, psi_ins, counts = inputs(left, psi_by, range(n_early, n_blk))
    right_ins = [(block, VMEM) for block in right]
    diags = [(x, VMEM) for x in both]

    tables = [(src, SMEM), (widths, SMEM)]
    narrow = ((n_blk, rows, 2 * cols), bf16, VMEM)
    dots = ((n_dev, 1, LANES), f32, VMEM)
    wide = ((n_blk, rows, 2 * cols), f32, VMEM)
    sends = [((2 - e % 2, n_blk, step, 2 * cols), bf16, VMEM) for e in range(1, n_op)]
    inter = pltpu.VMEM((n_blk + 1, n_pair * terms, rows, 2 * cols), bf16)
    left_late = (n_late, n_pair, terms, rows, rows)
    cost = dict(flops=2 * n_blk * rows * 2 * cols * terms * n_pair * (rows + 2 * cols), nbytes=6 << 20)

    def totals(parts):
        return lax.all_to_all(parts, ("blk", "op"), 0, 0, tiled=True)

    part1, raw, kept, dots1 = kernel(
        functools.partial(first_body, n_blk, n_pair, counts),
        tables + left_ins + right_ins + psi_ins + [(raw_early, VMEM), (inter_early, VMEM)] + diags,
        [narrow, narrow, (left_late, bf16, HBM), dots],
        [inter, pltpu.SemaphoreType.DMA((n_late * n_pair + 2,))],
        **cost,
    )
    parts1 = totals(dots1)
    sig, *out1 = kernel(
        sigma_body,
        [(x, VMEM) for x in (part1, swap(part1, 1, n_op), raw)] + diags,
        [wide] + sends[1::2],
        nbytes=4 << 20,
    )
    got1 = [swap(block, 2 * e, n_op) for e, block in enumerate(out1, 1)]
    dots2, own, *out2 = kernel(
        functools.partial(second_body, n_blk, n_pair, count),
        tables + [(left_early, HBM), (kept, HBM)] + right_ins
        + [(x, VMEM) for x in (parts1, raw, sig)] + diags,
        [dots, ((4, n_blk, step, 2 * cols), bf16, VMEM)] + sends,
        [
            inter,
            pltpu.VMEM((n_blk, rows, 2 * cols), f32),
            pltpu.VMEM((n_blk, rows, 2 * cols), bf16),
            pltpu.VMEM((n_blk, rows, 2 * cols), bf16),
            pltpu.VMEM((n_blk, *left_late[1:]), bf16),
            pltpu.SemaphoreType.DMA((n_blk,)),
        ],
        flops=4 * cost["flops"],
        nbytes=24 << 20,
    )
    near, got1 = lax.optimization_barrier((out2[0], got1))
    parts2 = totals(dots2)
    got2 = [swap(near, 1, n_op)] + [swap(block, e, n_op) for e, block in enumerate(out2[1:], 2)]
    final = ((n_blk, step, n_op * cols), bf16, VMEM)
    new, res, energy = kernel(
        functools.partial(third_body, n_blk, n_op, count),
        [(slots, SMEM)] + [(x, VMEM) for x in (parts1, parts2)] + diags
        + [(x, VMEM) for x in (own, *got1, *got2)],
        [final, final, ((1,), f32, SMEM)],
        nbytes=4 << 20,
    )
    return new, res, energy


def solution(mesh):
    placed = (
        P(("grp", "blk"), None, None),
        P("op", ("grp", "blk"), None, None),
        P("op", ("grp", "blk"), None, None),
        P("op"),
        P("grp"),
        P("grp"),
        P("grp", None),
        P(("grp", "blk")),
    )

    def body(*args):
        psi, left_ops, right_ops, diag_right = args[0], args[1], args[2], args[7]
        n_op = mesh.shape["op"]
        cols = diag_right.shape[0] // n_op
        fits = (
            psi.shape[0] == 1
            and diag_right.shape[0] % n_op == 0
            and cols == LANES
            and n_op % 2 == 0
            and cols % right_ops.shape[2] == 0
            and cols // right_ops.shape[2] * n_op == right_ops.shape[1]
            and psi.shape[1] % (16 * n_op) == 0
            and n_op & (n_op - 1) == 0
            and mesh.shape["blk"] > n_op.bit_length() - 1
        )
        return (per_device if fits else per_device_general)(*args)

    return jax.shard_map(
        body,
        mesh=mesh,
        in_specs=placed,
        out_specs=(P("grp", "op", "blk"), P("grp", "op", "blk"), P("grp")),
        check_vma=False,
    )
```

```python
import functools

import jax
import jax.numpy as jnp
from jax import lax
from jax.experimental import pallas as pl
from jax.experimental.pallas import tpu as pltpu
from jax.sharding import PartitionSpec as P

EPS = 1e-06
LANES = 128
VMEM_LIMIT = 20 * 1024 * 1024


def per_device_general(
    psi, left_ops, right_ops, term_shift, slot_sector, sector_width, diag_left, diag_right
):
    sec_dev, rows, ncols = psi.shape
    nsec = slot_sector.shape[0]
    terms_dev = left_ops.shape[0]
    right_local = right_ops.shape[1]
    right_width = right_ops.shape[2]
    local_cols = diag_right.shape[0]
    count = float(nsec * rows * ncols)
    match = slot_sector[:, None] == jnp.arange(nsec)[None, :]
    widths = jnp.sum(jnp.where(match, sector_width[None, :], 0), axis=1)
    mask_all = (jnp.arange(rows)[None, :] < widths[:, None]).astype(jnp.float32)
    own_mask = lax.dynamic_slice_in_dim(mask_all, lax.axis_index("blk") * sec_dev, sec_dev, 0)
    raw = psi.astype(jnp.float32) * own_mask[:, :, None]
    squares = lax.psum(jnp.sum(raw * raw), "blk")
    v_left = (raw * lax.rsqrt(squares / count + EPS)).astype(jnp.bfloat16)
    onehots = (
        slot_sector[None, None, :] == slot_sector[None, :, None] - term_shift[:, None, None]
    ).astype(jnp.bfloat16)
    op_rows = rows // lax.axis_size("op")
    op_start = lax.axis_index("op") * op_rows
    dmat = diag_left[:, :, None] + diag_right[None, None, :]

    def left_local(field):
        return jnp.einsum(
            "ksij,sjc->ksic", left_ops, field, preferred_element_type=jnp.float32
        ).astype(jnp.bfloat16)

    def right_part(moved_in):
        flat = moved_in.reshape(terms_dev, nsec, rows * local_cols)
        shifted = jnp.einsum(
            "kts,ksx->ktx", onehots, flat, preferred_element_type=jnp.float32
        ).astype(jnp.bfloat16)
        shifted = shifted.reshape(terms_dev, nsec, rows, right_local, right_width)
        accum = jnp.einsum(
            "ktwrc,krdc->twrd", shifted, right_ops, preferred_element_type=jnp.float32
        )
        return accum.reshape(nsec, rows, local_cols) * mask_all[:, :, None]

    def op_total(partial_value):
        return lax.psum(partial_value.astype(jnp.bfloat16), "op").astype(jnp.float32)

    def final_rows(array):
        return lax.dynamic_slice_in_dim(array, op_start, op_rows, 1)

    def reduce_dots(values):
        sums = lax.psum(values, "blk")
        return tuple((item / count for item in sums))

    moved_first, v_moved = (
        lax.all_to_all(left_local(v_left), "blk", split_axis=3, concat_axis=1, tiled=True),
        lax.all_to_all(v_left[None], "blk", split_axis=3, concat_axis=1, tiled=True),
    )
    v_right = v_moved[0]
    vec32 = v_right.astype(jnp.float32)
    first_sigma = op_total(right_part(moved_first)) + dmat * vec32
    theta = reduce_dots((jnp.sum(vec32 * first_sigma),))[0]
    resid = first_sigma - theta * vec32
    den = dmat - theta
    corr = resid * den / jnp.maximum(den * den, 0.25)
    along = reduce_dots((jnp.sum(vec32 * corr),))[0]
    orth = corr - along * vec32
    norm_sq = reduce_dots((jnp.sum(orth * orth),))[0]
    update = (orth * lax.rsqrt(norm_sq + EPS)).astype(jnp.bfloat16)
    upd32 = update.astype(jnp.float32)
    upd_left = lax.all_to_all(update, "blk", split_axis=0, concat_axis=2, tiled=True)
    moved_second = lax.all_to_all(
        left_local(upd_left), "blk", split_axis=3, concat_axis=1, tiled=True
    )
    second_sigma = op_total(right_part(moved_second)) + dmat * upd32
    v_s1, u_s0, u_s1 = reduce_dots(
        (jnp.sum(vec32 * second_sigma), jnp.sum(upd32 * first_sigma), jnp.sum(upd32 * second_sigma))
    )
    h_mix = 0.5 * (v_s1 + u_s0)
    coef_v, coef_u, energy = ritz(theta, h_mix, u_s1)
    newvec = coef_v * vec32 + coef_u * upd32
    image = coef_v * first_sigma + coef_u * second_sigma
    new_out = final_rows(newvec.astype(jnp.bfloat16))
    res_out = final_rows((image - energy * newvec).astype(jnp.bfloat16))
    return (new_out, res_out, jnp.reshape(energy, (1,)))


def ritz(theta, h_mix, h_two):
    angle = 0.5 * jnp.arctan2(2.0 * h_mix, theta - h_two)
    sine = jnp.sin(angle)
    flip = jnp.where(sine > 0, -1.0, 1.0)
    coef_v = -sine * flip
    coef_u = jnp.cos(angle) * flip
    half = 0.5 * (theta - h_two)
    energy = 0.5 * (theta + h_two) - jnp.sqrt(half * half + h_mix * h_mix)
    return coef_v, coef_u, energy


VMEM, SMEM, HBM = pltpu.VMEM, pltpu.SMEM, pltpu.HBM


def kernel(body, ins, outs, scratch=(), flops=0, nbytes=0):
    return pl.pallas_call(
        body,
        out_shape=[
            HBM(shape, dtype) if space == HBM else jax.ShapeDtypeStruct(shape, dtype)
            for shape, dtype, space in outs
        ],
        in_specs=[pl.BlockSpec(memory_space=space) for _, space in ins],
        out_specs=[pl.BlockSpec(memory_space=space) for _, _, space in outs],
        scratch_shapes=list(scratch),
        compiler_params=pltpu.CompilerParams(vmem_limit_bytes=VMEM_LIMIT),
        cost_estimate=pl.CostEstimate(flops=flops, bytes_accessed=nbytes, transcendentals=0),
    )(*[pltpu.with_memory_space_constraint(x, HBM) if space == HBM else x for x, space in ins])


def ring_at(place, n_blk):
    place = place % n_blk if isinstance(place, int) else lax.rem(place + n_blk, n_blk)
    even, odd = 2 * place, 2 * (n_blk - place) - 1
    if isinstance(place, int):
        return even if even < n_blk else odd
    return jnp.where(even < n_blk, even, odd)


def ring_place(index, n_blk):
    return jnp.where(lax.rem(index, 2) == 1, n_blk - (index + 1) // 2, index // 2)


def onward(block, d, n_blk):
    pairs = [(ring_at(i, n_blk), ring_at(i + d, n_blk)) for i in range(n_blk)]
    return lax.ppermute(block, "blk", pairs)


def swap(block, e, n_op):
    return lax.ppermute(block, "op", [(i, i ^ e) for i in range(n_op)])


def gather(own, n_blk, n_op, pack, table, early):
    bits = [1 << b for b in reversed(range(1, n_op.bit_length() - 1))]
    order = sorted(range(1, n_blk), key=lambda d: min(d, n_blk - d))
    left, psi, right, tables, columns = {(0, 0): own}, {}, None, None, None
    waiting, across, made = {(0, 0): 0}, {}, None
    for j in range(n_blk + len(bits)):
        new, moved = {}, {}
        for (d, e), done in waiting.items():
            if e == 0 and d + 1 < n_blk:
                new[d + 1, 0] = onward(left[d, 0], 1, n_blk), 0
            for b in range(done, len(bits)):
                new[d, e ^ bits[b]] = swap(left[d, e], bits[b], n_op), b + 1
        left.update({key: block for key, (block, _) in new.items()})
        kept = {key: block for key, (block, _) in new.items() if key[1] == 0}
        kept.update(across)
        across = {key: block for key, (block, _) in new.items() if key[1] != 0}
        if j == 0:
            columns, packed = pack()
            right = [packed[0]]
            right += [swap(part, 2 * e, n_op) for e, part in enumerate(packed[1:], 1)]
            moved["columns"] = columns
        due = order[j : j + 1] if j < 2 else order[2:] if j == n_blk - 1 else []
        moved["psi"] = {d: onward(columns[d], d, n_blk) for d in due}
        if j == 0:
            moved["right"] = right
        if j == 1:
            moved["tables"] = table(right)
        if j == n_blk - 1 and j >= len(bits) + 1:
            n_early = min(2, n_blk - 1)
            psi[0] = [columns[0]]
            moved["early"] = early(left, psi, n_early, tables)
        if 1 <= j <= 2:
            moved["other"] = {d: swap(psi[d][0], 1, n_op) for d in order[j - 1 : j]}
        if not kept:
            break
        waiting = {key: done for key, (_, done) in new.items()}
        kept, moved = lax.optimization_barrier((kept, moved))
        left.update(kept)
        right, tables = moved.get("right", right), moved.get("tables", tables)
        columns = moved.get("columns", columns)
        made = moved.get("early", made)
        psi.update({d: [block] for d, block in moved["psi"].items()})
        for d, block in moved.get("other", {}).items():
            psi[d].append(block)
    return left, psi, right, tables, made


def place_of():
    return lax.axis_index("blk"), lax.axis_index("op")


def pack_body(n_blk, n_op, shift, _, psi, right_in, *outs):
    n_pair = n_op // 2
    psi_out, right_out, right, sems = outs[:n_blk], outs[n_blk : n_blk + n_pair], outs[-2], outs[-1]
    terms, local, width, _ = right.shape
    cols = local * width // n_op
    per = cols // width
    own_blk, own_op = place_of()
    fetch = pltpu.make_async_copy(right_in, right, sems.at[2 * n_blk])
    fetch.start()
    copies = []
    for d in range(n_blk):
        there = ring_at(ring_place(own_blk, n_blk) + d, n_blk) * n_op
        for h in range(psi_out[d].shape[1] // cols):
            start = pl.multiple_of((there + (own_op ^ h)) * cols, LANES)
            copy = pltpu.make_async_copy(
                psi.at[0, :, pl.ds(start, cols)],
                psi_out[d].at[:, h * cols : (h + 1) * cols],
                sems.at[2 * d + h],
            )
            copy.start()
            copies.append(copy)
    lane = lax.broadcasted_iota(jnp.int32, (16, 2 * cols), 1)
    line = jnp.zeros((16, 2 * cols), jnp.float32)
    for k in range(terms):
        line = jnp.where(lane == k, shift[k].astype(jnp.float32), line)
    square = [lax.broadcasted_iota(jnp.int32, (width, width), axis) for axis in (0, 1)]
    unit = (square[0] == square[1]).astype(jnp.bfloat16)
    fetch.wait()
    for e in range(n_pair):
        for k in range(terms):
            turned = []
            for h in range(2):
                first = (own_op ^ (2 * e) ^ h) * per
                for r in range(per):
                    turned.append(
                        lax.dot_general(
                            right[k, first + r], unit, (((0,), (0,)), ((), ())),
                            preferred_element_type=jnp.float32,
                        )
                    )
            side_by_side = jnp.concatenate(turned, axis=1).astype(jnp.bfloat16)
            right_out[e][k * width : (k + 1) * width] = side_by_side
        right_out[e][terms * width :] = line.astype(jnp.bfloat16)
    for copy in copies:
        copy.wait()


def table_body(n_blk, terms, sector, width, left_diag, right_diag, *refs):
    tails, src, widths, slots, diag, right_out = refs[:-5], *refs[-5:]
    right_out[...] = right_diag[...]
    n_pair = len(tails)
    rows, cols = tails[0].shape
    own_blk, _ = place_of()
    lane = lax.broadcasted_iota(jnp.int32, (16, cols), 1)
    for d in range(n_blk):
        slot = ring_at(ring_place(own_blk, n_blk) - d, n_blk)
        slots[d] = slot
        widths[d] = width[sector[slot]]
    for e in range(n_pair):
        tail = tails[e][rows - 16 :].astype(jnp.float32)
        for k in range(terms):
            shift = jnp.max(jnp.where(lane == k, tail, -1e9)).astype(jnp.int32)
            for t in range(n_blk):
                want = sector[slots[t]] - shift
                found = jnp.int32(n_blk)
                for d in range(n_blk):
                    found = jnp.where(sector[slots[d]] == want, d, found)
                src[(t * n_pair + e) * terms + k] = found
    for d in range(n_blk):
        row = left_diag[pl.ds(slots[d], 1), :]
        diag[d] = jnp.transpose(jnp.broadcast_to(row, (diag.shape[2], row.shape[1])))


def diagonal(diag, right_diag, d, h):
    cols = diag.shape[2]
    _, own_op = place_of()
    start = pl.multiple_of((own_op ^ h) * cols, LANES)
    return diag[d] + right_diag[:, pl.ds(start, cols)]


def row_mask(width, shape):
    return lax.broadcasted_iota(jnp.int32, shape, 0) < width


def fold(x):
    return jnp.sum(x.reshape(-1, 8, x.shape[-1]), axis=0)


def whole(x):
    return jnp.sum(jnp.sum(x, axis=0, keepdims=True), axis=1, keepdims=True)


def spread(values, out):
    lane = lax.broadcasted_iota(jnp.int32, out.shape[1:], 1)
    row = jnp.zeros(out.shape[1:], jnp.float32)
    for j, value in enumerate(values):
        row = jnp.where(lane == j, value, row)
    for d in range(out.shape[0]):
        out[d] = row


def by_block(packed, terms, k):
    rows, cols = packed.shape
    width = (rows - 16) // terms
    lane = lax.broadcasted_iota(jnp.int32, (width, cols), 1)
    block = packed[k * width : (k + 1) * width].astype(jnp.float32)
    parts = []
    for r in range(cols // width):
        inside = (lane >= r * width) & (lane < (r + 1) * width)
        parts.append(jnp.where(inside, block, 0.0).astype(jnp.bfloat16))
    return jnp.concatenate(parts, axis=0)


def left_products(block, left, inter):
    n_terms, rows, cols = inter.shape
    at = 0
    while at < n_terms:
        ops = left(at)
        terms = ops.shape[0]
        prod = jnp.dot(ops.reshape(terms * rows, rows), block, preferred_element_type=jnp.float32)
        inter[at : at + terms] = prod.astype(jnp.bfloat16).reshape(terms, rows, cols)
        at += terms


def sum_terms(src, widths, inter, right, out, emit):
    n_blk, n_terms, _, _ = inter.shape
    n_blk -= 1
    terms = n_terms // len(right)
    turned = [by_block(right[j // terms], terms, j % terms) for j in range(n_terms)]
    for t in range(n_blk):
        total = None
        for j in range(n_terms):
            part = jnp.dot(
                inter[src[t * n_terms + j], j], turned[j], preferred_element_type=jnp.float32
            )
            total = part if total is None else total + part
        total = jnp.where(row_mask(widths[t], total.shape), total, 0.0)
        out[t] = total.astype(jnp.bfloat16)
        emit(t, total)


def keep(left, left_out, sems):
    copies = []
    for d, line in enumerate(left):
        for e, ref in enumerate(line):
            copies.append(pltpu.make_async_copy(ref, left_out.at[d, e], sems.at[d * len(line) + e]))
            copies[-1].start()
    return copies


def masked(psi, width, out):
    at = 0
    for ref in psi:
        block = ref[...].astype(jnp.float32)
        block = jnp.where(row_mask(width, block.shape), block, 0.0)
        out[:, at : at + block.shape[1]] = block.astype(jnp.bfloat16)
        at += block.shape[1]


def take(refs, counts):
    out = []
    for count in counts:
        out.append(refs[:count])
        refs = refs[count:]
    return out, refs


def products_of(psi, left, widths, first, raw_out, inter):
    for d, line in enumerate(left):
        masked(psi[d], widths[first + d], raw_out.at[d])
        terms = line[0].shape[0]
        left_products(raw_out[d], lambda at: line[at // terms][...], inter.at[d])


def early_body(n_pair, counts, widths, *refs):
    left, refs = take(refs, [n_pair] * len(counts))
    psi, (raw_out, inter_out, left_out, sems) = take(refs, counts)
    copies = keep(left, left_out, sems)
    products_of(psi, left, widths, 0, raw_out, inter_out)
    for copy in copies:
        copy.wait()


def first_body(n_blk, n_pair, counts, src, widths, *refs):
    n_late = len(counts)
    n_early = n_blk - n_late
    left, refs = take(refs, [n_pair] * n_late)
    (right,), refs = take(refs, [n_pair])
    psi, refs = take(refs, counts)
    raw_in, inter_in, diag, right_diag, part_out, raw_out, left_out, dots_out, inter, sems = refs
    ready = []
    for j, (given, own) in enumerate(((inter_in, inter), (raw_in, raw_out))):
        ready.append(
            pltpu.make_async_copy(given, own.at[:n_early], sems.at[n_late * n_pair + j])
        )
        ready[-1].start()
    copies = keep(left, left_out, sems)
    inter[n_blk] = jnp.zeros_like(inter[n_blk])
    products_of(
        psi, left, widths, n_early, raw_out.at[n_early:], inter.at[n_early:n_blk]
    )
    for copy in ready:
        copy.wait()
    cols = diag.shape[2]
    zero = jnp.zeros((8, cols), jnp.float32)
    sums = [zero, zero]

    def emit(d, total):
        for h in range(2):
            part = slice(h * cols, (h + 1) * cols)
            raw = raw_out[d, :, part].astype(jnp.float32)
            image = total[:, part]
            if h == 0:
                image = image + diagonal(diag, right_diag, d, h) * raw
                sums[0] = sums[0] + fold(raw * raw)
            sums[1] = sums[1] + fold(raw * image)

    sum_terms(src, widths, inter, right, part_out, emit)
    spread([whole(x) for x in sums], dots_out)
    for copy in copies:
        copy.wait()


def send_rows(e, send, d, *refs):
    _, own_op = place_of()
    step = send.shape[2]
    rows = pl.ds(pl.multiple_of((own_op ^ e) * step, step), step)
    for j, ref in enumerate(refs):
        send[j, d] = ref[d, rows].astype(send.dtype)


def total_of(mine, other, d, h, cols):
    own = mine[d, :, h * cols : (h + 1) * cols].astype(jnp.float32)
    return own + other[d, :, (1 - h) * cols : (2 - h) * cols].astype(jnp.float32)


def sigma_body(mine, other, raw_in, diag, right_diag, sig_out, *sends):
    n_blk, _, cols = diag.shape
    for d in range(n_blk):
        for h in range(2):
            part = slice(h * cols, (h + 1) * cols)
            raw = raw_in[d, :, part].astype(jnp.float32)
            sigma = total_of(mine, other, d, h, cols) + diagonal(diag, right_diag, d, h) * raw
            sig_out[d, :, part] = sigma
        for e, send in enumerate(sends, 1):
            send_rows(2 * e, send, d, raw_in, sig_out)


def norm_theta(parts, count):
    tot = jnp.sum(parts, axis=0) * (1.0 / count)
    scale = lax.rsqrt(tot[:, 0:1] + EPS)
    return scale, tot[:, 1:2] * scale * scale


def second_body(n_blk, n_pair, count, src, widths, left_early, left_late, *refs):
    right, refs = refs[:n_pair], refs[n_pair:]
    parts, raw_in, sig, diag, right_diag, dots_out, own_out = refs[:7]
    sends, (inter, corr, fld, part_out, held, sems) = refs[7:-6], refs[-6:]
    copies = []
    n_early = left_early.shape[0]
    for d in range(n_blk):
        kept = left_early.at[d] if d < n_early else left_late.at[d - n_early]
        copies.append(pltpu.make_async_copy(kept, held.at[d], sems.at[d]))
        copies[-1].start()
    inter[n_blk] = jnp.zeros_like(inter[n_blk])
    scale, theta = norm_theta(parts[...], count)
    cols = diag.shape[2]
    halves = []
    for h in range(2):
        part = slice(h * cols, (h + 1) * cols)
        vv = vc = vs = jnp.zeros((8, cols), jnp.float32)
        for d in range(n_blk):
            vec = raw_in[d, :, part].astype(jnp.float32) * scale
            sigma = sig[d, :, part] * scale
            den = diagonal(diag, right_diag, d, h) - theta
            item = (sigma - theta * vec) * den / jnp.maximum(den * den, 0.25)
            corr[d, :, part] = item
            vv, vc = vv + fold(vec * vec), vc + fold(vec * item)
            if h == 0:
                vs = vs + fold(vec * sigma)
        halves.append((whole(vv), whole(vc), vs))
    along = (halves[0][1] + halves[1][1]) / jnp.maximum(halves[0][0] + halves[1][0], 1e-30)
    terms = held.shape[2]
    for copy in copies:
        copy.wait()
    for d in range(n_blk):
        for h in range(2):
            part = slice(h * cols, (h + 1) * cols)
            vec = raw_in[d, :, part].astype(jnp.float32) * scale
            fld[d, :, part] = (corr[d, :, part] - along * vec).astype(jnp.bfloat16)
        left_products(fld[d], lambda at: held[d, at // terms], inter.at[d])
    zero = jnp.zeros((8, cols), jnp.float32)
    sums = [zero for _ in range(5)]

    def emit(d, total):
        for h in range(2):
            part = slice(h * cols, (h + 1) * cols)
            field = fld[d, :, part].astype(jnp.float32)
            raw = raw_in[d, :, part].astype(jnp.float32)
            image = total[:, part]
            if h == 0:
                image = image + diagonal(diag, right_diag, d, h) * field
                for j, prod in enumerate((field * field, raw * field, field * sig[d, :, part])):
                    sums[j] = sums[j] + fold(prod)
            sums[3] = sums[3] + fold(raw * image)
            sums[4] = sums[4] + fold(field * image)
        for e, send in enumerate(sends, 1):
            send_rows(e, send, d, *((part_out,) if e % 2 else (fld, part_out)))
        rows = pl.ds(pl.multiple_of(own_op * step, step), step)
        for j, ref in enumerate((raw_in, sig, fld, part_out)):
            own_out[j, d] = ref[d, rows].astype(own_out.dtype)

    _, own_op = place_of()
    step = own_out.shape[2]
    sum_terms(src, widths, inter, right, part_out, emit)
    vv, vc, vs = halves[0]
    ff, vf, fs, vt, ft = (whole(x) for x in sums)
    spread([vv, vc, whole(vs), ff, vf * scale, fs * scale, vt * scale, ft], dots_out)


def ritz_pair(theta, h_mix, h_two):
    diff, twice = theta - h_two, 2.0 * h_mix
    size = jnp.sqrt(diff * diff + twice * twice)
    some = size > 0.0
    safe = jnp.where(some, size, 1.0)
    big = jnp.sqrt(0.5 + 0.5 * jnp.abs(diff) / safe)
    small = 0.5 * jnp.abs(twice) / (safe * big)
    sine = jnp.where(diff >= 0.0, small, big)
    cosine = jnp.where(diff >= 0.0, big, small)
    sine = jnp.where(some, sine, 0.0)
    cosine = jnp.where(some, cosine, 1.0)
    upward = (twice > 0.0) | ((twice == 0.0) & (diff < 0.0))
    return sine, jnp.where(upward, -cosine, cosine), 0.5 * (theta + h_two) - 0.5 * size


def third_body(n_blk, n_op, count, slots, parts1, parts2, diag, right_diag, own, *refs):
    n_far = n_op // 2 - 1
    got1, got2 = refs[:n_far], refs[n_far : n_far + n_op - 1]
    new_out, res_out, energy_out = refs[n_far + n_op - 1 :]
    step, cols = new_out.shape[1], new_out.shape[2] // n_op
    own_blk, own_op = place_of()
    scale, theta = norm_theta(parts1[...], count)
    pairs = parts2[...].reshape(n_blk * n_op // 2, 2, *parts2.shape[1:])
    pairs = pairs[:, 0] + pairs[:, 1]
    vv, vc, vs, ff, vf, fs, vt, ft = (pairs[:, 0, j : j + 1] for j in range(8))

    def mean(x):
        return jnp.sum(x, axis=0, keepdims=True) * (1.0 / count)

    def nearest(vv, vc):
        return vc / jnp.maximum(vv, 1e-30)

    along = mean(vc)
    beta = nearest(vv, vc) - along
    norm_sq = mean(ff + 2.0 * beta * vf + beta * beta * vv)
    unit = lax.rsqrt(jnp.maximum(norm_sq, 0.0) + EPS)
    v_s1 = unit * mean(vt + beta * vs)
    u_s0 = unit * mean(fs + beta * vs)
    u_s1 = unit * unit * mean(ft + beta * (vt + fs) + beta * beta * vs)
    cv, cu, energy = ritz_pair(theta, 0.5 * (v_s1 + u_s0), u_s1)
    energy_out[0] = jnp.max(energy)
    cu = cu * unit
    mine = pl.ds(pl.multiple_of(own_op * step, step), step)
    for e in range(0, n_op, 2):
        there = own_blk * n_op + (own_op ^ e)
        pair = parts2[there] + parts2[own_blk * n_op + (own_op ^ e ^ 1)]
        on_vec = cv + cu * (nearest(pair[:, 0:1], pair[:, 1:2]) - along)
        for h in range(2):
            at = pl.multiple_of((own_op ^ e ^ h) * cols, LANES)
            part, crossed = slice(h * cols, (h + 1) * cols), slice((1 - h) * cols, (2 - h) * cols)
            for d in range(n_blk):
                dmat = diag[d, mine] + right_diag[:, pl.ds(at, cols)]
                blocks = [own.at[j] for j in range(4)]
                if e:
                    far, near = got1[e // 2 - 1], got2[e - 1]
                    blocks = far.at[0], far.at[1], near.at[0], near.at[1]
                raw, sigma, fld, image = (x[d, :, part].astype(jnp.float32) for x in blocks)
                vec, sigma = raw * scale, sigma * scale
                image = image + got2[e][0, d, :, crossed].astype(jnp.float32) + dmat * fld
                newvec = on_vec * vec + cu * fld
                res = on_vec * sigma + cu * image - energy * newvec
                new_out[slots[d], :, pl.ds(at, cols)] = newvec.astype(jnp.bfloat16)
                res_out[slots[d], :, pl.ds(at, cols)] = res.astype(jnp.bfloat16)


def per_device(
    psi, left_ops, right_ops, term_shift, slot_sector, sector_width, diag_left, diag_right
):
    n_blk, n_op = lax.axis_size("blk"), lax.axis_size("op")
    _, rows, ncols = psi.shape
    terms, _, width, _ = right_ops.shape
    n_pair = n_op // 2
    cols = diag_right.shape[0] // n_op
    step = rows // n_op
    count = float(n_blk * rows * ncols)
    n_dev = n_blk * n_op
    bf16, f32, i32 = jnp.bfloat16, jnp.float32, jnp.int32
    far = sorted(range(1, n_blk), key=lambda d: min(d, n_blk - d))[2:]

    def pack():
        first = swap(term_shift, 1, n_op)
        sent = kernel(
            functools.partial(pack_body, n_blk, n_op),
            [(term_shift, SMEM), (first, SMEM), (psi, HBM), (right_ops, HBM)],
            [((rows, 2 * cols if d in (0, *far) else cols), bf16, VMEM) for d in range(n_blk)]
            + [((terms * width + 16, 2 * cols), bf16, VMEM)] * n_pair,
            [pltpu.VMEM(right_ops.shape, bf16), pltpu.SemaphoreType.DMA((2 * n_blk + 1,))],
            nbytes=1 << 20,
        )
        return sent[:n_blk], sent[n_blk:]

    def table(right):
        return kernel(
            functools.partial(table_body, n_blk, terms),
            [(slot_sector, SMEM), (sector_width, SMEM), (diag_left, VMEM), (diag_right[None], VMEM)]
            + [(block, VMEM) for block in right],
            [((n_blk * n_pair * terms,), i32, SMEM)]
            + [((n_blk,), i32, SMEM)] * 2
            + [((n_blk, rows, LANES), f32, VMEM), ((1, n_op * cols), f32, VMEM)],
        )

    def inputs(left, psi, those):
        blocks = [left[d, 2 * e] for d in those for e in range(n_pair)]
        halves = [half for d in those for half in psi[d]]
        return [(x, VMEM) for x in blocks], [(x, VMEM) for x in halves], [len(psi[d]) for d in those]

    def early(left, psi, n_early, tables):
        left_ins, psi_ins, counts = inputs(left, psi, range(n_early))
        return kernel(
            functools.partial(early_body, n_pair, counts),
            [(tables[1], SMEM)] + left_ins + psi_ins,
            [
                ((n_early, rows, 2 * cols), bf16, VMEM),
                ((n_early, n_pair * terms, rows, 2 * cols), bf16, VMEM),
                ((n_early, n_pair, terms, rows, rows), bf16, HBM),
            ],
            [pltpu.SemaphoreType.DMA((n_early * n_pair,))],
            flops=2 * n_early * rows * rows * 2 * cols * terms * n_pair,
            nbytes=4 << 20,
        )

    left, psi_by, right, (src, widths, slots, *both), (raw_early, inter_early, left_early) = gather(
        left_ops[:, 0], n_blk, n_op, pack, table, early
    )
    n_early = raw_early.shape[0]
    n_late = n_blk - n_early
    left_ins, psi_ins, counts = inputs(left, psi_by, range(n_early, n_blk))
    right_ins = [(block, VMEM) for block in right]
    diags = [(x, VMEM) for x in both]

    tables = [(src, SMEM), (widths, SMEM)]
    narrow = ((n_blk, rows, 2 * cols), bf16, VMEM)
    dots = ((n_dev, 1, LANES), f32, VMEM)
    wide = ((n_blk, rows, 2 * cols), f32, VMEM)
    sends = [((2 - e % 2, n_blk, step, 2 * cols), bf16, VMEM) for e in range(1, n_op)]
    inter = pltpu.VMEM((n_blk + 1, n_pair * terms, rows, 2 * cols), bf16)
    left_late = (n_late, n_pair, terms, rows, rows)
    cost = dict(flops=2 * n_blk * rows * 2 * cols * terms * n_pair * (rows + 2 * cols), nbytes=6 << 20)

    def totals(parts):
        return lax.all_to_all(parts, ("blk", "op"), 0, 0, tiled=True)

    part1, raw, kept, dots1 = kernel(
        functools.partial(first_body, n_blk, n_pair, counts),
        tables + left_ins + right_ins + psi_ins + [(raw_early, VMEM), (inter_early, VMEM)] + diags,
        [narrow, narrow, (left_late, bf16, HBM), dots],
        [inter, pltpu.SemaphoreType.DMA((n_late * n_pair + 2,))],
        **cost,
    )
    parts1 = totals(dots1)
    sig, *out1 = kernel(
        sigma_body,
        [(x, VMEM) for x in (part1, swap(part1, 1, n_op), raw)] + diags,
        [wide] + sends[1::2],
        nbytes=4 << 20,
    )
    got1 = [swap(block, 2 * e, n_op) for e, block in enumerate(out1, 1)]
    dots2, own, *out2 = kernel(
        functools.partial(second_body, n_blk, n_pair, count),
        tables + [(left_early, HBM), (kept, HBM)] + right_ins
        + [(x, VMEM) for x in (parts1, raw, sig)] + diags,
        [dots, ((4, n_blk, step, 2 * cols), bf16, VMEM)] + sends,
        [
            inter,
            pltpu.VMEM((n_blk, rows, 2 * cols), f32),
            pltpu.VMEM((n_blk, rows, 2 * cols), bf16),
            pltpu.VMEM((n_blk, rows, 2 * cols), bf16),
            pltpu.VMEM((n_blk, *left_late[1:]), bf16),
            pltpu.SemaphoreType.DMA((n_blk,)),
        ],
        flops=4 * cost["flops"],
        nbytes=24 << 20,
    )
    near, got1 = lax.optimization_barrier((out2[0], got1))
    parts2 = totals(dots2)
    got2 = [swap(near, 1, n_op)] + [swap(block, e, n_op) for e, block in enumerate(out2[1:], 2)]
    final = ((n_blk, step, n_op * cols), bf16, VMEM)
    new, res, energy = kernel(
        functools.partial(third_body, n_blk, n_op, count),
        [(slots, SMEM)] + [(x, VMEM) for x in (parts1, parts2)] + diags
        + [(x, VMEM) for x in (own, *got1, *got2)],
        [final, final, ((1,), f32, SMEM)],
        nbytes=4 << 20,
    )
    return new, res, energy


def solution(mesh):
    placed = (
        P(("grp", "blk"), None, None),
        P("op", ("grp", "blk"), None, None),
        P("op", ("grp", "blk"), None, None),
        P("op"),
        P("grp"),
        P("grp"),
        P("grp", None),
        P(("grp", "blk")),
    )

    def body(*args):
        psi, left_ops, right_ops, diag_right = args[0], args[1], args[2], args[7]
        n_op = mesh.shape["op"]
        cols = diag_right.shape[0] // n_op
        fits = (
            psi.shape[0] == 1
            and diag_right.shape[0] % n_op == 0
            and cols == LANES
            and n_op % 2 == 0
            and cols % right_ops.shape[2] == 0
            and cols // right_ops.shape[2] * n_op == right_ops.shape[1]
            and psi.shape[1] % (16 * n_op) == 0
            and n_op & (n_op - 1) == 0
            and mesh.shape["blk"] > n_op.bit_length() - 1
        )
        return (per_device if fits else per_device_general)(*args)

    return jax.shard_map(
        body,
        mesh=mesh,
        in_specs=placed,
        out_specs=(P("grp", "op", "blk"), P("grp", "op", "blk"), P("grp")),
        check_vma=False,
    )
```

```python
import functools

import jax
import jax.numpy as jnp
from jax import lax
from jax.experimental import pallas as pl
from jax.experimental.pallas import tpu as pltpu
from jax.sharding import PartitionSpec as P

EPS = 1e-06
LANES = 128
VMEM_LIMIT = 20 * 1024 * 1024


def per_device_general(
    psi, left_ops, right_ops, term_shift, slot_sector, sector_width, diag_left, diag_right
):
    sec_dev, rows, ncols = psi.shape
    nsec = slot_sector.shape[0]
    terms_dev = left_ops.shape[0]
    right_local = right_ops.shape[1]
    right_width = right_ops.shape[2]
    local_cols = diag_right.shape[0]
    count = float(nsec * rows * ncols)
    match = slot_sector[:, None] == jnp.arange(nsec)[None, :]
    widths = jnp.sum(jnp.where(match, sector_width[None, :], 0), axis=1)
    mask_all = (jnp.arange(rows)[None, :] < widths[:, None]).astype(jnp.float32)
    own_mask = lax.dynamic_slice_in_dim(mask_all, lax.axis_index("blk") * sec_dev, sec_dev, 0)
    raw = psi.astype(jnp.float32) * own_mask[:, :, None]
    squares = lax.psum(jnp.sum(raw * raw), "blk")
    v_left = (raw * lax.rsqrt(squares / count + EPS)).astype(jnp.bfloat16)
    onehots = (
        slot_sector[None, None, :] == slot_sector[None, :, None] - term_shift[:, None, None]
    ).astype(jnp.bfloat16)
    op_rows = rows // lax.axis_size("op")
    op_start = lax.axis_index("op") * op_rows
    dmat = diag_left[:, :, None] + diag_right[None, None, :]

    def left_local(field):
        return jnp.einsum(
            "ksij,sjc->ksic", left_ops, field, preferred_element_type=jnp.float32
        ).astype(jnp.bfloat16)

    def right_part(moved_in):
        flat = moved_in.reshape(terms_dev, nsec, rows * local_cols)
        shifted = jnp.einsum(
            "kts,ksx->ktx", onehots, flat, preferred_element_type=jnp.float32
        ).astype(jnp.bfloat16)
        shifted = shifted.reshape(terms_dev, nsec, rows, right_local, right_width)
        accum = jnp.einsum(
            "ktwrc,krdc->twrd", shifted, right_ops, preferred_element_type=jnp.float32
        )
        return accum.reshape(nsec, rows, local_cols) * mask_all[:, :, None]

    def op_total(partial_value):
        return lax.psum(partial_value.astype(jnp.bfloat16), "op").astype(jnp.float32)

    def final_rows(array):
        return lax.dynamic_slice_in_dim(array, op_start, op_rows, 1)

    def reduce_dots(values):
        sums = lax.psum(values, "blk")
        return tuple((item / count for item in sums))

    moved_first, v_moved = (
        lax.all_to_all(left_local(v_left), "blk", split_axis=3, concat_axis=1, tiled=True),
        lax.all_to_all(v_left[None], "blk", split_axis=3, concat_axis=1, tiled=True),
    )
    v_right = v_moved[0]
    vec32 = v_right.astype(jnp.float32)
    first_sigma = op_total(right_part(moved_first)) + dmat * vec32
    theta = reduce_dots((jnp.sum(vec32 * first_sigma),))[0]
    resid = first_sigma - theta * vec32
    den = dmat - theta
    corr = resid * den / jnp.maximum(den * den, 0.25)
    along = reduce_dots((jnp.sum(vec32 * corr),))[0]
    orth = corr - along * vec32
    norm_sq = reduce_dots((jnp.sum(orth * orth),))[0]
    update = (orth * lax.rsqrt(norm_sq + EPS)).astype(jnp.bfloat16)
    upd32 = update.astype(jnp.float32)
    upd_left = lax.all_to_all(update, "blk", split_axis=0, concat_axis=2, tiled=True)
    moved_second = lax.all_to_all(
        left_local(upd_left), "blk", split_axis=3, concat_axis=1, tiled=True
    )
    second_sigma = op_total(right_part(moved_second)) + dmat * upd32
    v_s1, u_s0, u_s1 = reduce_dots(
        (jnp.sum(vec32 * second_sigma), jnp.sum(upd32 * first_sigma), jnp.sum(upd32 * second_sigma))
    )
    h_mix = 0.5 * (v_s1 + u_s0)
    coef_v, coef_u, energy = ritz(theta, h_mix, u_s1)
    newvec = coef_v * vec32 + coef_u * upd32
    image = coef_v * first_sigma + coef_u * second_sigma
    new_out = final_rows(newvec.astype(jnp.bfloat16))
    res_out = final_rows((image - energy * newvec).astype(jnp.bfloat16))
    return (new_out, res_out, jnp.reshape(energy, (1,)))


def ritz(theta, h_mix, h_two):
    angle = 0.5 * jnp.arctan2(2.0 * h_mix, theta - h_two)
    sine = jnp.sin(angle)
    flip = jnp.where(sine > 0, -1.0, 1.0)
    coef_v = -sine * flip
    coef_u = jnp.cos(angle) * flip
    half = 0.5 * (theta - h_two)
    energy = 0.5 * (theta + h_two) - jnp.sqrt(half * half + h_mix * h_mix)
    return coef_v, coef_u, energy


VMEM, SMEM, HBM = pltpu.VMEM, pltpu.SMEM, pltpu.HBM


def kernel(body, ins, outs, scratch=(), flops=0, nbytes=0):
    return pl.pallas_call(
        body,
        out_shape=[
            HBM(shape, dtype) if space == HBM else jax.ShapeDtypeStruct(shape, dtype)
            for shape, dtype, space in outs
        ],
        in_specs=[pl.BlockSpec(memory_space=space) for _, space in ins],
        out_specs=[pl.BlockSpec(memory_space=space) for _, _, space in outs],
        scratch_shapes=list(scratch),
        compiler_params=pltpu.CompilerParams(vmem_limit_bytes=VMEM_LIMIT),
        cost_estimate=pl.CostEstimate(flops=flops, bytes_accessed=nbytes, transcendentals=0),
    )(*[pltpu.with_memory_space_constraint(x, HBM) if space == HBM else x for x, space in ins])


def ring_at(place, n_blk):
    place = place % n_blk if isinstance(place, int) else lax.rem(place + n_blk, n_blk)
    even, odd = 2 * place, 2 * (n_blk - place) - 1
    if isinstance(place, int):
        return even if even < n_blk else odd
    return jnp.where(even < n_blk, even, odd)


def ring_place(index, n_blk):
    return jnp.where(lax.rem(index, 2) == 1, n_blk - (index + 1) // 2, index // 2)


def onward(block, d, n_blk):
    pairs = [(ring_at(i, n_blk), ring_at(i + d, n_blk)) for i in range(n_blk)]
    return lax.ppermute(block, "blk", pairs)


def swap(block, e, n_op):
    return lax.ppermute(block, "op", [(i, i ^ e) for i in range(n_op)])


def gather(own, n_blk, n_op, pack, table, early):
    bits = [1 << b for b in reversed(range(1, n_op.bit_length() - 1))]
    order = sorted(range(1, n_blk), key=lambda d: min(d, n_blk - d))
    left, psi, right, tables, columns = {(0, 0): own}, {}, None, None, None
    waiting, across, late, made = {(0, 0): 0}, {}, None, None
    for j in range(n_blk + len(bits)):
        new, moved = {}, {}
        for (d, e), done in waiting.items():
            if e == 0 and d + 1 < n_blk:
                new[d + 1, 0] = onward(left[d, 0], 1, n_blk), 0
            for b in range(done, len(bits)):
                new[d, e ^ bits[b]] = swap(left[d, e], bits[b], n_op), b + 1
        left.update({key: block for key, (block, _) in new.items()})
        kept = {key: block for key, (block, _) in new.items() if key[1] == 0}
        kept.update(across)
        across = {key: block for key, (block, _) in new.items() if key[1] != 0}
        if late is not None:
            moved["psi"] = late
        if j == 0:
            columns, packed = pack()
            right = [packed[0]]
            right += [swap(part, 2 * e, n_op) for e, part in enumerate(packed[1:], 1)]
            moved["columns"] = columns
        if j == 0:
            moved["right"] = right
        if j == 1:
            moved["tables"] = table(right)
        if j == n_blk - 1 and j >= len(bits) + 1:
            n_early = min(2, n_blk - 1)
            psi[0] = [columns[0]]
            moved["early"] = early(left, psi, n_early, tables)
        if 2 <= j < n_blk:
            moved["other"] = swap(psi[order[j - 2]][0], 1, n_op)
        late = onward(columns[order[j]], order[j], n_blk) if j < n_blk - 1 else None
        if not kept:
            break
        waiting = {key: done for key, (_, done) in new.items()}
        kept, moved = lax.optimization_barrier((kept, moved))
        left.update(kept)
        right, tables = moved.get("right", right), moved.get("tables", tables)
        columns = moved.get("columns", columns)
        made = moved.get("early", made)
        if "psi" in moved:
            psi[order[j - 1]] = [moved["psi"]]
        if "other" in moved:
            psi[order[j - 2]].append(moved["other"])
    return left, psi, right, tables, made


def place_of():
    return lax.axis_index("blk"), lax.axis_index("op")


def pack_body(n_blk, n_op, shift, _, psi, right_in, *outs):
    n_pair = n_op // 2
    psi_out, right_out, right, sems = outs[:n_blk], outs[n_blk : n_blk + n_pair], outs[-2], outs[-1]
    terms, local, width, _ = right.shape
    cols = local * width // n_op
    per = cols // width
    own_blk, own_op = place_of()
    fetch = pltpu.make_async_copy(right_in, right, sems.at[2 * n_blk])
    fetch.start()
    copies = []
    for d in range(n_blk):
        there = ring_at(ring_place(own_blk, n_blk) + d, n_blk) * n_op
        for h in range(psi_out[d].shape[1] // cols):
            start = pl.multiple_of((there + (own_op ^ h)) * cols, LANES)
            copy = pltpu.make_async_copy(
                psi.at[0, :, pl.ds(start, cols)],
                psi_out[d].at[:, h * cols : (h + 1) * cols],
                sems.at[2 * d + h],
            )
            copy.start()
            copies.append(copy)
    lane = lax.broadcasted_iota(jnp.int32, (16, 2 * cols), 1)
    line = jnp.zeros((16, 2 * cols), jnp.float32)
    for k in range(terms):
        line = jnp.where(lane == k, shift[k].astype(jnp.float32), line)
    square = [lax.broadcasted_iota(jnp.int32, (width, width), axis) for axis in (0, 1)]
    unit = (square[0] == square[1]).astype(jnp.bfloat16)
    fetch.wait()
    for e in range(n_pair):
        for k in range(terms):
            turned = []
            for h in range(2):
                first = (own_op ^ (2 * e) ^ h) * per
                for r in range(per):
                    turned.append(
                        lax.dot_general(
                            right[k, first + r], unit, (((0,), (0,)), ((), ())),
                            preferred_element_type=jnp.float32,
                        )
                    )
            side_by_side = jnp.concatenate(turned, axis=1).astype(jnp.bfloat16)
            right_out[e][k * width : (k + 1) * width] = side_by_side
        right_out[e][terms * width :] = line.astype(jnp.bfloat16)
    for copy in copies:
        copy.wait()


def table_body(n_blk, terms, sector, width, left_diag, right_diag, *refs):
    tails, src, widths, slots, diag, right_out = refs[:-5], *refs[-5:]
    right_out[...] = right_diag[...]
    n_pair = len(tails)
    rows, cols = tails[0].shape
    own_blk, _ = place_of()
    lane = lax.broadcasted_iota(jnp.int32, (16, cols), 1)
    for d in range(n_blk):
        slot = ring_at(ring_place(own_blk, n_blk) - d, n_blk)
        slots[d] = slot
        widths[d] = width[sector[slot]]
    for e in range(n_pair):
        tail = tails[e][rows - 16 :].astype(jnp.float32)
        for k in range(terms):
            shift = jnp.max(jnp.where(lane == k, tail, -1e9)).astype(jnp.int32)
            for t in range(n_blk):
                want = sector[slots[t]] - shift
                found = jnp.int32(n_blk)
                for d in range(n_blk):
                    found = jnp.where(sector[slots[d]] == want, d, found)
                src[(t * n_pair + e) * terms + k] = found
    for d in range(n_blk):
        row = left_diag[pl.ds(slots[d], 1), :]
        diag[d] = jnp.transpose(jnp.broadcast_to(row, (diag.shape[2], row.shape[1])))


def diagonal(diag, right_diag, d, h):
    cols = diag.shape[2]
    _, own_op = place_of()
    start = pl.multiple_of((own_op ^ h) * cols, LANES)
    return diag[d] + right_diag[:, pl.ds(start, cols)]


def row_mask(width, shape):
    return lax.broadcasted_iota(jnp.int32, shape, 0) < width


def fold(x):
    return jnp.sum(x.reshape(-1, 8, x.shape[-1]), axis=0)


def whole(x):
    return jnp.sum(jnp.sum(x, axis=0, keepdims=True), axis=1, keepdims=True)


def spread(values, out):
    lane = lax.broadcasted_iota(jnp.int32, out.shape[1:], 1)
    row = jnp.zeros(out.shape[1:], jnp.float32)
    for j, value in enumerate(values):
        row = jnp.where(lane == j, value, row)
    for d in range(out.shape[0]):
        out[d] = row


def by_block(packed, terms, k):
    rows, cols = packed.shape
    width = (rows - 16) // terms
    lane = lax.broadcasted_iota(jnp.int32, (width, cols), 1)
    block = packed[k * width : (k + 1) * width].astype(jnp.float32)
    parts = []
    for r in range(cols // width):
        inside = (lane >= r * width) & (lane < (r + 1) * width)
        parts.append(jnp.where(inside, block, 0.0).astype(jnp.bfloat16))
    return jnp.concatenate(parts, axis=0)


def left_products(block, left, inter):
    n_terms, rows, cols = inter.shape
    at = 0
    while at < n_terms:
        ops = left(at)
        terms = ops.shape[0]
        prod = jnp.dot(ops.reshape(terms * rows, rows), block, preferred_element_type=jnp.float32)
        inter[at : at + terms] = prod.astype(jnp.bfloat16).reshape(terms, rows, cols)
        at += terms


def sum_terms(src, widths, inter, right, out, emit):
    n_blk, n_terms, _, _ = inter.shape
    n_blk -= 1
    terms = n_terms // len(right)
    turned = [by_block(right[j // terms], terms, j % terms) for j in range(n_terms)]
    for t in range(n_blk):
        total = None
        for j in range(n_terms):
            part = jnp.dot(
                inter[src[t * n_terms + j], j], turned[j], preferred_element_type=jnp.float32
            )
            total = part if total is None else total + part
        total = jnp.where(row_mask(widths[t], total.shape), total, 0.0)
        out[t] = total.astype(jnp.bfloat16)
        emit(t, total)


def keep(left, left_out, sems):
    copies = []
    for d, line in enumerate(left):
        for e, ref in enumerate(line):
            copies.append(pltpu.make_async_copy(ref, left_out.at[d, e], sems.at[d * len(line) + e]))
            copies[-1].start()
    return copies


def masked(psi, width, out):
    at = 0
    for ref in psi:
        block = ref[...].astype(jnp.float32)
        block = jnp.where(row_mask(width, block.shape), block, 0.0)
        out[:, at : at + block.shape[1]] = block.astype(jnp.bfloat16)
        at += block.shape[1]


def take(refs, counts):
    out = []
    for count in counts:
        out.append(refs[:count])
        refs = refs[count:]
    return out, refs


def products_of(psi, left, widths, first, raw_out, inter):
    for d, line in enumerate(left):
        masked(psi[d], widths[first + d], raw_out.at[d])
        terms = line[0].shape[0]
        left_products(raw_out[d], lambda at: line[at // terms][...], inter.at[d])


def early_body(n_pair, counts, widths, *refs):
    left, refs = take(refs, [n_pair] * len(counts))
    psi, (raw_out, inter_out, left_out, sems) = take(refs, counts)
    copies = keep(left, left_out, sems)
    products_of(psi, left, widths, 0, raw_out, inter_out)
    for copy in copies:
        copy.wait()


def first_body(n_blk, n_pair, counts, src, widths, *refs):
    n_late = len(counts)
    n_early = n_blk - n_late
    left, refs = take(refs, [n_pair] * n_late)
    (right,), refs = take(refs, [n_pair])
    psi, refs = take(refs, counts)
    raw_in, inter_in, diag, right_diag, part_out, raw_out, left_out, dots_out, inter, sems = refs
    ready = []
    for j, (given, own) in enumerate(((inter_in, inter), (raw_in, raw_out))):
        ready.append(
            pltpu.make_async_copy(given, own.at[:n_early], sems.at[n_late * n_pair + j])
        )
        ready[-1].start()
    copies = keep(left, left_out, sems)
    inter[n_blk] = jnp.zeros_like(inter[n_blk])
    products_of(
        psi, left, widths, n_early, raw_out.at[n_early:], inter.at[n_early:n_blk]
    )
    for copy in ready:
        copy.wait()
    cols = diag.shape[2]
    zero = jnp.zeros((8, cols), jnp.float32)
    sums = [zero, zero]

    def emit(d, total):
        for h in range(2):
            part = slice(h * cols, (h + 1) * cols)
            raw = raw_out[d, :, part].astype(jnp.float32)
            image = total[:, part]
            if h == 0:
                image = image + diagonal(diag, right_diag, d, h) * raw
                sums[0] = sums[0] + fold(raw * raw)
            sums[1] = sums[1] + fold(raw * image)

    sum_terms(src, widths, inter, right, part_out, emit)
    spread([whole(x) for x in sums], dots_out)
    for copy in copies:
        copy.wait()


def send_rows(e, send, d, *refs):
    _, own_op = place_of()
    step = send.shape[2]
    rows = pl.ds(pl.multiple_of((own_op ^ e) * step, step), step)
    for j, ref in enumerate(refs):
        send[j, d] = ref[d, rows].astype(send.dtype)


def total_of(mine, other, d, h, cols):
    own = mine[d, :, h * cols : (h + 1) * cols].astype(jnp.float32)
    return own + other[d, :, (1 - h) * cols : (2 - h) * cols].astype(jnp.float32)


def sigma_body(mine, other, raw_in, diag, right_diag, sig_out, *sends):
    n_blk, _, cols = diag.shape
    for d in range(n_blk):
        for h in range(2):
            part = slice(h * cols, (h + 1) * cols)
            raw = raw_in[d, :, part].astype(jnp.float32)
            sigma = total_of(mine, other, d, h, cols) + diagonal(diag, right_diag, d, h) * raw
            sig_out[d, :, part] = sigma
        for e, send in enumerate(sends, 1):
            send_rows(2 * e, send, d, raw_in, sig_out)


def norm_theta(parts, count):
    tot = jnp.sum(parts, axis=0) * (1.0 / count)
    scale = lax.rsqrt(tot[:, 0:1] + EPS)
    return scale, tot[:, 1:2] * scale * scale


def second_body(n_blk, n_pair, count, src, widths, left_early, left_late, *refs):
    right, refs = refs[:n_pair], refs[n_pair:]
    parts, raw_in, sig, diag, right_diag, dots_out, own_out = refs[:7]
    sends, (inter, corr, fld, part_out, held, sems) = refs[7:-6], refs[-6:]
    copies = []
    n_early = left_early.shape[0]
    for d in range(n_blk):
        kept = left_early.at[d] if d < n_early else left_late.at[d - n_early]
        copies.append(pltpu.make_async_copy(kept, held.at[d], sems.at[d]))
        copies[-1].start()
    inter[n_blk] = jnp.zeros_like(inter[n_blk])
    scale, theta = norm_theta(parts[...], count)
    cols = diag.shape[2]
    halves = []
    for h in range(2):
        part = slice(h * cols, (h + 1) * cols)
        vv = vc = vs = jnp.zeros((8, cols), jnp.float32)
        for d in range(n_blk):
            vec = raw_in[d, :, part].astype(jnp.float32) * scale
            sigma = sig[d, :, part] * scale
            den = diagonal(diag, right_diag, d, h) - theta
            item = (sigma - theta * vec) * den / jnp.maximum(den * den, 0.25)
            corr[d, :, part] = item
            vv, vc = vv + fold(vec * vec), vc + fold(vec * item)
            if h == 0:
                vs = vs + fold(vec * sigma)
        halves.append((whole(vv), whole(vc), vs))
    along = (halves[0][1] + halves[1][1]) / jnp.maximum(halves[0][0] + halves[1][0], 1e-30)
    terms = held.shape[2]
    for d in range(n_blk):
        for h in range(2):
            part = slice(h * cols, (h + 1) * cols)
            vec = raw_in[d, :, part].astype(jnp.float32) * scale
            fld[d, :, part] = (corr[d, :, part] - along * vec).astype(jnp.bfloat16)
    for d in range(n_blk):
        copies[d].wait()
        left_products(fld[d], lambda at: held[d, at // terms], inter.at[d])
    zero = jnp.zeros((8, cols), jnp.float32)
    sums = [zero for _ in range(5)]

    def emit(d, total):
        for h in range(2):
            part = slice(h * cols, (h + 1) * cols)
            field = fld[d, :, part].astype(jnp.float32)
            raw = raw_in[d, :, part].astype(jnp.float32)
            image = total[:, part]
            if h == 0:
                image = image + diagonal(diag, right_diag, d, h) * field
                for j, prod in enumerate((field * field, raw * field, field * sig[d, :, part])):
                    sums[j] = sums[j] + fold(prod)
            sums[3] = sums[3] + fold(raw * image)
            sums[4] = sums[4] + fold(field * image)
        for e, send in enumerate(sends, 1):
            send_rows(e, send, d, *((part_out,) if e % 2 else (fld, part_out)))
        rows = pl.ds(pl.multiple_of(own_op * step, step), step)
        for j, ref in enumerate((raw_in, sig, fld, part_out)):
            own_out[j, d] = ref[d, rows].astype(own_out.dtype)

    _, own_op = place_of()
    step = own_out.shape[2]
    sum_terms(src, widths, inter, right, part_out, emit)
    vv, vc, vs = halves[0]
    ff, vf, fs, vt, ft = (whole(x) for x in sums)
    spread([vv, vc, whole(vs), ff, vf * scale, fs * scale, vt * scale, ft], dots_out)


def ritz_pair(theta, h_mix, h_two):
    diff, twice = theta - h_two, 2.0 * h_mix
    size = jnp.sqrt(diff * diff + twice * twice)
    some = size > 0.0
    safe = jnp.where(some, size, 1.0)
    big = jnp.sqrt(0.5 + 0.5 * jnp.abs(diff) / safe)
    small = 0.5 * jnp.abs(twice) / (safe * big)
    sine = jnp.where(diff >= 0.0, small, big)
    cosine = jnp.where(diff >= 0.0, big, small)
    sine = jnp.where(some, sine, 0.0)
    cosine = jnp.where(some, cosine, 1.0)
    upward = (twice > 0.0) | ((twice == 0.0) & (diff < 0.0))
    return sine, jnp.where(upward, -cosine, cosine), 0.5 * (theta + h_two) - 0.5 * size


def third_body(n_blk, n_op, count, slots, parts1, parts2, diag, right_diag, own, *refs):
    n_far = n_op // 2 - 1
    got1, got2 = refs[:n_far], refs[n_far : n_far + n_op - 1]
    new_out, res_out, energy_out = refs[n_far + n_op - 1 :]
    step, cols = new_out.shape[1], new_out.shape[2] // n_op
    own_blk, own_op = place_of()
    scale, theta = norm_theta(parts1[...], count)
    pairs = parts2[...].reshape(n_blk * n_op // 2, 2, *parts2.shape[1:])
    pairs = pairs[:, 0] + pairs[:, 1]
    vv, vc, vs, ff, vf, fs, vt, ft = (pairs[:, 0, j : j + 1] for j in range(8))

    def mean(x):
        return jnp.sum(x, axis=0, keepdims=True) * (1.0 / count)

    def nearest(vv, vc):
        return vc / jnp.maximum(vv, 1e-30)

    along = mean(vc)
    beta = nearest(vv, vc) - along
    norm_sq = mean(ff + 2.0 * beta * vf + beta * beta * vv)
    unit = lax.rsqrt(jnp.maximum(norm_sq, 0.0) + EPS)
    v_s1 = unit * mean(vt + beta * vs)
    u_s0 = unit * mean(fs + beta * vs)
    u_s1 = unit * unit * mean(ft + beta * (vt + fs) + beta * beta * vs)
    cv, cu, energy = ritz_pair(theta, 0.5 * (v_s1 + u_s0), u_s1)
    energy_out[0] = jnp.max(energy)
    cu = cu * unit
    mine = pl.ds(pl.multiple_of(own_op * step, step), step)
    for e in range(0, n_op, 2):
        there = own_blk * n_op + (own_op ^ e)
        pair = parts2[there] + parts2[own_blk * n_op + (own_op ^ e ^ 1)]
        on_vec = cv + cu * (nearest(pair[:, 0:1], pair[:, 1:2]) - along)
        for h in range(2):
            at = pl.multiple_of((own_op ^ e ^ h) * cols, LANES)
            part, crossed = slice(h * cols, (h + 1) * cols), slice((1 - h) * cols, (2 - h) * cols)
            for d in range(n_blk):
                dmat = diag[d, mine] + right_diag[:, pl.ds(at, cols)]
                blocks = [own.at[j] for j in range(4)]
                if e:
                    far, near = got1[e // 2 - 1], got2[e - 1]
                    blocks = far.at[0], far.at[1], near.at[0], near.at[1]
                raw, sigma, fld, image = (x[d, :, part].astype(jnp.float32) for x in blocks)
                vec, sigma = raw * scale, sigma * scale
                image = image + got2[e][0, d, :, crossed].astype(jnp.float32) + dmat * fld
                newvec = on_vec * vec + cu * fld
                res = on_vec * sigma + cu * image - energy * newvec
                new_out[slots[d], :, pl.ds(at, cols)] = newvec.astype(jnp.bfloat16)
                res_out[slots[d], :, pl.ds(at, cols)] = res.astype(jnp.bfloat16)


def per_device(
    psi, left_ops, right_ops, term_shift, slot_sector, sector_width, diag_left, diag_right
):
    n_blk, n_op = lax.axis_size("blk"), lax.axis_size("op")
    _, rows, ncols = psi.shape
    terms, _, width, _ = right_ops.shape
    n_pair = n_op // 2
    cols = diag_right.shape[0] // n_op
    step = rows // n_op
    count = float(n_blk * rows * ncols)
    n_dev = n_blk * n_op
    bf16, f32, i32 = jnp.bfloat16, jnp.float32, jnp.int32
    last = sorted(range(1, n_blk), key=lambda d: min(d, n_blk - d))[-1]

    def pack():
        first = swap(term_shift, 1, n_op)
        sent = kernel(
            functools.partial(pack_body, n_blk, n_op),
            [(term_shift, SMEM), (first, SMEM), (psi, HBM), (right_ops, HBM)],
            [((rows, 2 * cols if d in (0, last) else cols), bf16, VMEM) for d in range(n_blk)]
            + [((terms * width + 16, 2 * cols), bf16, VMEM)] * n_pair,
            [pltpu.VMEM(right_ops.shape, bf16), pltpu.SemaphoreType.DMA((2 * n_blk + 1,))],
            nbytes=1 << 20,
        )
        return sent[:n_blk], sent[n_blk:]

    def table(right):
        return kernel(
            functools.partial(table_body, n_blk, terms),
            [(slot_sector, SMEM), (sector_width, SMEM), (diag_left, VMEM), (diag_right[None], VMEM)]
            + [(block, VMEM) for block in right],
            [((n_blk * n_pair * terms,), i32, SMEM)]
            + [((n_blk,), i32, SMEM)] * 2
            + [((n_blk, rows, LANES), f32, VMEM), ((1, n_op * cols), f32, VMEM)],
        )

    def inputs(left, psi, those):
        blocks = [left[d, 2 * e] for d in those for e in range(n_pair)]
        halves = [half for d in those for half in psi[d]]
        return [(x, VMEM) for x in blocks], [(x, VMEM) for x in halves], [len(psi[d]) for d in those]

    def early(left, psi, n_early, tables):
        left_ins, psi_ins, counts = inputs(left, psi, range(n_early))
        return kernel(
            functools.partial(early_body, n_pair, counts),
            [(tables[1], SMEM)] + left_ins + psi_ins,
            [
                ((n_early, rows, 2 * cols), bf16, VMEM),
                ((n_early, n_pair * terms, rows, 2 * cols), bf16, VMEM),
                ((n_early, n_pair, terms, rows, rows), bf16, HBM),
            ],
            [pltpu.SemaphoreType.DMA((n_early * n_pair,))],
            flops=2 * n_early * rows * rows * 2 * cols * terms * n_pair,
            nbytes=4 << 20,
        )

    left, psi_by, right, (src, widths, slots, *both), (raw_early, inter_early, left_early) = gather(
        left_ops[:, 0], n_blk, n_op, pack, table, early
    )
    n_early = raw_early.shape[0]
    n_late = n_blk - n_early
    left_ins, psi_ins, counts = inputs(left, psi_by, range(n_early, n_blk))
    right_ins = [(block, VMEM) for block in right]
    diags = [(x, VMEM) for x in both]

    tables = [(src, SMEM), (widths, SMEM)]
    narrow = ((n_blk, rows, 2 * cols), bf16, VMEM)
    dots = ((n_dev, 1, LANES), f32, VMEM)
    wide = ((n_blk, rows, 2 * cols), f32, VMEM)
    sends = [((2 - e % 2, n_blk, step, 2 * cols), bf16, VMEM) for e in range(1, n_op)]
    inter = pltpu.VMEM((n_blk + 1, n_pair * terms, rows, 2 * cols), bf16)
    left_late = (n_late, n_pair, terms, rows, rows)
    cost = dict(flops=2 * n_blk * rows * 2 * cols * terms * n_pair * (rows + 2 * cols), nbytes=6 << 20)

    def totals(parts):
        return lax.all_to_all(parts, ("blk", "op"), 0, 0, tiled=True)

    part1, raw, kept, dots1 = kernel(
        functools.partial(first_body, n_blk, n_pair, counts),
        tables + left_ins + right_ins + psi_ins + [(raw_early, VMEM), (inter_early, VMEM)] + diags,
        [narrow, narrow, (left_late, bf16, HBM), dots],
        [inter, pltpu.SemaphoreType.DMA((n_late * n_pair + 2,))],
        **cost,
    )
    parts1 = totals(dots1)
    sig, *out1 = kernel(
        sigma_body,
        [(x, VMEM) for x in (part1, swap(part1, 1, n_op), raw)] + diags,
        [wide] + sends[1::2],
        nbytes=4 << 20,
    )
    got1 = [swap(block, 2 * e, n_op) for e, block in enumerate(out1, 1)]
    dots2, own, *out2 = kernel(
        functools.partial(second_body, n_blk, n_pair, count),
        tables + [(left_early, HBM), (kept, HBM)] + right_ins
        + [(x, VMEM) for x in (parts1, raw, sig)] + diags,
        [dots, ((4, n_blk, step, 2 * cols), bf16, VMEM)] + sends,
        [
            inter,
            pltpu.VMEM((n_blk, rows, 2 * cols), f32),
            pltpu.VMEM((n_blk, rows, 2 * cols), bf16),
            pltpu.VMEM((n_blk, rows, 2 * cols), bf16),
            pltpu.VMEM((n_blk, *left_late[1:]), bf16),
            pltpu.SemaphoreType.DMA((n_blk,)),
        ],
        flops=4 * cost["flops"],
        nbytes=24 << 20,
    )
    near, got1 = lax.optimization_barrier((out2[0], got1))
    parts2 = totals(dots2)
    got2 = [swap(near, 1, n_op)] + [swap(block, e, n_op) for e, block in enumerate(out2[1:], 2)]
    final = ((n_blk, step, n_op * cols), bf16, VMEM)
    new, res, energy = kernel(
        functools.partial(third_body, n_blk, n_op, count),
        [(slots, SMEM)] + [(x, VMEM) for x in (parts1, parts2)] + diags
        + [(x, VMEM) for x in (own, *got1, *got2)],
        [final, final, ((1,), f32, SMEM)],
        nbytes=4 << 20,
    )
    return new, res, energy


def solution(mesh):
    placed = (
        P(("grp", "blk"), None, None),
        P("op", ("grp", "blk"), None, None),
        P("op", ("grp", "blk"), None, None),
        P("op"),
        P("grp"),
        P("grp"),
        P("grp", None),
        P(("grp", "blk")),
    )

    def body(*args):
        psi, left_ops, right_ops, diag_right = args[0], args[1], args[2], args[7]
        n_op = mesh.shape["op"]
        cols = diag_right.shape[0] // n_op
        fits = (
            psi.shape[0] == 1
            and diag_right.shape[0] % n_op == 0
            and cols == LANES
            and n_op % 2 == 0
            and cols % right_ops.shape[2] == 0
            and cols // right_ops.shape[2] * n_op == right_ops.shape[1]
            and psi.shape[1] % (16 * n_op) == 0
            and n_op & (n_op - 1) == 0
            and mesh.shape["blk"] > n_op.bit_length() - 1
        )
        return (per_device if fits else per_device_general)(*args)

    return jax.shard_map(
        body,
        mesh=mesh,
        in_specs=placed,
        out_specs=(P("grp", "op", "blk"), P("grp", "op", "blk"), P("grp")),
        check_vma=False,
    )
```
